32 devices in a mesh: fsdp: 8 (over y, x, core), seq: 4 (over z).
Axes of the slice: x: 2, y: 2, z: 4, core: 2. Of those that a mesh axis runs over, the one named last changes fastest.
Arguments:
- tokens: bfloat16 [24, 1024, 768], P('fsdp', 'seq'), may hold values from -6 to 6
- lengths: int32 [24, 10], P('fsdp'), may hold values from 0 to 1024, as said below
- pictures: int32 [24, 1024], P('fsdp', 'seq'), may hold values from 0 to 8, as said below
- first_gain: bfloat16 [768], P('fsdp'), may hold values from 0.5 to 1.5
- mix_weight: bfloat16 [768, 2304], P('fsdp'), may hold values from -0.21875 to 0.21875
- query_gain: bfloat16 [768], P('fsdp'), may hold values from 0.796875 to 2
- key_gain: bfloat16 [768], P('fsdp'), may hold values from 0.796875 to 2
- out_weight: bfloat16 [768, 768], P('fsdp'), may hold values from -1.75 to 1.75
- second_gain: bfloat16 [768], P('fsdp'), may hold values from 0.5 to 1.5
- up_weight: bfloat16 [768, 3072], P('fsdp'), may hold values from -0.21875 to 0.21875
- down_weight: bfloat16 [3072, 768], P('fsdp'), may hold values from -0.109375 to 0.109375
- cotangent: bfloat16 [24, 1024, 768], P('fsdp', 'seq'), may hold values from -6 to 6
Outputs:
- output: bfloat16 [24, 1024, 768], P('fsdp', 'seq')
- input_grad: bfloat16 [24, 1024, 768], P('fsdp', 'seq')
- first_gain_grad: float32 [768], P('fsdp')
- mix_weight_grad: float32 [768, 2304], P('fsdp')
- query_gain_grad: float32 [768], P('fsdp')
- key_gain_grad: float32 [768], P('fsdp')
- out_weight_grad: float32 [768, 768], P('fsdp')
- second_gain_grad: float32 [768], P('fsdp')
- up_weight_grad: float32 [768, 3072], P('fsdp')
- down_weight_grad: float32 [3072, 768], P('fsdp')
The draws below stay inside these ranges and needn't reach their ends.
Inputs may be any that keep to these rules, and one draw needn't show every extreme that they name: In each row the nonzero lengths come first, each 100 or more, and sum to 922 or more and 1024 or less; later entries are 0. Rows whose index is a multiple of 8 hold one picture of 1024 patches; rows whose index leaves 1 after division by 8 hold (922) // 100 pictures. Slot s of a row holds the number (from 0, in the order of lengths) of the picture whose patches cover s when the row's pictures are laid end to end by lengths; slots after the last picture hold the last picture's number. Numbers never fall along a row.
All inputs are finite; a program needn't handle non-finite values.
Results may differ from the reference program's by a relative error of at most 0.017.
Values may be sent and summed in bfloat16 or wider, within the bound.
A program may use at most 128 MiB of HBM per device.

```python
import jax
import jax.numpy as jnp
from jax import lax

D = 768
HEADS = 12
HEAD = 64
FF = 3072
LEN = 1024
PIC_MIN = 100
ROWS = 24
PICS = 10


def picture_lengths(key):
    least_total = LEN - LEN // 10
    most_count = least_total // PIC_MIN
    row_index = jnp.arange(ROWS)
    counts = jax.random.randint(jax.random.fold_in(key, 11), (ROWS,), 1, most_count + 1)
    counts = jnp.where(row_index % 8 == 0, 1, jnp.where(row_index % 8 == 1, most_count, counts))
    filled = jax.random.randint(jax.random.fold_in(key, 12), (ROWS,), least_total, LEN + 1)
    filled = jnp.where(row_index % 8 == 0, LEN, filled)
    slot_index = jnp.arange(PICS)
    live_slot = slot_index[None, :] < counts[:, None]
    shares = jnp.where(live_slot, jax.random.randint(jax.random.fold_in(key, 13), (ROWS, PICS), 1, 1001), 0)
    spare_room = filled - PIC_MIN * counts
    extra_share = spare_room[:, None] * shares // jnp.sum(shares, axis=1, keepdims=True)
    leftover = spare_room - jnp.sum(extra_share, axis=1)
    extra_share = extra_share + jnp.where(slot_index[None, :] == 0, leftover[:, None], 0)
    return jnp.where(live_slot, PIC_MIN + extra_share, 0).astype(jnp.int32)


def draw_lengths(key, part):
    return picture_lengths(key)


def draw_pictures(key, part):
    lengths = picture_lengths(key)
    starts = jnp.cumsum(lengths, axis=1) - lengths
    position = jnp.arange(LEN)
    has_begun = (starts[:, None, :] <= position[None, :, None]) & (lengths[:, None, :] > 0)
    return (jnp.sum(has_begun.astype(jnp.int32), axis=2) - 1).astype(jnp.int32)


def block_scale(own_key, extent, pieces, least, high):
    factor_of, own = 1.0, jax.random.fold_in(own_key, 6)
    for axis_at, shards_of in pieces:
        heights = jnp.exp(jax.random.uniform(jax.random.fold_in(own, axis_at), (shards_of,), jnp.float32, least / len(pieces), high / len(pieces)))
        factor_of = factor_of * jnp.repeat(heights, extent[axis_at] // shards_of).reshape([-1 if axis == axis_at else 1 for axis in range(len(extent))])
    return factor_of


def scatter_about(stream_key, extent, scale, most, split=(), kind=jnp.bfloat16):
    loudness = block_scale(stream_key, extent, split, -0.22, 0.18) if split else 1.0
    values = jax.random.normal(stream_key, extent, jnp.float32) * scale * loudness
    return jnp.minimum(jnp.maximum(values, -most), most).astype(kind)


def setup_inputs(seed: int = 0) -> dict:
    seeds = jax.random.split(jax.random.key(seed), 13)
    return {
        "tokens": scatter_about(seeds[0], (ROWS, LEN, D), 1.0, 6.0, ((0, 8), (1, 4))),
        "lengths": draw_lengths(jax.random.fold_in(seeds[12], 71), 0),
        "pictures": draw_pictures(jax.random.fold_in(seeds[12], 71), 0),
        "first_gain": jnp.clip(0.5 + 1.0 * jax.random.uniform(seeds[3], (D,), jnp.float32) ** block_scale(seeds[3], (D,), ((0, 8),), -0.2, 0.2), 0.5, 1.5).astype(jnp.bfloat16),
        "mix_weight": scatter_about(seeds[4], (D, 3 * D), D ** -0.5, 0.21875, ((0, 8),)),
        "query_gain": jnp.clip(0.796875 + 1.203125 * jax.random.uniform(seeds[5], (D,), jnp.float32) ** block_scale(seeds[5], (D,), ((0, 8),), -0.2, 0.2), 0.796875, 2.0).astype(jnp.bfloat16),
        "key_gain": jnp.clip(0.796875 + 1.203125 * jax.random.uniform(seeds[6], (D,), jnp.float32) ** block_scale(seeds[6], (D,), ((0, 8),), -0.2, 0.2), 0.796875, 2.0).astype(jnp.bfloat16),
        "out_weight": scatter_about(seeds[7], (D, D), (max(D // 64, 1)) ** -0.5, 1.75, ((0, 8),)),
        "second_gain": jnp.clip(0.5 + 1.0 * jax.random.uniform(seeds[8], (D,), jnp.float32) ** block_scale(seeds[8], (D,), ((0, 8),), -0.2, 0.2), 0.5, 1.5).astype(jnp.bfloat16),
        "up_weight": scatter_about(seeds[9], (D, FF), D ** -0.5, 0.21875, ((0, 8),)),
        "down_weight": scatter_about(seeds[10], (FF, D), FF ** -0.5, 0.109375, ((0, 8),)),
        "cotangent": scatter_about(seeds[11], (ROWS, LEN, D), 1.0, 6.0, ((0, 8), (1, 4))),
    }


@jax.custom_vjp
def low(v):
    return lax.optimization_barrier(v.astype(jnp.bfloat16)).astype(jnp.float32)

@jax.custom_vjp
def low_back(v):
    return v

def low_keep(v):
    return (low(v), None)

def low_pass(kept, grad):
    return (grad,)

def back_keep(v):
    return (v, None)

def back_low(kept, grad):
    return (low(grad),)
low.defvjp(low_keep, low_pass)
low_back.defvjp(back_keep, back_low)
EPSILON = 1e-06
HIGHEST = lax.Precision.HIGHEST

def norm_rows(values, gain_row):
    center = values - lax.optimization_barrier(jnp.mean(values, axis=-1, keepdims=True))
    spread = lax.optimization_barrier(jnp.mean(center * center, axis=-1, keepdims=True))
    return center * lax.rsqrt(spread + EPSILON) * gain_row

def attend_row(inputs):
    queries, keys_row, values_row, lower_bound, upper_bound = inputs
    key_place = jnp.arange(keys_row.shape[0])
    allowed = (key_place[None, :] >= lower_bound[:, None]) & (key_place[None, :] < upper_bound[:, None])
    scores = jnp.einsum('qhc,khc->hqk', queries, keys_row, precision=HIGHEST) * HEAD ** (-0.5)
    scores = low_back(scores)
    scores = jnp.where(allowed[None], scores, -jnp.inf)
    log_total = jax.nn.logsumexp(scores, axis=-1, keepdims=True)
    soft_weights = low(jnp.exp(scores - log_total))
    return jnp.einsum('hqk,khc->qhc', soft_weights, values_row, precision=HIGHEST)

def forward(tokens_in, first_gain, mix_weight, query_gain, key_gain, out_weight, second_gain, up_weight, down_weight, lower_bound, upper_bound):
    row_count = tokens_in.shape[0]
    row_length = tokens_in.shape[1]
    normed = low(norm_rows(tokens_in, first_gain))
    mixed_all = low_back(jnp.einsum('rsd,de->rse', normed, mix_weight, precision=HIGHEST))
    mixed_parts = mixed_all.reshape(row_count, row_length, 3, HEADS, HEAD)
    queries = low_back(low(norm_rows(mixed_parts[:, :, 0], query_gain.reshape(HEADS, HEAD))))
    keys_all = low_back(low(norm_rows(mixed_parts[:, :, 1], key_gain.reshape(HEADS, HEAD))))
    values_all = low_back(low(mixed_parts[:, :, 2]))
    attended = lax.map(jax.checkpoint(attend_row), (queries, keys_all, values_all, lower_bound, upper_bound))
    attended = low_back(low(attended)).reshape(row_count, row_length, D)
    branch = low_back(jnp.einsum('rsd,de->rse', attended, out_weight, precision=HIGHEST))
    middle = tokens_in + branch
    second = low(norm_rows(middle, second_gain))
    hidden_pre = low_back(jnp.einsum('rsd,df->rsf', second, up_weight, precision=HIGHEST))
    hidden = low(jax.nn.gelu(hidden_pre, approximate=False))
    return middle + low_back(jnp.einsum('rsf,fd->rsd', hidden, down_weight, precision=HIGHEST))

def reference(tokens, lengths, pictures, first_gain, mix_weight, query_gain, key_gain, out_weight, second_gain, up_weight, down_weight, cotangent):
    params = tuple((weight_arg.astype(jnp.float32) for weight_arg in (first_gain, mix_weight, query_gain, key_gain, out_weight, second_gain, up_weight, down_weight)))
    starts = (jnp.cumsum(lengths, axis=1) - lengths).astype(jnp.int32)
    lower_bound = jnp.take_along_axis(starts, pictures.astype(jnp.int32), axis=1).astype(jnp.int32)
    upper_bound = (lower_bound + jnp.take_along_axis(lengths, pictures.astype(jnp.int32), axis=1)).astype(jnp.int32)
    filled = lax.optimization_barrier(jnp.sum(lengths, axis=1))
    valid_slot = (jnp.arange(LEN)[None, :] < filled[:, None]).astype(jnp.float32)
    groups = ROWS // 4

    def shape_rows(array):
        return array.reshape((groups, 4) + array.shape[1:])

    def one_group(carry_sums, inputs):
        block_tokens, block_lower, block_upper, block_valid, block_cot = inputs

        def run_rows(token_rows, gain_a, weight_mix, gain_query, gain_key, weight_out, gain_b, weight_up, weight_down):
            return forward(token_rows, gain_a, weight_mix, gain_query, gain_key, weight_out, gain_b, weight_up, weight_down, block_lower, block_upper)
        result, pullback = jax.vjp(run_rows, block_tokens.astype(jnp.float32), params[0], params[1], params[2], params[3], params[4], params[5], params[6], params[7])
        gradients = pullback(block_cot.astype(jnp.float32) * block_valid[..., None])
        summed = tuple((held_sum + fresh_grad for held_sum, fresh_grad in zip(carry_sums, gradients[1:])))
        return (summed, (result.astype(jnp.bfloat16), gradients[0].astype(jnp.bfloat16)))
    start_sums = tuple((jnp.zeros_like(weight_arg) for weight_arg in params))
    grad_sums, (outputs, input_grads) = lax.scan(one_group, start_sums, (shape_rows(tokens), shape_rows(lower_bound), shape_rows(upper_bound), shape_rows(valid_slot), shape_rows(cotangent)))
    return (outputs.reshape(ROWS, LEN, D), input_grads.reshape(ROWS, LEN, D), grad_sums[0], grad_sums[1], grad_sums[2], grad_sums[3], grad_sums[4], grad_sums[5], grad_sums[6], grad_sums[7])
```

```python
import functools

import jax
import jax.numpy as jnp
from jax import lax
from jax.experimental import pallas as pl
from jax.experimental.pallas import tpu as pltpu
from jax.sharding import Mesh, PartitionSpec as P

HEADS = 12
HEAD = 64
EPSILON = 1e-06
BLOCK = 256
MARK = 32.0
EXP2_FACTOR = HEAD**-0.5 * 1.4426950408889634
F32 = jnp.float32
BF16 = jnp.bfloat16
VMEM_LIMIT = 56 * 1024 * 1024

SEQ = ("zp", "zq")
COLUMN = ("core", "zp", "zq")
KEEP = [
    (core * 4 + z, (z // 2) * 4 + 2 * core + z % 2) for core in range(2) for z in range(4)
]
CROSS = [
    (core * 4 + z, (z // 2) * 4 + 2 * core + 1 - z % 2) for core in range(2) for z in range(4)
]


def inverse(pairs):
    return [(target, source) for source, target in pairs]


def swap(array, name, bit=1):
    count = lax.axis_size(name)
    return lax.ppermute(array, name, [(i, i ^ bit) for i in range(count)])


def pick(array, index, axis=0):
    return lax.dynamic_index_in_dim(array, index, axis, keepdims=False)


def ordered(mine, other, place, axis):
    first = jnp.where(place == 0, mine, other)
    second = jnp.where(place == 0, other, mine)
    return jnp.concatenate([first, second], axis=axis)


def chip_bits():
    count = lax.axis_size("chip")
    bits = count.bit_length() - 1
    return bits, [(lax.axis_index("chip") >> b) & 1 for b in range(bits)]


def gather_one(block, order):
    bits, mine = chip_bits()
    done = []
    for b in order:
        other = swap(block, "chip", 1 << b)
        axis = sum(1 for d in done if d > b)
        low = jnp.where(mine[b] == 0, block, other)
        high = jnp.where(mine[b] == 0, other, block)
        block = jnp.stack([low, high], axis=axis)
        done.append(b)
    return block.reshape((1 << bits,) + block.shape[bits:])


def gather_chips(block):
    bits, _ = chip_bits()
    half = block.shape[-1] // 2 // 128 * 128
    order = list(range(bits))
    turned = order[1:] + order[:1]
    return jnp.concatenate(
        [gather_one(block[..., :half], order), gather_one(block[..., half:], turned)], axis=-1
    )


def reduce_one(parts, order):
    bits, mine = chip_bits()
    parts = parts.reshape((2,) * bits + parts.shape[1:])
    left = list(range(bits))
    for b in order:
        axis = sum(1 for d in left if d > b)
        keep = pick(parts, mine[b], axis)
        sent = pick(parts, 1 - mine[b], axis)
        parts = (keep.astype(F32) + swap(sent, "chip", 1 << b).astype(F32)).astype(BF16)
        left.remove(b)
    return parts


def reduce_chips(parts):
    bits, _ = chip_bits()
    half = parts.shape[-1] // 2 // 128 * 128
    order = list(range(bits))
    turned = order[1:] + order[:1]
    return jnp.concatenate(
        [reduce_one(parts[..., :half], order), reduce_one(parts[..., half:], turned)], axis=-1
    )


def sum_seq(array):
    rows = array.shape[0] // 4
    z = lax.axis_index(SEQ)
    parts = array.reshape(4, rows, array.shape[1])
    total = pick(parts, z).astype(F32)
    for hop in (1, 2, 3):
        total = total + swap(pick(parts, z ^ hop), SEQ, hop).astype(F32)
    total = total.astype(BF16)
    around = [total] + [swap(total, SEQ, hop) for hop in (1, 2, 3)]
    square = jnp.stack(around).reshape(2, 2, rows, array.shape[1])
    square = jnp.where(lax.axis_index("zq") == 1, square[:, ::-1], square)
    square = jnp.where(lax.axis_index("zp") == 1, square[::-1], square)
    return square.reshape(array.shape)


def group_ones(scale):
    row = lax.broadcasted_iota(jnp.int32, (128, 128), 0) // HEAD
    column = lax.broadcasted_iota(jnp.int32, (128, 128), 1) // HEAD
    return jnp.where(row == column, scale, 0.0).astype(BF16)


def group_sum(values, ones):
    high = values.astype(BF16)
    low = (values - high.astype(F32)).astype(BF16)
    return jnp.dot(high, ones, preferred_element_type=F32) + jnp.dot(
        low, ones, preferred_element_type=F32
    )


def project_kernel(x_ref, gain_ref, weight_ref, qg_ref, kg_ref, normed_ref, q_ref, k_ref, v_ref, raw_ref):
    width = q_ref.shape[1]
    x = x_ref[...].astype(F32)
    center = x - jnp.mean(x, axis=-1, keepdims=True)
    spread = jnp.mean(center * center, axis=-1, keepdims=True)
    normed = (center * lax.rsqrt(spread + EPSILON) * gain_ref[...]).astype(BF16)
    normed_ref[...] = normed
    mixed = jnp.dot(normed, weight_ref[...], preferred_element_type=F32)
    raw_ref[...] = mixed[:, : 2 * width]
    ones = group_ones(1.0 / HEAD)
    for part, (out_ref, g_ref) in enumerate(((q_ref, qg_ref), (k_ref, kg_ref))):
        for at in range(0, width, 128):
            raw = mixed[:, part * width + at : part * width + at + 128]
            c = raw - group_sum(raw, ones)
            n = c * lax.rsqrt(group_sum(c * c, ones) + EPSILON)
            out_ref[:, at : at + 128] = (n * g_ref[:, at : at + 128]).astype(BF16)
    v_ref[...] = mixed[:, 2 * width :].astype(BF16)


def project(x, gain, weight, query_gain, key_gain):
    tokens, model = x.shape
    width = weight.shape[1] // 3
    whole = lambda shape: pl.BlockSpec(shape, lambda i: (0, 0))
    rows = lambda columns: pl.BlockSpec((BLOCK, columns), lambda i: (i, 0))
    return pl.pallas_call(
        project_kernel,
        grid=(tokens // BLOCK,),
        in_specs=[
            rows(model),
            whole((1, model)),
            whole(weight.shape),
            whole((1, width)),
            whole((1, width)),
        ],
        out_specs=[rows(model), rows(width), rows(width), rows(width), rows(2 * width)],
        out_shape=[
            jax.ShapeDtypeStruct((tokens, model), BF16),
            jax.ShapeDtypeStruct((tokens, width), BF16),
            jax.ShapeDtypeStruct((tokens, width), BF16),
            jax.ShapeDtypeStruct((tokens, width), BF16),
            jax.ShapeDtypeStruct((tokens, 2 * width), F32),
        ],
        compiler_params=pltpu.CompilerParams(vmem_limit_bytes=VMEM_LIMIT),
        cost_estimate=pl.CostEstimate(
            flops=2 * tokens * model * 3 * width, bytes_accessed=tokens * model * 12, transcendentals=0
        ),
        name="project",
    )(x, gain, weight, query_gain, key_gain)


def marks(bounds_ref, length, pics, end_row):
    place = lax.broadcasted_iota(jnp.int32, (length, 128), 0)
    inside = (place >= bounds_ref[0:1, :]) & (place < bounds_ref[end_row : end_row + 1, :])
    return jnp.where(inside, MARK, 0.0)


def nt(a, b):
    return lax.dot_general(a, b, (((1,), (1,)), ((), ())), preferred_element_type=F32)


def tn(a, b):
    return lax.dot_general(a, b, (((0,), (0,)), ((), ())), preferred_element_type=F32)


def attend_kernel(pics, info_ref, q_ref, k_ref, v_ref, bounds_ref, out_ref, aug_ref, kaug, vaug):
    length = q_ref.shape[0]
    blocks = length // BLOCK
    pair = pl.program_id(0)
    lane = lax.broadcasted_iota(jnp.int32, (1, 128), 1)
    place = lane % HEAD
    key_marks = marks(bounds_ref, length, pics, 1)
    key_marks = jnp.where(place == pics, -MARK, key_marks)
    key_marks = jnp.where((place > pics) & (place < pics + 4), 1.0, key_marks).astype(BF16)
    query_marks = marks(bounds_ref, length, pics, 2)
    query_marks = jnp.where(place == pics, MARK, query_marks).astype(BF16)
    out_ref[...] = jnp.zeros_like(out_ref)
    for h in range(2):
        inside = (lane < HEAD) if h == 0 else (lane >= HEAD)
        active = info_ref[pair * 2 + h] == 1

        @pl.when(active)
        def _():
            kaug[...] = jnp.where(inside, k_ref[...], key_marks)
            vaug[...] = jnp.where(inside, v_ref[...], jnp.ones_like(v_ref))
            for b in range(blocks):
                rows = pl.ds(b * BLOCK, BLOCK)
                query = jnp.where(inside, q_ref[rows, :], query_marks[b * BLOCK : (b + 1) * BLOCK])

                def step(j, total):
                    keys = pl.ds(pl.multiple_of(j * BLOCK, BLOCK), BLOCK)
                    scores = nt(query, kaug[keys, :])
                    weights = jnp.exp2(scores * EXP2_FACTOR).astype(BF16)
                    return total + jnp.dot(weights, vaug[keys, :], preferred_element_type=F32)

                base = 6 + 2 * b
                total = lax.fori_loop(
                    info_ref[base], info_ref[base + 1], step, jnp.zeros((BLOCK, 128), F32)
                )
                result = total / pltpu.roll(total, HEAD, 1)
                old = out_ref[rows, :]
                out_ref[rows, :] = jnp.where(inside, result.astype(BF16), old)
                log_total = jnp.log(jnp.where(inside, 1.0, total)) * -(HEAD**0.5)
                first = log_total.astype(BF16)
                rest = log_total - first.astype(F32)
                middle = rest.astype(BF16)
                last = (rest - middle.astype(F32)).astype(BF16)
                other = jnp.logical_not(inside)
                query = jnp.where(other & (place == pics + 1), first, query)
                query = jnp.where(other & (place == pics + 2), middle, query)
                query = jnp.where(other & (place == pics + 3), last, query)
                aug_ref[h, rows, :] = query

        @pl.when(jnp.logical_not(active))
        def _():
            aug_ref[h] = jnp.zeros(aug_ref.shape[1:], BF16)


def attend(info, q, k, v, bounds, pics):
    length, width = q.shape
    pairs = width // 128
    column = pl.BlockSpec((length, 128), lambda p, info: (0, p))
    return pl.pallas_call(
        functools.partial(attend_kernel, pics),
        grid_spec=pltpu.PrefetchScalarGridSpec(
            num_scalar_prefetch=1,
            grid=(pairs,),
            in_specs=[column, column, column, pl.BlockSpec((8, 128), lambda p, info: (0, 0))],
            out_specs=[column, pl.BlockSpec((2, length, 128), lambda p, info: (p, 0, 0))],
            scratch_shapes=[pltpu.VMEM((length, 128), BF16), pltpu.VMEM((length, 128), BF16)],
        ),
        out_shape=[
            jax.ShapeDtypeStruct((length, width), BF16),
            jax.ShapeDtypeStruct((2 * pairs, length, 128), BF16),
        ],
        compiler_params=pltpu.CompilerParams(vmem_limit_bytes=VMEM_LIMIT),
        cost_estimate=pl.CostEstimate(
            flops=8 * length * length * width, bytes_accessed=length * width * 12, transcendentals=0
        ),
        name="attend",
    )(info, q, k, v, bounds)


def attend_back_kernel(
    pics, info_ref, aug_ref, k_ref, v_ref, out_ref, do_ref, rawq_ref, rawk_ref, qg_ref, kg_ref, bounds_ref,
    dq_ref, dk_ref, dv_ref, qgg_ref, kgg_ref, kaug, vaug, doaug, qsum, ksum, vsum,
):
    length = k_ref.shape[0]
    blocks = length // BLOCK
    pair = pl.program_id(0)
    lane = lax.broadcasted_iota(jnp.int32, (1, 128), 1)
    place = lane % HEAD
    key_marks = marks(bounds_ref, length, pics, 1)
    key_marks = jnp.where(place == pics, -MARK, key_marks)
    key_marks = jnp.where((place > pics) & (place < pics + 4), 1.0, key_marks).astype(BF16)
    value_marks = jnp.where((place == 0) | (place == 1), 1.0, 0.0).astype(BF16)
    ones = group_ones(1.0)
    inner = group_sum(do_ref[...].astype(F32) * out_ref[...].astype(F32), ones)
    inner = -pltpu.roll(inner, HEAD, 1)
    inner_high = inner.astype(BF16)
    inner_low = (inner - inner_high.astype(F32)).astype(BF16)
    zero = jnp.zeros((), BF16)
    grad_marks = jnp.where(place == 0, inner_high, jnp.where(place == 1, inner_low, zero))
    for h in range(2):
        inside = (lane < HEAD) if h == 0 else (lane >= HEAD)
        active = info_ref[pair * 2 + h] == 1
        qsum[h] = jnp.zeros((length, 128), F32)

        @pl.when(active)
        def _():
            kaug[...] = jnp.where(inside, k_ref[...], key_marks)
            vaug[...] = jnp.where(inside, v_ref[...], value_marks)
            doaug[...] = jnp.where(inside, do_ref[...], grad_marks)
            for b in range(blocks):
                keys = pl.ds(b * BLOCK, BLOCK)
                key_block = kaug[keys, :]
                value_block = vaug[keys, :]

                def step(j, sums):
                    dk, dv = sums
                    rows = pl.ds(pl.multiple_of(j * BLOCK, BLOCK), BLOCK)
                    query = aug_ref[h, rows, :]
                    grad = doaug[rows, :]
                    weights = jnp.exp2(nt(key_block, query) * EXP2_FACTOR)
                    score_grad = (weights * nt(value_block, grad)).astype(BF16)
                    dv = dv + jnp.dot(weights.astype(BF16), grad, preferred_element_type=F32)
                    dk = dk + jnp.dot(score_grad, query, preferred_element_type=F32)
                    qsum[h, rows, :] += tn(score_grad, key_block)
                    return dk, dv

                empty = jnp.zeros((BLOCK, 128), F32)
                base = 6 + 2 * blocks + 2 * b
                dk, dv = lax.fori_loop(info_ref[base], info_ref[base + 1], step, (empty, empty))
                ksum[h, keys, :] = dk
                vsum[h, keys, :] = dv

        @pl.when(jnp.logical_not(active))
        def _():
            ksum[h] = jnp.zeros((length, 128), F32)
            vsum[h] = jnp.zeros((length, 128), F32)

    left = lane < HEAD
    means = group_ones(1.0 / HEAD)
    for sums, raw_ref, g_ref, grad_ref, gain_ref in (
        (qsum, rawq_ref, qg_ref, dq_ref, qgg_ref),
        (ksum, rawk_ref, kg_ref, dk_ref, kgg_ref),
    ):
        gain_sum = jnp.zeros((1, 128), F32)
        for b in range(blocks):
            rows = pl.ds(b * BLOCK, BLOCK)
            e = jnp.where(left, sums[0, rows, :], sums[1, rows, :]) * HEAD**-0.5
            e = e.astype(BF16).astype(F32)
            raw = raw_ref[rows, :]
            c = raw - group_sum(raw, means)
            r = lax.rsqrt(group_sum(c * c, means) + EPSILON)
            n = c * r
            gain_sum = gain_sum + jnp.sum(e * n, axis=0, keepdims=True)
            t = e * g_ref[...]
            grad = r * (t - group_sum(t, means) - n * group_sum(t * n, means))
            grad_ref[rows, :] = grad.astype(BF16)
        gain_ref[...] = gain_sum
    dv_ref[...] = jnp.where(left, vsum[0], vsum[1]).astype(BF16)


def attend_back(info, aug, k, v, out, do, raw, query_gain, key_gain, bounds, pics):
    length, width = k.shape
    pairs = width // 128
    column = pl.BlockSpec((length, 128), lambda p, info: (0, p))
    gain = pl.BlockSpec((1, 128), lambda p, info: (0, p))
    return pl.pallas_call(
        functools.partial(attend_back_kernel, pics),
        grid_spec=pltpu.PrefetchScalarGridSpec(
            num_scalar_prefetch=1,
            grid=(pairs,),
            in_specs=[
                pl.BlockSpec((2, length, 128), lambda p, info: (p, 0, 0)),
                column,
                column,
                column,
                column,
                column,
                pl.BlockSpec((length, 128), lambda p, info: (0, pairs + p)),
                gain,
                gain,
                pl.BlockSpec((8, 128), lambda p, info: (0, 0)),
            ],
            out_specs=[column, column, column, gain, gain],
            scratch_shapes=[
                pltpu.VMEM((length, 128), BF16),
                pltpu.VMEM((length, 128), BF16),
                pltpu.VMEM((length, 128), BF16),
                pltpu.VMEM((2, length, 128), F32),
                pltpu.VMEM((2, length, 128), F32),
                pltpu.VMEM((2, length, 128), F32),
            ],
        ),
        out_shape=[
            jax.ShapeDtypeStruct((length, width), BF16),
            jax.ShapeDtypeStruct((length, width), BF16),
            jax.ShapeDtypeStruct((length, width), BF16),
            jax.ShapeDtypeStruct((1, width), F32),
            jax.ShapeDtypeStruct((1, width), F32),
        ],
        compiler_params=pltpu.CompilerParams(vmem_limit_bytes=VMEM_LIMIT),
        cost_estimate=pl.CostEstimate(
            flops=20 * length * length * width, bytes_accessed=length * width * 20, transcendentals=0
        ),
        name="attend_back",
    )(info, aug, k, v, out, do, raw, raw, query_gain, key_gain, bounds)


def gelu_pair(h):
    size = jnp.abs(h)
    bell = jnp.exp2(h * h * -0.7213475204444817)
    t = 1.0 / (1.0 + 0.23164189 * size)
    series = t * (0.127414796 + t * (-0.142248368 + t * (0.7107068705 + t * (-0.7265760135 + t * 0.5307027145))))
    tail = series * bell
    below = jnp.where(h < 0.0, tail, 1.0 - tail)
    return h * below, below + h * (bell * 0.3989422804014327)


def mlp_kernel(second_ref, grad_ref, up_ref, down_ref, out_ref, back_ref, upg_ref, downg_ref):
    first = pl.program_id(0) == 0

    @pl.when(first)
    def _():
        out_ref[...] = jnp.zeros_like(out_ref)
        back_ref[...] = jnp.zeros_like(back_ref)

    second = second_ref[...]
    grad = grad_ref[...]
    up = up_ref[...]
    down = down_ref[...]
    pre = jnp.dot(second, up, preferred_element_type=F32)
    hidden, slope = gelu_pair(pre)
    hidden = hidden.astype(BF16)
    out_ref[...] += jnp.dot(hidden, down, preferred_element_type=F32)
    pre_grad = (nt(grad, down) * slope).astype(BF16)
    downg_ref[...] = tn(hidden, grad).astype(BF16)
    upg_ref[...] = tn(second, pre_grad).astype(BF16)
    back_ref[...] += nt(pre_grad, up)


def mlp(second, grad, up, down):
    tokens, model = second.shape
    hidden = up.shape[1]
    tile = 512
    whole = pl.BlockSpec((tokens, model), lambda i: (0, 0))
    wide = pl.BlockSpec((model, tile), lambda i: (0, i))
    tall = pl.BlockSpec((tile, model), lambda i: (i, 0))
    return pl.pallas_call(
        mlp_kernel,
        grid=(hidden // tile,),
        in_specs=[whole, whole, wide, tall],
        out_specs=[whole, whole, wide, tall],
        out_shape=[
            jax.ShapeDtypeStruct((tokens, model), F32),
            jax.ShapeDtypeStruct((tokens, model), F32),
            jax.ShapeDtypeStruct((model, hidden), BF16),
            jax.ShapeDtypeStruct((hidden, model), BF16),
        ],
        compiler_params=pltpu.CompilerParams(vmem_limit_bytes=VMEM_LIMIT),
        cost_estimate=pl.CostEstimate(
            flops=12 * tokens * model * hidden, bytes_accessed=8 * model * hidden, transcendentals=0
        ),
        name="mlp",
    )(second, grad, up, down)


def norm_parts(values):
    center = values - jnp.mean(values, axis=-1, keepdims=True)
    spread = lax.rsqrt(jnp.mean(center * center, axis=-1, keepdims=True) + EPSILON)
    return center * spread, spread


def norm_back(upstream, n, r, gain):
    t = upstream * gain
    return (
        r * (t - jnp.mean(t, axis=-1, keepdims=True) - n * jnp.mean(t * n, axis=-1, keepdims=True)),
        jnp.sum(upstream * n, axis=0),
    )


def row_layout(lengths_row, length):
    pics = lengths_row.shape[0]
    blocks = length // BLOCK
    ends = jnp.cumsum(lengths_row)
    starts = ends - lengths_row
    live = lengths_row > 0
    last = jnp.arange(pics) == jnp.sum(live) - 1
    query_ends = jnp.where(last, length, ends)
    fill = jnp.full((HEAD - pics,), 2 * length, jnp.int32)
    lanes = lambda values: jnp.tile(jnp.concatenate([values.astype(jnp.int32), fill]), 2)
    bounds = jnp.stack([lanes(starts), lanes(ends), lanes(query_ends)] + [lanes(ends)] * 5)
    edge = jnp.arange(blocks) * BLOCK
    holds = lambda slots: (starts[None, :] <= slots[:, None]) & (slots[:, None] < query_ends[None, :])
    low = jnp.sum(jnp.where(holds(edge), starts[None, :], 0), axis=1) // BLOCK
    high = (jnp.sum(jnp.where(holds(edge + BLOCK - 1), ends[None, :], 0), axis=1) - 1) // BLOCK + 1
    at = jnp.arange(blocks)
    query_low = jnp.sum(high[None, :] <= at[:, None], axis=1)
    query_high = jnp.sum(low[None, :] <= at[:, None], axis=1)
    ranges = jnp.concatenate(
        [jnp.stack([low, high], axis=1).reshape(-1), jnp.stack([query_low, query_high], axis=1).reshape(-1)]
    )
    return bounds, ranges.astype(jnp.int32), ends[-1]


def local(
    tokens, lengths, pictures, first_gain, mix_weight, query_gain, key_gain, out_weight,
    second_gain, up_weight, down_weight, cotangent,
):
    core, zp, zq = lax.axis_index("core"), lax.axis_index("zp"), lax.axis_index("zq")
    chips = lax.axis_size("chip")
    _, part, model = tokens.shape
    length = 4 * part
    half = 2 * part
    heads_core = HEADS // 2
    width = heads_core * HEAD
    third = width // 2
    pics = lengths.shape[1]
    shard = mix_weight.shape[0]

    def spread(array):
        mine = lax.ppermute(pick(array, zq), COLUMN, KEEP)
        cross = lax.ppermute(pick(array, 1 - zq), COLUMN, CROSS)
        shared = lax.ppermute(array[2], COLUMN, KEEP)
        return ordered(mine, cross, zq, 0), shared

    def collect(array):
        first, second, shared = array[:part], array[part:half], array[half:]
        mine = lax.ppermute(jnp.where(zq == 0, first, second), COLUMN, inverse(KEEP))
        cross = lax.ppermute(jnp.where(zq == 0, second, first), COLUMN, inverse(CROSS))
        shared = lax.ppermute(shared, COLUMN, inverse(KEEP))
        return jnp.stack([jnp.where(zq == 0, mine, cross), jnp.where(zq == 0, cross, mine), shared])

    own_half, own_quarter = spread(tokens)
    row_tokens = ordered(own_half, swap(own_half, "core"), core, 0)
    shared_half = ordered(own_quarter, swap(own_quarter, "zq"), zq, 0)
    shared_tokens = ordered(shared_half, swap(shared_half, "core"), core, 0)
    grad_half, grad_quarter = spread(cotangent)

    lengths_owner = jnp.where(core == zp, lengths, swap(lengths, "core"))
    row_bounds, row_ranges, row_filled = row_layout(pick(lengths_owner, zq), length)
    shared_bounds, shared_ranges, shared_filled = row_layout(lengths_owner[2], length)
    row_info = jnp.concatenate([jnp.ones((heads_core,), jnp.int32), row_ranges])
    mine_heads = (jnp.arange(heads_core) // (heads_core // 2) == zq).astype(jnp.int32)
    shared_info = jnp.concatenate([mine_heads, shared_ranges])

    gains = jnp.concatenate([first_gain, query_gain, key_gain, second_gain])
    gains = jnp.pad(gains[None], ((0, 15), (0, 3 * width - 4 * shard)))
    mix_split = mix_weight.reshape(shard, 3, 2, width)
    mine_mix = jnp.concatenate([pick(mix_split, core, 2).reshape(shard, 3 * width), gains])
    sent_mix = jnp.concatenate([pick(mix_split, 1 - core, 2).reshape(shard, 3 * width), gains])
    other_mix = swap(sent_mix, "core")
    mix_pair = ordered(mine_mix[None], other_mix[None], core, 0).reshape(-1, 3 * width)
    mix_all = gather_chips(mix_pair).reshape(2 * chips, shard + 16, 3 * width)
    mix_half = mix_all[:, :shard].reshape(model, 3 * width)
    gains = mix_all[:, shard, : 4 * shard].reshape(2 * chips, 4, shard).astype(F32)
    gains = jnp.transpose(gains, (1, 0, 2)).reshape(4, 1, model)
    gain_first, gain_query, gain_key, gain_second = gains[0], gains[1], gains[2], gains[3]
    gain_query = pick(gain_query.reshape(2, 1, width), core)
    gain_key = pick(gain_key.reshape(2, 1, width), core)

    def gather_whole(weight):
        mine = gather_chips(weight)
        return ordered(mine[:, None], swap(mine, "core")[:, None], core, 1).reshape(-1, weight.shape[1])

    out_matrix = gather_whole(out_weight)
    up_matrix = gather_whole(up_weight)
    down_matrix = gather_whole(down_weight)

    row_normed, row_q, row_k, row_v, row_raw = project(row_tokens, gain_first, mix_half, gain_query, gain_key)
    row_out, row_aug = attend(row_info, row_q, row_k, row_v, row_bounds, pics)
    shared_normed, shared_q, shared_k, shared_v, shared_raw = project(
        shared_tokens, gain_first, mix_half, gain_query, gain_key
    )
    shared_out, shared_aug = attend(shared_info, shared_q, shared_k, shared_v, shared_bounds, pics)

    square = pick(shared_out.reshape(2, 2, part, 2, third), zq, 3)
    kept = pick(square, zq, 1)
    got = swap(pick(square, 1 - zq, 1), "zq")
    quarters = ordered(kept, got, zq, 2)
    row_halves = row_out.reshape(2, half, width)
    mine = jnp.concatenate([pick(row_halves, core), pick(quarters, core)])
    other = swap(jnp.concatenate([pick(row_halves, 1 - core), pick(quarters, 1 - core)]), "core")
    attended = ordered(mine, other, core, 1)

    inputs = jnp.concatenate([own_half, own_quarter]).astype(F32)
    middle = inputs + jnp.dot(attended, out_matrix, preferred_element_type=F32)
    n_second, r_second = norm_parts(middle)
    second = (n_second * gain_second).astype(BF16)
    row_place = core * half + jnp.arange(half)
    shared_place = (2 * core + zq) * part + jnp.arange(part)
    valid = jnp.concatenate([row_place < row_filled, shared_place < shared_filled])
    grad_low = jnp.concatenate([grad_half, grad_quarter]) * valid[:, None].astype(BF16)

    delta, second_grad, up_grad, down_grad = mlp(second, grad_low, up_matrix, down_matrix)
    output = collect((middle + delta).astype(BF16))

    middle_part, gain_second_grad = norm_back(second_grad, n_second, r_second, gain_second)
    middle_grad = grad_low.astype(F32) + middle_part
    branch = middle_grad.astype(BF16)
    attended_grad = nt(branch, out_matrix).astype(BF16)
    out_grad = tn(attended, branch).astype(BF16)

    def reduce_whole(grad):
        columns = grad.shape[1]
        split = grad.reshape(chips, 2, -1, columns)
        mine, sent = pick(split, core, 1), pick(split, 1 - core, 1)
        paired = (mine.astype(F32) + swap(sent, "core").astype(F32)).astype(BF16)
        return sum_seq(reduce_chips(paired)).astype(F32)

    up_out = reduce_whole(up_grad)
    down_out = reduce_whole(down_grad)
    outw_out = reduce_whole(out_grad)

    grad_split = attended_grad.reshape(-1, 2, width)
    mine = pick(grad_split, core, 1)
    other = swap(pick(grad_split, 1 - core, 1), "core")
    row_grad = ordered(mine[:half], other[:half], core, 0)
    quarters = ordered(mine[None, half:], other[None, half:], core, 0).reshape(2, part, 2, third)
    kept = pick(quarters, zq, 2)
    got = swap(pick(quarters, 1 - zq, 2), "zq")
    square = ordered(kept[:, None], got[:, None], zq, 1).reshape(length, 1, third)
    shared_grad = jnp.where(jnp.arange(2)[None, :, None] == zq, square, 0).reshape(length, width)

    shared_dq, shared_dk, shared_dv, shared_qgg, shared_kgg = attend_back(
        shared_info, shared_aug, shared_k, shared_v, shared_out, shared_grad, shared_raw,
        gain_query, gain_key, shared_bounds, pics,
    )
    row_dq, row_dk, row_dv, row_qgg, row_kgg = attend_back(
        row_info, row_aug, row_k, row_v, row_out, row_grad, row_raw, gain_query, gain_key, row_bounds, pics
    )
    shared_mixed = jnp.concatenate([shared_dq, shared_dk, shared_dv], axis=1)
    row_mixed = jnp.concatenate([row_dq, row_dk, row_dv], axis=1)
    square = pick(shared_mixed.reshape(2, 2, part, 3, 2, third), zq, 4)
    kept = pick(square, zq, 1)
    got = swap(pick(square, 1 - zq, 1), "zq")
    quarters = ordered(kept[:, :, :, None], got[:, :, :, None], zq, 3).reshape(half, 3 * width)

    mix_grad = tn(
        jnp.concatenate([row_normed, shared_normed]), jnp.concatenate([row_mixed, shared_mixed])
    ).astype(BF16)
    partial = nt(jnp.concatenate([row_mixed, quarters]), mix_half)
    row_partial = partial[:length].reshape(2, half, model)
    shared_partial = partial[length:].reshape(2, part, model)
    mine = jnp.concatenate([pick(row_partial, core), pick(shared_partial, core)])
    sent = jnp.concatenate([pick(row_partial, 1 - core), pick(shared_partial, 1 - core)])
    normed_grad = mine + swap(sent.astype(BF16), "core").astype(F32)
    n_first, r_first = norm_parts(inputs)
    input_part, gain_first_grad = norm_back(normed_grad, n_first, r_first, gain_first)
    input_grad = collect((middle_grad + input_part).astype(BF16))

    def place_heads(values):
        return jnp.where(jnp.arange(2)[:, None] == core, values, 0.0).reshape(model)

    gain_grads = jnp.stack(
        [gain_first_grad, place_heads(row_qgg + shared_qgg), place_heads(row_kgg + shared_kgg), gain_second_grad]
    )
    gain_grads = gain_grads.reshape(4, chips, 2 * shard).transpose(1, 0, 2).reshape(chips, 1, -1)
    gain_grads = jnp.pad(gain_grads, ((0, 0), (0, 15), (0, 3 * width - gain_grads.shape[2]))).astype(BF16)
    payload = jnp.concatenate([mix_grad.reshape(chips, 2 * shard, 3 * width), gain_grads], axis=1)
    reduced = reduce_chips(payload)
    mix_rows = reduced[: 2 * shard].reshape(2, shard, 3 * width)
    gain_rows = reduced[2 * shard :]
    other = swap(jnp.concatenate([pick(mix_rows, 1 - core), gain_rows]), "core")
    mix_columns = ordered(
        pick(mix_rows, core).reshape(shard, 3, 1, width), other[:shard].reshape(shard, 3, 1, width), core, 2
    )
    gain_rows = (gain_rows.astype(F32) + other[shard:].astype(F32)).astype(BF16)
    final = jnp.concatenate([mix_columns.reshape(2 * shard, 3 * width), gain_rows])
    spare = -final.shape[0] % 64
    final = sum_seq(jnp.pad(final, ((0, spare), (0, 0)))).astype(F32)
    mix_out = final[: 2 * shard].reshape(shard, 6 * width)
    gains_out = pick(final[2 * shard, : 8 * shard].reshape(4, 2, shard), core, 1)
    return (
        output,
        input_grad,
        gains_out[0],
        mix_out,
        gains_out[1],
        gains_out[2],
        outw_out,
        gains_out[3],
        up_out,
        down_out,
    )


def solution(mesh):
    fsdp = mesh.shape["fsdp"]
    split = Mesh(mesh.devices.reshape(fsdp // 2, 2, 2, 2), ("chip", "core", "zp", "zq"))
    rows = ("chip", "core")
    return jax.shard_map(
        local,
        mesh=split,
        in_specs=(
            P(rows, SEQ, None),
            P(rows, None),
            P(rows, SEQ),
            P(rows),
            P(rows, None),
            P(rows),
            P(rows),
            P(rows, None),
            P(rows),
            P(rows, None),
            P(rows, None),
            P(rows, SEQ, None),
        ),
        out_specs=(
            P(rows, SEQ, None),
            P(rows, SEQ, None),
            P(rows),
            P(rows, None),
            P(rows),
            P(rows),
            P(rows, None),
            P(rows),
            P(rows, None),
            P(rows, None),
        ),
        check_vma=False,
    )
```

```python
import functools

import jax
import jax.numpy as jnp
from jax import lax
from jax.experimental import pallas as pl
from jax.experimental.pallas import tpu as pltpu
from jax.sharding import Mesh, PartitionSpec as P

HEADS = 12
HEAD = 64
EPSILON = 1e-06
BLOCK = 256
STEP = 512
MARK = 32.0
EXP2_FACTOR = HEAD**-0.5 * 1.4426950408889634
F32 = jnp.float32
BF16 = jnp.bfloat16
VMEM_LIMIT = 56 * 1024 * 1024

SEQ = ("zp", "zq")
COLUMN = ("core", "zp", "zq")
KEEP = [
    (core * 4 + z, (z // 2) * 4 + 2 * core + z % 2) for core in range(2) for z in range(4)
]
CROSS = [
    (core * 4 + z, (z // 2) * 4 + 2 * core + 1 - z % 2) for core in range(2) for z in range(4)
]


def swap(array, name, bit=1):
    count = lax.axis_size(name)
    return lax.ppermute(array, name, [(i, i ^ bit) for i in range(count)])


def pick(array, index, axis=0):
    return lax.dynamic_index_in_dim(array, index, axis, keepdims=False)


def group_ones(scale):
    row = lax.broadcasted_iota(jnp.int32, (128, 128), 0) // HEAD
    column = lax.broadcasted_iota(jnp.int32, (128, 128), 1) // HEAD
    return jnp.where(row == column, scale, 0.0).astype(BF16)


def group_sum(values, ones):
    high = values.astype(BF16)
    low = (values - high.astype(F32)).astype(BF16)
    return jnp.dot(high, ones, preferred_element_type=F32) + jnp.dot(
        low, ones, preferred_element_type=F32
    )


def project_kernel(x_ref, gain_ref, weight_ref, qg_ref, kg_ref, normed_ref, q_ref, k_ref, v_ref, raw_ref):
    width = q_ref.shape[1]
    x = x_ref[...].astype(F32)
    center = x - jnp.mean(x, axis=-1, keepdims=True)
    spread = jnp.mean(center * center, axis=-1, keepdims=True)
    normed = (center * lax.rsqrt(spread + EPSILON) * gain_ref[...]).astype(BF16)
    normed_ref[...] = normed
    mixed = jnp.dot(normed, weight_ref[...], preferred_element_type=F32)
    raw_ref[...] = mixed[:, : 2 * width]
    ones = group_ones(1.0 / HEAD)
    for part, (out_ref, g_ref) in enumerate(((q_ref, qg_ref), (k_ref, kg_ref))):
        for at in range(0, width, 128):
            raw = mixed[:, part * width + at : part * width + at + 128]
            c = raw - group_sum(raw, ones)
            n = c * lax.rsqrt(group_sum(c * c, ones) + EPSILON)
            out_ref[:, at : at + 128] = (n * g_ref[:, at : at + 128]).astype(BF16)
    v_ref[...] = mixed[:, 2 * width :].astype(BF16)


def project(x, gain, weight, query_gain, key_gain):
    tokens, model = x.shape
    width = weight.shape[1] // 3
    whole = lambda shape: pl.BlockSpec(shape, lambda i: (0, 0))
    rows = lambda columns: pl.BlockSpec((BLOCK, columns), lambda i: (i, 0))
    return pl.pallas_call(
        project_kernel,
        grid=(tokens // BLOCK,),
        in_specs=[
            rows(model),
            whole((1, model)),
            whole(weight.shape),
            whole((1, width)),
            whole((1, width)),
        ],
        out_specs=[rows(model), rows(width), rows(width), rows(width), rows(2 * width)],
        out_shape=[
            jax.ShapeDtypeStruct((tokens, model), BF16),
            jax.ShapeDtypeStruct((tokens, width), BF16),
            jax.ShapeDtypeStruct((tokens, width), BF16),
            jax.ShapeDtypeStruct((tokens, width), BF16),
            jax.ShapeDtypeStruct((tokens, 2 * width), F32),
        ],
        compiler_params=pltpu.CompilerParams(vmem_limit_bytes=VMEM_LIMIT),
        cost_estimate=pl.CostEstimate(
            flops=2 * tokens * model * 3 * width, bytes_accessed=tokens * model * 12, transcendentals=0
        ),
        name="project",
    )(x, gain, weight, query_gain, key_gain)


def nt(a, b):
    return lax.dot_general(a, b, (((1,), (1,)), ((), ())), preferred_element_type=F32)


def tn(a, b):
    return lax.dot_general(a, b, (((0,), (0,)), ((), ())), preferred_element_type=F32)


def slots(queries, length, part):
    at = lax.broadcasted_iota(jnp.int32, (queries, 128), 0)
    if queries == length:
        return at
    return at % part + part * (lax.axis_index("zq") + 2 * (at // part))


def own_rows(ref, start, count, queries, part):
    if queries == ref.shape[0]:
        return ref[pl.ds(start, count), :]
    zq = lax.axis_index("zq")
    pieces = [
        ref[pl.ds(pl.multiple_of((zq + 2 * i) * part, part), part), :]
        for i in range(start // part, (start + count) // part)
    ]
    return jnp.concatenate(pieces, axis=0)


def query_marks(bounds_ref, place, queries, length, part, pics):
    at = slots(queries, length, part)
    inside = (at >= bounds_ref[0:1, :]) & (at < bounds_ref[2:3, :])
    values = jnp.where(inside, MARK, 0.0)
    return jnp.where(place == pics, MARK, values).astype(BF16)


def key_marks(bounds_ref, place, length, pics):
    at = lax.broadcasted_iota(jnp.int32, (length, 128), 0)
    inside = (at >= bounds_ref[0:1, :]) & (at < bounds_ref[1:2, :])
    values = jnp.where(inside, MARK, 0.0)
    values = jnp.where(place == pics, -MARK, values)
    return jnp.where((place > pics) & (place < pics + 4), 1.0, values).astype(BF16)


def attend_kernel(pics, q_ref, k_ref, v_ref, bounds_ref, out_ref, aug_ref, kaug, vaug, qaug):
    length = k_ref.shape[0]
    queries = out_ref.shape[0]
    part = length // 4
    lane = lax.broadcasted_iota(jnp.int32, (1, 128), 1)
    place = lane % HEAD
    sides = [lane < HEAD, lane >= HEAD]
    kmarks = key_marks(bounds_ref, place, length, pics)
    qmarks = query_marks(bounds_ref, place, queries, length, part, pics)
    qaug[...] = qmarks
    for h in range(2):
        kaug[h] = jnp.where(sides[h], k_ref[...], kmarks)
        vaug[h] = jnp.where(sides[h], v_ref[...], jnp.ones_like(v_ref))
    for b in range(queries // STEP):
        rows = pl.ds(b * STEP, STEP)
        mine = own_rows(q_ref, b * STEP, STEP, queries, part)
        query = [jnp.where(sides[h], mine, qaug[rows, :]) for h in range(2)]
        total = [jnp.zeros((STEP, 128), F32)] * 2
        for j in range(length // STEP):
            keys = pl.ds(j * STEP, STEP)
            scores = [nt(query[h], kaug[h, keys, :]) for h in range(2)]
            weights = [jnp.exp2(x * EXP2_FACTOR).astype(BF16) for x in scores]
            total = [
                total[h] + jnp.dot(weights[h], vaug[h, keys, :], preferred_element_type=F32) for h in range(2)
            ]
        results = []
        for h in range(2):
            results.append(total[h] / pltpu.roll(total[h], HEAD, 1))
            log_total = jnp.log(jnp.where(sides[h], 1.0, total[h])) * -(HEAD**0.5)
            first = log_total.astype(BF16)
            rest = log_total - first.astype(F32)
            middle = rest.astype(BF16)
            last = (rest - middle.astype(F32)).astype(BF16)
            logs = jnp.where(place == pics + 1, first, jnp.where(place == pics + 2, middle, last))
            slot = jnp.logical_not(sides[h]) & (place > pics) & (place < pics + 4)
            aug_ref[h, rows, :] = jnp.where(slot, logs, query[h])
        out_ref[rows, :] = jnp.where(sides[0], results[0], results[1]).astype(BF16)


def attend(q, k, v, bounds, pics, queries):
    length, width = k.shape
    pairs = width // 128
    column = pl.BlockSpec((length, 128), lambda p: (0, p))
    return pl.pallas_call(
        functools.partial(attend_kernel, pics),
        grid=(pairs,),
        in_specs=[column, column, column, pl.BlockSpec((8, 128), lambda p: (0, 0))],
        out_specs=[
            pl.BlockSpec((queries, 128), lambda p: (0, p)),
            pl.BlockSpec((2, queries, 128), lambda p: (p, 0, 0)),
        ],
        scratch_shapes=[
            pltpu.VMEM((2, length, 128), BF16),
            pltpu.VMEM((2, length, 128), BF16),
            pltpu.VMEM((queries, 128), BF16),
        ],
        out_shape=[
            jax.ShapeDtypeStruct((queries, width), BF16),
            jax.ShapeDtypeStruct((2 * pairs, queries, 128), BF16),
        ],
        compiler_params=pltpu.CompilerParams(vmem_limit_bytes=VMEM_LIMIT),
        cost_estimate=pl.CostEstimate(
            flops=16 * length * queries * width, bytes_accessed=length * width * 12, transcendentals=0
        ),
        name="attend",
    )(q, k, v, bounds)


def head_norm_back(e, raw, gain, means):
    c = raw - group_sum(raw, means)
    r = lax.rsqrt(group_sum(c * c, means) + EPSILON)
    n = c * r
    t = e * gain
    grad = r * (t - group_sum(t, means) - n * group_sum(t * n, means))
    return grad.astype(BF16), jnp.sum(e * n, axis=0, keepdims=True)


def attend_back_kernel(
    pics, aug_ref, k_ref, v_ref, out_ref, do_ref, rawq_ref, rawk_ref, qg_ref, kg_ref, bounds_ref,
    dq_ref, dk_ref, dv_ref, qgg_ref, kgg_ref, kaug, vaug, doaug, qsum, ksum,
):
    length = k_ref.shape[0]
    queries = do_ref.shape[0]
    part = length // 4
    whole = queries == length
    lane = lax.broadcasted_iota(jnp.int32, (1, 128), 1)
    place = lane % HEAD
    sides = [lane < HEAD, lane >= HEAD]
    kmarks = key_marks(bounds_ref, place, length, pics)
    vmarks = jnp.where(place < 2, 1.0, 0.0).astype(BF16)
    ones = group_ones(1.0)
    inner = group_sum(do_ref[...].astype(F32) * out_ref[...].astype(F32), ones)
    inner = -pltpu.roll(inner, HEAD, 1)
    inner_high = inner.astype(BF16)
    inner_low = (inner - inner_high.astype(F32)).astype(BF16)
    zero = jnp.zeros((), BF16)
    gmarks = jnp.where(place == 0, inner_high, jnp.where(place == 1, inner_low, zero))
    for h in range(2):
        kaug[h] = jnp.where(sides[h], k_ref[...], kmarks)
        vaug[h] = jnp.where(sides[h], v_ref[...], vmarks)
        doaug[h] = jnp.where(sides[h], do_ref[...], gmarks)
    for b in range(length // STEP):
        keys = pl.ds(b * STEP, STEP)
        key = [kaug[h, keys, :] for h in range(2)]
        value = [vaug[h, keys, :] for h in range(2)]
        dk = [jnp.zeros((STEP, 128), F32)] * 2
        dv = [jnp.zeros((STEP, 128), F32)] * 2
        for j in range(queries // STEP):
            rows = pl.ds(j * STEP, STEP)
            query = [aug_ref[h, rows, :] for h in range(2)]
            grad = [doaug[h, rows, :] for h in range(2)]
            scores = [nt(key[h], query[h]) for h in range(2)]
            soft_grad = [nt(value[h], grad[h]) for h in range(2)]
            weights = [jnp.exp2(x * EXP2_FACTOR) for x in scores]
            score_grad = [(weights[h] * soft_grad[h]).astype(BF16) for h in range(2)]
            for h in range(2):
                part_sum = tn(score_grad[h], key[h])
                if b == 0:
                    qsum[h, rows, :] = part_sum
                else:
                    qsum[h, rows, :] += part_sum
                dk[h] = dk[h] + jnp.dot(score_grad[h], query[h], preferred_element_type=F32)
                dv[h] = dv[h] + jnp.dot(weights[h].astype(BF16), grad[h], preferred_element_type=F32)
        ksum[keys, :] = jnp.where(sides[0], dk[0], dk[1]) * HEAD**-0.5
        dv_ref[keys, :] = jnp.where(sides[0], dv[0], dv[1]).astype(BF16)

    means = group_ones(1.0 / HEAD)
    gain_sum = jnp.zeros((1, 128), F32)
    for b in range(queries // part):
        rows = pl.ds(b * part, part)
        e = jnp.where(sides[0], qsum[0, rows, :], qsum[1, rows, :]) * HEAD**-0.5
        raw = own_rows(rawq_ref, b * part, part, queries, part)
        dq_ref[rows, :], more = head_norm_back(e.astype(BF16).astype(F32), raw, qg_ref[...], means)
        gain_sum = gain_sum + more
    qgg_ref[...] = gain_sum
    gain_sum = jnp.zeros((1, 128), F32)
    for b in range(length // part):
        rows = pl.ds(b * part, part)
        e = ksum[rows, :].astype(BF16)
        if whole:
            dk_ref[rows, :], more = head_norm_back(e.astype(F32), rawk_ref[rows, :], kg_ref[...], means)
            gain_sum = gain_sum + more
        else:
            dk_ref[rows, :] = e
    kgg_ref[...] = gain_sum


def attend_back(aug, k, v, out, do, raw, query_gain, key_gain, bounds, pics):
    length, width = k.shape
    queries = do.shape[0]
    pairs = width // 128
    column = pl.BlockSpec((length, 128), lambda p: (0, p))
    own = pl.BlockSpec((queries, 128), lambda p: (0, p))
    gain = pl.BlockSpec((1, 128), lambda p: (0, p))
    return pl.pallas_call(
        functools.partial(attend_back_kernel, pics),
        grid=(pairs,),
        in_specs=[
            pl.BlockSpec((2, queries, 128), lambda p: (p, 0, 0)),
            column,
            column,
            own,
            own,
            column,
            pl.BlockSpec((length, 128), lambda p: (0, pairs + p)),
            gain,
            gain,
            pl.BlockSpec((8, 128), lambda p: (0, 0)),
        ],
        out_specs=[own, column, column, gain, gain],
        scratch_shapes=[
            pltpu.VMEM((2, length, 128), BF16),
            pltpu.VMEM((2, length, 128), BF16),
            pltpu.VMEM((2, queries, 128), BF16),
            pltpu.VMEM((2, queries, 128), F32),
            pltpu.VMEM((length, 128), F32),
        ],
        out_shape=[
            jax.ShapeDtypeStruct((queries, width), BF16),
            jax.ShapeDtypeStruct((length, width), BF16),
            jax.ShapeDtypeStruct((length, width), BF16),
            jax.ShapeDtypeStruct((1, width), F32),
            jax.ShapeDtypeStruct((1, width), F32),
        ],
        compiler_params=pltpu.CompilerParams(vmem_limit_bytes=VMEM_LIMIT),
        cost_estimate=pl.CostEstimate(
            flops=40 * length * queries * width, bytes_accessed=length * width * 20, transcendentals=0
        ),
        name="attend_back",
    )(aug, k, v, out, do, raw, raw, query_gain, key_gain, bounds)


def shared_keys_kernel(dk_ref, dv_ref, gotk_ref, gotv_ref, rawk_ref, kg_ref, outk_ref, outv_ref, kgg_ref):
    count = outk_ref.shape[0]
    part = count // 2
    means = group_ones(1.0 / HEAD)
    gain_sum = jnp.zeros((1, 128), F32)
    for b in range(2):
        rows = pl.ds(b * part, part)
        own = lambda ref: own_rows(ref, b * part, part, count, part)
        e = own(dk_ref).astype(F32) + gotk_ref[rows, :].astype(F32)
        outk_ref[rows, :], more = head_norm_back(e, own(rawk_ref), kg_ref[...], means)
        gain_sum = gain_sum + more
        outv_ref[rows, :] = (own(dv_ref).astype(F32) + gotv_ref[rows, :].astype(F32)).astype(BF16)
    kgg_ref[...] = gain_sum


def shared_keys(dk, dv, got_k, got_v, raw, key_gain):
    length, width = dk.shape
    pairs = width // 128
    column = pl.BlockSpec((length, 128), lambda p: (0, p))
    own = pl.BlockSpec((length // 2, 128), lambda p: (0, p))
    gain = pl.BlockSpec((1, 128), lambda p: (0, p))
    return pl.pallas_call(
        shared_keys_kernel,
        grid=(pairs,),
        in_specs=[column, column, own, own, pl.BlockSpec((length, 128), lambda p: (0, pairs + p)), gain],
        out_specs=[own, own, gain],
        out_shape=[
            jax.ShapeDtypeStruct((length // 2, width), BF16),
            jax.ShapeDtypeStruct((length // 2, width), BF16),
            jax.ShapeDtypeStruct((1, width), F32),
        ],
        compiler_params=pltpu.CompilerParams(vmem_limit_bytes=VMEM_LIMIT),
        name="shared_keys",
    )(dk, dv, got_k, got_v, raw, key_gain)


def gelu_pair(h):
    size = jnp.abs(h)
    bell = jnp.exp2(h * h * -0.7213475204444817)
    t = 1.0 / (1.0 + 0.23164189 * size)
    series = t * (0.127414796 + t * (-0.142248368 + t * (0.7107068705 + t * (-0.7265760135 + t * 0.5307027145))))
    tail = series * bell
    below = jnp.where(h < 0.0, tail, 1.0 - tail)
    return h * below, below + h * (bell * 0.3989422804014327)


def norm_parts(values):
    center = values - jnp.mean(values, axis=-1, keepdims=True)
    spread = lax.rsqrt(jnp.mean(center * center, axis=-1, keepdims=True) + EPSILON)
    return center * spread, spread


def norm_back(upstream, n, r, gain):
    t = upstream * gain
    grad = r * (t - jnp.mean(t, axis=-1, keepdims=True) - n * jnp.mean(t * n, axis=-1, keepdims=True))
    return grad, jnp.sum(upstream * n, axis=0, keepdims=True)


def dense_kernel(
    attended_ref, x_ref, outw_ref, gain_ref, grad_ref, up_ref, down_ref,
    output_ref, midg_ref, attg_ref, outg_ref, upg_ref, downg_ref, gaing_ref,
    middle, second, forward, backward,
):
    step = pl.program_id(0)
    tokens = x_ref.shape[0]
    blocks = [pl.ds(b * BLOCK, BLOCK) for b in range(tokens // BLOCK)]

    @pl.when(step == 0)
    def _():
        for rows in blocks:
            value = x_ref[rows, :].astype(F32) + jnp.dot(
                attended_ref[rows, :], outw_ref[...], preferred_element_type=F32
            )
            middle[rows, :] = value
            second[rows, :] = (norm_parts(value)[0] * gain_ref[...]).astype(BF16)
        forward[...] = jnp.zeros_like(forward)
        backward[...] = jnp.zeros_like(backward)

    up = up_ref[...]
    down = down_ref[...]
    pre = jnp.dot(second[...], up, preferred_element_type=F32)
    hidden, slope = gelu_pair(pre)
    hidden = hidden.astype(BF16)
    forward[...] += jnp.dot(hidden, down, preferred_element_type=F32)
    pre_grad = (nt(grad_ref[...], down) * slope).astype(BF16)
    downg_ref[...] = tn(hidden, grad_ref[...]).astype(BF16)
    upg_ref[...] = tn(second[...], pre_grad).astype(BF16)
    backward[...] += nt(pre_grad, up)

    @pl.when(step == pl.num_programs(0) - 1)
    def _():
        gain_sum = jnp.zeros(gaing_ref.shape, F32)
        for rows in blocks:
            value = middle[rows, :]
            output_ref[rows, :] = (value + forward[rows, :]).astype(BF16)
            n, r = norm_parts(value)
            part, more = norm_back(backward[rows, :], n, r, gain_ref[...])
            gain_sum = gain_sum + more
            value = grad_ref[rows, :].astype(F32) + part
            midg_ref[rows, :] = value
            branch = value.astype(BF16)
            second[rows, :] = branch
            attg_ref[rows, :] = nt(branch, outw_ref[...]).astype(BF16)
        gaing_ref[...] = gain_sum
        outg_ref[...] = tn(attended_ref[...], second[...]).astype(BF16)


def dense(attended, x, out_matrix, gain, grad, up, down):
    tokens, model = x.shape
    hidden = up.shape[1]
    tile = 512
    whole = pl.BlockSpec((tokens, model), lambda i: (0, 0))
    square = pl.BlockSpec((model, model), lambda i: (0, 0))
    line = pl.BlockSpec((1, model), lambda i: (0, 0))
    wide = pl.BlockSpec((model, tile), lambda i: (0, i))
    tall = pl.BlockSpec((tile, model), lambda i: (i, 0))
    return pl.pallas_call(
        dense_kernel,
        grid=(hidden // tile,),
        in_specs=[whole, whole, square, line, whole, wide, tall],
        out_specs=[whole, whole, whole, square, wide, tall, line],
        out_shape=[
            jax.ShapeDtypeStruct((tokens, model), BF16),
            jax.ShapeDtypeStruct((tokens, model), F32),
            jax.ShapeDtypeStruct((tokens, model), BF16),
            jax.ShapeDtypeStruct((model, model), BF16),
            jax.ShapeDtypeStruct((model, hidden), BF16),
            jax.ShapeDtypeStruct((hidden, model), BF16),
            jax.ShapeDtypeStruct((1, model), F32),
        ],
        scratch_shapes=[
            pltpu.VMEM((tokens, model), F32),
            pltpu.VMEM((tokens, model), BF16),
            pltpu.VMEM((tokens, model), F32),
            pltpu.VMEM((tokens, model), F32),
        ],
        compiler_params=pltpu.CompilerParams(vmem_limit_bytes=VMEM_LIMIT),
        cost_estimate=pl.CostEstimate(
            flops=16 * tokens * model * hidden, bytes_accessed=8 * model * hidden, transcendentals=0
        ),
        name="dense",
    )(attended, x, out_matrix, gain, grad, up, down)


MESH_ID = pl.DeviceIdType.MESH


def here():
    return lax.axis_index("chip"), lax.axis_index("core"), lax.axis_index("zp"), lax.axis_index("zq")


def remote(source, target, sems, at, device):
    sent, got = sems
    return pltpu.make_async_remote_copy(
        src_ref=source, dst_ref=target, send_sem=sent.at[at], recv_sem=got.at[at],
        device_id=device, device_id_type=MESH_ID,
    )


def greet(devices, maybe=None, moves=None):
    barrier = pltpu.get_barrier_semaphore()
    for device in devices:
        pl.semaphore_signal(barrier, inc=1, device_id=device, device_id_type=MESH_ID)
    if maybe is None:
        pl.semaphore_wait(barrier, len(devices))
        return

    @pl.when(moves)
    def _():
        pl.semaphore_signal(barrier, inc=1, device_id=maybe, device_id_type=MESH_ID)

    pl.semaphore_wait(barrier, len(devices) + jnp.where(moves, 1, 0))


def rows_at(start, count):
    return pl.ds(pl.multiple_of(start, 16), count)


def gather_kernel(
    with_mix, tokens_ref, lens_ref, mix_ref, gains_ref,
    row_ref, shared_ref, lens_out, mix_out, gains_out, sent, got, local_sem,
):
    chip, core, zp, zq = here()
    z = 2 * zp + zq
    part = tokens_ref.shape[1]
    sems = (sent, got)
    partner = (chip, 1 - core, zp, zq)
    side = (chip, core, zp, 1 - zq)
    keep = (chip, zp, core, zq)
    cross = (chip, zp, core, 1 - zq)
    moves = core != zp
    near_x = (chip ^ 1, core, zp, zq)
    near_y = (chip ^ 2, core, zp, zq)
    greet([partner, side, cross] + ([near_x, near_y] if with_mix else []), keep, moves)

    def quarter(ref, index):
        return ref.at[rows_at(index * part, part)]

    own_row = remote(tokens_ref.at[zq], quarter(row_ref, z), sems, 0, keep)
    own_shared = remote(tokens_ref.at[2], quarter(shared_ref, z), sems, 2, keep)
    stay_row = pltpu.make_async_copy(tokens_ref.at[zq], quarter(row_ref, z), local_sem.at[0])
    stay_shared = pltpu.make_async_copy(tokens_ref.at[2], quarter(shared_ref, z), local_sem.at[1])

    @pl.when(moves)
    def _():
        own_row.start()

    @pl.when(jnp.logical_not(moves))
    def _():
        stay_row.start()

    cross_row = remote(tokens_ref.at[1 - zq], quarter(row_ref, z), sems, 1, cross)
    cross_row.start()

    @pl.when(moves)
    def _():
        own_shared.start()

    @pl.when(jnp.logical_not(moves))
    def _():
        stay_shared.start()

    lens_copy = remote(lens_ref, lens_out.at[core], sems, 8, partner)
    lens_copy.start()
    lens_stay = pltpu.make_async_copy(lens_ref, lens_out.at[core], local_sem.at[2])
    lens_stay.start()
    if with_mix:
        shard = mix_ref.shape[1]

        def piece(index):
            return mix_out.at[rows_at(index * shard, shard)]

        mine, theirs = 2 * chip + core, 2 * chip + 1 - core
        x_mine, y_other = 2 * (chip ^ 1) + core, 2 * (chip ^ 2) + 1 - core

        def move(source, gain_source, index, at, device):
            copies = (
                remote(source, piece(index), sems, 9 + 2 * at, device),
                remote(gain_source, gains_out.at[index], sems, 10 + 2 * at, device),
            )
            for copy in copies:
                copy.start()
            return copies

        def arrived(copies):
            for copy in copies:
                copy.wait_recv()

        to_core = move(mix_ref.at[1 - core], gains_ref, mine, 0, partner)
        a_x = move(mix_ref.at[core], gains_ref, mine, 1, near_x)
        a_y = move(mix_ref.at[core], gains_ref, mine, 2, near_y)
        mix_stay = pltpu.make_async_copy(mix_ref.at[core], piece(mine), local_sem.at[3])
        mix_stay.start()
        gain_stay = pltpu.make_async_copy(gains_ref, gains_out.at[mine], local_sem.at[4])
        gain_stay.start()
        arrived(to_core)
        b_x = move(piece(theirs), gains_out.at[theirs], theirs, 3, near_x)
        b_y = move(piece(theirs), gains_out.at[theirs], theirs, 4, near_y)
        arrived(a_x)
        a_far = move(piece(x_mine), gains_out.at[x_mine], x_mine, 5, near_y)
        arrived(b_y)
        b_far = move(piece(y_other), gains_out.at[y_other], y_other, 6, near_x)

    @pl.when(moves)
    def _():
        own_row.wait_recv()

    @pl.when(jnp.logical_not(moves))
    def _():
        stay_row.wait()

    first, second = 2 * core + zq, 2 * core + 1 - zq
    row_one = remote(quarter(row_ref, first), quarter(row_ref, first), sems, 3, partner)
    row_one.start()
    cross_row.wait_recv()
    row_two = remote(quarter(row_ref, second), quarter(row_ref, second), sems, 4, partner)
    row_two.start()

    @pl.when(moves)
    def _():
        own_shared.wait_recv()

    @pl.when(jnp.logical_not(moves))
    def _():
        stay_shared.wait()

    to_side = remote(quarter(shared_ref, first), quarter(shared_ref, first), sems, 5, side)
    to_side.start()
    shared_one = remote(quarter(shared_ref, first), quarter(shared_ref, first), sems, 6, partner)
    shared_one.start()
    to_side.wait_recv()
    shared_two = remote(quarter(shared_ref, second), quarter(shared_ref, second), sems, 7, partner)
    shared_two.start()

    lens_copy.wait()
    lens_stay.wait()
    if with_mix:
        mix_stay.wait()
        gain_stay.wait()
        for copies in (a_y, b_x, a_far, b_far):
            arrived(copies)
        for copies in (to_core, a_x, a_y, b_x, b_y, a_far, b_far):
            for copy in copies:
                copy.wait_send()
    for copy in (row_one, row_two, shared_one, shared_two):
        copy.wait()
    to_side.wait_send()
    cross_row.wait_send()

    @pl.when(moves)
    def _():
        own_row.wait_send()
        own_shared.wait_send()


def gather_rows(tokens, lens, mix, gains, with_mix):
    _, part, model = tokens.shape
    pieces = mix.shape[1] * 8
    anywhere = pl.BlockSpec(memory_space=pl.ANY)
    return pl.pallas_call(
        functools.partial(gather_kernel, with_mix),
        in_specs=[anywhere] * 4,
        out_specs=[anywhere] * 5,
        out_shape=[
            jax.ShapeDtypeStruct((4 * part, model), BF16),
            jax.ShapeDtypeStruct((4 * part, model), BF16),
            jax.ShapeDtypeStruct((2,) + lens.shape, jnp.int32),
            jax.ShapeDtypeStruct((pieces, mix.shape[2]), BF16),
            jax.ShapeDtypeStruct((8,) + gains.shape, BF16),
        ],
        scratch_shapes=[
            pltpu.SemaphoreType.DMA((23,)),
            pltpu.SemaphoreType.DMA((23,)),
            pltpu.SemaphoreType.DMA((5,)),
        ],
        compiler_params=pltpu.CompilerParams(collective_id=0, has_side_effects=True),
        name="gather_rows",
    )(tokens, lens, mix, gains)


def to_tokens_kernel(row_ref, shared_ref, out_ref, sent, got, local_sem):
    chip, core, zp, zq = here()
    partner = (chip, 1 - core, zp, zq)
    half, width = row_ref.shape[0] // 2, row_ref.shape[1]
    part = half // 2
    greet([partner])
    lanes = pl.ds(pl.multiple_of(core * width, 128), width)
    top, bottom = out_ref.at[pl.ds(0, half), lanes], out_ref.at[pl.ds(half, part), lanes]
    copies = [
        remote(row_ref.at[rows_at((1 - core) * half, half)], top, (sent, got), 0, partner),
        remote(shared_ref.at[rows_at((1 - core) * part, part)], bottom, (sent, got), 1, partner),
        pltpu.make_async_copy(row_ref.at[rows_at(core * half, half)], top, local_sem.at[0]),
        pltpu.make_async_copy(shared_ref.at[rows_at(core * part, part)], bottom, local_sem.at[1]),
    ]
    for copy in copies:
        copy.start()
    for copy in copies:
        copy.wait()


def to_heads_kernel(grad_ref, row_ref, shared_ref, sent, got, local_sem):
    chip, core, zp, zq = here()
    partner = (chip, 1 - core, zp, zq)
    half, width = row_ref.shape[0] // 2, row_ref.shape[1]
    part = half // 2
    greet([partner])

    def source(first, count, side):
        return grad_ref.at[pl.ds(first, count), pl.ds(pl.multiple_of(side * width, 128), width)]

    top, bottom = row_ref.at[rows_at(core * half, half)], shared_ref.at[rows_at(core * part, part)]
    copies = [
        remote(source(0, half, 1 - core), top, (sent, got), 0, partner),
        remote(source(half, part, 1 - core), bottom, (sent, got), 1, partner),
        pltpu.make_async_copy(source(0, half, core), top, local_sem.at[0]),
        pltpu.make_async_copy(source(half, part, core), bottom, local_sem.at[1]),
    ]
    for copy in copies:
        copy.start()
    for copy in copies:
        copy.wait()


def core_exchange(kernel, ident, outs, *arrays):
    anywhere = pl.BlockSpec(memory_space=pl.ANY)
    return pl.pallas_call(
        kernel,
        in_specs=[anywhere] * len(arrays),
        out_specs=[anywhere] * len(outs),
        out_shape=[jax.ShapeDtypeStruct(shape, BF16) for shape in outs],
        scratch_shapes=[
            pltpu.SemaphoreType.DMA((2,)),
            pltpu.SemaphoreType.DMA((2,)),
            pltpu.SemaphoreType.DMA((2,)),
        ],
        compiler_params=pltpu.CompilerParams(collective_id=ident, has_side_effects=True),
        name="core_exchange",
    )(*arrays)


def finish_kernel(
    grad_ref, mix_ref, out_ref, total_ref, gains_ref,
    relay, final, core_got, chunks, gain_parts, chunk_got, gain_got, sent, got, local_sem,
):
    chip, core, zp, zq = here()
    z = 2 * zp + zq
    sems = (sent, got)
    part = out_ref.shape[1]
    shard = mix_ref.shape[1] - 16
    quarter = shard // 2
    columns = mix_ref.shape[2]
    partner = (chip, 1 - core, zp, zq)
    keep = (chip, zp, core, zq)
    cross = (chip, zp, core, 1 - zq)
    moves = core != zp
    near_x = (chip ^ 1, core, zp, zq)
    near_y = (chip ^ 2, core, zp, zq)
    along = [(chip, core, zp, 1 - zq), (chip, core, 1 - zp, zq), (chip, core, 1 - zp, 1 - zq)]
    greet([partner, cross, near_x, near_y] + along, keep, moves)

    mine, theirs = 2 * chip + core, 2 * chip + 1 - core
    x_mine, x_other = 2 * (chip ^ 1) + core, 2 * (chip ^ 1) + 1 - core
    y_mine, y_other = 2 * (chip ^ 2) + core, 2 * (chip ^ 2) + 1 - core
    far_mine, far_other = 2 * (chip ^ 3) + core, 2 * (chip ^ 3) + 1 - core
    first = remote(mix_ref.at[far_mine], relay.at[0], sems, 0, near_y)
    second = remote(mix_ref.at[far_other], relay.at[1], sems, 1, near_x)
    first.start()
    second.start()
    direct_x = remote(mix_ref.at[x_other], final.at[0], sems, 2, near_x)
    direct_y = remote(mix_ref.at[y_mine], final.at[1], sems, 3, near_y)
    direct_x.start()
    direct_y.start()

    own = pl.ds(pl.multiple_of(zq * part, 16), part)
    own_row = remote(grad_ref.at[own], out_ref.at[zq], sems, 4, keep)
    own_shared = remote(grad_ref.at[pl.ds(2 * part, part)], out_ref.at[2], sems, 5, keep)
    stay_row = pltpu.make_async_copy(grad_ref.at[own], out_ref.at[zq], local_sem.at[0])
    stay_shared = pltpu.make_async_copy(grad_ref.at[pl.ds(2 * part, part)], out_ref.at[2], local_sem.at[1])

    @pl.when(moves)
    def _():
        own_row.start()
        own_shared.start()

    @pl.when(jnp.logical_not(moves))
    def _():
        stay_row.start()
        stay_shared.start()

    cross_row = remote(grad_ref.at[rows_at((1 - zq) * part, part)], out_ref.at[zq], sems, 6, cross)
    cross_row.start()

    def add(*terms):
        total = terms[0].astype(F32)
        for term in terms[1:]:
            total = total + term.astype(F32)
        return total

    first.wait_recv()
    relay[2] = add(relay[0], mix_ref[x_mine]).astype(BF16)
    onward_x = remote(relay.at[2], final.at[2], sems, 7, near_x)
    onward_x.start()
    second.wait_recv()
    relay[3] = add(relay[1], mix_ref[y_other]).astype(BF16)
    onward_y = remote(relay.at[3], final.at[3], sems, 8, near_y)
    onward_y.start()
    direct_x.wait_recv()
    onward_y.wait_recv()
    relay[4] = add(mix_ref[theirs], final[0], final[3]).astype(BF16)
    to_core = remote(relay.at[4], core_got, sems, 9, partner)
    to_core.start()
    direct_y.wait_recv()
    onward_x.wait_recv()
    kept = add(mix_ref[mine], final[1], final[2])
    for i in range(2):
        chunks[2 * core + i] = kept[i * quarter : (i + 1) * quarter].astype(BF16)
    to_core.wait_recv()
    for i in range(2):
        chunks[2 * (1 - core) + i] = core_got[i * quarter : (i + 1) * quarter]
    gain_parts[0] = (kept[shard:] + core_got[shard:].astype(F32)).astype(BF16)
    hops = [z ^ 1, z ^ 2, z ^ 3]
    copies = []
    for i in range(3):
        copies.append(remote(chunks.at[hops[i]], chunk_got.at[i], sems, 10 + i, along[i]))
        copies.append(remote(gain_parts.at[0], gain_got.at[i], sems, 13 + i, along[i]))
    for copy in copies:
        copy.start()
    for copy in copies:
        copy.wait_recv()
    gains_ref[...] = add(gain_parts[0], gain_got[0], gain_got[1], gain_got[2])
    chunk_got[3] = add(chunks[z], chunk_got[0], chunk_got[1], chunk_got[2]).astype(BF16)
    spread = [remote(chunk_got.at[3], chunk_got.at[4 + i], sems, 16 + i, along[i]) for i in range(3)]
    for copy in spread:
        copy.start()

    def place(index, values):
        half, up = index // 2, index % 2
        third = columns // 3
        values = values.astype(F32)
        for h in range(2):
            for u in range(2):

                @pl.when((half == h) & (up == u))
                def _():
                    for p in range(3):
                        total_ref[u * quarter : (u + 1) * quarter, (2 * p + h) * third : (2 * p + h + 1) * third] = (
                            values[:, p * third : (p + 1) * third]
                        )

    place(z, chunk_got[3])
    for i in range(3):
        spread[i].wait_recv()
        place(hops[i], chunk_got[4 + i])
    for copy in copies + spread + [first, second, direct_x, direct_y, onward_x, onward_y, to_core]:
        copy.wait_send()
    cross_row.wait()

    @pl.when(moves)
    def _():
        own_row.wait()
        own_shared.wait()

    @pl.when(jnp.logical_not(moves))
    def _():
        stay_row.wait()
        stay_shared.wait()


def finish(grad, mix):
    tokens, model = grad.shape
    _, rows, columns = mix.shape
    shard = rows - 16
    anywhere = pl.BlockSpec(memory_space=pl.ANY)
    local_space = pl.BlockSpec(memory_space=pltpu.VMEM)
    buffers = lambda count, size: pltpu.VMEM((count, size, columns), BF16)
    return pl.pallas_call(
        finish_kernel,
        in_specs=[anywhere, local_space],
        out_specs=[anywhere, local_space, local_space],
        out_shape=[
            jax.ShapeDtypeStruct((3, tokens // 3, model), BF16),
            jax.ShapeDtypeStruct((shard, 2 * columns), F32),
            jax.ShapeDtypeStruct((16, columns), F32),
        ],
        scratch_shapes=[
            buffers(5, rows),
            buffers(4, rows),
            pltpu.VMEM((rows, columns), BF16),
            buffers(4, shard // 2),
            buffers(1, 16),
            buffers(7, shard // 2),
            buffers(3, 16),
            pltpu.SemaphoreType.DMA((19,)),
            pltpu.SemaphoreType.DMA((19,)),
            pltpu.SemaphoreType.DMA((2,)),
        ],
        compiler_params=pltpu.CompilerParams(
            collective_id=3, has_side_effects=True, vmem_limit_bytes=VMEM_LIMIT
        ),
        name="finish",
    )(grad, mix)


def row_bounds(lengths_row, length):
    pics = lengths_row.shape[0]
    ends = jnp.cumsum(lengths_row)
    starts = ends - lengths_row
    last = jnp.arange(pics) == jnp.sum(lengths_row > 0) - 1
    table = jnp.stack([starts, ends, jnp.where(last, length, ends)]).astype(jnp.int32)
    table = jnp.pad(table, ((0, 5), (0, HEAD - pics)), constant_values=2 * length)
    return jnp.tile(table, (1, 2)), ends[-1]


def local(
    tokens, lengths, pictures, first_gain, mix_weight, query_gain, key_gain, out_weight,
    second_gain, up_weight, down_weight, cotangent,
):
    chip, core, zp, zq = here()
    chips = lax.axis_size("chip")
    square = chips == 4
    rows = ("chip", "core")
    _, part, model = tokens.shape
    length = 4 * part
    half = 2 * part
    width = HEADS // 2 * HEAD
    pics = lengths.shape[1]
    shard = mix_weight.shape[0]

    gains = jnp.stack([first_gain, query_gain, key_gain, second_gain])
    gains = jnp.pad(gains, ((0, 12), (0, 128 - shard)))
    mix_split = mix_weight.reshape(shard, 3, 2, width).transpose(2, 0, 1, 3).reshape(2, shard, 3 * width)
    lens = jnp.pad(lengths, ((0, 5), (0, 128 - pics)))
    row_tokens, shared_tokens, lens, mix_half, gain_parts = gather_rows(tokens, lens, mix_split, gains, square)
    if not square:
        whole = lax.all_gather(mix_weight, rows, axis=0, tiled=True)
        mix_half = pick(whole.reshape(model, 3, 2, width), core, 2).reshape(model, 3 * width)
        gain_parts = lax.all_gather(gains, rows, axis=0, tiled=False)
    out_matrix = lax.all_gather(out_weight, rows, axis=0, tiled=True)
    up_matrix = lax.all_gather(up_weight, rows, axis=0, tiled=True)
    down_matrix = lax.all_gather(down_weight, rows, axis=0, tiled=True)
    gains = gain_parts[:, :4, :shard].transpose(1, 0, 2).reshape(4, 1, model).astype(F32)
    gain_first, gain_second = gains[0], gains[3]
    gain_query = pick(gains[1].reshape(2, 1, width), core)
    gain_key = pick(gains[2].reshape(2, 1, width), core)
    owner_lengths = pick(lens, zp)[:3, :pics]
    bounds, filled = row_bounds(pick(owner_lengths, zq), length)
    shared_bounds, shared_filled = row_bounds(owner_lengths[2], length)

    def spread(array):
        mine = lax.ppermute(pick(array, zq), COLUMN, KEEP)
        cross = lax.ppermute(pick(array, 1 - zq), COLUMN, CROSS)
        shared = lax.ppermute(array[2], COLUMN, KEEP)
        return jnp.concatenate([jnp.where(zq == 0, mine, cross), jnp.where(zq == 0, cross, mine), shared])

    def collect(array):
        first, second, shared = array[:part], array[part:half], array[half:]
        mine = lax.ppermute(jnp.where(zq == 0, first, second), COLUMN, KEEP)
        cross = lax.ppermute(jnp.where(zq == 0, second, first), COLUMN, CROSS)
        shared = lax.ppermute(shared, COLUMN, KEEP)
        return jnp.stack([jnp.where(zq == 0, mine, cross), jnp.where(zq == 0, cross, mine), shared])

    grad_tokens = spread(cotangent)

    normed, q, k, v, raw = project(row_tokens, gain_first, mix_half, gain_query, gain_key)
    out, aug = attend(q, k, v, bounds, pics, length)
    shared_normed, shared_q, shared_k, shared_v, shared_raw = project(
        shared_tokens, gain_first, mix_half, gain_query, gain_key
    )
    shared_out, shared_aug = attend(shared_q, shared_k, shared_v, shared_bounds, pics, half)
    (attended,) = core_exchange(to_tokens_kernel, 1, [(3 * part, model)], out, shared_out)

    own_tokens = jnp.concatenate(
        [
            lax.dynamic_slice_in_dim(row_tokens, core * half, half),
            lax.dynamic_slice_in_dim(shared_tokens, (2 * core + zq) * part, part),
        ]
    )
    place = core * half + jnp.arange(half)
    shared_place = (2 * core + zq) * part + jnp.arange(part)
    valid = jnp.concatenate([place < filled, shared_place < shared_filled])
    grad_low = jnp.where(valid[:, None], grad_tokens, 0)
    output, middle_grad, attended_grad, out_grad, up_grad, down_grad, second_gain_grad = dense(
        attended, own_tokens, out_matrix, gain_second, grad_low, up_matrix, down_matrix
    )
    output = collect(output)

    def reduce(grad):
        return lax.psum(lax.psum_scatter(grad, rows, scatter_dimension=0, tiled=True), SEQ).astype(F32)

    up_out = reduce(up_grad)
    down_out = reduce(down_grad)
    outw_out = reduce(out_grad)

    grad, shared_grad = core_exchange(to_heads_kernel, 2, [(length, width), (half, width)], attended_grad)
    shared_dq, part_k, part_v, shared_qgg, _ = attend_back(
        shared_aug, shared_k, shared_v, shared_out, shared_grad, shared_raw, gain_query, gain_key,
        shared_bounds, pics,
    )

    def to_side(array):
        return swap(pick(array.reshape(2, 2, part, width), 1 - zq, 1), "zq").reshape(half, width)

    got_k, got_v = to_side(part_k), to_side(part_v)
    dq, dk, dv, qgg, kgg = attend_back(
        aug, k, v, out, grad, raw, gain_query, gain_key, bounds, pics
    )
    shared_dk, shared_dv, shared_kgg = shared_keys(part_k, part_v, got_k, got_v, shared_raw, gain_key)
    mixed = jnp.concatenate(
        [jnp.concatenate([dq, shared_dq]), jnp.concatenate([dk, shared_dk]), jnp.concatenate([dv, shared_dv])],
        axis=1,
    )
    own_shared = pick(shared_normed.reshape(2, 2, part, model), zq, 1).reshape(half, model)
    mix_grad = tn(jnp.concatenate([normed, own_shared]), mixed).astype(BF16)
    partial = nt(mixed, mix_half)
    row_partial = partial[:length].reshape(2, half, model)
    shared_partial = partial[length:].reshape(2, part, model)
    mine = jnp.concatenate([pick(row_partial, core), pick(shared_partial, core)])
    sent = jnp.concatenate([pick(row_partial, 1 - core), pick(shared_partial, 1 - core)])
    normed_grad = mine + swap(sent.astype(BF16), "core").astype(F32)
    n_first, r_first = norm_parts(own_tokens.astype(F32))
    input_part, first_gain_grad = norm_back(normed_grad, n_first, r_first, gain_first)
    input_grad = (middle_grad + input_part).astype(BF16)

    def place_heads(values):
        return jnp.where(jnp.arange(2)[:, None] == core, values, 0.0).reshape(1, model)

    gain_grads = jnp.concatenate(
        [first_gain_grad, place_heads(qgg + shared_qgg), place_heads(kgg + shared_kgg), second_gain_grad]
    )
    gain_grads = gain_grads.reshape(4, 2 * chips, shard).transpose(1, 0, 2).astype(BF16)
    if square:
        gain_rows = jnp.pad(gain_grads, ((0, 0), (0, 12), (0, 3 * width - shard)))
        payload = jnp.concatenate([mix_grad.reshape(2 * chips, shard, 3 * width), gain_rows], axis=1)
        input_out, mix_out, gains_out = finish(input_grad, payload)
        gains_out = gains_out[:4, :shard]
    else:
        input_out = collect(input_grad)
        spread_mix = jnp.where(
            jnp.arange(2)[None, None, :, None] == core, mix_grad.reshape(model, 3, 1, width), 0
        ).reshape(model, 6 * width)
        mix_out = reduce(spread_mix)
        gains_out = reduce(gain_grads).reshape(4, shard)
    return (
        output, input_out, gains_out[0], mix_out, gains_out[1], gains_out[2], outw_out, gains_out[3],
        up_out, down_out,
    )


def solution(mesh):
    fsdp = mesh.shape["fsdp"]
    split = Mesh(mesh.devices.reshape(fsdp // 2, 2, 2, 2), ("chip", "core", "zp", "zq"))
    rows = ("chip", "core")
    return jax.shard_map(
        local,
        mesh=split,
        in_specs=(
            P(rows, SEQ, None),
            P(rows, None),
            P(rows, SEQ),
            P(rows),
            P(rows, None),
            P(rows),
            P(rows),
            P(rows, None),
            P(rows),
            P(rows, None),
            P(rows, None),
            P(rows, SEQ, None),
        ),
        out_specs=(
            P(rows, SEQ, None),
            P(rows, SEQ, None),
            P(rows),
            P(rows, None),
            P(rows),
            P(rows),
            P(rows, None),
            P(rows),
            P(rows, None),
            P(rows, None),
        ),
        check_vma=False,
    )
```

```python
import functools

import jax
import jax.numpy as jnp
from jax import lax
from jax.experimental import pallas as pl
from jax.experimental.pallas import tpu as pltpu
from jax.sharding import Mesh, PartitionSpec as P

HEADS = 12
HEAD = 64
EPSILON = 1e-06
BLOCK = 256
STEP = 512
MARK = 32.0
EXP2_FACTOR = HEAD**-0.5 * 1.4426950408889634
F32 = jnp.float32
BF16 = jnp.bfloat16
VMEM_LIMIT = 56 * 1024 * 1024

SEQ = ("zp", "zq")
COLUMN = ("core", "zp", "zq")
KEEP = [
    (core * 4 + z, (z // 2) * 4 + 2 * core + z % 2) for core in range(2) for z in range(4)
]
CROSS = [
    (core * 4 + z, (z // 2) * 4 + 2 * core + 1 - z % 2) for core in range(2) for z in range(4)
]


def swap(array, name, bit=1):
    count = lax.axis_size(name)
    return lax.ppermute(array, name, [(i, i ^ bit) for i in range(count)])


def pick(array, index, axis=0):
    return lax.dynamic_index_in_dim(array, index, axis, keepdims=False)


def group_ones(scale):
    row = lax.broadcasted_iota(jnp.int32, (128, 128), 0) // HEAD
    column = lax.broadcasted_iota(jnp.int32, (128, 128), 1) // HEAD
    return jnp.where(row == column, scale, 0.0).astype(BF16)


def group_sum(values, ones):
    return jnp.dot(values.astype(BF16), ones, preferred_element_type=F32)


def group_sum_fine(values, ones):
    high = values.astype(BF16)
    return group_sum(high, ones) + group_sum(values - high.astype(F32), ones)


def project_kernel(x_ref, gain_ref, weight_ref, qg_ref, kg_ref, normed_ref, q_ref, k_ref, v_ref, raw_ref):
    width = q_ref.shape[1]
    x = x_ref[...].astype(F32)
    center = x - jnp.mean(x, axis=-1, keepdims=True)
    spread = jnp.mean(center * center, axis=-1, keepdims=True)
    normed = (center * lax.rsqrt(spread + EPSILON) * gain_ref[...]).astype(BF16)
    normed_ref[...] = normed
    mixed = jnp.dot(normed, weight_ref[...], preferred_element_type=F32)
    raw_ref[...] = mixed[:, : 2 * width]
    ones = group_ones(1.0 / HEAD)
    for part, (out_ref, g_ref) in enumerate(((q_ref, qg_ref), (k_ref, kg_ref))):
        for at in range(0, width, 128):
            raw = mixed[:, part * width + at : part * width + at + 128]
            c = raw - group_sum_fine(raw, ones)
            n = c * lax.rsqrt(group_sum(c * c, ones) + EPSILON)
            out_ref[:, at : at + 128] = (n * g_ref[:, at : at + 128]).astype(BF16)
    v_ref[...] = mixed[:, 2 * width :].astype(BF16)


def project(x, gain, weight, query_gain, key_gain):
    tokens, model = x.shape
    width = weight.shape[1] // 3
    whole = lambda shape: pl.BlockSpec(shape, lambda i: (0, 0))
    rows = lambda columns: pl.BlockSpec((BLOCK, columns), lambda i: (i, 0))
    return pl.pallas_call(
        project_kernel,
        grid=(tokens // BLOCK,),
        in_specs=[
            rows(model),
            whole((1, model)),
            whole(weight.shape),
            whole((1, width)),
            whole((1, width)),
        ],
        out_specs=[rows(model), rows(width), rows(width), rows(width), rows(2 * width)],
        out_shape=[
            jax.ShapeDtypeStruct((tokens, model), BF16),
            jax.ShapeDtypeStruct((tokens, width), BF16),
            jax.ShapeDtypeStruct((tokens, width), BF16),
            jax.ShapeDtypeStruct((tokens, width), BF16),
            jax.ShapeDtypeStruct((tokens, 2 * width), F32),
        ],
        compiler_params=pltpu.CompilerParams(vmem_limit_bytes=VMEM_LIMIT),
        cost_estimate=pl.CostEstimate(
            flops=2 * tokens * model * 3 * width, bytes_accessed=tokens * model * 12, transcendentals=0
        ),
        name="project",
    )(x, gain, weight, query_gain, key_gain)


def nt(a, b):
    return lax.dot_general(a, b, (((1,), (1,)), ((), ())), preferred_element_type=F32)


def tn(a, b):
    return lax.dot_general(a, b, (((0,), (0,)), ((), ())), preferred_element_type=F32)


def slots(queries, length, part):
    at = lax.broadcasted_iota(jnp.int32, (queries, 128), 0)
    if queries == length:
        return at
    return at % part + part * (lax.axis_index("zq") + 2 * (at // part))


def own_rows(ref, start, count, queries, part):
    if queries == ref.shape[0]:
        return ref[pl.ds(start, count), :]
    zq = lax.axis_index("zq")
    pieces = [
        ref[pl.ds(pl.multiple_of((zq + 2 * i) * part, part), part), :]
        for i in range(start // part, (start + count) // part)
    ]
    return jnp.concatenate(pieces, axis=0)


def query_marks(bounds_ref, place, queries, length, part, pics):
    at = slots(queries, length, part)
    inside = (at >= bounds_ref[0:1, :]) & (at < bounds_ref[2:3, :])
    values = jnp.where(inside, MARK, 0.0)
    return jnp.where(place == pics, MARK, values).astype(BF16)


def key_marks(bounds_ref, place, length, pics):
    at = lax.broadcasted_iota(jnp.int32, (length, 128), 0)
    inside = (at >= bounds_ref[0:1, :]) & (at < bounds_ref[1:2, :])
    values = jnp.where(inside, MARK, 0.0)
    values = jnp.where(place == pics, -MARK, values)
    return jnp.where((place > pics) & (place < pics + 4), 1.0, values).astype(BF16)


def attend_kernel(pics, q_ref, k_ref, v_ref, bounds_ref, out_ref, aug_ref, kaug, vaug, qaug):
    length = k_ref.shape[0]
    queries = out_ref.shape[0]
    part = length // 4
    lane = lax.broadcasted_iota(jnp.int32, (1, 128), 1)
    place = lane % HEAD
    sides = [lane < HEAD, lane >= HEAD]
    kmarks = key_marks(bounds_ref, place, length, pics)
    qmarks = query_marks(bounds_ref, place, queries, length, part, pics)
    qaug[...] = qmarks
    for h in range(2):
        kaug[h] = jnp.where(sides[h], k_ref[...], kmarks)
        vaug[h] = jnp.where(sides[h], v_ref[...], jnp.ones_like(v_ref))
    for b in range(queries // STEP):
        rows = pl.ds(b * STEP, STEP)
        mine = own_rows(q_ref, b * STEP, STEP, queries, part)
        query = [jnp.where(sides[h], mine, qaug[rows, :]) for h in range(2)]
        total = [jnp.zeros((STEP, 128), F32)] * 2
        for j in range(length // STEP):
            keys = pl.ds(j * STEP, STEP)
            scores = [nt(query[h], kaug[h, keys, :]) for h in range(2)]
            weights = [jnp.exp2(x * EXP2_FACTOR).astype(BF16) for x in scores]
            total = [
                total[h] + jnp.dot(weights[h], vaug[h, keys, :], preferred_element_type=F32) for h in range(2)
            ]
        results = []
        for h in range(2):
            results.append(total[h] / pltpu.roll(total[h], HEAD, 1))
            log_total = jnp.log(jnp.where(sides[h], 1.0, total[h])) * -(HEAD**0.5)
            first = log_total.astype(BF16)
            rest = log_total - first.astype(F32)
            middle = rest.astype(BF16)
            last = (rest - middle.astype(F32)).astype(BF16)
            logs = jnp.where(place == pics + 1, first, jnp.where(place == pics + 2, middle, last))
            slot = jnp.logical_not(sides[h]) & (place > pics) & (place < pics + 4)
            aug_ref[h, rows, :] = jnp.where(slot, logs, query[h])
        out_ref[rows, :] = jnp.where(sides[0], results[0], results[1]).astype(BF16)


def attend(q, k, v, bounds, pics, queries):
    length, width = k.shape
    pairs = width // 128
    column = pl.BlockSpec((length, 128), lambda p: (0, p))
    return pl.pallas_call(
        functools.partial(attend_kernel, pics),
        grid=(pairs,),
        in_specs=[column, column, column, pl.BlockSpec((8, 128), lambda p: (0, 0))],
        out_specs=[
            pl.BlockSpec((queries, 128), lambda p: (0, p)),
            pl.BlockSpec((2, queries, 128), lambda p: (p, 0, 0)),
        ],
        scratch_shapes=[
            pltpu.VMEM((2, length, 128), BF16),
            pltpu.VMEM((2, length, 128), BF16),
            pltpu.VMEM((queries, 128), BF16),
        ],
        out_shape=[
            jax.ShapeDtypeStruct((queries, width), BF16),
            jax.ShapeDtypeStruct((2 * pairs, queries, 128), BF16),
        ],
        compiler_params=pltpu.CompilerParams(vmem_limit_bytes=VMEM_LIMIT),
        cost_estimate=pl.CostEstimate(
            flops=16 * length * queries * width, bytes_accessed=length * width * 12, transcendentals=0
        ),
        name="attend",
    )(q, k, v, bounds)


def head_norm_back(e, raw, gain, means):
    c = raw - group_sum_fine(raw, means)
    r = lax.rsqrt(group_sum(c * c, means) + EPSILON)
    n = c * r
    t = e * gain
    grad = r * (t - group_sum(t, means) - n * group_sum(t * n, means))
    return grad.astype(BF16), jnp.sum(e * n, axis=0, keepdims=True)


def attend_back_kernel(
    pics, aug_ref, k_ref, v_ref, out_ref, do_ref, rawq_ref, rawk_ref, qg_ref, kg_ref, bounds_ref,
    dq_ref, dk_ref, dv_ref, qgg_ref, kgg_ref, kaug, vaug, doaug, qsum, ksum,
):
    length = k_ref.shape[0]
    queries = do_ref.shape[0]
    part = length // 4
    whole = queries == length
    lane = lax.broadcasted_iota(jnp.int32, (1, 128), 1)
    place = lane % HEAD
    sides = [lane < HEAD, lane >= HEAD]
    kmarks = key_marks(bounds_ref, place, length, pics)
    vmarks = jnp.where(place < 2, 1.0, 0.0).astype(BF16)
    ones = group_ones(1.0)
    inner = group_sum_fine(do_ref[...].astype(F32) * out_ref[...].astype(F32), ones)
    inner = -pltpu.roll(inner, HEAD, 1)
    inner_high = inner.astype(BF16)
    inner_low = (inner - inner_high.astype(F32)).astype(BF16)
    zero = jnp.zeros((), BF16)
    gmarks = jnp.where(place == 0, inner_high, jnp.where(place == 1, inner_low, zero))
    for h in range(2):
        kaug[h] = jnp.where(sides[h], k_ref[...], kmarks)
        vaug[h] = jnp.where(sides[h], v_ref[...], vmarks)
        doaug[h] = jnp.where(sides[h], do_ref[...], gmarks)
    for b in range(length // STEP):
        keys = pl.ds(b * STEP, STEP)
        key = [kaug[h, keys, :] for h in range(2)]
        value = [vaug[h, keys, :] for h in range(2)]
        dk = [jnp.zeros((STEP, 128), F32)] * 2
        dv = [jnp.zeros((STEP, 128), F32)] * 2
        for j in range(queries // STEP):
            rows = pl.ds(j * STEP, STEP)
            query = [aug_ref[h, rows, :] for h in range(2)]
            grad = [doaug[h, rows, :] for h in range(2)]
            scores = [nt(key[h], query[h]) for h in range(2)]
            soft_grad = [nt(value[h], grad[h]) for h in range(2)]
            weights = [jnp.exp2(x * EXP2_FACTOR) for x in scores]
            score_grad = [(weights[h] * soft_grad[h]).astype(BF16) for h in range(2)]
            for h in range(2):
                part_sum = tn(score_grad[h], key[h])
                if b == 0:
                    qsum[h, rows, :] = part_sum
                else:
                    qsum[h, rows, :] += part_sum
                dk[h] = dk[h] + jnp.dot(score_grad[h], query[h], preferred_element_type=F32)
                dv[h] = dv[h] + jnp.dot(weights[h].astype(BF16), grad[h], preferred_element_type=F32)
        ksum[keys, :] = jnp.where(sides[0], dk[0], dk[1]) * HEAD**-0.5
        dv_ref[keys, :] = jnp.where(sides[0], dv[0], dv[1]).astype(BF16)

    means = group_ones(1.0 / HEAD)
    gain_sum = jnp.zeros((1, 128), F32)
    for b in range(queries // part):
        rows = pl.ds(b * part, part)
        e = jnp.where(sides[0], qsum[0, rows, :], qsum[1, rows, :]) * HEAD**-0.5
        raw = own_rows(rawq_ref, b * part, part, queries, part)
        dq_ref[rows, :], more = head_norm_back(e.astype(BF16).astype(F32), raw, qg_ref[...], means)
        gain_sum = gain_sum + more
    qgg_ref[...] = gain_sum
    gain_sum = jnp.zeros((1, 128), F32)
    for b in range(length // part):
        rows = pl.ds(b * part, part)
        e = ksum[rows, :].astype(BF16)
        if whole:
            dk_ref[rows, :], more = head_norm_back(e.astype(F32), rawk_ref[rows, :], kg_ref[...], means)
            gain_sum = gain_sum + more
        else:
            dk_ref[rows, :] = e
    kgg_ref[...] = gain_sum


def attend_back(aug, k, v, out, do, raw, query_gain, key_gain, bounds, pics):
    length, width = k.shape
    queries = do.shape[0]
    pairs = width // 128
    column = pl.BlockSpec((length, 128), lambda p: (0, p))
    own = pl.BlockSpec((queries, 128), lambda p: (0, p))
    gain = pl.BlockSpec((1, 128), lambda p: (0, p))
    return pl.pallas_call(
        functools.partial(attend_back_kernel, pics),
        grid=(pairs,),
        in_specs=[
            pl.BlockSpec((2, queries, 128), lambda p: (p, 0, 0)),
            column,
            column,
            own,
            own,
            column,
            pl.BlockSpec((length, 128), lambda p: (0, pairs + p)),
            gain,
            gain,
            pl.BlockSpec((8, 128), lambda p: (0, 0)),
        ],
        out_specs=[own, column, column, gain, gain],
        scratch_shapes=[
            pltpu.VMEM((2, length, 128), BF16),
            pltpu.VMEM((2, length, 128), BF16),
            pltpu.VMEM((2, queries, 128), BF16),
            pltpu.VMEM((2, queries, 128), F32),
            pltpu.VMEM((length, 128), F32),
        ],
        out_shape=[
            jax.ShapeDtypeStruct((queries, width), BF16),
            jax.ShapeDtypeStruct((length, width), BF16),
            jax.ShapeDtypeStruct((length, width), BF16),
            jax.ShapeDtypeStruct((1, width), F32),
            jax.ShapeDtypeStruct((1, width), F32),
        ],
        compiler_params=pltpu.CompilerParams(vmem_limit_bytes=VMEM_LIMIT),
        cost_estimate=pl.CostEstimate(
            flops=40 * length * queries * width, bytes_accessed=length * width * 20, transcendentals=0
        ),
        name="attend_back",
    )(aug, k, v, out, do, raw, raw, query_gain, key_gain, bounds)


def shared_keys_kernel(dk_ref, dv_ref, gotk_ref, gotv_ref, rawk_ref, kg_ref, outk_ref, outv_ref, kgg_ref):
    count = outk_ref.shape[0]
    part = count // 2
    means = group_ones(1.0 / HEAD)
    gain_sum = jnp.zeros((1, 128), F32)
    for b in range(2):
        rows = pl.ds(b * part, part)
        own = lambda ref: own_rows(ref, b * part, part, count, part)
        e = own(dk_ref).astype(F32) + gotk_ref[rows, :].astype(F32)
        outk_ref[rows, :], more = head_norm_back(e, own(rawk_ref), kg_ref[...], means)
        gain_sum = gain_sum + more
        outv_ref[rows, :] = (own(dv_ref).astype(F32) + gotv_ref[rows, :].astype(F32)).astype(BF16)
    kgg_ref[...] = gain_sum


def shared_keys(dk, dv, got_k, got_v, raw, key_gain):
    length, width = dk.shape
    pairs = width // 128
    column = pl.BlockSpec((length, 128), lambda p: (0, p))
    own = pl.BlockSpec((length // 2, 128), lambda p: (0, p))
    gain = pl.BlockSpec((1, 128), lambda p: (0, p))
    return pl.pallas_call(
        shared_keys_kernel,
        grid=(pairs,),
        in_specs=[column, column, own, own, pl.BlockSpec((length, 128), lambda p: (0, pairs + p)), gain],
        out_specs=[own, own, gain],
        out_shape=[
            jax.ShapeDtypeStruct((length // 2, width), BF16),
            jax.ShapeDtypeStruct((length // 2, width), BF16),
            jax.ShapeDtypeStruct((1, width), F32),
        ],
        compiler_params=pltpu.CompilerParams(vmem_limit_bytes=VMEM_LIMIT),
        name="shared_keys",
    )(dk, dv, got_k, got_v, raw, key_gain)


def gelu_pair(h):
    size = jnp.abs(h)
    bell = jnp.exp2(h * h * -0.7213475204444817)
    t = 1.0 / (1.0 + 0.23164189 * size)
    series = t * (0.127414796 + t * (-0.142248368 + t * (0.7107068705 + t * (-0.7265760135 + t * 0.5307027145))))
    tail = series * bell
    below = jnp.where(h < 0.0, tail, 1.0 - tail)
    return h * below, below + h * (bell * 0.3989422804014327)


def norm_parts(values):
    center = values - jnp.mean(values, axis=-1, keepdims=True)
    spread = lax.rsqrt(jnp.mean(center * center, axis=-1, keepdims=True) + EPSILON)
    return center * spread, spread


def norm_back(upstream, n, r, gain):
    t = upstream * gain
    grad = r * (t - jnp.mean(t, axis=-1, keepdims=True) - n * jnp.mean(t * n, axis=-1, keepdims=True))
    return grad, jnp.sum(upstream * n, axis=0, keepdims=True)


MESH_ID = pl.DeviceIdType.MESH


def here():
    return lax.axis_index("chip"), lax.axis_index("core"), lax.axis_index("zp"), lax.axis_index("zq")


def remote(source, target, sems, at, device):
    sent, got = sems
    return pltpu.make_async_remote_copy(
        src_ref=source, dst_ref=target, send_sem=sent.at[at], recv_sem=got.at[at],
        device_id=device, device_id_type=MESH_ID,
    )


def greet(devices, maybe=None, moves=None):
    barrier = pltpu.get_barrier_semaphore()
    for device in devices:
        pl.semaphore_signal(barrier, inc=1, device_id=device, device_id_type=MESH_ID)
    if maybe is None:
        pl.semaphore_wait(barrier, len(devices))
        return

    @pl.when(moves)
    def _():
        pl.semaphore_signal(barrier, inc=1, device_id=maybe, device_id_type=MESH_ID)

    pl.semaphore_wait(barrier, len(devices) + jnp.where(moves, 1, 0))


def rows_at(start, count):
    return pl.ds(pl.multiple_of(start, 16), count)


def write_bounds(pics, lens_ref, bounds_ref, zp, zq, length):
    lane = lax.broadcasted_iota(jnp.int32, (8, 128), 1)
    lens = jnp.where(zp == 0, lens_ref[0], lens_ref[1])
    ends = lens
    for hop in (1, 2, 4, 8):
        ends = ends + jnp.where(lane >= hop, pltpu.roll(ends, hop, 1), 0)
    starts = ends - lens
    last = (lens > 0) & (pltpu.roll(lens, 127, 1) == 0)
    query_ends = jnp.where(last, length, ends)
    total = jnp.max(jnp.where(lane < pics, ends, 0), axis=1, keepdims=True)

    def both(values):
        values = jnp.where(lane < HEAD, jnp.where(lane < pics, values, 2 * length), 0)
        return values + pltpu.roll(values, HEAD, 1)

    tables = [both(starts), both(ends), both(query_ends), jnp.broadcast_to(total, (8, 128))]
    for t in range(4):
        table = tables[t]
        bounds_ref[0, t : t + 1, :] = jnp.where(zq == 0, table[0:1], table[1:2])
        bounds_ref[1, t : t + 1, :] = table[2:3]
    bounds_ref[:, 4:, :] = jnp.zeros((2, 4, 128), jnp.int32)


def gather_kernel(
    with_mix, pics, tokens_ref, lens_ref, mix_ref, gains_ref,
    row_ref, shared_ref, bounds_ref, mix_out, first_ref, second_ref, query_ref, key_ref,
    lens_out, gains_out, sent, got, local_sem,
):
    chip, core, zp, zq = here()
    z = 2 * zp + zq
    part = tokens_ref.shape[1]
    sems = (sent, got)
    partner = (chip, 1 - core, zp, zq)
    side = (chip, core, zp, 1 - zq)
    keep = (chip, zp, core, zq)
    cross = (chip, zp, core, 1 - zq)
    moves = core != zp
    near_x = (chip ^ 1, core, zp, zq)
    near_y = (chip ^ 2, core, zp, zq)
    greet([partner, side, cross] + ([near_x, near_y] if with_mix else []), keep, moves)

    def quarter(ref, index):
        return ref.at[rows_at(index * part, part)]

    own_row = remote(tokens_ref.at[zq], quarter(row_ref, z), sems, 0, keep)
    own_shared = remote(tokens_ref.at[2], quarter(shared_ref, z), sems, 2, keep)
    stay_row = pltpu.make_async_copy(tokens_ref.at[zq], quarter(row_ref, z), local_sem.at[0])
    stay_shared = pltpu.make_async_copy(tokens_ref.at[2], quarter(shared_ref, z), local_sem.at[1])

    @pl.when(moves)
    def _():
        own_row.start()

    @pl.when(jnp.logical_not(moves))
    def _():
        stay_row.start()

    cross_row = remote(tokens_ref.at[1 - zq], quarter(row_ref, z), sems, 1, cross)
    cross_row.start()

    @pl.when(moves)
    def _():
        own_shared.start()

    @pl.when(jnp.logical_not(moves))
    def _():
        stay_shared.start()

    lens_copy = remote(lens_ref, lens_out.at[core], sems, 8, partner)
    lens_copy.start()
    lens_stay = pltpu.make_async_copy(lens_ref, lens_out.at[core], local_sem.at[2])
    lens_stay.start()
    if with_mix:
        shard = mix_ref.shape[1]

        def piece(index):
            return mix_out.at[rows_at(index * shard, shard)]

        mine, theirs = 2 * chip + core, 2 * chip + 1 - core
        x_mine, y_other = 2 * (chip ^ 1) + core, 2 * (chip ^ 2) + 1 - core

        def move(source, gain_source, index, at, device):
            copies = (
                remote(source, piece(index), sems, 9 + 2 * at, device),
                remote(gain_source, gains_out.at[index], sems, 10 + 2 * at, device),
            )
            for copy in copies:
                copy.start()
            return copies

        def arrived(copies):
            for copy in copies:
                copy.wait_recv()

        to_core = move(mix_ref.at[1 - core], gains_ref, mine, 0, partner)
        a_x = move(mix_ref.at[core], gains_ref, mine, 1, near_x)
        a_y = move(mix_ref.at[core], gains_ref, mine, 2, near_y)
        mix_stay = pltpu.make_async_copy(mix_ref.at[core], piece(mine), local_sem.at[3])
        mix_stay.start()
        gain_stay = pltpu.make_async_copy(gains_ref, gains_out.at[mine], local_sem.at[4])
        gain_stay.start()
        arrived(to_core)
        b_x = move(piece(theirs), gains_out.at[theirs], theirs, 3, near_x)
        b_y = move(piece(theirs), gains_out.at[theirs], theirs, 4, near_y)
        arrived(a_x)
        a_far = move(piece(x_mine), gains_out.at[x_mine], x_mine, 5, near_y)
        arrived(b_y)
        b_far = move(piece(y_other), gains_out.at[y_other], y_other, 6, near_x)

    lens_copy.wait()
    lens_stay.wait()
    write_bounds(pics, lens_out, bounds_ref, zp, zq, 4 * part)

    @pl.when(moves)
    def _():
        own_row.wait_recv()

    @pl.when(jnp.logical_not(moves))
    def _():
        stay_row.wait()

    first, second = 2 * core + zq, 2 * core + 1 - zq
    row_one = remote(quarter(row_ref, first), quarter(row_ref, first), sems, 3, partner)
    row_one.start()
    cross_row.wait_recv()
    row_two = remote(quarter(row_ref, second), quarter(row_ref, second), sems, 4, partner)
    row_two.start()

    @pl.when(moves)
    def _():
        own_shared.wait_recv()

    @pl.when(jnp.logical_not(moves))
    def _():
        stay_shared.wait()

    to_side = remote(quarter(shared_ref, first), quarter(shared_ref, first), sems, 5, side)
    to_side.start()
    shared_one = remote(quarter(shared_ref, first), quarter(shared_ref, first), sems, 6, partner)
    shared_one.start()
    to_side.wait_recv()
    shared_two = remote(quarter(shared_ref, second), quarter(shared_ref, second), sems, 7, partner)
    shared_two.start()

    if with_mix:
        mix_stay.wait()
        gain_stay.wait()
        for copies in (a_y, b_x, a_far, b_far):
            arrived(copies)
        for p in range(gains_out.shape[0]):
            lanes = slice(p * shard, (p + 1) * shard)
            values = gains_out[p, :, :shard].astype(F32)
            first_ref[:, lanes] = values[0:1]
            second_ref[:, lanes] = values[3:4]
            half_pieces = gains_out.shape[0] // 2

            @pl.when(core == p // half_pieces)
            def _():
                at = (p % half_pieces) * shard
                query_ref[:, at : at + shard] = values[1:2]
                key_ref[:, at : at + shard] = values[2:3]
        for copies in (to_core, a_x, a_y, b_x, b_y, a_far, b_far):
            for copy in copies:
                copy.wait_send()
    for copy in (row_one, row_two, shared_one, shared_two):
        copy.wait()
    to_side.wait_send()
    cross_row.wait_send()

    @pl.when(moves)
    def _():
        own_row.wait_send()
        own_shared.wait_send()


def gather_rows(tokens, lens, mix, gains, with_mix, pics):
    _, part, model = tokens.shape
    pieces = mix.shape[1] * 8
    here_space = pl.BlockSpec(memory_space=pltpu.VMEM)
    return pl.pallas_call(
        functools.partial(gather_kernel, with_mix, pics),
        in_specs=[here_space] * 4,
        out_specs=[here_space] * 8,
        out_shape=[
            jax.ShapeDtypeStruct((4 * part, model), BF16),
            jax.ShapeDtypeStruct((4 * part, model), BF16),
            jax.ShapeDtypeStruct((2, 8, 128), jnp.int32),
            jax.ShapeDtypeStruct((pieces, mix.shape[2]), BF16),
            jax.ShapeDtypeStruct((1, model), F32),
            jax.ShapeDtypeStruct((1, model), F32),
            jax.ShapeDtypeStruct((1, model // 2), F32),
            jax.ShapeDtypeStruct((1, model // 2), F32),
        ],
        scratch_shapes=[
            pltpu.VMEM((2,) + lens.shape, jnp.int32),
            pltpu.VMEM((8,) + gains.shape, BF16),
            pltpu.SemaphoreType.DMA((23,)),
            pltpu.SemaphoreType.DMA((23,)),
            pltpu.SemaphoreType.DMA((5,)),
        ],
        compiler_params=pltpu.CompilerParams(
            collective_id=0, has_side_effects=True, vmem_limit_bytes=VMEM_LIMIT
        ),
        name="gather_rows",
    )(tokens, lens, mix, gains)


def dense_kernel(
    square, out_ref, shared_ref, row_tokens, shared_tokens, keep_ref, cross_ref, third_ref, outw_ref, gain_ref,
    bounds_ref, up_ref, down_ref,
    out_keep, out_cross, out_third, midg_ref, row_grad, shared_grad, packed, gaing_ref,
    x, att_other, second, grad, hidden_all, pre_all, forward, backward, middle, ups, downs,
    parts_out, parts_in, heads_out, cols_out, cols_in, sent, got, local_sem, tile_sem,
):
    chip, core, zp, zq = here()
    sems = (sent, got)
    partner = (chip, 1 - core, zp, zq)
    tokens, model = midg_ref.shape
    part = tokens // 3
    half = 2 * part
    width = out_ref.shape[1]
    tile = ups.shape[2]
    other = 1 - core
    mine, theirs = pl.ds(0, tokens), pl.ds(tokens, tokens)

    for i in range(4):
        column = (2 * i + core if square else 4 * core + i) * tile
        pltpu.make_async_copy(
            up_ref.at[:, pl.ds(pl.multiple_of(column, 128), tile)], ups.at[i], tile_sem.at[0, i]
        ).start()
        pltpu.make_async_copy(down_ref.at[pl.ds(i * tile, tile)], downs.at[i], tile_sem.at[1, i]).start()
    loads = [
        pltpu.make_async_copy(row_tokens.at[rows_at(core * half, half)], x.at[pl.ds(0, half)], local_sem.at[0]),
        pltpu.make_async_copy(
            shared_tokens.at[rows_at((2 * core + zq) * part, part)], x.at[pl.ds(half, part)], local_sem.at[1]
        ),
    ]
    for copy in loads:
        copy.start()
    greet([partner])
    att_sends = [
        remote(out_ref.at[rows_at(other * half, half)], att_other.at[pl.ds(0, half)], sems, 0, partner),
        remote(shared_ref.at[rows_at(other * part, part)], att_other.at[pl.ds(half, part)], sems, 1, partner),
    ]
    for copy in att_sends:
        copy.start()

    slot = lax.broadcasted_iota(jnp.int32, (part, 1), 0)
    filled, shared_filled = bounds_ref[0, 3:4, 0:1], bounds_ref[1, 3:4, 0:1]
    none = jnp.zeros((), BF16)
    for source, at, start, limit in (
        (keep_ref, zq * part, (2 * core + zq) * part, filled),
        (cross_ref, (1 - zq) * part, (2 * core + 1 - zq) * part, filled),
        (third_ref, half, (2 * core + zq) * part, shared_filled),
    ):
        grad[rows_at(at, part), :] = jnp.where(slot + start < limit, source[...], none)
    grad_send = remote(grad.at[mine], grad.at[theirs], sems, 2, partner)
    grad_send.start()

    for copy in loads:
        copy.wait()
    own_rows_of = lambda b: (
        out_ref[rows_at(core * half + b * part, part), :] if b < 2 else shared_ref[rows_at(core * part, part), :]
    )
    own_weight = outw_ref[rows_at(core * width, width), :]
    other_weight = outw_ref[rows_at(other * width, width), :]
    blocks = [pl.ds(b * part, part) for b in range(3)]
    for b in range(3):
        middle[blocks[b], :] = x[blocks[b], :].astype(F32) + jnp.dot(
            own_rows_of(b), own_weight, preferred_element_type=F32
        )
    for copy in att_sends:
        copy.wait_recv()
    for rows in blocks:
        value = middle[rows, :] + jnp.dot(att_other[rows, :], other_weight, preferred_element_type=F32)
        middle[rows, :] = value
        second[rows, :] = (norm_parts(value)[0] * gain_ref[...]).astype(BF16)
    second_send = remote(second.at[mine], second.at[theirs], sems, 3, partner)
    second_send.start()
    forward[...] = jnp.zeros_like(forward)
    backward[...] = jnp.zeros_like(backward)
    second_send.wait_recv()
    grad_send.wait_recv()

    def one_tile(i, _):
        pltpu.make_async_copy(up_ref.at[:, pl.ds(0, tile)], ups.at[i], tile_sem.at[0, i]).wait()
        pltpu.make_async_copy(down_ref.at[pl.ds(0, tile)], downs.at[i], tile_sem.at[1, i]).wait()
        up, down = ups[i], downs[i]
        for rows in (mine, theirs):
            pre = jnp.dot(second[rows, :], up, preferred_element_type=F32)
            hidden, slope = gelu_pair(pre)
            hidden = hidden.astype(BF16)
            hidden_all[rows, :] = hidden
            forward[rows, :] += jnp.dot(hidden, down, preferred_element_type=F32)
            pre_grad = (nt(grad[rows, :], down) * slope).astype(BF16)
            pre_all[rows, :] = pre_grad
            backward[rows, :] += nt(pre_grad, up)
        packed[i, pl.ds(0, tile), :] = tn(hidden_all[...], grad[...]).astype(BF16)
        up_grad = tn(second[...], pre_all[...]).astype(BF16)
        quarter = model // 4
        for c in range(4):
            place = (rows_at(tile + (i // 2) * quarter, quarter), pl.ds(pl.multiple_of((i % 2) * tile, 128), tile))
            packed[c, place[0], place[1]] = up_grad[c * quarter : (c + 1) * quarter, :]
        return 0

    lax.fori_loop(0, 4, one_tile, 0)

    parts_out[0] = forward[theirs, :].astype(BF16)
    first_part = remote(parts_out.at[0], parts_in.at[0], sems, 4, partner)
    first_part.start()
    parts_out[1] = backward[theirs, :].astype(BF16)
    second_part = remote(parts_out.at[1], parts_in.at[1], sems, 5, partner)
    second_part.start()
    second_send.wait_send()
    first_part.wait_recv()
    for rows in blocks:
        value = middle[rows, :] + forward[rows, :] + parts_in[0, rows, :].astype(F32)
        forward[rows, :] = value
    out_keep[...] = forward[rows_at(zq * part, part), :].astype(BF16)
    out_cross[...] = forward[rows_at((1 - zq) * part, part), :].astype(BF16)
    out_third[...] = forward[pl.ds(half, part), :].astype(BF16)
    second_part.wait_recv()
    gain_sum = jnp.zeros(gaing_ref.shape, F32)
    for b in range(3):
        rows = blocks[b]
        n, r = norm_parts(middle[rows, :])
        upstream = backward[rows, :] + parts_in[1, rows, :].astype(F32)
        more, gain_more = norm_back(upstream, n, r, gain_ref[...])
        gain_sum = gain_sum + gain_more
        value = grad[rows, :].astype(F32) + more
        midg_ref[rows, :] = value
        branch = value.astype(BF16)
        second[rows, :] = branch
        heads_out[rows, :] = nt(branch, other_weight).astype(BF16)
    gaing_ref[...] = gain_sum
    head_sends = [
        remote(heads_out.at[pl.ds(0, half)], row_grad.at[rows_at(core * half, half)], sems, 6, partner),
        remote(heads_out.at[pl.ds(half, part)], shared_grad.at[rows_at(core * part, part)], sems, 7, partner),
    ]
    for copy in head_sends:
        copy.start()
    branch = second[mine, :]
    out_grads = [
        tn(out_ref[rows_at(core * half, half), :], second[pl.ds(0, half), :])
        + tn(shared_ref[rows_at(core * part, part), :], second[pl.ds(half, part), :]),
        tn(att_other[...], branch),
    ]
    for turn, heads in ((0, core), (1, other)):
        rows = rows_at(heads * width, width)
        forward[rows, :] = out_grads[turn]
    lanes = lambda side: pl.ds(pl.multiple_of(side * width, 128), width)
    cols_out[...] = forward[pl.ds(0, model), lanes(other)].astype(BF16)
    cols_send = remote(cols_out, cols_in, sems, 8, partner)
    cols_send.start()
    for b in range(3):
        value = nt(second[blocks[b], :], own_weight).astype(BF16)
        if b < 2:
            row_grad[rows_at(core * half + b * part, part), :] = value
        else:
            shared_grad[rows_at(core * part, part), :] = value
    cols_send.wait_recv()
    total = (forward[pl.ds(0, model), lanes(core)] + cols_in[...].astype(F32)).astype(BF16)
    eighth = model // 8
    for c in range(4):
        for h in range(2):
            at = (2 * c + h) * eighth
            packed[c, pl.ds(2 * tile, eighth), h * width : (h + 1) * width] = total[at : at + eighth, :]
    for copy in head_sends:
        copy.wait_recv()
    for copy in att_sends + head_sends + [grad_send, first_part, second_part, cols_send]:
        copy.wait_send()


def dense(square, out, shared_out, row_tokens, shared_tokens, grads, out_matrix, gain, bounds, up, down):
    model = row_tokens.shape[1]
    part = grads[0].shape[0]
    tokens = 3 * part
    length, width = out.shape
    hidden = down.shape[0]
    tile = hidden // 4
    anywhere = pl.BlockSpec(memory_space=pl.ANY)
    near = pl.BlockSpec(memory_space=pltpu.VMEM)
    both = 2 * tokens
    return pl.pallas_call(
        functools.partial(dense_kernel, square),
        in_specs=[near, near, anywhere, anywhere, near, near, near, near, near, near, anywhere, anywhere],
        out_specs=[near] * 8,
        out_shape=[
            jax.ShapeDtypeStruct((part, model), BF16),
            jax.ShapeDtypeStruct((part, model), BF16),
            jax.ShapeDtypeStruct((part, model), BF16),
            jax.ShapeDtypeStruct((tokens, model), F32),
            jax.ShapeDtypeStruct((length, width), BF16),
            jax.ShapeDtypeStruct((length // 2, width), BF16),
            jax.ShapeDtypeStruct((4, 2 * tile + model // 8, model), BF16),
            jax.ShapeDtypeStruct((1, model), F32),
        ],
        scratch_shapes=[
            pltpu.VMEM((tokens, model), BF16),
            pltpu.VMEM((tokens, width), BF16),
            pltpu.VMEM((both, model), BF16),
            pltpu.VMEM((both, model), BF16),
            pltpu.VMEM((both, tile), BF16),
            pltpu.VMEM((both, tile), BF16),
            pltpu.VMEM((both, model), F32),
            pltpu.VMEM((both, model), F32),
            pltpu.VMEM((tokens, model), F32),
            pltpu.VMEM((4, model, tile), BF16),
            pltpu.VMEM((4, tile, model), BF16),
            pltpu.VMEM((2, tokens, model), BF16),
            pltpu.VMEM((2, tokens, model), BF16),
            pltpu.VMEM((tokens, width), BF16),
            pltpu.VMEM((model, width), BF16),
            pltpu.VMEM((model, width), BF16),
            pltpu.SemaphoreType.DMA((9,)),
            pltpu.SemaphoreType.DMA((9,)),
            pltpu.SemaphoreType.DMA((2,)),
            pltpu.SemaphoreType.DMA((2, 4)),
        ],
        compiler_params=pltpu.CompilerParams(
            collective_id=1, has_side_effects=True, vmem_limit_bytes=60 * 1024 * 1024
        ),
        cost_estimate=pl.CostEstimate(
            flops=32 * tokens * model * hidden, bytes_accessed=16 * model * hidden, transcendentals=0
        ),
        name="dense",
    )(out, shared_out, row_tokens, shared_tokens, *grads, out_matrix, gain, bounds, up, down)


def finish_kernel(
    grad_ref, mix_ref, out_ref, total_ref, gains_ref,
    relay, final, core_got, chunks, gain_parts, chunk_got, gain_got, sent, got, local_sem,
):
    chip, core, zp, zq = here()
    z = 2 * zp + zq
    sems = (sent, got)
    part = out_ref.shape[1]
    shard = mix_ref.shape[1] - 16
    quarter = shard // 2
    columns = mix_ref.shape[2]
    partner = (chip, 1 - core, zp, zq)
    keep = (chip, zp, core, zq)
    cross = (chip, zp, core, 1 - zq)
    moves = core != zp
    near_x = (chip ^ 1, core, zp, zq)
    near_y = (chip ^ 2, core, zp, zq)
    along = [(chip, core, zp, 1 - zq), (chip, core, 1 - zp, zq), (chip, core, 1 - zp, 1 - zq)]
    greet([partner, cross, near_x, near_y] + along, keep, moves)

    mine, theirs = 2 * chip + core, 2 * chip + 1 - core
    x_mine, x_other = 2 * (chip ^ 1) + core, 2 * (chip ^ 1) + 1 - core
    y_mine, y_other = 2 * (chip ^ 2) + core, 2 * (chip ^ 2) + 1 - core
    far_mine, far_other = 2 * (chip ^ 3) + core, 2 * (chip ^ 3) + 1 - core
    first = remote(mix_ref.at[far_mine], relay.at[0], sems, 0, near_y)
    second = remote(mix_ref.at[far_other], relay.at[1], sems, 1, near_x)
    first.start()
    second.start()
    direct_x = remote(mix_ref.at[x_other], final.at[0], sems, 2, near_x)
    direct_y = remote(mix_ref.at[y_mine], final.at[1], sems, 3, near_y)
    direct_x.start()
    direct_y.start()

    own = pl.ds(pl.multiple_of(zq * part, 16), part)
    own_row = remote(grad_ref.at[own], out_ref.at[zq], sems, 4, keep)
    own_shared = remote(grad_ref.at[pl.ds(2 * part, part)], out_ref.at[2], sems, 5, keep)
    stay_row = pltpu.make_async_copy(grad_ref.at[own], out_ref.at[zq], local_sem.at[0])
    stay_shared = pltpu.make_async_copy(grad_ref.at[pl.ds(2 * part, part)], out_ref.at[2], local_sem.at[1])

    @pl.when(moves)
    def _():
        own_row.start()
        own_shared.start()

    @pl.when(jnp.logical_not(moves))
    def _():
        stay_row.start()
        stay_shared.start()

    cross_row = remote(grad_ref.at[rows_at((1 - zq) * part, part)], out_ref.at[zq], sems, 6, cross)
    cross_row.start()

    def add(*terms):
        total = terms[0].astype(F32)
        for term in terms[1:]:
            total = total + term.astype(F32)
        return total

    first.wait_recv()
    relay[2] = add(relay[0], mix_ref[x_mine]).astype(BF16)
    onward_x = remote(relay.at[2], final.at[2], sems, 7, near_x)
    onward_x.start()
    second.wait_recv()
    relay[3] = add(relay[1], mix_ref[y_other]).astype(BF16)
    onward_y = remote(relay.at[3], final.at[3], sems, 8, near_y)
    onward_y.start()
    direct_x.wait_recv()
    onward_y.wait_recv()
    relay[4] = add(mix_ref[theirs], final[0], final[3]).astype(BF16)
    to_core = remote(relay.at[4], core_got, sems, 9, partner)
    to_core.start()
    direct_y.wait_recv()
    onward_x.wait_recv()
    kept = add(mix_ref[mine], final[1], final[2])
    for i in range(2):
        chunks[2 * core + i] = kept[i * quarter : (i + 1) * quarter].astype(BF16)
    to_core.wait_recv()
    for i in range(2):
        chunks[2 * (1 - core) + i] = core_got[i * quarter : (i + 1) * quarter]
    gain_parts[0] = (kept[shard:] + core_got[shard:].astype(F32)).astype(BF16)
    hops = [z ^ 1, z ^ 2, z ^ 3]
    copies = []
    for i in range(3):
        copies.append(remote(chunks.at[hops[i]], chunk_got.at[i], sems, 10 + i, along[i]))
        copies.append(remote(gain_parts.at[0], gain_got.at[i], sems, 13 + i, along[i]))
    for copy in copies:
        copy.start()
    for copy in copies:
        copy.wait_recv()
    gains_ref[...] = add(gain_parts[0], gain_got[0], gain_got[1], gain_got[2])
    chunk_got[3] = add(chunks[z], chunk_got[0], chunk_got[1], chunk_got[2]).astype(BF16)
    spread = [remote(chunk_got.at[3], chunk_got.at[4 + i], sems, 16 + i, along[i]) for i in range(3)]
    for copy in spread:
        copy.start()

    def place(index, values):
        half, up = index // 2, index % 2
        third = columns // 3
        values = values.astype(F32)
        for h in range(2):
            for u in range(2):

                @pl.when((half == h) & (up == u))
                def _():
                    for p in range(3):
                        total_ref[u * quarter : (u + 1) * quarter, (2 * p + h) * third : (2 * p + h + 1) * third] = (
                            values[:, p * third : (p + 1) * third]
                        )

    place(z, chunk_got[3])
    for i in range(3):
        spread[i].wait_recv()
        place(hops[i], chunk_got[4 + i])
    for copy in copies + spread + [first, second, direct_x, direct_y, onward_x, onward_y, to_core]:
        copy.wait_send()
    cross_row.wait()

    @pl.when(moves)
    def _():
        own_row.wait()
        own_shared.wait()

    @pl.when(jnp.logical_not(moves))
    def _():
        stay_row.wait()
        stay_shared.wait()


def finish(grad, mix):
    tokens, model = grad.shape
    _, rows, columns = mix.shape
    shard = rows - 16
    local_space = pl.BlockSpec(memory_space=pltpu.VMEM)
    buffers = lambda count, size: pltpu.VMEM((count, size, columns), BF16)
    return pl.pallas_call(
        finish_kernel,
        in_specs=[local_space, local_space],
        out_specs=[local_space, local_space, local_space],
        out_shape=[
            jax.ShapeDtypeStruct((3, tokens // 3, model), BF16),
            jax.ShapeDtypeStruct((shard, 2 * columns), F32),
            jax.ShapeDtypeStruct((16, columns), F32),
        ],
        scratch_shapes=[
            buffers(5, rows),
            buffers(4, rows),
            pltpu.VMEM((rows, columns), BF16),
            buffers(4, shard // 2),
            buffers(1, 16),
            buffers(7, shard // 2),
            buffers(3, 16),
            pltpu.SemaphoreType.DMA((19,)),
            pltpu.SemaphoreType.DMA((19,)),
            pltpu.SemaphoreType.DMA((2,)),
        ],
        compiler_params=pltpu.CompilerParams(
            collective_id=3, has_side_effects=True, vmem_limit_bytes=VMEM_LIMIT
        ),
        name="finish",
    )(grad, mix)


def local(
    tokens, lengths, pictures, first_gain, mix_weight, query_gain, key_gain, out_weight,
    second_gain, up_weight, down_weight, cotangent,
):
    chip, core, zp, zq = here()
    chips = lax.axis_size("chip")
    square = chips == 4
    rows = ("chip", "core")
    _, part, model = tokens.shape
    length = 4 * part
    half = 2 * part
    width = HEADS // 2 * HEAD
    pics = lengths.shape[1]
    shard = mix_weight.shape[0]

    gains = jnp.stack([first_gain, query_gain, key_gain, second_gain])
    gains = jnp.pad(gains, ((0, 12), (0, 128 - shard)))
    mix_split = mix_weight.reshape(shard, 3, 2, width).transpose(2, 0, 1, 3).reshape(2, shard, 3 * width)
    lens = jnp.pad(lengths, ((0, 5), (0, 128 - pics)))
    row_tokens, shared_tokens, bounds, mix_half, gain_first, gain_second, gain_query, gain_key = gather_rows(
        tokens, lens, mix_split, gains, square, pics
    )
    if not square:
        whole = lax.all_gather(mix_weight, rows, axis=0, tiled=True)
        mix_half = pick(whole.reshape(model, 3, 2, width), core, 2).reshape(model, 3 * width)
        gains = lax.all_gather(gains, rows, axis=0, tiled=False)
        gains = gains[:, :4, :shard].transpose(1, 0, 2).reshape(4, 1, model).astype(F32)
        gain_first, gain_second = gains[0], gains[3]
        gain_query = pick(gains[1].reshape(2, 1, width), core)
        gain_key = pick(gains[2].reshape(2, 1, width), core)
    out_matrix = lax.all_gather(out_weight, rows, axis=0, tiled=True)
    up_matrix = lax.all_gather(up_weight, rows, axis=0, tiled=True)
    if square:
        down_half = lax.all_gather(down_weight, "chip", axis=0, tiled=True)
    else:
        down_half = lax.all_gather(down_weight, rows, axis=0, tiled=True)
        down_half = pick(down_half.reshape(2, -1, model), core)

    def spread(array):
        mine = lax.ppermute(pick(array, zq), COLUMN, KEEP)
        cross = lax.ppermute(pick(array, 1 - zq), COLUMN, CROSS)
        return mine, cross, lax.ppermute(array[2], COLUMN, KEEP)

    def collect(mine, cross, third):
        mine = lax.ppermute(mine, COLUMN, KEEP)
        cross = lax.ppermute(cross, COLUMN, CROSS)
        third = lax.ppermute(third, COLUMN, KEEP)
        return jnp.stack([jnp.where(zq == 0, mine, cross), jnp.where(zq == 0, cross, mine), third])

    cotangent, row_tokens = lax.optimization_barrier((cotangent, row_tokens))
    grads = spread(cotangent)

    normed, q, k, v, raw = project(row_tokens, gain_first, mix_half, gain_query, gain_key)
    out, aug = attend(q, k, v, bounds[0], pics, length)
    shared_normed, shared_q, shared_k, shared_v, shared_raw = project(
        shared_tokens, gain_first, mix_half, gain_query, gain_key
    )
    shared_out, shared_aug = attend(shared_q, shared_k, shared_v, bounds[1], pics, half)

    out_keep, out_cross, out_third, middle_grad, grad, shared_grad, packed, second_gain_grad = dense(
        square, out, shared_out, row_tokens, shared_tokens, grads, out_matrix, gain_second, bounds,
        up_matrix, down_half,
    )
    output = collect(out_keep, out_cross, out_third)

    def reduce(grad):
        return lax.psum(lax.psum_scatter(grad, rows, scatter_dimension=0, tiled=True), SEQ).astype(F32)

    hidden = up_weight.shape[1]
    tile = hidden // 8
    eighth = model // 8
    if square:
        size = packed.shape[1]
        mine = lax.psum_scatter(packed.reshape(4 * size, model), "chip", scatter_dimension=0, tiled=True)
        mine = lax.psum(mine, SEQ)
        down_out = mine[:tile].astype(F32)
        up_mine = mine[tile : 2 * tile].reshape(2, 2, shard, 2, tile).transpose(1, 2, 0, 3, 4)
        up_mine = up_mine.reshape(2, shard, 4, tile)
        outw_mine = mine[2 * tile :].reshape(shard, 2, width).transpose(1, 0, 2)
        up_other = swap(pick(up_mine, 1 - core).reshape(shard, 4 * tile), "core").reshape(shard, 4, tile)
        outw_other = swap(pick(outw_mine, 1 - core), "core")
        up_mine, outw_mine = pick(up_mine, core), pick(outw_mine, core)
        low = jnp.where(core == 0, up_mine, up_other)
        high = jnp.where(core == 0, up_other, up_mine)
        up_out = jnp.stack([low, high], axis=2).reshape(shard, hidden).astype(F32)
        low = jnp.where(core == 0, outw_mine, outw_other)
        high = jnp.where(core == 0, outw_other, outw_mine)
        outw_out = jnp.concatenate([low, high], axis=1).astype(F32)
    else:
        own_core = jnp.arange(2) == core
        down_grad = packed[:, :tile].reshape(1, 4 * tile, model)
        down_out = reduce(jnp.where(own_core[:, None, None], down_grad, 0).reshape(hidden, model))
        up_grad = packed[:, tile : 2 * tile].reshape(4, 2, 2 * eighth, 2, tile).transpose(0, 2, 1, 3, 4)
        up_grad = up_grad.reshape(model, 1, 4 * tile)
        up_out = reduce(jnp.where(own_core[None, :, None], up_grad, 0).reshape(model, hidden))
        out_grad = packed[:, 2 * tile :].reshape(4, eighth, 2, width).transpose(0, 2, 1, 3)
        out_grad = out_grad.reshape(model, 1, width)
        outw_out = reduce(jnp.where(own_core[None, :, None], out_grad, 0).reshape(model, model))

    shared_dq, part_k, part_v, shared_qgg, _ = attend_back(
        shared_aug, shared_k, shared_v, shared_out, shared_grad, shared_raw, gain_query, gain_key,
        bounds[1], pics,
    )

    def to_side(array):
        return swap(pick(array.reshape(2, 2, part, width), 1 - zq, 1), "zq").reshape(half, width)

    got_k, got_v = to_side(part_k), to_side(part_v)
    dq, dk, dv, qgg, kgg = attend_back(
        aug, k, v, out, grad, raw, gain_query, gain_key, bounds[0], pics
    )
    shared_dk, shared_dv, shared_kgg = shared_keys(part_k, part_v, got_k, got_v, shared_raw, gain_key)
    mixed = jnp.concatenate(
        [jnp.concatenate([dq, shared_dq]), jnp.concatenate([dk, shared_dk]), jnp.concatenate([dv, shared_dv])],
        axis=1,
    )
    own_shared = pick(shared_normed.reshape(2, 2, part, model), zq, 1).reshape(half, model)
    mix_grad = tn(jnp.concatenate([normed, own_shared]), mixed).astype(BF16)
    partial = nt(mixed, mix_half)
    row_partial = partial[:length].reshape(2, half, model)
    shared_partial = partial[length:].reshape(2, part, model)
    mine = jnp.concatenate([pick(row_partial, core), pick(shared_partial, core)])
    sent = jnp.concatenate([pick(row_partial, 1 - core), pick(shared_partial, 1 - core)])
    normed_grad = mine + swap(sent.astype(BF16), "core").astype(F32)
    own_tokens = jnp.concatenate(
        [
            lax.dynamic_slice_in_dim(row_tokens, core * half, half),
            lax.dynamic_slice_in_dim(shared_tokens, (2 * core + zq) * part, part),
        ]
    )
    n_first, r_first = norm_parts(own_tokens.astype(F32))
    input_part, first_gain_grad = norm_back(normed_grad, n_first, r_first, gain_first)
    input_grad = (middle_grad + input_part).astype(BF16)

    def place_heads(values):
        return jnp.where(jnp.arange(2)[:, None] == core, values, 0.0).reshape(1, model)

    gain_grads = jnp.concatenate(
        [first_gain_grad, place_heads(qgg + shared_qgg), place_heads(kgg + shared_kgg), second_gain_grad]
    )
    gain_grads = gain_grads.reshape(4, 2 * chips, shard).transpose(1, 0, 2).astype(BF16)
    if square:
        gain_rows = jnp.pad(gain_grads, ((0, 0), (0, 12), (0, 3 * width - shard)))
        payload = jnp.concatenate([mix_grad.reshape(2 * chips, shard, 3 * width), gain_rows], axis=1)
        input_out, mix_out, gains_out = finish(input_grad, payload)
        gains_out = gains_out[:4, :shard]
    else:
        first, second = input_grad[:part], input_grad[part:half]
        input_out = collect(
            jnp.where(zq == 0, first, second), jnp.where(zq == 0, second, first), input_grad[half:]
        )
        spread_mix = jnp.where(
            jnp.arange(2)[None, None, :, None] == core, mix_grad.reshape(model, 3, 1, width), 0
        ).reshape(model, 6 * width)
        mix_out = reduce(spread_mix)
        gains_out = reduce(gain_grads).reshape(4, shard)
    return (
        output, input_out, gains_out[0], mix_out, gains_out[1], gains_out[2], outw_out, gains_out[3],
        up_out, down_out,
    )


def solution(mesh):
    fsdp = mesh.shape["fsdp"]
    split = Mesh(mesh.devices.reshape(fsdp // 2, 2, 2, 2), ("chip", "core", "zp", "zq"))
    rows = ("chip", "core")
    return jax.shard_map(
        local,
        mesh=split,
        in_specs=(
            P(rows, SEQ, None),
            P(rows, None),
            P(rows, SEQ),
            P(rows),
            P(rows, None),
            P(rows),
            P(rows),
            P(rows, None),
            P(rows),
            P(rows, None),
            P(rows, None),
            P(rows, SEQ, None),
        ),
        out_specs=(
            P(rows, SEQ, None),
            P(rows, SEQ, None),
            P(rows),
            P(rows, None),
            P(rows),
            P(rows),
            P(rows, None),
            P(rows),
            P(rows, None),
            P(rows, None),
        ),
        check_vma=False,
    )
```

```python
import functools

import jax
import jax.numpy as jnp
from jax import lax
from jax.experimental import pallas as pl
from jax.experimental.pallas import tpu as pltpu
from jax.sharding import Mesh, PartitionSpec as P

HEADS = 12
HEAD = 64
EPSILON = 1e-06
BLOCK = 256
STEP = 512
MARK = 32.0
EXP2_FACTOR = HEAD**-0.5 * 1.4426950408889634
F32 = jnp.float32
BF16 = jnp.bfloat16
VMEM_LIMIT = 56 * 1024 * 1024

SEQ = ("zp", "zq")
COLUMN = ("core", "zp", "zq")
KEEP = [
    (core * 4 + z, (z // 2) * 4 + 2 * core + z % 2) for core in range(2) for z in range(4)
]
CROSS = [
    (core * 4 + z, (z // 2) * 4 + 2 * core + 1 - z % 2) for core in range(2) for z in range(4)
]


def swap(array, name, bit=1):
    count = lax.axis_size(name)
    return lax.ppermute(array, name, [(i, i ^ bit) for i in range(count)])


def pick(array, index, axis=0):
    return lax.dynamic_index_in_dim(array, index, axis, keepdims=False)


def group_ones(scale):
    row = lax.broadcasted_iota(jnp.int32, (128, 128), 0) // HEAD
    column = lax.broadcasted_iota(jnp.int32, (128, 128), 1) // HEAD
    return jnp.where(row == column, scale, 0.0).astype(BF16)


def group_sum(values, ones):
    return jnp.dot(values.astype(BF16), ones, preferred_element_type=F32)


def group_sum_fine(values, ones):
    high = values.astype(BF16)
    return group_sum(high, ones) + group_sum(values - high.astype(F32), ones)


def project_kernel(x_ref, gain_ref, weight_ref, qg_ref, kg_ref, normed_ref, q_ref, k_ref, v_ref, raw_ref):
    width = q_ref.shape[1]
    x = x_ref[...].astype(F32)
    center = x - jnp.mean(x, axis=-1, keepdims=True)
    spread = jnp.mean(center * center, axis=-1, keepdims=True)
    normed = (center * lax.rsqrt(spread + EPSILON) * gain_ref[...]).astype(BF16)
    normed_ref[...] = normed
    mixed = jnp.dot(normed, weight_ref[...], preferred_element_type=F32)
    raw_ref[...] = mixed[:, : 2 * width].astype(BF16)
    ones = group_ones(1.0 / HEAD)
    for part, (out_ref, g_ref) in enumerate(((q_ref, qg_ref), (k_ref, kg_ref))):
        for at in range(0, width, 128):
            raw = mixed[:, part * width + at : part * width + at + 128]
            c = raw - group_sum_fine(raw, ones)
            n = c * lax.rsqrt(group_sum(c * c, ones) + EPSILON)
            out_ref[:, at : at + 128] = (n * g_ref[:, at : at + 128]).astype(BF16)
    v_ref[...] = mixed[:, 2 * width :].astype(BF16)


def nt(a, b):
    return lax.dot_general(a, b, (((1,), (1,)), ((), ())), preferred_element_type=F32)


def tn(a, b):
    return lax.dot_general(a, b, (((0,), (0,)), ((), ())), preferred_element_type=F32)


def slots(queries, length, part):
    at = lax.broadcasted_iota(jnp.int32, (queries, 128), 0)
    if queries == length:
        return at
    return at % part + part * (lax.axis_index("zq") + 2 * (at // part))


def own_rows(ref, start, count, queries, part):
    if queries == ref.shape[0]:
        return ref[pl.ds(start, count), :]
    zq = lax.axis_index("zq")
    pieces = [
        ref[pl.ds(pl.multiple_of((zq + 2 * i) * part, part), part), :]
        for i in range(start // part, (start + count) // part)
    ]
    return jnp.concatenate(pieces, axis=0)


def query_marks(bounds_ref, place, queries, length, part, pics):
    at = slots(queries, length, part)
    inside = (at >= bounds_ref[0:1, :]) & (at < bounds_ref[2:3, :])
    values = jnp.where(inside, MARK, 0.0)
    return jnp.where(place == pics, MARK, values).astype(BF16)


def key_marks(bounds_ref, place, length, pics):
    at = lax.broadcasted_iota(jnp.int32, (length, 128), 0)
    inside = (at >= bounds_ref[0:1, :]) & (at < bounds_ref[1:2, :])
    values = jnp.where(inside, MARK, 0.0)
    values = jnp.where(place == pics, -MARK, values)
    return jnp.where((place > pics) & (place < pics + 4), 1.0, values).astype(BF16)


def attend_kernel(pics, q_ref, k_ref, v_ref, bounds_ref, out_ref, aug_ref, kaug, vaug, qaug):
    length = k_ref.shape[0]
    queries = out_ref.shape[0]
    part = length // 4
    lane = lax.broadcasted_iota(jnp.int32, (1, 128), 1)
    place = lane % HEAD
    sides = [lane < HEAD, lane >= HEAD]
    kmarks = key_marks(bounds_ref, place, length, pics)
    qmarks = query_marks(bounds_ref, place, queries, length, part, pics)
    qaug[...] = qmarks
    for h in range(2):
        kaug[h] = jnp.where(sides[h], k_ref[...], kmarks)
        vaug[h] = jnp.where(sides[h], v_ref[...], jnp.ones_like(v_ref))
    for b in range(queries // STEP):
        rows = pl.ds(b * STEP, STEP)
        mine = own_rows(q_ref, b * STEP, STEP, queries, part)
        query = [jnp.where(sides[h], mine, qaug[rows, :]) for h in range(2)]
        total = [jnp.zeros((STEP, 128), F32)] * 2
        for j in range(length // STEP):
            keys = pl.ds(j * STEP, STEP)
            scores = [nt(query[h], kaug[h, keys, :]) for h in range(2)]
            weights = [jnp.exp2(x * EXP2_FACTOR).astype(BF16) for x in scores]
            total = [
                total[h] + jnp.dot(weights[h], vaug[h, keys, :], preferred_element_type=F32) for h in range(2)
            ]
        results = []
        for h in range(2):
            results.append(total[h] / pltpu.roll(total[h], HEAD, 1))
            log_total = jnp.log(jnp.where(sides[h], 1.0, total[h])) * -(HEAD**0.5)
            first = log_total.astype(BF16)
            rest = log_total - first.astype(F32)
            middle = rest.astype(BF16)
            last = (rest - middle.astype(F32)).astype(BF16)
            logs = jnp.where(place == pics + 1, first, jnp.where(place == pics + 2, middle, last))
            slot = jnp.logical_not(sides[h]) & (place > pics) & (place < pics + 4)
            aug_ref[h, rows, :] = jnp.where(slot, logs, query[h])
        out_ref[rows, :] = jnp.where(sides[0], results[0], results[1]).astype(BF16)


def head_norm_back(e, raw, gain, means):
    raw = raw.astype(F32)
    c = raw - group_sum(raw, means)
    r = lax.rsqrt(group_sum(c * c, means) + EPSILON)
    n = c * r
    t = e * gain
    grad = r * (t - group_sum(t, means) - n * group_sum(t * n, means))
    return grad.astype(BF16), jnp.sum(e * n, axis=0, keepdims=True)


def attend_back_kernel(
    pics, aug_ref, k_ref, v_ref, out_ref, do_ref, rawq_ref, rawk_ref, qg_ref, kg_ref, bounds_ref,
    dq_ref, dk_ref, dv_ref, qgg_ref, kgg_ref, kaug, vaug, doaug, qsum, ksum,
):
    length = k_ref.shape[0]
    queries = do_ref.shape[0]
    part = length // 4
    whole = queries == length
    lane = lax.broadcasted_iota(jnp.int32, (1, 128), 1)
    place = lane % HEAD
    sides = [lane < HEAD, lane >= HEAD]
    kmarks = key_marks(bounds_ref, place, length, pics)
    vmarks = jnp.where(place < 2, 1.0, 0.0).astype(BF16)
    ones = group_ones(1.0)
    inner = group_sum_fine(do_ref[...].astype(F32) * out_ref[...].astype(F32), ones)
    inner = -pltpu.roll(inner, HEAD, 1)
    inner_high = inner.astype(BF16)
    inner_low = (inner - inner_high.astype(F32)).astype(BF16)
    zero = jnp.zeros((), BF16)
    gmarks = jnp.where(place == 0, inner_high, jnp.where(place == 1, inner_low, zero))
    for h in range(2):
        kaug[h] = jnp.where(sides[h], k_ref[...], kmarks)
        vaug[h] = jnp.where(sides[h], v_ref[...], vmarks)
        doaug[h] = jnp.where(sides[h], do_ref[...], gmarks)
    for b in range(length // STEP):
        keys = pl.ds(b * STEP, STEP)
        key = [kaug[h, keys, :] for h in range(2)]
        value = [vaug[h, keys, :] for h in range(2)]
        dk = [jnp.zeros((STEP, 128), F32)] * 2
        dv = [jnp.zeros((STEP, 128), F32)] * 2
        for j in range(queries // STEP):
            rows = pl.ds(j * STEP, STEP)
            query = [aug_ref[h, rows, :] for h in range(2)]
            grad = [doaug[h, rows, :] for h in range(2)]
            scores = [nt(key[h], query[h]) for h in range(2)]
            soft_grad = [nt(value[h], grad[h]) for h in range(2)]
            weights = [jnp.exp2(x * EXP2_FACTOR) for x in scores]
            score_grad = [(weights[h] * soft_grad[h]).astype(BF16) for h in range(2)]
            for h in range(2):
                part_sum = tn(score_grad[h], key[h])
                if b == 0:
                    qsum[h, rows, :] = part_sum
                else:
                    qsum[h, rows, :] += part_sum
                dk[h] = dk[h] + jnp.dot(score_grad[h], query[h], preferred_element_type=F32)
                dv[h] = dv[h] + jnp.dot(weights[h].astype(BF16), grad[h], preferred_element_type=F32)
        ksum[keys, :] = jnp.where(sides[0], dk[0], dk[1]) * HEAD**-0.5
        dv_ref[keys, :] = jnp.where(sides[0], dv[0], dv[1]).astype(BF16)

    means = group_ones(1.0 / HEAD)
    gain_sum = jnp.zeros((1, 128), F32)
    for b in range(queries // part):
        rows = pl.ds(b * part, part)
        e = jnp.where(sides[0], qsum[0, rows, :], qsum[1, rows, :]) * HEAD**-0.5
        raw = own_rows(rawq_ref, b * part, part, queries, part)
        dq_ref[rows, :], more = head_norm_back(e.astype(BF16).astype(F32), raw, qg_ref[...], means)
        gain_sum = gain_sum + more
    qgg_ref[...] = gain_sum
    gain_sum = jnp.zeros((1, 128), F32)
    for b in range(length // part):
        rows = pl.ds(b * part, part)
        e = ksum[rows, :].astype(BF16)
        if whole:
            dk_ref[rows, :], more = head_norm_back(e.astype(F32), rawk_ref[rows, :], kg_ref[...], means)
            gain_sum = gain_sum + more
        else:
            dk_ref[rows, :] = e
    kgg_ref[...] = gain_sum


def attend_back(aug, k, v, out, do, raw, query_gain, key_gain, bounds, pics):
    length, width = k.shape
    queries = do.shape[0]
    pairs = width // 128
    column = pl.BlockSpec((length, 128), lambda p: (0, p))
    own = pl.BlockSpec((queries, 128), lambda p: (0, p))
    gain = pl.BlockSpec((1, 128), lambda p: (0, p))
    return pl.pallas_call(
        functools.partial(attend_back_kernel, pics),
        grid=(pairs,),
        in_specs=[
            pl.BlockSpec((2, queries, 128), lambda p: (p, 0, 0)),
            column,
            column,
            own,
            own,
            column,
            pl.BlockSpec((length, 128), lambda p: (0, pairs + p)),
            gain,
            gain,
            pl.BlockSpec((8, 128), lambda p: (0, 0)),
        ],
        out_specs=[own, column, column, gain, gain],
        scratch_shapes=[
            pltpu.VMEM((2, length, 128), BF16),
            pltpu.VMEM((2, length, 128), BF16),
            pltpu.VMEM((2, queries, 128), BF16),
            pltpu.VMEM((2, queries, 128), F32),
            pltpu.VMEM((length, 128), F32),
        ],
        out_shape=[
            jax.ShapeDtypeStruct((queries, width), BF16),
            jax.ShapeDtypeStruct((length, width), BF16),
            jax.ShapeDtypeStruct((length, width), BF16),
            jax.ShapeDtypeStruct((1, width), F32),
            jax.ShapeDtypeStruct((1, width), F32),
        ],
        compiler_params=pltpu.CompilerParams(vmem_limit_bytes=VMEM_LIMIT),
        cost_estimate=pl.CostEstimate(
            flops=40 * length * queries * width, bytes_accessed=length * width * 20, transcendentals=0
        ),
        name="attend_back",
    )(aug, k, v, out, do, raw, raw, query_gain, key_gain, bounds)


def shared_keys_kernel(dk_ref, dv_ref, gotk_ref, gotv_ref, rawk_ref, kg_ref, outk_ref, outv_ref, kgg_ref):
    count = outk_ref.shape[0]
    part = count // 2
    means = group_ones(1.0 / HEAD)
    gain_sum = jnp.zeros((1, 128), F32)
    for b in range(2):
        rows = pl.ds(b * part, part)
        own = lambda ref: own_rows(ref, b * part, part, count, part)
        e = own(dk_ref).astype(F32) + gotk_ref[rows, :].astype(F32)
        outk_ref[rows, :], more = head_norm_back(e, own(rawk_ref), kg_ref[...], means)
        gain_sum = gain_sum + more
        outv_ref[rows, :] = (own(dv_ref).astype(F32) + gotv_ref[rows, :].astype(F32)).astype(BF16)
    kgg_ref[...] = gain_sum


def shared_keys(dk, dv, got_k, got_v, raw, key_gain):
    length, width = dk.shape
    pairs = width // 128
    column = pl.BlockSpec((length, 128), lambda p: (0, p))
    own = pl.BlockSpec((length // 2, 128), lambda p: (0, p))
    gain = pl.BlockSpec((1, 128), lambda p: (0, p))
    return pl.pallas_call(
        shared_keys_kernel,
        grid=(pairs,),
        in_specs=[column, column, own, own, pl.BlockSpec((length, 128), lambda p: (0, pairs + p)), gain],
        out_specs=[own, own, gain],
        out_shape=[
            jax.ShapeDtypeStruct((length // 2, width), BF16),
            jax.ShapeDtypeStruct((length // 2, width), BF16),
            jax.ShapeDtypeStruct((1, width), F32),
        ],
        compiler_params=pltpu.CompilerParams(vmem_limit_bytes=VMEM_LIMIT),
        name="shared_keys",
    )(dk, dv, got_k, got_v, raw, key_gain)


def gelu_pair(h):
    size = jnp.abs(h)
    bell = jnp.exp2(h * h * -0.7213475204444817)
    t = 1.0 / (1.0 + 0.23164189 * size)
    series = t * (0.127414796 + t * (-0.142248368 + t * (0.7107068705 + t * (-0.7265760135 + t * 0.5307027145))))
    tail = series * bell
    below = jnp.where(h < 0.0, tail, 1.0 - tail)
    return h * below, below + h * (bell * 0.3989422804014327)


def norm_parts(values):
    center = values - jnp.mean(values, axis=-1, keepdims=True)
    spread = lax.rsqrt(jnp.mean(center * center, axis=-1, keepdims=True) + EPSILON)
    return center * spread, spread


def norm_back(upstream, n, r, gain):
    t = upstream * gain
    grad = r * (t - jnp.mean(t, axis=-1, keepdims=True) - n * jnp.mean(t * n, axis=-1, keepdims=True))
    return grad, jnp.sum(upstream * n, axis=0, keepdims=True)


MESH_ID = pl.DeviceIdType.MESH


def here():
    return lax.axis_index("chip"), lax.axis_index("core"), lax.axis_index("zp"), lax.axis_index("zq")


def remote(source, target, sems, at, device):
    sent, got = sems
    return pltpu.make_async_remote_copy(
        src_ref=source, dst_ref=target, send_sem=sent.at[at], recv_sem=got.at[at],
        device_id=device, device_id_type=MESH_ID,
    )


def greet(devices, maybe=None, moves=None):
    barrier = pltpu.get_barrier_semaphore()
    for device in devices:
        pl.semaphore_signal(barrier, inc=1, device_id=device, device_id_type=MESH_ID)
    if maybe is None:
        pl.semaphore_wait(barrier, len(devices))
        return

    @pl.when(moves)
    def _():
        pl.semaphore_signal(barrier, inc=1, device_id=maybe, device_id_type=MESH_ID)

    pl.semaphore_wait(barrier, len(devices) + jnp.where(moves, 1, 0))


def rows_at(start, count):
    return pl.ds(pl.multiple_of(start, 16), count)


def write_bounds(pics, lens_ref, bounds_ref, zp, zq, length):
    lane = lax.broadcasted_iota(jnp.int32, (8, 128), 1)
    lens = jnp.where(zp == 0, lens_ref[0], lens_ref[1])
    ends = lens
    for hop in (1, 2, 4, 8):
        ends = ends + jnp.where(lane >= hop, pltpu.roll(ends, hop, 1), 0)
    starts = ends - lens
    last = (lens > 0) & (pltpu.roll(lens, 127, 1) == 0)
    query_ends = jnp.where(last, length, ends)
    total = jnp.max(jnp.where(lane < pics, ends, 0), axis=1, keepdims=True)

    def both(values):
        values = jnp.where(lane < HEAD, jnp.where(lane < pics, values, 2 * length), 0)
        return values + pltpu.roll(values, HEAD, 1)

    tables = [both(starts), both(ends), both(query_ends), jnp.broadcast_to(total, (8, 128))]
    for t in range(4):
        table = tables[t]
        bounds_ref[0, t : t + 1, :] = jnp.where(zq == 0, table[0:1], table[1:2])
        bounds_ref[1, t : t + 1, :] = table[2:3]
    bounds_ref[:, 4:, :] = jnp.zeros((2, 4, 128), jnp.int32)


def forward_kernel(square, pics, *refs):
    refs = list(refs)
    take = lambda count: [refs.pop(0) for _ in range(count)]
    tokens_ref, cot_ref, lens_ref, mix_ref, gains_ref = take(5)
    if square:
        up_ref, down_ref, outw_ref = take(3)
    else:
        gain_first, gain_query, gain_key = take(3)
    x_out, bounds_ref, mix_hbm, second_ref, query_out, key_out, cot_hbm = take(7)
    names = ("normed", "k", "v", "raw", "out", "aug")
    outs = [dict(zip(names, take(6))) for _ in range(2)]
    if square:
        up_hbm, down_hbm, outw_hbm = take(3)
    row_ref, shared_ref, cot_out, lens_out = take(4)
    scratch = [dict(zip(names + ("q",), take(7))) for _ in range(2)]
    kaug, vaug, qaug = take(3)
    if square:
        mix_out, gains_out, gain_first, gain_query, gain_key, up_out, down_out, outw_out = take(8)
    sent, got, local_sem, write_sem = take(4)

    chip, core, zp, zq = here()
    z = 2 * zp + zq
    part = tokens_ref.shape[1]
    half, length = 2 * part, 4 * part
    sems = (sent, got)
    partner = (chip, 1 - core, zp, zq)
    side = (chip, core, zp, 1 - zq)
    keep = (chip, zp, core, zq)
    cross = (chip, zp, core, 1 - zq)
    moves = core != zp
    near_x = (chip ^ 1, core, zp, zq)
    near_y = (chip ^ 2, core, zp, zq)
    greet([partner, side, cross] + ([near_x, near_y] if square else []), keep, moves)

    def quarter(ref, index):
        return ref.at[rows_at(index * part, part)]

    own_row = remote(tokens_ref.at[zq], quarter(row_ref, z), sems, 0, keep)
    own_shared = remote(tokens_ref.at[2], quarter(shared_ref, z), sems, 2, keep)
    stay_row = pltpu.make_async_copy(tokens_ref.at[zq], quarter(row_ref, z), local_sem.at[0])
    stay_shared = pltpu.make_async_copy(tokens_ref.at[2], quarter(shared_ref, z), local_sem.at[1])

    @pl.when(moves)
    def _():
        own_row.start()

    @pl.when(jnp.logical_not(moves))
    def _():
        stay_row.start()

    cross_row = remote(tokens_ref.at[1 - zq], quarter(row_ref, z), sems, 1, cross)
    cross_row.start()

    @pl.when(moves)
    def _():
        own_shared.start()

    @pl.when(jnp.logical_not(moves))
    def _():
        stay_shared.start()

    lens_copy = remote(lens_ref, lens_out.at[core], sems, 8, partner)
    lens_copy.start()
    lens_stay = pltpu.make_async_copy(lens_ref, lens_out.at[core], local_sem.at[2])
    lens_stay.start()
    waits = []
    if square:
        shard = mix_ref.shape[1]
        down_rows = down_ref.shape[0]
        mine, theirs = 2 * chip + core, 2 * chip + 1 - core
        slot = [9]

        def send(source, target, device):
            copy = remote(source, target, sems, slot[0], device)
            slot[0] += 1
            copy.start()
            waits.append(copy)
            return copy

        def stay(source, target, at):
            copy = pltpu.make_async_copy(source, target, local_sem.at[at])
            copy.start()
            return copy

        def block(ref, start, count):
            return ref.at[rows_at(start, count)]

        mix_piece = lambda index: (block(mix_out, index * shard, shard), gains_out.at[index])

        def send_mix(sources, index, device):
            return [send(source, target, device) for source, target in zip(sources, mix_piece(index))]

        def arrived(copies):
            for copy in copies:
                copy.wait_recv()

        x_mine, y_other = 2 * (chip ^ 1) + core, 2 * (chip ^ 2) + 1 - core
        to_core = send_mix((mix_ref.at[1 - core], gains_ref), mine, partner)
        a_x = send_mix((mix_ref.at[core], gains_ref), mine, near_x)
        a_y = send_mix((mix_ref.at[core], gains_ref), mine, near_y)
        up_core = send(up_ref.at[1 - core], block(up_out, mine * shard, shard), partner)
        out_core = send(outw_ref, block(outw_out, mine * shard, shard), partner)
        stays = [
            stay(mix_ref.at[core], mix_piece(mine)[0], 3),
            stay(gains_ref, gains_out.at[mine], 4),
            stay(up_ref.at[core], block(up_out, mine * shard, shard), 5),
            stay(down_ref, block(down_out, chip * down_rows, down_rows), 6),
            stay(outw_ref, block(outw_out, mine * shard, shard), 7),
        ]
        arrived(to_core)
        b_x = send_mix(mix_piece(theirs), theirs, near_x)
        b_y = send_mix(mix_piece(theirs), theirs, near_y)
        arrived(a_x)
        a_far = send_mix(mix_piece(x_mine), x_mine, near_y)
        arrived(b_y)
        b_far = send_mix(mix_piece(y_other), y_other, near_x)
        for copy in stays:
            copy.wait()
        arrived([up_core])
        dhalf, ohalf = down_rows // 2, shard // 2

        def bundle(first, from_chip):
            same, twin = 2 * from_chip + core, 2 * from_chip + 1 - core
            part_of = 0 if first else 1
            return [
                block(up_out, (same if first else twin) * shard, shard),
                block(down_out, from_chip * down_rows + part_of * dhalf, dhalf),
                block(outw_out, same * shard + part_of * ohalf, ohalf),
            ]

        def send_bundle(first, from_chip, device):
            return [send(ref, ref, device) for ref in bundle(first, from_chip)]

        first_x = send_bundle(True, chip, near_x)
        first_y = send_bundle(True, chip, near_y)
        second_x = send_bundle(False, chip, near_x)
        second_y = send_bundle(False, chip, near_y)

    lens_copy.wait()
    lens_stay.wait()
    write_bounds(pics, lens_out, bounds_ref, zp, zq, length)
    if square:
        arrived(a_y + b_x + a_far + b_far)
        for p in range(gains_out.shape[0]):
            lanes = slice(p * shard, (p + 1) * shard)
            values = gains_out[p, :, :shard].astype(F32)
            gain_first[:, lanes] = values[0:1]
            second_ref[:, lanes] = values[3:4]
            half_pieces = gains_out.shape[0] // 2

            @pl.when(core == p // half_pieces)
            def _():
                at = (p % half_pieces) * shard
                gain_query[:, at : at + shard] = values[1:2]
                gain_key[:, at : at + shard] = values[2:3]
        weight = mix_out
    else:
        weight = mix_ref
        second_ref[...] = jnp.zeros_like(second_ref)
    writes = []

    def write(source, target, at):
        copy = pltpu.make_async_copy(source, target, write_sem.at[at])
        copy.start()
        writes.append(copy)

    query_out[0] = gain_query[...]
    query_out[1] = gain_first[:, : gain_query.shape[1]]
    key_out[0] = gain_key[...]
    key_out[1] = gain_first[:, gain_query.shape[1] :]
    write(weight, mix_hbm, 0)

    @pl.when(moves)
    def _():
        own_row.wait_recv()

    @pl.when(jnp.logical_not(moves))
    def _():
        stay_row.wait()

    first, second = 2 * core + zq, 2 * core + 1 - zq
    row_one = remote(quarter(row_ref, first), quarter(row_ref, first), sems, 3, partner)
    row_one.start()
    cross_row.wait_recv()
    row_two = remote(quarter(row_ref, second), quarter(row_ref, second), sems, 4, partner)
    row_two.start()

    def project(tokens, bufs):
        def one(i, _):
            rows = pl.ds(pl.multiple_of(i * BLOCK, BLOCK), BLOCK)
            project_kernel(
                tokens.at[rows], gain_first, weight, gain_query, gain_key, bufs["normed"].at[rows],
                bufs["q"].at[rows], bufs["k"].at[rows], bufs["v"].at[rows], bufs["raw"].at[rows],
            )
            return 0

        lax.fori_loop(0, length // BLOCK, one, 0)

    def attend(bufs, bounds):
        def one(p, _):
            lanes = pl.ds(pl.multiple_of(p * 128, 128), 128)
            attend_kernel(
                pics, bufs["q"].at[:, lanes], bufs["k"].at[:, lanes], bufs["v"].at[:, lanes], bounds,
                bufs["out"].at[:, lanes], bufs["aug"].at[pl.ds(2 * p, 2)], kaug, vaug, qaug.at[pl.ds(0, bufs["out"].shape[0])],
            )
            return 0

        lax.fori_loop(0, gain_query.shape[1] // 128, one, 0)

    row_one.wait_recv()
    row_two.wait_recv()
    project(row_ref, scratch[0])
    for i, name in enumerate(("normed", "k", "v", "raw")):
        write(scratch[0][name], outs[0][name], 1 + i)
    write(row_ref.at[rows_at(core * half, half)], x_out.at[pl.ds(0, half)], 5)

    @pl.when(moves)
    def _():
        own_shared.wait_recv()

    @pl.when(jnp.logical_not(moves))
    def _():
        stay_shared.wait()

    to_side = remote(quarter(shared_ref, first), quarter(shared_ref, first), sems, 5, side)
    to_side.start()
    shared_one = remote(quarter(shared_ref, first), quarter(shared_ref, first), sems, 6, partner)
    shared_one.start()
    cot_own = pl.ds(pl.multiple_of(zq * part, part), part)
    cot_shared = pl.ds(half, part)
    cot_moves = [
        remote(cot_ref.at[zq], cot_out.at[cot_own], sems, 46, keep),
        remote(cot_ref.at[2], cot_out.at[cot_shared], sems, 47, keep),
    ]
    cot_stays = [
        pltpu.make_async_copy(cot_ref.at[zq], cot_out.at[cot_own], local_sem.at[0]),
        pltpu.make_async_copy(cot_ref.at[2], cot_out.at[cot_shared], local_sem.at[1]),
    ]
    cot_cross = remote(cot_ref.at[1 - zq], cot_out.at[cot_own], sems, 48, cross)

    @pl.when(moves)
    def _():
        for copy in cot_moves:
            copy.start()

    @pl.when(jnp.logical_not(moves))
    def _():
        for copy in cot_stays:
            copy.start()

    cot_cross.start()
    attend(scratch[0], bounds_ref.at[0])
    write(scratch[0]["out"], outs[0]["out"], 6)
    write(scratch[0]["aug"], outs[0]["aug"], 7)
    to_side.wait_recv()
    shared_two = remote(quarter(shared_ref, second), quarter(shared_ref, second), sems, 7, partner)
    shared_two.start()
    if square:
        arrived(first_x + second_y)
        far_first = send_bundle(True, chip ^ 1, near_y)
        far_second = send_bundle(False, chip ^ 2, near_x)
    shared_one.wait_recv()
    shared_two.wait_recv()
    project(shared_ref, scratch[1])
    for i, name in enumerate(("normed", "k", "v", "raw")):
        write(scratch[1][name], outs[1][name], 8 + i)
    write(shared_ref.at[rows_at(first * part, part)], x_out.at[pl.ds(half, part)], 12)
    attend(scratch[1], bounds_ref.at[1])
    write(scratch[1]["out"], outs[1]["out"], 13)
    write(scratch[1]["aug"], outs[1]["aug"], 14)

    if square:
        arrived(first_y + second_x + far_first + far_second)
        sent_pieces = []
        for c in (chip ^ 1, chip ^ 2, chip ^ 3):
            target = block(outw_out, (2 * c + core) * shard, shard)
            sent_pieces.append(send(target, target, partner))
        write(up_out, up_hbm, 15)
        write(down_out, down_hbm, 16)
        arrived(sent_pieces + [out_core])
        write(outw_out, outw_hbm, 17)
        for copy in waits:
            copy.wait_send()
    cot_cross.wait()

    @pl.when(moves)
    def _():
        for copy in cot_moves:
            copy.wait()

    @pl.when(jnp.logical_not(moves))
    def _():
        for copy in cot_stays:
            copy.wait()

    write(cot_out, cot_hbm, 18)
    for copy in (row_one, row_two, shared_one, shared_two, to_side, cross_row):
        copy.wait_send()

    @pl.when(moves)
    def _():
        own_row.wait_send()
        own_shared.wait_send()

    for copy in writes:
        copy.wait()


def forward_pass(square, pics, tokens, cotangent, lens, mix, gains, *more):
    _, part, model = tokens.shape
    length, half, width = 4 * part, 2 * part, model // 2
    near = pl.BlockSpec(memory_space=pltpu.VMEM)
    anywhere = pl.BlockSpec(memory_space=pl.ANY)
    low = lambda *shape: (shape, BF16)
    wide = lambda *shape: (shape, F32)
    outs = [
        (low(3 * part, model), anywhere),
        (((2, 8, 128), jnp.int32), near),
        (low(model, 3 * width), anywhere),
        (wide(1, model), near),
        (wide(2, 1, width), near),
        (wide(2, 1, width), near),
        (low(3 * part, model), anywhere),
    ]
    bufs = []
    for queries in (length, half):
        shapes = [
            low(length, model), low(length, width), low(length, width), low(length, 2 * width),
            low(queries, width), low(2 * (width // 128), queries, 128),
        ]
        outs += [(shape, anywhere) for shape in shapes]
        bufs += shapes + [low(length, width)]
    scratch = [low(length, model), low(length, model), low(3 * part, model), ((2,) + lens.shape, jnp.int32)] + bufs
    scratch += [low(2, length, 128), low(2, length, 128), low(length, 128)]
    if square:
        up, down, outw = more
        landed = [low(model, up.shape[2]), low(4 * down.shape[0], model), low(model, model)]
        outs += [(shape, anywhere) for shape in landed]
        scratch += [low(model, 3 * width), low(8, *gains.shape), wide(1, model), wide(1, width), wide(1, width)]
        scratch += landed
    return pl.pallas_call(
        functools.partial(forward_kernel, square, pics),
        in_specs=[near] * (5 + len(more)),
        out_specs=[spec for _, spec in outs],
        out_shape=[jax.ShapeDtypeStruct(*shape) for shape, _ in outs],
        scratch_shapes=[pltpu.VMEM(*shape) for shape in scratch]
        + [
            pltpu.SemaphoreType.DMA((49,)),
            pltpu.SemaphoreType.DMA((49,)),
            pltpu.SemaphoreType.DMA((8,)),
            pltpu.SemaphoreType.DMA((19,)),
        ],
        compiler_params=pltpu.CompilerParams(
            collective_id=0, has_side_effects=True, vmem_limit_bytes=60 * 1024 * 1024
        ),
        name="forward_pass",
    )(tokens, cotangent, lens, mix, gains, *more)


def dense_kernel(
    out_ref, shared_ref, x, grad_ref, outw_ref, gain_ref,
    bounds_ref, up_ref, down_ref,
    out_keep, out_cross, out_third, midg_ref, row_grad, shared_grad, packed, gaing_ref,
    att_other, second, grad, hidden_all, pre_all, forward, backward, middle, ups, downs,
    parts_out, parts_in, heads_out, cols_out, cols_in, sent, got, tile_sem,
):
    chip, core, zp, zq = here()
    sems = (sent, got)
    partner = (chip, 1 - core, zp, zq)
    tokens, model = midg_ref.shape
    part = tokens // 3
    half = 2 * part
    width = out_ref.shape[1]
    tile = ups.shape[2]
    other = 1 - core
    mine, theirs = pl.ds(0, tokens), pl.ds(tokens, tokens)

    for i in range(4):
        pltpu.make_async_copy(up_ref.at[:, pl.ds(i * tile, tile)], ups.at[i], tile_sem.at[0, i]).start()
        pltpu.make_async_copy(down_ref.at[pl.ds(i * tile, tile)], downs.at[i], tile_sem.at[1, i]).start()
    greet([partner])
    att_sends = [
        remote(out_ref.at[rows_at(other * half, half)], att_other.at[pl.ds(0, half)], sems, 0, partner),
        remote(shared_ref.at[rows_at(other * part, part)], att_other.at[pl.ds(half, part)], sems, 1, partner),
    ]
    for copy in att_sends:
        copy.start()

    slot = lax.broadcasted_iota(jnp.int32, (part, 1), 0)
    filled, shared_filled = bounds_ref[0, 3:4, 0:1], bounds_ref[1, 3:4, 0:1]
    none = jnp.zeros((), BF16)
    for b, start, limit in (
        (0, 2 * core * part, filled),
        (1, (2 * core + 1) * part, filled),
        (2, (2 * core + zq) * part, shared_filled),
    ):
        rows = pl.ds(b * part, part)
        grad[rows, :] = jnp.where(slot + start < limit, grad_ref[rows, :], none)
    grad_send = remote(grad.at[mine], grad.at[theirs], sems, 2, partner)
    grad_send.start()

    own_rows_of = lambda b: (
        out_ref[rows_at(core * half + b * part, part), :] if b < 2 else shared_ref[rows_at(core * part, part), :]
    )
    own_weight = outw_ref[rows_at(core * width, width), :]
    other_weight = outw_ref[rows_at(other * width, width), :]
    blocks = [pl.ds(b * part, part) for b in range(3)]
    for b in range(3):
        middle[blocks[b], :] = x[blocks[b], :].astype(F32) + jnp.dot(
            own_rows_of(b), own_weight, preferred_element_type=F32
        )
    for copy in att_sends:
        copy.wait_recv()
    for rows in blocks:
        value = middle[rows, :] + jnp.dot(att_other[rows, :], other_weight, preferred_element_type=F32)
        middle[rows, :] = value
        second[rows, :] = (norm_parts(value)[0] * gain_ref[...]).astype(BF16)
    second_send = remote(second.at[mine], second.at[theirs], sems, 3, partner)
    second_send.start()
    forward[...] = jnp.zeros_like(forward)
    backward[...] = jnp.zeros_like(backward)
    second_send.wait_recv()
    grad_send.wait_recv()

    def one_tile(i, _):
        pltpu.make_async_copy(up_ref.at[:, pl.ds(0, tile)], ups.at[i], tile_sem.at[0, i]).wait()
        pltpu.make_async_copy(down_ref.at[pl.ds(0, tile)], downs.at[i], tile_sem.at[1, i]).wait()
        up, down = ups[i], downs[i]
        for rows in (mine, theirs):
            pre = jnp.dot(second[rows, :], up, preferred_element_type=F32)
            hidden, slope = gelu_pair(pre)
            hidden = hidden.astype(BF16)
            hidden_all[rows, :] = hidden
            forward[rows, :] += jnp.dot(hidden, down, preferred_element_type=F32)
            pre_grad = (nt(grad[rows, :], down) * slope).astype(BF16)
            pre_all[rows, :] = pre_grad
            backward[rows, :] += nt(pre_grad, up)
        packed[i, pl.ds(0, tile), :] = tn(hidden_all[...], grad[...]).astype(BF16)
        up_grad = tn(second[...], pre_all[...]).astype(BF16)
        quarter = model // 4
        for c in range(4):
            place = (rows_at(tile + (i // 2) * quarter, quarter), pl.ds(pl.multiple_of((i % 2) * tile, 128), tile))
            packed[c, place[0], place[1]] = up_grad[c * quarter : (c + 1) * quarter, :]
        return 0

    lax.fori_loop(0, 4, one_tile, 0)

    parts_out[0] = forward[theirs, :].astype(BF16)
    first_part = remote(parts_out.at[0], parts_in.at[0], sems, 4, partner)
    first_part.start()
    parts_out[1] = backward[theirs, :].astype(BF16)
    second_part = remote(parts_out.at[1], parts_in.at[1], sems, 5, partner)
    second_part.start()
    second_send.wait_send()
    first_part.wait_recv()
    for rows in blocks:
        value = middle[rows, :] + forward[rows, :] + parts_in[0, rows, :].astype(F32)
        forward[rows, :] = value
    out_keep[...] = forward[rows_at(zq * part, part), :].astype(BF16)
    out_cross[...] = forward[rows_at((1 - zq) * part, part), :].astype(BF16)
    out_third[...] = forward[pl.ds(half, part), :].astype(BF16)
    second_part.wait_recv()
    gain_sum = jnp.zeros(gaing_ref.shape, F32)
    for b in range(3):
        rows = blocks[b]
        n, r = norm_parts(middle[rows, :])
        upstream = backward[rows, :] + parts_in[1, rows, :].astype(F32)
        more, gain_more = norm_back(upstream, n, r, gain_ref[...])
        gain_sum = gain_sum + gain_more
        value = grad[rows, :].astype(F32) + more
        midg_ref[rows, :] = value
        branch = value.astype(BF16)
        second[rows, :] = branch
        heads_out[rows, :] = nt(branch, other_weight).astype(BF16)
    gaing_ref[...] = gain_sum
    head_sends = [
        remote(heads_out.at[pl.ds(0, half)], row_grad.at[rows_at(core * half, half)], sems, 6, partner),
        remote(heads_out.at[pl.ds(half, part)], shared_grad.at[rows_at(core * part, part)], sems, 7, partner),
    ]
    for copy in head_sends:
        copy.start()
    branch = second[mine, :]
    out_grads = [
        tn(out_ref[rows_at(core * half, half), :], second[pl.ds(0, half), :])
        + tn(shared_ref[rows_at(core * part, part), :], second[pl.ds(half, part), :]),
        tn(att_other[...], branch),
    ]
    for turn, heads in ((0, core), (1, other)):
        rows = rows_at(heads * width, width)
        forward[rows, :] = out_grads[turn]
    lanes = lambda side: pl.ds(pl.multiple_of(side * width, 128), width)
    cols_out[...] = forward[pl.ds(0, model), lanes(other)].astype(BF16)
    cols_send = remote(cols_out, cols_in, sems, 8, partner)
    cols_send.start()
    for b in range(3):
        value = nt(second[blocks[b], :], own_weight).astype(BF16)
        if b < 2:
            row_grad[rows_at(core * half + b * part, part), :] = value
        else:
            shared_grad[rows_at(core * part, part), :] = value
    cols_send.wait_recv()
    total = (forward[pl.ds(0, model), lanes(core)] + cols_in[...].astype(F32)).astype(BF16)
    eighth = model // 8
    for c in range(4):
        for h in range(2):
            at = (2 * c + h) * eighth
            packed[c, pl.ds(2 * tile, eighth), h * width : (h + 1) * width] = total[at : at + eighth, :]
    for copy in head_sends:
        copy.wait_recv()
    for copy in att_sends + head_sends + [grad_send, first_part, second_part, cols_send]:
        copy.wait_send()


def dense(out, shared_out, x, grad, out_matrix, gain, bounds, up, down):
    model = x.shape[1]
    tokens = x.shape[0]
    part = tokens // 3
    length, width = out.shape
    hidden = down.shape[0]
    tile = hidden // 4
    anywhere = pl.BlockSpec(memory_space=pl.ANY)
    near = pl.BlockSpec(memory_space=pltpu.VMEM)
    both = 2 * tokens
    return pl.pallas_call(
        dense_kernel,
        in_specs=[near] * 7 + [anywhere, anywhere],
        out_specs=[near] * 8,
        out_shape=[
            jax.ShapeDtypeStruct((part, model), BF16),
            jax.ShapeDtypeStruct((part, model), BF16),
            jax.ShapeDtypeStruct((part, model), BF16),
            jax.ShapeDtypeStruct((tokens, model), F32),
            jax.ShapeDtypeStruct((length, width), BF16),
            jax.ShapeDtypeStruct((length // 2, width), BF16),
            jax.ShapeDtypeStruct((4, 2 * tile + model // 8, model), BF16),
            jax.ShapeDtypeStruct((1, model), F32),
        ],
        scratch_shapes=[
            pltpu.VMEM((tokens, width), BF16),
            pltpu.VMEM((both, model), BF16),
            pltpu.VMEM((both, model), BF16),
            pltpu.VMEM((both, tile), BF16),
            pltpu.VMEM((both, tile), BF16),
            pltpu.VMEM((both, model), F32),
            pltpu.VMEM((both, model), F32),
            pltpu.VMEM((tokens, model), F32),
            pltpu.VMEM((4, model, tile), BF16),
            pltpu.VMEM((4, tile, model), BF16),
            pltpu.VMEM((2, tokens, model), BF16),
            pltpu.VMEM((2, tokens, model), BF16),
            pltpu.VMEM((tokens, width), BF16),
            pltpu.VMEM((model, width), BF16),
            pltpu.VMEM((model, width), BF16),
            pltpu.SemaphoreType.DMA((9,)),
            pltpu.SemaphoreType.DMA((9,)),
            pltpu.SemaphoreType.DMA((2, 4)),
        ],
        compiler_params=pltpu.CompilerParams(
            collective_id=1, has_side_effects=True, vmem_limit_bytes=60 * 1024 * 1024
        ),
        cost_estimate=pl.CostEstimate(
            flops=32 * tokens * model * hidden, bytes_accessed=16 * model * hidden, transcendentals=0
        ),
        name="dense",
    )(out, shared_out, x, grad, out_matrix, gain, bounds, up, down)


def finish_kernel(
    grad_ref, mix_ref, out_ref, total_ref, gains_ref,
    relay, final, core_got, chunks, gain_parts, chunk_got, gain_got, sent, got, local_sem,
):
    chip, core, zp, zq = here()
    z = 2 * zp + zq
    sems = (sent, got)
    part = out_ref.shape[1]
    shard = mix_ref.shape[1] - 16
    quarter = shard // 2
    columns = mix_ref.shape[2]
    partner = (chip, 1 - core, zp, zq)
    keep = (chip, zp, core, zq)
    cross = (chip, zp, core, 1 - zq)
    moves = core != zp
    near_x = (chip ^ 1, core, zp, zq)
    near_y = (chip ^ 2, core, zp, zq)
    along = [(chip, core, zp, 1 - zq), (chip, core, 1 - zp, zq), (chip, core, 1 - zp, 1 - zq)]
    greet([partner, cross, near_x, near_y] + along, keep, moves)

    mine, theirs = 2 * chip + core, 2 * chip + 1 - core
    x_mine, x_other = 2 * (chip ^ 1) + core, 2 * (chip ^ 1) + 1 - core
    y_mine, y_other = 2 * (chip ^ 2) + core, 2 * (chip ^ 2) + 1 - core
    far_mine, far_other = 2 * (chip ^ 3) + core, 2 * (chip ^ 3) + 1 - core
    first = remote(mix_ref.at[far_mine], relay.at[0], sems, 0, near_y)
    second = remote(mix_ref.at[far_other], relay.at[1], sems, 1, near_x)
    first.start()
    second.start()
    direct_x = remote(mix_ref.at[x_other], final.at[0], sems, 2, near_x)
    direct_y = remote(mix_ref.at[y_mine], final.at[1], sems, 3, near_y)
    direct_x.start()
    direct_y.start()

    own = pl.ds(pl.multiple_of(zq * part, 16), part)
    own_row = remote(grad_ref.at[own], out_ref.at[zq], sems, 4, keep)
    own_shared = remote(grad_ref.at[pl.ds(2 * part, part)], out_ref.at[2], sems, 5, keep)
    stay_row = pltpu.make_async_copy(grad_ref.at[own], out_ref.at[zq], local_sem.at[0])
    stay_shared = pltpu.make_async_copy(grad_ref.at[pl.ds(2 * part, part)], out_ref.at[2], local_sem.at[1])

    @pl.when(moves)
    def _():
        own_row.start()
        own_shared.start()

    @pl.when(jnp.logical_not(moves))
    def _():
        stay_row.start()
        stay_shared.start()

    cross_row = remote(grad_ref.at[rows_at((1 - zq) * part, part)], out_ref.at[zq], sems, 6, cross)
    cross_row.start()

    def add(*terms):
        total = terms[0].astype(F32)
        for term in terms[1:]:
            total = total + term.astype(F32)
        return total

    first.wait_recv()
    relay[2] = add(relay[0], mix_ref[x_mine]).astype(BF16)
    onward_x = remote(relay.at[2], final.at[2], sems, 7, near_x)
    onward_x.start()
    second.wait_recv()
    relay[3] = add(relay[1], mix_ref[y_other]).astype(BF16)
    onward_y = remote(relay.at[3], final.at[3], sems, 8, near_y)
    onward_y.start()
    direct_x.wait_recv()
    onward_y.wait_recv()
    relay[4] = add(mix_ref[theirs], final[0], final[3]).astype(BF16)
    to_core = remote(relay.at[4], core_got, sems, 9, partner)
    to_core.start()
    direct_y.wait_recv()
    onward_x.wait_recv()
    kept = add(mix_ref[mine], final[1], final[2])
    for i in range(2):
        chunks[2 * core + i] = kept[i * quarter : (i + 1) * quarter].astype(BF16)
    to_core.wait_recv()
    for i in range(2):
        chunks[2 * (1 - core) + i] = core_got[i * quarter : (i + 1) * quarter]
    gain_parts[0] = (kept[shard:] + core_got[shard:].astype(F32)).astype(BF16)
    hops = [z ^ 1, z ^ 2, z ^ 3]
    copies = []
    for i in range(3):
        copies.append(remote(chunks.at[hops[i]], chunk_got.at[i], sems, 10 + i, along[i]))
        copies.append(remote(gain_parts.at[0], gain_got.at[i], sems, 13 + i, along[i]))
    for copy in copies:
        copy.start()
    for copy in copies:
        copy.wait_recv()
    gains_ref[...] = add(gain_parts[0], gain_got[0], gain_got[1], gain_got[2])
    chunk_got[3] = add(chunks[z], chunk_got[0], chunk_got[1], chunk_got[2]).astype(BF16)
    spread = [remote(chunk_got.at[3], chunk_got.at[4 + i], sems, 16 + i, along[i]) for i in range(3)]
    for copy in spread:
        copy.start()

    def place(index, values):
        half, up = index // 2, index % 2
        third = columns // 3
        values = values.astype(F32)
        for h in range(2):
            for u in range(2):

                @pl.when((half == h) & (up == u))
                def _():
                    for p in range(3):
                        total_ref[u * quarter : (u + 1) * quarter, (2 * p + h) * third : (2 * p + h + 1) * third] = (
                            values[:, p * third : (p + 1) * third]
                        )

    place(z, chunk_got[3])
    for i in range(3):
        spread[i].wait_recv()
        place(hops[i], chunk_got[4 + i])
    for copy in copies + spread + [first, second, direct_x, direct_y, onward_x, onward_y, to_core]:
        copy.wait_send()
    cross_row.wait()

    @pl.when(moves)
    def _():
        own_row.wait()
        own_shared.wait()

    @pl.when(jnp.logical_not(moves))
    def _():
        stay_row.wait()
        stay_shared.wait()


def finish(grad, mix):
    tokens, model = grad.shape
    _, rows, columns = mix.shape
    shard = rows - 16
    local_space = pl.BlockSpec(memory_space=pltpu.VMEM)
    buffers = lambda count, size: pltpu.VMEM((count, size, columns), BF16)
    return pl.pallas_call(
        finish_kernel,
        in_specs=[local_space, local_space],
        out_specs=[local_space, local_space, local_space],
        out_shape=[
            jax.ShapeDtypeStruct((3, tokens // 3, model), BF16),
            jax.ShapeDtypeStruct((shard, 2 * columns), F32),
            jax.ShapeDtypeStruct((16, columns), F32),
        ],
        scratch_shapes=[
            buffers(5, rows),
            buffers(4, rows),
            pltpu.VMEM((rows, columns), BF16),
            buffers(4, shard // 2),
            buffers(1, 16),
            buffers(7, shard // 2),
            buffers(3, 16),
            pltpu.SemaphoreType.DMA((19,)),
            pltpu.SemaphoreType.DMA((19,)),
            pltpu.SemaphoreType.DMA((2,)),
        ],
        compiler_params=pltpu.CompilerParams(
            collective_id=3, has_side_effects=True, vmem_limit_bytes=VMEM_LIMIT
        ),
        name="finish",
    )(grad, mix)


def local(
    tokens, lengths, pictures, first_gain, mix_weight, query_gain, key_gain, out_weight,
    second_gain, up_weight, down_weight, cotangent,
):
    chip, core, zp, zq = here()
    chips = lax.axis_size("chip")
    square = chips == 4
    rows = ("chip", "core")
    _, part, model = tokens.shape
    length = 4 * part
    half = 2 * part
    width = HEADS // 2 * HEAD
    pics = lengths.shape[1]
    shard = mix_weight.shape[0]

    gains = jnp.stack([first_gain, query_gain, key_gain, second_gain])
    gains = jnp.pad(gains, ((0, 12), (0, 128 - shard)))
    mix_split = mix_weight.reshape(shard, 3, 2, width).transpose(2, 0, 1, 3).reshape(2, shard, 3 * width)
    lens = jnp.pad(lengths, ((0, 5), (0, 128 - pics)))
    hidden = up_weight.shape[1]
    tile = hidden // 8
    if square:
        up_split = up_weight.reshape(shard, 4, 2, tile).transpose(2, 0, 1, 3).reshape(2, shard, 4 * tile)
        forward = forward_pass(
            True, pics, tokens, cotangent, lens, mix_split, gains, up_split, down_weight, out_weight
        )
        up_half, down_half, out_matrix = forward[19:]
        gain_second = forward[3]
    else:
        gather = lambda weight: lax.all_gather(weight, rows, axis=0, tiled=True)
        half_of = lambda weight, axis: pick(weight, core, axis)
        mix_half = half_of(gather(mix_weight).reshape(model, 3, 2, width), 2).reshape(model, 3 * width)
        up_half = half_of(gather(up_weight).reshape(model, 4, 2, tile), 2).reshape(model, 4 * tile)
        down_half = half_of(gather(down_weight).reshape(4, 2, tile, model), 1).reshape(4 * tile, model)
        out_matrix = gather(out_weight)
        spread_gains = lax.all_gather(gains, rows, axis=0, tiled=False)
        spread_gains = spread_gains[:, :4, :shard].transpose(1, 0, 2).reshape(4, 1, model).astype(F32)
        gain_second = spread_gains[3]
        forward = forward_pass(
            False, pics, tokens, cotangent, lens, mix_half, gains, spread_gains[0],
            half_of(spread_gains[1].reshape(2, 1, width), 0), half_of(spread_gains[2].reshape(2, 1, width), 0),
        )
    own_tokens, bounds, mix_half, _, query_first, key_first, grad_tokens = forward[:7]
    gain_query, gain_key = query_first[0], key_first[0]
    gain_first = jnp.concatenate([query_first[1], key_first[1]], axis=1)
    normed, k, v, raw, out, aug = forward[7:13]
    shared_normed, shared_k, shared_v, shared_raw, shared_out, shared_aug = forward[13:19]

    def collect(mine, cross, third):
        mine = lax.ppermute(mine, COLUMN, KEEP)
        cross = lax.ppermute(cross, COLUMN, CROSS)
        third = lax.ppermute(third, COLUMN, KEEP)
        return jnp.stack([jnp.where(zq == 0, mine, cross), jnp.where(zq == 0, cross, mine), third])

    out_keep, out_cross, out_third, middle_grad, grad, shared_grad, packed, second_gain_grad = dense(
        out, shared_out, own_tokens, grad_tokens, out_matrix, gain_second, bounds, up_half, down_half
    )
    output = collect(out_keep, out_cross, out_third)

    def reduce(grad):
        return lax.psum(lax.psum_scatter(grad, rows, scatter_dimension=0, tiled=True), SEQ).astype(F32)

    eighth = model // 8
    if square:
        size = packed.shape[1]
        mine = lax.psum_scatter(packed.reshape(4 * size, model), "chip", scatter_dimension=0, tiled=True)
        mine = lax.psum(mine, SEQ)
        down_out = mine[:tile].astype(F32)
        up_mine = mine[tile : 2 * tile].reshape(2, 2, shard, 2, tile).transpose(1, 2, 0, 3, 4)
        up_mine = up_mine.reshape(2, shard, 4, tile)
        outw_mine = mine[2 * tile :].reshape(shard, 2, width).transpose(1, 0, 2)
        up_other = swap(pick(up_mine, 1 - core).reshape(shard, 4 * tile), "core").reshape(shard, 4, tile)
        outw_other = swap(pick(outw_mine, 1 - core), "core")
        up_mine, outw_mine = pick(up_mine, core), pick(outw_mine, core)
        low = jnp.where(core == 0, up_mine, up_other)
        high = jnp.where(core == 0, up_other, up_mine)
        up_out = jnp.stack([low, high], axis=2).reshape(shard, hidden).astype(F32)
        low = jnp.where(core == 0, outw_mine, outw_other)
        high = jnp.where(core == 0, outw_other, outw_mine)
        outw_out = jnp.concatenate([low, high], axis=1).astype(F32)
    else:
        own_core = jnp.arange(2) == core
        down_grad = packed[:, None, :tile]
        down_out = reduce(jnp.where(own_core[None, :, None, None], down_grad, 0).reshape(hidden, model))
        up_grad = packed[:, tile : 2 * tile].reshape(4, 2, 2 * eighth, 2, tile).transpose(0, 2, 1, 3, 4)
        up_grad = up_grad.reshape(model, 4, 1, tile)
        up_out = reduce(jnp.where(own_core[None, None, :, None], up_grad, 0).reshape(model, hidden))
        out_grad = packed[:, 2 * tile :].reshape(4, eighth, 2, width).transpose(0, 2, 1, 3)
        out_grad = out_grad.reshape(model, 1, width)
        outw_out = reduce(jnp.where(own_core[None, :, None], out_grad, 0).reshape(model, model))

    shared_dq, part_k, part_v, shared_qgg, _ = attend_back(
        shared_aug, shared_k, shared_v, shared_out, shared_grad, shared_raw, gain_query, gain_key,
        bounds[1], pics,
    )

    def to_side(array):
        return swap(pick(array.reshape(2, 2, part, width), 1 - zq, 1), "zq").reshape(half, width)

    got_k, got_v = to_side(part_k), to_side(part_v)
    dq, dk, dv, qgg, kgg = attend_back(
        aug, k, v, out, grad, raw, gain_query, gain_key, bounds[0], pics
    )
    shared_dk, shared_dv, shared_kgg = shared_keys(part_k, part_v, got_k, got_v, shared_raw, gain_key)
    mixed = jnp.concatenate(
        [jnp.concatenate([dq, shared_dq]), jnp.concatenate([dk, shared_dk]), jnp.concatenate([dv, shared_dv])],
        axis=1,
    )
    own_shared = pick(shared_normed.reshape(2, 2, part, model), zq, 1).reshape(half, model)
    mix_grad = tn(jnp.concatenate([normed, own_shared]), mixed).astype(BF16)
    partial = nt(mixed, mix_half)
    row_partial = partial[:length].reshape(2, half, model)
    shared_partial = partial[length:].reshape(2, part, model)
    mine = jnp.concatenate([pick(row_partial, core), pick(shared_partial, core)])
    sent = jnp.concatenate([pick(row_partial, 1 - core), pick(shared_partial, 1 - core)])
    normed_grad = mine + swap(sent.astype(BF16), "core").astype(F32)
    n_first, r_first = norm_parts(own_tokens.astype(F32))
    input_part, first_gain_grad = norm_back(normed_grad, n_first, r_first, gain_first)
    input_grad = (middle_grad + input_part).astype(BF16)

    def place_heads(values):
        return jnp.where(jnp.arange(2)[:, None] == core, values, 0.0).reshape(1, model)

    gain_grads = jnp.concatenate(
        [first_gain_grad, place_heads(qgg + shared_qgg), place_heads(kgg + shared_kgg), second_gain_grad]
    )
    gain_grads = gain_grads.reshape(4, 2 * chips, shard).transpose(1, 0, 2).astype(BF16)
    if square:
        gain_rows = jnp.pad(gain_grads, ((0, 0), (0, 12), (0, 3 * width - shard)))
        payload = jnp.concatenate([mix_grad.reshape(2 * chips, shard, 3 * width), gain_rows], axis=1)
        input_out, mix_out, gains_out = finish(input_grad, payload)
        gains_out = gains_out[:4, :shard]
    else:
        first, second = input_grad[:part], input_grad[part:half]
        input_out = collect(
            jnp.where(zq == 0, first, second), jnp.where(zq == 0, second, first), input_grad[half:]
        )
        spread_mix = jnp.where(
            jnp.arange(2)[None, None, :, None] == core, mix_grad.reshape(model, 3, 1, width), 0
        ).reshape(model, 6 * width)
        mix_out = reduce(spread_mix)
        gains_out = reduce(gain_grads).reshape(4, shard)
    return (
        output, input_out, gains_out[0], mix_out, gains_out[1], gains_out[2], outw_out, gains_out[3],
        up_out, down_out,
    )


def solution(mesh):
    fsdp = mesh.shape["fsdp"]
    split = Mesh(mesh.devices.reshape(fsdp // 2, 2, 2, 2), ("chip", "core", "zp", "zq"))
    rows = ("chip", "core")
    return jax.shard_map(
        local,
        mesh=split,
        in_specs=(
            P(rows, SEQ, None),
            P(rows, None),
            P(rows, SEQ),
            P(rows),
            P(rows, None),
            P(rows),
            P(rows),
            P(rows, None),
            P(rows),
            P(rows, None),
            P(rows, None),
            P(rows, SEQ, None),
        ),
        out_specs=(
            P(rows, SEQ, None),
            P(rows, SEQ, None),
            P(rows),
            P(rows, None),
            P(rows),
            P(rows),
            P(rows, None),
            P(rows),
            P(rows, None),
            P(rows, None),
        ),
        check_vma=False,
    )
```

```python
import functools

import jax
import jax.numpy as jnp
from jax import lax
from jax.experimental import pallas as pl
from jax.experimental.pallas import tpu as pltpu
from jax.sharding import Mesh, PartitionSpec as P

HEADS = 12
HEAD = 64
EPSILON = 1e-06
BLOCK = 256
STEP = 512
MARK = 32.0
EXP2_FACTOR = HEAD**-0.5 * 1.4426950408889634
F32 = jnp.float32
BF16 = jnp.bfloat16
VMEM_LIMIT = 56 * 1024 * 1024

SEQ = ("zp", "zq")
COLUMN = ("core", "zp", "zq")
KEEP = [
    (core * 4 + z, (z // 2) * 4 + 2 * core + z % 2) for core in range(2) for z in range(4)
]
CROSS = [
    (core * 4 + z, (z // 2) * 4 + 2 * core + 1 - z % 2) for core in range(2) for z in range(4)
]


def swap(array, name, bit=1):
    count = lax.axis_size(name)
    return lax.ppermute(array, name, [(i, i ^ bit) for i in range(count)])


def pick(array, index, axis=0):
    return lax.dynamic_index_in_dim(array, index, axis, keepdims=False)


def group_ones(scale):
    row = lax.broadcasted_iota(jnp.int32, (128, 128), 0) // HEAD
    column = lax.broadcasted_iota(jnp.int32, (128, 128), 1) // HEAD
    return jnp.where(row == column, scale, 0.0).astype(BF16)


def group_sum(values, ones):
    return jnp.dot(values.astype(BF16), ones, preferred_element_type=F32)


def group_sum_fine(values, ones):
    high = values.astype(BF16)
    return group_sum(high, ones) + group_sum(values - high.astype(F32), ones)


def project_kernel(x_ref, gain_ref, weight_ref, qg_ref, kg_ref, normed_ref, q_ref, k_ref, v_ref, raw_ref):
    width = q_ref.shape[1]
    x = x_ref[...].astype(F32)
    center = x - jnp.mean(x, axis=-1, keepdims=True)
    spread = jnp.mean(center * center, axis=-1, keepdims=True)
    normed = (center * lax.rsqrt(spread + EPSILON) * gain_ref[...]).astype(BF16)
    normed_ref[...] = normed
    mixed = jnp.dot(normed, weight_ref[...], preferred_element_type=F32)
    raw_ref[...] = mixed[:, : 2 * width].astype(BF16)
    ones = group_ones(1.0 / HEAD)
    for part, (out_ref, g_ref) in enumerate(((q_ref, qg_ref), (k_ref, kg_ref))):
        for at in range(0, width, 128):
            raw = mixed[:, part * width + at : part * width + at + 128]
            c = raw - group_sum_fine(raw, ones)
            n = c * lax.rsqrt(group_sum(c * c, ones) + EPSILON)
            out_ref[:, at : at + 128] = (n * g_ref[:, at : at + 128]).astype(BF16)
    v_ref[...] = mixed[:, 2 * width :].astype(BF16)


def nt(a, b):
    return lax.dot_general(a, b, (((1,), (1,)), ((), ())), preferred_element_type=F32)


def tn(a, b):
    return lax.dot_general(a, b, (((0,), (0,)), ((), ())), preferred_element_type=F32)


def slots(queries, length, part):
    at = lax.broadcasted_iota(jnp.int32, (queries, 128), 0)
    if queries == length:
        return at
    return at % part + part * (lax.axis_index("zq") + 2 * (at // part))


def own_rows(ref, start, count, queries, part):
    if queries == ref.shape[0]:
        return ref[pl.ds(start, count), :]
    zq = lax.axis_index("zq")
    pieces = [
        ref[pl.ds(pl.multiple_of((zq + 2 * i) * part, part), part), :]
        for i in range(start // part, (start + count) // part)
    ]
    return jnp.concatenate(pieces, axis=0)


def query_marks(bounds_ref, place, queries, length, part, pics):
    at = slots(queries, length, part)
    inside = (at >= bounds_ref[0:1, :]) & (at < bounds_ref[2:3, :])
    values = jnp.where(inside, MARK, 0.0)
    return jnp.where(place == pics, MARK, values).astype(BF16)


def key_marks(bounds_ref, place, length, pics):
    at = lax.broadcasted_iota(jnp.int32, (length, 128), 0)
    inside = (at >= bounds_ref[0:1, :]) & (at < bounds_ref[1:2, :])
    values = jnp.where(inside, MARK, 0.0)
    values = jnp.where(place == pics, -MARK, values)
    return jnp.where((place > pics) & (place < pics + 4), 1.0, values).astype(BF16)


def attend_kernel(pics, q_ref, k_ref, v_ref, bounds_ref, out_ref, aug_ref, kaug, vaug, qaug):
    length = k_ref.shape[0]
    queries = out_ref.shape[0]
    part = length // 4
    lane = lax.broadcasted_iota(jnp.int32, (1, 128), 1)
    place = lane % HEAD
    sides = [lane < HEAD, lane >= HEAD]
    kmarks = key_marks(bounds_ref, place, length, pics)
    qmarks = query_marks(bounds_ref, place, queries, length, part, pics)
    qaug[...] = qmarks
    for h in range(2):
        kaug[h] = jnp.where(sides[h], k_ref[...], kmarks)
        vaug[h] = jnp.where(sides[h], v_ref[...], jnp.ones_like(v_ref))
    for b in range(queries // STEP):
        rows = pl.ds(b * STEP, STEP)
        mine = own_rows(q_ref, b * STEP, STEP, queries, part)
        query = [jnp.where(sides[h], mine, qaug[rows, :]) for h in range(2)]
        total = [jnp.zeros((STEP, 128), F32)] * 2
        for j in range(length // STEP):
            keys = pl.ds(j * STEP, STEP)
            scores = [nt(query[h], kaug[h, keys, :]) for h in range(2)]
            weights = [jnp.exp2(x * EXP2_FACTOR).astype(BF16) for x in scores]
            total = [
                total[h] + jnp.dot(weights[h], vaug[h, keys, :], preferred_element_type=F32) for h in range(2)
            ]
        results = []
        for h in range(2):
            results.append(total[h] / pltpu.roll(total[h], HEAD, 1))
            log_total = jnp.log(jnp.where(sides[h], 1.0, total[h])) * -(HEAD**0.5)
            first = log_total.astype(BF16)
            rest = log_total - first.astype(F32)
            middle = rest.astype(BF16)
            last = (rest - middle.astype(F32)).astype(BF16)
            logs = jnp.where(place == pics + 1, first, jnp.where(place == pics + 2, middle, last))
            slot = jnp.logical_not(sides[h]) & (place > pics) & (place < pics + 4)
            aug_ref[h, rows, :] = jnp.where(slot, logs, query[h])
        out_ref[rows, :] = jnp.where(sides[0], results[0], results[1]).astype(BF16)


def head_norm_back(e, raw, gain, means):
    raw = raw.astype(F32)
    c = raw - group_sum(raw, means)
    r = lax.rsqrt(group_sum(c * c, means) + EPSILON)
    n = c * r
    t = e * gain
    grad = r * (t - group_sum(t, means) - n * group_sum(t * n, means))
    return grad.astype(BF16), jnp.sum(e * n, axis=0, keepdims=True)


def attend_back_kernel(
    pics, aug_ref, k_ref, v_ref, out_ref, do_ref, rawq_ref, rawk_ref, qg_ref, kg_ref, bounds_ref,
    dq_ref, dk_ref, dv_ref, qgg_ref, kgg_ref, kaug, vaug, doaug, qsum, ksum,
):
    length = k_ref.shape[0]
    queries = do_ref.shape[0]
    part = length // 4
    whole = queries == length
    lane = lax.broadcasted_iota(jnp.int32, (1, 128), 1)
    place = lane % HEAD
    sides = [lane < HEAD, lane >= HEAD]
    kmarks = key_marks(bounds_ref, place, length, pics)
    vmarks = jnp.where(place < 2, 1.0, 0.0).astype(BF16)
    ones = group_ones(1.0)
    inner = group_sum_fine(do_ref[...].astype(F32) * out_ref[...].astype(F32), ones)
    inner = -pltpu.roll(inner, HEAD, 1)
    inner_high = inner.astype(BF16)
    inner_low = (inner - inner_high.astype(F32)).astype(BF16)
    zero = jnp.zeros((), BF16)
    gmarks = jnp.where(place == 0, inner_high, jnp.where(place == 1, inner_low, zero))
    for h in range(2):
        kaug[h] = jnp.where(sides[h], k_ref[...], kmarks)
        vaug[h] = jnp.where(sides[h], v_ref[...], vmarks)
        doaug[h] = jnp.where(sides[h], do_ref[...], gmarks)
    for b in range(length // STEP):
        keys = pl.ds(b * STEP, STEP)
        key = [kaug[h, keys, :] for h in range(2)]
        value = [vaug[h, keys, :] for h in range(2)]
        dk = [jnp.zeros((STEP, 128), F32)] * 2
        dv = [jnp.zeros((STEP, 128), F32)] * 2
        for j in range(queries // STEP):
            rows = pl.ds(j * STEP, STEP)
            query = [aug_ref[h, rows, :] for h in range(2)]
            grad = [doaug[h, rows, :] for h in range(2)]
            scores = [nt(key[h], query[h]) for h in range(2)]
            soft_grad = [nt(value[h], grad[h]) for h in range(2)]
            weights = [jnp.exp2(x * EXP2_FACTOR) for x in scores]
            score_grad = [(weights[h] * soft_grad[h]).astype(BF16) for h in range(2)]
            for h in range(2):
                part_sum = tn(score_grad[h], key[h])
                if b == 0:
                    qsum[h, rows, :] = part_sum
                else:
                    qsum[h, rows, :] += part_sum
                dk[h] = dk[h] + jnp.dot(score_grad[h], query[h], preferred_element_type=F32)
                dv[h] = dv[h] + jnp.dot(weights[h].astype(BF16), grad[h], preferred_element_type=F32)
        ksum[keys, :] = jnp.where(sides[0], dk[0], dk[1]) * HEAD**-0.5
        dv_ref[keys, :] = jnp.where(sides[0], dv[0], dv[1]).astype(BF16)

    means = group_ones(1.0 / HEAD)
    gain_sum = jnp.zeros((1, 128), F32)
    for b in range(queries // part):
        rows = pl.ds(b * part, part)
        e = jnp.where(sides[0], qsum[0, rows, :], qsum[1, rows, :]) * HEAD**-0.5
        raw = own_rows(rawq_ref, b * part, part, queries, part)
        dq_ref[rows, :], more = head_norm_back(e.astype(BF16).astype(F32), raw, qg_ref[...], means)
        gain_sum = gain_sum + more
    qgg_ref[...] = gain_sum
    gain_sum = jnp.zeros((1, 128), F32)
    for b in range(length // part):
        rows = pl.ds(b * part, part)
        e = ksum[rows, :].astype(BF16)
        if whole:
            dk_ref[rows, :], more = head_norm_back(e.astype(F32), rawk_ref[rows, :], kg_ref[...], means)
            gain_sum = gain_sum + more
        else:
            dk_ref[rows, :] = e
    kgg_ref[...] = gain_sum


def shared_keys_kernel(dk_ref, dv_ref, gotk_ref, gotv_ref, rawk_ref, kg_ref, outk_ref, outv_ref, kgg_ref):
    count = outk_ref.shape[0]
    part = count // 2
    means = group_ones(1.0 / HEAD)
    gain_sum = jnp.zeros((1, 128), F32)
    for b in range(2):
        rows = pl.ds(b * part, part)
        own = lambda ref: own_rows(ref, b * part, part, count, part)
        e = own(dk_ref).astype(F32) + gotk_ref[rows, :].astype(F32)
        outk_ref[rows, :], more = head_norm_back(e, own(rawk_ref), kg_ref[...], means)
        gain_sum = gain_sum + more
        outv_ref[rows, :] = (own(dv_ref).astype(F32) + gotv_ref[rows, :].astype(F32)).astype(BF16)
    kgg_ref[...] = gain_sum


def gelu_pair(h):
    size = jnp.abs(h)
    bell = jnp.exp2(h * h * -0.7213475204444817)
    t = 1.0 / (1.0 + 0.23164189 * size)
    series = t * (0.127414796 + t * (-0.142248368 + t * (0.7107068705 + t * (-0.7265760135 + t * 0.5307027145))))
    tail = series * bell
    below = jnp.where(h < 0.0, tail, 1.0 - tail)
    return h * below, below + h * (bell * 0.3989422804014327)


def norm_parts(values):
    center = values - jnp.mean(values, axis=-1, keepdims=True)
    spread = lax.rsqrt(jnp.mean(center * center, axis=-1, keepdims=True) + EPSILON)
    return center * spread, spread


def norm_back(upstream, n, r, gain):
    t = upstream * gain
    grad = r * (t - jnp.mean(t, axis=-1, keepdims=True) - n * jnp.mean(t * n, axis=-1, keepdims=True))
    return grad, jnp.sum(upstream * n, axis=0, keepdims=True)


MESH_ID = pl.DeviceIdType.MESH


def here():
    return lax.axis_index("chip"), lax.axis_index("core"), lax.axis_index("zp"), lax.axis_index("zq")


def remote(source, target, sems, at, device):
    sent, got = sems
    return pltpu.make_async_remote_copy(
        src_ref=source, dst_ref=target, send_sem=sent.at[at], recv_sem=got.at[at],
        device_id=device, device_id_type=MESH_ID,
    )


def greet(devices, maybe=None, moves=None):
    barrier = pltpu.get_barrier_semaphore()
    for device in devices:
        pl.semaphore_signal(barrier, inc=1, device_id=device, device_id_type=MESH_ID)
    if maybe is None:
        pl.semaphore_wait(barrier, len(devices))
        return

    @pl.when(moves)
    def _():
        pl.semaphore_signal(barrier, inc=1, device_id=maybe, device_id_type=MESH_ID)

    pl.semaphore_wait(barrier, len(devices) + jnp.where(moves, 1, 0))


def rows_at(start, count):
    return pl.ds(pl.multiple_of(start, 16), count)


def write_bounds(pics, lens_ref, bounds_ref, zp, zq, length):
    lane = lax.broadcasted_iota(jnp.int32, (8, 128), 1)
    lens = jnp.where(zp == 0, lens_ref[0], lens_ref[1])
    ends = lens
    for hop in (1, 2, 4, 8):
        ends = ends + jnp.where(lane >= hop, pltpu.roll(ends, hop, 1), 0)
    starts = ends - lens
    last = (lens > 0) & (pltpu.roll(lens, 127, 1) == 0)
    query_ends = jnp.where(last, length, ends)
    total = jnp.max(jnp.where(lane < pics, ends, 0), axis=1, keepdims=True)

    def both(values):
        values = jnp.where(lane < HEAD, jnp.where(lane < pics, values, 2 * length), 0)
        return values + pltpu.roll(values, HEAD, 1)

    tables = [both(starts), both(ends), both(query_ends), jnp.broadcast_to(total, (8, 128))]
    for t in range(4):
        table = tables[t]
        bounds_ref[0, t : t + 1, :] = jnp.where(zq == 0, table[0:1], table[1:2])
        bounds_ref[1, t : t + 1, :] = table[2:3]
    bounds_ref[:, 4:, :] = jnp.zeros((2, 4, 128), jnp.int32)


def forward_kernel(square, pics, *refs):
    refs = list(refs)
    take = lambda count: [refs.pop(0) for _ in range(count)]
    tokens_ref, cot_ref, lens_ref, mix_ref, gains_ref = take(5)
    if square:
        up_ref, down_ref, outw_ref = take(3)
    else:
        gain_first, gain_query, gain_key = take(3)
    x_out, bounds_ref, mix_hbm, second_ref, query_out, key_out, cot_hbm = take(7)
    names = ("normed", "k", "v", "raw", "out", "aug")
    outs = [dict(zip(names, take(6))) for _ in range(2)]
    if square:
        up_hbm, down_hbm, outw_hbm = take(3)
    row_ref, shared_ref, cot_out, lens_out = take(4)
    scratch = [dict(zip(names + ("q",), take(7))) for _ in range(2)]
    kaug, vaug, qaug = take(3)
    if square:
        mix_out, gains_out, gain_first, gain_query, gain_key, up_out, down_out, outw_out = take(8)
    sent, got, local_sem, write_sem = take(4)

    chip, core, zp, zq = here()
    z = 2 * zp + zq
    part = tokens_ref.shape[1]
    half, length = 2 * part, 4 * part
    sems = (sent, got)
    partner = (chip, 1 - core, zp, zq)
    side = (chip, core, zp, 1 - zq)
    keep = (chip, zp, core, zq)
    cross = (chip, zp, core, 1 - zq)
    moves = core != zp
    near_x = (chip ^ 1, core, zp, zq)
    near_y = (chip ^ 2, core, zp, zq)
    greet([partner, side, cross] + ([near_x, near_y] if square else []), keep, moves)

    def quarter(ref, index):
        return ref.at[rows_at(index * part, part)]

    own_row = remote(tokens_ref.at[zq], quarter(row_ref, z), sems, 0, keep)
    own_shared = remote(tokens_ref.at[2], quarter(shared_ref, z), sems, 2, keep)
    stay_row = pltpu.make_async_copy(tokens_ref.at[zq], quarter(row_ref, z), local_sem.at[0])
    stay_shared = pltpu.make_async_copy(tokens_ref.at[2], quarter(shared_ref, z), local_sem.at[1])

    @pl.when(moves)
    def _():
        own_row.start()

    @pl.when(jnp.logical_not(moves))
    def _():
        stay_row.start()

    cross_row = remote(tokens_ref.at[1 - zq], quarter(row_ref, z), sems, 1, cross)
    cross_row.start()

    @pl.when(moves)
    def _():
        own_shared.start()

    @pl.when(jnp.logical_not(moves))
    def _():
        stay_shared.start()

    lens_copy = remote(lens_ref, lens_out.at[core], sems, 8, partner)
    lens_copy.start()
    lens_stay = pltpu.make_async_copy(lens_ref, lens_out.at[core], local_sem.at[2])
    lens_stay.start()
    waits = []
    if square:
        shard = mix_ref.shape[1]
        down_rows = down_ref.shape[0]
        mine, theirs = 2 * chip + core, 2 * chip + 1 - core
        slot = [9]

        def send(source, target, device):
            copy = remote(source, target, sems, slot[0], device)
            slot[0] += 1
            copy.start()
            waits.append(copy)
            return copy

        def stay(source, target, at):
            copy = pltpu.make_async_copy(source, target, local_sem.at[at])
            copy.start()
            return copy

        def block(ref, start, count):
            return ref.at[rows_at(start, count)]

        mix_piece = lambda index: (block(mix_out, index * shard, shard), gains_out.at[index])

        def send_mix(sources, index, device):
            return [send(source, target, device) for source, target in zip(sources, mix_piece(index))]

        def arrived(copies):
            for copy in copies:
                copy.wait_recv()

        x_mine, y_other = 2 * (chip ^ 1) + core, 2 * (chip ^ 2) + 1 - core
        to_core = send_mix((mix_ref.at[1 - core], gains_ref), mine, partner)
        a_x = send_mix((mix_ref.at[core], gains_ref), mine, near_x)
        a_y = send_mix((mix_ref.at[core], gains_ref), mine, near_y)
        up_core = send(up_ref.at[1 - core], block(up_out, mine * shard, shard), partner)
        out_core = send(outw_ref, block(outw_out, mine * shard, shard), partner)
        stays = [
            stay(mix_ref.at[core], mix_piece(mine)[0], 3),
            stay(gains_ref, gains_out.at[mine], 4),
            stay(up_ref.at[core], block(up_out, mine * shard, shard), 5),
            stay(down_ref, block(down_out, chip * down_rows, down_rows), 6),
            stay(outw_ref, block(outw_out, mine * shard, shard), 7),
        ]
        arrived(to_core)
        b_x = send_mix(mix_piece(theirs), theirs, near_x)
        b_y = send_mix(mix_piece(theirs), theirs, near_y)
        arrived(a_x)
        a_far = send_mix(mix_piece(x_mine), x_mine, near_y)
        arrived(b_y)
        b_far = send_mix(mix_piece(y_other), y_other, near_x)
        for copy in stays:
            copy.wait()
        arrived([up_core])
        dhalf, ohalf = down_rows // 2, shard // 2

        def bundle(first, from_chip):
            same, twin = 2 * from_chip + core, 2 * from_chip + 1 - core
            part_of = 0 if first else 1
            return [
                block(up_out, (same if first else twin) * shard, shard),
                block(down_out, from_chip * down_rows + part_of * dhalf, dhalf),
                block(outw_out, same * shard + part_of * ohalf, ohalf),
            ]

        def send_bundle(first, from_chip, device):
            return [send(ref, ref, device) for ref in bundle(first, from_chip)]

        first_x = send_bundle(True, chip, near_x)
        first_y = send_bundle(True, chip, near_y)
        second_x = send_bundle(False, chip, near_x)
        second_y = send_bundle(False, chip, near_y)

    lens_copy.wait()
    lens_stay.wait()
    write_bounds(pics, lens_out, bounds_ref, zp, zq, length)
    if square:
        arrived(a_y + b_x + a_far + b_far)
        for p in range(gains_out.shape[0]):
            lanes = slice(p * shard, (p + 1) * shard)
            values = gains_out[p, :, :shard].astype(F32)
            gain_first[:, lanes] = values[0:1]
            second_ref[:, lanes] = values[3:4]
            half_pieces = gains_out.shape[0] // 2

            @pl.when(core == p // half_pieces)
            def _():
                at = (p % half_pieces) * shard
                gain_query[:, at : at + shard] = values[1:2]
                gain_key[:, at : at + shard] = values[2:3]
        weight = mix_out
    else:
        weight = mix_ref
        second_ref[...] = jnp.zeros_like(second_ref)
    writes = []

    def write(source, target, at):
        copy = pltpu.make_async_copy(source, target, write_sem.at[at])
        copy.start()
        writes.append(copy)

    query_out[0] = gain_query[...]
    query_out[1] = gain_first[:, : gain_query.shape[1]]
    key_out[0] = gain_key[...]
    key_out[1] = gain_first[:, gain_query.shape[1] :]
    write(weight, mix_hbm, 0)

    @pl.when(moves)
    def _():
        own_row.wait_recv()

    @pl.when(jnp.logical_not(moves))
    def _():
        stay_row.wait()

    first, second = 2 * core + zq, 2 * core + 1 - zq
    row_one = remote(quarter(row_ref, first), quarter(row_ref, first), sems, 3, partner)
    row_one.start()
    cross_row.wait_recv()
    row_two = remote(quarter(row_ref, second), quarter(row_ref, second), sems, 4, partner)
    row_two.start()

    def project(tokens, bufs):
        def one(i, _):
            rows = pl.ds(pl.multiple_of(i * BLOCK, BLOCK), BLOCK)
            project_kernel(
                tokens.at[rows], gain_first, weight, gain_query, gain_key, bufs["normed"].at[rows],
                bufs["q"].at[rows], bufs["k"].at[rows], bufs["v"].at[rows], bufs["raw"].at[rows],
            )
            return 0

        lax.fori_loop(0, length // BLOCK, one, 0)

    def attend(bufs, bounds):
        def one(p, _):
            lanes = pl.ds(pl.multiple_of(p * 128, 128), 128)
            attend_kernel(
                pics, bufs["q"].at[:, lanes], bufs["k"].at[:, lanes], bufs["v"].at[:, lanes], bounds,
                bufs["out"].at[:, lanes], bufs["aug"].at[pl.ds(2 * p, 2)], kaug, vaug, qaug.at[pl.ds(0, bufs["out"].shape[0])],
            )
            return 0

        lax.fori_loop(0, gain_query.shape[1] // 128, one, 0)

    row_one.wait_recv()
    row_two.wait_recv()
    project(row_ref, scratch[0])
    for i, name in enumerate(("normed", "k", "v", "raw")):
        write(scratch[0][name], outs[0][name], 1 + i)
    write(row_ref.at[rows_at(core * half, half)], x_out.at[pl.ds(0, half)], 5)

    @pl.when(moves)
    def _():
        own_shared.wait_recv()

    @pl.when(jnp.logical_not(moves))
    def _():
        stay_shared.wait()

    to_side = remote(quarter(shared_ref, first), quarter(shared_ref, first), sems, 5, side)
    to_side.start()
    shared_one = remote(quarter(shared_ref, first), quarter(shared_ref, first), sems, 6, partner)
    shared_one.start()
    cot_own = pl.ds(pl.multiple_of(zq * part, part), part)
    cot_shared = pl.ds(half, part)
    cot_moves = [
        remote(cot_ref.at[zq], cot_out.at[cot_own], sems, 46, keep),
        remote(cot_ref.at[2], cot_out.at[cot_shared], sems, 47, keep),
    ]
    cot_stays = [
        pltpu.make_async_copy(cot_ref.at[zq], cot_out.at[cot_own], local_sem.at[0]),
        pltpu.make_async_copy(cot_ref.at[2], cot_out.at[cot_shared], local_sem.at[1]),
    ]
    cot_cross = remote(cot_ref.at[1 - zq], cot_out.at[cot_own], sems, 48, cross)

    @pl.when(moves)
    def _():
        for copy in cot_moves:
            copy.start()

    @pl.when(jnp.logical_not(moves))
    def _():
        for copy in cot_stays:
            copy.start()

    cot_cross.start()
    attend(scratch[0], bounds_ref.at[0])
    write(scratch[0]["out"], outs[0]["out"], 6)
    write(scratch[0]["aug"], outs[0]["aug"], 7)
    to_side.wait_recv()
    shared_two = remote(quarter(shared_ref, second), quarter(shared_ref, second), sems, 7, partner)
    shared_two.start()
    if square:
        arrived(first_x + second_y)
        far_first = send_bundle(True, chip ^ 1, near_y)
        far_second = send_bundle(False, chip ^ 2, near_x)
    shared_one.wait_recv()
    shared_two.wait_recv()
    project(shared_ref, scratch[1])
    for i, name in enumerate(("normed", "k", "v", "raw")):
        write(scratch[1][name], outs[1][name], 8 + i)
    write(shared_ref.at[rows_at(first * part, part)], x_out.at[pl.ds(half, part)], 12)
    attend(scratch[1], bounds_ref.at[1])
    write(scratch[1]["out"], outs[1]["out"], 13)
    write(scratch[1]["aug"], outs[1]["aug"], 14)

    if square:
        arrived(first_y + second_x + far_first + far_second)
        sent_pieces = []
        for c in (chip ^ 1, chip ^ 2, chip ^ 3):
            target = block(outw_out, (2 * c + core) * shard, shard)
            sent_pieces.append(send(target, target, partner))
        write(up_out, up_hbm, 15)
        write(down_out, down_hbm, 16)
        arrived(sent_pieces + [out_core])
        write(outw_out, outw_hbm, 17)
        for copy in waits:
            copy.wait_send()
    cot_cross.wait()

    @pl.when(moves)
    def _():
        for copy in cot_moves:
            copy.wait()

    @pl.when(jnp.logical_not(moves))
    def _():
        for copy in cot_stays:
            copy.wait()

    write(cot_out, cot_hbm, 18)
    for copy in (row_one, row_two, shared_one, shared_two, to_side, cross_row):
        copy.wait_send()

    @pl.when(moves)
    def _():
        own_row.wait_send()
        own_shared.wait_send()

    for copy in writes:
        copy.wait()


def forward_pass(square, pics, tokens, cotangent, lens, mix, gains, *more):
    _, part, model = tokens.shape
    length, half, width = 4 * part, 2 * part, model // 2
    near = pl.BlockSpec(memory_space=pltpu.VMEM)
    anywhere = pl.BlockSpec(memory_space=pl.ANY)
    low = lambda *shape: (shape, BF16)
    wide = lambda *shape: (shape, F32)
    outs = [
        (low(3 * part, model), anywhere),
        (((2, 8, 128), jnp.int32), near),
        (low(model, 3 * width), anywhere),
        (wide(1, model), near),
        (wide(2, 1, width), near),
        (wide(2, 1, width), near),
        (low(3 * part, model), anywhere),
    ]
    bufs = []
    for queries in (length, half):
        shapes = [
            low(length, model), low(length, width), low(length, width), low(length, 2 * width),
            low(queries, width), low(2 * (width // 128), queries, 128),
        ]
        outs += [(shape, anywhere) for shape in shapes]
        bufs += shapes + [low(length, width)]
    scratch = [low(length, model), low(length, model), low(3 * part, model), ((2,) + lens.shape, jnp.int32)] + bufs
    scratch += [low(2, length, 128), low(2, length, 128), low(length, 128)]
    if square:
        up, down, outw = more
        landed = [low(model, up.shape[2]), low(4 * down.shape[0], model), low(model, model)]
        outs += [(shape, anywhere) for shape in landed]
        scratch += [low(model, 3 * width), low(8, *gains.shape), wide(1, model), wide(1, width), wide(1, width)]
        scratch += landed
    return pl.pallas_call(
        functools.partial(forward_kernel, square, pics),
        in_specs=[near] * (5 + len(more)),
        out_specs=[spec for _, spec in outs],
        out_shape=[jax.ShapeDtypeStruct(*shape) for shape, _ in outs],
        scratch_shapes=[pltpu.VMEM(*shape) for shape in scratch]
        + [
            pltpu.SemaphoreType.DMA((49,)),
            pltpu.SemaphoreType.DMA((49,)),
            pltpu.SemaphoreType.DMA((8,)),
            pltpu.SemaphoreType.DMA((19,)),
        ],
        compiler_params=pltpu.CompilerParams(
            collective_id=0, has_side_effects=True, vmem_limit_bytes=60 * 1024 * 1024
        ),
        name="forward_pass",
    )(tokens, cotangent, lens, mix, gains, *more)


def dense_kernel(
    out_ref, shared_ref, x, grad_ref, outw_ref, gain_ref,
    bounds_ref, up_ref, down_ref,
    out_keep, out_cross, out_third, midg_ref, row_grad, shared_grad, packed, gaing_ref,
    att_other, second, grad, hidden_all, pre_all, forward, backward, middle, ups, downs,
    parts_out, parts_in, heads_out, cols_out, cols_in, sent, got, tile_sem,
):
    chip, core, zp, zq = here()
    sems = (sent, got)
    partner = (chip, 1 - core, zp, zq)
    tokens, model = midg_ref.shape
    part = tokens // 3
    half = 2 * part
    width = out_ref.shape[1]
    tile = ups.shape[2]
    other = 1 - core
    mine, theirs = pl.ds(0, tokens), pl.ds(tokens, tokens)

    for i in range(4):
        pltpu.make_async_copy(up_ref.at[:, pl.ds(i * tile, tile)], ups.at[i], tile_sem.at[0, i]).start()
        pltpu.make_async_copy(down_ref.at[pl.ds(i * tile, tile)], downs.at[i], tile_sem.at[1, i]).start()
    greet([partner])
    att_sends = [
        remote(out_ref.at[rows_at(other * half, half)], att_other.at[pl.ds(0, half)], sems, 0, partner),
        remote(shared_ref.at[rows_at(other * part, part)], att_other.at[pl.ds(half, part)], sems, 1, partner),
    ]
    for copy in att_sends:
        copy.start()

    slot = lax.broadcasted_iota(jnp.int32, (part, 1), 0)
    filled, shared_filled = bounds_ref[0, 3:4, 0:1], bounds_ref[1, 3:4, 0:1]
    none = jnp.zeros((), BF16)
    for b, start, limit in (
        (0, 2 * core * part, filled),
        (1, (2 * core + 1) * part, filled),
        (2, (2 * core + zq) * part, shared_filled),
    ):
        rows = pl.ds(b * part, part)
        grad[rows, :] = jnp.where(slot + start < limit, grad_ref[rows, :], none)
    grad_send = remote(grad.at[mine], grad.at[theirs], sems, 2, partner)
    grad_send.start()

    own_rows_of = lambda b: (
        out_ref[rows_at(core * half + b * part, part), :] if b < 2 else shared_ref[rows_at(core * part, part), :]
    )
    own_weight = outw_ref[rows_at(core * width, width), :]
    other_weight = outw_ref[rows_at(other * width, width), :]
    blocks = [pl.ds(b * part, part) for b in range(3)]
    for b in range(3):
        middle[blocks[b], :] = x[blocks[b], :].astype(F32) + jnp.dot(
            own_rows_of(b), own_weight, preferred_element_type=F32
        )
    for copy in att_sends:
        copy.wait_recv()
    for rows in blocks:
        value = middle[rows, :] + jnp.dot(att_other[rows, :], other_weight, preferred_element_type=F32)
        middle[rows, :] = value
        second[rows, :] = (norm_parts(value)[0] * gain_ref[...]).astype(BF16)
    second_send = remote(second.at[mine], second.at[theirs], sems, 3, partner)
    second_send.start()
    forward[...] = jnp.zeros_like(forward)
    backward[...] = jnp.zeros_like(backward)
    second_send.wait_recv()
    grad_send.wait_recv()

    def one_tile(i, _):
        pltpu.make_async_copy(up_ref.at[:, pl.ds(0, tile)], ups.at[i], tile_sem.at[0, i]).wait()
        pltpu.make_async_copy(down_ref.at[pl.ds(0, tile)], downs.at[i], tile_sem.at[1, i]).wait()
        up, down = ups[i], downs[i]
        for rows in (mine, theirs):
            pre = jnp.dot(second[rows, :], up, preferred_element_type=F32)
            hidden, slope = gelu_pair(pre)
            hidden = hidden.astype(BF16)
            hidden_all[rows, :] = hidden
            forward[rows, :] += jnp.dot(hidden, down, preferred_element_type=F32)
            pre_grad = (nt(grad[rows, :], down) * slope).astype(BF16)
            pre_all[rows, :] = pre_grad
            backward[rows, :] += nt(pre_grad, up)
        packed[i, pl.ds(0, tile), :] = tn(hidden_all[...], grad[...]).astype(BF16)
        up_grad = tn(second[...], pre_all[...]).astype(BF16)
        quarter = model // 4
        for c in range(4):
            place = (rows_at(tile + (i // 2) * quarter, quarter), pl.ds(pl.multiple_of((i % 2) * tile, 128), tile))
            packed[c, place[0], place[1]] = up_grad[c * quarter : (c + 1) * quarter, :]
        return 0

    lax.fori_loop(0, 4, one_tile, 0)

    parts_out[0] = forward[theirs, :].astype(BF16)
    first_part = remote(parts_out.at[0], parts_in.at[0], sems, 4, partner)
    first_part.start()
    parts_out[1] = backward[theirs, :].astype(BF16)
    second_part = remote(parts_out.at[1], parts_in.at[1], sems, 5, partner)
    second_part.start()
    second_send.wait_send()
    first_part.wait_recv()
    for rows in blocks:
        value = middle[rows, :] + forward[rows, :] + parts_in[0, rows, :].astype(F32)
        forward[rows, :] = value
    out_keep[...] = forward[rows_at(zq * part, part), :].astype(BF16)
    out_cross[...] = forward[rows_at((1 - zq) * part, part), :].astype(BF16)
    out_third[...] = forward[pl.ds(half, part), :].astype(BF16)
    second_part.wait_recv()
    gain_sum = jnp.zeros(gaing_ref.shape, F32)
    for b in range(3):
        rows = blocks[b]
        n, r = norm_parts(middle[rows, :])
        upstream = backward[rows, :] + parts_in[1, rows, :].astype(F32)
        more, gain_more = norm_back(upstream, n, r, gain_ref[...])
        gain_sum = gain_sum + gain_more
        value = grad[rows, :].astype(F32) + more
        midg_ref[rows, :] = value
        branch = value.astype(BF16)
        second[rows, :] = branch
        heads_out[rows, :] = nt(branch, other_weight).astype(BF16)
    gaing_ref[...] = gain_sum
    head_sends = [
        remote(heads_out.at[pl.ds(0, half)], row_grad.at[rows_at(core * half, half)], sems, 6, partner),
        remote(heads_out.at[pl.ds(half, part)], shared_grad.at[rows_at(core * part, part)], sems, 7, partner),
    ]
    for copy in head_sends:
        copy.start()
    branch = second[mine, :]
    out_grads = [
        tn(out_ref[rows_at(core * half, half), :], second[pl.ds(0, half), :])
        + tn(shared_ref[rows_at(core * part, part), :], second[pl.ds(half, part), :]),
        tn(att_other[...], branch),
    ]
    for turn, heads in ((0, core), (1, other)):
        rows = rows_at(heads * width, width)
        forward[rows, :] = out_grads[turn]
    lanes = lambda side: pl.ds(pl.multiple_of(side * width, 128), width)
    cols_out[...] = forward[pl.ds(0, model), lanes(other)].astype(BF16)
    cols_send = remote(cols_out, cols_in, sems, 8, partner)
    cols_send.start()
    for b in range(3):
        value = nt(second[blocks[b], :], own_weight).astype(BF16)
        if b < 2:
            row_grad[rows_at(core * half + b * part, part), :] = value
        else:
            shared_grad[rows_at(core * part, part), :] = value
    cols_send.wait_recv()
    total = (forward[pl.ds(0, model), lanes(core)] + cols_in[...].astype(F32)).astype(BF16)
    eighth = model // 8
    filled_rows = 2 * tile + eighth
    packed[:, filled_rows:, :] = jnp.zeros((4, packed.shape[1] - filled_rows, model), BF16)
    for c in range(4):
        for h in range(2):
            at = (2 * c + h) * eighth
            packed[c, pl.ds(2 * tile, eighth), h * width : (h + 1) * width] = total[at : at + eighth, :]
    for copy in head_sends:
        copy.wait_recv()
    for copy in att_sends + head_sends + [grad_send, first_part, second_part, cols_send]:
        copy.wait_send()


def dense(out, shared_out, x, grad, out_matrix, gain, bounds, up, down):
    model = x.shape[1]
    tokens = x.shape[0]
    part = tokens // 3
    length, width = out.shape
    hidden = down.shape[0]
    tile = hidden // 4
    anywhere = pl.BlockSpec(memory_space=pl.ANY)
    near = pl.BlockSpec(memory_space=pltpu.VMEM)
    both = 2 * tokens
    return pl.pallas_call(
        dense_kernel,
        in_specs=[near] * 7 + [anywhere, anywhere],
        out_specs=[near] * 8,
        out_shape=[
            jax.ShapeDtypeStruct((part, model), BF16),
            jax.ShapeDtypeStruct((part, model), BF16),
            jax.ShapeDtypeStruct((part, model), BF16),
            jax.ShapeDtypeStruct((tokens, model), F32),
            jax.ShapeDtypeStruct((length, width), BF16),
            jax.ShapeDtypeStruct((length // 2, width), BF16),
            jax.ShapeDtypeStruct((4, -(-(2 * tile + model // 8) // 64) * 64, model), BF16),
            jax.ShapeDtypeStruct((1, model), F32),
        ],
        scratch_shapes=[
            pltpu.VMEM((tokens, width), BF16),
            pltpu.VMEM((both, model), BF16),
            pltpu.VMEM((both, model), BF16),
            pltpu.VMEM((both, tile), BF16),
            pltpu.VMEM((both, tile), BF16),
            pltpu.VMEM((both, model), F32),
            pltpu.VMEM((both, model), F32),
            pltpu.VMEM((tokens, model), F32),
            pltpu.VMEM((4, model, tile), BF16),
            pltpu.VMEM((4, tile, model), BF16),
            pltpu.VMEM((2, tokens, model), BF16),
            pltpu.VMEM((2, tokens, model), BF16),
            pltpu.VMEM((tokens, width), BF16),
            pltpu.VMEM((model, width), BF16),
            pltpu.VMEM((model, width), BF16),
            pltpu.SemaphoreType.DMA((9,)),
            pltpu.SemaphoreType.DMA((9,)),
            pltpu.SemaphoreType.DMA((2, 4)),
        ],
        compiler_params=pltpu.CompilerParams(
            collective_id=1, has_side_effects=True, vmem_limit_bytes=60 * 1024 * 1024
        ),
        cost_estimate=pl.CostEstimate(
            flops=32 * tokens * model * hidden, bytes_accessed=16 * model * hidden, transcendentals=0
        ),
        name="dense",
    )(out, shared_out, x, grad, out_matrix, gain, bounds, up, down)


def add(*terms):
    total = terms[0].astype(F32)
    for term in terms[1:]:
        total = total + term.astype(F32)
    return total


def backward_kernel(square, pics, *refs):
    refs = list(refs)
    take = lambda count: [refs.pop(0) for _ in range(count)]
    names = ("aug", "k", "v", "out", "do", "raw", "normed")
    row_in = dict(zip(names, take(7)))
    shared_in = dict(zip(names, take(7)))
    mix_in, x_in, midg_in, gain_first, gain_query, gain_key, gain_second_grad, bounds_ref = take(8)
    if square:
        packed_in, keep_in, cross_in, third_in = take(4)
        output_ref, grad_out, total_ref, gains_ref, up_ref, down_ref, outw_ref = take(7)
    else:
        grad_own, mix_grad_ref, gains_sum = take(3)
    names = names[:-1]
    row = dict(zip(names, take(6)))
    shared = dict(zip(names, take(6)))
    normed, weight, x, midg = take(4)
    kaug, vaug, doaug, qsum, ksum, mixed, part_k, part_v, got_k, got_v = take(10)
    gain_sums, parts_out, parts_in = take(3)
    if square:
        grad_own, payload, gains_sum = take(3)
        held, far_in, onward_out, onward_in, direct_in, line, near_in, second_sum, far_quarter, whole_line = take(10)
        up_out, up_got, outw_out, outw_got = take(4)
        relay, final, core_got, chunks, gain_parts, chunk_got, gain_got = take(7)
    sent, got, load_sem, local_sem = take(4)

    chip, core, zp, zq = here()
    z = 2 * zp + zq
    sems = (sent, got)
    partner = (chip, 1 - core, zp, zq)
    keep = (chip, zp, core, zq)
    cross = (chip, zp, core, 1 - zq)
    moves = core != zp
    near_x = (chip ^ 1, core, zp, zq)
    near_y = (chip ^ 2, core, zp, zq)
    along = [(chip, core, zp, 1 - zq), (chip, core, 1 - zp, zq), (chip, core, 1 - zp, 1 - zq)]
    tokens, model = x.shape
    part = tokens // 3
    half, length = 2 * part, 4 * part
    width = model // 2
    queries = half
    waits = []

    def load(source, target, at):
        copy = pltpu.make_async_copy(source, target, load_sem.at[at])
        copy.start()
        return copy

    def send(source, target, at, device):
        copy = remote(source, target, sems, at, device)
        copy.start()
        waits.append(copy)
        return copy

    if square:
        rows_count = packed_in.shape[1]
        span = rows_count // 2
        first_half, second_half = pl.ds(0, span), pl.ds(span, span)
        held_loads = [
            load(packed_in.at[chip ^ 1, first_half], held.at[0], 24),
            load(packed_in.at[chip ^ 2, second_half], held.at[1], 25),
            load(packed_in.at[chip, first_half], held.at[2], 26),
            load(packed_in.at[chip, second_half], held.at[3], 27),
        ]
    shared_loads = [load(shared_in[name], shared[name], i) for i, name in enumerate(names)]
    row_loads = [load(row_in[name], row[name], 6 + i) for i, name in enumerate(names)]
    late_loads = [
        load(row_in["normed"], normed.at[pl.ds(0, length)], 12),
        load(shared_in["normed"].at[rows_at(zq * part, part)], normed.at[pl.ds(length, part)], 13),
        load(
            shared_in["normed"].at[rows_at((2 + zq) * part, part)], normed.at[pl.ds(length + part, part)], 14
        ),
        load(mix_in, weight, 15),
        load(x_in, x, 16),
        load(midg_in, midg, 17),
    ]
    if square:
        greet([partner, cross, near_x, near_y] + along, keep, moves)
        bulk_first = send(packed_in.at[chip ^ 3, first_half], far_in.at[0], 0, near_y)
        bulk_second = send(packed_in.at[chip ^ 3, second_half], far_in.at[1], 1, near_x)
        bulk_x = send(packed_in.at[chip ^ 1, second_half], direct_in.at[0], 2, near_x)
        bulk_y = send(packed_in.at[chip ^ 2, first_half], direct_in.at[1], 3, near_y)

        def collect(sources, target, at, turn):
            moved = [
                remote(sources[0], target.at[zq], sems, at, keep),
                remote(sources[2], target.at[2], sems, at + 1, keep),
            ]
            stays = [
                pltpu.make_async_copy(sources[0], target.at[zq], local_sem.at[2 * turn]),
                pltpu.make_async_copy(sources[2], target.at[2], local_sem.at[2 * turn + 1]),
            ]
            crossed = remote(sources[1], target.at[zq], sems, at + 2, cross)

            @pl.when(moves)
            def _():
                for copy in moved:
                    copy.start()

            @pl.when(jnp.logical_not(moves))
            def _():
                for copy in stays:
                    copy.start()

            crossed.start()
            return moved, stays, crossed

        def collected(copies):
            moved, stays, crossed = copies
            crossed.wait()

            @pl.when(moves)
            def _():
                for copy in moved:
                    copy.wait()

            @pl.when(jnp.logical_not(moves))
            def _():
                for copy in stays:
                    copy.wait()

        output_copies = collect((keep_in, cross_in, third_in), output_ref, 4, 0)
    else:
        greet([partner, along[0]])

    gain_sums[...] = jnp.zeros_like(gain_sums)

    def attend_back(bufs, bounds, count, q_lanes_to, k_to, v_to, at):
        def one(p, _):
            lanes = pl.ds(pl.multiple_of(p * 128, 128), 128)
            key_lanes = pl.ds(pl.multiple_of(width + p * 128, 128), 128)
            attend_back_kernel(
                pics, bufs["aug"].at[pl.ds(2 * p, 2)], bufs["k"].at[:, lanes], bufs["v"].at[:, lanes],
                bufs["out"].at[:, lanes], bufs["do"].at[:, lanes], bufs["raw"].at[:, lanes],
                bufs["raw"].at[:, key_lanes], gain_query.at[:, lanes], gain_key.at[:, lanes], bounds,
                q_lanes_to(p), k_to(p), v_to(p), gain_sums.at[pl.ds(at, 1), lanes], gain_sums.at[pl.ds(at + 1, 1), lanes],
                kaug, vaug, doaug.at[:, pl.ds(0, count)], qsum.at[:, pl.ds(0, count)], ksum,
            )
            return 0

        lax.fori_loop(0, width // 128, one, 0)

    def mixed_at(start, count, side):
        return lambda p: mixed.at[pl.ds(start, count), pl.ds(pl.multiple_of(side * width + p * 128, 128), 128)]

    whole_lanes = lambda ref: lambda p: ref.at[:, pl.ds(pl.multiple_of(p * 128, 128), 128)]
    for copy in shared_loads:
        copy.wait()
    attend_back(
        shared, bounds_ref.at[1], queries, mixed_at(length, queries, 0), whole_lanes(part_k), whole_lanes(part_v), 0
    )
    side_sends = []
    for i in range(2):
        theirs = rows_at((2 * i + 1 - zq) * part, part)
        there = pl.ds(i * part, part)
        side_sends.append(send(part_k.at[theirs], got_k.at[there], 7 + 2 * i, along[0]))
        side_sends.append(send(part_v.at[theirs], got_v.at[there], 8 + 2 * i, along[0]))
    if square:
        for copy in held_loads:
            copy.wait()
        bulk_first.wait_recv()
        onward_out[0] = add(far_in[0], held[0]).astype(BF16)
        bulk_on_x = send(onward_out.at[0], onward_in.at[0], 11, near_x)
        bulk_second.wait_recv()
        onward_out[1] = add(far_in[1], held[1]).astype(BF16)
        bulk_on_y = send(onward_out.at[1], onward_in.at[1], 12, near_y)
    for copy in row_loads:
        copy.wait()
    attend_back(
        row, bounds_ref.at[0], length, mixed_at(0, length, 0), mixed_at(0, length, 1), mixed_at(0, length, 2), 2
    )

    for copy in side_sends:
        copy.wait_recv()

    def shared_pair(p, _):
        lanes = pl.ds(pl.multiple_of(p * 128, 128), 128)
        key_lanes = pl.ds(pl.multiple_of(width + p * 128, 128), 128)
        shared_keys_kernel(
            part_k.at[:, lanes], part_v.at[:, lanes], got_k.at[:, lanes], got_v.at[:, lanes],
            shared["raw"].at[:, key_lanes], gain_key.at[:, lanes], mixed_at(length, queries, 1)(p),
            mixed_at(length, queries, 2)(p), gain_sums.at[pl.ds(4, 1), lanes],
        )
        return 0

    lax.fori_loop(0, width // 128, shared_pair, 0)
    for copy in late_loads:
        copy.wait()
    other = 1 - core
    block_rows = lambda side, b: (
        rows_at(side * half + b * part, part) if b < 2 else rows_at(length + side * part, part)
    )
    for b in range(3):
        parts_out[pl.ds(b * part, part), :] = nt(mixed[block_rows(other, b), :], weight[...]).astype(BF16)
    part_send = send(parts_out, parts_in, 13, partner)
    if square:
        bulk_y.wait_recv()
        bulk_on_x.wait_recv()
        bulk_x.wait_recv()
        bulk_on_y.wait_recv()
        quarter_rows = rows_count // 4
        first_sum = add(held[2], onward_in[0], direct_in[1]).astype(BF16)
        second_half_sum = add(held[3], onward_in[1], direct_in[0]).astype(BF16)
        for i in range(2):
            line[i] = first_sum[i * quarter_rows : (i + 1) * quarter_rows]
            line[2 + i] = second_half_sum[i * quarter_rows : (i + 1) * quarter_rows]
        line_near = [send(line.at[2 * i + 1 - zq], near_in.at[i], 14 + i, along[0]) for i in range(2)]
    shard = model // 8
    if square:
        for i in range(3):
            lanes = slice(i * width, (i + 1) * width)
            value = tn(normed[...], mixed[:, lanes]).astype(BF16)
            for p in range(8):
                payload[p, :shard, lanes] = value[p * shard : (p + 1) * shard]
    else:
        for i in range(3):
            lanes = slice(i * width, (i + 1) * width)
            mix_grad_ref[:, lanes] = tn(normed[...], mixed[:, lanes]).astype(BF16)
    part_send.wait_recv()
    first_sum_gain = jnp.zeros((1, model), F32)
    for b in range(3):
        rows = pl.ds(b * part, part)
        upstream = nt(mixed[block_rows(core, b), :], weight[...]) + parts_in[rows, :].astype(F32)
        n, r = norm_parts(x[rows, :].astype(F32))
        value, more = norm_back(upstream, n, r, gain_first[...])
        first_sum_gain = first_sum_gain + more
        grad_own[rows, :] = (midg[rows, :] + value).astype(BF16)
    gains_sum[...] = jnp.zeros_like(gains_sum)
    gains_sum[0:1, :] = first_sum_gain
    mine_lanes = pl.ds(pl.multiple_of(core * width, 128), width)
    gains_sum[1:2, mine_lanes] = gain_sums[0:1, :] + gain_sums[2:3, :]
    gains_sum[2:3, mine_lanes] = gain_sums[3:4, :] + gain_sums[4:5, :]
    gains_sum[3:4, :] = gain_second_grad[...]

    if square:
        grad_copies = collect(
            (
                grad_own.at[rows_at(zq * part, part)],
                grad_own.at[rows_at((1 - zq) * part, part)],
                grad_own.at[pl.ds(half, part)],
            ),
            grad_out, 16, 1,
        )
        for p in range(8):
            payload[p, shard:, :] = jnp.zeros((16, 3 * width), BF16)
            payload[p, shard:, :shard] = gains_sum[:, p * shard : (p + 1) * shard].astype(BF16)
        mine, theirs = 2 * chip + core, 2 * chip + 1 - core
        x_mine, x_other = 2 * (chip ^ 1) + core, 2 * (chip ^ 1) + 1 - core
        y_mine, y_other = 2 * (chip ^ 2) + core, 2 * (chip ^ 2) + 1 - core
        far_mine, far_other = 2 * (chip ^ 3) + core, 2 * (chip ^ 3) + 1 - core
        first = send(payload.at[far_mine], relay.at[0], 19, near_y)
        second = send(payload.at[far_other], relay.at[1], 20, near_x)
        direct_x = send(payload.at[x_other], final.at[0], 21, near_x)
        direct_y = send(payload.at[y_mine], final.at[1], 22, near_y)

        for copy in line_near:
            copy.wait_recv()
        for i in range(2):
            second_sum[i] = add(line[2 * i + zq], near_in[i]).astype(BF16)
        line_far = send(second_sum.at[1 - zp], far_quarter, 23, along[1])
        first.wait_recv()
        relay[2] = add(relay[0], payload[x_mine]).astype(BF16)
        onward_x = send(relay.at[2], final.at[2], 24, near_x)
        second.wait_recv()
        relay[3] = add(relay[1], payload[y_other]).astype(BF16)
        onward_y = send(relay.at[3], final.at[3], 25, near_y)
        direct_x.wait_recv()
        onward_y.wait_recv()
        relay[4] = add(payload[theirs], final[0], final[3]).astype(BF16)
        to_core = send(relay.at[4], core_got, 26, partner)
        direct_y.wait_recv()
        onward_x.wait_recv()
        kept = add(payload[mine], final[1], final[2])
        quarter = shard // 2
        for i in range(2):
            chunks[2 * core + i] = kept[i * quarter : (i + 1) * quarter].astype(BF16)
        to_core.wait_recv()
        for i in range(2):
            chunks[2 * (1 - core) + i] = core_got[i * quarter : (i + 1) * quarter]
        gain_parts[0] = (kept[shard:] + core_got[shard:].astype(F32)).astype(BF16)
        hops = [z ^ 1, z ^ 2, z ^ 3]
        copies = []
        for i in range(3):
            copies.append(send(chunks.at[hops[i]], chunk_got.at[i], 27 + i, along[i]))
            copies.append(send(gain_parts.at[0], gain_got.at[i], 30 + i, along[i]))
        line_far.wait_recv()
        whole_line[z] = add(second_sum[zp], far_quarter[...]).astype(BF16)
        line_back = send(whole_line.at[z], whole_line.at[z], 33, along[1])
        for copy in copies:
            copy.wait_recv()
        gains_ref[...] = add(gain_parts[0], gain_got[0], gain_got[1], gain_got[2])
        chunk_got[3] = add(chunks[z], chunk_got[0], chunk_got[1], chunk_got[2]).astype(BF16)
        spread = [send(chunk_got.at[3], chunk_got.at[4 + i], 34 + i, along[i]) for i in range(3)]
        line_back.wait_recv()
        line_last = [
            send(whole_line.at[z], whole_line.at[z], 37, along[0]),
            send(whole_line.at[z ^ 2], whole_line.at[z ^ 2], 38, along[0]),
        ]

        def place(index, values):
            side, up = index // 2, index % 2
            values = values.astype(F32)
            rows = rows_at(up * quarter, quarter)
            for p in range(3):
                lanes = pl.ds(pl.multiple_of((2 * p + side) * width, 128), width)
                total_ref[rows, lanes] = values[:, p * width : (p + 1) * width]

        place(z, chunk_got[3])
        for i in range(3):
            spread[i].wait_recv()
            place(hops[i], chunk_got[4 + i])

        for copy in line_last:
            copy.wait_recv()
        flat = jnp.concatenate([whole_line[i] for i in range(4)], axis=0)
        tile = down_ref.shape[0]
        down_ref[...] = flat[:tile].astype(F32)
        ups = [flat[tile + 2 * shard * i : tile + 2 * shard * (i + 1)] for i in range(2)]
        outs = flat[2 * tile : 2 * tile + shard]
        for i in range(2):
            up_out[i] = jnp.where(core == 0, ups[i][shard:], ups[i][:shard])
        outw_out[...] = jnp.where(core == 0, outs[:, width:], outs[:, :width])
        up_send = send(up_out, up_got, 39, partner)
        outw_send = send(outw_out, outw_got, 40, partner)

        def place_up(side, i, values):
            values = values.astype(F32)
            for j in range(2):
                lanes = pl.ds(pl.multiple_of((2 * (2 * i + j) + side) * tile, 128), tile)
                up_ref[:, lanes] = values[:, j * tile : (j + 1) * tile]

        for i in range(2):
            place_up(core, i, jnp.where(core == 0, ups[i][:shard], ups[i][shard:]))
        outw_ref[:, mine_lanes] = jnp.where(core == 0, outs[:, :width], outs[:, width:]).astype(F32)
        up_send.wait_recv()
        outw_send.wait_recv()
        for i in range(2):
            place_up(other, i, up_got[i])
        outw_ref[:, pl.ds(pl.multiple_of(other * width, 128), width)] = outw_got[...].astype(F32)
        collected(output_copies)
        collected(grad_copies)
    for copy in waits:
        copy.wait_send()


def backward_pass(square, pics, row, shared, weights, gains, bounds, *more):
    length, width = row[1].shape
    model = 2 * width
    part = length // 4
    half, tokens = 2 * part, 3 * part
    shard = model // 8
    near = pl.BlockSpec(memory_space=pltpu.VMEM)
    anywhere = pl.BlockSpec(memory_space=pl.ANY)
    low = lambda *shape: (shape, BF16)
    wide = lambda *shape: (shape, F32)
    if square:
        rows = more[0].shape[1]
        tile = more[4]
        more = more[:4]
        outs = [
            (low(3, part, model), anywhere),
            (low(3, part, model), anywhere),
            (wide(shard, 6 * width), near),
            (wide(16, 3 * width), near),
            (wide(shard, 8 * tile), near),
            (wide(tile, model), near),
            (wide(shard, model), near),
        ]
    else:
        outs = [(low(tokens, model), near), (low(model, 3 * width), near), (wide(16, model), near)]
    scratch = []
    for queries in (length, half):
        scratch += [
            low(2 * (width // 128), queries, 128), low(length, width), low(length, width), low(queries, width),
            low(queries, width), low(length, 2 * width),
        ]
    scratch += [
        low(length + half, model), low(model, 3 * width), low(tokens, model), wide(tokens, model),
        low(2, length, 128), low(2, length, 128), low(2, length, 128), wide(2, length, 128), wide(length, 128),
        low(length + half, 3 * width), low(length, width), low(length, width), low(half, width), low(half, width),
        wide(8, width), low(tokens, model), low(tokens, model),
    ]
    if square:
        span = rows // 2
        pieces = shard + 16
        scratch += [
            low(tokens, model), low(8, pieces, 3 * width), wide(16, model),
            low(4, span, model), low(2, span, model), low(2, span, model), low(2, span, model), low(2, span, model),
            low(4, rows // 4, model), low(2, rows // 4, model), low(2, rows // 4, model), low(rows // 4, model),
            low(4, rows // 4, model),
            low(2, shard, model), low(2, shard, model), low(shard, width), low(shard, width),
            low(5, pieces, 3 * width), low(4, pieces, 3 * width), low(pieces, 3 * width), low(4, shard // 2, 3 * width),
            low(1, 16, 3 * width), low(7, shard // 2, 3 * width), low(3, 16, 3 * width),
        ]
    return pl.pallas_call(
        functools.partial(backward_kernel, square, pics),
        in_specs=[anywhere] * 17 + [near] * 5 + [anywhere] * len(more),
        out_specs=[spec for _, spec in outs],
        out_shape=[jax.ShapeDtypeStruct(*shape) for shape, _ in outs],
        scratch_shapes=[pltpu.VMEM(*shape) for shape in scratch]
        + [
            pltpu.SemaphoreType.DMA((41,)),
            pltpu.SemaphoreType.DMA((41,)),
            pltpu.SemaphoreType.DMA((28,)),
            pltpu.SemaphoreType.DMA((4,)),
        ],
        compiler_params=pltpu.CompilerParams(
            collective_id=2, has_side_effects=True, vmem_limit_bytes=62 * 1024 * 1024
        ),
        name="backward_pass",
    )(*row, *shared, *weights, *gains, bounds, *more)


def local(
    tokens, lengths, pictures, first_gain, mix_weight, query_gain, key_gain, out_weight,
    second_gain, up_weight, down_weight, cotangent,
):
    chip, core, zp, zq = here()
    chips = lax.axis_size("chip")
    square = chips == 4
    rows = ("chip", "core")
    _, part, model = tokens.shape
    length = 4 * part
    half = 2 * part
    width = HEADS // 2 * HEAD
    pics = lengths.shape[1]
    shard = mix_weight.shape[0]

    gains = jnp.stack([first_gain, query_gain, key_gain, second_gain])
    gains = jnp.pad(gains, ((0, 12), (0, 128 - shard)))
    mix_split = mix_weight.reshape(shard, 3, 2, width).transpose(2, 0, 1, 3).reshape(2, shard, 3 * width)
    lens = jnp.pad(lengths, ((0, 5), (0, 128 - pics)))
    hidden = up_weight.shape[1]
    tile = hidden // 8
    if square:
        up_split = up_weight.reshape(shard, 4, 2, tile).transpose(2, 0, 1, 3).reshape(2, shard, 4 * tile)
        forward = forward_pass(
            True, pics, tokens, cotangent, lens, mix_split, gains, up_split, down_weight, out_weight
        )
        up_half, down_half, out_matrix = forward[19:]
        gain_second = forward[3]
    else:
        gather = lambda weight: lax.all_gather(weight, rows, axis=0, tiled=True)
        half_of = lambda weight, axis: pick(weight, core, axis)
        mix_half = half_of(gather(mix_weight).reshape(model, 3, 2, width), 2).reshape(model, 3 * width)
        up_half = half_of(gather(up_weight).reshape(model, 4, 2, tile), 2).reshape(model, 4 * tile)
        down_half = half_of(gather(down_weight).reshape(4, 2, tile, model), 1).reshape(4 * tile, model)
        out_matrix = gather(out_weight)
        spread_gains = lax.all_gather(gains, rows, axis=0, tiled=False)
        spread_gains = spread_gains[:, :4, :shard].transpose(1, 0, 2).reshape(4, 1, model).astype(F32)
        gain_second = spread_gains[3]
        forward = forward_pass(
            False, pics, tokens, cotangent, lens, mix_half, gains, spread_gains[0],
            half_of(spread_gains[1].reshape(2, 1, width), 0), half_of(spread_gains[2].reshape(2, 1, width), 0),
        )
    own_tokens, bounds, mix_half, _, query_first, key_first, grad_tokens = forward[:7]
    gain_query, gain_key = query_first[0], key_first[0]
    gain_first = jnp.concatenate([query_first[1], key_first[1]], axis=1)
    normed, k, v, raw, out, aug = forward[7:13]
    shared_normed, shared_k, shared_v, shared_raw, shared_out, shared_aug = forward[13:19]

    def collect(mine, cross, third):
        mine = lax.ppermute(mine, COLUMN, KEEP)
        cross = lax.ppermute(cross, COLUMN, CROSS)
        third = lax.ppermute(third, COLUMN, KEEP)
        return jnp.stack([jnp.where(zq == 0, mine, cross), jnp.where(zq == 0, cross, mine), third])

    out_keep, out_cross, out_third, middle_grad, grad, shared_grad, packed, second_gain_grad = dense(
        out, shared_out, own_tokens, grad_tokens, out_matrix, gain_second, bounds, up_half, down_half
    )
    row_side = (aug, k, v, out, grad, raw, normed)
    shared_side = (shared_aug, shared_k, shared_v, shared_out, shared_grad, shared_raw, shared_normed)
    weights = (mix_half, own_tokens, middle_grad)
    gains = (gain_first, gain_query, gain_key, second_gain_grad)
    if square:
        output, input_out, mix_out, gains_out, up_out, down_out, outw_out = backward_pass(
            True, pics, row_side, shared_side, weights, gains, bounds, packed, out_keep, out_cross, out_third, tile
        )
        gains_out = gains_out[:4, :shard]
    else:
        input_grad, mix_grad, gain_grads = backward_pass(
            False, pics, row_side, shared_side, weights, gains, bounds
        )

        def reduce(grad):
            return lax.psum(lax.psum_scatter(grad, rows, scatter_dimension=0, tiled=True), SEQ).astype(F32)

        output = collect(out_keep, out_cross, out_third)
        first, second = input_grad[:part], input_grad[part:half]
        input_out = collect(
            jnp.where(zq == 0, first, second), jnp.where(zq == 0, second, first), input_grad[half:]
        )
        own_core = jnp.arange(2) == core
        eighth = model // 8
        down_grad = packed[:, None, :tile]
        down_out = reduce(jnp.where(own_core[None, :, None, None], down_grad, 0).reshape(hidden, model))
        up_grad = packed[:, tile : 2 * tile].reshape(4, 2, 2 * eighth, 2, tile).transpose(0, 2, 1, 3, 4)
        up_grad = up_grad.reshape(model, 4, 1, tile)
        up_out = reduce(jnp.where(own_core[None, None, :, None], up_grad, 0).reshape(model, hidden))
        out_grad = packed[:, 2 * tile : 2 * tile + eighth].reshape(4, eighth, 2, width).transpose(0, 2, 1, 3)
        out_grad = out_grad.reshape(model, 1, width)
        outw_out = reduce(jnp.where(own_core[None, :, None], out_grad, 0).reshape(model, model))
        mix_out = reduce(
            jnp.where(own_core[None, None, :, None], mix_grad.reshape(model, 3, 1, width), 0).reshape(model, 6 * width)
        )
        gain_grads = gain_grads[:4].reshape(4, 2 * chips, shard).transpose(1, 0, 2).astype(BF16)
        gains_out = reduce(gain_grads).reshape(4, shard)
    return (
        output, input_out, gains_out[0], mix_out, gains_out[1], gains_out[2], outw_out, gains_out[3],
        up_out, down_out,
    )


def solution(mesh):
    fsdp = mesh.shape["fsdp"]
    split = Mesh(mesh.devices.reshape(fsdp // 2, 2, 2, 2), ("chip", "core", "zp", "zq"))
    rows = ("chip", "core")
    return jax.shard_map(
        local,
        mesh=split,
        in_specs=(
            P(rows, SEQ, None),
            P(rows, None),
            P(rows, SEQ),
            P(rows),
            P(rows, None),
            P(rows),
            P(rows),
            P(rows, None),
            P(rows),
            P(rows, None),
            P(rows, None),
            P(rows, SEQ, None),
        ),
        out_specs=(
            P(rows, SEQ, None),
            P(rows, SEQ, None),
            P(rows),
            P(rows, None),
            P(rows),
            P(rows),
            P(rows, None),
            P(rows),
            P(rows, None),
            P(rows, None),
        ),
        check_vma=False,
    )
```

```python
import functools

import jax
import jax.numpy as jnp
from jax import lax
from jax.experimental import pallas as pl
from jax.experimental.pallas import tpu as pltpu
from jax.sharding import Mesh, PartitionSpec as P

HEADS = 12
HEAD = 64
EPSILON = 1e-06
BLOCK = 256
STEP = 512
MARK = 32.0
EXP2_FACTOR = HEAD**-0.5 * 1.4426950408889634
F32 = jnp.float32
BF16 = jnp.bfloat16
VMEM_LIMIT = 56 * 1024 * 1024

SEQ = ("zp", "zq")
COLUMN = ("core", "zp", "zq")
KEEP = [
    (core * 4 + z, (z // 2) * 4 + 2 * core + z % 2) for core in range(2) for z in range(4)
]
CROSS = [
    (core * 4 + z, (z // 2) * 4 + 2 * core + 1 - z % 2) for core in range(2) for z in range(4)
]


def swap(array, name, bit=1):
    count = lax.axis_size(name)
    return lax.ppermute(array, name, [(i, i ^ bit) for i in range(count)])


def pick(array, index, axis=0):
    return lax.dynamic_index_in_dim(array, index, axis, keepdims=False)


def group_ones(scale, size=128):
    row = lax.broadcasted_iota(jnp.int32, (size, size), 0) // HEAD
    column = lax.broadcasted_iota(jnp.int32, (size, size), 1) // HEAD
    return jnp.where(row == column, scale, 0.0).astype(BF16)


def group_sum(values, ones):
    return jnp.dot(values.astype(BF16), ones, preferred_element_type=F32)


def group_sum_fine(values, ones):
    high = values.astype(BF16)
    return group_sum(high, ones) + group_sum(values - high.astype(F32), ones)


def project_kernel(x_ref, gain_ref, weight_ref, qkg_ref, normed_ref, qk_ref, v_ref, raw_ref):
    both = qk_ref.shape[1]
    x = x_ref[...].astype(F32)
    center = x - jnp.mean(x, axis=-1, keepdims=True)
    spread = jnp.mean(center * center, axis=-1, keepdims=True)
    normed = (center * lax.rsqrt(spread + EPSILON) * gain_ref[...]).astype(BF16)
    normed_ref[...] = normed
    ones = group_ones(1.0 / HEAD, 256)
    for at in range(0, both, 256):
        lanes = slice(at, at + 256)
        raw = jnp.dot(normed, weight_ref[:, lanes], preferred_element_type=F32)
        raw_ref[:, lanes] = raw.astype(BF16)
        c = raw - group_sum(raw, ones)
        n = c * lax.rsqrt(group_sum(c * c, ones) + EPSILON)
        qk_ref[:, lanes] = (n * qkg_ref[:, lanes]).astype(BF16)
    v_ref[...] = jnp.dot(normed, weight_ref[:, both:], preferred_element_type=F32).astype(BF16)


def nt(a, b):
    return lax.dot_general(a, b, (((1,), (1,)), ((), ())), preferred_element_type=F32)


def tn(a, b):
    return lax.dot_general(a, b, (((0,), (0,)), ((), ())), preferred_element_type=F32)


def slots(queries, length, part):
    at = lax.broadcasted_iota(jnp.int32, (queries, 128), 0)
    if queries == length:
        return at
    return at % part + part * (lax.axis_index("zq") + 2 * (at // part))


def own_rows(ref, start, count, queries, part):
    if queries == ref.shape[0]:
        return ref[pl.ds(start, count), :]
    zq = lax.axis_index("zq")
    pieces = [
        ref[pl.ds(pl.multiple_of((zq + 2 * i) * part, part), part), :]
        for i in range(start // part, (start + count) // part)
    ]
    return jnp.concatenate(pieces, axis=0)


def query_marks(bounds_ref, place, queries, length, part, pics):
    at = slots(queries, length, part)
    inside = (at >= bounds_ref[0:1, :]) & (at < bounds_ref[2:3, :])
    values = jnp.where(inside, MARK, 0.0)
    return jnp.where(place == pics, MARK, values).astype(BF16)


def key_marks(bounds_ref, place, length, pics):
    at = lax.broadcasted_iota(jnp.int32, (length, 128), 0)
    inside = (at >= bounds_ref[0:1, :]) & (at < bounds_ref[1:2, :])
    values = jnp.where(inside, MARK, 0.0)
    values = jnp.where(place == pics, -MARK, values)
    return jnp.where((place > pics) & (place < pics + 4), 1.0, values).astype(BF16)


def attend_kernel(pics, q_ref, k_ref, v_ref, bounds_ref, out_ref, aug_ref, kaug, vaug, qaug):
    length = k_ref.shape[0]
    queries = out_ref.shape[0]
    part = length // 4
    lane = lax.broadcasted_iota(jnp.int32, (1, 128), 1)
    place = lane % HEAD
    sides = [lane < HEAD, lane >= HEAD]
    kmarks = key_marks(bounds_ref, place, length, pics)
    qmarks = query_marks(bounds_ref, place, queries, length, part, pics)
    qaug[...] = qmarks
    for h in range(2):
        kaug[h] = jnp.where(sides[h], k_ref[...], kmarks)
        vaug[h] = jnp.where(sides[h], v_ref[...], jnp.ones_like(v_ref))
    for b in range(queries // STEP):
        rows = pl.ds(b * STEP, STEP)
        mine = own_rows(q_ref, b * STEP, STEP, queries, part)
        query = [jnp.where(sides[h], mine, qaug[rows, :]) for h in range(2)]
        total = [jnp.zeros((STEP, 128), F32)] * 2
        for j in range(length // STEP):
            keys = pl.ds(j * STEP, STEP)
            scores = [nt(query[h], kaug[h, keys, :]) for h in range(2)]
            weights = [jnp.exp2(x * EXP2_FACTOR).astype(BF16) for x in scores]
            total = [
                total[h] + jnp.dot(weights[h], vaug[h, keys, :], preferred_element_type=F32) for h in range(2)
            ]
        results = []
        for h in range(2):
            results.append(total[h] / pltpu.roll(total[h], HEAD, 1))
            log_total = jnp.log(jnp.where(sides[h], 1.0, total[h])) * -(HEAD**0.5)
            first = log_total.astype(BF16)
            rest = log_total - first.astype(F32)
            middle = rest.astype(BF16)
            last = (rest - middle.astype(F32)).astype(BF16)
            logs = jnp.where(place == pics + 1, first, jnp.where(place == pics + 2, middle, last))
            slot = jnp.logical_not(sides[h]) & (place > pics) & (place < pics + 4)
            aug_ref[h, rows, :] = jnp.where(slot, logs, query[h])
        out_ref[rows, :] = jnp.where(sides[0], results[0], results[1]).astype(BF16)


def head_norm_back(e, raw, gain, means):
    raw = raw.astype(F32)
    c = raw - group_sum(raw, means)
    r = lax.rsqrt(group_sum(c * c, means) + EPSILON)
    n = c * r
    t = e * gain
    grad = r * (t - group_sum(t, means) - n * group_sum(t * n, means))
    return grad.astype(BF16), jnp.sum(e * n, axis=0, keepdims=True)


def attend_back_kernel(
    pics, aug_ref, k_ref, v_ref, out_ref, do_ref, rawq_ref, rawk_ref, qg_ref, kg_ref, bounds_ref,
    dq_ref, dk_ref, dv_ref, qgg_ref, kgg_ref, kaug, vaug, doaug, qsum, ksum,
):
    length = k_ref.shape[0]
    queries = do_ref.shape[0]
    part = length // 4
    whole = queries == length
    lane = lax.broadcasted_iota(jnp.int32, (1, 128), 1)
    place = lane % HEAD
    sides = [lane < HEAD, lane >= HEAD]
    kmarks = key_marks(bounds_ref, place, length, pics)
    vmarks = jnp.where(place < 2, 1.0, 0.0).astype(BF16)
    ones = group_ones(1.0)
    inner = group_sum_fine(do_ref[...].astype(F32) * out_ref[...].astype(F32), ones)
    inner = -pltpu.roll(inner, HEAD, 1)
    inner_high = inner.astype(BF16)
    inner_low = (inner - inner_high.astype(F32)).astype(BF16)
    zero = jnp.zeros((), BF16)
    gmarks = jnp.where(place == 0, inner_high, jnp.where(place == 1, inner_low, zero))
    for h in range(2):
        kaug[h] = jnp.where(sides[h], k_ref[...], kmarks)
        vaug[h] = jnp.where(sides[h], v_ref[...], vmarks)
        doaug[h] = jnp.where(sides[h], do_ref[...], gmarks)
    for b in range(length // STEP):
        keys = pl.ds(b * STEP, STEP)
        key = [kaug[h, keys, :] for h in range(2)]
        value = [vaug[h, keys, :] for h in range(2)]
        dk = [jnp.zeros((STEP, 128), F32)] * 2
        dv = [jnp.zeros((STEP, 128), F32)] * 2
        for j in range(queries // STEP):
            rows = pl.ds(j * STEP, STEP)
            query = [aug_ref[h, rows, :] for h in range(2)]
            grad = [doaug[h, rows, :] for h in range(2)]
            scores = [nt(key[h], query[h]) for h in range(2)]
            soft_grad = [nt(value[h], grad[h]) for h in range(2)]
            weights = [jnp.exp2(x * EXP2_FACTOR) for x in scores]
            score_grad = [(weights[h] * soft_grad[h]).astype(BF16) for h in range(2)]
            for h in range(2):
                part_sum = tn(score_grad[h], key[h])
                if b == 0:
                    qsum[h, rows, :] = part_sum
                else:
                    qsum[h, rows, :] += part_sum
                dk[h] = dk[h] + jnp.dot(score_grad[h], query[h], preferred_element_type=F32)
                dv[h] = dv[h] + jnp.dot(weights[h].astype(BF16), grad[h], preferred_element_type=F32)
        ksum[keys, :] = jnp.where(sides[0], dk[0], dk[1]) * HEAD**-0.5
        dv_ref[keys, :] = jnp.where(sides[0], dv[0], dv[1]).astype(BF16)

    means = group_ones(1.0 / HEAD)
    gain_sum = jnp.zeros((1, 128), F32)
    for b in range(queries // part):
        rows = pl.ds(b * part, part)
        e = jnp.where(sides[0], qsum[0, rows, :], qsum[1, rows, :]) * HEAD**-0.5
        raw = own_rows(rawq_ref, b * part, part, queries, part)
        dq_ref[rows, :], more = head_norm_back(e.astype(BF16).astype(F32), raw, qg_ref[...], means)
        gain_sum = gain_sum + more
    qgg_ref[...] = gain_sum
    gain_sum = jnp.zeros((1, 128), F32)
    for b in range(length // part):
        rows = pl.ds(b * part, part)
        e = ksum[rows, :].astype(BF16)
        if whole:
            dk_ref[rows, :], more = head_norm_back(e.astype(F32), rawk_ref[rows, :], kg_ref[...], means)
            gain_sum = gain_sum + more
        else:
            dk_ref[rows, :] = e
    kgg_ref[...] = gain_sum


def shared_keys_kernel(dk_ref, dv_ref, gotk_ref, gotv_ref, rawk_ref, kg_ref, outk_ref, outv_ref, kgg_ref):
    count = outk_ref.shape[0]
    part = count // 2
    means = group_ones(1.0 / HEAD)
    gain_sum = jnp.zeros((1, 128), F32)
    for b in range(2):
        rows = pl.ds(b * part, part)
        own = lambda ref: own_rows(ref, b * part, part, count, part)
        e = own(dk_ref).astype(F32) + gotk_ref[rows, :].astype(F32)
        outk_ref[rows, :], more = head_norm_back(e, own(rawk_ref), kg_ref[...], means)
        gain_sum = gain_sum + more
        outv_ref[rows, :] = (own(dv_ref).astype(F32) + gotv_ref[rows, :].astype(F32)).astype(BF16)
    kgg_ref[...] = gain_sum


def gelu_pair(h):
    size = jnp.abs(h)
    bell = jnp.exp2(h * h * -0.7213475204444817)
    t = 1.0 / (1.0 + 0.23164189 * size)
    series = t * (0.127414796 + t * (-0.142248368 + t * (0.7107068705 + t * (-0.7265760135 + t * 0.5307027145))))
    tail = series * bell
    below = jnp.where(h < 0.0, tail, 1.0 - tail)
    return h * below, below + h * (bell * 0.3989422804014327)


def norm_parts(values):
    center = values - jnp.mean(values, axis=-1, keepdims=True)
    spread = lax.rsqrt(jnp.mean(center * center, axis=-1, keepdims=True) + EPSILON)
    return center * spread, spread


def norm_back(upstream, n, r, gain):
    t = upstream * gain
    grad = r * (t - jnp.mean(t, axis=-1, keepdims=True) - n * jnp.mean(t * n, axis=-1, keepdims=True))
    return grad, jnp.sum(upstream * n, axis=0, keepdims=True)


MESH_ID = pl.DeviceIdType.MESH


def here():
    return lax.axis_index("chip"), lax.axis_index("core"), lax.axis_index("zp"), lax.axis_index("zq")


def remote(source, target, sems, at, device):
    sent, got = sems
    return pltpu.make_async_remote_copy(
        src_ref=source, dst_ref=target, send_sem=sent.at[at], recv_sem=got.at[at],
        device_id=device, device_id_type=MESH_ID,
    )


def greet(devices, maybe=None, moves=None):
    barrier = pltpu.get_barrier_semaphore()
    for device in devices:
        pl.semaphore_signal(barrier, inc=1, device_id=device, device_id_type=MESH_ID)
    if maybe is None:
        pl.semaphore_wait(barrier, len(devices))
        return

    @pl.when(moves)
    def _():
        pl.semaphore_signal(barrier, inc=1, device_id=maybe, device_id_type=MESH_ID)

    pl.semaphore_wait(barrier, len(devices) + jnp.where(moves, 1, 0))


def rows_at(start, count):
    return pl.ds(pl.multiple_of(start, 16), count)


def write_bounds(pics, lens_ref, bounds_ref, zp, zq, length):
    lane = lax.broadcasted_iota(jnp.int32, (8, 128), 1)
    lens = jnp.where(zp == 0, lens_ref[0], lens_ref[1])
    ends = lens
    for hop in (1, 2, 4, 8):
        ends = ends + jnp.where(lane >= hop, pltpu.roll(ends, hop, 1), 0)
    starts = ends - lens
    last = (lens > 0) & (pltpu.roll(lens, 127, 1) == 0)
    query_ends = jnp.where(last, length, ends)
    total = jnp.max(jnp.where(lane < pics, ends, 0), axis=1, keepdims=True)

    def both(values):
        values = jnp.where(lane < HEAD, jnp.where(lane < pics, values, 2 * length), 0)
        return values + pltpu.roll(values, HEAD, 1)

    tables = [both(starts), both(ends), both(query_ends), jnp.broadcast_to(total, (8, 128))]
    for t in range(4):
        table = tables[t]
        bounds_ref[0, t : t + 1, :] = jnp.where(zq == 0, table[0:1], table[1:2])
        bounds_ref[1, t : t + 1, :] = table[2:3]
    bounds_ref[:, 4:, :] = jnp.zeros((2, 4, 128), jnp.int32)


def forward_kernel(square, pics, *refs):
    refs = list(refs)
    take = lambda count: [refs.pop(0) for _ in range(count)]
    tokens_ref, cot_ref, lengths_ref, weight_in = take(4)
    if square:
        gain_in = take(4)
        up_in, down_ref, outw_ref = take(3)
    else:
        gain_first_in, gain_qk_in = take(2)
    x_out, bounds_ref, mix_hbm, cot_hbm, gain_first, second_ref, gain_qk = take(7)
    names = ("normed", "qk", "v", "raw", "out", "aug")
    outs = [dict(zip(names, take(6))) for _ in range(2)]
    if square:
        up_hbm, down_hbm, outw_hbm = take(3)
    row_ref, shared_ref, cot_out, lens_ref, lens_out = take(5)
    scratch = [dict(zip(names, take(6))) for _ in range(2)]
    kaug, vaug, qaug = take(3)
    if square:
        mix_ref, gains_ref, up_ref, mix_out, gains_out, up_out, down_out, outw_out = take(8)
    sent, got, local_sem, write_sem = take(4)

    chip, core, zp, zq = here()
    z = 2 * zp + zq
    part = tokens_ref.shape[1]
    half, length = 2 * part, 4 * part
    sems = (sent, got)
    partner = (chip, 1 - core, zp, zq)
    side = (chip, core, zp, 1 - zq)
    keep = (chip, zp, core, zq)
    cross = (chip, zp, core, 1 - zq)
    moves = core != zp
    near_x = (chip ^ 1, core, zp, zq)
    near_y = (chip ^ 2, core, zp, zq)
    greet([partner, side, cross] + ([near_x, near_y] if square else []), keep, moves)

    def quarter(ref, index):
        return ref.at[rows_at(index * part, part)]

    own_row = remote(tokens_ref.at[zq], quarter(row_ref, z), sems, 0, keep)
    own_shared = remote(tokens_ref.at[2], quarter(shared_ref, z), sems, 2, keep)
    stay_row = pltpu.make_async_copy(tokens_ref.at[zq], quarter(row_ref, z), local_sem.at[0])
    stay_shared = pltpu.make_async_copy(tokens_ref.at[2], quarter(shared_ref, z), local_sem.at[1])

    @pl.when(moves)
    def _():
        own_row.start()

    @pl.when(jnp.logical_not(moves))
    def _():
        stay_row.start()

    cross_row = remote(tokens_ref.at[1 - zq], quarter(row_ref, z), sems, 1, cross)
    cross_row.start()

    @pl.when(moves)
    def _():
        own_shared.start()

    @pl.when(jnp.logical_not(moves))
    def _():
        stay_shared.start()

    lens_ref[...] = jnp.zeros_like(lens_ref)
    lens_ref[: lengths_ref.shape[0], :pics] = lengths_ref[...]
    lens_copy = remote(lens_ref, lens_out.at[core], sems, 8, partner)
    lens_copy.start()
    lens_stay = pltpu.make_async_copy(lens_ref, lens_out.at[core], local_sem.at[2])
    lens_stay.start()
    waits = []
    if square:
        shard = mix_ref.shape[1]
        down_rows = down_ref.shape[0]
        width = mix_ref.shape[2] // 3
        for h in range(2):
            for i in range(3):
                mix_ref[h, :, i * width : (i + 1) * width] = weight_in[:, (2 * i + h) * width : (2 * i + h + 1) * width]
        gains_ref[...] = jnp.zeros_like(gains_ref)
        for i in range(4):
            gains_ref[i : i + 1, :shard] = gain_in[i][...].astype(F32)
        mine, theirs = 2 * chip + core, 2 * chip + 1 - core
        slot = [9]

        def send(source, target, device):
            copy = remote(source, target, sems, slot[0], device)
            slot[0] += 1
            copy.start()
            waits.append(copy)
            return copy

        def stay(source, target, at):
            copy = pltpu.make_async_copy(source, target, local_sem.at[at])
            copy.start()
            return copy

        def block(ref, start, count):
            return ref.at[rows_at(start, count)]

        mix_piece = lambda index: (block(mix_out, index * shard, shard), gains_out.at[index])

        def send_mix(sources, index, device):
            return [send(source, target, device) for source, target in zip(sources, mix_piece(index))]

        def arrived(copies):
            for copy in copies:
                copy.wait_recv()

        x_mine, y_other = 2 * (chip ^ 1) + core, 2 * (chip ^ 2) + 1 - core
        to_core = send_mix((mix_ref.at[1 - core], gains_ref), mine, partner)
        a_x = send_mix((mix_ref.at[core], gains_ref), mine, near_x)
        a_y = send_mix((mix_ref.at[core], gains_ref), mine, near_y)
        for h in range(2):
            for i in range(4):
                lanes = slice(i * down_rows, (i + 1) * down_rows)
                up_ref[h, :, lanes] = up_in[:, (2 * i + h) * down_rows : (2 * i + h + 1) * down_rows]
        up_core = send(up_ref.at[1 - core], block(up_out, mine * shard, shard), partner)
        out_core = send(outw_ref, block(outw_out, mine * shard, shard), partner)
        stays = [
            stay(mix_ref.at[core], mix_piece(mine)[0], 3),
            stay(gains_ref, gains_out.at[mine], 4),
            stay(up_ref.at[core], block(up_out, mine * shard, shard), 5),
            stay(down_ref, block(down_out, chip * down_rows, down_rows), 6),
            stay(outw_ref, block(outw_out, mine * shard, shard), 7),
        ]
        arrived(to_core)
        b_x = send_mix(mix_piece(theirs), theirs, near_x)
        b_y = send_mix(mix_piece(theirs), theirs, near_y)
        arrived(a_x)
        a_far = send_mix(mix_piece(x_mine), x_mine, near_y)
        arrived(b_y)
        b_far = send_mix(mix_piece(y_other), y_other, near_x)
        for copy in stays:
            copy.wait()
        arrived([up_core])
        dhalf, ohalf = down_rows // 2, shard // 2

        def bundle(first, from_chip):
            same, twin = 2 * from_chip + core, 2 * from_chip + 1 - core
            part_of = 0 if first else 1
            return [
                block(up_out, (same if first else twin) * shard, shard),
                block(down_out, from_chip * down_rows + part_of * dhalf, dhalf),
                block(outw_out, same * shard + part_of * ohalf, ohalf),
            ]

        def send_bundle(first, from_chip, device):
            return [send(ref, ref, device) for ref in bundle(first, from_chip)]

        first_x = send_bundle(True, chip, near_x)
        first_y = send_bundle(True, chip, near_y)
        second_x = send_bundle(False, chip, near_x)
        second_y = send_bundle(False, chip, near_y)

    lens_copy.wait()
    lens_stay.wait()
    write_bounds(pics, lens_out, bounds_ref, zp, zq, length)
    if square:
        arrived(a_y + b_x + a_far + b_far)
        for p in range(gains_out.shape[0]):
            lanes = slice(p * shard, (p + 1) * shard)
            values = gains_out[p, :, :shard]
            gain_first[:, lanes] = values[0:1]
            second_ref[:, lanes] = values[3:4]
            half_pieces = gains_out.shape[0] // 2

            @pl.when(core == p // half_pieces)
            def _():
                at = (p % half_pieces) * shard
                gain_qk[:, at : at + shard] = values[1:2]
                gain_qk[:, width + at : width + at + shard] = values[2:3]
        weight = mix_out
    else:
        weight = weight_in
        width = weight.shape[1] // 3
        second_ref[...] = jnp.zeros_like(second_ref)
        gain_first[...] = gain_first_in[...]
        gain_qk[...] = gain_qk_in[...]
    writes = []

    def write(source, target, at):
        copy = pltpu.make_async_copy(source, target, write_sem.at[at])
        copy.start()
        writes.append(copy)

    write(weight, mix_hbm, 0)
    first, second = 2 * core + zq, 2 * core + 1 - zq
    other_first, other_second = 2 * (1 - core) + zq, 2 * (1 - core) + 1 - zq

    def forwarded(ref, index, at):
        return remote(quarter(ref, index), quarter(ref, index), sems, at, partner)

    def project(tokens, bufs, at):
        rows = rows_at(at * part, part)
        project_kernel(
            tokens.at[rows], gain_first, weight, gain_qk, bufs["normed"].at[rows], bufs["qk"].at[rows],
            bufs["v"].at[rows], bufs["raw"].at[rows],
        )

    def project_row(i, _):
        @pl.when(i == 0)
        def _():
            @pl.when(moves)
            def _():
                own_row.wait_recv()

            @pl.when(jnp.logical_not(moves))
            def _():
                stay_row.wait()

            forwarded(row_ref, first, 3).start()

        @pl.when(i == 1)
        def _():
            cross_row.wait_recv()
            forwarded(row_ref, second, 4).start()

        @pl.when(i == 2)
        def _():
            forwarded(row_ref, other_first, 3).wait_recv()

        @pl.when(i == 3)
        def _():
            forwarded(row_ref, other_second, 4).wait_recv()

        order = jnp.where(i == 0, first, jnp.where(i == 1, second, jnp.where(i == 2, other_first, other_second)))
        project(row_ref, scratch[0], order)
        return 0

    row_one, row_two = forwarded(row_ref, first, 3), forwarded(row_ref, second, 4)

    def attend(bufs, bounds):
        def one(p, _):
            lanes = pl.ds(pl.multiple_of(p * 128, 128), 128)
            attend_kernel(
                pics, bufs["qk"].at[:, lanes],
                bufs["qk"].at[:, pl.ds(pl.multiple_of(width + p * 128, 128), 128)], bufs["v"].at[:, lanes], bounds,
                bufs["out"].at[:, lanes], bufs["aug"].at[pl.ds(2 * p, 2)], kaug, vaug, qaug.at[pl.ds(0, bufs["out"].shape[0])],
            )
            return 0

        lax.fori_loop(0, width // 128, one, 0)

    lax.fori_loop(0, 4, project_row, 0)
    for i, name in enumerate(("normed", "qk", "v", "raw")):
        write(scratch[0][name], outs[0][name], 1 + i)
    write(row_ref.at[rows_at(core * half, half)], x_out.at[pl.ds(0, half)], 5)

    @pl.when(moves)
    def _():
        own_shared.wait_recv()

    @pl.when(jnp.logical_not(moves))
    def _():
        stay_shared.wait()

    to_side = remote(quarter(shared_ref, first), quarter(shared_ref, first), sems, 5, side)
    to_side.start()
    shared_one = remote(quarter(shared_ref, first), quarter(shared_ref, first), sems, 6, partner)
    shared_one.start()
    cot_own = pl.ds(pl.multiple_of(zq * part, part), part)
    cot_shared = pl.ds(half, part)
    cot_moves = [
        remote(cot_ref.at[zq], cot_out.at[cot_own], sems, 46, keep),
        remote(cot_ref.at[2], cot_out.at[cot_shared], sems, 47, keep),
    ]
    cot_stays = [
        pltpu.make_async_copy(cot_ref.at[zq], cot_out.at[cot_own], local_sem.at[0]),
        pltpu.make_async_copy(cot_ref.at[2], cot_out.at[cot_shared], local_sem.at[1]),
    ]
    cot_cross = remote(cot_ref.at[1 - zq], cot_out.at[cot_own], sems, 48, cross)

    @pl.when(moves)
    def _():
        for copy in cot_moves:
            copy.start()

    @pl.when(jnp.logical_not(moves))
    def _():
        for copy in cot_stays:
            copy.start()

    cot_cross.start()
    attend(scratch[0], bounds_ref.at[0])
    write(scratch[0]["out"], outs[0]["out"], 6)
    write(scratch[0]["aug"], outs[0]["aug"], 7)
    to_side.wait_recv()
    shared_two = forwarded(shared_ref, second, 7)
    shared_two.start()
    if square:
        arrived(first_x + second_y)
        far_first = send_bundle(True, chip ^ 1, near_y)
        far_second = send_bundle(False, chip ^ 2, near_x)
    shared_one.wait_recv()
    shared_two.wait_recv()

    def project_shared(i, _):
        project(shared_ref, scratch[1], i)
        return 0

    lax.fori_loop(0, 4, project_shared, 0)
    for i, name in enumerate(("normed", "qk", "v", "raw")):
        write(scratch[1][name], outs[1][name], 8 + i)
    write(shared_ref.at[rows_at(first * part, part)], x_out.at[pl.ds(half, part)], 12)
    attend(scratch[1], bounds_ref.at[1])
    write(scratch[1]["out"], outs[1]["out"], 13)
    write(scratch[1]["aug"], outs[1]["aug"], 14)

    if square:
        arrived(first_y + second_x + far_first + far_second)
        sent_pieces = []
        for c in (chip ^ 1, chip ^ 2, chip ^ 3):
            target = block(outw_out, (2 * c + core) * shard, shard)
            sent_pieces.append(send(target, target, partner))
        write(up_out, up_hbm, 15)
        write(down_out, down_hbm, 16)
        arrived(sent_pieces + [out_core])
        write(outw_out, outw_hbm, 17)
        for copy in waits:
            copy.wait_send()
    cot_cross.wait()

    @pl.when(moves)
    def _():
        for copy in cot_moves:
            copy.wait()

    @pl.when(jnp.logical_not(moves))
    def _():
        for copy in cot_stays:
            copy.wait()

    write(cot_out, cot_hbm, 18)
    for copy in (row_one, row_two, shared_one, shared_two, to_side, cross_row):
        copy.wait_send()

    @pl.when(moves)
    def _():
        own_row.wait_send()
        own_shared.wait_send()

    for copy in writes:
        copy.wait()


def forward_pass(square, pics, tokens, cotangent, lengths, weight, *more):
    _, part, model = tokens.shape
    length, half, width = 4 * part, 2 * part, model // 2
    near = pl.BlockSpec(memory_space=pltpu.VMEM)
    anywhere = pl.BlockSpec(memory_space=pl.ANY)
    low = lambda *shape: (shape, BF16)
    wide = lambda *shape: (shape, F32)
    outs = [
        (low(3 * part, model), anywhere),
        (((2, 8, 128), jnp.int32), near),
        (low(model, 3 * width), anywhere),
        (low(3 * part, model), anywhere),
        (wide(1, model), near),
        (wide(1, model), near),
        (wide(1, model), near),
    ]
    bufs = []
    for queries in (length, half):
        shapes = [
            low(length, model), low(length, 2 * width), low(length, width), low(length, 2 * width),
            low(queries, width), low(2 * (width // 128), queries, 128),
        ]
        outs += [(shape, anywhere) for shape in shapes]
        bufs += shapes
    table = ((8, 128), jnp.int32)
    scratch = [low(length, model), low(length, model), low(3 * part, model), table, ((2, 8, 128), jnp.int32)] + bufs
    scratch += [low(2, length, 128), low(2, length, 128), low(length, 128)]
    if square:
        up, down, _ = more[4:]
        shard, hidden = up.shape
        landed = [low(model, hidden // 2), low(4 * down.shape[0], model), low(model, model)]
        outs += [(shape, anywhere) for shape in landed]
        scratch += [low(2, shard, 3 * width), wide(8, 128), low(2, shard, hidden // 2)]
        scratch += [low(model, 3 * width), wide(8, 8, 128)] + landed
    return pl.pallas_call(
        functools.partial(forward_kernel, square, pics),
        in_specs=[near] * (4 + len(more)),
        out_specs=[spec for _, spec in outs],
        out_shape=[jax.ShapeDtypeStruct(*shape) for shape, _ in outs],
        scratch_shapes=[pltpu.VMEM(*shape) for shape in scratch]
        + [
            pltpu.SemaphoreType.DMA((49,)),
            pltpu.SemaphoreType.DMA((49,)),
            pltpu.SemaphoreType.DMA((8,)),
            pltpu.SemaphoreType.DMA((19,)),
        ],
        compiler_params=pltpu.CompilerParams(
            collective_id=0, has_side_effects=True, vmem_limit_bytes=60 * 1024 * 1024
        ),
        name="forward_pass",
    )(tokens, cotangent, lengths, weight, *more)


def dense_kernel(
    square, out_ref, shared_ref, x, grad_ref, outw_ref, gain_ref, bounds_ref, up_ref, down_ref,
    out_keep, out_cross, out_third, midg_ref, row_grad, shared_grad, outg_ref, gaing_ref, packed_ref, far_ref,
    att_other, second, turned, grad, hidden_all, pre_all, forward, backward, middle, up, down,
    parts_out, parts_in, heads_out, cols_out, cols_in, stage, far_in, sent, got, load_sem, write_sem,
):
    chip, core, zp, zq = here()
    sems = (sent, got)
    partner = (chip, 1 - core, zp, zq)
    near_x = (chip ^ 1, core, zp, zq)
    near_y = (chip ^ 2, core, zp, zq)
    tokens, model = midg_ref.shape
    part = tokens // 3
    half = 2 * part
    width = out_ref.shape[1]
    units = up.shape[1]
    tile = units // 4
    other = 1 - core
    mine, theirs = pl.ds(0, tokens), pl.ds(tokens, tokens)
    loads = [
        pltpu.make_async_copy(up_ref, up, load_sem.at[0]),
        pltpu.make_async_copy(down_ref, down, load_sem.at[1]),
    ]
    for copy in loads:
        copy.start()
    greet([partner] + ([near_x, near_y] if square else []))
    att_sends = [
        remote(out_ref.at[rows_at(other * half, half)], att_other.at[pl.ds(0, half)], sems, 0, partner),
        remote(shared_ref.at[rows_at(other * part, part)], att_other.at[pl.ds(half, part)], sems, 1, partner),
    ]
    for copy in att_sends:
        copy.start()

    slot = lax.broadcasted_iota(jnp.int32, (part, 1), 0)
    filled, shared_filled = bounds_ref[0, 3:4, 0:1], bounds_ref[1, 3:4, 0:1]
    none = jnp.zeros((), BF16)
    for b, start, limit in (
        (0, 2 * core * part, filled),
        (1, (2 * core + 1) * part, filled),
        (2, (2 * core + zq) * part, shared_filled),
    ):
        rows = pl.ds(b * part, part)
        grad[rows, :] = jnp.where(slot + start < limit, grad_ref[rows, :], none)
    grad_send = remote(grad.at[mine], grad.at[theirs], sems, 2, partner)
    grad_send.start()

    own_rows_of = lambda b: (
        out_ref[rows_at(core * half + b * part, part), :] if b < 2 else shared_ref[rows_at(core * part, part), :]
    )
    own_weight = outw_ref[rows_at(core * width, width), :]
    other_weight = outw_ref[rows_at(other * width, width), :]
    blocks = [pl.ds(b * part, part) for b in range(3)]
    for b in range(3):
        middle[blocks[b], :] = x[blocks[b], :].astype(F32) + jnp.dot(
            own_rows_of(b), own_weight, preferred_element_type=F32
        )
    for copy in att_sends:
        copy.wait_recv()
    for rows in blocks:
        value = middle[rows, :] + jnp.dot(att_other[rows, :], other_weight, preferred_element_type=F32)
        middle[rows, :] = value
        second[rows, :] = (norm_parts(value)[0] * gain_ref[...]).astype(BF16)
    second_send = remote(second.at[mine], second.at[theirs], sems, 3, partner)
    second_send.start()
    for copy in loads:
        copy.wait()

    def hidden_units(start):
        rows = pl.ds(start, tokens)

        def one_tile(i, _):
            units_here = pl.ds(pl.multiple_of(i * tile, 128), tile)
            pre = jnp.dot(second[rows, :], up[:, units_here], preferred_element_type=F32)
            hidden, slope = gelu_pair(pre)
            hidden_all[rows, units_here] = hidden.astype(BF16)
            pre_grad = nt(grad[rows, :], down[rows_at(i * tile, tile), :]) * slope
            pre_all[rows, units_here] = pre_grad.astype(BF16)
            return 0

        lax.fori_loop(0, 4, one_tile, 0)

    hidden_units(0)
    for rows in blocks:
        forward[rows, :] = jnp.dot(hidden_all[rows, :], down[...], preferred_element_type=F32)
        backward[rows, :] = nt(pre_all[rows, :], up[...])
    second_send.wait_recv()
    grad_send.wait_recv()
    hidden_units(tokens)
    for b in range(3):
        rows, there = pl.ds(tokens + b * part, part), blocks[b]
        parts_out[0, there, :] = jnp.dot(hidden_all[rows, :], down[...], preferred_element_type=F32).astype(BF16)
    first_part = remote(parts_out.at[0], parts_in.at[0], sems, 4, partner)
    first_part.start()
    for b in range(3):
        rows, there = pl.ds(tokens + b * part, part), blocks[b]
        parts_out[1, there, :] = nt(pre_all[rows, :], up[...]).astype(BF16)
    second_part = remote(parts_out.at[1], parts_in.at[1], sems, 5, partner)
    second_part.start()

    turned[...] = second[...].T
    quarter = model // 4

    def weight_grads(i, _):
        target = chip ^ (3 - i) if square else 3 - i
        place = jnp.where(i == 0, 0, 1 + i % 2)

        @pl.when(i == 3)
        def _():
            pltpu.make_async_copy(stage.at[place], packed_ref.at[target], write_sem.at[place]).wait()

        units_here = pl.ds(pl.multiple_of(target * tile, 128), tile)
        stage[place, pl.ds(0, tile), :] = tn(hidden_all[:, units_here], grad[...]).astype(BF16)
        values = jnp.dot(
            turned[rows_at(target * quarter, quarter), :], pre_all[...], preferred_element_type=F32
        ).astype(BF16)
        for j in range(2):
            stage[place, pl.ds(tile + j * quarter, quarter), :] = values[:, j * model : (j + 1) * model]
        pltpu.make_async_copy(stage.at[place], packed_ref.at[target], write_sem.at[place]).start()
        if square:

            @pl.when(i == 0)
            def _():
                remote(stage.at[0, pl.ds(0, tile)], far_in.at[0], sems, 9, near_y).start()
                remote(stage.at[0, pl.ds(tile, tile)], far_in.at[1], sems, 10, near_x).start()

        return 0

    lax.fori_loop(0, 4, weight_grads, 0)

    second_send.wait_send()
    first_part.wait_recv()
    for rows in blocks:
        forward[rows, :] = middle[rows, :] + forward[rows, :] + parts_in[0, rows, :].astype(F32)
    out_keep[...] = forward[rows_at(zq * part, part), :].astype(BF16)
    out_cross[...] = forward[rows_at((1 - zq) * part, part), :].astype(BF16)
    out_third[...] = forward[pl.ds(half, part), :].astype(BF16)
    second_part.wait_recv()
    gain_sum = jnp.zeros(gaing_ref.shape, F32)
    for rows in blocks:
        n, r = norm_parts(middle[rows, :])
        upstream = backward[rows, :] + parts_in[1, rows, :].astype(F32)
        more, gain_more = norm_back(upstream, n, r, gain_ref[...])
        gain_sum = gain_sum + gain_more
        value = grad[rows, :].astype(F32) + more
        midg_ref[rows, :] = value
        branch = value.astype(BF16)
        second[rows, :] = branch
        heads_out[rows, :] = nt(branch, other_weight).astype(BF16)
    gaing_ref[...] = gain_sum
    head_sends = [
        remote(heads_out.at[pl.ds(0, half)], row_grad.at[rows_at(core * half, half)], sems, 6, partner),
        remote(heads_out.at[pl.ds(half, part)], shared_grad.at[rows_at(core * part, part)], sems, 7, partner),
    ]
    for copy in head_sends:
        copy.start()
    branch = second[mine, :]
    forward[rows_at(core * width, width), :] = tn(
        out_ref[rows_at(core * half, half), :], second[pl.ds(0, half), :]
    ) + tn(shared_ref[rows_at(core * part, part), :], second[pl.ds(half, part), :])
    forward[rows_at(other * width, width), :] = tn(att_other[...], branch)
    lanes = lambda side: pl.ds(pl.multiple_of(side * width, 128), width)
    cols_out[...] = forward[pl.ds(0, model), lanes(other)].astype(BF16)
    cols_send = remote(cols_out, cols_in, sems, 8, partner)
    cols_send.start()
    for b in range(3):
        value = nt(second[blocks[b], :], own_weight).astype(BF16)
        if b < 2:
            row_grad[rows_at(core * half + b * part, part), :] = value
        else:
            shared_grad[rows_at(core * part, part), :] = value
    cols_send.wait_recv()
    outg_ref[...] = (forward[pl.ds(0, model), lanes(core)] + cols_in[...].astype(F32)).astype(BF16)
    for copy in head_sends:
        copy.wait_recv()
    for copy in att_sends + head_sends + [grad_send, first_part, second_part, cols_send]:
        copy.wait_send()
    if square:
        remote(stage.at[0, pl.ds(0, tile)], far_in.at[0], sems, 9, near_y).wait()
        remote(stage.at[0, pl.ds(tile, tile)], far_in.at[1], sems, 10, near_x).wait()
    far_write = pltpu.make_async_copy(far_in, far_ref, load_sem.at[0])
    far_write.start()
    for place in range(3):
        pltpu.make_async_copy(stage.at[place], packed_ref.at[0], write_sem.at[place]).wait()
    far_write.wait()


def dense(square, out, shared_out, x, grad, out_matrix, gain, bounds, up, down):
    model = x.shape[1]
    tokens = x.shape[0]
    part = tokens // 3
    length, width = out.shape
    units = down.shape[0]
    tile = units // 4
    anywhere = pl.BlockSpec(memory_space=pl.ANY)
    near = pl.BlockSpec(memory_space=pltpu.VMEM)
    both = 2 * tokens
    low = lambda *shape: pltpu.VMEM(shape, BF16)
    wide = lambda *shape: pltpu.VMEM(shape, F32)
    return pl.pallas_call(
        functools.partial(dense_kernel, square),
        in_specs=[near] * 7 + [anywhere, anywhere],
        out_specs=[near] * 8 + [anywhere, anywhere],
        out_shape=[
            jax.ShapeDtypeStruct((part, model), BF16),
            jax.ShapeDtypeStruct((part, model), BF16),
            jax.ShapeDtypeStruct((part, model), BF16),
            jax.ShapeDtypeStruct((tokens, model), F32),
            jax.ShapeDtypeStruct((length, width), BF16),
            jax.ShapeDtypeStruct((length // 2, width), BF16),
            jax.ShapeDtypeStruct((model, width), BF16),
            jax.ShapeDtypeStruct((1, model), F32),
            jax.ShapeDtypeStruct((4, 2 * tile, model), BF16),
            jax.ShapeDtypeStruct((2, tile, model), BF16),
        ],
        scratch_shapes=[
            low(tokens, width), low(both, model), low(model, both), low(both, model), low(both, units),
            low(both, units), wide(tokens, model), wide(tokens, model), wide(tokens, model), low(model, units),
            low(units, model), low(2, tokens, model), low(2, tokens, model), low(tokens, width), low(model, width),
            low(model, width), low(3, 2 * tile, model), low(2, tile, model),
            pltpu.SemaphoreType.DMA((11,)),
            pltpu.SemaphoreType.DMA((11,)),
            pltpu.SemaphoreType.DMA((2,)),
            pltpu.SemaphoreType.DMA((3,)),
        ],
        compiler_params=pltpu.CompilerParams(
            collective_id=1, has_side_effects=True, vmem_limit_bytes=62 * 1024 * 1024
        ),
        name="dense",
    )(out, shared_out, x, grad, out_matrix, gain, bounds, up, down)


def add(*terms):
    total = terms[0].astype(F32)
    for term in terms[1:]:
        total = total + term.astype(F32)
    return total


def backward_kernel(square, pics, *refs):
    refs = list(refs)
    take = lambda count: [refs.pop(0) for _ in range(count)]
    names = ("aug", "qk", "v", "out", "do", "raw", "normed")
    row_in = dict(zip(names, take(7)))
    shared_in = dict(zip(names, take(7)))
    mix_in, x_in, midg_in, gain_first, gain_qk, gain_second_grad, bounds_ref = take(7)
    if square:
        packed_in, far_ref, outg_in, keep_in, cross_in, third_in = take(6)
        output_ref, grad_out, total_ref, gains_ref, up_ref, down_ref, outw_ref = take(7)
    else:
        grad_own, mix_grad_ref, gains_sum = take(3)
    names = names[:-1]
    row = dict(zip(names, take(6)))
    shared = dict(zip(names, take(6)))
    normed, weight, x, midg = take(4)
    kaug, vaug, doaug, qsum, ksum, mixed, part_k, part_v, got_k, got_v = take(10)
    gain_sums, parts_out, parts_in = take(3)
    if square:
        grad_own, payload, gains_sum, outg = take(4)
        held, far_in, onward_out, onward_in, direct_in, line, near_in, second_sum, far_quarter, whole_line = take(10)
        up_out, up_got = take(2)
        relay, final, core_got, chunks, gain_parts, chunk_got, gain_got = take(7)
    sent, got, load_sem, local_sem = take(4)

    chip, core, zp, zq = here()
    z = 2 * zp + zq
    sems = (sent, got)
    partner = (chip, 1 - core, zp, zq)
    keep = (chip, zp, core, zq)
    cross = (chip, zp, core, 1 - zq)
    moves = core != zp
    near_x = (chip ^ 1, core, zp, zq)
    near_y = (chip ^ 2, core, zp, zq)
    along = [(chip, core, zp, 1 - zq), (chip, core, 1 - zp, zq), (chip, core, 1 - zp, 1 - zq)]
    tokens, model = x.shape
    part = tokens // 3
    half, length = 2 * part, 4 * part
    width = model // 2
    queries = half
    waits = []

    def load(source, target, at):
        copy = pltpu.make_async_copy(source, target, load_sem.at[at])
        copy.start()
        return copy

    def send(source, target, at, device):
        copy = remote(source, target, sems, at, device)
        copy.start()
        waits.append(copy)
        return copy

    if square:
        rows_count = packed_in.shape[1]
        span = rows_count // 2
        first_half, second_half = pl.ds(0, span), pl.ds(span, span)
        held_loads = [
            load(packed_in.at[chip ^ 1, first_half], held.at[0], 24),
            load(packed_in.at[chip ^ 2, second_half], held.at[1], 25),
            load(packed_in.at[chip, first_half], held.at[2], 26),
            load(packed_in.at[chip, second_half], held.at[3], 27),
        ]
        far_loads = [load(far_ref.at[i], far_in.at[i], 28 + i) for i in range(2)]
    keys_of = lambda ref: ref.at[:, pl.ds(width, width)]
    load_bufs = lambda source, target, at: [
        load(keys_of(source[name]) if name == "qk" else source[name], target[name], at + i)
        for i, name in enumerate(names)
    ]
    shared_loads = load_bufs(shared_in, shared, 0)
    row_loads = load_bufs(row_in, row, 6)
    late_loads = [
        load(row_in["normed"], normed.at[pl.ds(0, length)], 12),
        load(shared_in["normed"].at[rows_at(zq * part, part)], normed.at[pl.ds(length, part)], 13),
        load(
            shared_in["normed"].at[rows_at((2 + zq) * part, part)], normed.at[pl.ds(length + part, part)], 14
        ),
        load(mix_in, weight, 15),
        load(x_in, x, 16),
        load(midg_in, midg, 17),
    ]
    if square:
        late_loads.append(load(outg_in, outg, 18))
    if square:
        greet([partner, cross, near_x, near_y] + along, keep, moves)
        for copy in held_loads + far_loads:
            copy.wait()
        onward_out[0] = add(far_in[0], held[0]).astype(BF16)
        bulk_on_x = send(onward_out.at[0], onward_in.at[0], 11, near_x)
        onward_out[1] = add(far_in[1], held[1]).astype(BF16)
        bulk_on_y = send(onward_out.at[1], onward_in.at[1], 12, near_y)
        bulk_x = send(packed_in.at[chip ^ 1, second_half], direct_in.at[0], 2, near_x)
        bulk_y = send(packed_in.at[chip ^ 2, first_half], direct_in.at[1], 3, near_y)

        def collect(sources, target, at, turn):
            moved = [
                remote(sources[0], target.at[zq], sems, at, keep),
                remote(sources[2], target.at[2], sems, at + 1, keep),
            ]
            stays = [
                pltpu.make_async_copy(sources[0], target.at[zq], local_sem.at[2 * turn]),
                pltpu.make_async_copy(sources[2], target.at[2], local_sem.at[2 * turn + 1]),
            ]
            crossed = remote(sources[1], target.at[zq], sems, at + 2, cross)

            @pl.when(moves)
            def _():
                for copy in moved:
                    copy.start()

            @pl.when(jnp.logical_not(moves))
            def _():
                for copy in stays:
                    copy.start()

            crossed.start()
            return moved, stays, crossed

        def collected(copies):
            moved, stays, crossed = copies
            crossed.wait()

            @pl.when(moves)
            def _():
                for copy in moved:
                    copy.wait()

            @pl.when(jnp.logical_not(moves))
            def _():
                for copy in stays:
                    copy.wait()

        output_copies = collect((keep_in, cross_in, third_in), output_ref, 4, 0)
    else:
        greet([partner, along[0]])

    gain_sums[...] = jnp.zeros_like(gain_sums)

    def attend_back(bufs, bounds, count, q_lanes_to, k_to, v_to, at, between=None):
        def one(p, _):
            if between is not None:
                pl.when(p == 2)(between)
            lanes = pl.ds(pl.multiple_of(p * 128, 128), 128)
            key_lanes = pl.ds(pl.multiple_of(width + p * 128, 128), 128)
            attend_back_kernel(
                pics, bufs["aug"].at[pl.ds(2 * p, 2)], bufs["qk"].at[:, lanes], bufs["v"].at[:, lanes],
                bufs["out"].at[:, lanes], bufs["do"].at[:, lanes], bufs["raw"].at[:, lanes],
                bufs["raw"].at[:, key_lanes], gain_qk.at[:, lanes], gain_qk.at[:, key_lanes], bounds,
                q_lanes_to(p), k_to(p), v_to(p), gain_sums.at[pl.ds(at, 1), lanes], gain_sums.at[pl.ds(at + 1, 1), lanes],
                kaug, vaug, doaug.at[:, pl.ds(0, count)], qsum.at[:, pl.ds(0, count)], ksum,
            )
            return 0

        lax.fori_loop(0, width // 128, one, 0)

    def mixed_at(start, count, side):
        return lambda p: mixed.at[pl.ds(start, count), pl.ds(pl.multiple_of(side * width + p * 128, 128), 128)]

    whole_lanes = lambda ref: lambda p: ref.at[:, pl.ds(pl.multiple_of(p * 128, 128), 128)]
    for copy in shared_loads:
        copy.wait()
    attend_back(
        shared, bounds_ref.at[1], queries, mixed_at(length, queries, 0), whole_lanes(part_k), whole_lanes(part_v), 0
    )
    side_sends = []
    for i in range(2):
        theirs = rows_at((2 * i + 1 - zq) * part, part)
        there = pl.ds(i * part, part)
        side_sends.append(send(part_k.at[theirs], got_k.at[there], 7 + 2 * i, along[0]))
        side_sends.append(send(part_v.at[theirs], got_v.at[there], 8 + 2 * i, along[0]))
    for copy in row_loads:
        copy.wait()
    def near_line(i):
        return remote(line.at[2 * i + 1 - zq], near_in.at[i], sems, 14 + i, along[0])

    def start_line():
        for copy in (bulk_y, bulk_on_x, bulk_x, bulk_on_y):
            copy.wait_recv()
        first_sum = add(held[2], onward_in[0], direct_in[1]).astype(BF16)
        second_half_sum = add(held[3], onward_in[1], direct_in[0]).astype(BF16)
        for i in range(2):
            line[i] = first_sum[i * quarter_rows : (i + 1) * quarter_rows]
            line[2 + i] = second_half_sum[i * quarter_rows : (i + 1) * quarter_rows]
        for i in range(2):
            near_line(i).start()

    if square:
        quarter_rows = rows_count // 4
    attend_back(
        row, bounds_ref.at[0], length, mixed_at(0, length, 0), mixed_at(0, length, 1), mixed_at(0, length, 2), 2,
        start_line if square else None,
    )

    for copy in side_sends:
        copy.wait_recv()

    def shared_pair(p, _):
        lanes = pl.ds(pl.multiple_of(p * 128, 128), 128)
        key_lanes = pl.ds(pl.multiple_of(width + p * 128, 128), 128)
        shared_keys_kernel(
            part_k.at[:, lanes], part_v.at[:, lanes], got_k.at[:, lanes], got_v.at[:, lanes],
            shared["raw"].at[:, key_lanes], gain_qk.at[:, key_lanes], mixed_at(length, queries, 1)(p),
            mixed_at(length, queries, 2)(p), gain_sums.at[pl.ds(4, 1), lanes],
        )
        return 0

    lax.fori_loop(0, width // 128, shared_pair, 0)
    for copy in late_loads:
        copy.wait()
    other = 1 - core
    block_rows = lambda side, b: (
        rows_at(side * half + b * part, part) if b < 2 else rows_at(length + side * part, part)
    )
    for b in range(3):
        parts_out[pl.ds(b * part, part), :] = nt(mixed[block_rows(other, b), :], weight[...]).astype(BF16)
    part_send = send(parts_out, parts_in, 13, partner)
    if square:
        line_near = [near_line(i) for i in range(2)]
        for copy in line_near:
            copy.wait_recv()
        for i in range(2):
            second_sum[i] = add(line[2 * i + zq], near_in[i]).astype(BF16)
        line_far = send(second_sum.at[1 - zp], far_quarter, 23, along[1])
        waits.extend(line_near)
    shard = model // 8
    if square:
        for i in range(3):
            lanes = slice(i * width, (i + 1) * width)
            value = tn(normed[...], mixed[:, lanes]).astype(BF16)
            for p in range(8):
                payload[p, :shard, lanes] = value[p * shard : (p + 1) * shard]
    else:
        for i in range(3):
            lanes = slice(i * width, (i + 1) * width)
            mix_grad_ref[:, lanes] = tn(normed[...], mixed[:, lanes]).astype(BF16)
    part_send.wait_recv()
    first_sum_gain = jnp.zeros((1, model), F32)
    for b in range(3):
        rows = pl.ds(b * part, part)
        upstream = nt(mixed[block_rows(core, b), :], weight[...]) + parts_in[rows, :].astype(F32)
        n, r = norm_parts(x[rows, :].astype(F32))
        value, more = norm_back(upstream, n, r, gain_first[...])
        first_sum_gain = first_sum_gain + more
        grad_own[rows, :] = (midg[rows, :] + value).astype(BF16)
    gains_sum[...] = jnp.zeros_like(gains_sum)
    gains_sum[0:1, :] = first_sum_gain
    mine_lanes = pl.ds(pl.multiple_of(core * width, 128), width)
    gains_sum[1:2, mine_lanes] = gain_sums[0:1, :] + gain_sums[2:3, :]
    gains_sum[2:3, mine_lanes] = gain_sums[3:4, :] + gain_sums[4:5, :]
    gains_sum[3:4, :] = gain_second_grad[...]

    if square:
        grad_copies = collect(
            (
                grad_own.at[rows_at(zq * part, part)],
                grad_own.at[rows_at((1 - zq) * part, part)],
                grad_own.at[pl.ds(half, part)],
            ),
            grad_out, 16, 1,
        )
        gain_row = shard + shard // 3
        for p in range(8):
            payload[p, gain_row:, :] = jnp.zeros((16, 3 * width), BF16)
            payload[p, gain_row:, :shard] = gains_sum[:, p * shard : (p + 1) * shard].astype(BF16)
            for i in range(3):
                at = p * shard + i * (shard // 3)
                payload[p, shard:gain_row, i * width : (i + 1) * width] = outg[at : at + shard // 3, :]
        mine, theirs = 2 * chip + core, 2 * chip + 1 - core
        x_mine, x_other = 2 * (chip ^ 1) + core, 2 * (chip ^ 1) + 1 - core
        y_mine, y_other = 2 * (chip ^ 2) + core, 2 * (chip ^ 2) + 1 - core
        far_mine, far_other = 2 * (chip ^ 3) + core, 2 * (chip ^ 3) + 1 - core
        first = send(payload.at[far_mine], relay.at[0], 19, near_y)
        second = send(payload.at[far_other], relay.at[1], 20, near_x)
        direct_x = send(payload.at[x_other], final.at[0], 21, near_x)
        direct_y = send(payload.at[y_mine], final.at[1], 22, near_y)

        line_far.wait_recv()
        whole_line[z] = add(second_sum[zp], far_quarter[...]).astype(BF16)
        line_back = send(whole_line.at[z], whole_line.at[z], 33, along[1])
        first.wait_recv()
        relay[2] = add(relay[0], payload[x_mine]).astype(BF16)
        onward_x = send(relay.at[2], final.at[2], 24, near_x)
        second.wait_recv()
        relay[3] = add(relay[1], payload[y_other]).astype(BF16)
        onward_y = send(relay.at[3], final.at[3], 25, near_y)
        direct_x.wait_recv()
        onward_y.wait_recv()
        relay[4] = add(payload[theirs], final[0], final[3]).astype(BF16)
        to_core = send(relay.at[4], core_got, 26, partner)
        direct_y.wait_recv()
        onward_x.wait_recv()
        kept = add(payload[mine], final[1], final[2])
        quarter = gain_row // 2
        for i in range(2):
            chunks[2 * core + i] = kept[i * quarter : (i + 1) * quarter].astype(BF16)
        to_core.wait_recv()
        for i in range(2):
            chunks[2 * (1 - core) + i] = core_got[i * quarter : (i + 1) * quarter]
        gain_parts[0] = (kept[gain_row:] + core_got[gain_row:].astype(F32)).astype(BF16)
        hops = [z ^ 1, z ^ 2, z ^ 3]
        copies = []
        for i in range(3):
            copies.append(send(chunks.at[hops[i]], chunk_got.at[i], 27 + i, along[i]))
            copies.append(send(gain_parts.at[0], gain_got.at[i], 30 + i, along[i]))
        line_back.wait_recv()
        line_last = [
            send(whole_line.at[z], whole_line.at[z], 37, along[0]),
            send(whole_line.at[z ^ 2], whole_line.at[z ^ 2], 38, along[0]),
        ]
        for copy in copies:
            copy.wait_recv()
        gains_ref[...] = add(gain_parts[0], gain_got[0], gain_got[1], gain_got[2])
        chunk_got[3] = add(chunks[z], chunk_got[0], chunk_got[1], chunk_got[2]).astype(BF16)
        spread = [send(chunk_got.at[3], chunk_got.at[4 + i], 34 + i, along[i]) for i in range(3)]

        def place(index, values):
            side, up = index // 2, index % 2
            lanes_of = lambda p: pl.ds(pl.multiple_of((2 * p + side) * width, 128), width)
            below = shard - quarter

            @pl.when(up == 0)
            def _():
                for p in range(3):
                    total_ref[0:quarter, lanes_of(p)] = values[:, p * width : (p + 1) * width]

            @pl.when(up == 1)
            def _():
                for p in range(3):
                    total_ref[quarter:shard, lanes_of(p)] = values[:below, p * width : (p + 1) * width]
                    rows = slice(p * (shard // 3), (p + 1) * (shard // 3))
                    outw_ref[rows, pl.ds(pl.multiple_of(side * width, 128), width)] = values[
                        below:, p * width : (p + 1) * width
                    ]

        place(z, chunk_got[3])
        for i in range(3):
            spread[i].wait_recv()
            place(hops[i], chunk_got[4 + i])

        for copy in line_last:
            copy.wait_recv()
        flat = jnp.concatenate([whole_line[i] for i in range(4)], axis=0)
        tile = down_ref.shape[0]
        down_ref[...] = flat[:tile]
        ups = [flat[tile + 2 * shard * i : tile + 2 * shard * (i + 1)] for i in range(2)]
        for i in range(2):
            up_out[i] = jnp.where(core == 0, ups[i][shard:], ups[i][:shard])
        up_send = send(up_out, up_got, 39, partner)

        def place_up(side, i, values):
            for j in range(2):
                lanes = pl.ds(pl.multiple_of((2 * (2 * i + j) + side) * tile, 128), tile)
                up_ref[:, lanes] = values[:, j * tile : (j + 1) * tile]

        for i in range(2):
            place_up(core, i, jnp.where(core == 0, ups[i][:shard], ups[i][shard:]))
        up_send.wait_recv()
        for i in range(2):
            place_up(other, i, up_got[i])
        collected(output_copies)
        collected(grad_copies)
    for copy in waits:
        copy.wait_send()


def backward_pass(square, pics, row, shared, weights, gains, bounds, *more):
    length, model = row[1].shape
    width = model // 2
    part = length // 4
    half, tokens = 2 * part, 3 * part
    shard = model // 8
    near = pl.BlockSpec(memory_space=pltpu.VMEM)
    anywhere = pl.BlockSpec(memory_space=pl.ANY)
    low = lambda *shape: (shape, BF16)
    wide = lambda *shape: (shape, F32)
    if square:
        rows = more[0].shape[1]
        tile = rows // 2
        outs = [
            (low(3, part, model), anywhere),
            (low(3, part, model), anywhere),
            (low(shard, 6 * width), near),
            (wide(16, 3 * width), near),
            (low(shard, 8 * tile), near),
            (low(tile, model), near),
            (low(shard, model), near),
        ]
    else:
        outs = [(low(tokens, model), near), (low(model, 3 * width), near), (wide(16, model), near)]
    scratch = []
    for queries in (length, half):
        scratch += [
            low(2 * (width // 128), queries, 128), low(length, width), low(length, width), low(queries, width),
            low(queries, width), low(length, 2 * width),
        ]
    scratch += [
        low(length + half, model), low(model, 3 * width), low(tokens, model), wide(tokens, model),
        low(2, length, 128), low(2, length, 128), low(2, length, 128), wide(2, length, 128), wide(length, 128),
        low(length + half, 3 * width), low(length, width), low(length, width), low(half, width), low(half, width),
        wide(8, width), low(tokens, model), low(tokens, model),
    ]
    if square:
        span = rows // 2
        pieces = shard + shard // 3 + 16
        chunk = (pieces - 16) // 2
        scratch += [
            low(tokens, model), low(8, pieces, 3 * width), wide(16, model), low(model, width),
            low(4, span, model), low(2, span, model), low(2, span, model), low(2, span, model), low(2, span, model),
            low(4, rows // 4, model), low(2, rows // 4, model), low(2, rows // 4, model), low(rows // 4, model),
            low(4, rows // 4, model),
            low(2, shard, model), low(2, shard, model),
            low(5, pieces, 3 * width), low(4, pieces, 3 * width), low(pieces, 3 * width), low(4, chunk, 3 * width),
            low(1, 16, 3 * width), low(7, chunk, 3 * width), low(3, 16, 3 * width),
        ]
    return pl.pallas_call(
        functools.partial(backward_kernel, square, pics),
        in_specs=[anywhere] * 17 + [near] * 4 + [anywhere] * len(more),
        out_specs=[spec for _, spec in outs],
        out_shape=[jax.ShapeDtypeStruct(*shape) for shape, _ in outs],
        scratch_shapes=[pltpu.VMEM(*shape) for shape in scratch]
        + [
            pltpu.SemaphoreType.DMA((41,)),
            pltpu.SemaphoreType.DMA((41,)),
            pltpu.SemaphoreType.DMA((30,)),
            pltpu.SemaphoreType.DMA((4,)),
        ],
        compiler_params=pltpu.CompilerParams(
            collective_id=2, has_side_effects=True, vmem_limit_bytes=62 * 1024 * 1024
        ),
        name="backward_pass",
    )(*row, *shared, *weights, *gains, bounds, *more)


def local(
    tokens, lengths, pictures, first_gain, mix_weight, query_gain, key_gain, out_weight,
    second_gain, up_weight, down_weight, cotangent,
):
    chip, core, zp, zq = here()
    chips = lax.axis_size("chip")
    square = chips == 4
    rows = ("chip", "core")
    _, part, model = tokens.shape
    length = 4 * part
    half = 2 * part
    width = HEADS // 2 * HEAD
    pics = lengths.shape[1]
    shard = mix_weight.shape[0]

    hidden = up_weight.shape[1]
    tile = hidden // 8
    gains = [gain[None] for gain in (first_gain, query_gain, key_gain, second_gain)]
    if square:
        forward = forward_pass(
            True, pics, tokens, cotangent, lengths, mix_weight, *gains, up_weight, down_weight, out_weight
        )
        up_half, down_half, out_matrix = forward[19:]
        gain_second = forward[5]
    else:
        gather = lambda weight: lax.all_gather(weight, rows, axis=0, tiled=True)
        half_of = lambda weight, axis: pick(weight, core, axis)
        mix_half = half_of(gather(mix_weight).reshape(model, 3, 2, width), 2).reshape(model, 3 * width)
        up_half = half_of(gather(up_weight).reshape(model, 4, 2, tile), 2).reshape(model, 4 * tile)
        down_half = half_of(gather(down_weight).reshape(4, 2, tile, model), 1).reshape(4 * tile, model)
        out_matrix = gather(out_weight)
        gains = lax.all_gather(jnp.concatenate(gains), rows, axis=0, tiled=False)
        gains = gains.transpose(1, 0, 2).reshape(4, 1, model).astype(F32)
        gain_second = gains[3]
        gain_qk = half_of(gains[1:3].reshape(2, 2, width), 1).reshape(1, model)
        forward = forward_pass(False, pics, tokens, cotangent, lengths, mix_half, gains[0], gain_qk)
    own_tokens, bounds, mix_half, grad_tokens, gain_first, _, gain_qk = forward[:7]
    normed, qk, v, raw, out, aug = forward[7:13]
    shared_normed, shared_qk, shared_v, shared_raw, shared_out, shared_aug = forward[13:19]

    def collect(mine, cross, third):
        mine = lax.ppermute(mine, COLUMN, KEEP)
        cross = lax.ppermute(cross, COLUMN, CROSS)
        third = lax.ppermute(third, COLUMN, KEEP)
        return jnp.stack([jnp.where(zq == 0, mine, cross), jnp.where(zq == 0, cross, mine), third])

    out_keep, out_cross, out_third, middle_grad, grad, shared_grad, out_grad, second_gain_grad, packed, far = dense(
        square, out, shared_out, own_tokens, grad_tokens, out_matrix, gain_second, bounds, up_half, down_half
    )
    row_side = (aug, qk, v, out, grad, raw, normed)
    shared_side = (shared_aug, shared_qk, shared_v, shared_out, shared_grad, shared_raw, shared_normed)
    weights = (mix_half, own_tokens, middle_grad)
    gains = (gain_first, gain_qk, second_gain_grad)
    if square:
        output, input_out, mix_out, gains_out, up_out, down_out, outw_out = backward_pass(
            True, pics, row_side, shared_side, weights, gains, bounds, packed, far, out_grad,
            out_keep, out_cross, out_third,
        )
        gains_out = gains_out[:4, :shard]
        mix_out, up_out, down_out, outw_out = (
            array.astype(F32) for array in (mix_out, up_out, down_out, outw_out)
        )
    else:
        input_grad, mix_grad, gain_grads = backward_pass(
            False, pics, row_side, shared_side, weights, gains, bounds
        )

        def reduce(grad):
            return lax.psum(lax.psum_scatter(grad, rows, scatter_dimension=0, tiled=True), SEQ).astype(F32)

        output = collect(out_keep, out_cross, out_third)
        first, second = input_grad[:part], input_grad[part:half]
        input_out = collect(
            jnp.where(zq == 0, first, second), jnp.where(zq == 0, second, first), input_grad[half:]
        )
        own_core = jnp.arange(2) == core
        eighth = model // 8
        down_grad = packed[:, None, :tile]
        down_out = reduce(jnp.where(own_core[None, :, None, None], down_grad, 0).reshape(hidden, model))
        up_grad = packed[:, tile : 2 * tile].reshape(4, 2, 2 * eighth, 2, tile).transpose(0, 2, 1, 3, 4)
        up_grad = up_grad.reshape(model, 4, 1, tile)
        up_out = reduce(jnp.where(own_core[None, None, :, None], up_grad, 0).reshape(model, hidden))
        out_grad = out_grad.reshape(model, 1, width)
        outw_out = reduce(jnp.where(own_core[None, :, None], out_grad, 0).reshape(model, model))
        mix_out = reduce(
            jnp.where(own_core[None, None, :, None], mix_grad.reshape(model, 3, 1, width), 0).reshape(model, 6 * width)
        )
        gain_grads = gain_grads[:4].reshape(4, 2 * chips, shard).transpose(1, 0, 2).astype(BF16)
        gains_out = reduce(gain_grads).reshape(4, shard)
    return (
        output, input_out, gains_out[0], mix_out, gains_out[1], gains_out[2], outw_out, gains_out[3],
        up_out, down_out,
    )


def solution(mesh):
    fsdp = mesh.shape["fsdp"]
    split = Mesh(mesh.devices.reshape(fsdp // 2, 2, 2, 2), ("chip", "core", "zp", "zq"))
    rows = ("chip", "core")
    return jax.shard_map(
        local,
        mesh=split,
        in_specs=(
            P(rows, SEQ, None),
            P(rows, None),
            P(rows, SEQ),
            P(rows),
            P(rows, None),
            P(rows),
            P(rows),
            P(rows, None),
            P(rows),
            P(rows, None),
            P(rows, None),
            P(rows, SEQ, None),
        ),
        out_specs=(
            P(rows, SEQ, None),
            P(rows, SEQ, None),
            P(rows),
            P(rows, None),
            P(rows),
            P(rows),
            P(rows, None),
            P(rows),
            P(rows, None),
            P(rows, None),
        ),
        check_vma=False,
    )
```

```python
import functools

import jax
import jax.numpy as jnp
from jax import lax
from jax.experimental import pallas as pl
from jax.experimental.pallas import tpu as pltpu
from jax.sharding import Mesh, PartitionSpec as P

HEADS = 12
HEAD = 64
EPSILON = 1e-06
BLOCK = 256
STEP = 512
MARK = 32.0
EXP2_FACTOR = HEAD**-0.5 * 1.4426950408889634
F32 = jnp.float32
BF16 = jnp.bfloat16
VMEM_LIMIT = 56 * 1024 * 1024

SEQ = ("zp", "zq")
COLUMN = ("core", "zp", "zq")
KEEP = [
    (core * 4 + z, (z // 2) * 4 + 2 * core + z % 2) for core in range(2) for z in range(4)
]
CROSS = [
    (core * 4 + z, (z // 2) * 4 + 2 * core + 1 - z % 2) for core in range(2) for z in range(4)
]


def swap(array, name, bit=1):
    count = lax.axis_size(name)
    return lax.ppermute(array, name, [(i, i ^ bit) for i in range(count)])


def pick(array, index, axis=0):
    return lax.dynamic_index_in_dim(array, index, axis, keepdims=False)


def group_ones(scale, size=128):
    row = lax.broadcasted_iota(jnp.int32, (size, size), 0) // HEAD
    column = lax.broadcasted_iota(jnp.int32, (size, size), 1) // HEAD
    return jnp.where(row == column, scale, 0.0).astype(BF16)


def group_sum(values, ones):
    return jnp.dot(values.astype(BF16), ones, preferred_element_type=F32)


def group_sum_fine(values, ones):
    high = values.astype(BF16)
    return group_sum(high, ones) + group_sum(values - high.astype(F32), ones)


def project_kernel(x_ref, gain_ref, weight_ref, qkg_ref, normed_ref, qk_ref, v_ref, raw_ref):
    both = qk_ref.shape[1]
    x = x_ref[...].astype(F32)
    center = x - jnp.mean(x, axis=-1, keepdims=True)
    spread = jnp.mean(center * center, axis=-1, keepdims=True)
    normed = (center * lax.rsqrt(spread + EPSILON) * gain_ref[...]).astype(BF16)
    normed_ref[...] = normed
    ones = group_ones(1.0 / HEAD, 256)
    for at in range(0, both, 256):
        lanes = slice(at, at + 256)
        raw = jnp.dot(normed, weight_ref[:, lanes], preferred_element_type=F32)
        raw_ref[:, lanes] = raw.astype(BF16)
        c = raw - group_sum(raw, ones)
        n = c * lax.rsqrt(group_sum(c * c, ones) + EPSILON)
        qk_ref[:, lanes] = (n * qkg_ref[:, lanes]).astype(BF16)
    v_ref[...] = jnp.dot(normed, weight_ref[:, both:], preferred_element_type=F32).astype(BF16)


def nt(a, b):
    return lax.dot_general(a, b, (((1,), (1,)), ((), ())), preferred_element_type=F32)


def tn(a, b):
    return lax.dot_general(a, b, (((0,), (0,)), ((), ())), preferred_element_type=F32)


def slots(queries, length, part):
    at = lax.broadcasted_iota(jnp.int32, (queries, 128), 0)
    if queries == length:
        return at
    return at % part + part * (lax.axis_index("zq") + 2 * (at // part))


def own_rows(ref, start, count, queries, part):
    if queries == ref.shape[0]:
        return ref[pl.ds(start, count), :]
    zq = lax.axis_index("zq")
    pieces = [
        ref[pl.ds(pl.multiple_of((zq + 2 * i) * part, part), part), :]
        for i in range(start // part, (start + count) // part)
    ]
    return jnp.concatenate(pieces, axis=0)


def query_marks(bounds_ref, place, queries, length, part, pics):
    at = slots(queries, length, part)
    inside = (at >= bounds_ref[0:1, :]) & (at < bounds_ref[2:3, :])
    values = jnp.where(inside, MARK, 0.0)
    return jnp.where(place == pics, MARK, values).astype(BF16)


def key_marks(bounds_ref, place, length, pics):
    at = lax.broadcasted_iota(jnp.int32, (length, 128), 0)
    inside = (at >= bounds_ref[0:1, :]) & (at < bounds_ref[1:2, :])
    values = jnp.where(inside, MARK, 0.0)
    values = jnp.where(place == pics, -MARK, values)
    return jnp.where((place > pics) & (place < pics + 4), 1.0, values).astype(BF16)


def attend_kernel(pics, q_ref, k_ref, v_ref, bounds_ref, out_ref, aug_ref, kaug, vaug, qaug):
    length = k_ref.shape[0]
    queries = out_ref.shape[0]
    part = length // 4
    lane = lax.broadcasted_iota(jnp.int32, (1, 128), 1)
    place = lane % HEAD
    sides = [lane < HEAD, lane >= HEAD]
    kmarks = key_marks(bounds_ref, place, length, pics)
    qmarks = query_marks(bounds_ref, place, queries, length, part, pics)
    qaug[...] = qmarks
    for h in range(2):
        kaug[h] = jnp.where(sides[h], k_ref[...], kmarks)
        vaug[h] = jnp.where(sides[h], v_ref[...], jnp.ones_like(v_ref))
    for b in range(queries // STEP):
        rows = pl.ds(b * STEP, STEP)
        mine = own_rows(q_ref, b * STEP, STEP, queries, part)
        query = [jnp.where(sides[h], mine, qaug[rows, :]) for h in range(2)]
        total = [jnp.zeros((STEP, 128), F32)] * 2
        for j in range(length // STEP):
            keys = pl.ds(j * STEP, STEP)
            scores = [nt(query[h], kaug[h, keys, :]) for h in range(2)]
            weights = [jnp.exp2(x * EXP2_FACTOR).astype(BF16) for x in scores]
            total = [
                total[h] + jnp.dot(weights[h], vaug[h, keys, :], preferred_element_type=F32) for h in range(2)
            ]
        results = []
        for h in range(2):
            results.append(total[h] / pltpu.roll(total[h], HEAD, 1))
            log_total = jnp.log(jnp.where(sides[h], 1.0, total[h])) * -(HEAD**0.5)
            first = log_total.astype(BF16)
            rest = log_total - first.astype(F32)
            middle = rest.astype(BF16)
            last = (rest - middle.astype(F32)).astype(BF16)
            logs = jnp.where(place == pics + 1, first, jnp.where(place == pics + 2, middle, last))
            slot = jnp.logical_not(sides[h]) & (place > pics) & (place < pics + 4)
            aug_ref[h, rows, :] = jnp.where(slot, logs, query[h])
        out_ref[rows, :] = jnp.where(sides[0], results[0], results[1]).astype(BF16)


def head_norm_back(e, raw, gain, means):
    raw = raw.astype(F32)
    c = raw - group_sum(raw, means)
    r = lax.rsqrt(group_sum(c * c, means) + EPSILON)
    n = c * r
    t = e * gain
    grad = r * (t - group_sum(t, means) - n * group_sum(t * n, means))
    return grad.astype(BF16), jnp.sum(e * n, axis=0, keepdims=True)


def attend_back_kernel(
    pics, aug_ref, k_ref, v_ref, out_ref, do_ref, rawq_ref, rawk_ref, qg_ref, kg_ref, bounds_ref,
    dq_ref, dk_ref, dv_ref, qgg_ref, kgg_ref, kaug, vaug, doaug, qsum, ksum,
):
    length = k_ref.shape[0]
    queries = do_ref.shape[0]
    part = length // 4
    whole = queries == length
    lane = lax.broadcasted_iota(jnp.int32, (1, 128), 1)
    place = lane % HEAD
    sides = [lane < HEAD, lane >= HEAD]
    kmarks = key_marks(bounds_ref, place, length, pics)
    vmarks = jnp.where(place < 2, 1.0, 0.0).astype(BF16)
    ones = group_ones(1.0)
    inner = group_sum_fine(do_ref[...].astype(F32) * out_ref[...].astype(F32), ones)
    inner = -pltpu.roll(inner, HEAD, 1)
    inner_high = inner.astype(BF16)
    inner_low = (inner - inner_high.astype(F32)).astype(BF16)
    zero = jnp.zeros((), BF16)
    gmarks = jnp.where(place == 0, inner_high, jnp.where(place == 1, inner_low, zero))
    for h in range(2):
        kaug[h] = jnp.where(sides[h], k_ref[...], kmarks)
        vaug[h] = jnp.where(sides[h], v_ref[...], vmarks)
        doaug[h] = jnp.where(sides[h], do_ref[...], gmarks)
    for b in range(length // STEP):
        keys = pl.ds(b * STEP, STEP)
        key = [kaug[h, keys, :] for h in range(2)]
        value = [vaug[h, keys, :] for h in range(2)]
        dk = [jnp.zeros((STEP, 128), F32)] * 2
        dv = [jnp.zeros((STEP, 128), F32)] * 2
        for j in range(queries // STEP):
            rows = pl.ds(j * STEP, STEP)
            query = [aug_ref[h, rows, :] for h in range(2)]
            grad = [doaug[h, rows, :] for h in range(2)]
            scores = [nt(key[h], query[h]) for h in range(2)]
            soft_grad = [nt(value[h], grad[h]) for h in range(2)]
            weights = [jnp.exp2(x * EXP2_FACTOR) for x in scores]
            score_grad = [(weights[h] * soft_grad[h]).astype(BF16) for h in range(2)]
            for h in range(2):
                part_sum = tn(score_grad[h], key[h])
                if b == 0:
                    qsum[h, rows, :] = part_sum
                else:
                    qsum[h, rows, :] += part_sum
                dk[h] = dk[h] + jnp.dot(score_grad[h], query[h], preferred_element_type=F32)
                dv[h] = dv[h] + jnp.dot(weights[h].astype(BF16), grad[h], preferred_element_type=F32)
        ksum[keys, :] = jnp.where(sides[0], dk[0], dk[1]) * HEAD**-0.5
        dv_ref[keys, :] = jnp.where(sides[0], dv[0], dv[1]).astype(BF16)

    means = group_ones(1.0 / HEAD)
    gain_sum = jnp.zeros((1, 128), F32)
    for b in range(queries // part):
        rows = pl.ds(b * part, part)
        e = jnp.where(sides[0], qsum[0, rows, :], qsum[1, rows, :]) * HEAD**-0.5
        raw = own_rows(rawq_ref, b * part, part, queries, part)
        dq_ref[rows, :], more = head_norm_back(e.astype(BF16).astype(F32), raw, qg_ref[...], means)
        gain_sum = gain_sum + more
    qgg_ref[...] = gain_sum
    gain_sum = jnp.zeros((1, 128), F32)
    for b in range(length // part):
        rows = pl.ds(b * part, part)
        e = ksum[rows, :].astype(BF16)
        if whole:
            dk_ref[rows, :], more = head_norm_back(e.astype(F32), rawk_ref[rows, :], kg_ref[...], means)
            gain_sum = gain_sum + more
        else:
            dk_ref[rows, :] = e
    kgg_ref[...] = gain_sum


def shared_keys_kernel(dk_ref, dv_ref, gotk_ref, gotv_ref, rawk_ref, kg_ref, outk_ref, outv_ref, kgg_ref):
    count = outk_ref.shape[0]
    part = count // 2
    means = group_ones(1.0 / HEAD)
    gain_sum = jnp.zeros((1, 128), F32)
    for b in range(2):
        rows = pl.ds(b * part, part)
        own = lambda ref: own_rows(ref, b * part, part, count, part)
        e = own(dk_ref).astype(F32) + gotk_ref[rows, :].astype(F32)
        outk_ref[rows, :], more = head_norm_back(e, own(rawk_ref), kg_ref[...], means)
        gain_sum = gain_sum + more
        outv_ref[rows, :] = (own(dv_ref).astype(F32) + gotv_ref[rows, :].astype(F32)).astype(BF16)
    kgg_ref[...] = gain_sum


def gelu_pair(h):
    size = jnp.abs(h)
    bell = jnp.exp2(h * h * -0.7213475204444817)
    t = 1.0 / (1.0 + 0.23164189 * size)
    series = t * (0.127414796 + t * (-0.142248368 + t * (0.7107068705 + t * (-0.7265760135 + t * 0.5307027145))))
    tail = series * bell
    below = jnp.where(h < 0.0, tail, 1.0 - tail)
    return h * below, below + h * (bell * 0.3989422804014327)


def norm_parts(values):
    center = values - jnp.mean(values, axis=-1, keepdims=True)
    spread = lax.rsqrt(jnp.mean(center * center, axis=-1, keepdims=True) + EPSILON)
    return center * spread, spread


def norm_back(upstream, n, r, gain):
    t = upstream * gain
    grad = r * (t - jnp.mean(t, axis=-1, keepdims=True) - n * jnp.mean(t * n, axis=-1, keepdims=True))
    return grad, jnp.sum(upstream * n, axis=0, keepdims=True)


MESH_ID = pl.DeviceIdType.MESH


def here():
    return lax.axis_index("chip"), lax.axis_index("core"), lax.axis_index("zp"), lax.axis_index("zq")


def remote(source, target, sems, at, device):
    sent, got = sems
    return pltpu.make_async_remote_copy(
        src_ref=source, dst_ref=target, send_sem=sent.at[at], recv_sem=got.at[at],
        device_id=device, device_id_type=MESH_ID,
    )


def greet(devices, maybe=None, moves=None):
    barrier = pltpu.get_barrier_semaphore()
    for device in devices:
        pl.semaphore_signal(barrier, inc=1, device_id=device, device_id_type=MESH_ID)
    if maybe is None:
        pl.semaphore_wait(barrier, len(devices))
        return

    @pl.when(moves)
    def _():
        pl.semaphore_signal(barrier, inc=1, device_id=maybe, device_id_type=MESH_ID)

    pl.semaphore_wait(barrier, len(devices) + jnp.where(moves, 1, 0))


def rows_at(start, count):
    return pl.ds(pl.multiple_of(start, 16), count)


class Moves:
    def __init__(self, moved, stays, crossed, moves):
        self.moved, self.stays, self.crossed, self.moves = moved, stays, crossed, moves

    def each(self, act):
        if self.crossed is not None:
            act(self.crossed)

        @pl.when(self.moves)
        def _():
            for copy in self.moved:
                act(copy)

        @pl.when(jnp.logical_not(self.moves))
        def _():
            for copy in self.stays:
                act(copy)

    def start(self):
        self.each(lambda copy: copy.start())

    def wait(self):
        self.each(lambda copy: copy.wait())


class Line:
    def __init__(self, parts, whole, right, left, sems, at):
        chip, core, zp, zq = here()
        self.z = 2 * zp + zq
        up, down = jnp.minimum(self.z + 1, 3), jnp.maximum(self.z - 1, 0)
        self.next = (chip, core, up // 2, up % 2)
        self.last = (chip, core, down // 2, down % 2)
        self.parts, self.whole, self.right, self.left = parts, whole, right, left
        self.sems, self.at, self.sends = sems, at, []

    def at_chip(self, z, *acts):
        @pl.when(self.z == z)
        def _():
            for act in acts:
                act()

    def part_copy(self, c, rightward):
        if rightward:
            return remote(self.parts.at[c], self.right.at[3 - c], self.sems, self.at + 3 - c, self.next)
        return remote(self.parts.at[c], self.left.at[c], self.sems, self.at + 3 + c, self.last)

    def whole_copy(self, c, rightward):
        if rightward:
            return remote(self.whole.at[c], self.whole.at[c], self.sems, self.at + 6 + c, self.next)
        return remote(self.whole.at[c], self.whole.at[c], self.sems, self.at + 8 + c, self.last)

    def send(self, z, make, c, rightward):
        self.sends.append((z, make, c, rightward))
        return lambda: make(c, rightward).start()

    def take(self, c, rightward):
        def act():
            self.part_copy(c, rightward).wait_recv()
            came = self.right[3 - c] if rightward else self.left[c]
            self.parts[c] = add(self.parts[c], came).astype(BF16)

        return act

    def got(self, c, rightward):
        return lambda: self.whole_copy(c, rightward).wait_recv()

    def start(self):
        part = self.part_copy
        self.at_chip(0, *[self.send(0, part, c, True) for c in (3, 2, 1)])
        self.at_chip(3, *[self.send(3, part, c, False) for c in (0, 1, 2)])

    def first(self):
        self.at_chip(1, self.take(3, True), self.send(1, self.part_copy, 3, True))
        self.at_chip(2, self.take(0, False), self.send(2, self.part_copy, 0, False))

    def second(self):
        part = self.part_copy
        self.at_chip(
            1, self.take(2, True), self.send(1, part, 2, True), self.take(0, False), self.send(1, part, 0, False)
        )
        self.at_chip(
            2, self.take(1, False), self.send(2, part, 1, False), self.take(3, True), self.send(2, part, 3, True)
        )

    def third(self):
        self.at_chip(0, self.take(0, False))
        self.at_chip(1, self.take(1, True), self.take(1, False))
        self.at_chip(2, self.take(2, True), self.take(2, False))
        self.at_chip(3, self.take(3, True))
        self.whole[self.z] = self.parts[self.z]
        for z in range(4):
            acts = [self.send(z, self.whole_copy, z, True)] if z < 3 else []
            acts += [self.send(z, self.whole_copy, z, False)] if z > 0 else []
            self.at_chip(z, *acts)

    def fourth(self):
        whole = self.whole_copy
        for z in (1, 2):
            self.at_chip(
                z, self.got(z - 1, True), self.send(z, whole, z - 1, True), self.got(z + 1, False),
                self.send(z, whole, z + 1, False),
            )

    def fifth(self):
        whole = self.whole_copy
        self.at_chip(1, self.got(3, False), self.send(1, whole, 3, False))
        self.at_chip(2, self.got(0, True), self.send(2, whole, 0, True))

    def sixth(self):
        self.at_chip(0, *[self.got(c, False) for c in (1, 2, 3)])
        self.at_chip(3, *[self.got(c, True) for c in (2, 1, 0)])

    def wait_sends(self):
        for z in range(4):
            mine = [make(c, rightward) for at, make, c, rightward in self.sends if at == z]
            self.at_chip(z, *[copy.wait_send for copy in mine])


def write_bounds(pics, lens_ref, bounds_ref, zp, zq, length):
    lane = lax.broadcasted_iota(jnp.int32, (8, 128), 1)
    lens = jnp.where(zp == 0, lens_ref[0], lens_ref[1])
    ends = lens
    for hop in (1, 2, 4, 8):
        ends = ends + jnp.where(lane >= hop, pltpu.roll(ends, hop, 1), 0)
    starts = ends - lens
    last = (lens > 0) & (pltpu.roll(lens, 127, 1) == 0)
    query_ends = jnp.where(last, length, ends)
    total = jnp.max(jnp.where(lane < pics, ends, 0), axis=1, keepdims=True)

    def both(values):
        values = jnp.where(lane < HEAD, jnp.where(lane < pics, values, 2 * length), 0)
        return values + pltpu.roll(values, HEAD, 1)

    tables = [both(starts), both(ends), both(query_ends), jnp.broadcast_to(total, (8, 128))]
    for t in range(4):
        table = tables[t]
        bounds_ref[0, t : t + 1, :] = jnp.where(zq == 0, table[0:1], table[1:2])
        bounds_ref[1, t : t + 1, :] = table[2:3]
    bounds_ref[:, 4:, :] = jnp.zeros((2, 4, 128), jnp.int32)


def forward_kernel(square, pics, *refs):
    refs = list(refs)
    take = lambda count: [refs.pop(0) for _ in range(count)]
    tokens_ref, cot_ref, lengths_ref, weight_in = take(4)
    if square:
        gain_in = take(4)
        up_in, outw_ref = take(2)
    else:
        gain_first_in, gain_qk_in = take(2)
    x_out, bounds_ref, mix_hbm, cot_hbm, gain_first, second_ref, gain_qk = take(7)
    names = ("normed", "qk", "v", "raw", "out", "aug")
    outs = [dict(zip(names, take(6))) for _ in range(2)]
    if square:
        up_hbm, outw_hbm = take(2)
    row_ref, shared_ref, cot_out, lens_ref, lens_out = take(5)
    scratch = [dict(zip(names, take(6))) for _ in range(2)]
    kaug, vaug, qaug = take(3)
    if square:
        mix_ref, gains_ref, up_ref, mix_out, gains_out, up_out, outw_out = take(7)
    sent, got, local_sem, write_sem = take(4)

    chip, core, zp, zq = here()
    z = 2 * zp + zq
    part = tokens_ref.shape[1]
    half, length = 2 * part, 4 * part
    sems = (sent, got)
    partner = (chip, 1 - core, zp, zq)
    side = (chip, core, zp, 1 - zq)
    keep = (chip, zp, core, zq)
    cross = (chip, zp, core, 1 - zq)
    moves = core != zp
    near_x = (chip ^ 1, core, zp, zq)
    near_y = (chip ^ 2, core, zp, zq)
    greet([partner, side, cross] + ([near_x, near_y] if square else []), keep, moves)

    def quarter(ref, index):
        return ref.at[rows_at(index * part, part)]

    own_row = remote(tokens_ref.at[zq], quarter(row_ref, z), sems, 0, keep)
    own_shared = remote(tokens_ref.at[2], quarter(shared_ref, z), sems, 2, keep)
    stay_row = pltpu.make_async_copy(tokens_ref.at[zq], quarter(row_ref, z), local_sem.at[0])
    stay_shared = pltpu.make_async_copy(tokens_ref.at[2], quarter(shared_ref, z), local_sem.at[1])

    @pl.when(moves)
    def _():
        own_row.start()

    @pl.when(jnp.logical_not(moves))
    def _():
        stay_row.start()

    cross_row = remote(tokens_ref.at[1 - zq], quarter(row_ref, z), sems, 1, cross)
    cross_row.start()

    @pl.when(moves)
    def _():
        own_shared.start()

    @pl.when(jnp.logical_not(moves))
    def _():
        stay_shared.start()

    lens_ref[...] = jnp.zeros_like(lens_ref)
    lens_ref[: lengths_ref.shape[0], :pics] = lengths_ref[...]
    lens_copy = remote(lens_ref, lens_out.at[core], sems, 8, partner)
    lens_copy.start()
    lens_stay = pltpu.make_async_copy(lens_ref, lens_out.at[core], local_sem.at[2])
    lens_stay.start()
    waits = []
    if square:
        shard = mix_ref.shape[1]
        tile = up_ref.shape[2] // 4
        width = mix_ref.shape[2] // 3
        for h in range(2):
            for i in range(3):
                mix_ref[h, :, i * width : (i + 1) * width] = weight_in[:, (2 * i + h) * width : (2 * i + h + 1) * width]
        gains_ref[...] = jnp.zeros_like(gains_ref)
        for i in range(4):
            gains_ref[i : i + 1, :shard] = gain_in[i][...].astype(F32)
        mine, theirs = 2 * chip + core, 2 * chip + 1 - core
        slot = [9]

        def send(source, target, device):
            copy = remote(source, target, sems, slot[0], device)
            slot[0] += 1
            copy.start()
            waits.append(copy)
            return copy

        def stay(source, target, at):
            copy = pltpu.make_async_copy(source, target, local_sem.at[at])
            copy.start()
            return copy

        def block(ref, start, count):
            return ref.at[rows_at(start, count)]

        mix_piece = lambda index: (block(mix_out, index * shard, shard), gains_out.at[index])

        def send_mix(sources, index, device):
            return [send(source, target, device) for source, target in zip(sources, mix_piece(index))]

        def arrived(copies):
            for copy in copies:
                copy.wait_recv()

        x_mine, y_other = 2 * (chip ^ 1) + core, 2 * (chip ^ 2) + 1 - core
        to_core = send_mix((mix_ref.at[1 - core], gains_ref), mine, partner)
        a_x = send_mix((mix_ref.at[core], gains_ref), mine, near_x)
        a_y = send_mix((mix_ref.at[core], gains_ref), mine, near_y)
        for h in range(2):
            for i in range(4):
                up_ref[h, :, i * tile : (i + 1) * tile] = up_in[:, (2 * i + h) * tile : (2 * i + h + 1) * tile]
        up_core = send(up_ref.at[1 - core], block(up_out, mine * shard, shard), partner)
        out_core = send(outw_ref, block(outw_out, mine * shard, shard), partner)
        stays = [
            stay(mix_ref.at[core], mix_piece(mine)[0], 3),
            stay(gains_ref, gains_out.at[mine], 4),
            stay(up_ref.at[core], block(up_out, mine * shard, shard), 5),
            stay(outw_ref, block(outw_out, mine * shard, shard), 6),
        ]
        arrived(to_core)
        b_x = send_mix(mix_piece(theirs), theirs, near_x)
        b_y = send_mix(mix_piece(theirs), theirs, near_y)
        arrived(a_x)
        a_far = send_mix(mix_piece(x_mine), x_mine, near_y)
        arrived(b_y)
        b_far = send_mix(mix_piece(y_other), y_other, near_x)
        for copy in stays:
            copy.wait()
        arrived([up_core])
        ohalf = shard // 2

        def bundle(first, from_chip):
            same, twin = 2 * from_chip + core, 2 * from_chip + 1 - core
            part_of = 0 if first else 1
            return [
                block(up_out, (same if first else twin) * shard, shard),
                block(outw_out, same * shard + part_of * ohalf, ohalf),
            ]

        def send_bundle(first, from_chip, device):
            return [send(ref, ref, device) for ref in bundle(first, from_chip)]

        first_x = send_bundle(True, chip, near_x)
        first_y = send_bundle(True, chip, near_y)
        second_x = send_bundle(False, chip, near_x)
        second_y = send_bundle(False, chip, near_y)

    lens_copy.wait()
    lens_stay.wait()
    write_bounds(pics, lens_out, bounds_ref, zp, zq, length)
    if square:
        arrived(a_y + b_x + a_far + b_far)
        for p in range(gains_out.shape[0]):
            lanes = slice(p * shard, (p + 1) * shard)
            values = gains_out[p, :, :shard]
            gain_first[:, lanes] = values[0:1]
            second_ref[:, lanes] = values[3:4]
            half_pieces = gains_out.shape[0] // 2

            @pl.when(core == p // half_pieces)
            def _():
                at = (p % half_pieces) * shard
                gain_qk[:, at : at + shard] = values[1:2]
                gain_qk[:, width + at : width + at + shard] = values[2:3]
        weight = mix_out
    else:
        weight = weight_in
        width = weight.shape[1] // 3
        second_ref[...] = jnp.zeros_like(second_ref)
        gain_first[...] = gain_first_in[...]
        gain_qk[...] = gain_qk_in[...]
    writes = []

    def write(source, target, at):
        copy = pltpu.make_async_copy(source, target, write_sem.at[at])
        copy.start()
        writes.append(copy)

    write(weight, mix_hbm, 0)
    first, second = 2 * core + zq, 2 * core + 1 - zq
    other_first, other_second = 2 * (1 - core) + zq, 2 * (1 - core) + 1 - zq

    def forwarded(ref, index, at):
        return remote(quarter(ref, index), quarter(ref, index), sems, at, partner)

    def project(tokens, bufs, at):
        rows = rows_at(at * part, part)
        project_kernel(
            tokens.at[rows], gain_first, weight, gain_qk, bufs["normed"].at[rows], bufs["qk"].at[rows],
            bufs["v"].at[rows], bufs["raw"].at[rows],
        )

    def project_row(i, _):
        @pl.when(i == 0)
        def _():
            @pl.when(moves)
            def _():
                own_row.wait_recv()

            @pl.when(jnp.logical_not(moves))
            def _():
                stay_row.wait()

            forwarded(row_ref, first, 3).start()

        @pl.when(i == 1)
        def _():
            cross_row.wait_recv()
            forwarded(row_ref, second, 4).start()

        @pl.when(i == 2)
        def _():
            forwarded(row_ref, other_first, 3).wait_recv()

        @pl.when(i == 3)
        def _():
            forwarded(row_ref, other_second, 4).wait_recv()

        order = jnp.where(i == 0, first, jnp.where(i == 1, second, jnp.where(i == 2, other_first, other_second)))
        project(row_ref, scratch[0], order)
        return 0

    row_one, row_two = forwarded(row_ref, first, 3), forwarded(row_ref, second, 4)

    def attend(bufs, bounds):
        def one(p, _):
            lanes = pl.ds(pl.multiple_of(p * 128, 128), 128)
            attend_kernel(
                pics, bufs["qk"].at[:, lanes],
                bufs["qk"].at[:, pl.ds(pl.multiple_of(width + p * 128, 128), 128)], bufs["v"].at[:, lanes], bounds,
                bufs["out"].at[:, lanes], bufs["aug"].at[pl.ds(2 * p, 2)], kaug, vaug, qaug.at[pl.ds(0, bufs["out"].shape[0])],
            )
            return 0

        lax.fori_loop(0, width // 128, one, 0)

    lax.fori_loop(0, 4, project_row, 0)
    for i, name in enumerate(("normed", "qk", "v", "raw")):
        write(scratch[0][name], outs[0][name], 1 + i)
    write(row_ref.at[rows_at(core * half, half)], x_out.at[pl.ds(0, half)], 5)

    @pl.when(moves)
    def _():
        own_shared.wait_recv()

    @pl.when(jnp.logical_not(moves))
    def _():
        stay_shared.wait()

    to_side = remote(quarter(shared_ref, first), quarter(shared_ref, first), sems, 5, side)
    to_side.start()
    shared_one = remote(quarter(shared_ref, first), quarter(shared_ref, first), sems, 6, partner)
    shared_one.start()
    cot_own = pl.ds(pl.multiple_of(zq * part, part), part)
    cot_moves = Moves(
        [remote(cot_ref.at[zq], cot_out.at[cot_own], sems, 46, keep)],
        [pltpu.make_async_copy(cot_ref.at[zq], cot_out.at[cot_own], local_sem.at[0])],
        remote(cot_ref.at[1 - zq], cot_out.at[cot_own], sems, 48, cross),
        moves,
    )
    cot_moves.start()
    attend(scratch[0], bounds_ref.at[0])
    write(scratch[0]["out"], outs[0]["out"], 6)
    write(scratch[0]["aug"], outs[0]["aug"], 7)
    to_side.wait_recv()
    shared_two = forwarded(shared_ref, second, 7)
    shared_two.start()
    if square:
        arrived(first_x + second_y)
        far_first = send_bundle(True, chip ^ 1, near_y)
        far_second = send_bundle(False, chip ^ 2, near_x)
    shared_one.wait_recv()
    shared_two.wait_recv()

    def project_shared(i, _):
        project(shared_ref, scratch[1], i)
        return 0

    lax.fori_loop(0, 4, project_shared, 0)
    for i, name in enumerate(("normed", "qk", "v", "raw")):
        write(scratch[1][name], outs[1][name], 8 + i)
    write(shared_ref.at[rows_at(first * part, part)], x_out.at[pl.ds(half, part)], 12)
    attend(scratch[1], bounds_ref.at[1])
    write(scratch[1]["out"], outs[1]["out"], 13)
    write(scratch[1]["aug"], outs[1]["aug"], 14)

    if square:
        arrived(first_y + second_x + far_first + far_second)
        sent_pieces = []
        for c in (chip ^ 1, chip ^ 2, chip ^ 3):
            target = block(outw_out, (2 * c + core) * shard, shard)
            sent_pieces.append(send(target, target, partner))
        write(up_out, up_hbm, 15)
        arrived(sent_pieces + [out_core])
        write(outw_out, outw_hbm, 17)
        for copy in waits:
            copy.wait_send()
    cot_moves.wait()
    write(cot_out, cot_hbm, 18)
    for copy in (row_one, row_two, shared_one, shared_two, to_side, cross_row):
        copy.wait_send()

    @pl.when(moves)
    def _():
        own_row.wait_send()
        own_shared.wait_send()

    for copy in writes:
        copy.wait()


def forward_pass(square, pics, tokens, cotangent, lengths, weight, *more):
    _, part, model = tokens.shape
    length, half, width = 4 * part, 2 * part, model // 2
    near = pl.BlockSpec(memory_space=pltpu.VMEM)
    anywhere = pl.BlockSpec(memory_space=pl.ANY)
    low = lambda *shape: (shape, BF16)
    wide = lambda *shape: (shape, F32)
    outs = [
        (low(3 * part, model), anywhere),
        (((2, 8, 128), jnp.int32), near),
        (low(model, 3 * width), anywhere),
        (low(half, model), anywhere),
        (wide(1, model), near),
        (wide(1, model), near),
        (wide(1, model), near),
    ]
    bufs = []
    for queries in (length, half):
        shapes = [
            low(length, model), low(length, 2 * width), low(length, width), low(length, 2 * width),
            low(queries, width), low(2 * (width // 128), queries, 128),
        ]
        outs += [(shape, anywhere) for shape in shapes]
        bufs += shapes
    table = ((8, 128), jnp.int32)
    scratch = [low(length, model), low(length, model), low(half, model), table, ((2, 8, 128), jnp.int32)] + bufs
    scratch += [low(2, length, 128), low(2, length, 128), low(length, 128)]
    if square:
        up, _ = more[4:]
        shard, hidden = up.shape
        landed = [low(model, hidden // 2), low(model, model)]
        outs += [(shape, anywhere) for shape in landed]
        scratch += [low(2, shard, 3 * width), wide(8, 128), low(2, shard, hidden // 2)]
        scratch += [low(model, 3 * width), wide(8, 8, 128)] + landed
    return pl.pallas_call(
        functools.partial(forward_kernel, square, pics),
        in_specs=[near] * (4 + len(more)),
        out_specs=[spec for _, spec in outs],
        out_shape=[jax.ShapeDtypeStruct(*shape) for shape, _ in outs],
        scratch_shapes=[pltpu.VMEM(*shape) for shape in scratch]
        + [
            pltpu.SemaphoreType.DMA((49,)),
            pltpu.SemaphoreType.DMA((49,)),
            pltpu.SemaphoreType.DMA((8,)),
            pltpu.SemaphoreType.DMA((19,)),
        ],
        compiler_params=pltpu.CompilerParams(
            collective_id=0, has_side_effects=True, vmem_limit_bytes=60 * 1024 * 1024
        ),
        name="forward_pass",
    )(tokens, cotangent, lengths, weight, *more)


def dense_kernel(
    square, out_ref, shared_ref, x, grad_ref, cot_ref, outw_ref, gain_ref, bounds_ref, up_ref, down_ref,
    output_ref, midg_ref, row_grad, shared_grad, outg_ref, gaing_ref, packed_ref, far_ref,
    att_other, second, turned, grad, third, hidden_all, pre_all, forward, backward, middle, up, down,
    results, parts_out, parts_in, heads_out, cols_out, cols_in, stage, far_in,
    sent, got, load_sem, write_sem, local_sem,
):
    chip, core, zp, zq = here()
    sems = (sent, got)
    partner = (chip, 1 - core, zp, zq)
    keep = (chip, zp, core, zq)
    cross = (chip, zp, core, 1 - zq)
    moves = core != zp
    near_x = (chip ^ 1, core, zp, zq)
    near_y = (chip ^ 2, core, zp, zq)
    tokens, model = midg_ref.shape
    part = tokens // 3
    half = 2 * part
    width = out_ref.shape[1]
    units = up.shape[1]
    tile = units // 4
    other = 1 - core
    mine, theirs = pl.ds(0, tokens), pl.ds(tokens, tokens)
    own_down = down.at[rows_at(chip * tile, tile)] if square else down
    loads = [
        pltpu.make_async_copy(up_ref, up, load_sem.at[0]),
        pltpu.make_async_copy(down_ref, own_down, load_sem.at[1]),
    ]
    for copy in loads:
        copy.start()
    greet([partner, cross] + ([near_x, near_y] if square else []), keep, moves)
    att_sends = [
        remote(out_ref.at[rows_at(other * half, half)], att_other.at[pl.ds(0, half)], sems, 0, partner),
        remote(shared_ref.at[rows_at(other * part, part)], att_other.at[pl.ds(half, part)], sems, 1, partner),
    ]
    for copy in att_sends:
        copy.start()
    third_move = Moves(
        [remote(cot_ref.at[2], third, sems, 11, keep)],
        [pltpu.make_async_copy(cot_ref.at[2], third, local_sem.at[0])],
        None,
        moves,
    )
    third_move.start()

    def down_half(index, which):
        return down.at[rows_at(index * tile + which * (tile // 2), tile // 2)]

    def send_down(index, which, at, device):
        copy = remote(down_half(index, which), down_half(index, which), sems, at, device)
        copy.start()
        return copy

    slot = lax.broadcasted_iota(jnp.int32, (part, 1), 0)
    filled, shared_filled = bounds_ref[0, 3:4, 0:1], bounds_ref[1, 3:4, 0:1]
    none = jnp.zeros((), BF16)
    for b in range(2):
        rows = pl.ds(b * part, part)
        grad[rows, :] = jnp.where(slot + (2 * core + b) * part < filled, grad_ref[rows, :], none)
    grad_sends = [remote(grad.at[pl.ds(0, half)], grad.at[pl.ds(tokens, half)], sems, 2, partner)]
    grad_sends[0].start()

    own_rows_of = lambda b: (
        out_ref[rows_at(core * half + b * part, part), :] if b < 2 else shared_ref[rows_at(core * part, part), :]
    )
    own_weight = outw_ref[rows_at(core * width, width), :]
    other_weight = outw_ref[rows_at(other * width, width), :]
    blocks = [pl.ds(b * part, part) for b in range(3)]
    for b in range(3):
        middle[blocks[b], :] = x[blocks[b], :].astype(F32) + jnp.dot(
            own_rows_of(b), own_weight, preferred_element_type=F32
        )
    for copy in loads:
        copy.wait()
    if square:
        down_sends = [
            send_down(chip, 0, 12, near_x), send_down(chip, 1, 13, near_y), send_down(chip, 0, 14, near_y),
            send_down(chip, 1, 15, near_x),
        ]
    for copy in att_sends:
        copy.wait_recv()
    for rows in blocks:
        value = middle[rows, :] + jnp.dot(att_other[rows, :], other_weight, preferred_element_type=F32)
        middle[rows, :] = value
        second[rows, :] = (norm_parts(value)[0] * gain_ref[...]).astype(BF16)
    second_send = remote(second.at[mine], second.at[theirs], sems, 3, partner)
    second_send.start()

    def hidden_forward(start):
        rows = pl.ds(start, tokens)

        def one_tile(i, _):
            here_units = pl.ds(pl.multiple_of(i * tile, 128), tile)
            hidden, slope = gelu_pair(jnp.dot(second[rows, :], up[:, here_units], preferred_element_type=F32))
            hidden_all[rows, here_units] = hidden.astype(BF16)
            pre_all[rows, here_units] = slope.astype(BF16)
            return 0

        lax.fori_loop(0, 4, one_tile, 0)

    def hidden_backward(start):
        rows = pl.ds(start, tokens)

        def one_tile(i, _):
            here_units = pl.ds(pl.multiple_of(i * tile, 128), tile)
            pre_grad = nt(grad[rows, :], down[rows_at(i * tile, tile), :]) * pre_all[rows, here_units].astype(F32)
            pre_all[rows, here_units] = pre_grad.astype(BF16)
            return 0

        lax.fori_loop(0, 4, one_tile, 0)

    hidden_forward(0)
    if square:
        down_sends[0].wait_recv()
        down_sends[1].wait_recv()
        down_sends += [send_down(chip ^ 1, 0, 16, near_y), send_down(chip ^ 2, 1, 17, near_x)]
    third_move.wait()
    grad[blocks[2], :] = jnp.where(slot + (2 * core + zq) * part < shared_filled, third[...], none)
    grad_sends.append(remote(grad.at[blocks[2]], grad.at[pl.ds(tokens + half, part)], sems, 18, partner))
    grad_sends[1].start()
    second_send.wait_recv()
    hidden_forward(tokens)
    if square:
        for copy in down_sends[2:]:
            copy.wait_recv()
    for b in range(3):
        rows, there = pl.ds(tokens + b * part, part), blocks[b]
        parts_out[0, there, :] = jnp.dot(hidden_all[rows, :], down[...], preferred_element_type=F32).astype(BF16)
    first_part = remote(parts_out.at[0], parts_in.at[0], sems, 4, partner)
    first_part.start()
    for rows in blocks:
        forward[rows, :] = middle[rows, :] + jnp.dot(hidden_all[rows, :], down[...], preferred_element_type=F32)
    first_part.wait_recv()
    for rows in blocks:
        results[rows, :] = (forward[rows, :] + parts_in[0, rows, :].astype(F32)).astype(BF16)
    kept_rows, third_rows = results.at[rows_at(zq * part, part)], results.at[pl.ds(half, part)]
    output_moves = Moves(
        [
            remote(kept_rows, output_ref.at[zq], sems, 19, keep),
            remote(third_rows, output_ref.at[2], sems, 20, keep),
        ],
        [
            pltpu.make_async_copy(kept_rows, output_ref.at[zq], local_sem.at[1]),
            pltpu.make_async_copy(third_rows, output_ref.at[2], local_sem.at[2]),
        ],
        remote(results.at[rows_at((1 - zq) * part, part)], output_ref.at[zq], sems, 21, cross),
        moves,
    )
    output_moves.start()
    for copy in grad_sends:
        copy.wait_recv()
    hidden_backward(tokens)
    for b in range(3):
        rows, there = pl.ds(tokens + b * part, part), blocks[b]
        parts_out[1, there, :] = nt(pre_all[rows, :], up[...]).astype(BF16)
    second_part = remote(parts_out.at[1], parts_in.at[1], sems, 5, partner)
    second_part.start()
    hidden_backward(0)
    for rows in blocks:
        backward[rows, :] = nt(pre_all[rows, :], up[...])

    turned[...] = second[...].T
    quarter = model // 4
    far_sends = [
        remote(stage.at[0, pl.ds(0, tile)], far_in.at[0], sems, 9, near_y),
        remote(stage.at[0, pl.ds(tile, tile)], far_in.at[1], sems, 10, near_x),
    ]

    def weight_grads(i, _):
        target = chip ^ (3 - i) if square else 3 - i
        place = jnp.where(i == 0, 0, 1 + i % 2)

        @pl.when(i == 3)
        def _():
            pltpu.make_async_copy(stage.at[place], packed_ref.at[target], write_sem.at[place]).wait()

        here_units = pl.ds(pl.multiple_of(target * tile, 128), tile)
        stage[place, pl.ds(0, tile), :] = tn(hidden_all[:, here_units], grad[...]).astype(BF16)
        values = jnp.dot(
            turned[rows_at(target * quarter, quarter), :], pre_all[...], preferred_element_type=F32
        ).astype(BF16)
        for j in range(2):
            stage[place, pl.ds(tile + j * quarter, quarter), :] = values[:, j * model : (j + 1) * model]
        pltpu.make_async_copy(stage.at[place], packed_ref.at[target], write_sem.at[place]).start()
        if square:

            @pl.when(i == 0)
            def _():
                for copy in far_sends:
                    copy.start()

        return 0

    lax.fori_loop(0, 4, weight_grads, 0)

    second_send.wait_send()
    second_part.wait_recv()
    gain_sum = jnp.zeros(gaing_ref.shape, F32)
    for rows in blocks:
        n, r = norm_parts(middle[rows, :])
        upstream = backward[rows, :] + parts_in[1, rows, :].astype(F32)
        more, gain_more = norm_back(upstream, n, r, gain_ref[...])
        gain_sum = gain_sum + gain_more
        value = grad[rows, :].astype(F32) + more
        midg_ref[rows, :] = value
        branch = value.astype(BF16)
        second[rows, :] = branch
        heads_out[rows, :] = nt(branch, other_weight).astype(BF16)
    gaing_ref[...] = gain_sum
    head_sends = [
        remote(heads_out.at[pl.ds(0, half)], row_grad.at[rows_at(core * half, half)], sems, 6, partner),
        remote(heads_out.at[pl.ds(half, part)], shared_grad.at[rows_at(core * part, part)], sems, 7, partner),
    ]
    for copy in head_sends:
        copy.start()
    branch = second[mine, :]
    forward[rows_at(core * width, width), :] = tn(
        out_ref[rows_at(core * half, half), :], second[pl.ds(0, half), :]
    ) + tn(shared_ref[rows_at(core * part, part), :], second[pl.ds(half, part), :])
    forward[rows_at(other * width, width), :] = tn(att_other[...], branch)
    lanes = lambda side: pl.ds(pl.multiple_of(side * width, 128), width)
    cols_out[...] = forward[pl.ds(0, model), lanes(other)].astype(BF16)
    cols_send = remote(cols_out, cols_in, sems, 8, partner)
    cols_send.start()
    for b in range(3):
        value = nt(second[blocks[b], :], own_weight).astype(BF16)
        if b < 2:
            row_grad[rows_at(core * half + b * part, part), :] = value
        else:
            shared_grad[rows_at(core * part, part), :] = value
    cols_send.wait_recv()
    outg_ref[...] = (forward[pl.ds(0, model), lanes(core)] + cols_in[...].astype(F32)).astype(BF16)
    for copy in head_sends:
        copy.wait_recv()
    for copy in att_sends + head_sends + grad_sends + [first_part, second_part, cols_send]:
        copy.wait_send()
    if square:
        for copy in down_sends:
            copy.wait_send()
        for copy in far_sends:
            copy.wait()
    far_write = pltpu.make_async_copy(far_in, far_ref, load_sem.at[0])
    far_write.start()
    for place in range(3):
        pltpu.make_async_copy(stage.at[place], packed_ref.at[0], write_sem.at[place]).wait()
    output_moves.wait()
    far_write.wait()


def dense(square, out, shared_out, x, grad, cotangent, out_matrix, gain, bounds, up, down):
    model = x.shape[1]
    tokens = x.shape[0]
    part = tokens // 3
    length, width = out.shape
    units = up.shape[1]
    tile = units // 4
    anywhere = pl.BlockSpec(memory_space=pl.ANY)
    near = pl.BlockSpec(memory_space=pltpu.VMEM)
    both = 2 * tokens
    low = lambda *shape: pltpu.VMEM(shape, BF16)
    wide = lambda *shape: pltpu.VMEM(shape, F32)
    return pl.pallas_call(
        functools.partial(dense_kernel, square),
        in_specs=[near] * 4 + [anywhere] + [near] * 3 + [anywhere] * 2,
        out_specs=[anywhere] + [near] * 5 + [anywhere, anywhere],
        out_shape=[
            jax.ShapeDtypeStruct((3, part, model), BF16),
            jax.ShapeDtypeStruct((tokens, model), F32),
            jax.ShapeDtypeStruct((length, width), BF16),
            jax.ShapeDtypeStruct((length // 2, width), BF16),
            jax.ShapeDtypeStruct((model, width), BF16),
            jax.ShapeDtypeStruct((1, model), F32),
            jax.ShapeDtypeStruct((4, 2 * tile, model), BF16),
            jax.ShapeDtypeStruct((2, tile, model), BF16),
        ],
        scratch_shapes=[
            low(tokens, width), low(both, model), low(model, both), low(both, model), low(part, model),
            low(both, units), low(both, units), wide(tokens, model), wide(tokens, model), wide(tokens, model),
            low(model, units), low(units, model), low(tokens, model), low(2, tokens, model), low(2, tokens, model),
            low(tokens, width), low(model, width), low(model, width), low(3, 2 * tile, model), low(2, tile, model),
            pltpu.SemaphoreType.DMA((22,)),
            pltpu.SemaphoreType.DMA((22,)),
            pltpu.SemaphoreType.DMA((2,)),
            pltpu.SemaphoreType.DMA((3,)),
            pltpu.SemaphoreType.DMA((3,)),
        ],
        compiler_params=pltpu.CompilerParams(
            collective_id=1, has_side_effects=True, vmem_limit_bytes=63 * 1024 * 1024
        ),
        name="dense",
    )(out, shared_out, x, grad, cotangent, out_matrix, gain, bounds, up, down)


def add(*terms):
    total = terms[0].astype(F32)
    for term in terms[1:]:
        total = total + term.astype(F32)
    return total


def backward_kernel(square, pics, *refs):
    refs = list(refs)
    take = lambda count: [refs.pop(0) for _ in range(count)]
    names = ("aug", "qk", "v", "out", "do", "raw", "normed")
    row_in = dict(zip(names, take(7)))
    shared_in = dict(zip(names, take(7)))
    mix_in, x_in, midg_in, gain_first, gain_qk, gain_second_grad, bounds_ref = take(7)
    if square:
        packed_in, far_ref, outg_in = take(3)
        grad_out, total_ref, gains_ref, up_ref, down_ref, outw_ref = take(6)
    else:
        grad_own, mix_grad_ref, gains_sum = take(3)
    names = names[:-1]
    row = dict(zip(names, take(6)))
    shared = dict(zip(names, take(6)))
    normed, weight, x, midg = take(4)
    kaug, vaug, doaug, qsum, ksum, mixed, part_k, part_v, got_k, got_v = take(10)
    gain_sums, parts_out, parts_in = take(3)
    if square:
        grad_own, payload, gains_sum, outg = take(4)
        held, far_in, onward_out, onward_in, direct_in, line, whole_line, line_right, line_left = take(9)
        up_out, up_got = take(2)
        relay, final, core_got, chunks, chunk_whole, chunk_right, chunk_left, gain_parts, gain_got = take(9)
    sent, got, load_sem, local_sem = take(4)

    chip, core, zp, zq = here()
    z = 2 * zp + zq
    sems = (sent, got)
    partner = (chip, 1 - core, zp, zq)
    keep = (chip, zp, core, zq)
    cross = (chip, zp, core, 1 - zq)
    moves = core != zp
    near_x = (chip ^ 1, core, zp, zq)
    near_y = (chip ^ 2, core, zp, zq)
    along = [(chip, core, zp, 1 - zq), (chip, core, 1 - zp, zq), (chip, core, 1 - zp, 1 - zq)]
    tokens, model = x.shape
    part = tokens // 3
    half, length = 2 * part, 4 * part
    width = model // 2
    queries = half
    waits = []

    def load(source, target, at):
        copy = pltpu.make_async_copy(source, target, load_sem.at[at])
        copy.start()
        return copy

    def send(source, target, at, device):
        copy = remote(source, target, sems, at, device)
        copy.start()
        waits.append(copy)
        return copy

    if square:
        rows_count = packed_in.shape[1]
        span = rows_count // 2
        first_half, second_half = pl.ds(0, span), pl.ds(span, span)
        held_loads = [
            load(packed_in.at[chip ^ 1, first_half], held.at[0], 24),
            load(packed_in.at[chip ^ 2, second_half], held.at[1], 25),
            load(packed_in.at[chip, first_half], held.at[2], 26),
            load(packed_in.at[chip, second_half], held.at[3], 27),
        ]
        far_loads = [load(far_ref.at[i], far_in.at[i], 28 + i) for i in range(2)]
    keys_of = lambda ref: ref.at[:, pl.ds(width, width)]
    load_bufs = lambda source, target, at: [
        load(keys_of(source[name]) if name == "qk" else source[name], target[name], at + i)
        for i, name in enumerate(names)
    ]
    shared_loads = load_bufs(shared_in, shared, 0)
    row_loads = load_bufs(row_in, row, 6)
    late_loads = [
        load(row_in["normed"], normed.at[pl.ds(0, length)], 12),
        load(shared_in["normed"].at[rows_at(zq * part, part)], normed.at[pl.ds(length, part)], 13),
        load(
            shared_in["normed"].at[rows_at((2 + zq) * part, part)], normed.at[pl.ds(length + part, part)], 14
        ),
        load(mix_in, weight, 15),
        load(x_in, x, 16),
        load(midg_in, midg, 17),
    ]
    if square:
        late_loads.append(load(outg_in, outg, 18))
    if square:
        greet([partner, cross, near_x, near_y] + along, keep, moves)
        for copy in held_loads + far_loads:
            copy.wait()
        onward_out[0] = add(far_in[0], held[0]).astype(BF16)
        bulk_on_x = send(onward_out.at[0], onward_in.at[0], 11, near_x)
        onward_out[1] = add(far_in[1], held[1]).astype(BF16)
        bulk_on_y = send(onward_out.at[1], onward_in.at[1], 12, near_y)
        bulk_x = send(packed_in.at[chip ^ 1, second_half], direct_in.at[0], 2, near_x)
        bulk_y = send(packed_in.at[chip ^ 2, first_half], direct_in.at[1], 3, near_y)

        bulk_line = Line(line, whole_line, line_right, line_left, sems, 14)
        mix_line = Line(chunks, chunk_whole, chunk_right, chunk_left, sems, 26)
    else:
        greet([partner, along[0]])

    gain_sums[...] = jnp.zeros_like(gain_sums)

    def attend_back(bufs, bounds, count, q_lanes_to, k_to, v_to, at, between=None):
        def one(p, _):
            if between is not None:
                pl.when(p == 2)(between)
            lanes = pl.ds(pl.multiple_of(p * 128, 128), 128)
            key_lanes = pl.ds(pl.multiple_of(width + p * 128, 128), 128)
            attend_back_kernel(
                pics, bufs["aug"].at[pl.ds(2 * p, 2)], bufs["qk"].at[:, lanes], bufs["v"].at[:, lanes],
                bufs["out"].at[:, lanes], bufs["do"].at[:, lanes], bufs["raw"].at[:, lanes],
                bufs["raw"].at[:, key_lanes], gain_qk.at[:, lanes], gain_qk.at[:, key_lanes], bounds,
                q_lanes_to(p), k_to(p), v_to(p), gain_sums.at[pl.ds(at, 1), lanes], gain_sums.at[pl.ds(at + 1, 1), lanes],
                kaug, vaug, doaug.at[:, pl.ds(0, count)], qsum.at[:, pl.ds(0, count)], ksum,
            )
            return 0

        lax.fori_loop(0, width // 128, one, 0)

    def mixed_at(start, count, side):
        return lambda p: mixed.at[pl.ds(start, count), pl.ds(pl.multiple_of(side * width + p * 128, 128), 128)]

    whole_lanes = lambda ref: lambda p: ref.at[:, pl.ds(pl.multiple_of(p * 128, 128), 128)]
    for copy in shared_loads:
        copy.wait()
    attend_back(
        shared, bounds_ref.at[1], queries, mixed_at(length, queries, 0), whole_lanes(part_k), whole_lanes(part_v), 0
    )
    side_sends = []
    for i in range(2):
        theirs = rows_at((2 * i + 1 - zq) * part, part)
        there = pl.ds(i * part, part)
        side_sends.append(send(part_k.at[theirs], got_k.at[there], 7 + 2 * i, along[0]))
        side_sends.append(send(part_v.at[theirs], got_v.at[there], 8 + 2 * i, along[0]))
    for copy in row_loads:
        copy.wait()
    def start_line():
        for copy in (bulk_y, bulk_on_x, bulk_x, bulk_on_y):
            copy.wait_recv()
        first_sum = add(held[2], onward_in[0], direct_in[1]).astype(BF16)
        second_half_sum = add(held[3], onward_in[1], direct_in[0]).astype(BF16)
        for i in range(2):
            line[i] = first_sum[i * quarter_rows : (i + 1) * quarter_rows]
            line[2 + i] = second_half_sum[i * quarter_rows : (i + 1) * quarter_rows]
        bulk_line.start()

    if square:
        quarter_rows = rows_count // 4
    attend_back(
        row, bounds_ref.at[0], length, mixed_at(0, length, 0), mixed_at(0, length, 1), mixed_at(0, length, 2), 2,
        start_line if square else None,
    )

    if square:
        bulk_line.first()
    for copy in side_sends:
        copy.wait_recv()

    def shared_pair(p, _):
        lanes = pl.ds(pl.multiple_of(p * 128, 128), 128)
        key_lanes = pl.ds(pl.multiple_of(width + p * 128, 128), 128)
        shared_keys_kernel(
            part_k.at[:, lanes], part_v.at[:, lanes], got_k.at[:, lanes], got_v.at[:, lanes],
            shared["raw"].at[:, key_lanes], gain_qk.at[:, key_lanes], mixed_at(length, queries, 1)(p),
            mixed_at(length, queries, 2)(p), gain_sums.at[pl.ds(4, 1), lanes],
        )
        return 0

    lax.fori_loop(0, width // 128, shared_pair, 0)
    for copy in late_loads:
        copy.wait()
    other = 1 - core
    block_rows = lambda side, b: (
        rows_at(side * half + b * part, part) if b < 2 else rows_at(length + side * part, part)
    )
    for b in range(3):
        parts_out[pl.ds(b * part, part), :] = nt(mixed[block_rows(other, b), :], weight[...]).astype(BF16)
    part_send = send(parts_out, parts_in, 13, partner)
    if square:
        bulk_line.second()
    shard = model // 8
    if square:
        for i in range(3):
            lanes = slice(i * width, (i + 1) * width)
            value = tn(normed[...], mixed[:, lanes]).astype(BF16)
            for p in range(8):
                payload[p, :shard, lanes] = value[p * shard : (p + 1) * shard]
        bulk_line.third()
    else:
        for i in range(3):
            lanes = slice(i * width, (i + 1) * width)
            mix_grad_ref[:, lanes] = tn(normed[...], mixed[:, lanes]).astype(BF16)
    part_send.wait_recv()
    first_sum_gain = jnp.zeros((1, model), F32)
    for b in range(3):
        rows = pl.ds(b * part, part)
        upstream = nt(mixed[block_rows(core, b), :], weight[...]) + parts_in[rows, :].astype(F32)
        n, r = norm_parts(x[rows, :].astype(F32))
        value, more = norm_back(upstream, n, r, gain_first[...])
        first_sum_gain = first_sum_gain + more
        grad_own[rows, :] = (midg[rows, :] + value).astype(BF16)
    gains_sum[...] = jnp.zeros_like(gains_sum)
    gains_sum[0:1, :] = first_sum_gain
    mine_lanes = pl.ds(pl.multiple_of(core * width, 128), width)
    gains_sum[1:2, mine_lanes] = gain_sums[0:1, :] + gain_sums[2:3, :]
    gains_sum[2:3, mine_lanes] = gain_sums[3:4, :] + gain_sums[4:5, :]
    gains_sum[3:4, :] = gain_second_grad[...]

    if square:
        kept_rows, third_rows = grad_own.at[rows_at(zq * part, part)], grad_own.at[pl.ds(half, part)]
        grad_moves = Moves(
            [
                remote(kept_rows, grad_out.at[zq], sems, 0, keep),
                remote(third_rows, grad_out.at[2], sems, 1, keep),
            ],
            [
                pltpu.make_async_copy(kept_rows, grad_out.at[zq], local_sem.at[0]),
                pltpu.make_async_copy(third_rows, grad_out.at[2], local_sem.at[1]),
            ],
            remote(grad_own.at[rows_at((1 - zq) * part, part)], grad_out.at[zq], sems, 4, cross),
            moves,
        )
        grad_moves.start()
        gain_row = shard + shard // 3
        for p in range(8):
            payload[p, gain_row:, :] = jnp.zeros((16, 3 * width), BF16)
            payload[p, gain_row:, :shard] = gains_sum[:, p * shard : (p + 1) * shard].astype(BF16)
            for i in range(3):
                at = p * shard + i * (shard // 3)
                payload[p, shard:gain_row, i * width : (i + 1) * width] = outg[at : at + shard // 3, :]
        mine, theirs = 2 * chip + core, 2 * chip + 1 - core
        x_mine, x_other = 2 * (chip ^ 1) + core, 2 * (chip ^ 1) + 1 - core
        y_mine, y_other = 2 * (chip ^ 2) + core, 2 * (chip ^ 2) + 1 - core
        far_mine, far_other = 2 * (chip ^ 3) + core, 2 * (chip ^ 3) + 1 - core
        first = send(payload.at[far_mine], relay.at[0], 38, near_y)
        second = send(payload.at[far_other], relay.at[1], 39, near_x)
        direct_x = send(payload.at[x_other], final.at[0], 40, near_x)
        direct_y = send(payload.at[y_mine], final.at[1], 41, near_y)

        first.wait_recv()
        relay[2] = add(relay[0], payload[x_mine]).astype(BF16)
        onward_x = send(relay.at[2], final.at[2], 42, near_x)
        second.wait_recv()
        relay[3] = add(relay[1], payload[y_other]).astype(BF16)
        onward_y = send(relay.at[3], final.at[3], 43, near_y)
        bulk_line.fourth()
        direct_x.wait_recv()
        onward_y.wait_recv()
        relay[4] = add(payload[theirs], final[0], final[3]).astype(BF16)
        to_core = send(relay.at[4], core_got, 44, partner)
        direct_y.wait_recv()
        onward_x.wait_recv()
        kept = add(payload[mine], final[1], final[2])
        quarter = gain_row // 2
        for i in range(2):
            chunks[2 * core + i] = kept[i * quarter : (i + 1) * quarter].astype(BF16)
        to_core.wait_recv()
        for i in range(2):
            chunks[2 * (1 - core) + i] = core_got[i * quarter : (i + 1) * quarter]
        gain_parts[0] = (kept[gain_row:] + core_got[gain_row:].astype(F32)).astype(BF16)
        mix_line.start()
        gain_lanes = pl.ds(0, 128)
        gain_sends = [
            send(gain_parts.at[0, :, gain_lanes], gain_got.at[i, :, gain_lanes], 45 + i, along[i]) for i in range(3)
        ]
        bulk_line.fifth()
        mix_line.first()
        mix_line.second()
        mix_line.third()
        for copy in gain_sends:
            copy.wait_recv()
        gains_ref[...] = add(
            gain_parts[0, :, :128], gain_got[0, :, :128], gain_got[1, :, :128], gain_got[2, :, :128]
        )
        mix_line.fourth()
        bulk_line.sixth()

        def place(index, values):
            side, up = index // 2, index % 2
            lanes_of = lambda p: slice((2 * p + side) * width, (2 * p + side + 1) * width)
            below = shard - quarter
            for p in range(3):
                part_of = values[:, p * width : (p + 1) * width]
                if up == 0:
                    total_ref[0:quarter, lanes_of(p)] = part_of
                else:
                    total_ref[quarter:shard, lanes_of(p)] = part_of[:below]
                    rows = slice(p * (shard // 3), (p + 1) * (shard // 3))
                    outw_ref[rows, side * width : (side + 1) * width] = part_of[below:]

        flat = jnp.concatenate([whole_line[i] for i in range(4)], axis=0)
        tile = down_ref.shape[0]
        down_ref[...] = flat[:tile]
        ups = [flat[tile + 2 * shard * i : tile + 2 * shard * (i + 1)] for i in range(2)]
        for i in range(2):
            up_out[i] = jnp.where(core == 0, ups[i][shard:], ups[i][:shard])
        up_send = send(up_out, up_got, 48, partner)

        def place_up(side, i, values):
            for j in range(2):
                lanes = pl.ds(pl.multiple_of((2 * (2 * i + j) + side) * tile, 128), tile)
                up_ref[:, lanes] = values[:, j * tile : (j + 1) * tile]

        for i in range(2):
            place_up(core, i, jnp.where(core == 0, ups[i][:shard], ups[i][shard:]))
        up_send.wait_recv()
        for i in range(2):
            place_up(other, i, up_got[i])
        mix_line.fifth()
        mix_line.sixth()
        for i in range(4):
            place(i, chunk_whole[i])
        bulk_line.wait_sends()
        mix_line.wait_sends()
        grad_moves.wait()
    for copy in waits:
        copy.wait_send()


def backward_pass(square, pics, row, shared, weights, gains, bounds, *more):
    length, model = row[1].shape
    width = model // 2
    part = length // 4
    half, tokens = 2 * part, 3 * part
    shard = model // 8
    near = pl.BlockSpec(memory_space=pltpu.VMEM)
    anywhere = pl.BlockSpec(memory_space=pl.ANY)
    low = lambda *shape: (shape, BF16)
    wide = lambda *shape: (shape, F32)
    if square:
        rows = more[0].shape[1]
        tile = rows // 2
        outs = [
            (low(3, part, model), anywhere),
            (low(shard, 6 * width), near),
            (wide(16, 128), near),
            (low(shard, 8 * tile), near),
            (low(tile, model), near),
            (low(shard, model), near),
        ]
    else:
        outs = [(low(tokens, model), near), (low(model, 3 * width), near), (wide(16, model), near)]
    scratch = []
    for queries in (length, half):
        scratch += [
            low(2 * (width // 128), queries, 128), low(length, width), low(length, width), low(queries, width),
            low(queries, width), low(length, 2 * width),
        ]
    scratch += [
        low(length + half, model), low(model, 3 * width), low(tokens, model), wide(tokens, model),
        low(2, length, 128), low(2, length, 128), low(2, length, 128), wide(2, length, 128), wide(length, 128),
        low(length + half, 3 * width), low(length, width), low(length, width), low(half, width), low(half, width),
        wide(8, width), low(tokens, model), low(tokens, model),
    ]
    if square:
        span = rows // 2
        pieces = shard + shard // 3 + 16
        chunk = (pieces - 16) // 2
        scratch += [
            low(tokens, model), low(8, pieces, 3 * width), wide(16, model), low(model, width),
            low(4, span, model), low(2, span, model), low(2, span, model), low(2, span, model), low(2, span, model),
            low(4, rows // 4, model), low(4, rows // 4, model), low(3, rows // 4, model), low(3, rows // 4, model),
            low(2, shard, model), low(2, shard, model),
            low(5, pieces, 3 * width), low(4, pieces, 3 * width), low(pieces, 3 * width), low(4, chunk, 3 * width),
            low(4, chunk, 3 * width), low(3, chunk, 3 * width), low(3, chunk, 3 * width), low(1, 16, 3 * width),
            low(3, 16, 3 * width),
        ]
    return pl.pallas_call(
        functools.partial(backward_kernel, square, pics),
        in_specs=[anywhere] * 17 + [near] * 4 + [anywhere] * len(more),
        out_specs=[spec for _, spec in outs],
        out_shape=[jax.ShapeDtypeStruct(*shape) for shape, _ in outs],
        scratch_shapes=[pltpu.VMEM(*shape) for shape in scratch]
        + [
            pltpu.SemaphoreType.DMA((49,)),
            pltpu.SemaphoreType.DMA((49,)),
            pltpu.SemaphoreType.DMA((30,)),
            pltpu.SemaphoreType.DMA((2,)),
        ],
        compiler_params=pltpu.CompilerParams(
            collective_id=2, has_side_effects=True, vmem_limit_bytes=62 * 1024 * 1024
        ),
        name="backward_pass",
    )(*row, *shared, *weights, *gains, bounds, *more)


def local(
    tokens, lengths, pictures, first_gain, mix_weight, query_gain, key_gain, out_weight,
    second_gain, up_weight, down_weight, cotangent,
):
    chip, core, zp, zq = here()
    chips = lax.axis_size("chip")
    square = chips == 4
    rows = ("chip", "core")
    _, part, model = tokens.shape
    length = 4 * part
    half = 2 * part
    width = HEADS // 2 * HEAD
    pics = lengths.shape[1]
    shard = mix_weight.shape[0]

    hidden = up_weight.shape[1]
    tile = hidden // 8
    gains = [gain[None] for gain in (first_gain, query_gain, key_gain, second_gain)]
    if square:
        forward = forward_pass(
            True, pics, tokens, cotangent, lengths, mix_weight, *gains, up_weight, out_weight
        )
        up_half, out_matrix = forward[19:]
        down_half = down_weight
        gain_second = forward[5]
    else:
        gather = lambda weight: lax.all_gather(weight, rows, axis=0, tiled=True)
        half_of = lambda weight, axis: pick(weight, core, axis)
        mix_half = half_of(gather(mix_weight).reshape(model, 3, 2, width), 2).reshape(model, 3 * width)
        up_half = half_of(gather(up_weight).reshape(model, 4, 2, tile), 2).reshape(model, 4 * tile)
        down_half = half_of(gather(down_weight).reshape(4, 2, tile, model), 1).reshape(4 * tile, model)
        out_matrix = gather(out_weight)
        gains = lax.all_gather(jnp.concatenate(gains), rows, axis=0, tiled=False)
        gains = gains.transpose(1, 0, 2).reshape(4, 1, model).astype(F32)
        gain_second = gains[3]
        gain_qk = half_of(gains[1:3].reshape(2, 2, width), 1).reshape(1, model)
        forward = forward_pass(False, pics, tokens, cotangent, lengths, mix_half, gains[0], gain_qk)
    own_tokens, bounds, mix_half, grad_tokens, gain_first, _, gain_qk = forward[:7]
    normed, qk, v, raw, out, aug = forward[7:13]
    shared_normed, shared_qk, shared_v, shared_raw, shared_out, shared_aug = forward[13:19]

    def collect(mine, cross, third):
        mine = lax.ppermute(mine, COLUMN, KEEP)
        cross = lax.ppermute(cross, COLUMN, CROSS)
        third = lax.ppermute(third, COLUMN, KEEP)
        return jnp.stack([jnp.where(zq == 0, mine, cross), jnp.where(zq == 0, cross, mine), third])

    output, middle_grad, grad, shared_grad, out_grad, second_gain_grad, packed, far = dense(
        square, out, shared_out, own_tokens, grad_tokens, cotangent, out_matrix, gain_second, bounds,
        up_half, down_half,
    )
    row_side = (aug, qk, v, out, grad, raw, normed)
    shared_side = (shared_aug, shared_qk, shared_v, shared_out, shared_grad, shared_raw, shared_normed)
    weights = (mix_half, own_tokens, middle_grad)
    gains = (gain_first, gain_qk, second_gain_grad)
    if square:
        input_out, mix_out, gains_out, up_out, down_out, outw_out = backward_pass(
            True, pics, row_side, shared_side, weights, gains, bounds, packed, far, out_grad
        )
        gains_out = gains_out[:4, :shard]
        mix_out, up_out, down_out, outw_out = (
            array.astype(F32) for array in (mix_out, up_out, down_out, outw_out)
        )
    else:
        input_grad, mix_grad, gain_grads = backward_pass(
            False, pics, row_side, shared_side, weights, gains, bounds
        )

        def reduce(grad):
            return lax.psum(lax.psum_scatter(grad, rows, scatter_dimension=0, tiled=True), SEQ).astype(F32)

        first, second = input_grad[:part], input_grad[part:half]
        input_out = collect(
            jnp.where(zq == 0, first, second), jnp.where(zq == 0, second, first), input_grad[half:]
        )
        own_core = jnp.arange(2) == core
        eighth = model // 8
        down_grad = packed[:, None, :tile]
        down_out = reduce(jnp.where(own_core[None, :, None, None], down_grad, 0).reshape(hidden, model))
        up_grad = packed[:, tile : 2 * tile].reshape(4, 2, 2 * eighth, 2, tile).transpose(0, 2, 1, 3, 4)
        up_grad = up_grad.reshape(model, 4, 1, tile)
        up_out = reduce(jnp.where(own_core[None, None, :, None], up_grad, 0).reshape(model, hidden))
        out_grad = out_grad.reshape(model, 1, width)
        outw_out = reduce(jnp.where(own_core[None, :, None], out_grad, 0).reshape(model, model))
        mix_out = reduce(
            jnp.where(own_core[None, None, :, None], mix_grad.reshape(model, 3, 1, width), 0).reshape(model, 6 * width)
        )
        gain_grads = gain_grads[:4].reshape(4, 2 * chips, shard).transpose(1, 0, 2).astype(BF16)
        gains_out = reduce(gain_grads).reshape(4, shard)
    return (
        output, input_out, gains_out[0], mix_out, gains_out[1], gains_out[2], outw_out, gains_out[3],
        up_out, down_out,
    )


def solution(mesh):
    fsdp = mesh.shape["fsdp"]
    split = Mesh(mesh.devices.reshape(fsdp // 2, 2, 2, 2), ("chip", "core", "zp", "zq"))
    rows = ("chip", "core")
    return jax.shard_map(
        local,
        mesh=split,
        in_specs=(
            P(rows, SEQ, None),
            P(rows, None),
            P(rows, SEQ),
            P(rows),
            P(rows, None),
            P(rows),
            P(rows),
            P(rows, None),
            P(rows),
            P(rows, None),
            P(rows, None),
            P(rows, SEQ, None),
        ),
        out_specs=(
            P(rows, SEQ, None),
            P(rows, SEQ, None),
            P(rows),
            P(rows, None),
            P(rows),
            P(rows),
            P(rows, None),
            P(rows),
            P(rows, None),
            P(rows, None),
        ),
        check_vma=False,
    )
```

```python
import functools

import jax
import jax.numpy as jnp
from jax import lax
from jax.experimental import pallas as pl
from jax.experimental.pallas import tpu as pltpu
from jax.sharding import Mesh, PartitionSpec as P

HEADS = 12
HEAD = 64
EPSILON = 1e-06
BLOCK = 256
STEP = 512
MARK = 32.0
EXP2_FACTOR = HEAD**-0.5 * 1.4426950408889634
F32 = jnp.float32
BF16 = jnp.bfloat16
VMEM_LIMIT = 56 * 1024 * 1024

SEQ = ("zp", "zq")
COLUMN = ("core", "zp", "zq")
KEEP = [
    (core * 4 + z, (z // 2) * 4 + 2 * core + z % 2) for core in range(2) for z in range(4)
]
CROSS = [
    (core * 4 + z, (z // 2) * 4 + 2 * core + 1 - z % 2) for core in range(2) for z in range(4)
]


def swap(array, name, bit=1):
    count = lax.axis_size(name)
    return lax.ppermute(array, name, [(i, i ^ bit) for i in range(count)])


def pick(array, index, axis=0):
    return lax.dynamic_index_in_dim(array, index, axis, keepdims=False)


def group_ones(scale, size=128):
    row = lax.broadcasted_iota(jnp.int32, (size, size), 0) // HEAD
    column = lax.broadcasted_iota(jnp.int32, (size, size), 1) // HEAD
    return jnp.where(row == column, scale, 0.0).astype(BF16)


def group_sum(values, ones):
    return jnp.dot(values.astype(BF16), ones, preferred_element_type=F32)


def group_sum_fine(values, ones):
    high = values.astype(BF16)
    return group_sum(high, ones) + group_sum(values - high.astype(F32), ones)


def project_kernel(x_ref, gain_ref, weight_ref, qkg_ref, normed_ref, qk_ref, v_ref, raw_ref):
    both = qk_ref.shape[1]
    x = x_ref[...].astype(F32)
    center = x - jnp.mean(x, axis=-1, keepdims=True)
    spread = jnp.mean(center * center, axis=-1, keepdims=True)
    normed = (center * lax.rsqrt(spread + EPSILON) * gain_ref[...]).astype(BF16)
    normed_ref[...] = normed
    ones = group_ones(1.0 / HEAD, 256)
    for at in range(0, both, 256):
        lanes = slice(at, at + 256)
        raw = jnp.dot(normed, weight_ref[:, lanes], preferred_element_type=F32)
        raw_ref[:, lanes] = raw.astype(BF16)
        c = raw - group_sum(raw, ones)
        n = c * lax.rsqrt(group_sum(c * c, ones) + EPSILON)
        qk_ref[:, lanes] = (n * qkg_ref[:, lanes]).astype(BF16)
    v_ref[...] = jnp.dot(normed, weight_ref[:, both:], preferred_element_type=F32).astype(BF16)


def nt(a, b):
    return lax.dot_general(a, b, (((1,), (1,)), ((), ())), preferred_element_type=F32)


def tn(a, b):
    return lax.dot_general(a, b, (((0,), (0,)), ((), ())), preferred_element_type=F32)


def slots(queries, length, part):
    at = lax.broadcasted_iota(jnp.int32, (queries, 128), 0)
    if queries == length:
        return at
    return at % part + part * (lax.axis_index("zq") + 2 * (at // part))


def own_rows(ref, start, count, queries, part):
    if queries == ref.shape[0]:
        return ref[pl.ds(start, count), :]
    zq = lax.axis_index("zq")
    pieces = [
        ref[pl.ds(pl.multiple_of((zq + 2 * i) * part, part), part), :]
        for i in range(start // part, (start + count) // part)
    ]
    return jnp.concatenate(pieces, axis=0)


def query_marks(bounds_ref, place, queries, length, part, pics):
    at = slots(queries, length, part)
    inside = (at >= bounds_ref[0:1, :]) & (at < bounds_ref[2:3, :])
    values = jnp.where(inside, MARK, 0.0)
    return jnp.where(place == pics, MARK, values).astype(BF16)


def key_marks(bounds_ref, place, length, pics):
    at = lax.broadcasted_iota(jnp.int32, (length, 128), 0)
    inside = (at >= bounds_ref[0:1, :]) & (at < bounds_ref[1:2, :])
    values = jnp.where(inside, MARK, 0.0)
    values = jnp.where(place == pics, -MARK, values)
    return jnp.where((place > pics) & (place < pics + 4), 1.0, values).astype(BF16)


def attend_kernel(pics, q_ref, k_ref, v_ref, bounds_ref, out_ref, aug_ref, kaug, vaug, qaug):
    length = k_ref.shape[0]
    queries = out_ref.shape[0]
    part = length // 4
    lane = lax.broadcasted_iota(jnp.int32, (1, 128), 1)
    place = lane % HEAD
    sides = [lane < HEAD, lane >= HEAD]
    kmarks = key_marks(bounds_ref, place, length, pics)
    qmarks = query_marks(bounds_ref, place, queries, length, part, pics)
    qaug[...] = qmarks
    for h in range(2):
        kaug[h] = jnp.where(sides[h], k_ref[...], kmarks)
        vaug[h] = jnp.where(sides[h], v_ref[...], jnp.ones_like(v_ref))
    for b in range(queries // STEP):
        rows = pl.ds(b * STEP, STEP)
        mine = own_rows(q_ref, b * STEP, STEP, queries, part)
        query = [jnp.where(sides[h], mine, qaug[rows, :]) for h in range(2)]
        total = [jnp.zeros((STEP, 128), F32)] * 2
        for j in range(length // STEP):
            keys = pl.ds(j * STEP, STEP)
            scores = [nt(query[h], kaug[h, keys, :]) for h in range(2)]
            weights = [jnp.exp2(x * EXP2_FACTOR).astype(BF16) for x in scores]
            total = [
                total[h] + jnp.dot(weights[h], vaug[h, keys, :], preferred_element_type=F32) for h in range(2)
            ]
        results = []
        for h in range(2):
            results.append(total[h] / pltpu.roll(total[h], HEAD, 1))
            log_total = jnp.log(jnp.where(sides[h], 1.0, total[h])) * -(HEAD**0.5)
            first = log_total.astype(BF16)
            rest = log_total - first.astype(F32)
            middle = rest.astype(BF16)
            last = (rest - middle.astype(F32)).astype(BF16)
            logs = jnp.where(place == pics + 1, first, jnp.where(place == pics + 2, middle, last))
            slot = jnp.logical_not(sides[h]) & (place > pics) & (place < pics + 4)
            aug_ref[h, rows, :] = jnp.where(slot, logs, query[h])
        out_ref[rows, :] = jnp.where(sides[0], results[0], results[1]).astype(BF16)


def head_norm_back(e, raw, gain, means):
    raw = raw.astype(F32)
    c = raw - group_sum(raw, means)
    r = lax.rsqrt(group_sum(c * c, means) + EPSILON)
    n = c * r
    t = e * gain
    grad = r * (t - group_sum(t, means) - n * group_sum(t * n, means))
    return grad.astype(BF16), jnp.sum(e * n, axis=0, keepdims=True)


def attend_back_kernel(
    pics, aug_ref, k_ref, v_ref, out_ref, do_ref, rawq_ref, rawk_ref, qg_ref, kg_ref, bounds_ref,
    dq_ref, dk_ref, dv_ref, qgg_ref, kgg_ref, kaug, vaug, doaug, qsum, ksum,
):
    length = k_ref.shape[0]
    queries = do_ref.shape[0]
    part = length // 4
    whole = queries == length
    lane = lax.broadcasted_iota(jnp.int32, (1, 128), 1)
    place = lane % HEAD
    sides = [lane < HEAD, lane >= HEAD]
    kmarks = key_marks(bounds_ref, place, length, pics)
    vmarks = jnp.where(place < 2, 1.0, 0.0).astype(BF16)
    ones = group_ones(1.0)
    inner = group_sum_fine(do_ref[...].astype(F32) * out_ref[...].astype(F32), ones)
    inner = -pltpu.roll(inner, HEAD, 1)
    inner_high = inner.astype(BF16)
    inner_low = (inner - inner_high.astype(F32)).astype(BF16)
    zero = jnp.zeros((), BF16)
    gmarks = jnp.where(place == 0, inner_high, jnp.where(place == 1, inner_low, zero))
    for h in range(2):
        kaug[h] = jnp.where(sides[h], k_ref[...], kmarks)
        vaug[h] = jnp.where(sides[h], v_ref[...], vmarks)
        doaug[h] = jnp.where(sides[h], do_ref[...], gmarks)
    for b in range(length // STEP):
        keys = pl.ds(b * STEP, STEP)
        key = [kaug[h, keys, :] for h in range(2)]
        value = [vaug[h, keys, :] for h in range(2)]
        dk = [jnp.zeros((STEP, 128), F32)] * 2
        dv = [jnp.zeros((STEP, 128), F32)] * 2
        for j in range(queries // STEP):
            rows = pl.ds(j * STEP, STEP)
            query = [aug_ref[h, rows, :] for h in range(2)]
            grad = [doaug[h, rows, :] for h in range(2)]
            scores = [nt(key[h], query[h]) for h in range(2)]
            soft_grad = [nt(value[h], grad[h]) for h in range(2)]
            weights = [jnp.exp2(x * EXP2_FACTOR) for x in scores]
            score_grad = [(weights[h] * soft_grad[h]).astype(BF16) for h in range(2)]
            for h in range(2):
                part_sum = tn(score_grad[h], key[h])
                if b == 0:
                    qsum[h, rows, :] = part_sum
                else:
                    qsum[h, rows, :] += part_sum
                dk[h] = dk[h] + jnp.dot(score_grad[h], query[h], preferred_element_type=F32)
                dv[h] = dv[h] + jnp.dot(weights[h].astype(BF16), grad[h], preferred_element_type=F32)
        ksum[keys, :] = jnp.where(sides[0], dk[0], dk[1]) * HEAD**-0.5
        dv_ref[keys, :] = jnp.where(sides[0], dv[0], dv[1]).astype(BF16)

    means = group_ones(1.0 / HEAD)
    gain_sum = jnp.zeros((1, 128), F32)
    for b in range(queries // part):
        rows = pl.ds(b * part, part)
        e = jnp.where(sides[0], qsum[0, rows, :], qsum[1, rows, :]) * HEAD**-0.5
        raw = own_rows(rawq_ref, b * part, part, queries, part)
        dq_ref[rows, :], more = head_norm_back(e.astype(BF16).astype(F32), raw, qg_ref[...], means)
        gain_sum = gain_sum + more
    qgg_ref[...] = gain_sum
    gain_sum = jnp.zeros((1, 128), F32)
    for b in range(length // part):
        rows = pl.ds(b * part, part)
        e = ksum[rows, :].astype(BF16)
        if whole:
            dk_ref[rows, :], more = head_norm_back(e.astype(F32), rawk_ref[rows, :], kg_ref[...], means)
            gain_sum = gain_sum + more
        else:
            dk_ref[rows, :] = e
    kgg_ref[...] = gain_sum


def shared_keys_kernel(dk_ref, dv_ref, gotk_ref, gotv_ref, rawk_ref, kg_ref, outk_ref, outv_ref, kgg_ref):
    count = outk_ref.shape[0]
    part = count // 2
    means = group_ones(1.0 / HEAD)
    gain_sum = jnp.zeros((1, 128), F32)
    for b in range(2):
        rows = pl.ds(b * part, part)
        own = lambda ref: own_rows(ref, b * part, part, count, part)
        e = own(dk_ref).astype(F32) + gotk_ref[rows, :].astype(F32)
        outk_ref[rows, :], more = head_norm_back(e, own(rawk_ref), kg_ref[...], means)
        gain_sum = gain_sum + more
        outv_ref[rows, :] = (own(dv_ref).astype(F32) + gotv_ref[rows, :].astype(F32)).astype(BF16)
    kgg_ref[...] = gain_sum


def gelu_pair(h):
    size = jnp.abs(h)
    bell = jnp.exp2(h * h * -0.7213475204444817)
    t = 1.0 / (1.0 + 0.23164189 * size)
    series = t * (0.127414796 + t * (-0.142248368 + t * (0.7107068705 + t * (-0.7265760135 + t * 0.5307027145))))
    tail = series * bell
    below = jnp.where(h < 0.0, tail, 1.0 - tail)
    return h * below, below + h * (bell * 0.3989422804014327)


def norm_parts(values):
    center = values - jnp.mean(values, axis=-1, keepdims=True)
    spread = lax.rsqrt(jnp.mean(center * center, axis=-1, keepdims=True) + EPSILON)
    return center * spread, spread


def norm_back(upstream, n, r, gain):
    t = upstream * gain
    grad = r * (t - jnp.mean(t, axis=-1, keepdims=True) - n * jnp.mean(t * n, axis=-1, keepdims=True))
    return grad, jnp.sum(upstream * n, axis=0, keepdims=True)


MESH_ID = pl.DeviceIdType.MESH


def here():
    return lax.axis_index("chip"), lax.axis_index("core"), lax.axis_index("zp"), lax.axis_index("zq")


def remote(source, target, sems, at, device):
    sent, got = sems
    return pltpu.make_async_remote_copy(
        src_ref=source, dst_ref=target, send_sem=sent.at[at], recv_sem=got.at[at],
        device_id=device, device_id_type=MESH_ID,
    )


def greet(devices, maybe=None, moves=None):
    barrier = pltpu.get_barrier_semaphore()
    for device in devices:
        pl.semaphore_signal(barrier, inc=1, device_id=device, device_id_type=MESH_ID)
    if maybe is None:
        pl.semaphore_wait(barrier, len(devices))
        return

    @pl.when(moves)
    def _():
        pl.semaphore_signal(barrier, inc=1, device_id=maybe, device_id_type=MESH_ID)

    pl.semaphore_wait(barrier, len(devices) + jnp.where(moves, 1, 0))


def rows_at(start, count):
    return pl.ds(pl.multiple_of(start, 16), count)


class Moves:
    def __init__(self, moved, stays, crossed, moves):
        self.moved, self.stays, self.crossed, self.moves = moved, stays, crossed, moves

    def each(self, act):
        if self.crossed is not None:
            act(self.crossed)

        @pl.when(self.moves)
        def _():
            for copy in self.moved:
                act(copy)

        @pl.when(jnp.logical_not(self.moves))
        def _():
            for copy in self.stays:
                act(copy)

    def start(self):
        self.each(lambda copy: copy.start())

    def wait(self):
        self.each(lambda copy: copy.wait())


class PlaneSum:
    def __init__(self, payload, relay, final, came, sems, at, waits):
        self.chip, self.core, zp, zq = here()
        self.payload, self.relay, self.final, self.came = payload, relay, final, came
        self.sems, self.at, self.waits = sems, at, waits
        self.near_x = (self.chip ^ 1, self.core, zp, zq)
        self.near_y = (self.chip ^ 2, self.core, zp, zq)
        self.partner = (self.chip, 1 - self.core, zp, zq)

    def send(self, source, target, at, device):
        copy = remote(source, target, self.sems, self.at + at, device)
        copy.start()
        self.waits.append(copy)
        return copy

    def same(self, hop):
        return 2 * (self.chip ^ hop) + self.core

    def twin(self, hop):
        return 2 * (self.chip ^ hop) + 1 - self.core

    def start(self):
        payload = self.payload
        self.first = self.send(payload.at[self.same(3)], self.relay.at[0], 0, self.near_y)
        self.second = self.send(payload.at[self.twin(3)], self.relay.at[1], 1, self.near_x)
        self.direct_x = self.send(payload.at[self.twin(1)], self.final.at[0], 2, self.near_x)
        self.direct_y = self.send(payload.at[self.same(2)], self.final.at[1], 3, self.near_y)

    def pass_on(self):
        self.first.wait_recv()
        self.relay[2] = add(self.relay[0], self.payload[self.same(1)]).astype(BF16)
        self.onward_x = self.send(self.relay.at[2], self.final.at[2], 4, self.near_x)
        self.second.wait_recv()
        self.relay[3] = add(self.relay[1], self.payload[self.twin(2)]).astype(BF16)
        self.onward_y = self.send(self.relay.at[3], self.final.at[3], 5, self.near_y)

    def to_core(self):
        self.direct_x.wait_recv()
        self.onward_y.wait_recv()
        self.relay[4] = add(self.payload[self.twin(0)], self.final[0], self.final[3]).astype(BF16)
        self.crossing = self.send(self.relay.at[4], self.came, 6, self.partner)

    def finish(self):
        self.direct_y.wait_recv()
        self.onward_x.wait_recv()
        kept = add(self.payload[self.same(0)], self.final[1], self.final[2])
        self.crossing.wait_recv()
        return kept


class Line:
    def __init__(self, parts, whole, right, left, sems, at):
        chip, core, zp, zq = here()
        self.z = 2 * zp + zq
        up, down = jnp.minimum(self.z + 1, 3), jnp.maximum(self.z - 1, 0)
        self.next = (chip, core, up // 2, up % 2)
        self.last = (chip, core, down // 2, down % 2)
        self.parts, self.whole, self.right, self.left = parts, whole, right, left
        self.sems, self.at, self.sends = sems, at, []

    def at_chip(self, z, *acts):
        @pl.when(self.z == z)
        def _():
            for act in acts:
                act()

    def part_copy(self, c, rightward):
        if rightward:
            return remote(self.parts.at[c], self.right.at[3 - c], self.sems, self.at + 3 - c, self.next)
        return remote(self.parts.at[c], self.left.at[c], self.sems, self.at + 3 + c, self.last)

    def whole_copy(self, c, rightward):
        if rightward:
            return remote(self.whole.at[c], self.whole.at[c], self.sems, self.at + 6 + c, self.next)
        return remote(self.whole.at[c], self.whole.at[c], self.sems, self.at + 8 + c, self.last)

    def send(self, z, make, c, rightward):
        self.sends.append((z, make, c, rightward))
        return lambda: make(c, rightward).start()

    def take(self, c, rightward):
        def act():
            self.part_copy(c, rightward).wait_recv()
            came = self.right[3 - c] if rightward else self.left[c]
            self.parts[c] = add(self.parts[c], came).astype(BF16)

        return act

    def got(self, c, rightward):
        return lambda: self.whole_copy(c, rightward).wait_recv()

    def start(self):
        part = self.part_copy
        self.at_chip(0, *[self.send(0, part, c, True) for c in (3, 2, 1)])
        self.at_chip(3, *[self.send(3, part, c, False) for c in (0, 1, 2)])

    def first(self):
        self.at_chip(1, self.take(3, True), self.send(1, self.part_copy, 3, True))
        self.at_chip(2, self.take(0, False), self.send(2, self.part_copy, 0, False))

    def second(self):
        part = self.part_copy
        self.at_chip(
            1, self.take(2, True), self.send(1, part, 2, True), self.take(0, False), self.send(1, part, 0, False)
        )
        self.at_chip(
            2, self.take(1, False), self.send(2, part, 1, False), self.take(3, True), self.send(2, part, 3, True)
        )

    def third(self):
        self.at_chip(0, self.take(0, False))
        self.at_chip(1, self.take(1, True), self.take(1, False))
        self.at_chip(2, self.take(2, True), self.take(2, False))
        self.at_chip(3, self.take(3, True))
        self.whole[self.z] = self.parts[self.z]
        for z in range(4):
            acts = [self.send(z, self.whole_copy, z, True)] if z < 3 else []
            acts += [self.send(z, self.whole_copy, z, False)] if z > 0 else []
            self.at_chip(z, *acts)

    def fourth(self):
        whole = self.whole_copy
        for z in (1, 2):
            self.at_chip(
                z, self.got(z - 1, True), self.send(z, whole, z - 1, True), self.got(z + 1, False),
                self.send(z, whole, z + 1, False),
            )

    def fifth(self):
        whole = self.whole_copy
        self.at_chip(1, self.got(3, False), self.send(1, whole, 3, False))
        self.at_chip(2, self.got(0, True), self.send(2, whole, 0, True))

    def sixth(self):
        self.at_chip(0, *[self.got(c, False) for c in (1, 2, 3)])
        self.at_chip(3, *[self.got(c, True) for c in (2, 1, 0)])

    def wait_sends(self):
        for z in range(4):
            mine = [make(c, rightward) for at, make, c, rightward in self.sends if at == z]
            self.at_chip(z, *[copy.wait_send for copy in mine])


def write_bounds(pics, lens_ref, bounds_ref, zp, zq, length):
    lane = lax.broadcasted_iota(jnp.int32, (8, 128), 1)
    lens = jnp.where(zp == 0, lens_ref[0], lens_ref[1])
    ends = lens
    for hop in (1, 2, 4, 8):
        ends = ends + jnp.where(lane >= hop, pltpu.roll(ends, hop, 1), 0)
    starts = ends - lens
    last = (lens > 0) & (pltpu.roll(lens, 127, 1) == 0)
    query_ends = jnp.where(last, length, ends)
    total = jnp.max(jnp.where(lane < pics, ends, 0), axis=1, keepdims=True)

    def both(values):
        values = jnp.where(lane < HEAD, jnp.where(lane < pics, values, 2 * length), 0)
        return values + pltpu.roll(values, HEAD, 1)

    tables = [both(starts), both(ends), both(query_ends), jnp.broadcast_to(total, (8, 128))]
    for t in range(4):
        table = tables[t]
        bounds_ref[0, t : t + 1, :] = jnp.where(zq == 0, table[0:1], table[1:2])
        bounds_ref[1, t : t + 1, :] = table[2:3]
    bounds_ref[:, 4:, :] = jnp.zeros((2, 4, 128), jnp.int32)


def forward_kernel(square, pics, *refs):
    refs = list(refs)
    take = lambda count: [refs.pop(0) for _ in range(count)]
    tokens_ref, cot_ref, lengths_ref, weight_in = take(4)
    if square:
        gain_in = take(4)
        up_in, outw_ref = take(2)
    else:
        gain_first_in, gain_qk_in = take(2)
    x_out, bounds_ref, mix_hbm, cot_hbm, gain_first, second_ref, gain_qk = take(7)
    names = ("normed", "qk", "v", "raw", "out", "aug")
    outs = [dict(zip(names, take(6))) for _ in range(2)]
    if square:
        up_hbm, outw_hbm = take(2)
    row_ref, shared_ref, cot_out, lens_ref, lens_out = take(5)
    scratch = [dict(zip(names, take(6))) for _ in range(2)]
    kaug, vaug, qaug = take(3)
    if square:
        mix_ref, gains_ref, up_ref, mix_out, gains_out, up_out, outw_out = take(7)
    sent, got, local_sem, write_sem = take(4)

    chip, core, zp, zq = here()
    z = 2 * zp + zq
    part = tokens_ref.shape[1]
    half, length = 2 * part, 4 * part
    sems = (sent, got)
    partner = (chip, 1 - core, zp, zq)
    side = (chip, core, zp, 1 - zq)
    keep = (chip, zp, core, zq)
    cross = (chip, zp, core, 1 - zq)
    moves = core != zp
    near_x = (chip ^ 1, core, zp, zq)
    near_y = (chip ^ 2, core, zp, zq)
    greet([partner, side, cross] + ([near_x, near_y] if square else []), keep, moves)

    def quarter(ref, index):
        return ref.at[rows_at(index * part, part)]

    own_row = remote(tokens_ref.at[zq], quarter(row_ref, z), sems, 0, keep)
    own_shared = remote(tokens_ref.at[2], quarter(shared_ref, z), sems, 2, keep)
    stay_row = pltpu.make_async_copy(tokens_ref.at[zq], quarter(row_ref, z), local_sem.at[0])
    stay_shared = pltpu.make_async_copy(tokens_ref.at[2], quarter(shared_ref, z), local_sem.at[1])

    @pl.when(moves)
    def _():
        own_row.start()

    @pl.when(jnp.logical_not(moves))
    def _():
        stay_row.start()

    cross_row = remote(tokens_ref.at[1 - zq], quarter(row_ref, z), sems, 1, cross)
    cross_row.start()

    @pl.when(moves)
    def _():
        own_shared.start()

    @pl.when(jnp.logical_not(moves))
    def _():
        stay_shared.start()

    lens_ref[...] = jnp.zeros_like(lens_ref)
    lens_ref[: lengths_ref.shape[0], :pics] = lengths_ref[...]
    lens_copy = remote(lens_ref, lens_out.at[core], sems, 8, partner)
    lens_copy.start()
    lens_stay = pltpu.make_async_copy(lens_ref, lens_out.at[core], local_sem.at[2])
    lens_stay.start()
    waits = []
    if square:
        shard = mix_ref.shape[1]
        tile = up_ref.shape[2] // 4
        width = mix_ref.shape[2] // 3
        for h in range(2):
            for i in range(3):
                mix_ref[h, :, i * width : (i + 1) * width] = weight_in[:, (2 * i + h) * width : (2 * i + h + 1) * width]
        gains_ref[...] = jnp.zeros_like(gains_ref)
        for i in range(4):
            gains_ref[i : i + 1, :shard] = gain_in[i][...].astype(F32)
        mine, theirs = 2 * chip + core, 2 * chip + 1 - core
        slot = [9]

        def send(source, target, device):
            copy = remote(source, target, sems, slot[0], device)
            slot[0] += 1
            copy.start()
            waits.append(copy)
            return copy

        def stay(source, target, at):
            copy = pltpu.make_async_copy(source, target, local_sem.at[at])
            copy.start()
            return copy

        def block(ref, start, count):
            return ref.at[rows_at(start, count)]

        mix_piece = lambda index: (block(mix_out, index * shard, shard), gains_out.at[index])

        def send_mix(sources, index, device):
            return [send(source, target, device) for source, target in zip(sources, mix_piece(index))]

        def arrived(copies):
            for copy in copies:
                copy.wait_recv()

        x_mine, y_other = 2 * (chip ^ 1) + core, 2 * (chip ^ 2) + 1 - core
        to_core = send_mix((mix_ref.at[1 - core], gains_ref), mine, partner)
        a_x = send_mix((mix_ref.at[core], gains_ref), mine, near_x)
        a_y = send_mix((mix_ref.at[core], gains_ref), mine, near_y)
        for h in range(2):
            for i in range(4):
                up_ref[h, :, i * tile : (i + 1) * tile] = up_in[:, (2 * i + h) * tile : (2 * i + h + 1) * tile]
        up_core = send(up_ref.at[1 - core], block(up_out, mine * shard, shard), partner)
        out_core = send(outw_ref, block(outw_out, mine * shard, shard), partner)
        stays = [
            stay(mix_ref.at[core], mix_piece(mine)[0], 3),
            stay(gains_ref, gains_out.at[mine], 4),
            stay(up_ref.at[core], block(up_out, mine * shard, shard), 5),
            stay(outw_ref, block(outw_out, mine * shard, shard), 6),
        ]
        arrived(to_core)
        b_x = send_mix(mix_piece(theirs), theirs, near_x)
        b_y = send_mix(mix_piece(theirs), theirs, near_y)
        arrived(a_x)
        a_far = send_mix(mix_piece(x_mine), x_mine, near_y)
        arrived(b_y)
        b_far = send_mix(mix_piece(y_other), y_other, near_x)
        for copy in stays:
            copy.wait()
        arrived([up_core])
        ohalf = shard // 2

        def bundle(first, from_chip):
            same, twin = 2 * from_chip + core, 2 * from_chip + 1 - core
            part_of = 0 if first else 1
            return [
                block(up_out, (same if first else twin) * shard, shard),
                block(outw_out, same * shard + part_of * ohalf, ohalf),
            ]

        def send_bundle(first, from_chip, device):
            return [send(ref, ref, device) for ref in bundle(first, from_chip)]

        first_x = send_bundle(True, chip, near_x)
        first_y = send_bundle(True, chip, near_y)
        second_x = send_bundle(False, chip, near_x)
        second_y = send_bundle(False, chip, near_y)

    lens_copy.wait()
    lens_stay.wait()
    write_bounds(pics, lens_out, bounds_ref, zp, zq, length)
    if square:
        arrived(a_y + b_x + a_far + b_far)
        for p in range(gains_out.shape[0]):
            lanes = slice(p * shard, (p + 1) * shard)
            values = gains_out[p, :, :shard]
            gain_first[:, lanes] = values[0:1]
            second_ref[:, lanes] = values[3:4]
            half_pieces = gains_out.shape[0] // 2

            @pl.when(core == p // half_pieces)
            def _():
                at = (p % half_pieces) * shard
                gain_qk[:, at : at + shard] = values[1:2]
                gain_qk[:, width + at : width + at + shard] = values[2:3]
        weight = mix_out
    else:
        weight = weight_in
        width = weight.shape[1] // 3
        second_ref[...] = jnp.zeros_like(second_ref)
        gain_first[...] = gain_first_in[...]
        gain_qk[...] = gain_qk_in[...]
    writes = []

    def write(source, target, at):
        copy = pltpu.make_async_copy(source, target, write_sem.at[at])
        copy.start()
        writes.append(copy)

    write(weight, mix_hbm, 0)
    first, second = 2 * core + zq, 2 * core + 1 - zq
    other_first, other_second = 2 * (1 - core) + zq, 2 * (1 - core) + 1 - zq

    def forwarded(ref, index, at):
        return remote(quarter(ref, index), quarter(ref, index), sems, at, partner)

    def project(tokens, bufs, at):
        rows = rows_at(at * part, part)
        project_kernel(
            tokens.at[rows], gain_first, weight, gain_qk, bufs["normed"].at[rows], bufs["qk"].at[rows],
            bufs["v"].at[rows], bufs["raw"].at[rows],
        )

    def project_row(i, _):
        @pl.when(i == 0)
        def _():
            @pl.when(moves)
            def _():
                own_row.wait_recv()

            @pl.when(jnp.logical_not(moves))
            def _():
                stay_row.wait()

            forwarded(row_ref, first, 3).start()

        @pl.when(i == 1)
        def _():
            cross_row.wait_recv()
            forwarded(row_ref, second, 4).start()

        @pl.when(i == 2)
        def _():
            forwarded(row_ref, other_first, 3).wait_recv()

        @pl.when(i == 3)
        def _():
            forwarded(row_ref, other_second, 4).wait_recv()

        order = jnp.where(i == 0, first, jnp.where(i == 1, second, jnp.where(i == 2, other_first, other_second)))
        project(row_ref, scratch[0], order)
        return 0

    row_one, row_two = forwarded(row_ref, first, 3), forwarded(row_ref, second, 4)

    def attend(bufs, bounds):
        def one(p, _):
            lanes = pl.ds(pl.multiple_of(p * 128, 128), 128)
            attend_kernel(
                pics, bufs["qk"].at[:, lanes],
                bufs["qk"].at[:, pl.ds(pl.multiple_of(width + p * 128, 128), 128)], bufs["v"].at[:, lanes], bounds,
                bufs["out"].at[:, lanes], bufs["aug"].at[pl.ds(2 * p, 2)], kaug, vaug, qaug.at[pl.ds(0, bufs["out"].shape[0])],
            )
            return 0

        lax.fori_loop(0, width // 128, one, 0)

    lax.fori_loop(0, 4, project_row, 0)
    for i, name in enumerate(("normed", "qk", "v", "raw")):
        write(scratch[0][name], outs[0][name], 1 + i)
    write(row_ref.at[rows_at(core * half, half)], x_out.at[pl.ds(0, half)], 5)

    @pl.when(moves)
    def _():
        own_shared.wait_recv()

    @pl.when(jnp.logical_not(moves))
    def _():
        stay_shared.wait()

    to_side = remote(quarter(shared_ref, first), quarter(shared_ref, first), sems, 5, side)
    to_side.start()
    shared_one = remote(quarter(shared_ref, first), quarter(shared_ref, first), sems, 6, partner)
    shared_one.start()
    attend(scratch[0], bounds_ref.at[0])
    cot_moves = Moves(
        [remote(cot_ref.at[zq], cot_out, sems, 43, keep)],
        [pltpu.make_async_copy(cot_ref.at[zq], cot_out, local_sem.at[0])],
        None,
        moves,
    )
    cot_moves.start()
    write(scratch[0]["out"], outs[0]["out"], 6)
    write(scratch[0]["aug"], outs[0]["aug"], 7)
    to_side.wait_recv()
    shared_two = forwarded(shared_ref, second, 7)
    shared_two.start()
    if square:
        arrived(first_x + second_y)
        far_first = send_bundle(True, chip ^ 1, near_y)
        far_second = send_bundle(False, chip ^ 2, near_x)
    shared_one.wait_recv()
    shared_two.wait_recv()

    def project_shared(i, _):
        project(shared_ref, scratch[1], i)
        return 0

    lax.fori_loop(0, 4, project_shared, 0)
    for i, name in enumerate(("normed", "qk", "v", "raw")):
        write(scratch[1][name], outs[1][name], 8 + i)
    write(shared_ref.at[rows_at(first * part, part)], x_out.at[pl.ds(half, part)], 12)
    attend(scratch[1], bounds_ref.at[1])
    write(scratch[1]["out"], outs[1]["out"], 13)
    write(scratch[1]["aug"], outs[1]["aug"], 14)

    if square:
        arrived(first_y + second_x + far_first + far_second)
        sent_pieces = []
        for c in (chip ^ 1, chip ^ 2, chip ^ 3):
            target = block(outw_out, (2 * c + core) * shard, shard)
            sent_pieces.append(send(target, target, partner))
        write(up_out, up_hbm, 15)
        arrived(sent_pieces + [out_core])
        write(outw_out, outw_hbm, 17)
        for copy in waits:
            copy.wait_send()
    cot_moves.wait()
    write(cot_out, cot_hbm, 18)
    for copy in (row_one, row_two, shared_one, shared_two, to_side, cross_row):
        copy.wait_send()

    @pl.when(moves)
    def _():
        own_row.wait_send()
        own_shared.wait_send()

    for copy in writes:
        copy.wait()


def forward_pass(square, pics, tokens, cotangent, lengths, weight, *more):
    _, part, model = tokens.shape
    length, half, width = 4 * part, 2 * part, model // 2
    near = pl.BlockSpec(memory_space=pltpu.VMEM)
    anywhere = pl.BlockSpec(memory_space=pl.ANY)
    low = lambda *shape: (shape, BF16)
    wide = lambda *shape: (shape, F32)
    outs = [
        (low(3 * part, model), anywhere),
        (((2, 8, 128), jnp.int32), near),
        (low(model, 3 * width), anywhere),
        (low(part, model), anywhere),
        (wide(1, model), near),
        (wide(1, model), near),
        (wide(1, model), near),
    ]
    bufs = []
    for queries in (length, half):
        shapes = [
            low(length, model), low(length, 2 * width), low(length, width), low(length, 2 * width),
            low(queries, width), low(2 * (width // 128), queries, 128),
        ]
        outs += [(shape, anywhere) for shape in shapes]
        bufs += shapes
    table = ((8, 128), jnp.int32)
    scratch = [low(length, model), low(length, model), low(part, model), table, ((2, 8, 128), jnp.int32)] + bufs
    scratch += [low(2, length, 128), low(2, length, 128), low(length, 128)]
    if square:
        up, _ = more[4:]
        shard, hidden = up.shape
        landed = [low(model, hidden // 2), low(model, model)]
        outs += [(shape, anywhere) for shape in landed]
        scratch += [low(2, shard, 3 * width), wide(8, 128), low(2, shard, hidden // 2)]
        scratch += [low(model, 3 * width), wide(8, 8, 128)] + landed
    return pl.pallas_call(
        functools.partial(forward_kernel, square, pics),
        in_specs=[near] * (4 + len(more)),
        out_specs=[spec for _, spec in outs],
        out_shape=[jax.ShapeDtypeStruct(*shape) for shape, _ in outs],
        scratch_shapes=[pltpu.VMEM(*shape) for shape in scratch]
        + [
            pltpu.SemaphoreType.DMA((49,)),
            pltpu.SemaphoreType.DMA((49,)),
            pltpu.SemaphoreType.DMA((8,)),
            pltpu.SemaphoreType.DMA((19,)),
        ],
        compiler_params=pltpu.CompilerParams(
            collective_id=0, has_side_effects=True, vmem_limit_bytes=60 * 1024 * 1024
        ),
        name="forward_pass",
    )(tokens, cotangent, lengths, weight, *more)


def dense_kernel(
    square, out_ref, shared_ref, x, grad_ref, cot_ref, outw_ref, gain_ref, bounds_ref, up_ref, down_ref,
    output_ref, third_ref, midg_ref, row_grad, shared_grad, outg_ref, gaing_ref, packed_ref, far_ref,
    att_other, second, turned, grad, cot_in, hidden_all, pre_all, forward, backward, middle, up, down,
    results, parts_out, parts_in, heads_out, cols_out, cols_in, stage, far_in,
    sent, got, load_sem, write_sem, local_sem,
):
    chip, core, zp, zq = here()
    sems = (sent, got)
    partner = (chip, 1 - core, zp, zq)
    keep = (chip, zp, core, zq)
    cross = (chip, zp, core, 1 - zq)
    moves = core != zp
    near_x = (chip ^ 1, core, zp, zq)
    near_y = (chip ^ 2, core, zp, zq)
    tokens, model = midg_ref.shape
    part = tokens // 3
    half = 2 * part
    width = out_ref.shape[1]
    units = up.shape[1]
    tile = units // 4
    other = 1 - core
    mine, theirs = pl.ds(0, tokens), pl.ds(tokens, tokens)
    own_down = down.at[rows_at(chip * tile, tile)] if square else down
    loads = [
        pltpu.make_async_copy(up_ref, up, load_sem.at[0]),
        pltpu.make_async_copy(down_ref, own_down, load_sem.at[1]),
    ]
    for copy in loads:
        copy.start()
    greet([partner, cross] + ([near_x, near_y] if square else []), keep, moves)
    att_sends = [
        remote(out_ref.at[rows_at(other * half, half)], att_other.at[pl.ds(0, half)], sems, 0, partner),
        remote(shared_ref.at[rows_at(other * part, part)], att_other.at[pl.ds(half, part)], sems, 1, partner),
    ]
    for copy in att_sends:
        copy.start()
    cot_move = Moves(
        [remote(cot_ref.at[2], cot_in.at[1], sems, 11, keep)],
        [pltpu.make_async_copy(cot_ref.at[2], cot_in.at[1], local_sem.at[0])],
        remote(cot_ref.at[1 - zq], cot_in.at[0], sems, 22, cross),
        moves,
    )
    cot_move.start()

    def down_half(index, which):
        return down.at[rows_at(index * tile + which * (tile // 2), tile // 2)]

    def send_down(index, which, at, device):
        copy = remote(down_half(index, which), down_half(index, which), sems, at, device)
        copy.start()
        return copy

    slot = lax.broadcasted_iota(jnp.int32, (part, 1), 0)
    filled, shared_filled = bounds_ref[0, 3:4, 0:1], bounds_ref[1, 3:4, 0:1]
    none = jnp.zeros((), BF16)

    def take_grad(values, at, start, limit, sem):
        rows = rows_at(at, part)
        grad[rows, :] = jnp.where(slot + start < limit, values, none)
        copy = remote(grad.at[rows], grad.at[rows_at(tokens + at, part)], sems, sem, partner)
        copy.start()
        return copy

    grad_sends = [take_grad(grad_ref[...], zq * part, (2 * core + zq) * part, filled, 2)]

    own_rows_of = lambda b: (
        out_ref[rows_at(core * half + b * part, part), :] if b < 2 else shared_ref[rows_at(core * part, part), :]
    )
    own_weight = outw_ref[rows_at(core * width, width), :]
    other_weight = outw_ref[rows_at(other * width, width), :]
    blocks = [pl.ds(b * part, part) for b in range(3)]
    for b in range(3):
        middle[blocks[b], :] = x[blocks[b], :].astype(F32) + jnp.dot(
            own_rows_of(b), own_weight, preferred_element_type=F32
        )
    for copy in loads:
        copy.wait()
    if square:
        down_sends = [
            send_down(chip, 0, 12, near_x), send_down(chip, 1, 13, near_y), send_down(chip, 0, 14, near_y),
            send_down(chip, 1, 15, near_x),
        ]
    for copy in att_sends:
        copy.wait_recv()
    for rows in blocks:
        value = middle[rows, :] + jnp.dot(att_other[rows, :], other_weight, preferred_element_type=F32)
        middle[rows, :] = value
        second[rows, :] = (norm_parts(value)[0] * gain_ref[...]).astype(BF16)
    second_send = remote(second.at[mine], second.at[theirs], sems, 3, partner)
    second_send.start()

    def hidden_forward(start):
        rows = pl.ds(start, tokens)

        def one_tile(i, _):
            here_units = pl.ds(pl.multiple_of(i * tile, 128), tile)
            hidden, slope = gelu_pair(jnp.dot(second[rows, :], up[:, here_units], preferred_element_type=F32))
            hidden_all[rows, here_units] = hidden.astype(BF16)
            pre_all[rows, here_units] = slope.astype(BF16)
            return 0

        lax.fori_loop(0, 4, one_tile, 0)

    def hidden_backward(start):
        rows = pl.ds(start, tokens)

        def one_tile(i, _):
            here_units = pl.ds(pl.multiple_of(i * tile, 128), tile)
            pre_grad = nt(grad[rows, :], down[rows_at(i * tile, tile), :]) * pre_all[rows, here_units].astype(F32)
            pre_all[rows, here_units] = pre_grad.astype(BF16)
            return 0

        lax.fori_loop(0, 4, one_tile, 0)

    hidden_forward(0)
    if square:
        down_sends[0].wait_recv()
        down_sends[1].wait_recv()
        down_sends += [send_down(chip ^ 1, 0, 16, near_y), send_down(chip ^ 2, 1, 17, near_x)]
    second_send.wait_recv()
    hidden_forward(tokens)
    if square:
        for copy in down_sends[2:]:
            copy.wait_recv()
    for b in range(3):
        rows, there = pl.ds(tokens + b * part, part), blocks[b]
        parts_out[0, there, :] = jnp.dot(hidden_all[rows, :], down[...], preferred_element_type=F32).astype(BF16)
    first_part = remote(parts_out.at[0], parts_in.at[0], sems, 4, partner)
    first_part.start()
    for rows in blocks:
        forward[rows, :] = middle[rows, :] + jnp.dot(hidden_all[rows, :], down[...], preferred_element_type=F32)
    first_part.wait_recv()
    for rows in blocks:
        results[rows, :] = (forward[rows, :] + parts_in[0, rows, :].astype(F32)).astype(BF16)
    kept_rows = results.at[rows_at(zq * part, part)]
    output_moves = Moves(
        [remote(kept_rows, output_ref.at[zq], sems, 19, keep)],
        [pltpu.make_async_copy(kept_rows, output_ref.at[zq], local_sem.at[1])],
        remote(results.at[rows_at((1 - zq) * part, part)], output_ref.at[zq], sems, 21, cross),
        moves,
    )
    third_ref[...] = results[pl.ds(half, part), :]
    output_moves.start()
    cot_move.wait()
    grad_sends.append(take_grad(cot_in[0], (1 - zq) * part, (2 * core + 1 - zq) * part, filled, 18))
    grad_sends.append(take_grad(cot_in[1], half, (2 * core + zq) * part, shared_filled, 23))
    hidden_backward(0)
    for copy in grad_sends:
        copy.wait_recv()
    hidden_backward(tokens)
    for b in range(3):
        rows, there = pl.ds(tokens + b * part, part), blocks[b]
        parts_out[1, there, :] = nt(pre_all[rows, :], up[...]).astype(BF16)
    second_part = remote(parts_out.at[1], parts_in.at[1], sems, 5, partner)
    second_part.start()
    for rows in blocks:
        backward[rows, :] = nt(pre_all[rows, :], up[...])

    turned[...] = second[...].T
    quarter = model // 4
    far_sends = [
        remote(stage.at[0, pl.ds(0, tile)], far_in.at[0], sems, 9, near_y),
        remote(stage.at[0, pl.ds(tile, tile)], far_in.at[1], sems, 10, near_x),
    ]

    def weight_grads(i, _):
        target = chip ^ (3 - i) if square else 3 - i
        place = jnp.where(i == 0, 0, 1 + i % 2)

        @pl.when(i == 3)
        def _():
            pltpu.make_async_copy(stage.at[place], packed_ref.at[target], write_sem.at[place]).wait()

        here_units = pl.ds(pl.multiple_of(target * tile, 128), tile)
        stage[place, pl.ds(0, tile), :] = tn(hidden_all[:, here_units], grad[...]).astype(BF16)
        values = jnp.dot(
            turned[rows_at(target * quarter, quarter), :], pre_all[...], preferred_element_type=F32
        ).astype(BF16)
        for j in range(2):
            stage[place, pl.ds(tile + j * quarter, quarter), :] = values[:, j * model : (j + 1) * model]
        pltpu.make_async_copy(stage.at[place], packed_ref.at[target], write_sem.at[place]).start()
        if square:

            @pl.when(i == 0)
            def _():
                for copy in far_sends:
                    copy.start()

        return 0

    lax.fori_loop(0, 4, weight_grads, 0)

    second_send.wait_send()
    second_part.wait_recv()
    gain_sum = jnp.zeros(gaing_ref.shape, F32)
    for rows in blocks:
        n, r = norm_parts(middle[rows, :])
        upstream = backward[rows, :] + parts_in[1, rows, :].astype(F32)
        more, gain_more = norm_back(upstream, n, r, gain_ref[...])
        gain_sum = gain_sum + gain_more
        value = grad[rows, :].astype(F32) + more
        midg_ref[rows, :] = value
        branch = value.astype(BF16)
        second[rows, :] = branch
        heads_out[rows, :] = nt(branch, other_weight).astype(BF16)
    gaing_ref[...] = gain_sum
    head_sends = [
        remote(heads_out.at[pl.ds(0, half)], row_grad.at[rows_at(core * half, half)], sems, 6, partner),
        remote(heads_out.at[pl.ds(half, part)], shared_grad.at[rows_at(core * part, part)], sems, 7, partner),
    ]
    for copy in head_sends:
        copy.start()
    branch = second[mine, :]
    forward[rows_at(core * width, width), :] = tn(
        out_ref[rows_at(core * half, half), :], second[pl.ds(0, half), :]
    ) + tn(shared_ref[rows_at(core * part, part), :], second[pl.ds(half, part), :])
    forward[rows_at(other * width, width), :] = tn(att_other[...], branch)
    lanes = lambda side: pl.ds(pl.multiple_of(side * width, 128), width)
    cols_out[...] = forward[pl.ds(0, model), lanes(other)].astype(BF16)
    cols_send = remote(cols_out, cols_in, sems, 8, partner)
    cols_send.start()
    for b in range(3):
        value = nt(second[blocks[b], :], own_weight).astype(BF16)
        if b < 2:
            row_grad[rows_at(core * half + b * part, part), :] = value
        else:
            shared_grad[rows_at(core * part, part), :] = value
    cols_send.wait_recv()
    outg_ref[...] = (forward[pl.ds(0, model), lanes(core)] + cols_in[...].astype(F32)).astype(BF16)
    for copy in head_sends:
        copy.wait_recv()
    for copy in att_sends + head_sends + grad_sends + [first_part, second_part, cols_send]:
        copy.wait_send()
    if square:
        for copy in down_sends:
            copy.wait_send()
        for copy in far_sends:
            copy.wait()
    far_write = pltpu.make_async_copy(far_in, far_ref, load_sem.at[0])
    far_write.start()
    for place in range(3):
        pltpu.make_async_copy(stage.at[place], packed_ref.at[0], write_sem.at[place]).wait()
    output_moves.wait()
    far_write.wait()


def dense(square, out, shared_out, x, grad, cotangent, out_matrix, gain, bounds, up, down):
    model = x.shape[1]
    tokens = x.shape[0]
    part = tokens // 3
    length, width = out.shape
    units = up.shape[1]
    tile = units // 4
    anywhere = pl.BlockSpec(memory_space=pl.ANY)
    near = pl.BlockSpec(memory_space=pltpu.VMEM)
    both = 2 * tokens
    low = lambda *shape: pltpu.VMEM(shape, BF16)
    wide = lambda *shape: pltpu.VMEM(shape, F32)
    return pl.pallas_call(
        functools.partial(dense_kernel, square),
        in_specs=[near] * 4 + [anywhere] + [near] * 3 + [anywhere] * 2,
        out_specs=[anywhere] + [near] * 6 + [anywhere, anywhere],
        out_shape=[
            jax.ShapeDtypeStruct((2, part, model), BF16),
            jax.ShapeDtypeStruct((part, model), BF16),
            jax.ShapeDtypeStruct((tokens, model), F32),
            jax.ShapeDtypeStruct((length, width), BF16),
            jax.ShapeDtypeStruct((length // 2, width), BF16),
            jax.ShapeDtypeStruct((model, width), BF16),
            jax.ShapeDtypeStruct((1, model), F32),
            jax.ShapeDtypeStruct((4, 2 * tile, model), BF16),
            jax.ShapeDtypeStruct((2, tile, model), BF16),
        ],
        scratch_shapes=[
            low(tokens, width), low(both, model), low(model, both), low(both, model), low(2, part, model),
            low(both, units), low(both, units), wide(tokens, model), wide(tokens, model), wide(tokens, model),
            low(model, units), low(units, model), low(tokens, model), low(2, tokens, model), low(2, tokens, model),
            low(tokens, width), low(model, width), low(model, width), low(3, 2 * tile, model), low(2, tile, model),
            pltpu.SemaphoreType.DMA((24,)),
            pltpu.SemaphoreType.DMA((24,)),
            pltpu.SemaphoreType.DMA((2,)),
            pltpu.SemaphoreType.DMA((3,)),
            pltpu.SemaphoreType.DMA((3,)),
        ],
        compiler_params=pltpu.CompilerParams(
            collective_id=1, has_side_effects=True, vmem_limit_bytes=63 * 1024 * 1024
        ),
        name="dense",
    )(out, shared_out, x, grad, cotangent, out_matrix, gain, bounds, up, down)


def add(*terms):
    total = terms[0].astype(F32)
    for term in terms[1:]:
        total = total + term.astype(F32)
    return total


def backward_kernel(square, pics, *refs):
    refs = list(refs)
    take = lambda count: [refs.pop(0) for _ in range(count)]
    names = ("aug", "qk", "v", "out", "do", "raw", "normed")
    row_in = dict(zip(names, take(7)))
    shared_in = dict(zip(names, take(7)))
    mix_in, x_in, midg_in, gain_first, gain_qk, gain_second_grad, bounds_ref = take(7)
    third_in = take(1)[0]
    if square:
        packed_in, far_ref, outg_in = take(3)
        third_out, grad_out, total_ref, gains_ref, up_ref, down_ref, outw_ref = take(7)
    else:
        third_out, grad_own, mix_grad_ref, gains_sum = take(4)
    names = names[:-1]
    row = dict(zip(names, take(6)))
    shared = dict(zip(names, take(6)))
    normed, turned, weight, x, midg = take(5)
    kaug, vaug, doaug, qsum, ksum, mixed, part_k, part_v, got_k, got_v = take(10)
    gain_sums, parts_in = take(2)
    if square:
        gains_sum, outg = take(2)
        held, far_in, onward_in, direct_in, line, whole_line, line_right, line_left = take(8)
        up_out, up_got = take(2)
        planes = [take(4) for _ in range(3)]
        lines = [take(4) for _ in range(2)]
        gain_part, gain_got = take(2)
    sent, got, load_sem, local_sem = take(4)

    chip, core, zp, zq = here()
    z = 2 * zp + zq
    sems = (sent, got)
    partner = (chip, 1 - core, zp, zq)
    keep = (chip, zp, core, zq)
    cross = (chip, zp, core, 1 - zq)
    moves = core != zp
    near_x = (chip ^ 1, core, zp, zq)
    near_y = (chip ^ 2, core, zp, zq)
    along = [(chip, core, zp, 1 - zq), (chip, core, 1 - zp, zq), (chip, core, 1 - zp, 1 - zq)]
    tokens, model = x.shape
    part = tokens // 3
    half, length = 2 * part, 4 * part
    width = model // 2
    queries = half
    waits = []

    def load(source, target, at):
        copy = pltpu.make_async_copy(source, target, load_sem.at[at])
        copy.start()
        return copy

    def send(source, target, at, device):
        copy = remote(source, target, sems, at, device)
        copy.start()
        waits.append(copy)
        return copy

    if square:
        rows_count = packed_in.shape[1]
        span = rows_count // 2
        first_half, second_half = pl.ds(0, span), pl.ds(span, span)
        held_loads = [
            load(packed_in.at[chip ^ 1, first_half], held.at[0], 24),
            load(packed_in.at[chip ^ 2, second_half], held.at[1], 25),
            load(packed_in.at[chip, first_half], held.at[2], 26),
            load(packed_in.at[chip, second_half], held.at[3], 27),
        ]
        far_loads = [load(far_ref.at[i], far_in.at[i], 28 + i) for i in range(2)]
    keys_of = lambda ref: ref.at[:, pl.ds(width, width)]
    load_bufs = lambda source, target, at: [
        load(keys_of(source[name]) if name == "qk" else source[name], target[name], at + i)
        for i, name in enumerate(names)
    ]
    shared_loads = load_bufs(shared_in, shared, 0)
    row_loads = load_bufs(row_in, row, 6)
    late_loads = [
        load(row_in["normed"], normed.at[pl.ds(0, length)], 12),
        load(shared_in["normed"].at[rows_at(zq * part, part)], normed.at[pl.ds(length, part)], 13),
        load(
            shared_in["normed"].at[rows_at((2 + zq) * part, part)], normed.at[pl.ds(length + part, part)], 14
        ),
        load(mix_in, weight, 15),
        load(x_in, x, 16),
        load(midg_in, midg, 17),
    ]
    if square:
        late_loads.append(load(outg_in, outg, 18))
    if square:
        greet([partner, cross, near_x, near_y] + along, keep, moves)
        for copy in held_loads + far_loads:
            copy.wait()
        far_in[0] = add(far_in[0], held[0]).astype(BF16)
        bulk_on_x = send(far_in.at[0], onward_in.at[0], 11, near_x)
        far_in[1] = add(far_in[1], held[1]).astype(BF16)
        bulk_on_y = send(far_in.at[1], onward_in.at[1], 12, near_y)
        bulk_x = send(packed_in.at[chip ^ 1, second_half], direct_in.at[0], 2, near_x)
        bulk_y = send(packed_in.at[chip ^ 2, first_half], direct_in.at[1], 3, near_y)

        bulk_line = Line(line, whole_line, line_right, line_left, sems, 14)
        plane_a, plane_b, plane_gains = (
            PlaneSum(*refs_of, sems, 26 + 7 * i, waits) for i, refs_of in enumerate(planes)
        )
        line_a, line_b = (Line(*refs_of, sems, 47 + 12 * i) for i, refs_of in enumerate(lines))
    else:
        greet([partner, along[0]], keep, moves)
    third_moves = Moves(
        [remote(third_in, third_out, sems, 5, keep)],
        [pltpu.make_async_copy(third_in, third_out, local_sem.at[2])],
        None,
        moves,
    )
    third_moves.start()

    gain_sums[...] = jnp.zeros_like(gain_sums)

    pairs = width // 128

    def attend_back(bufs, bounds, count, q_lanes_to, k_to, v_to, at, span=(0, pairs)):
        def one(p, _):
            lanes = pl.ds(pl.multiple_of(p * 128, 128), 128)
            key_lanes = pl.ds(pl.multiple_of(width + p * 128, 128), 128)
            attend_back_kernel(
                pics, bufs["aug"].at[pl.ds(2 * p, 2)], bufs["qk"].at[:, lanes], bufs["v"].at[:, lanes],
                bufs["out"].at[:, lanes], bufs["do"].at[:, lanes], bufs["raw"].at[:, lanes],
                bufs["raw"].at[:, key_lanes], gain_qk.at[:, lanes], gain_qk.at[:, key_lanes], bounds,
                q_lanes_to(p), k_to(p), v_to(p), gain_sums.at[pl.ds(at, 1), lanes], gain_sums.at[pl.ds(at + 1, 1), lanes],
                kaug, vaug, doaug.at[:, pl.ds(0, count)], qsum.at[:, pl.ds(0, count)], ksum,
            )
            return 0

        lax.fori_loop(span[0], span[1], one, 0)

    def mixed_at(start, count, side):
        return lambda p: mixed.at[pl.ds(start, count), pl.ds(pl.multiple_of(side * width + p * 128, 128), 128)]

    whole_lanes = lambda ref: lambda p: ref.at[:, pl.ds(pl.multiple_of(p * 128, 128), 128)]
    for copy in shared_loads:
        copy.wait()
    attend_back(
        shared, bounds_ref.at[1], queries, mixed_at(length, queries, 0), whole_lanes(part_k), whole_lanes(part_v), 0
    )
    side_sends = []
    for i in range(2):
        theirs = rows_at((2 * i + 1 - zq) * part, part)
        there = pl.ds(i * part, part)
        side_sends.append(send(part_k.at[theirs], got_k.at[there], 7 + 2 * i, along[0]))
        side_sends.append(send(part_v.at[theirs], got_v.at[there], 8 + 2 * i, along[0]))
    for copy in row_loads + late_loads:
        copy.wait()
    turned[...] = normed[...].T
    parts_out = normed.at[pl.ds(0, tokens)]
    if square:
        grad_own = normed.at[pl.ds(tokens, tokens)]
    shard = model // 8
    other = 1 - core
    row_to = (mixed_at(0, length, 0), mixed_at(0, length, 1), mixed_at(0, length, 2), 2)
    attend_back(row, bounds_ref.at[0], length, *row_to, (0, pairs - 1))
    if square:
        quarter_rows = rows_count // 4
        for copy in (bulk_y, bulk_on_x, bulk_x, bulk_on_y):
            copy.wait_recv()
        first_sum = add(held[2], onward_in[0], direct_in[1]).astype(BF16)
        second_half_sum = add(held[3], onward_in[1], direct_in[0]).astype(BF16)
        for i in range(2):
            line[i] = first_sum[i * quarter_rows : (i + 1) * quarter_rows]
            line[2 + i] = second_half_sum[i * quarter_rows : (i + 1) * quarter_rows]
        bulk_line.start()

    for copy in side_sends:
        copy.wait_recv()

    def shared_pair(p, _):
        lanes = pl.ds(pl.multiple_of(p * 128, 128), 128)
        key_lanes = pl.ds(pl.multiple_of(width + p * 128, 128), 128)
        shared_keys_kernel(
            part_k.at[:, lanes], part_v.at[:, lanes], got_k.at[:, lanes], got_v.at[:, lanes],
            shared["raw"].at[:, key_lanes], gain_qk.at[:, key_lanes], mixed_at(length, queries, 1)(p),
            mixed_at(length, queries, 2)(p), gain_sums.at[pl.ds(4, 1), lanes],
        )
        return 0

    lax.fori_loop(0, pairs, shared_pair, 0)

    def mix_gradient(start, count, payload):
        for t in range(3):
            lanes = slice(t * width + start, t * width + start + count)
            value = jnp.dot(turned[...], mixed[:, lanes], preferred_element_type=F32).astype(BF16)
            if payload is None:
                mix_grad_ref[:, lanes] = value
                continue
            for p in range(8):
                payload[p, :shard, t * count : (t + 1) * count] = value[p * shard : (p + 1) * shard]

    early = width - 128
    mix_gradient(0, early, plane_a.payload if square else None)
    if square:
        outs_end = shard + shard // 2
        for p in range(8):
            for i in range(2):
                at = p * shard + i * (shard // 2)
                plane_a.payload[p, shard:outs_end, i * width : (i + 1) * width] = outg[at : at + shard // 2, :]
            plane_a.payload[p, outs_end:, :] = jnp.zeros((16, 3 * early), BF16)
        plane_a.start()
        bulk_line.first()
    attend_back(row, bounds_ref.at[0], length, *row_to, (pairs - 1, pairs))
    block_rows = lambda side, b: (
        rows_at(side * half + b * part, part) if b < 2 else rows_at(length + side * part, part)
    )
    for b in range(3):
        parts_out[pl.ds(b * part, part), :] = nt(mixed[block_rows(other, b), :], weight[...]).astype(BF16)
    part_send = send(parts_out, parts_in, 13, partner)
    if square:
        plane_a.pass_on()
        bulk_line.second()
    mix_gradient(early, 128, plane_b.payload if square else None)
    if square:
        plane_b.start()
    part_send.wait_recv()
    first_sum_gain = jnp.zeros((1, model), F32)
    for b in range(3):
        rows = pl.ds(b * part, part)
        upstream = nt(mixed[block_rows(core, b), :], weight[...]) + parts_in[rows, :].astype(F32)
        n, r = norm_parts(x[rows, :].astype(F32))
        value, more = norm_back(upstream, n, r, gain_first[...])
        first_sum_gain = first_sum_gain + more
        grad_own[rows, :] = (midg[rows, :] + value).astype(BF16)
    gains_sum[...] = jnp.zeros_like(gains_sum)
    gains_sum[0:1, :] = first_sum_gain
    mine_lanes = pl.ds(pl.multiple_of(core * width, 128), width)
    gains_sum[1:2, mine_lanes] = gain_sums[0:1, :] + gain_sums[2:3, :]
    gains_sum[2:3, mine_lanes] = gain_sums[3:4, :] + gain_sums[4:5, :]
    gains_sum[3:4, :] = gain_second_grad[...]

    if square:
        kept_rows, third_rows = grad_own.at[rows_at(zq * part, part)], grad_own.at[pl.ds(half, part)]
        grad_moves = Moves(
            [
                remote(kept_rows, grad_out.at[zq], sems, 0, keep),
                remote(third_rows, grad_out.at[2], sems, 1, keep),
            ],
            [
                pltpu.make_async_copy(kept_rows, grad_out.at[zq], local_sem.at[0]),
                pltpu.make_async_copy(third_rows, grad_out.at[2], local_sem.at[1]),
            ],
            remote(grad_own.at[rows_at((1 - zq) * part, part)], grad_out.at[zq], sems, 4, cross),
            moves,
        )
        grad_moves.start()
        for p in range(8):
            plane_gains.payload[p] = jnp.zeros((16, 128), BF16)
            plane_gains.payload[p, :, :shard] = gains_sum[:, p * shard : (p + 1) * shard].astype(BF16)
        plane_gains.start()

        def to_line(plane, target):
            kept = plane.finish()
            rows = target.parts.shape[1]
            for i in range(2):
                target.parts[2 * core + i] = kept[i * rows : (i + 1) * rows].astype(BF16)
                target.parts[2 * (1 - core) + i] = plane.came[i * rows : (i + 1) * rows]
            target.start()

        plane_a.to_core()
        bulk_line.third()
        plane_b.pass_on()
        to_line(plane_a, line_a)
        plane_gains.pass_on()
        bulk_line.fourth()
        line_a.first()
        plane_b.to_core()
        plane_gains.to_core()
        line_a.second()
        to_line(plane_b, line_b)
        gain_part[...] = (plane_gains.finish() + plane_gains.came[...].astype(F32)).astype(BF16)
        gain_sends = [send(gain_part, gain_got.at[i], 71 + i, along[i]) for i in range(3)]
        bulk_line.fifth()
        line_a.third()
        line_b.first()
        line_a.fourth()
        line_b.second()
        bulk_line.sixth()

        flat = jnp.concatenate([whole_line[i] for i in range(4)], axis=0)
        tile = down_ref.shape[0]
        ups = [flat[tile + 2 * shard * i : tile + 2 * shard * (i + 1)] for i in range(2)]
        for i in range(2):
            up_out[i] = jnp.where(core == 0, ups[i][shard:], ups[i][:shard])
        up_send = send(up_out, up_got, 74, partner)
        line_b.third()
        line_a.fifth()
        line_b.fourth()
        down_ref[...] = flat[:tile]

        def place_up(side, i, values):
            for j in range(2):
                lanes = pl.ds(pl.multiple_of((2 * (2 * i + j) + side) * tile, 128), tile)
                up_ref[:, lanes] = values[:, j * tile : (j + 1) * tile]

        for i in range(2):
            place_up(core, i, jnp.where(core == 0, ups[i][:shard], ups[i][shard:]))
        line_b.fifth()
        line_a.sixth()
        up_send.wait_recv()
        for i in range(2):
            place_up(other, i, up_got[i])

        def place(target, start, count):
            for index in range(4):
                side, low_half = index // 2, index % 2
                values = target.whole[index]
                rows = values.shape[0]
                first_row = low_half * rows
                taken = min(rows, shard - first_row)
                for t in range(3):
                    lanes = slice((2 * t + side) * width + start, (2 * t + side) * width + start + count)
                    total_ref[first_row : first_row + taken, lanes] = values[:taken, t * count : (t + 1) * count]
                if taken < rows:
                    for i in range(2):
                        outw_ref[i * (shard // 2) : (i + 1) * (shard // 2), side * width : (side + 1) * width] = values[
                            taken : taken + shard // 2, i * width : (i + 1) * width
                        ]

        place(line_a, 0, early)
        for copy in gain_sends:
            copy.wait_recv()
        gains_ref[...] = add(gain_part[...], gain_got[0], gain_got[1], gain_got[2])
        line_b.sixth()
        place(line_b, early, 128)
        for target in (bulk_line, line_a, line_b):
            target.wait_sends()
        grad_moves.wait()
    third_moves.wait()
    for copy in waits:
        copy.wait_send()


def backward_pass(square, pics, row, shared, weights, gains, bounds, *more):
    length, model = row[1].shape
    width = model // 2
    part = length // 4
    half, tokens = 2 * part, 3 * part
    shard = model // 8
    near = pl.BlockSpec(memory_space=pltpu.VMEM)
    anywhere = pl.BlockSpec(memory_space=pl.ANY)
    low = lambda *shape: (shape, BF16)
    wide = lambda *shape: (shape, F32)
    if square:
        rows = more[1].shape[1]
        tile = rows // 2
        outs = [
            (low(part, model), anywhere),
            (low(3, part, model), anywhere),
            (low(shard, 6 * width), near),
            (wide(16, 128), near),
            (low(shard, 8 * tile), near),
            (low(tile, model), near),
            (low(shard, model), near),
        ]
    else:
        outs = [
            (low(part, model), anywhere),
            (low(tokens, model), near),
            (low(model, 3 * width), near),
            (wide(16, model), near),
        ]
    scratch = []
    for queries in (length, half):
        scratch += [
            low(2 * (width // 128), queries, 128), low(length, width), low(length, width), low(queries, width),
            low(queries, width), low(length, 2 * width),
        ]
    scratch += [
        low(length + half, model), low(model, length + half), low(model, 3 * width), low(tokens, model),
        wide(tokens, model),
        low(2, length, 128), low(2, length, 128), low(2, length, 128), wide(2, length, 128), wide(length, 128),
        low(length + half, 3 * width), low(length, width), low(length, width), low(half, width), low(half, width),
        wide(8, width), low(tokens, model),
    ]
    if square:
        span = rows // 2
        early = 3 * (width - 128)
        plane = lambda count, columns: [
            low(8, count, columns), low(5, count, columns), low(4, count, columns), low(count, columns)
        ]
        chunked = lambda count, columns: [low(size, count, columns) for size in (4, 4, 3, 3)]
        early_rows = shard + shard // 2 + 16
        scratch += [
            wide(16, model), low(model, width),
            low(4, span, model), low(2, span, model), low(2, span, model), low(2, span, model),
            low(4, rows // 4, model), low(4, rows // 4, model), low(3, rows // 4, model), low(3, rows // 4, model),
            low(2, shard, model), low(2, shard, model),
            *plane(early_rows, early), *plane(shard, 3 * 128), *plane(16, 128),
            *chunked(early_rows // 2, early), *chunked(shard // 2, 3 * 128), low(16, 128), low(3, 16, 128),
        ]
    return pl.pallas_call(
        functools.partial(backward_kernel, square, pics),
        in_specs=[anywhere] * 17 + [near] * 4 + [anywhere] * len(more),
        out_specs=[spec for _, spec in outs],
        out_shape=[jax.ShapeDtypeStruct(*shape) for shape, _ in outs],
        scratch_shapes=[pltpu.VMEM(*shape) for shape in scratch]
        + [
            pltpu.SemaphoreType.DMA((75,)),
            pltpu.SemaphoreType.DMA((75,)),
            pltpu.SemaphoreType.DMA((30,)),
            pltpu.SemaphoreType.DMA((3,)),
        ],
        compiler_params=pltpu.CompilerParams(
            collective_id=2, has_side_effects=True, vmem_limit_bytes=63 * 1024 * 1024
        ),
        name="backward_pass",
    )(*row, *shared, *weights, *gains, bounds, *more)


def local(
    tokens, lengths, pictures, first_gain, mix_weight, query_gain, key_gain, out_weight,
    second_gain, up_weight, down_weight, cotangent,
):
    chip, core, zp, zq = here()
    chips = lax.axis_size("chip")
    square = chips == 4
    rows = ("chip", "core")
    _, part, model = tokens.shape
    length = 4 * part
    half = 2 * part
    width = HEADS // 2 * HEAD
    pics = lengths.shape[1]
    shard = mix_weight.shape[0]

    hidden = up_weight.shape[1]
    tile = hidden // 8
    gains = [gain[None] for gain in (first_gain, query_gain, key_gain, second_gain)]
    if square:
        forward = forward_pass(
            True, pics, tokens, cotangent, lengths, mix_weight, *gains, up_weight, out_weight
        )
        up_half, out_matrix = forward[19:]
        down_half = down_weight
        gain_second = forward[5]
    else:
        gather = lambda weight: lax.all_gather(weight, rows, axis=0, tiled=True)
        half_of = lambda weight, axis: pick(weight, core, axis)
        mix_half = half_of(gather(mix_weight).reshape(model, 3, 2, width), 2).reshape(model, 3 * width)
        up_half = half_of(gather(up_weight).reshape(model, 4, 2, tile), 2).reshape(model, 4 * tile)
        down_half = half_of(gather(down_weight).reshape(4, 2, tile, model), 1).reshape(4 * tile, model)
        out_matrix = gather(out_weight)
        gains = lax.all_gather(jnp.concatenate(gains), rows, axis=0, tiled=False)
        gains = gains.transpose(1, 0, 2).reshape(4, 1, model).astype(F32)
        gain_second = gains[3]
        gain_qk = half_of(gains[1:3].reshape(2, 2, width), 1).reshape(1, model)
        forward = forward_pass(False, pics, tokens, cotangent, lengths, mix_half, gains[0], gain_qk)
    own_tokens, bounds, mix_half, grad_tokens, gain_first, _, gain_qk = forward[:7]
    normed, qk, v, raw, out, aug = forward[7:13]
    shared_normed, shared_qk, shared_v, shared_raw, shared_out, shared_aug = forward[13:19]

    def collect(mine, cross, third):
        mine = lax.ppermute(mine, COLUMN, KEEP)
        cross = lax.ppermute(cross, COLUMN, CROSS)
        third = lax.ppermute(third, COLUMN, KEEP)
        return jnp.stack([jnp.where(zq == 0, mine, cross), jnp.where(zq == 0, cross, mine), third])

    output, third, middle_grad, grad, shared_grad, out_grad, second_gain_grad, packed, far = dense(
        square, out, shared_out, own_tokens, grad_tokens, cotangent, out_matrix, gain_second, bounds,
        up_half, down_half,
    )
    row_side = (aug, qk, v, out, grad, raw, normed)
    shared_side = (shared_aug, shared_qk, shared_v, shared_out, shared_grad, shared_raw, shared_normed)
    weights = (mix_half, own_tokens, middle_grad)
    gains = (gain_first, gain_qk, second_gain_grad)
    if square:
        third, input_out, mix_out, gains_out, up_out, down_out, outw_out = backward_pass(
            True, pics, row_side, shared_side, weights, gains, bounds, third, packed, far, out_grad
        )
        gains_out = gains_out[:4, :shard]
        mix_out, up_out, down_out, outw_out = (
            array.astype(F32) for array in (mix_out, up_out, down_out, outw_out)
        )
    else:
        third, input_grad, mix_grad, gain_grads = backward_pass(
            False, pics, row_side, shared_side, weights, gains, bounds, third
        )

        def reduce(grad):
            return lax.psum(lax.psum_scatter(grad, rows, scatter_dimension=0, tiled=True), SEQ).astype(F32)

        first, second = input_grad[:part], input_grad[part:half]
        input_out = collect(
            jnp.where(zq == 0, first, second), jnp.where(zq == 0, second, first), input_grad[half:]
        )
        own_core = jnp.arange(2) == core
        eighth = model // 8
        down_grad = packed[:, None, :tile]
        down_out = reduce(jnp.where(own_core[None, :, None, None], down_grad, 0).reshape(hidden, model))
        up_grad = packed[:, tile : 2 * tile].reshape(4, 2, 2 * eighth, 2, tile).transpose(0, 2, 1, 3, 4)
        up_grad = up_grad.reshape(model, 4, 1, tile)
        up_out = reduce(jnp.where(own_core[None, None, :, None], up_grad, 0).reshape(model, hidden))
        out_grad = out_grad.reshape(model, 1, width)
        outw_out = reduce(jnp.where(own_core[None, :, None], out_grad, 0).reshape(model, model))
        mix_out = reduce(
            jnp.where(own_core[None, None, :, None], mix_grad.reshape(model, 3, 1, width), 0).reshape(model, 6 * width)
        )
        gain_grads = gain_grads[:4].reshape(4, 2 * chips, shard).transpose(1, 0, 2).astype(BF16)
        gains_out = reduce(gain_grads).reshape(4, shard)
    output = jnp.concatenate([output, third[None]])
    return (
        output, input_out, gains_out[0], mix_out, gains_out[1], gains_out[2], outw_out, gains_out[3],
        up_out, down_out,
    )


def solution(mesh):
    fsdp = mesh.shape["fsdp"]
    split = Mesh(mesh.devices.reshape(fsdp // 2, 2, 2, 2), ("chip", "core", "zp", "zq"))
    rows = ("chip", "core")
    return jax.shard_map(
        local,
        mesh=split,
        in_specs=(
            P(rows, SEQ, None),
            P(rows, None),
            P(rows, SEQ),
            P(rows),
            P(rows, None),
            P(rows),
            P(rows),
            P(rows, None),
            P(rows),
            P(rows, None),
            P(rows, None),
            P(rows, SEQ, None),
        ),
        out_specs=(
            P(rows, SEQ, None),
            P(rows, SEQ, None),
            P(rows),
            P(rows, None),
            P(rows),
            P(rows),
            P(rows, None),
            P(rows),
            P(rows, None),
            P(rows, None),
        ),
        check_vma=False,
    )
```

```python
import functools

import jax
import jax.numpy as jnp
from jax import lax
from jax.experimental import pallas as pl
from jax.experimental.pallas import tpu as pltpu
from jax.sharding import Mesh, PartitionSpec as P

HEADS = 12
HEAD = 64
EPSILON = 1e-06
BLOCK = 256
STEP = 512
MARK = 32.0
EXP2_FACTOR = HEAD**-0.5 * 1.4426950408889634
F32 = jnp.float32
BF16 = jnp.bfloat16
VMEM_LIMIT = 56 * 1024 * 1024

SEQ = ("zp", "zq")
COLUMN = ("core", "zp", "zq")
KEEP = [
    (core * 4 + z, (z // 2) * 4 + 2 * core + z % 2) for core in range(2) for z in range(4)
]
CROSS = [
    (core * 4 + z, (z // 2) * 4 + 2 * core + 1 - z % 2) for core in range(2) for z in range(4)
]


def swap(array, name, bit=1):
    count = lax.axis_size(name)
    return lax.ppermute(array, name, [(i, i ^ bit) for i in range(count)])


def pick(array, index, axis=0):
    return lax.dynamic_index_in_dim(array, index, axis, keepdims=False)


def group_ones(scale, size=128):
    row = lax.broadcasted_iota(jnp.int32, (size, size), 0) // HEAD
    column = lax.broadcasted_iota(jnp.int32, (size, size), 1) // HEAD
    return jnp.where(row == column, scale, 0.0).astype(BF16)


def group_sum(values, ones):
    return jnp.dot(values.astype(BF16), ones, preferred_element_type=F32)


def group_sum_fine(values, ones):
    high = values.astype(BF16)
    return group_sum(high, ones) + group_sum(values - high.astype(F32), ones)


def project_kernel(x_ref, gain_ref, weight_ref, qkg_ref, normed_ref, qk_ref, v_ref, raw_ref):
    both = qk_ref.shape[1]
    x = x_ref[...].astype(F32)
    center = x - jnp.mean(x, axis=-1, keepdims=True)
    spread = jnp.mean(center * center, axis=-1, keepdims=True)
    normed = (center * lax.rsqrt(spread + EPSILON) * gain_ref[...]).astype(BF16)
    normed_ref[...] = normed
    ones = group_ones(1.0 / HEAD, 256)
    for at in range(0, both, 256):
        lanes = slice(at, at + 256)
        raw = jnp.dot(normed, weight_ref[:, lanes], preferred_element_type=F32)
        raw_ref[:, lanes] = raw.astype(BF16)
        c = raw - group_sum(raw, ones)
        n = c * lax.rsqrt(group_sum(c * c, ones) + EPSILON)
        qk_ref[:, lanes] = (n * qkg_ref[:, lanes]).astype(BF16)
    v_ref[...] = jnp.dot(normed, weight_ref[:, both:], preferred_element_type=F32).astype(BF16)


def nt(a, b):
    return lax.dot_general(a, b, (((1,), (1,)), ((), ())), preferred_element_type=F32)


def tn(a, b):
    return lax.dot_general(a, b, (((0,), (0,)), ((), ())), preferred_element_type=F32)


def slots(queries, length, part):
    at = lax.broadcasted_iota(jnp.int32, (queries, 128), 0)
    if queries == length:
        return at
    return at % part + part * (lax.axis_index("zq") + 2 * (at // part))


def own_rows(ref, start, count, queries, part):
    if queries == ref.shape[0]:
        return ref[pl.ds(start, count), :]
    zq = lax.axis_index("zq")
    pieces = [
        ref[pl.ds(pl.multiple_of((zq + 2 * i) * part, part), part), :]
        for i in range(start // part, (start + count) // part)
    ]
    return jnp.concatenate(pieces, axis=0)


def query_marks(bounds_ref, place, queries, length, part, pics):
    at = slots(queries, length, part)
    inside = (at >= bounds_ref[0:1, :]) & (at < bounds_ref[2:3, :])
    values = jnp.where(inside, MARK, 0.0)
    return jnp.where(place == pics, MARK, values).astype(BF16)


def key_marks(bounds_ref, place, length, pics):
    at = lax.broadcasted_iota(jnp.int32, (length, 128), 0)
    inside = (at >= bounds_ref[0:1, :]) & (at < bounds_ref[1:2, :])
    values = jnp.where(inside, MARK, 0.0)
    values = jnp.where(place == pics, -MARK, values)
    return jnp.where((place > pics) & (place < pics + 4), 1.0, values).astype(BF16)


def attend_kernel(pics, q_ref, k_ref, v_ref, bounds_ref, out_ref, aug_ref, kaug, vaug, qaug):
    length = k_ref.shape[0]
    queries = out_ref.shape[0]
    part = length // 4
    lane = lax.broadcasted_iota(jnp.int32, (1, 128), 1)
    place = lane % HEAD
    sides = [lane < HEAD, lane >= HEAD]
    kmarks = key_marks(bounds_ref, place, length, pics)
    qmarks = query_marks(bounds_ref, place, queries, length, part, pics)
    qaug[...] = qmarks
    for h in range(2):
        kaug[h] = jnp.where(sides[h], k_ref[...], kmarks)
        vaug[h] = jnp.where(sides[h], v_ref[...], jnp.ones_like(v_ref))
    for b in range(queries // STEP):
        rows = pl.ds(b * STEP, STEP)
        mine = own_rows(q_ref, b * STEP, STEP, queries, part)
        query = [jnp.where(sides[h], mine, qaug[rows, :]) for h in range(2)]
        total = [jnp.zeros((STEP, 128), F32)] * 2
        for j in range(length // STEP):
            keys = pl.ds(j * STEP, STEP)
            scores = [nt(query[h], kaug[h, keys, :]) for h in range(2)]
            weights = [jnp.exp2(x * EXP2_FACTOR).astype(BF16) for x in scores]
            total = [
                total[h] + jnp.dot(weights[h], vaug[h, keys, :], preferred_element_type=F32) for h in range(2)
            ]
        results = []
        for h in range(2):
            results.append(total[h] / pltpu.roll(total[h], HEAD, 1))
            log_total = jnp.log(jnp.where(sides[h], 1.0, total[h])) * -(HEAD**0.5)
            first = log_total.astype(BF16)
            rest = log_total - first.astype(F32)
            middle = rest.astype(BF16)
            last = (rest - middle.astype(F32)).astype(BF16)
            logs = jnp.where(place == pics + 1, first, jnp.where(place == pics + 2, middle, last))
            slot = jnp.logical_not(sides[h]) & (place > pics) & (place < pics + 4)
            aug_ref[h, rows, :] = jnp.where(slot, logs, query[h])
        out_ref[rows, :] = jnp.where(sides[0], results[0], results[1]).astype(BF16)


def head_norm_back(e, raw, gain, means):
    raw = raw.astype(F32)
    c = raw - group_sum(raw, means)
    r = lax.rsqrt(group_sum(c * c, means) + EPSILON)
    n = c * r
    t = e * gain
    grad = r * (t - group_sum(t, means) - n * group_sum(t * n, means))
    return grad.astype(BF16), jnp.sum(e * n, axis=0, keepdims=True)


def attend_back_kernel(
    pics, aug_ref, k_ref, v_ref, out_ref, do_ref, rawq_ref, rawk_ref, qg_ref, kg_ref, bounds_ref,
    dq_ref, dk_ref, dv_ref, qgg_ref, kgg_ref, kaug, vaug, doaug, qsum, ksum,
):
    length = k_ref.shape[0]
    queries = do_ref.shape[0]
    part = length // 4
    whole = queries == length
    lane = lax.broadcasted_iota(jnp.int32, (1, 128), 1)
    place = lane % HEAD
    sides = [lane < HEAD, lane >= HEAD]
    kmarks = key_marks(bounds_ref, place, length, pics)
    vmarks = jnp.where(place < 2, 1.0, 0.0).astype(BF16)
    ones = group_ones(1.0)
    inner = group_sum_fine(do_ref[...].astype(F32) * out_ref[...].astype(F32), ones)
    inner = -pltpu.roll(inner, HEAD, 1)
    inner_high = inner.astype(BF16)
    inner_low = (inner - inner_high.astype(F32)).astype(BF16)
    zero = jnp.zeros((), BF16)
    gmarks = jnp.where(place == 0, inner_high, jnp.where(place == 1, inner_low, zero))
    for h in range(2):
        kaug[h] = jnp.where(sides[h], k_ref[...], kmarks)
        vaug[h] = jnp.where(sides[h], v_ref[...], vmarks)
        doaug[h] = jnp.where(sides[h], do_ref[...], gmarks)
    for b in range(length // STEP):
        keys = pl.ds(b * STEP, STEP)
        key = [kaug[h, keys, :] for h in range(2)]
        value = [vaug[h, keys, :] for h in range(2)]
        dk = [jnp.zeros((STEP, 128), F32)] * 2
        dv = [jnp.zeros((STEP, 128), F32)] * 2
        for j in range(queries // STEP):
            rows = pl.ds(j * STEP, STEP)
            query = [aug_ref[h, rows, :] for h in range(2)]
            grad = [doaug[h, rows, :] for h in range(2)]
            scores = [nt(key[h], query[h]) for h in range(2)]
            soft_grad = [nt(value[h], grad[h]) for h in range(2)]
            weights = [jnp.exp2(x * EXP2_FACTOR) for x in scores]
            score_grad = [(weights[h] * soft_grad[h]).astype(BF16) for h in range(2)]
            for h in range(2):
                part_sum = tn(score_grad[h], key[h])
                if b == 0:
                    qsum[h, rows, :] = part_sum
                else:
                    qsum[h, rows, :] += part_sum
                dk[h] = dk[h] + jnp.dot(score_grad[h], query[h], preferred_element_type=F32)
                dv[h] = dv[h] + jnp.dot(weights[h].astype(BF16), grad[h], preferred_element_type=F32)
        ksum[keys, :] = jnp.where(sides[0], dk[0], dk[1]) * HEAD**-0.5
        dv_ref[keys, :] = jnp.where(sides[0], dv[0], dv[1]).astype(BF16)

    means = group_ones(1.0 / HEAD)
    gain_sum = jnp.zeros((1, 128), F32)
    for b in range(queries // part):
        rows = pl.ds(b * part, part)
        e = jnp.where(sides[0], qsum[0, rows, :], qsum[1, rows, :]) * HEAD**-0.5
        raw = own_rows(rawq_ref, b * part, part, queries, part)
        dq_ref[rows, :], more = head_norm_back(e.astype(BF16).astype(F32), raw, qg_ref[...], means)
        gain_sum = gain_sum + more
    qgg_ref[...] = gain_sum
    gain_sum = jnp.zeros((1, 128), F32)
    for b in range(length // part):
        rows = pl.ds(b * part, part)
        e = ksum[rows, :].astype(BF16)
        if whole:
            dk_ref[rows, :], more = head_norm_back(e.astype(F32), rawk_ref[rows, :], kg_ref[...], means)
            gain_sum = gain_sum + more
        else:
            dk_ref[rows, :] = e
    kgg_ref[...] = gain_sum


def shared_keys_kernel(dk_ref, dv_ref, gotk_ref, gotv_ref, rawk_ref, kg_ref, outk_ref, outv_ref, kgg_ref):
    count = outk_ref.shape[0]
    part = count // 2
    means = group_ones(1.0 / HEAD)
    gain_sum = jnp.zeros((1, 128), F32)
    for b in range(2):
        rows = pl.ds(b * part, part)
        own = lambda ref: own_rows(ref, b * part, part, count, part)
        e = own(dk_ref).astype(F32) + gotk_ref[rows, :].astype(F32)
        outk_ref[rows, :], more = head_norm_back(e, own(rawk_ref), kg_ref[...], means)
        gain_sum = gain_sum + more
        outv_ref[rows, :] = (own(dv_ref).astype(F32) + gotv_ref[rows, :].astype(F32)).astype(BF16)
    kgg_ref[...] = gain_sum


def gelu_pair(h):
    size = jnp.abs(h)
    bell = jnp.exp2(h * h * -0.7213475204444817)
    t = 1.0 / (1.0 + 0.23164189 * size)
    series = t * (0.127414796 + t * (-0.142248368 + t * (0.7107068705 + t * (-0.7265760135 + t * 0.5307027145))))
    tail = series * bell
    below = jnp.where(h < 0.0, tail, 1.0 - tail)
    return h * below, below + h * (bell * 0.3989422804014327)


def norm_parts(values):
    center = values - jnp.mean(values, axis=-1, keepdims=True)
    spread = lax.rsqrt(jnp.mean(center * center, axis=-1, keepdims=True) + EPSILON)
    return center * spread, spread


def norm_back(upstream, n, r, gain):
    t = upstream * gain
    grad = r * (t - jnp.mean(t, axis=-1, keepdims=True) - n * jnp.mean(t * n, axis=-1, keepdims=True))
    return grad, jnp.sum(upstream * n, axis=0, keepdims=True)


MESH_ID = pl.DeviceIdType.MESH


def here():
    return lax.axis_index("chip"), lax.axis_index("core"), lax.axis_index("zp"), lax.axis_index("zq")


def remote(source, target, sems, at, device):
    sent, got = sems
    return pltpu.make_async_remote_copy(
        src_ref=source, dst_ref=target, send_sem=sent.at[at], recv_sem=got.at[at],
        device_id=device, device_id_type=MESH_ID,
    )


def greet(devices, maybe=None, moves=None):
    barrier = pltpu.get_barrier_semaphore()
    for device in devices:
        pl.semaphore_signal(barrier, inc=1, device_id=device, device_id_type=MESH_ID)
    if maybe is None:
        pl.semaphore_wait(barrier, len(devices))
        return

    @pl.when(moves)
    def _():
        pl.semaphore_signal(barrier, inc=1, device_id=maybe, device_id_type=MESH_ID)

    pl.semaphore_wait(barrier, len(devices) + jnp.where(moves, 1, 0))


def rows_at(start, count):
    return pl.ds(pl.multiple_of(start, 16), count)


class Moves:
    def __init__(self, moved, stays, crossed, moves):
        self.moved, self.stays, self.crossed, self.moves = moved, stays, crossed, moves

    def each(self, act):
        if self.crossed is not None:
            act(self.crossed)

        @pl.when(self.moves)
        def _():
            for copy in self.moved:
                act(copy)

        @pl.when(jnp.logical_not(self.moves))
        def _():
            for copy in self.stays:
                act(copy)

    def start(self):
        self.each(lambda copy: copy.start())

    def wait(self):
        self.each(lambda copy: copy.wait())


class Across:
    def __init__(self, parts, whole, came, sems, at, waits):
        chip, core, zp, zq = here()
        self.z = 2 * zp + zq
        self.along = [(chip, core, zp, 1 - zq), (chip, core, 1 - zp, zq), (chip, core, 1 - zp, 1 - zq)]
        self.parts, self.whole, self.came = parts, whole, came
        self.sems, self.at, self.waits = sems, at, waits

    def exchange(self, source_of, target_of, at):
        copies = []
        for i in range(3):
            copy = remote(source_of(i), target_of(i), self.sems, self.at + at + i, self.along[i])
            copy.start()
            copies.append(copy)
        self.waits.extend(copies)
        return copies

    def start(self):
        self.first = self.exchange(lambda i: self.parts.at[self.z ^ (i + 1)], lambda i: self.came.at[i], 0)

    def total(self):
        for copy in self.first:
            copy.wait_recv()
        self.whole[self.z] = add(self.parts[self.z], self.came[0], self.came[1], self.came[2]).astype(BF16)
        self.second = self.exchange(lambda i: self.whole.at[self.z], lambda i: self.whole.at[self.z], 3)

    def finish(self):
        for copy in self.second:
            copy.wait_recv()


class PlaneSum:
    def __init__(self, payload, relay, final, came, sems, at, waits):
        self.chip, self.core, zp, zq = here()
        self.payload, self.relay, self.final, self.came = payload, relay, final, came
        self.sems, self.at, self.waits = sems, at, waits
        self.near_x = (self.chip ^ 1, self.core, zp, zq)
        self.near_y = (self.chip ^ 2, self.core, zp, zq)
        self.partner = (self.chip, 1 - self.core, zp, zq)

    def send(self, source, target, at, device):
        copy = remote(source, target, self.sems, self.at + at, device)
        copy.start()
        self.waits.append(copy)
        return copy

    def same(self, hop):
        return 2 * (self.chip ^ hop) + self.core

    def twin(self, hop):
        return 2 * (self.chip ^ hop) + 1 - self.core

    def start(self):
        payload = self.payload
        self.first = self.send(payload.at[self.same(3)], self.relay.at[0], 0, self.near_y)
        self.second = self.send(payload.at[self.twin(3)], self.relay.at[1], 1, self.near_x)
        self.direct_x = self.send(payload.at[self.twin(1)], self.final.at[0], 2, self.near_x)
        self.direct_y = self.send(payload.at[self.same(2)], self.final.at[1], 3, self.near_y)

    def pass_on(self):
        self.first.wait_recv()
        self.relay[2] = add(self.relay[0], self.payload[self.same(1)]).astype(BF16)
        self.onward_x = self.send(self.relay.at[2], self.final.at[2], 4, self.near_x)
        self.second.wait_recv()
        self.relay[3] = add(self.relay[1], self.payload[self.twin(2)]).astype(BF16)
        self.onward_y = self.send(self.relay.at[3], self.final.at[3], 5, self.near_y)

    def to_core(self):
        self.direct_x.wait_recv()
        self.onward_y.wait_recv()
        self.relay[4] = add(self.payload[self.twin(0)], self.final[0], self.final[3]).astype(BF16)
        self.crossing = self.send(self.relay.at[4], self.came, 6, self.partner)

    def finish(self):
        self.direct_y.wait_recv()
        self.onward_x.wait_recv()
        kept = add(self.payload[self.same(0)], self.final[1], self.final[2])
        self.crossing.wait_recv()
        return kept


class Line:
    def __init__(self, parts, whole, right, left, sems, at):
        chip, core, zp, zq = here()
        self.z = 2 * zp + zq
        up, down = jnp.minimum(self.z + 1, 3), jnp.maximum(self.z - 1, 0)
        self.next = (chip, core, up // 2, up % 2)
        self.last = (chip, core, down // 2, down % 2)
        self.parts, self.whole, self.right, self.left = parts, whole, right, left
        self.sems, self.at, self.sends = sems, at, []

    def at_chip(self, z, *acts):
        @pl.when(self.z == z)
        def _():
            for act in acts:
                act()

    def part_copy(self, c, rightward):
        if rightward:
            return remote(self.parts.at[c], self.right.at[3 - c], self.sems, self.at + 3 - c, self.next)
        return remote(self.parts.at[c], self.left.at[c], self.sems, self.at + 3 + c, self.last)

    def whole_copy(self, c, rightward):
        if rightward:
            return remote(self.whole.at[c], self.whole.at[c], self.sems, self.at + 6 + c, self.next)
        return remote(self.whole.at[c], self.whole.at[c], self.sems, self.at + 8 + c, self.last)

    def send(self, z, make, c, rightward):
        self.sends.append((z, make, c, rightward))
        return lambda: make(c, rightward).start()

    def take(self, c, rightward):
        def act():
            self.part_copy(c, rightward).wait_recv()
            came = self.right[3 - c] if rightward else self.left[c]
            self.parts[c] = add(self.parts[c], came).astype(BF16)

        return act

    def got(self, c, rightward):
        return lambda: self.whole_copy(c, rightward).wait_recv()

    def start(self):
        part = self.part_copy
        self.at_chip(0, *[self.send(0, part, c, True) for c in (3, 2, 1)])
        self.at_chip(3, *[self.send(3, part, c, False) for c in (0, 1, 2)])

    def first(self):
        self.at_chip(1, self.take(3, True), self.send(1, self.part_copy, 3, True))
        self.at_chip(2, self.take(0, False), self.send(2, self.part_copy, 0, False))

    def second(self):
        part = self.part_copy
        self.at_chip(
            1, self.take(2, True), self.send(1, part, 2, True), self.take(0, False), self.send(1, part, 0, False)
        )
        self.at_chip(
            2, self.take(1, False), self.send(2, part, 1, False), self.take(3, True), self.send(2, part, 3, True)
        )

    def third(self):
        self.at_chip(0, self.take(0, False))
        self.at_chip(1, self.take(1, True), self.take(1, False))
        self.at_chip(2, self.take(2, True), self.take(2, False))
        self.at_chip(3, self.take(3, True))
        self.whole[self.z] = self.parts[self.z]
        for z in range(4):
            acts = [self.send(z, self.whole_copy, z, True)] if z < 3 else []
            acts += [self.send(z, self.whole_copy, z, False)] if z > 0 else []
            self.at_chip(z, *acts)

    def fourth(self):
        whole = self.whole_copy
        for z in (1, 2):
            self.at_chip(
                z, self.got(z - 1, True), self.send(z, whole, z - 1, True), self.got(z + 1, False),
                self.send(z, whole, z + 1, False),
            )

    def fifth(self):
        whole = self.whole_copy
        self.at_chip(1, self.got(3, False), self.send(1, whole, 3, False))
        self.at_chip(2, self.got(0, True), self.send(2, whole, 0, True))

    def sixth(self):
        self.at_chip(0, *[self.got(c, False) for c in (1, 2, 3)])
        self.at_chip(3, *[self.got(c, True) for c in (2, 1, 0)])

    def wait_sends(self):
        for z in range(4):
            mine = [make(c, rightward) for at, make, c, rightward in self.sends if at == z]
            self.at_chip(z, *[copy.wait_send for copy in mine])


def write_bounds(pics, lens_ref, bounds_ref, zp, zq, length):
    lane = lax.broadcasted_iota(jnp.int32, (8, 128), 1)
    lens = jnp.where(zp == 0, lens_ref[0], lens_ref[1])
    ends = lens
    for hop in (1, 2, 4, 8):
        ends = ends + jnp.where(lane >= hop, pltpu.roll(ends, hop, 1), 0)
    starts = ends - lens
    last = (lens > 0) & (pltpu.roll(lens, 127, 1) == 0)
    query_ends = jnp.where(last, length, ends)
    total = jnp.max(jnp.where(lane < pics, ends, 0), axis=1, keepdims=True)

    def both(values):
        values = jnp.where(lane < HEAD, jnp.where(lane < pics, values, 2 * length), 0)
        return values + pltpu.roll(values, HEAD, 1)

    tables = [both(starts), both(ends), both(query_ends), jnp.broadcast_to(total, (8, 128))]
    for t in range(4):
        table = tables[t]
        bounds_ref[0, t : t + 1, :] = jnp.where(zq == 0, table[0:1], table[1:2])
        bounds_ref[1, t : t + 1, :] = table[2:3]
    bounds_ref[:, 4:, :] = jnp.zeros((2, 4, 128), jnp.int32)


def forward_kernel(square, pics, *refs):
    refs = list(refs)
    take = lambda count: [refs.pop(0) for _ in range(count)]
    tokens_ref, cot_ref, lengths_ref, weight_in = take(4)
    if square:
        gain_in = take(4)
        up_in, outw_ref = take(2)
    else:
        gain_first_in, gain_qk_in = take(2)
    x_out, bounds_ref, mix_hbm, cot_hbm, gain_first, second_ref, gain_qk = take(7)
    names = ("normed", "qk", "v", "raw", "out", "aug")
    outs = [dict(zip(names, take(6))) for _ in range(2)]
    if square:
        up_hbm, outw_hbm = take(2)
    row_ref, shared_ref, cot_out, lens_ref, lens_out = take(5)
    scratch = [dict(zip(names, take(6))) for _ in range(2)]
    kaug, vaug, qaug = take(3)
    if square:
        mix_ref, gains_ref, up_ref, mix_out, gains_out, up_out, outw_out = take(7)
    sent, got, local_sem, write_sem = take(4)

    chip, core, zp, zq = here()
    z = 2 * zp + zq
    part = tokens_ref.shape[1]
    half, length = 2 * part, 4 * part
    sems = (sent, got)
    partner = (chip, 1 - core, zp, zq)
    side = (chip, core, zp, 1 - zq)
    keep = (chip, zp, core, zq)
    cross = (chip, zp, core, 1 - zq)
    moves = core != zp
    near_x = (chip ^ 1, core, zp, zq)
    near_y = (chip ^ 2, core, zp, zq)
    greet([partner, side, cross] + ([near_x, near_y] if square else []), keep, moves)

    def quarter(ref, index):
        return ref.at[rows_at(index * part, part)]

    own_row = remote(tokens_ref.at[zq], quarter(row_ref, z), sems, 0, keep)
    own_shared = remote(tokens_ref.at[2], quarter(shared_ref, z), sems, 2, keep)
    stay_row = pltpu.make_async_copy(tokens_ref.at[zq], quarter(row_ref, z), local_sem.at[0])
    stay_shared = pltpu.make_async_copy(tokens_ref.at[2], quarter(shared_ref, z), local_sem.at[1])

    @pl.when(moves)
    def _():
        own_row.start()

    @pl.when(jnp.logical_not(moves))
    def _():
        stay_row.start()

    cross_row = remote(tokens_ref.at[1 - zq], quarter(row_ref, z), sems, 1, cross)
    cross_row.start()

    @pl.when(moves)
    def _():
        own_shared.start()

    @pl.when(jnp.logical_not(moves))
    def _():
        stay_shared.start()

    lens_ref[...] = jnp.zeros_like(lens_ref)
    lens_ref[: lengths_ref.shape[0], :pics] = lengths_ref[...]
    lens_copy = remote(lens_ref, lens_out.at[core], sems, 8, partner)
    lens_copy.start()
    lens_stay = pltpu.make_async_copy(lens_ref, lens_out.at[core], local_sem.at[2])
    lens_stay.start()
    waits = []
    if square:
        shard = mix_ref.shape[1]
        tile = up_ref.shape[2] // 4
        width = mix_ref.shape[2] // 3
        for h in range(2):
            for i in range(3):
                mix_ref[h, :, i * width : (i + 1) * width] = weight_in[:, (2 * i + h) * width : (2 * i + h + 1) * width]
        gains_ref[...] = jnp.zeros_like(gains_ref)
        for i in range(4):
            gains_ref[i : i + 1, :shard] = gain_in[i][...].astype(F32)
        mine, theirs = 2 * chip + core, 2 * chip + 1 - core
        slot = [9]

        def send(source, target, device):
            copy = remote(source, target, sems, slot[0], device)
            slot[0] += 1
            copy.start()
            waits.append(copy)
            return copy

        def stay(source, target, at):
            copy = pltpu.make_async_copy(source, target, local_sem.at[at])
            copy.start()
            return copy

        def block(ref, start, count):
            return ref.at[rows_at(start, count)]

        mix_piece = lambda index: (block(mix_out, index * shard, shard), gains_out.at[index])

        def send_mix(sources, index, device):
            return [send(source, target, device) for source, target in zip(sources, mix_piece(index))]

        def arrived(copies):
            for copy in copies:
                copy.wait_recv()

        x_mine, y_other = 2 * (chip ^ 1) + core, 2 * (chip ^ 2) + 1 - core
        to_core = send_mix((mix_ref.at[1 - core], gains_ref), mine, partner)
        a_x = send_mix((mix_ref.at[core], gains_ref), mine, near_x)
        a_y = send_mix((mix_ref.at[core], gains_ref), mine, near_y)
        for h in range(2):
            for i in range(4):
                up_ref[h, :, i * tile : (i + 1) * tile] = up_in[:, (2 * i + h) * tile : (2 * i + h + 1) * tile]
        up_core = send(up_ref.at[1 - core], block(up_out, mine * shard, shard), partner)
        out_core = send(outw_ref, block(outw_out, mine * shard, shard), partner)
        stays = [
            stay(mix_ref.at[core], mix_piece(mine)[0], 3),
            stay(gains_ref, gains_out.at[mine], 4),
            stay(up_ref.at[core], block(up_out, mine * shard, shard), 5),
            stay(outw_ref, block(outw_out, mine * shard, shard), 6),
        ]
        arrived(to_core)
        b_x = send_mix(mix_piece(theirs), theirs, near_x)
        b_y = send_mix(mix_piece(theirs), theirs, near_y)
        arrived(a_x)
        a_far = send_mix(mix_piece(x_mine), x_mine, near_y)
        arrived(b_y)
        b_far = send_mix(mix_piece(y_other), y_other, near_x)
        for copy in stays:
            copy.wait()
        arrived([up_core])
        ohalf = shard // 2

        def bundle(first, from_chip):
            same, twin = 2 * from_chip + core, 2 * from_chip + 1 - core
            part_of = 0 if first else 1
            return [
                block(up_out, (same if first else twin) * shard, shard),
                block(outw_out, same * shard + part_of * ohalf, ohalf),
            ]

        def send_bundle(first, from_chip, device):
            return [send(ref, ref, device) for ref in bundle(first, from_chip)]

        first_x = send_bundle(True, chip, near_x)
        first_y = send_bundle(True, chip, near_y)
        second_x = send_bundle(False, chip, near_x)
        second_y = send_bundle(False, chip, near_y)

    lens_copy.wait()
    lens_stay.wait()
    write_bounds(pics, lens_out, bounds_ref, zp, zq, length)
    if square:
        arrived(a_y + b_x + a_far + b_far)
        for p in range(gains_out.shape[0]):
            lanes = slice(p * shard, (p + 1) * shard)
            values = gains_out[p, :, :shard]
            gain_first[:, lanes] = values[0:1]
            second_ref[:, lanes] = values[3:4]
            half_pieces = gains_out.shape[0] // 2

            @pl.when(core == p // half_pieces)
            def _():
                at = (p % half_pieces) * shard
                gain_qk[:, at : at + shard] = values[1:2]
                gain_qk[:, width + at : width + at + shard] = values[2:3]
        weight = mix_out
    else:
        weight = weight_in
        width = weight.shape[1] // 3
        second_ref[...] = jnp.zeros_like(second_ref)
        gain_first[...] = gain_first_in[...]
        gain_qk[...] = gain_qk_in[...]
    writes = []

    def write(source, target, at):
        copy = pltpu.make_async_copy(source, target, write_sem.at[at])
        copy.start()
        writes.append(copy)

    write(weight, mix_hbm, 0)
    first, second = 2 * core + zq, 2 * core + 1 - zq
    other_first, other_second = 2 * (1 - core) + zq, 2 * (1 - core) + 1 - zq

    def forwarded(ref, index, at):
        return remote(quarter(ref, index), quarter(ref, index), sems, at, partner)

    def project(tokens, bufs, at):
        rows = rows_at(at * part, part)
        project_kernel(
            tokens.at[rows], gain_first, weight, gain_qk, bufs["normed"].at[rows], bufs["qk"].at[rows],
            bufs["v"].at[rows], bufs["raw"].at[rows],
        )

    def project_row(i, _):
        @pl.when(i == 0)
        def _():
            @pl.when(moves)
            def _():
                own_row.wait_recv()

            @pl.when(jnp.logical_not(moves))
            def _():
                stay_row.wait()

            forwarded(row_ref, first, 3).start()

        @pl.when(i == 1)
        def _():
            cross_row.wait_recv()
            forwarded(row_ref, second, 4).start()

        @pl.when(i == 2)
        def _():
            forwarded(row_ref, other_first, 3).wait_recv()

        @pl.when(i == 3)
        def _():
            forwarded(row_ref, other_second, 4).wait_recv()

        order = jnp.where(i == 0, first, jnp.where(i == 1, second, jnp.where(i == 2, other_first, other_second)))
        project(row_ref, scratch[0], order)
        return 0

    row_one, row_two = forwarded(row_ref, first, 3), forwarded(row_ref, second, 4)

    def attend(bufs, bounds):
        def one(p, _):
            lanes = pl.ds(pl.multiple_of(p * 128, 128), 128)
            attend_kernel(
                pics, bufs["qk"].at[:, lanes],
                bufs["qk"].at[:, pl.ds(pl.multiple_of(width + p * 128, 128), 128)], bufs["v"].at[:, lanes], bounds,
                bufs["out"].at[:, lanes], bufs["aug"].at[pl.ds(2 * p, 2)], kaug, vaug, qaug.at[pl.ds(0, bufs["out"].shape[0])],
            )
            return 0

        lax.fori_loop(0, width // 128, one, 0)

    lax.fori_loop(0, 4, project_row, 0)
    for i, name in enumerate(("normed", "qk", "v", "raw")):
        write(scratch[0][name], outs[0][name], 1 + i)
    write(row_ref.at[rows_at(core * half, half)], x_out.at[pl.ds(0, half)], 5)

    @pl.when(moves)
    def _():
        own_shared.wait_recv()

    @pl.when(jnp.logical_not(moves))
    def _():
        stay_shared.wait()

    to_side = remote(quarter(shared_ref, first), quarter(shared_ref, first), sems, 5, side)
    to_side.start()
    shared_one = remote(quarter(shared_ref, first), quarter(shared_ref, first), sems, 6, partner)
    shared_one.start()
    attend(scratch[0], bounds_ref.at[0])
    cot_moves = Moves(
        [remote(cot_ref.at[zq], cot_out, sems, 43, keep)],
        [pltpu.make_async_copy(cot_ref.at[zq], cot_out, local_sem.at[0])],
        None,
        moves,
    )
    cot_moves.start()
    write(scratch[0]["out"], outs[0]["out"], 6)
    write(scratch[0]["aug"], outs[0]["aug"], 7)
    to_side.wait_recv()
    shared_two = forwarded(shared_ref, second, 7)
    shared_two.start()
    if square:
        arrived(first_x + second_y)
        far_first = send_bundle(True, chip ^ 1, near_y)
        far_second = send_bundle(False, chip ^ 2, near_x)
    shared_one.wait_recv()
    shared_two.wait_recv()

    def project_shared(i, _):
        project(shared_ref, scratch[1], i)
        return 0

    lax.fori_loop(0, 4, project_shared, 0)
    for i, name in enumerate(("normed", "qk", "v", "raw")):
        write(scratch[1][name], outs[1][name], 8 + i)
    write(shared_ref.at[rows_at(first * part, part)], x_out.at[pl.ds(half, part)], 12)
    attend(scratch[1], bounds_ref.at[1])
    write(scratch[1]["out"], outs[1]["out"], 13)
    write(scratch[1]["aug"], outs[1]["aug"], 14)

    if square:
        arrived(first_y + second_x + far_first + far_second)
        sent_pieces = []
        for c in (chip ^ 1, chip ^ 2, chip ^ 3):
            target = block(outw_out, (2 * c + core) * shard, shard)
            sent_pieces.append(send(target, target, partner))
        write(up_out, up_hbm, 15)
        arrived(sent_pieces + [out_core])
        write(outw_out, outw_hbm, 17)
        for copy in waits:
            copy.wait_send()
    cot_moves.wait()
    write(cot_out, cot_hbm, 18)
    for copy in (row_one, row_two, shared_one, shared_two, to_side, cross_row):
        copy.wait_send()

    @pl.when(moves)
    def _():
        own_row.wait_send()
        own_shared.wait_send()

    for copy in writes:
        copy.wait()


def forward_pass(square, pics, tokens, cotangent, lengths, weight, *more):
    _, part, model = tokens.shape
    length, half, width = 4 * part, 2 * part, model // 2
    near = pl.BlockSpec(memory_space=pltpu.VMEM)
    anywhere = pl.BlockSpec(memory_space=pl.ANY)
    low = lambda *shape: (shape, BF16)
    wide = lambda *shape: (shape, F32)
    outs = [
        (low(3 * part, model), anywhere),
        (((2, 8, 128), jnp.int32), near),
        (low(model, 3 * width), anywhere),
        (low(part, model), anywhere),
        (wide(1, model), near),
        (wide(1, model), near),
        (wide(1, model), near),
    ]
    bufs = []
    for queries in (length, half):
        shapes = [
            low(length, model), low(length, 2 * width), low(length, width), low(length, 2 * width),
            low(queries, width), low(2 * (width // 128), queries, 128),
        ]
        outs += [(shape, anywhere) for shape in shapes]
        bufs += shapes
    table = ((8, 128), jnp.int32)
    scratch = [low(length, model), low(length, model), low(part, model), table, ((2, 8, 128), jnp.int32)] + bufs
    scratch += [low(2, length, 128), low(2, length, 128), low(length, 128)]
    if square:
        up, _ = more[4:]
        shard, hidden = up.shape
        landed = [low(model, hidden // 2), low(model, model)]
        outs += [(shape, anywhere) for shape in landed]
        scratch += [low(2, shard, 3 * width), wide(8, 128), low(2, shard, hidden // 2)]
        scratch += [low(model, 3 * width), wide(8, 8, 128)] + landed
    return pl.pallas_call(
        functools.partial(forward_kernel, square, pics),
        in_specs=[near] * (4 + len(more)),
        out_specs=[spec for _, spec in outs],
        out_shape=[jax.ShapeDtypeStruct(*shape) for shape, _ in outs],
        scratch_shapes=[pltpu.VMEM(*shape) for shape in scratch]
        + [
            pltpu.SemaphoreType.DMA((49,)),
            pltpu.SemaphoreType.DMA((49,)),
            pltpu.SemaphoreType.DMA((8,)),
            pltpu.SemaphoreType.DMA((19,)),
        ],
        compiler_params=pltpu.CompilerParams(
            collective_id=0, has_side_effects=True, vmem_limit_bytes=60 * 1024 * 1024
        ),
        name="forward_pass",
    )(tokens, cotangent, lengths, weight, *more)


def dense_kernel(
    square, out_ref, shared_ref, x, grad_ref, cot_ref, outw_ref, gain_ref, bounds_ref, up_ref, down_ref,
    output_ref, third_ref, midg_ref, row_grad, shared_grad, outg_ref, gaing_ref, packed_ref, far_ref,
    att_other, second, turned, grad, cot_in, hidden_all, pre_all, forward, backward, middle, up, down,
    results, parts_out, parts_in, heads_out, cols_out, cols_in, stage, far_in,
    sent, got, load_sem, write_sem, local_sem,
):
    chip, core, zp, zq = here()
    sems = (sent, got)
    partner = (chip, 1 - core, zp, zq)
    keep = (chip, zp, core, zq)
    cross = (chip, zp, core, 1 - zq)
    moves = core != zp
    near_x = (chip ^ 1, core, zp, zq)
    near_y = (chip ^ 2, core, zp, zq)
    tokens, model = midg_ref.shape
    part = tokens // 3
    half = 2 * part
    width = out_ref.shape[1]
    units = up.shape[1]
    tile = units // 4
    other = 1 - core
    mine, theirs = pl.ds(0, tokens), pl.ds(tokens, tokens)
    own_down = down.at[rows_at(chip * tile, tile)] if square else down
    loads = [
        pltpu.make_async_copy(up_ref, up, load_sem.at[0]),
        pltpu.make_async_copy(down_ref, own_down, load_sem.at[1]),
    ]
    for copy in loads:
        copy.start()
    greet([partner, cross] + ([near_x, near_y] if square else []), keep, moves)
    att_sends = [
        remote(out_ref.at[rows_at(other * half, half)], att_other.at[pl.ds(0, half)], sems, 0, partner),
        remote(shared_ref.at[rows_at(other * part, part)], att_other.at[pl.ds(half, part)], sems, 1, partner),
    ]
    for copy in att_sends:
        copy.start()
    cot_move = Moves(
        [remote(cot_ref.at[2], cot_in.at[1], sems, 11, keep)],
        [pltpu.make_async_copy(cot_ref.at[2], cot_in.at[1], local_sem.at[0])],
        remote(cot_ref.at[1 - zq], cot_in.at[0], sems, 22, cross),
        moves,
    )
    cot_move.start()

    def down_half(index, which):
        return down.at[rows_at(index * tile + which * (tile // 2), tile // 2)]

    def send_down(index, which, at, device):
        copy = remote(down_half(index, which), down_half(index, which), sems, at, device)
        copy.start()
        return copy

    slot = lax.broadcasted_iota(jnp.int32, (part, 1), 0)
    filled, shared_filled = bounds_ref[0, 3:4, 0:1], bounds_ref[1, 3:4, 0:1]
    none = jnp.zeros((), BF16)

    def take_grad(values, at, start, limit, sem):
        rows = rows_at(at, part)
        grad[rows, :] = jnp.where(slot + start < limit, values, none)
        copy = remote(grad.at[rows], grad.at[rows_at(tokens + at, part)], sems, sem, partner)
        copy.start()
        return copy

    grad_sends = [take_grad(grad_ref[...], zq * part, (2 * core + zq) * part, filled, 2)]

    own_rows_of = lambda b: (
        out_ref[rows_at(core * half + b * part, part), :] if b < 2 else shared_ref[rows_at(core * part, part), :]
    )
    own_weight = outw_ref[rows_at(core * width, width), :]
    other_weight = outw_ref[rows_at(other * width, width), :]
    blocks = [pl.ds(b * part, part) for b in range(3)]
    for b in range(3):
        middle[blocks[b], :] = x[blocks[b], :].astype(F32) + jnp.dot(
            own_rows_of(b), own_weight, preferred_element_type=F32
        )
    for copy in loads:
        copy.wait()
    if square:
        down_sends = [
            send_down(chip, 0, 12, near_x), send_down(chip, 1, 13, near_y), send_down(chip, 0, 14, near_y),
            send_down(chip, 1, 15, near_x),
        ]
    for copy in att_sends:
        copy.wait_recv()
    for rows in blocks:
        value = middle[rows, :] + jnp.dot(att_other[rows, :], other_weight, preferred_element_type=F32)
        middle[rows, :] = value
        second[rows, :] = (norm_parts(value)[0] * gain_ref[...]).astype(BF16)
    second_send = remote(second.at[mine], second.at[theirs], sems, 3, partner)
    second_send.start()

    def hidden_forward(start):
        rows = pl.ds(start, tokens)

        def one_tile(i, _):
            here_units = pl.ds(pl.multiple_of(i * tile, 128), tile)
            hidden, slope = gelu_pair(jnp.dot(second[rows, :], up[:, here_units], preferred_element_type=F32))
            hidden_all[rows, here_units] = hidden.astype(BF16)
            pre_all[rows, here_units] = slope.astype(BF16)
            return 0

        lax.fori_loop(0, 4, one_tile, 0)

    def hidden_backward(start):
        rows = pl.ds(start, tokens)

        def one_tile(i, _):
            here_units = pl.ds(pl.multiple_of(i * tile, 128), tile)
            pre_grad = nt(grad[rows, :], down[rows_at(i * tile, tile), :]) * pre_all[rows, here_units].astype(F32)
            pre_all[rows, here_units] = pre_grad.astype(BF16)
            return 0

        lax.fori_loop(0, 4, one_tile, 0)

    hidden_forward(0)
    if square:
        down_sends[0].wait_recv()
        down_sends[1].wait_recv()
        down_sends += [send_down(chip ^ 1, 0, 16, near_y), send_down(chip ^ 2, 1, 17, near_x)]
    second_send.wait_recv()
    hidden_forward(tokens)
    if square:
        for copy in down_sends[2:]:
            copy.wait_recv()
    for b in range(3):
        rows, there = pl.ds(tokens + b * part, part), blocks[b]
        parts_out[0, there, :] = jnp.dot(hidden_all[rows, :], down[...], preferred_element_type=F32).astype(BF16)
    first_part = remote(parts_out.at[0], parts_in.at[0], sems, 4, partner)
    first_part.start()
    for rows in blocks:
        forward[rows, :] = middle[rows, :] + jnp.dot(hidden_all[rows, :], down[...], preferred_element_type=F32)
    first_part.wait_recv()
    for rows in blocks:
        results[rows, :] = (forward[rows, :] + parts_in[0, rows, :].astype(F32)).astype(BF16)
    kept_rows = results.at[rows_at(zq * part, part)]
    output_moves = Moves(
        [remote(kept_rows, output_ref.at[zq], sems, 19, keep)],
        [pltpu.make_async_copy(kept_rows, output_ref.at[zq], local_sem.at[1])],
        remote(results.at[rows_at((1 - zq) * part, part)], output_ref.at[zq], sems, 21, cross),
        moves,
    )
    third_ref[...] = results[pl.ds(half, part), :]
    output_moves.start()
    cot_move.wait()
    grad_sends.append(take_grad(cot_in[0], (1 - zq) * part, (2 * core + 1 - zq) * part, filled, 18))
    grad_sends.append(take_grad(cot_in[1], half, (2 * core + zq) * part, shared_filled, 23))
    hidden_backward(0)
    for copy in grad_sends:
        copy.wait_recv()
    hidden_backward(tokens)
    for b in range(3):
        rows, there = pl.ds(tokens + b * part, part), blocks[b]
        parts_out[1, there, :] = nt(pre_all[rows, :], up[...]).astype(BF16)
    second_part = remote(parts_out.at[1], parts_in.at[1], sems, 5, partner)
    second_part.start()
    for rows in blocks:
        backward[rows, :] = nt(pre_all[rows, :], up[...])

    turned[...] = second[...].T
    quarter = model // 4
    far_sends = [
        remote(stage.at[0, pl.ds(0, tile)], far_in.at[0], sems, 9, near_y),
        remote(stage.at[0, pl.ds(tile, tile)], far_in.at[1], sems, 10, near_x),
    ]

    def weight_grads(i, _):
        target = chip ^ (3 - i) if square else 3 - i
        place = jnp.where(i == 0, 0, 1 + i % 2)

        @pl.when(i == 3)
        def _():
            pltpu.make_async_copy(stage.at[place], packed_ref.at[target], write_sem.at[place]).wait()

        here_units = pl.ds(pl.multiple_of(target * tile, 128), tile)
        stage[place, pl.ds(0, tile), :] = tn(hidden_all[:, here_units], grad[...]).astype(BF16)
        values = jnp.dot(
            turned[rows_at(target * quarter, quarter), :], pre_all[...], preferred_element_type=F32
        ).astype(BF16)
        for j in range(2):
            stage[place, pl.ds(tile + j * quarter, quarter), :] = values[:, j * model : (j + 1) * model]
        pltpu.make_async_copy(stage.at[place], packed_ref.at[target], write_sem.at[place]).start()
        if square:

            @pl.when(i == 0)
            def _():
                for copy in far_sends:
                    copy.start()

        return 0

    lax.fori_loop(0, 4, weight_grads, 0)

    second_send.wait_send()
    second_part.wait_recv()
    gain_sum = jnp.zeros(gaing_ref.shape, F32)
    for rows in blocks:
        n, r = norm_parts(middle[rows, :])
        upstream = backward[rows, :] + parts_in[1, rows, :].astype(F32)
        more, gain_more = norm_back(upstream, n, r, gain_ref[...])
        gain_sum = gain_sum + gain_more
        value = grad[rows, :].astype(F32) + more
        midg_ref[rows, :] = value
        branch = value.astype(BF16)
        second[rows, :] = branch
        heads_out[rows, :] = nt(branch, other_weight).astype(BF16)
    gaing_ref[...] = gain_sum
    head_sends = [
        remote(heads_out.at[pl.ds(0, half)], row_grad.at[rows_at(core * half, half)], sems, 6, partner),
        remote(heads_out.at[pl.ds(half, part)], shared_grad.at[rows_at(core * part, part)], sems, 7, partner),
    ]
    for copy in head_sends:
        copy.start()
    branch = second[mine, :]
    forward[rows_at(core * width, width), :] = tn(
        out_ref[rows_at(core * half, half), :], second[pl.ds(0, half), :]
    ) + tn(shared_ref[rows_at(core * part, part), :], second[pl.ds(half, part), :])
    forward[rows_at(other * width, width), :] = tn(att_other[...], branch)
    lanes = lambda side: pl.ds(pl.multiple_of(side * width, 128), width)
    cols_out[...] = forward[pl.ds(0, model), lanes(other)].astype(BF16)
    cols_send = remote(cols_out, cols_in, sems, 8, partner)
    cols_send.start()
    for b in range(3):
        value = nt(second[blocks[b], :], own_weight).astype(BF16)
        if b < 2:
            row_grad[rows_at(core * half + b * part, part), :] = value
        else:
            shared_grad[rows_at(core * part, part), :] = value
    cols_send.wait_recv()
    outg_ref[...] = (forward[pl.ds(0, model), lanes(core)] + cols_in[...].astype(F32)).astype(BF16)
    for copy in head_sends:
        copy.wait_recv()
    for copy in att_sends + head_sends + grad_sends + [first_part, second_part, cols_send]:
        copy.wait_send()
    if square:
        for copy in down_sends:
            copy.wait_send()
        for copy in far_sends:
            copy.wait()
    far_write = pltpu.make_async_copy(far_in, far_ref, load_sem.at[0])
    far_write.start()
    for place in range(3):
        pltpu.make_async_copy(stage.at[place], packed_ref.at[0], write_sem.at[place]).wait()
    output_moves.wait()
    far_write.wait()


def dense(square, out, shared_out, x, grad, cotangent, out_matrix, gain, bounds, up, down):
    model = x.shape[1]
    tokens = x.shape[0]
    part = tokens // 3
    length, width = out.shape
    units = up.shape[1]
    tile = units // 4
    anywhere = pl.BlockSpec(memory_space=pl.ANY)
    near = pl.BlockSpec(memory_space=pltpu.VMEM)
    both = 2 * tokens
    low = lambda *shape: pltpu.VMEM(shape, BF16)
    wide = lambda *shape: pltpu.VMEM(shape, F32)
    return pl.pallas_call(
        functools.partial(dense_kernel, square),
        in_specs=[near] * 4 + [anywhere] + [near] * 3 + [anywhere] * 2,
        out_specs=[anywhere] + [near] * 6 + [anywhere, anywhere],
        out_shape=[
            jax.ShapeDtypeStruct((2, part, model), BF16),
            jax.ShapeDtypeStruct((part, model), BF16),
            jax.ShapeDtypeStruct((tokens, model), F32),
            jax.ShapeDtypeStruct((length, width), BF16),
            jax.ShapeDtypeStruct((length // 2, width), BF16),
            jax.ShapeDtypeStruct((model, width), BF16),
            jax.ShapeDtypeStruct((1, model), F32),
            jax.ShapeDtypeStruct((4, 2 * tile, model), BF16),
            jax.ShapeDtypeStruct((2, tile, model), BF16),
        ],
        scratch_shapes=[
            low(tokens, width), low(both, model), low(model, both), low(both, model), low(2, part, model),
            low(both, units), low(both, units), wide(tokens, model), wide(tokens, model), wide(tokens, model),
            low(model, units), low(units, model), low(tokens, model), low(2, tokens, model), low(2, tokens, model),
            low(tokens, width), low(model, width), low(model, width), low(3, 2 * tile, model), low(2, tile, model),
            pltpu.SemaphoreType.DMA((24,)),
            pltpu.SemaphoreType.DMA((24,)),
            pltpu.SemaphoreType.DMA((2,)),
            pltpu.SemaphoreType.DMA((3,)),
            pltpu.SemaphoreType.DMA((3,)),
        ],
        compiler_params=pltpu.CompilerParams(
            collective_id=1, has_side_effects=True, vmem_limit_bytes=63 * 1024 * 1024
        ),
        name="dense",
    )(out, shared_out, x, grad, cotangent, out_matrix, gain, bounds, up, down)


def add(*terms):
    total = terms[0].astype(F32)
    for term in terms[1:]:
        total = total + term.astype(F32)
    return total


def backward_kernel(square, pics, *refs):
    refs = list(refs)
    take = lambda count: [refs.pop(0) for _ in range(count)]
    names = ("aug", "qk", "v", "out", "do", "raw", "normed")
    row_in = dict(zip(names, take(7)))
    shared_in = dict(zip(names, take(7)))
    mix_in, x_in, midg_in, gain_first, gain_qk, gain_second_grad, bounds_ref = take(7)
    third_in = take(1)[0]
    if square:
        packed_in, far_ref, outg_in = take(3)
        third_out, grad_out, total_ref, gains_ref, up_ref, down_ref, outw_ref = take(7)
    else:
        third_out, grad_own, mix_grad_ref, gains_sum = take(4)
    names = names[:-1]
    row = dict(zip(names, take(6)))
    shared = dict(zip(names, take(6)))
    normed, turned, weight, x, midg = take(5)
    kaug, vaug, doaug, qsum, ksum, mixed, part_k, part_v, got_k, got_v = take(10)
    gain_sums, parts_in = take(2)
    if square:
        gains_sum, outg = take(2)
        held, far_in, onward_in, direct_in, line, whole_line, line_right, line_left = take(8)
        up_out, up_got = take(2)
        planes = [take(4) for _ in range(3)]
        lines = [take(4), take(3)]
        gain_part, gain_got = take(2)
    sent, got, load_sem, local_sem = take(4)

    chip, core, zp, zq = here()
    z = 2 * zp + zq
    sems = (sent, got)
    partner = (chip, 1 - core, zp, zq)
    keep = (chip, zp, core, zq)
    cross = (chip, zp, core, 1 - zq)
    moves = core != zp
    near_x = (chip ^ 1, core, zp, zq)
    near_y = (chip ^ 2, core, zp, zq)
    along = [(chip, core, zp, 1 - zq), (chip, core, 1 - zp, zq), (chip, core, 1 - zp, 1 - zq)]
    tokens, model = x.shape
    part = tokens // 3
    half, length = 2 * part, 4 * part
    width = model // 2
    queries = half
    waits = []

    def load(source, target, at):
        copy = pltpu.make_async_copy(source, target, load_sem.at[at])
        copy.start()
        return copy

    def send(source, target, at, device):
        copy = remote(source, target, sems, at, device)
        copy.start()
        waits.append(copy)
        return copy

    if square:
        rows_count = packed_in.shape[1]
        span = rows_count // 2
        first_half, second_half = pl.ds(0, span), pl.ds(span, span)
        held_loads = [
            load(packed_in.at[chip ^ 1, first_half], held.at[0], 24),
            load(packed_in.at[chip ^ 2, second_half], held.at[1], 25),
            load(packed_in.at[chip, first_half], held.at[2], 26),
            load(packed_in.at[chip, second_half], held.at[3], 27),
        ]
        far_loads = [load(far_ref.at[i], far_in.at[i], 28 + i) for i in range(2)]
    keys_of = lambda ref: ref.at[:, pl.ds(width, width)]
    load_bufs = lambda source, target, at: [
        load(keys_of(source[name]) if name == "qk" else source[name], target[name], at + i)
        for i, name in enumerate(names)
    ]
    shared_loads = load_bufs(shared_in, shared, 0)
    row_loads = load_bufs(row_in, row, 6)
    late_loads = [
        load(row_in["normed"], normed.at[pl.ds(0, length)], 12),
        load(shared_in["normed"].at[rows_at(zq * part, part)], normed.at[pl.ds(length, part)], 13),
        load(
            shared_in["normed"].at[rows_at((2 + zq) * part, part)], normed.at[pl.ds(length + part, part)], 14
        ),
        load(mix_in, weight, 15),
        load(x_in, x, 16),
        load(midg_in, midg, 17),
    ]
    if square:
        late_loads.append(load(outg_in, outg, 18))
    if square:
        greet([partner, cross, near_x, near_y] + along, keep, moves)
        for copy in held_loads + far_loads:
            copy.wait()
        far_in[0] = add(far_in[0], held[0]).astype(BF16)
        bulk_on_x = send(far_in.at[0], onward_in.at[0], 11, near_x)
        far_in[1] = add(far_in[1], held[1]).astype(BF16)
        bulk_on_y = send(far_in.at[1], onward_in.at[1], 12, near_y)
        bulk_x = send(packed_in.at[chip ^ 1, second_half], direct_in.at[0], 2, near_x)
        bulk_y = send(packed_in.at[chip ^ 2, first_half], direct_in.at[1], 3, near_y)

        bulk_line = Line(line, whole_line, line_right, line_left, sems, 14)
        plane_a, plane_b, plane_gains = (
            PlaneSum(*refs_of, sems, 26 + 7 * i, waits) for i, refs_of in enumerate(planes)
        )
        line_a = Line(*lines[0], sems, 47)
        across_b = Across(*lines[1], sems, 59, waits)
    else:
        greet([partner, along[0]], keep, moves)
    third_moves = Moves(
        [remote(third_in, third_out, sems, 5, keep)],
        [pltpu.make_async_copy(third_in, third_out, local_sem.at[2])],
        None,
        moves,
    )
    third_moves.start()

    gain_sums[...] = jnp.zeros_like(gain_sums)

    pairs = width // 128

    def attend_back(bufs, bounds, count, q_lanes_to, k_to, v_to, at, span=(0, pairs)):
        def one(p, _):
            lanes = pl.ds(pl.multiple_of(p * 128, 128), 128)
            key_lanes = pl.ds(pl.multiple_of(width + p * 128, 128), 128)
            attend_back_kernel(
                pics, bufs["aug"].at[pl.ds(2 * p, 2)], bufs["qk"].at[:, lanes], bufs["v"].at[:, lanes],
                bufs["out"].at[:, lanes], bufs["do"].at[:, lanes], bufs["raw"].at[:, lanes],
                bufs["raw"].at[:, key_lanes], gain_qk.at[:, lanes], gain_qk.at[:, key_lanes], bounds,
                q_lanes_to(p), k_to(p), v_to(p), gain_sums.at[pl.ds(at, 1), lanes], gain_sums.at[pl.ds(at + 1, 1), lanes],
                kaug, vaug, doaug.at[:, pl.ds(0, count)], qsum.at[:, pl.ds(0, count)], ksum,
            )
            return 0

        lax.fori_loop(span[0], span[1], one, 0)

    def mixed_at(start, count, side):
        return lambda p: mixed.at[pl.ds(start, count), pl.ds(pl.multiple_of(side * width + p * 128, 128), 128)]

    whole_lanes = lambda ref: lambda p: ref.at[:, pl.ds(pl.multiple_of(p * 128, 128), 128)]
    for copy in shared_loads:
        copy.wait()
    attend_back(
        shared, bounds_ref.at[1], queries, mixed_at(length, queries, 0), whole_lanes(part_k), whole_lanes(part_v), 0
    )
    side_sends = []
    for i in range(2):
        theirs = rows_at((2 * i + 1 - zq) * part, part)
        there = pl.ds(i * part, part)
        side_sends.append(send(part_k.at[theirs], got_k.at[there], 7 + 2 * i, along[0]))
        side_sends.append(send(part_v.at[theirs], got_v.at[there], 8 + 2 * i, along[0]))
    for copy in row_loads + late_loads:
        copy.wait()
    turned[...] = normed[...].T
    parts_out = normed.at[pl.ds(0, tokens)]
    if square:
        grad_own = normed.at[pl.ds(tokens, tokens)]
    shard = model // 8
    other = 1 - core
    row_to = (mixed_at(0, length, 0), mixed_at(0, length, 1), mixed_at(0, length, 2), 2)
    attend_back(row, bounds_ref.at[0], length, *row_to, (0, pairs - 1))
    if square:
        quarter_rows = rows_count // 4
        for copy in (bulk_y, bulk_on_x, bulk_x, bulk_on_y):
            copy.wait_recv()
        first_sum = add(held[2], onward_in[0], direct_in[1]).astype(BF16)
        second_half_sum = add(held[3], onward_in[1], direct_in[0]).astype(BF16)
        for i in range(2):
            line[i] = first_sum[i * quarter_rows : (i + 1) * quarter_rows]
            line[2 + i] = second_half_sum[i * quarter_rows : (i + 1) * quarter_rows]
        bulk_line.start()

    for copy in side_sends:
        copy.wait_recv()

    def shared_pair(p, _):
        lanes = pl.ds(pl.multiple_of(p * 128, 128), 128)
        key_lanes = pl.ds(pl.multiple_of(width + p * 128, 128), 128)
        shared_keys_kernel(
            part_k.at[:, lanes], part_v.at[:, lanes], got_k.at[:, lanes], got_v.at[:, lanes],
            shared["raw"].at[:, key_lanes], gain_qk.at[:, key_lanes], mixed_at(length, queries, 1)(p),
            mixed_at(length, queries, 2)(p), gain_sums.at[pl.ds(4, 1), lanes],
        )
        return 0

    lax.fori_loop(0, pairs, shared_pair, 0)

    def mix_gradient(start, count, payload):
        for t in range(3):
            lanes = slice(t * width + start, t * width + start + count)
            value = jnp.dot(turned[...], mixed[:, lanes], preferred_element_type=F32).astype(BF16)
            if payload is None:
                mix_grad_ref[:, lanes] = value
                continue
            for p in range(8):
                payload[p, :shard, t * count : (t + 1) * count] = value[p * shard : (p + 1) * shard]

    early = width - 128
    mix_gradient(0, early, plane_a.payload if square else None)
    if square:
        outs_end = shard + shard // 2
        for p in range(8):
            for i in range(2):
                at = p * shard + i * (shard // 2)
                plane_a.payload[p, shard:outs_end, i * width : (i + 1) * width] = outg[at : at + shard // 2, :]
            plane_a.payload[p, outs_end:, :] = jnp.zeros((16, 3 * early), BF16)
        plane_a.start()
        bulk_line.first()
    attend_back(row, bounds_ref.at[0], length, *row_to, (pairs - 1, pairs))
    block_rows = lambda side, b: (
        rows_at(side * half + b * part, part) if b < 2 else rows_at(length + side * part, part)
    )
    for b in range(3):
        parts_out[pl.ds(b * part, part), :] = nt(mixed[block_rows(other, b), :], weight[...]).astype(BF16)
    part_send = send(parts_out, parts_in, 13, partner)
    if square:
        plane_a.pass_on()
        bulk_line.second()
    mix_gradient(early, 128, plane_b.payload if square else None)
    if square:
        plane_b.start()
    part_send.wait_recv()
    first_sum_gain = jnp.zeros((1, model), F32)
    for b in range(3):
        rows = pl.ds(b * part, part)
        upstream = nt(mixed[block_rows(core, b), :], weight[...]) + parts_in[rows, :].astype(F32)
        n, r = norm_parts(x[rows, :].astype(F32))
        value, more = norm_back(upstream, n, r, gain_first[...])
        first_sum_gain = first_sum_gain + more
        grad_own[rows, :] = (midg[rows, :] + value).astype(BF16)
    gains_sum[...] = jnp.zeros_like(gains_sum)
    gains_sum[0:1, :] = first_sum_gain
    mine_lanes = pl.ds(pl.multiple_of(core * width, 128), width)
    gains_sum[1:2, mine_lanes] = gain_sums[0:1, :] + gain_sums[2:3, :]
    gains_sum[2:3, mine_lanes] = gain_sums[3:4, :] + gain_sums[4:5, :]
    gains_sum[3:4, :] = gain_second_grad[...]

    if square:
        kept_rows, third_rows = grad_own.at[rows_at(zq * part, part)], grad_own.at[pl.ds(half, part)]
        grad_moves = [
            Moves(
                [remote(kept_rows, grad_out.at[zq], sems, 0, keep)],
                [pltpu.make_async_copy(kept_rows, grad_out.at[zq], local_sem.at[0])],
                None,
                moves,
            ),
            Moves(
                [remote(third_rows, grad_out.at[2], sems, 1, keep)],
                [pltpu.make_async_copy(third_rows, grad_out.at[2], local_sem.at[1])],
                None,
                moves,
            ),
        ]
        grad_cross = remote(grad_own.at[rows_at((1 - zq) * part, part)], grad_out.at[zq], sems, 4, cross)
        grad_cross.start()
        for p in range(8):
            plane_gains.payload[p] = jnp.zeros((16, 128), BF16)
            plane_gains.payload[p, :, :shard] = gains_sum[:, p * shard : (p + 1) * shard].astype(BF16)
        plane_gains.start()

        def to_line(plane, target):
            kept = plane.finish()
            rows = target.parts.shape[1]
            for i in range(2):
                target.parts[2 * core + i] = kept[i * rows : (i + 1) * rows].astype(BF16)
                target.parts[2 * (1 - core) + i] = plane.came[i * rows : (i + 1) * rows]
            target.start()

        plane_a.to_core()
        bulk_line.third()
        plane_b.pass_on()
        to_line(plane_a, line_a)
        plane_gains.pass_on()
        bulk_line.fourth()
        line_a.first()
        plane_b.to_core()
        plane_gains.to_core()
        line_a.second()
        to_line(plane_b, across_b)
        grad_moves[0].start()
        gain_part[...] = (plane_gains.finish() + plane_gains.came[...].astype(F32)).astype(BF16)
        gain_sends = [send(gain_part, gain_got.at[i], 71 + i, along[i]) for i in range(3)]
        bulk_line.fifth()
        line_a.third()
        across_b.total()
        line_a.fourth()
        bulk_line.sixth()
        grad_moves[1].start()

        flat = jnp.concatenate([whole_line[i] for i in range(4)], axis=0)
        tile = down_ref.shape[0]
        ups = [flat[tile + 2 * shard * i : tile + 2 * shard * (i + 1)] for i in range(2)]
        for i in range(2):
            up_out[i] = jnp.where(core == 0, ups[i][shard:], ups[i][:shard])
        up_send = send(up_out, up_got, 74, partner)
        line_a.fifth()
        across_b.finish()
        down_ref[...] = flat[:tile]

        def place_up(side, i, values):
            for j in range(2):
                lanes = pl.ds(pl.multiple_of((2 * (2 * i + j) + side) * tile, 128), tile)
                up_ref[:, lanes] = values[:, j * tile : (j + 1) * tile]

        for i in range(2):
            place_up(core, i, jnp.where(core == 0, ups[i][:shard], ups[i][shard:]))
        line_a.sixth()
        up_send.wait_recv()
        for i in range(2):
            place_up(other, i, up_got[i])

        def place(target, start, count):
            for index in range(4):
                side, low_half = index // 2, index % 2
                values = target.whole[index]
                rows = values.shape[0]
                first_row = low_half * rows
                taken = min(rows, shard - first_row)
                for t in range(3):
                    lanes = slice((2 * t + side) * width + start, (2 * t + side) * width + start + count)
                    total_ref[first_row : first_row + taken, lanes] = values[:taken, t * count : (t + 1) * count]
                if taken < rows:
                    for i in range(2):
                        outw_ref[i * (shard // 2) : (i + 1) * (shard // 2), side * width : (side + 1) * width] = values[
                            taken : taken + shard // 2, i * width : (i + 1) * width
                        ]

        place(line_a, 0, early)
        for copy in gain_sends:
            copy.wait_recv()
        gains_ref[...] = add(gain_part[...], gain_got[0], gain_got[1], gain_got[2])
        place(across_b, early, 128)
        for target in (bulk_line, line_a):
            target.wait_sends()
        grad_cross.wait()
        for copy in grad_moves:
            copy.wait()
    third_moves.wait()
    for copy in waits:
        copy.wait_send()


def backward_pass(square, pics, row, shared, weights, gains, bounds, *more):
    length, model = row[1].shape
    width = model // 2
    part = length // 4
    half, tokens = 2 * part, 3 * part
    shard = model // 8
    near = pl.BlockSpec(memory_space=pltpu.VMEM)
    anywhere = pl.BlockSpec(memory_space=pl.ANY)
    low = lambda *shape: (shape, BF16)
    wide = lambda *shape: (shape, F32)
    if square:
        rows = more[1].shape[1]
        tile = rows // 2
        outs = [
            (low(part, model), anywhere),
            (low(3, part, model), anywhere),
            (low(shard, 6 * width), near),
            (wide(16, 128), near),
            (low(shard, 8 * tile), near),
            (low(tile, model), near),
            (low(shard, model), near),
        ]
    else:
        outs = [
            (low(part, model), anywhere),
            (low(tokens, model), near),
            (low(model, 3 * width), near),
            (wide(16, model), near),
        ]
    scratch = []
    for queries in (length, half):
        scratch += [
            low(2 * (width // 128), queries, 128), low(length, width), low(length, width), low(queries, width),
            low(queries, width), low(length, 2 * width),
        ]
    scratch += [
        low(length + half, model), low(model, length + half), low(model, 3 * width), low(tokens, model),
        wide(tokens, model),
        low(2, length, 128), low(2, length, 128), low(2, length, 128), wide(2, length, 128), wide(length, 128),
        low(length + half, 3 * width), low(length, width), low(length, width), low(half, width), low(half, width),
        wide(8, width), low(tokens, model),
    ]
    if square:
        span = rows // 2
        early = 3 * (width - 128)
        plane = lambda count, columns: [
            low(8, count, columns), low(5, count, columns), low(4, count, columns), low(count, columns)
        ]
        chunked = lambda count, columns, slots: [low(size, count, columns) for size in (4, 4) + slots]
        early_rows = shard + shard // 2 + 16
        scratch += [
            wide(16, model), low(model, width),
            low(4, span, model), low(2, span, model), low(2, span, model), low(2, span, model),
            low(4, rows // 4, model), low(4, rows // 4, model), low(3, rows // 4, model), low(3, rows // 4, model),
            low(2, shard, model), low(2, shard, model),
            *plane(early_rows, early), *plane(shard, 3 * 128), *plane(16, 128),
            *chunked(early_rows // 2, early, (3, 3)), *chunked(shard // 2, 3 * 128, (3,)), low(16, 128), low(3, 16, 128),
        ]
    return pl.pallas_call(
        functools.partial(backward_kernel, square, pics),
        in_specs=[anywhere] * 17 + [near] * 4 + [anywhere] * len(more),
        out_specs=[spec for _, spec in outs],
        out_shape=[jax.ShapeDtypeStruct(*shape) for shape, _ in outs],
        scratch_shapes=[pltpu.VMEM(*shape) for shape in scratch]
        + [
            pltpu.SemaphoreType.DMA((75,)),
            pltpu.SemaphoreType.DMA((75,)),
            pltpu.SemaphoreType.DMA((30,)),
            pltpu.SemaphoreType.DMA((3,)),
        ],
        compiler_params=pltpu.CompilerParams(
            collective_id=2, has_side_effects=True, vmem_limit_bytes=63 * 1024 * 1024
        ),
        name="backward_pass",
    )(*row, *shared, *weights, *gains, bounds, *more)


def local(
    tokens, lengths, pictures, first_gain, mix_weight, query_gain, key_gain, out_weight,
    second_gain, up_weight, down_weight, cotangent,
):
    chip, core, zp, zq = here()
    chips = lax.axis_size("chip")
    square = chips == 4
    rows = ("chip", "core")
    _, part, model = tokens.shape
    length = 4 * part
    half = 2 * part
    width = HEADS // 2 * HEAD
    pics = lengths.shape[1]
    shard = mix_weight.shape[0]

    hidden = up_weight.shape[1]
    tile = hidden // 8
    gains = [gain[None] for gain in (first_gain, query_gain, key_gain, second_gain)]
    if square:
        forward = forward_pass(
            True, pics, tokens, cotangent, lengths, mix_weight, *gains, up_weight, out_weight
        )
        up_half, out_matrix = forward[19:]
        down_half = down_weight
        gain_second = forward[5]
    else:
        gather = lambda weight: lax.all_gather(weight, rows, axis=0, tiled=True)
        half_of = lambda weight, axis: pick(weight, core, axis)
        mix_half = half_of(gather(mix_weight).reshape(model, 3, 2, width), 2).reshape(model, 3 * width)
        up_half = half_of(gather(up_weight).reshape(model, 4, 2, tile), 2).reshape(model, 4 * tile)
        down_half = half_of(gather(down_weight).reshape(4, 2, tile, model), 1).reshape(4 * tile, model)
        out_matrix = gather(out_weight)
        gains = lax.all_gather(jnp.concatenate(gains), rows, axis=0, tiled=False)
        gains = gains.transpose(1, 0, 2).reshape(4, 1, model).astype(F32)
        gain_second = gains[3]
        gain_qk = half_of(gains[1:3].reshape(2, 2, width), 1).reshape(1, model)
        forward = forward_pass(False, pics, tokens, cotangent, lengths, mix_half, gains[0], gain_qk)
    own_tokens, bounds, mix_half, grad_tokens, gain_first, _, gain_qk = forward[:7]
    normed, qk, v, raw, out, aug = forward[7:13]
    shared_normed, shared_qk, shared_v, shared_raw, shared_out, shared_aug = forward[13:19]

    def collect(mine, cross, third):
        mine = lax.ppermute(mine, COLUMN, KEEP)
        cross = lax.ppermute(cross, COLUMN, CROSS)
        third = lax.ppermute(third, COLUMN, KEEP)
        return jnp.stack([jnp.where(zq == 0, mine, cross), jnp.where(zq == 0, cross, mine), third])

    output, third, middle_grad, grad, shared_grad, out_grad, second_gain_grad, packed, far = dense(
        square, out, shared_out, own_tokens, grad_tokens, cotangent, out_matrix, gain_second, bounds,
        up_half, down_half,
    )
    row_side = (aug, qk, v, out, grad, raw, normed)
    shared_side = (shared_aug, shared_qk, shared_v, shared_out, shared_grad, shared_raw, shared_normed)
    weights = (mix_half, own_tokens, middle_grad)
    gains = (gain_first, gain_qk, second_gain_grad)
    if square:
        third, input_out, mix_out, gains_out, up_out, down_out, outw_out = backward_pass(
            True, pics, row_side, shared_side, weights, gains, bounds, third, packed, far, out_grad
        )
        gains_out = gains_out[:4, :shard]
        mix_out, up_out, down_out, outw_out = (
            array.astype(F32) for array in (mix_out, up_out, down_out, outw_out)
        )
    else:
        third, input_grad, mix_grad, gain_grads = backward_pass(
            False, pics, row_side, shared_side, weights, gains, bounds, third
        )

        def reduce(grad):
            return lax.psum(lax.psum_scatter(grad, rows, scatter_dimension=0, tiled=True), SEQ).astype(F32)

        first, second = input_grad[:part], input_grad[part:half]
        input_out = collect(
            jnp.where(zq == 0, first, second), jnp.where(zq == 0, second, first), input_grad[half:]
        )
        own_core = jnp.arange(2) == core
        eighth = model // 8
        down_grad = packed[:, None, :tile]
        down_out = reduce(jnp.where(own_core[None, :, None, None], down_grad, 0).reshape(hidden, model))
        up_grad = packed[:, tile : 2 * tile].reshape(4, 2, 2 * eighth, 2, tile).transpose(0, 2, 1, 3, 4)
        up_grad = up_grad.reshape(model, 4, 1, tile)
        up_out = reduce(jnp.where(own_core[None, None, :, None], up_grad, 0).reshape(model, hidden))
        out_grad = out_grad.reshape(model, 1, width)
        outw_out = reduce(jnp.where(own_core[None, :, None], out_grad, 0).reshape(model, model))
        mix_out = reduce(
            jnp.where(own_core[None, None, :, None], mix_grad.reshape(model, 3, 1, width), 0).reshape(model, 6 * width)
        )
        gain_grads = gain_grads[:4].reshape(4, 2 * chips, shard).transpose(1, 0, 2).astype(BF16)
        gains_out = reduce(gain_grads).reshape(4, shard)
    output = jnp.concatenate([output, third[None]])
    return (
        output, input_out, gains_out[0], mix_out, gains_out[1], gains_out[2], outw_out, gains_out[3],
        up_out, down_out,
    )


def solution(mesh):
    fsdp = mesh.shape["fsdp"]
    split = Mesh(mesh.devices.reshape(fsdp // 2, 2, 2, 2), ("chip", "core", "zp", "zq"))
    rows = ("chip", "core")
    return jax.shard_map(
        local,
        mesh=split,
        in_specs=(
            P(rows, SEQ, None),
            P(rows, None),
            P(rows, SEQ),
            P(rows),
            P(rows, None),
            P(rows),
            P(rows),
            P(rows, None),
            P(rows),
            P(rows, None),
            P(rows, None),
            P(rows, SEQ, None),
        ),
        out_specs=(
            P(rows, SEQ, None),
            P(rows, SEQ, None),
            P(rows),
            P(rows, None),
            P(rows),
            P(rows),
            P(rows, None),
            P(rows),
            P(rows, None),
            P(rows, None),
        ),
        check_vma=False,
    )
```

```python
import functools

import jax
import jax.numpy as jnp
from jax import lax
from jax.experimental import pallas as pl
from jax.experimental.pallas import tpu as pltpu
from jax.sharding import Mesh, PartitionSpec as P

HEADS = 12
HEAD = 64
EPSILON = 1e-06
BLOCK = 256
STEP = 512
MARK = 32.0
EXP2_FACTOR = HEAD**-0.5 * 1.4426950408889634
F32 = jnp.float32
BF16 = jnp.bfloat16
VMEM_LIMIT = 56 * 1024 * 1024

SEQ = ("zp", "zq")
COLUMN = ("core", "zp", "zq")
KEEP = [
    (core * 4 + z, (z // 2) * 4 + 2 * core + z % 2) for core in range(2) for z in range(4)
]
CROSS = [
    (core * 4 + z, (z // 2) * 4 + 2 * core + 1 - z % 2) for core in range(2) for z in range(4)
]


def swap(array, name, bit=1):
    count = lax.axis_size(name)
    return lax.ppermute(array, name, [(i, i ^ bit) for i in range(count)])


def pick(array, index, axis=0):
    return lax.dynamic_index_in_dim(array, index, axis, keepdims=False)


def group_ones(scale, size=128):
    row = lax.broadcasted_iota(jnp.int32, (size, size), 0) // HEAD
    column = lax.broadcasted_iota(jnp.int32, (size, size), 1) // HEAD
    return jnp.where(row == column, scale, 0.0).astype(BF16)


def group_sum(values, ones):
    return jnp.dot(values.astype(BF16), ones, preferred_element_type=F32)


def group_sum_fine(values, ones):
    high = values.astype(BF16)
    return group_sum(high, ones) + group_sum(values - high.astype(F32), ones)


def project_kernel(x_ref, gain_ref, weight_ref, qkg_ref, normed_ref, qk_ref, v_ref, raw_ref):
    both = qk_ref.shape[1]
    x = x_ref[...].astype(F32)
    center = x - jnp.mean(x, axis=-1, keepdims=True)
    spread = jnp.mean(center * center, axis=-1, keepdims=True)
    normed = (center * lax.rsqrt(spread + EPSILON) * gain_ref[...]).astype(BF16)
    normed_ref[...] = normed
    ones = group_ones(1.0 / HEAD, 256)
    for at in range(0, both, 256):
        lanes = slice(at, at + 256)
        raw = jnp.dot(normed, weight_ref[:, lanes], preferred_element_type=F32)
        raw_ref[:, lanes] = raw.astype(BF16)
        c = raw - group_sum(raw, ones)
        n = c * lax.rsqrt(group_sum(c * c, ones) + EPSILON)
        qk_ref[:, lanes] = (n * qkg_ref[:, lanes]).astype(BF16)
    v_ref[...] = jnp.dot(normed, weight_ref[:, both:], preferred_element_type=F32).astype(BF16)


def nt(a, b):
    return lax.dot_general(a, b, (((1,), (1,)), ((), ())), preferred_element_type=F32)


def tn(a, b):
    return lax.dot_general(a, b, (((0,), (0,)), ((), ())), preferred_element_type=F32)


def slots(queries, length, part):
    at = lax.broadcasted_iota(jnp.int32, (queries, 128), 0)
    if queries == length:
        return at
    return at % part + part * (lax.axis_index("zq") + 2 * (at // part))


def own_rows(ref, start, count, queries, part):
    if queries == ref.shape[0]:
        return ref[pl.ds(start, count), :]
    zq = lax.axis_index("zq")
    pieces = [
        ref[pl.ds(pl.multiple_of((zq + 2 * i) * part, part), part), :]
        for i in range(start // part, (start + count) // part)
    ]
    return jnp.concatenate(pieces, axis=0)


def query_marks(bounds_ref, place, queries, length, part, pics):
    at = slots(queries, length, part)
    inside = (at >= bounds_ref[0:1, :]) & (at < bounds_ref[2:3, :])
    values = jnp.where(inside, MARK, 0.0)
    return jnp.where(place == pics, MARK, values).astype(BF16)


def key_marks(bounds_ref, place, length, pics):
    at = lax.broadcasted_iota(jnp.int32, (length, 128), 0)
    inside = (at >= bounds_ref[0:1, :]) & (at < bounds_ref[1:2, :])
    values = jnp.where(inside, MARK, 0.0)
    values = jnp.where(place == pics, -MARK, values)
    return jnp.where((place > pics) & (place < pics + 4), 1.0, values).astype(BF16)


def attend_kernel(pics, q_ref, k_ref, v_ref, bounds_ref, out_ref, aug_ref, kaug, vaug, qaug):
    length = k_ref.shape[0]
    queries = out_ref.shape[0]
    part = length // 4
    lane = lax.broadcasted_iota(jnp.int32, (1, 128), 1)
    place = lane % HEAD
    sides = [lane < HEAD, lane >= HEAD]
    kmarks = key_marks(bounds_ref, place, length, pics)
    qmarks = query_marks(bounds_ref, place, queries, length, part, pics)
    qaug[...] = qmarks
    for h in range(2):
        kaug[h] = jnp.where(sides[h], k_ref[...], kmarks)
        vaug[h] = jnp.where(sides[h], v_ref[...], jnp.ones_like(v_ref))
    for b in range(queries // STEP):
        rows = pl.ds(b * STEP, STEP)
        mine = own_rows(q_ref, b * STEP, STEP, queries, part)
        query = [jnp.where(sides[h], mine, qaug[rows, :]) for h in range(2)]
        total = [jnp.zeros((STEP, 128), F32)] * 2
        for j in range(length // STEP):
            keys = pl.ds(j * STEP, STEP)
            scores = [nt(query[h], kaug[h, keys, :]) for h in range(2)]
            weights = [jnp.exp2(x * EXP2_FACTOR).astype(BF16) for x in scores]
            total = [
                total[h] + jnp.dot(weights[h], vaug[h, keys, :], preferred_element_type=F32) for h in range(2)
            ]
        results = []
        for h in range(2):
            results.append(total[h] / pltpu.roll(total[h], HEAD, 1))
            log_total = jnp.log(jnp.where(sides[h], 1.0, total[h])) * -(HEAD**0.5)
            first = log_total.astype(BF16)
            rest = log_total - first.astype(F32)
            middle = rest.astype(BF16)
            last = (rest - middle.astype(F32)).astype(BF16)
            logs = jnp.where(place == pics + 1, first, jnp.where(place == pics + 2, middle, last))
            slot = jnp.logical_not(sides[h]) & (place > pics) & (place < pics + 4)
            aug_ref[h, rows, :] = jnp.where(slot, logs, query[h])
        out_ref[rows, :] = jnp.where(sides[0], results[0], results[1]).astype(BF16)


def head_norm_back(e, raw, gain, means):
    raw = raw.astype(F32)
    c = raw - group_sum(raw, means)
    r = lax.rsqrt(group_sum(c * c, means) + EPSILON)
    n = c * r
    t = e * gain
    grad = r * (t - group_sum(t, means) - n * group_sum(t * n, means))
    return grad.astype(BF16), jnp.sum(e * n, axis=0, keepdims=True)


def attend_back_kernel(
    pics, aug_ref, k_ref, v_ref, out_ref, do_ref, rawq_ref, rawk_ref, qg_ref, kg_ref, bounds_ref,
    dq_ref, dk_ref, dv_ref, qgg_ref, kgg_ref, kaug, vaug, doaug, qsum, ksum,
):
    length = k_ref.shape[0]
    queries = do_ref.shape[0]
    part = length // 4
    whole = queries == length
    lane = lax.broadcasted_iota(jnp.int32, (1, 128), 1)
    place = lane % HEAD
    sides = [lane < HEAD, lane >= HEAD]
    kmarks = key_marks(bounds_ref, place, length, pics)
    vmarks = jnp.where(place < 2, 1.0, 0.0).astype(BF16)
    ones = group_ones(1.0)
    inner = group_sum_fine(do_ref[...].astype(F32) * out_ref[...].astype(F32), ones)
    inner = -pltpu.roll(inner, HEAD, 1)
    inner_high = inner.astype(BF16)
    inner_low = (inner - inner_high.astype(F32)).astype(BF16)
    zero = jnp.zeros((), BF16)
    gmarks = jnp.where(place == 0, inner_high, jnp.where(place == 1, inner_low, zero))
    for h in range(2):
        kaug[h] = jnp.where(sides[h], k_ref[...], kmarks)
        vaug[h] = jnp.where(sides[h], v_ref[...], vmarks)
        doaug[h] = jnp.where(sides[h], do_ref[...], gmarks)
    for b in range(length // STEP):
        keys = pl.ds(b * STEP, STEP)
        key = [kaug[h, keys, :] for h in range(2)]
        value = [vaug[h, keys, :] for h in range(2)]
        dk = [jnp.zeros((STEP, 128), F32)] * 2
        dv = [jnp.zeros((STEP, 128), F32)] * 2
        for j in range(queries // STEP):
            rows = pl.ds(j * STEP, STEP)
            query = [aug_ref[h, rows, :] for h in range(2)]
            grad = [doaug[h, rows, :] for h in range(2)]
            scores = [nt(key[h], query[h]) for h in range(2)]
            soft_grad = [nt(value[h], grad[h]) for h in range(2)]
            weights = [jnp.exp2(x * EXP2_FACTOR) for x in scores]
            score_grad = [(weights[h] * soft_grad[h]).astype(BF16) for h in range(2)]
            for h in range(2):
                part_sum = tn(score_grad[h], key[h])
                if b == 0:
                    qsum[h, rows, :] = part_sum
                else:
                    qsum[h, rows, :] += part_sum
                dk[h] = dk[h] + jnp.dot(score_grad[h], query[h], preferred_element_type=F32)
                dv[h] = dv[h] + jnp.dot(weights[h].astype(BF16), grad[h], preferred_element_type=F32)
        ksum[keys, :] = jnp.where(sides[0], dk[0], dk[1]) * HEAD**-0.5
        dv_ref[keys, :] = jnp.where(sides[0], dv[0], dv[1]).astype(BF16)

    means = group_ones(1.0 / HEAD)
    gain_sum = jnp.zeros((1, 128), F32)
    for b in range(queries // part):
        rows = pl.ds(b * part, part)
        e = jnp.where(sides[0], qsum[0, rows, :], qsum[1, rows, :]) * HEAD**-0.5
        raw = own_rows(rawq_ref, b * part, part, queries, part)
        dq_ref[rows, :], more = head_norm_back(e.astype(BF16).astype(F32), raw, qg_ref[...], means)
        gain_sum = gain_sum + more
    qgg_ref[...] = gain_sum
    gain_sum = jnp.zeros((1, 128), F32)
    for b in range(length // part):
        rows = pl.ds(b * part, part)
        e = ksum[rows, :].astype(BF16)
        if whole:
            dk_ref[rows, :], more = head_norm_back(e.astype(F32), rawk_ref[rows, :], kg_ref[...], means)
            gain_sum = gain_sum + more
        else:
            dk_ref[rows, :] = e
    kgg_ref[...] = gain_sum


def shared_keys_kernel(dk_ref, dv_ref, gotk_ref, gotv_ref, rawk_ref, kg_ref, outk_ref, outv_ref, kgg_ref):
    count = outk_ref.shape[0]
    part = count // 2
    means = group_ones(1.0 / HEAD)
    gain_sum = jnp.zeros((1, 128), F32)
    for b in range(2):
        rows = pl.ds(b * part, part)
        own = lambda ref: own_rows(ref, b * part, part, count, part)
        e = own(dk_ref).astype(F32) + gotk_ref[rows, :].astype(F32)
        outk_ref[rows, :], more = head_norm_back(e, own(rawk_ref), kg_ref[...], means)
        gain_sum = gain_sum + more
        outv_ref[rows, :] = (own(dv_ref).astype(F32) + gotv_ref[rows, :].astype(F32)).astype(BF16)
    kgg_ref[...] = gain_sum


def gelu_pair(h):
    size = jnp.abs(h)
    bell = jnp.exp2(h * h * -0.7213475204444817)
    t = 1.0 / (1.0 + 0.23164189 * size)
    series = t * (0.127414796 + t * (-0.142248368 + t * (0.7107068705 + t * (-0.7265760135 + t * 0.5307027145))))
    tail = series * bell
    below = jnp.where(h < 0.0, tail, 1.0 - tail)
    return h * below, below + h * (bell * 0.3989422804014327)


def norm_parts(values):
    center = values - jnp.mean(values, axis=-1, keepdims=True)
    spread = lax.rsqrt(jnp.mean(center * center, axis=-1, keepdims=True) + EPSILON)
    return center * spread, spread


def norm_back(upstream, n, r, gain):
    t = upstream * gain
    grad = r * (t - jnp.mean(t, axis=-1, keepdims=True) - n * jnp.mean(t * n, axis=-1, keepdims=True))
    return grad, jnp.sum(upstream * n, axis=0, keepdims=True)


MESH_ID = pl.DeviceIdType.MESH


def here():
    return lax.axis_index("chip"), lax.axis_index("core"), lax.axis_index("zp"), lax.axis_index("zq")


def remote(source, target, sems, at, device):
    sent, got = sems
    return pltpu.make_async_remote_copy(
        src_ref=source, dst_ref=target, send_sem=sent.at[at], recv_sem=got.at[at],
        device_id=device, device_id_type=MESH_ID,
    )


def greet(devices, maybe=None, moves=None):
    barrier = pltpu.get_barrier_semaphore()
    for device in devices:
        pl.semaphore_signal(barrier, inc=1, device_id=device, device_id_type=MESH_ID)
    if maybe is None:
        pl.semaphore_wait(barrier, len(devices))
        return

    @pl.when(moves)
    def _():
        pl.semaphore_signal(barrier, inc=1, device_id=maybe, device_id_type=MESH_ID)

    pl.semaphore_wait(barrier, len(devices) + jnp.where(moves, 1, 0))


def rows_at(start, count):
    return pl.ds(pl.multiple_of(start, 16), count)


class Moves:
    def __init__(self, moved, stays, crossed, moves):
        self.moved, self.stays, self.crossed, self.moves = moved, stays, crossed, moves

    def each(self, act):
        if self.crossed is not None:
            act(self.crossed)

        @pl.when(self.moves)
        def _():
            for copy in self.moved:
                act(copy)

        @pl.when(jnp.logical_not(self.moves))
        def _():
            for copy in self.stays:
                act(copy)

    def start(self):
        self.each(lambda copy: copy.start())

    def wait(self):
        self.each(lambda copy: copy.wait())


class Across:
    def __init__(self, parts, whole, came, sems, at, waits):
        chip, core, zp, zq = here()
        self.z = 2 * zp + zq
        self.along = [(chip, core, zp, 1 - zq), (chip, core, 1 - zp, zq), (chip, core, 1 - zp, 1 - zq)]
        self.parts, self.whole, self.came = parts, whole, came
        self.sems, self.at, self.waits = sems, at, waits

    def exchange(self, source_of, target_of, at):
        copies = []
        for i in range(3):
            copy = remote(source_of(i), target_of(i), self.sems, self.at + at + i, self.along[i])
            copy.start()
            copies.append(copy)
        self.waits.extend(copies)
        return copies

    def start(self):
        self.first = self.exchange(lambda i: self.parts.at[self.z ^ (i + 1)], lambda i: self.came.at[i], 0)

    def total(self):
        for copy in self.first:
            copy.wait_recv()
        self.whole[self.z] = add(self.parts[self.z], self.came[0], self.came[1], self.came[2]).astype(BF16)
        self.second = self.exchange(lambda i: self.whole.at[self.z], lambda i: self.whole.at[self.z], 3)

    def finish(self):
        for copy in self.second:
            copy.wait_recv()


class PlaneSum:
    def __init__(self, payload, relay, final, came, sems, at, waits):
        self.chip, self.core, zp, zq = here()
        self.payload, self.relay, self.final, self.came = payload, relay, final, came
        self.sems, self.at, self.waits = sems, at, waits
        self.near_x = (self.chip ^ 1, self.core, zp, zq)
        self.near_y = (self.chip ^ 2, self.core, zp, zq)
        self.partner = (self.chip, 1 - self.core, zp, zq)

    def send(self, source, target, at, device):
        copy = remote(source, target, self.sems, self.at + at, device)
        copy.start()
        self.waits.append(copy)
        return copy

    def same(self, hop):
        return 2 * (self.chip ^ hop) + self.core

    def twin(self, hop):
        return 2 * (self.chip ^ hop) + 1 - self.core

    def start(self):
        payload = self.payload
        self.first = self.send(payload.at[self.same(3)], self.relay.at[0], 0, self.near_y)
        self.second = self.send(payload.at[self.twin(3)], self.relay.at[1], 1, self.near_x)
        self.direct_x = self.send(payload.at[self.twin(1)], self.final.at[0], 2, self.near_x)
        self.direct_y = self.send(payload.at[self.same(2)], self.final.at[1], 3, self.near_y)

    def pass_on(self):
        self.first.wait_recv()
        self.relay[2] = add(self.relay[0], self.payload[self.same(1)]).astype(BF16)
        self.onward_x = self.send(self.relay.at[2], self.final.at[2], 4, self.near_x)
        self.second.wait_recv()
        self.relay[3] = add(self.relay[1], self.payload[self.twin(2)]).astype(BF16)
        self.onward_y = self.send(self.relay.at[3], self.final.at[3], 5, self.near_y)

    def to_core(self):
        self.direct_x.wait_recv()
        self.onward_y.wait_recv()
        self.relay[4] = add(self.payload[self.twin(0)], self.final[0], self.final[3]).astype(BF16)
        self.crossing = self.send(self.relay.at[4], self.came, 6, self.partner)

    def finish(self):
        self.direct_y.wait_recv()
        self.onward_x.wait_recv()
        kept = add(self.payload[self.same(0)], self.final[1], self.final[2])
        self.crossing.wait_recv()
        return kept


class Line:
    def __init__(self, parts, whole, right, left, sems, at):
        chip, core, zp, zq = here()
        self.z = 2 * zp + zq
        up, down = jnp.minimum(self.z + 1, 3), jnp.maximum(self.z - 1, 0)
        self.next = (chip, core, up // 2, up % 2)
        self.last = (chip, core, down // 2, down % 2)
        self.parts, self.whole, self.right, self.left = parts, whole, right, left
        self.sems, self.at, self.sends = sems, at, []

    def at_chip(self, z, *acts):
        @pl.when(self.z == z)
        def _():
            for act in acts:
                act()

    def part_copy(self, c, rightward):
        if rightward:
            return remote(self.parts.at[c], self.right.at[3 - c], self.sems, self.at + 3 - c, self.next)
        return remote(self.parts.at[c], self.left.at[c], self.sems, self.at + 3 + c, self.last)

    def whole_copy(self, c, rightward):
        if rightward:
            return remote(self.whole.at[c], self.whole.at[c], self.sems, self.at + 6 + c, self.next)
        return remote(self.whole.at[c], self.whole.at[c], self.sems, self.at + 8 + c, self.last)

    def send(self, z, make, c, rightward):
        self.sends.append((z, make, c, rightward))
        return lambda: make(c, rightward).start()

    def take(self, c, rightward):
        def act():
            self.part_copy(c, rightward).wait_recv()
            came = self.right[3 - c] if rightward else self.left[c]
            self.parts[c] = add(self.parts[c], came).astype(BF16)

        return act

    def got(self, c, rightward):
        return lambda: self.whole_copy(c, rightward).wait_recv()

    def start(self):
        part = self.part_copy
        self.at_chip(0, *[self.send(0, part, c, True) for c in (3, 2, 1)])
        self.at_chip(3, *[self.send(3, part, c, False) for c in (0, 1, 2)])

    def first(self):
        self.at_chip(1, self.take(3, True), self.send(1, self.part_copy, 3, True))
        self.at_chip(2, self.take(0, False), self.send(2, self.part_copy, 0, False))

    def second(self):
        part = self.part_copy
        self.at_chip(
            1, self.take(2, True), self.send(1, part, 2, True), self.take(0, False), self.send(1, part, 0, False)
        )
        self.at_chip(
            2, self.take(1, False), self.send(2, part, 1, False), self.take(3, True), self.send(2, part, 3, True)
        )

    def third(self):
        self.at_chip(0, self.take(0, False))
        self.at_chip(1, self.take(1, True), self.take(1, False))
        self.at_chip(2, self.take(2, True), self.take(2, False))
        self.at_chip(3, self.take(3, True))
        self.whole[self.z] = self.parts[self.z]
        for z in range(4):
            acts = [self.send(z, self.whole_copy, z, True)] if z < 3 else []
            acts += [self.send(z, self.whole_copy, z, False)] if z > 0 else []
            self.at_chip(z, *acts)

    def fourth(self):
        whole = self.whole_copy
        for z in (1, 2):
            self.at_chip(
                z, self.got(z - 1, True), self.send(z, whole, z - 1, True), self.got(z + 1, False),
                self.send(z, whole, z + 1, False),
            )

    def fifth(self):
        whole = self.whole_copy
        self.at_chip(1, self.got(3, False), self.send(1, whole, 3, False))
        self.at_chip(2, self.got(0, True), self.send(2, whole, 0, True))

    def sixth(self):
        self.at_chip(0, *[self.got(c, False) for c in (1, 2, 3)])
        self.at_chip(3, *[self.got(c, True) for c in (2, 1, 0)])

    def wait_sends(self):
        for z in range(4):
            mine = [make(c, rightward) for at, make, c, rightward in self.sends if at == z]
            self.at_chip(z, *[copy.wait_send for copy in mine])


def write_bounds(pics, lens_ref, bounds_ref, zp, zq, length):
    lane = lax.broadcasted_iota(jnp.int32, (8, 128), 1)
    lens = jnp.where(zp == 0, lens_ref[0], lens_ref[1])
    ends = lens
    for hop in (1, 2, 4, 8):
        ends = ends + jnp.where(lane >= hop, pltpu.roll(ends, hop, 1), 0)
    starts = ends - lens
    last = (lens > 0) & (pltpu.roll(lens, 127, 1) == 0)
    query_ends = jnp.where(last, length, ends)
    total = jnp.max(jnp.where(lane < pics, ends, 0), axis=1, keepdims=True)

    def both(values):
        values = jnp.where(lane < HEAD, jnp.where(lane < pics, values, 2 * length), 0)
        return values + pltpu.roll(values, HEAD, 1)

    tables = [both(starts), both(ends), both(query_ends), jnp.broadcast_to(total, (8, 128))]
    for t in range(4):
        table = tables[t]
        bounds_ref[0, t : t + 1, :] = jnp.where(zq == 0, table[0:1], table[1:2])
        bounds_ref[1, t : t + 1, :] = table[2:3]
    bounds_ref[:, 4:, :] = jnp.zeros((2, 4, 128), jnp.int32)


def forward_kernel(square, pics, *refs):
    refs = list(refs)
    take = lambda count: [refs.pop(0) for _ in range(count)]
    tokens_ref, cot_ref, lengths_ref, weight_in = take(4)
    if square:
        gain_in = take(4)
        up_in, outw_ref = take(2)
    else:
        gain_first_in, gain_qk_in = take(2)
    x_out, bounds_ref, mix_hbm, cot_hbm, gain_first, second_ref, gain_qk = take(7)
    names = ("normed", "qk", "v", "raw", "out", "aug")
    outs = [dict(zip(names, take(6))) for _ in range(2)]
    if square:
        up_hbm, outw_hbm = take(2)
    row_ref, shared_ref, cot_out, lens_ref, lens_out = take(5)
    scratch = [dict(zip(names, take(6))) for _ in range(2)]
    kaug, vaug, qaug = take(3)
    if square:
        mix_ref, gains_ref, up_ref, mix_out, gains_out, up_out, outw_out = take(7)
    sent, got, local_sem, write_sem = take(4)

    chip, core, zp, zq = here()
    z = 2 * zp + zq
    part = tokens_ref.shape[1]
    half, length = 2 * part, 4 * part
    sems = (sent, got)
    partner = (chip, 1 - core, zp, zq)
    side = (chip, core, zp, 1 - zq)
    keep = (chip, zp, core, zq)
    cross = (chip, zp, core, 1 - zq)
    moves = core != zp
    near_x = (chip ^ 1, core, zp, zq)
    near_y = (chip ^ 2, core, zp, zq)
    greet([partner, side, cross] + ([near_x, near_y] if square else []), keep, moves)

    def quarter(ref, index):
        return ref.at[rows_at(index * part, part)]

    own_row = remote(tokens_ref.at[zq], quarter(row_ref, z), sems, 0, keep)
    own_shared = remote(tokens_ref.at[2], quarter(shared_ref, z), sems, 2, keep)
    stay_row = pltpu.make_async_copy(tokens_ref.at[zq], quarter(row_ref, z), local_sem.at[0])
    stay_shared = pltpu.make_async_copy(tokens_ref.at[2], quarter(shared_ref, z), local_sem.at[1])

    @pl.when(moves)
    def _():
        own_row.start()

    @pl.when(jnp.logical_not(moves))
    def _():
        stay_row.start()

    cross_row = remote(tokens_ref.at[1 - zq], quarter(row_ref, z), sems, 1, cross)
    cross_row.start()

    @pl.when(moves)
    def _():
        own_shared.start()

    @pl.when(jnp.logical_not(moves))
    def _():
        stay_shared.start()

    lens_ref[...] = jnp.zeros_like(lens_ref)
    lens_ref[: lengths_ref.shape[0], :pics] = lengths_ref[...]
    lens_copy = remote(lens_ref, lens_out.at[core], sems, 8, partner)
    lens_copy.start()
    lens_stay = pltpu.make_async_copy(lens_ref, lens_out.at[core], local_sem.at[2])
    lens_stay.start()
    waits = []
    if square:
        shard = mix_ref.shape[1]
        tile = up_ref.shape[2] // 4
        width = mix_ref.shape[2] // 3
        for h in range(2):
            for i in range(3):
                mix_ref[h, :, i * width : (i + 1) * width] = weight_in[:, (2 * i + h) * width : (2 * i + h + 1) * width]
        gains_ref[...] = jnp.zeros_like(gains_ref)
        for i in range(4):
            gains_ref[i : i + 1, :shard] = gain_in[i][...].astype(F32)
        mine, theirs = 2 * chip + core, 2 * chip + 1 - core
        slot = [9]

        def send(source, target, device):
            copy = remote(source, target, sems, slot[0], device)
            slot[0] += 1
            copy.start()
            waits.append(copy)
            return copy

        def stay(source, target, at):
            copy = pltpu.make_async_copy(source, target, local_sem.at[at])
            copy.start()
            return copy

        def block(ref, start, count):
            return ref.at[rows_at(start, count)]

        mix_piece = lambda index: (block(mix_out, index * shard, shard), gains_out.at[index])

        def send_mix(sources, index, device):
            return [send(source, target, device) for source, target in zip(sources, mix_piece(index))]

        def arrived(copies):
            for copy in copies:
                copy.wait_recv()

        x_mine, y_other = 2 * (chip ^ 1) + core, 2 * (chip ^ 2) + 1 - core
        to_core = send_mix((mix_ref.at[1 - core], gains_ref), mine, partner)
        a_x = send_mix((mix_ref.at[core], gains_ref), mine, near_x)
        a_y = send_mix((mix_ref.at[core], gains_ref), mine, near_y)
        for h in range(2):
            for i in range(4):
                up_ref[h, :, i * tile : (i + 1) * tile] = up_in[:, (2 * i + h) * tile : (2 * i + h + 1) * tile]
        up_core = send(up_ref.at[1 - core], block(up_out, mine * shard, shard), partner)
        out_core = send(outw_ref, block(outw_out, mine * shard, shard), partner)
        stays = [
            stay(mix_ref.at[core], mix_piece(mine)[0], 3),
            stay(gains_ref, gains_out.at[mine], 4),
            stay(up_ref.at[core], block(up_out, mine * shard, shard), 5),
            stay(outw_ref, block(outw_out, mine * shard, shard), 6),
        ]
        arrived(to_core)
        b_x = send_mix(mix_piece(theirs), theirs, near_x)
        b_y = send_mix(mix_piece(theirs), theirs, near_y)
        arrived(a_x)
        a_far = send_mix(mix_piece(x_mine), x_mine, near_y)
        arrived(b_y)
        b_far = send_mix(mix_piece(y_other), y_other, near_x)
        for copy in stays:
            copy.wait()
        arrived([up_core])
        ohalf = shard // 2

        def bundle(first, from_chip):
            same, twin = 2 * from_chip + core, 2 * from_chip + 1 - core
            part_of = 0 if first else 1
            return [
                block(up_out, (same if first else twin) * shard, shard),
                block(outw_out, same * shard + part_of * ohalf, ohalf),
            ]

        def send_bundle(first, from_chip, device):
            return [send(ref, ref, device) for ref in bundle(first, from_chip)]

        first_x = send_bundle(True, chip, near_x)
        first_y = send_bundle(True, chip, near_y)
        second_x = send_bundle(False, chip, near_x)
        second_y = send_bundle(False, chip, near_y)

    lens_copy.wait()
    lens_stay.wait()
    write_bounds(pics, lens_out, bounds_ref, zp, zq, length)
    if square:
        arrived(a_y + b_x + a_far + b_far)
        for p in range(gains_out.shape[0]):
            lanes = slice(p * shard, (p + 1) * shard)
            values = gains_out[p, :, :shard]
            gain_first[:, lanes] = values[0:1]
            second_ref[:, lanes] = values[3:4]
            half_pieces = gains_out.shape[0] // 2

            @pl.when(core == p // half_pieces)
            def _():
                at = (p % half_pieces) * shard
                gain_qk[:, at : at + shard] = values[1:2]
                gain_qk[:, width + at : width + at + shard] = values[2:3]
        weight = mix_out
    else:
        weight = weight_in
        width = weight.shape[1] // 3
        second_ref[...] = jnp.zeros_like(second_ref)
        gain_first[...] = gain_first_in[...]
        gain_qk[...] = gain_qk_in[...]
    writes = []

    def write(source, target, at):
        copy = pltpu.make_async_copy(source, target, write_sem.at[at])
        copy.start()
        writes.append(copy)

    write(weight, mix_hbm, 0)
    first, second = 2 * core + zq, 2 * core + 1 - zq
    other_first, other_second = 2 * (1 - core) + zq, 2 * (1 - core) + 1 - zq

    def forwarded(ref, index, at):
        return remote(quarter(ref, index), quarter(ref, index), sems, at, partner)

    def project(tokens, bufs, at):
        rows = rows_at(at * part, part)
        project_kernel(
            tokens.at[rows], gain_first, weight, gain_qk, bufs["normed"].at[rows], bufs["qk"].at[rows],
            bufs["v"].at[rows], bufs["raw"].at[rows],
        )

    def project_row(i, _):
        @pl.when(i == 0)
        def _():
            @pl.when(moves)
            def _():
                own_row.wait_recv()

            @pl.when(jnp.logical_not(moves))
            def _():
                stay_row.wait()

            forwarded(row_ref, first, 3).start()

        @pl.when(i == 1)
        def _():
            cross_row.wait_recv()
            forwarded(row_ref, second, 4).start()

        @pl.when(i == 2)
        def _():
            forwarded(row_ref, other_first, 3).wait_recv()

        @pl.when(i == 3)
        def _():
            forwarded(row_ref, other_second, 4).wait_recv()

        order = jnp.where(i == 0, first, jnp.where(i == 1, second, jnp.where(i == 2, other_first, other_second)))
        project(row_ref, scratch[0], order)
        return 0

    row_one, row_two = forwarded(row_ref, first, 3), forwarded(row_ref, second, 4)

    def attend(bufs, bounds):
        def one(p, _):
            lanes = pl.ds(pl.multiple_of(p * 128, 128), 128)
            attend_kernel(
                pics, bufs["qk"].at[:, lanes],
                bufs["qk"].at[:, pl.ds(pl.multiple_of(width + p * 128, 128), 128)], bufs["v"].at[:, lanes], bounds,
                bufs["out"].at[:, lanes], bufs["aug"].at[pl.ds(2 * p, 2)], kaug, vaug, qaug.at[pl.ds(0, bufs["out"].shape[0])],
            )
            return 0

        lax.fori_loop(0, width // 128, one, 0)

    lax.fori_loop(0, 4, project_row, 0)
    for i, name in enumerate(("normed", "qk", "v", "raw")):
        write(scratch[0][name], outs[0][name], 1 + i)
    write(row_ref.at[rows_at(core * half, half)], x_out.at[pl.ds(0, half)], 5)

    @pl.when(moves)
    def _():
        own_shared.wait_recv()

    @pl.when(jnp.logical_not(moves))
    def _():
        stay_shared.wait()

    to_side = remote(quarter(shared_ref, first), quarter(shared_ref, first), sems, 5, side)
    to_side.start()
    shared_one = remote(quarter(shared_ref, first), quarter(shared_ref, first), sems, 6, partner)
    shared_one.start()
    attend(scratch[0], bounds_ref.at[0])
    cot_moves = Moves(
        [remote(cot_ref.at[zq], cot_out, sems, 43, keep)],
        [pltpu.make_async_copy(cot_ref.at[zq], cot_out, local_sem.at[0])],
        None,
        moves,
    )
    cot_moves.start()
    write(scratch[0]["out"], outs[0]["out"], 6)
    write(scratch[0]["aug"], outs[0]["aug"], 7)
    to_side.wait_recv()
    shared_two = forwarded(shared_ref, second, 7)
    shared_two.start()
    if square:
        arrived(first_x + second_y)
        far_first = send_bundle(True, chip ^ 1, near_y)
        far_second = send_bundle(False, chip ^ 2, near_x)
    shared_one.wait_recv()
    shared_two.wait_recv()

    def project_shared(i, _):
        project(shared_ref, scratch[1], i)
        return 0

    lax.fori_loop(0, 4, project_shared, 0)
    for i, name in enumerate(("normed", "qk", "v", "raw")):
        write(scratch[1][name], outs[1][name], 8 + i)
    write(shared_ref.at[rows_at(first * part, part)], x_out.at[pl.ds(half, part)], 12)
    attend(scratch[1], bounds_ref.at[1])
    write(scratch[1]["out"], outs[1]["out"], 13)
    write(scratch[1]["aug"], outs[1]["aug"], 14)

    if square:
        arrived(first_y + second_x + far_first + far_second)
        sent_pieces = []
        for c in (chip ^ 1, chip ^ 2, chip ^ 3):
            target = block(outw_out, (2 * c + core) * shard, shard)
            sent_pieces.append(send(target, target, partner))
        write(up_out, up_hbm, 15)
        arrived(sent_pieces + [out_core])
        write(outw_out, outw_hbm, 17)
        for copy in waits:
            copy.wait_send()
    cot_moves.wait()
    write(cot_out, cot_hbm, 18)
    for copy in (row_one, row_two, shared_one, shared_two, to_side, cross_row):
        copy.wait_send()

    @pl.when(moves)
    def _():
        own_row.wait_send()
        own_shared.wait_send()

    for copy in writes:
        copy.wait()


def forward_pass(square, pics, tokens, cotangent, lengths, weight, *more):
    _, part, model = tokens.shape
    length, half, width = 4 * part, 2 * part, model // 2
    near = pl.BlockSpec(memory_space=pltpu.VMEM)
    anywhere = pl.BlockSpec(memory_space=pl.ANY)
    low = lambda *shape: (shape, BF16)
    wide = lambda *shape: (shape, F32)
    outs = [
        (low(3 * part, model), anywhere),
        (((2, 8, 128), jnp.int32), near),
        (low(model, 3 * width), anywhere),
        (low(part, model), anywhere),
        (wide(1, model), near),
        (wide(1, model), near),
        (wide(1, model), near),
    ]
    bufs = []
    for queries in (length, half):
        shapes = [
            low(length, model), low(length, 2 * width), low(length, width), low(length, 2 * width),
            low(queries, width), low(2 * (width // 128), queries, 128),
        ]
        outs += [(shape, anywhere) for shape in shapes]
        bufs += shapes
    table = ((8, 128), jnp.int32)
    scratch = [low(length, model), low(length, model), low(part, model), table, ((2, 8, 128), jnp.int32)] + bufs
    scratch += [low(2, length, 128), low(2, length, 128), low(length, 128)]
    if square:
        up, _ = more[4:]
        shard, hidden = up.shape
        landed = [low(model, hidden // 2), low(model, model)]
        outs += [(shape, anywhere) for shape in landed]
        scratch += [low(2, shard, 3 * width), wide(8, 128), low(2, shard, hidden // 2)]
        scratch += [low(model, 3 * width), wide(8, 8, 128)] + landed
    return pl.pallas_call(
        functools.partial(forward_kernel, square, pics),
        in_specs=[near] * (4 + len(more)),
        out_specs=[spec for _, spec in outs],
        out_shape=[jax.ShapeDtypeStruct(*shape) for shape, _ in outs],
        scratch_shapes=[pltpu.VMEM(*shape) for shape in scratch]
        + [
            pltpu.SemaphoreType.DMA((49,)),
            pltpu.SemaphoreType.DMA((49,)),
            pltpu.SemaphoreType.DMA((8,)),
            pltpu.SemaphoreType.DMA((19,)),
        ],
        compiler_params=pltpu.CompilerParams(
            collective_id=0, has_side_effects=True, vmem_limit_bytes=60 * 1024 * 1024
        ),
        name="forward_pass",
    )(tokens, cotangent, lengths, weight, *more)


def dense_kernel(
    square, out_ref, shared_ref, x, grad_ref, cot_ref, outw_ref, gain_ref, bounds_ref, up_ref, down_ref,
    output_ref, midg_ref, row_grad, shared_grad, outg_ref, gaing_ref, packed_ref, far_ref,
    att_other, second, turned, grad, cot_in, hidden_all, pre_all, forward, backward, middle, up, down,
    results, parts_out, parts_in, heads_out, cols_out, cols_in, stage, far_in,
    sent, got, load_sem, write_sem, local_sem,
):
    chip, core, zp, zq = here()
    sems = (sent, got)
    partner = (chip, 1 - core, zp, zq)
    keep = (chip, zp, core, zq)
    cross = (chip, zp, core, 1 - zq)
    moves = core != zp
    near_x = (chip ^ 1, core, zp, zq)
    near_y = (chip ^ 2, core, zp, zq)
    tokens, model = midg_ref.shape
    part = tokens // 3
    half = 2 * part
    width = out_ref.shape[1]
    units = up.shape[1]
    tile = units // 4
    other = 1 - core
    mine, theirs = pl.ds(0, tokens), pl.ds(tokens, tokens)
    own_down = down.at[rows_at(chip * tile, tile)] if square else down
    loads = [
        pltpu.make_async_copy(up_ref, up, load_sem.at[0]),
        pltpu.make_async_copy(down_ref, own_down, load_sem.at[1]),
    ]
    for copy in loads:
        copy.start()
    greet([partner, cross] + ([near_x, near_y] if square else []), keep, moves)
    att_sends = [
        remote(out_ref.at[rows_at(other * half, half)], att_other.at[pl.ds(0, half)], sems, 0, partner),
        remote(shared_ref.at[rows_at(other * part, part)], att_other.at[pl.ds(half, part)], sems, 1, partner),
    ]
    for copy in att_sends:
        copy.start()
    cot_move = Moves(
        [remote(cot_ref.at[2], cot_in.at[1], sems, 11, keep)],
        [pltpu.make_async_copy(cot_ref.at[2], cot_in.at[1], local_sem.at[0])],
        remote(cot_ref.at[1 - zq], cot_in.at[0], sems, 22, cross),
        moves,
    )
    cot_move.start()

    def down_half(index, which):
        return down.at[rows_at(index * tile + which * (tile // 2), tile // 2)]

    def send_down(index, which, at, device):
        copy = remote(down_half(index, which), down_half(index, which), sems, at, device)
        copy.start()
        return copy

    slot = lax.broadcasted_iota(jnp.int32, (part, 1), 0)
    filled, shared_filled = bounds_ref[0, 3:4, 0:1], bounds_ref[1, 3:4, 0:1]
    none = jnp.zeros((), BF16)

    def take_grad(values, at, start, limit, sem):
        rows = rows_at(at, part)
        grad[rows, :] = jnp.where(slot + start < limit, values, none)
        copy = remote(grad.at[rows], grad.at[rows_at(tokens + at, part)], sems, sem, partner)
        copy.start()
        return copy

    grad_sends = [take_grad(grad_ref[...], zq * part, (2 * core + zq) * part, filled, 2)]

    own_rows_of = lambda b: (
        out_ref[rows_at(core * half + b * part, part), :] if b < 2 else shared_ref[rows_at(core * part, part), :]
    )
    own_weight = outw_ref[rows_at(core * width, width), :]
    other_weight = outw_ref[rows_at(other * width, width), :]
    blocks = [pl.ds(b * part, part) for b in range(3)]
    for b in range(3):
        middle[blocks[b], :] = x[blocks[b], :].astype(F32) + jnp.dot(
            own_rows_of(b), own_weight, preferred_element_type=F32
        )
    for copy in loads:
        copy.wait()
    if square:
        down_sends = [
            send_down(chip, 0, 12, near_x), send_down(chip, 1, 13, near_y), send_down(chip, 0, 14, near_y),
            send_down(chip, 1, 15, near_x),
        ]
    for copy in att_sends:
        copy.wait_recv()
    for rows in blocks:
        value = middle[rows, :] + jnp.dot(att_other[rows, :], other_weight, preferred_element_type=F32)
        middle[rows, :] = value
        second[rows, :] = (norm_parts(value)[0] * gain_ref[...]).astype(BF16)
    second_send = remote(second.at[mine], second.at[theirs], sems, 3, partner)
    second_send.start()

    def hidden_forward(start):
        rows = pl.ds(start, tokens)

        def one_tile(i, _):
            here_units = pl.ds(pl.multiple_of(i * tile, 128), tile)
            hidden, slope = gelu_pair(jnp.dot(second[rows, :], up[:, here_units], preferred_element_type=F32))
            hidden_all[rows, here_units] = hidden.astype(BF16)
            pre_all[rows, here_units] = slope.astype(BF16)
            return 0

        lax.fori_loop(0, 4, one_tile, 0)

    def hidden_backward(start):
        rows = pl.ds(start, tokens)

        def one_tile(i, _):
            here_units = pl.ds(pl.multiple_of(i * tile, 128), tile)
            pre_grad = nt(grad[rows, :], down[rows_at(i * tile, tile), :]) * pre_all[rows, here_units].astype(F32)
            pre_all[rows, here_units] = pre_grad.astype(BF16)
            return 0

        lax.fori_loop(0, 4, one_tile, 0)

    hidden_forward(0)
    if square:
        down_sends[0].wait_recv()
        down_sends[1].wait_recv()
        down_sends += [send_down(chip ^ 1, 0, 16, near_y), send_down(chip ^ 2, 1, 17, near_x)]
    second_send.wait_recv()
    hidden_forward(tokens)
    if square:
        for copy in down_sends[2:]:
            copy.wait_recv()
    for b in range(3):
        rows, there = pl.ds(tokens + b * part, part), blocks[b]
        parts_out[0, there, :] = jnp.dot(hidden_all[rows, :], down[...], preferred_element_type=F32).astype(BF16)
    first_part = remote(parts_out.at[0], parts_in.at[0], sems, 4, partner)
    first_part.start()
    for rows in blocks:
        forward[rows, :] = middle[rows, :] + jnp.dot(hidden_all[rows, :], down[...], preferred_element_type=F32)
    first_part.wait_recv()
    for rows in blocks:
        results[rows, :] = (forward[rows, :] + parts_in[0, rows, :].astype(F32)).astype(BF16)
    kept_rows, third_rows = results.at[rows_at(zq * part, part)], results.at[pl.ds(half, part)]
    output_moves = Moves(
        [
            remote(kept_rows, output_ref.at[zq], sems, 19, keep),
            remote(third_rows, output_ref.at[2], sems, 20, keep),
        ],
        [
            pltpu.make_async_copy(kept_rows, output_ref.at[zq], local_sem.at[1]),
            pltpu.make_async_copy(third_rows, output_ref.at[2], local_sem.at[2]),
        ],
        remote(results.at[rows_at((1 - zq) * part, part)], output_ref.at[zq], sems, 21, cross),
        moves,
    )
    output_moves.start()
    cot_move.wait()
    grad_sends.append(take_grad(cot_in[0], (1 - zq) * part, (2 * core + 1 - zq) * part, filled, 18))
    grad_sends.append(take_grad(cot_in[1], half, (2 * core + zq) * part, shared_filled, 23))
    hidden_backward(0)
    for copy in grad_sends:
        copy.wait_recv()
    hidden_backward(tokens)
    for b in range(3):
        rows, there = pl.ds(tokens + b * part, part), blocks[b]
        parts_out[1, there, :] = nt(pre_all[rows, :], up[...]).astype(BF16)
    second_part = remote(parts_out.at[1], parts_in.at[1], sems, 5, partner)
    second_part.start()
    for rows in blocks:
        backward[rows, :] = nt(pre_all[rows, :], up[...])

    turned[...] = second[...].T
    quarter = model // 4
    far_sends = [
        remote(stage.at[0, pl.ds(0, tile)], far_in.at[0], sems, 9, near_y),
        remote(stage.at[0, pl.ds(tile, tile)], far_in.at[1], sems, 10, near_x),
    ]

    def weight_grads(i, _):
        target = chip ^ (3 - i) if square else 3 - i
        place = jnp.where(i == 0, 0, 1 + i % 2)

        @pl.when(i == 3)
        def _():
            pltpu.make_async_copy(stage.at[place], packed_ref.at[target], write_sem.at[place]).wait()

        here_units = pl.ds(pl.multiple_of(target * tile, 128), tile)
        stage[place, pl.ds(0, tile), :] = tn(hidden_all[:, here_units], grad[...]).astype(BF16)
        values = jnp.dot(
            turned[rows_at(target * quarter, quarter), :], pre_all[...], preferred_element_type=F32
        ).astype(BF16)
        for j in range(2):
            stage[place, pl.ds(tile + j * quarter, quarter), :] = values[:, j * model : (j + 1) * model]
        pltpu.make_async_copy(stage.at[place], packed_ref.at[target], write_sem.at[place]).start()
        if square:

            @pl.when(i == 0)
            def _():
                for copy in far_sends:
                    copy.start()

        return 0

    lax.fori_loop(0, 4, weight_grads, 0)

    second_send.wait_send()
    second_part.wait_recv()
    gain_sum = jnp.zeros(gaing_ref.shape, F32)
    for rows in blocks:
        n, r = norm_parts(middle[rows, :])
        upstream = backward[rows, :] + parts_in[1, rows, :].astype(F32)
        more, gain_more = norm_back(upstream, n, r, gain_ref[...])
        gain_sum = gain_sum + gain_more
        value = grad[rows, :].astype(F32) + more
        midg_ref[rows, :] = value
        branch = value.astype(BF16)
        second[rows, :] = branch
        heads_out[rows, :] = nt(branch, other_weight).astype(BF16)
    gaing_ref[...] = gain_sum
    head_sends = [
        remote(heads_out.at[pl.ds(0, half)], row_grad.at[rows_at(core * half, half)], sems, 6, partner),
        remote(heads_out.at[pl.ds(half, part)], shared_grad.at[rows_at(core * part, part)], sems, 7, partner),
    ]
    for copy in head_sends:
        copy.start()
    branch = second[mine, :]
    forward[rows_at(core * width, width), :] = tn(
        out_ref[rows_at(core * half, half), :], second[pl.ds(0, half), :]
    ) + tn(shared_ref[rows_at(core * part, part), :], second[pl.ds(half, part), :])
    forward[rows_at(other * width, width), :] = tn(att_other[...], branch)
    lanes = lambda side: pl.ds(pl.multiple_of(side * width, 128), width)
    cols_out[...] = forward[pl.ds(0, model), lanes(other)].astype(BF16)
    cols_send = remote(cols_out, cols_in, sems, 8, partner)
    cols_send.start()
    for b in range(3):
        value = nt(second[blocks[b], :], own_weight).astype(BF16)
        if b < 2:
            row_grad[rows_at(core * half + b * part, part), :] = value
        else:
            shared_grad[rows_at(core * part, part), :] = value
    cols_send.wait_recv()
    outg_ref[...] = (forward[pl.ds(0, model), lanes(core)] + cols_in[...].astype(F32)).astype(BF16)
    for copy in head_sends:
        copy.wait_recv()
    for copy in att_sends + head_sends + grad_sends + [first_part, second_part, cols_send]:
        copy.wait_send()
    if square:
        for copy in down_sends:
            copy.wait_send()
        for copy in far_sends:
            copy.wait()
    far_write = pltpu.make_async_copy(far_in, far_ref, load_sem.at[0])
    far_write.start()
    for place in range(3):
        pltpu.make_async_copy(stage.at[place], packed_ref.at[0], write_sem.at[place]).wait()
    output_moves.wait()
    far_write.wait()


def dense(square, out, shared_out, x, grad, cotangent, out_matrix, gain, bounds, up, down):
    model = x.shape[1]
    tokens = x.shape[0]
    part = tokens // 3
    length, width = out.shape
    units = up.shape[1]
    tile = units // 4
    anywhere = pl.BlockSpec(memory_space=pl.ANY)
    near = pl.BlockSpec(memory_space=pltpu.VMEM)
    both = 2 * tokens
    low = lambda *shape: pltpu.VMEM(shape, BF16)
    wide = lambda *shape: pltpu.VMEM(shape, F32)
    return pl.pallas_call(
        functools.partial(dense_kernel, square),
        in_specs=[near] * 4 + [anywhere] + [near] * 3 + [anywhere] * 2,
        out_specs=[anywhere] + [near] * 5 + [anywhere, anywhere],
        out_shape=[
            jax.ShapeDtypeStruct((3, part, model), BF16),
            jax.ShapeDtypeStruct((tokens, model), F32),
            jax.ShapeDtypeStruct((length, width), BF16),
            jax.ShapeDtypeStruct((length // 2, width), BF16),
            jax.ShapeDtypeStruct((model, width), BF16),
            jax.ShapeDtypeStruct((1, model), F32),
            jax.ShapeDtypeStruct((4, 2 * tile, model), BF16),
            jax.ShapeDtypeStruct((2, tile, model), BF16),
        ],
        scratch_shapes=[
            low(tokens, width), low(both, model), low(model, both), low(both, model), low(2, part, model),
            low(both, units), low(both, units), wide(tokens, model), wide(tokens, model), wide(tokens, model),
            low(model, units), low(units, model), low(tokens, model), low(2, tokens, model), low(2, tokens, model),
            low(tokens, width), low(model, width), low(model, width), low(3, 2 * tile, model), low(2, tile, model),
            pltpu.SemaphoreType.DMA((24,)),
            pltpu.SemaphoreType.DMA((24,)),
            pltpu.SemaphoreType.DMA((2,)),
            pltpu.SemaphoreType.DMA((3,)),
            pltpu.SemaphoreType.DMA((3,)),
        ],
        compiler_params=pltpu.CompilerParams(
            collective_id=1, has_side_effects=True, vmem_limit_bytes=63 * 1024 * 1024
        ),
        name="dense",
    )(out, shared_out, x, grad, cotangent, out_matrix, gain, bounds, up, down)


def add(*terms):
    total = terms[0].astype(F32)
    for term in terms[1:]:
        total = total + term.astype(F32)
    return total


def backward_kernel(square, pics, *refs):
    refs = list(refs)
    take = lambda count: [refs.pop(0) for _ in range(count)]
    names = ("aug", "qk", "v", "out", "do", "raw", "normed")
    row_in = dict(zip(names, take(7)))
    shared_in = dict(zip(names, take(7)))
    mix_in, x_in, midg_in, gain_first, gain_qk, gain_second_grad, bounds_ref = take(7)
    if square:
        packed_in, far_ref, outg_in = take(3)
        grad_out, total_ref, gains_ref, up_ref, down_ref, outw_ref = take(6)
    else:
        grad_own, mix_grad_ref, gains_sum = take(3)
    names = names[:-1]
    row = dict(zip(names, take(6)))
    shared = dict(zip(names, take(6)))
    normed, turned, weight, midg = take(4)
    if not square:
        x = take(1)[0]
    kaug, vaug, doaug, qsum, ksum, mixed, part_k, part_v, got_k, got_v = take(10)
    gain_sums, parts_in = take(2)
    if square:
        gains_sum, outg = take(2)
        held, direct_out, far_in, onward_in, direct_in, line, whole_line, line_right, line_left = take(9)
        up_out, up_got = take(2)
        planes = [take(4) for _ in range(3)]
        lines = [take(4), take(3)]
        gain_part, gain_got = take(2)
    sent, got, load_sem, local_sem = take(4)

    chip, core, zp, zq = here()
    z = 2 * zp + zq
    sems = (sent, got)
    partner = (chip, 1 - core, zp, zq)
    keep = (chip, zp, core, zq)
    cross = (chip, zp, core, 1 - zq)
    moves = core != zp
    near_x = (chip ^ 1, core, zp, zq)
    near_y = (chip ^ 2, core, zp, zq)
    along = [(chip, core, zp, 1 - zq), (chip, core, 1 - zp, zq), (chip, core, 1 - zp, 1 - zq)]
    tokens, model = midg.shape
    part = tokens // 3
    half, length = 2 * part, 4 * part
    width = model // 2
    queries = half
    waits = []

    def load(source, target, at):
        copy = pltpu.make_async_copy(source, target, load_sem.at[at])
        copy.start()
        return copy

    def send(source, target, at, device):
        copy = remote(source, target, sems, at, device)
        copy.start()
        waits.append(copy)
        return copy

    if square:
        rows_count = packed_in.shape[1]
        span = rows_count // 2
        first_half, second_half = pl.ds(0, span), pl.ds(span, span)
        held_loads = [
            load(packed_in.at[chip ^ 1, first_half], held.at[0], 24),
            load(packed_in.at[chip ^ 2, second_half], held.at[1], 25),
            load(packed_in.at[chip, first_half], held.at[2], 26),
            load(packed_in.at[chip, second_half], held.at[3], 27),
            load(packed_in.at[chip ^ 1, second_half], direct_out.at[0], 18),
            load(packed_in.at[chip ^ 2, first_half], direct_out.at[1], 19),
        ]
        far_loads = [load(far_ref.at[i], far_in.at[i], 28 + i) for i in range(2)]
    keys_of = lambda ref: ref.at[:, pl.ds(width, width)]
    load_bufs = lambda source, target, at: [
        load(keys_of(source[name]) if name == "qk" else source[name], target[name], at + i)
        for i, name in enumerate(names)
    ]
    shared_loads = load_bufs(shared_in, shared, 0)
    row_loads = load_bufs(row_in, row, 6)
    late_loads = [
        load(row_in["normed"], normed.at[pl.ds(0, length)], 12),
        load(shared_in["normed"].at[rows_at(zq * part, part)], normed.at[pl.ds(length, part)], 13),
        load(
            shared_in["normed"].at[rows_at((2 + zq) * part, part)], normed.at[pl.ds(length + part, part)], 14
        ),
        load(mix_in, weight, 15),
        load(midg_in, midg, 17),
    ]
    late_loads.append(load(outg_in, outg, 20) if square else load(x_in, x, 16))
    if square:
        greet([partner, cross, near_x, near_y] + along, keep, moves)
        for copy in held_loads + far_loads:
            copy.wait()
        far_in[0] = add(far_in[0], held[0]).astype(BF16)
        bulk_on_x = remote(far_in.at[0], onward_in.at[0], sems, 11, near_x)
        bulk_on_x.start()
        far_in[1] = add(far_in[1], held[1]).astype(BF16)
        bulk_on_y = remote(far_in.at[1], onward_in.at[1], sems, 12, near_y)
        bulk_on_y.start()
        bulk_x = send(direct_out.at[0], direct_in.at[0], 2, near_x)
        bulk_y = send(direct_out.at[1], direct_in.at[1], 3, near_y)

        bulk_line = Line(line, whole_line, line_right, line_left, sems, 14)
        plane_a, plane_b, plane_gains = (
            PlaneSum(*refs_of, sems, 26 + 7 * i, waits) for i, refs_of in enumerate(planes)
        )
        line_a = Line(*lines[0], sems, 47)
        across_b = Across(*lines[1], sems, 59, waits)
    else:
        greet([partner, along[0]])

    gain_sums[...] = jnp.zeros_like(gain_sums)

    pairs = width // 128

    def attend_back(bufs, bounds, count, q_lanes_to, k_to, v_to, at, span=(0, pairs)):
        def one(p, _):
            lanes = pl.ds(pl.multiple_of(p * 128, 128), 128)
            key_lanes = pl.ds(pl.multiple_of(width + p * 128, 128), 128)
            attend_back_kernel(
                pics, bufs["aug"].at[pl.ds(2 * p, 2)], bufs["qk"].at[:, lanes], bufs["v"].at[:, lanes],
                bufs["out"].at[:, lanes], bufs["do"].at[:, lanes], bufs["raw"].at[:, lanes],
                bufs["raw"].at[:, key_lanes], gain_qk.at[:, lanes], gain_qk.at[:, key_lanes], bounds,
                q_lanes_to(p), k_to(p), v_to(p), gain_sums.at[pl.ds(at, 1), lanes], gain_sums.at[pl.ds(at + 1, 1), lanes],
                kaug, vaug, doaug.at[:, pl.ds(0, count)], qsum.at[:, pl.ds(0, count)], ksum,
            )
            return 0

        lax.fori_loop(span[0], span[1], one, 0)

    def mixed_at(start, count, side):
        return lambda p: mixed.at[pl.ds(start, count), pl.ds(pl.multiple_of(side * width + p * 128, 128), 128)]

    whole_lanes = lambda ref: lambda p: ref.at[:, pl.ds(pl.multiple_of(p * 128, 128), 128)]
    for copy in shared_loads:
        copy.wait()
    attend_back(
        shared, bounds_ref.at[1], queries, mixed_at(length, queries, 0), whole_lanes(part_k), whole_lanes(part_v), 0
    )
    side_sends = []
    for i in range(2):
        theirs = rows_at((2 * i + 1 - zq) * part, part)
        there = pl.ds(i * part, part)
        side_sends.append(send(part_k.at[theirs], got_k.at[there], 7 + 2 * i, along[0]))
        side_sends.append(send(part_v.at[theirs], got_v.at[there], 8 + 2 * i, along[0]))
    for copy in row_loads + late_loads:
        copy.wait()
    turned[...] = normed[...].T
    parts_out = normed.at[pl.ds(0, tokens)]
    if square:
        grad_own = normed.at[pl.ds(tokens, tokens)]
    shard = model // 8
    other = 1 - core
    row_to = (mixed_at(0, length, 0), mixed_at(0, length, 1), mixed_at(0, length, 2), 2)
    attend_back(row, bounds_ref.at[0], length, *row_to, (0, pairs - 1))
    if square:
        quarter_rows = rows_count // 4
        for copy in (bulk_y, bulk_on_x, bulk_x, bulk_on_y):
            copy.wait_recv()
        bulk_on_x.wait_send()
        bulk_on_y.wait_send()
        x_loads = [load(x_in.at[pl.ds(i * span, span)], far_in.at[i], 16 + 5 * i) for i in range(2)]
        first_sum = add(held[2], onward_in[0], direct_in[1]).astype(BF16)
        second_half_sum = add(held[3], onward_in[1], direct_in[0]).astype(BF16)
        for i in range(2):
            line[i] = first_sum[i * quarter_rows : (i + 1) * quarter_rows]
            line[2 + i] = second_half_sum[i * quarter_rows : (i + 1) * quarter_rows]
        bulk_line.start()

    for copy in side_sends:
        copy.wait_recv()

    def shared_pair(p, _):
        lanes = pl.ds(pl.multiple_of(p * 128, 128), 128)
        key_lanes = pl.ds(pl.multiple_of(width + p * 128, 128), 128)
        shared_keys_kernel(
            part_k.at[:, lanes], part_v.at[:, lanes], got_k.at[:, lanes], got_v.at[:, lanes],
            shared["raw"].at[:, key_lanes], gain_qk.at[:, key_lanes], mixed_at(length, queries, 1)(p),
            mixed_at(length, queries, 2)(p), gain_sums.at[pl.ds(4, 1), lanes],
        )
        return 0

    lax.fori_loop(0, pairs, shared_pair, 0)

    def mix_gradient(start, count, payload):
        for t in range(3):
            lanes = slice(t * width + start, t * width + start + count)
            value = jnp.dot(turned[...], mixed[:, lanes], preferred_element_type=F32).astype(BF16)
            if payload is None:
                mix_grad_ref[:, lanes] = value
                continue
            for p in range(8):
                payload[p, :shard, t * count : (t + 1) * count] = value[p * shard : (p + 1) * shard]

    early = width - 128
    mix_gradient(0, early, plane_a.payload if square else None)
    if square:
        outs_end = shard + shard // 2
        for p in range(8):
            for i in range(2):
                at = p * shard + i * (shard // 2)
                plane_a.payload[p, shard:outs_end, i * width : (i + 1) * width] = outg[at : at + shard // 2, :]
            plane_a.payload[p, outs_end:, :] = jnp.zeros((16, 3 * early), BF16)
        plane_a.start()
        bulk_line.first()
    attend_back(row, bounds_ref.at[0], length, *row_to, (pairs - 1, pairs))
    block_rows = lambda side, b: (
        rows_at(side * half + b * part, part) if b < 2 else rows_at(length + side * part, part)
    )
    for b in range(3):
        parts_out[pl.ds(b * part, part), :] = nt(mixed[block_rows(other, b), :], weight[...]).astype(BF16)
    part_send = send(parts_out, parts_in, 13, partner)
    if square:
        plane_a.pass_on()
        bulk_line.second()
    mix_gradient(early, 128, plane_b.payload if square else None)
    if square:
        plane_b.start()
    part_send.wait_recv()
    if square:
        for copy in x_loads:
            copy.wait()
        own_x = [
            far_in[0, :part],
            jnp.concatenate([far_in[0, part:], far_in[1, : half - span]], axis=0),
            far_in[1, half - span :],
        ]
    else:
        own_x = [x[pl.ds(b * part, part), :] for b in range(3)]
    first_sum_gain = jnp.zeros((1, model), F32)
    for b in range(3):
        rows = pl.ds(b * part, part)
        upstream = nt(mixed[block_rows(core, b), :], weight[...]) + parts_in[rows, :].astype(F32)
        n, r = norm_parts(own_x[b].astype(F32))
        value, more = norm_back(upstream, n, r, gain_first[...])
        first_sum_gain = first_sum_gain + more
        grad_own[rows, :] = (midg[rows, :] + value).astype(BF16)
    gains_sum[...] = jnp.zeros_like(gains_sum)
    gains_sum[0:1, :] = first_sum_gain
    mine_lanes = pl.ds(pl.multiple_of(core * width, 128), width)
    gains_sum[1:2, mine_lanes] = gain_sums[0:1, :] + gain_sums[2:3, :]
    gains_sum[2:3, mine_lanes] = gain_sums[3:4, :] + gain_sums[4:5, :]
    gains_sum[3:4, :] = gain_second_grad[...]

    if square:
        kept_rows, third_rows = grad_own.at[rows_at(zq * part, part)], grad_own.at[pl.ds(half, part)]
        grad_moves = [
            Moves(
                [remote(kept_rows, grad_out.at[zq], sems, 0, keep)],
                [pltpu.make_async_copy(kept_rows, grad_out.at[zq], local_sem.at[0])],
                None,
                moves,
            ),
            Moves(
                [remote(third_rows, grad_out.at[2], sems, 1, keep)],
                [pltpu.make_async_copy(third_rows, grad_out.at[2], local_sem.at[1])],
                None,
                moves,
            ),
        ]
        grad_cross = remote(grad_own.at[rows_at((1 - zq) * part, part)], grad_out.at[zq], sems, 4, cross)
        grad_cross.start()
        for p in range(8):
            plane_gains.payload[p] = jnp.zeros((16, 128), BF16)
            plane_gains.payload[p, :, :shard] = gains_sum[:, p * shard : (p + 1) * shard].astype(BF16)
        plane_gains.start()

        def to_line(plane, target):
            kept = plane.finish()
            rows = target.parts.shape[1]
            for i in range(2):
                target.parts[2 * core + i] = kept[i * rows : (i + 1) * rows].astype(BF16)
                target.parts[2 * (1 - core) + i] = plane.came[i * rows : (i + 1) * rows]
            target.start()

        plane_a.to_core()
        bulk_line.third()
        plane_b.pass_on()
        to_line(plane_a, line_a)
        plane_gains.pass_on()
        bulk_line.fourth()
        line_a.first()
        plane_b.to_core()
        plane_gains.to_core()
        line_a.second()
        to_line(plane_b, across_b)
        grad_moves[0].start()
        gain_part[...] = (plane_gains.finish() + plane_gains.came[...].astype(F32)).astype(BF16)
        gain_sends = [send(gain_part, gain_got.at[i], 71 + i, along[i]) for i in range(3)]
        bulk_line.fifth()
        line_a.third()
        across_b.total()
        line_a.fourth()
        bulk_line.sixth()
        grad_moves[1].start()

        flat = jnp.concatenate([whole_line[i] for i in range(4)], axis=0)
        tile = down_ref.shape[0]
        ups = [flat[tile + 2 * shard * i : tile + 2 * shard * (i + 1)] for i in range(2)]
        for i in range(2):
            up_out[i] = jnp.where(core == 0, ups[i][shard:], ups[i][:shard])
        up_send = send(up_out, up_got, 74, partner)
        line_a.fifth()
        across_b.finish()
        down_ref[...] = flat[:tile]

        def place_up(side, i, values):
            for j in range(2):
                lanes = pl.ds(pl.multiple_of((2 * (2 * i + j) + side) * tile, 128), tile)
                up_ref[:, lanes] = values[:, j * tile : (j + 1) * tile]

        for i in range(2):
            place_up(core, i, jnp.where(core == 0, ups[i][:shard], ups[i][shard:]))
        line_a.sixth()
        up_send.wait_recv()
        for i in range(2):
            place_up(other, i, up_got[i])

        def place(target, start, count):
            for index in range(4):
                side, low_half = index // 2, index % 2
                values = target.whole[index]
                rows = values.shape[0]
                first_row = low_half * rows
                taken = min(rows, shard - first_row)
                for t in range(3):
                    lanes = slice((2 * t + side) * width + start, (2 * t + side) * width + start + count)
                    total_ref[first_row : first_row + taken, lanes] = values[:taken, t * count : (t + 1) * count]
                if taken < rows:
                    for i in range(2):
                        outw_ref[i * (shard // 2) : (i + 1) * (shard // 2), side * width : (side + 1) * width] = values[
                            taken : taken + shard // 2, i * width : (i + 1) * width
                        ]

        place(line_a, 0, early)
        for copy in gain_sends:
            copy.wait_recv()
        gains_ref[...] = add(gain_part[...], gain_got[0], gain_got[1], gain_got[2])
        place(across_b, early, 128)
        for target in (bulk_line, line_a):
            target.wait_sends()
        grad_cross.wait()
        for copy in grad_moves:
            copy.wait()
    for copy in waits:
        copy.wait_send()


def backward_pass(square, pics, row, shared, weights, gains, bounds, *more):
    length, model = row[1].shape
    width = model // 2
    part = length // 4
    half, tokens = 2 * part, 3 * part
    shard = model // 8
    near = pl.BlockSpec(memory_space=pltpu.VMEM)
    anywhere = pl.BlockSpec(memory_space=pl.ANY)
    low = lambda *shape: (shape, BF16)
    wide = lambda *shape: (shape, F32)
    if square:
        rows = more[0].shape[1]
        tile = rows // 2
        outs = [
            (low(3, part, model), anywhere),
            (low(shard, 6 * width), near),
            (wide(16, 128), near),
            (low(shard, 8 * tile), near),
            (low(tile, model), near),
            (low(shard, model), near),
        ]
    else:
        outs = [
            (low(tokens, model), near),
            (low(model, 3 * width), near),
            (wide(16, model), near),
        ]
    scratch = []
    for queries in (length, half):
        scratch += [
            low(2 * (width // 128), queries, 128), low(length, width), low(length, width), low(queries, width),
            low(queries, width), low(length, 2 * width),
        ]
    scratch += [
        low(length + half, model), low(model, length + half), low(model, 3 * width), wide(tokens, model),
        *([] if square else [low(tokens, model)]),
        low(2, length, 128), low(2, length, 128), low(2, length, 128), wide(2, length, 128), wide(length, 128),
        low(length + half, 3 * width), low(length, width), low(length, width), low(half, width), low(half, width),
        wide(8, width), low(tokens, model),
    ]
    if square:
        span = rows // 2
        early = 3 * (width - 128)
        plane = lambda count, columns: [
            low(8, count, columns), low(5, count, columns), low(4, count, columns), low(count, columns)
        ]
        chunked = lambda count, columns, slots: [low(size, count, columns) for size in (4, 4) + slots]
        early_rows = shard + shard // 2 + 16
        scratch += [
            wide(16, model), low(model, width),
            low(4, span, model), low(2, span, model), low(2, span, model), low(2, span, model), low(2, span, model),
            low(4, rows // 4, model), low(4, rows // 4, model), low(3, rows // 4, model), low(3, rows // 4, model),
            low(2, shard, model), low(2, shard, model),
            *plane(early_rows, early), *plane(shard, 3 * 128), *plane(16, 128),
            *chunked(early_rows // 2, early, (3, 3)), *chunked(shard // 2, 3 * 128, (3,)), low(16, 128), low(3, 16, 128),
        ]
    return pl.pallas_call(
        functools.partial(backward_kernel, square, pics),
        in_specs=[anywhere] * 17 + [near] * 4 + [anywhere] * len(more),
        out_specs=[spec for _, spec in outs],
        out_shape=[jax.ShapeDtypeStruct(*shape) for shape, _ in outs],
        scratch_shapes=[pltpu.VMEM(*shape) for shape in scratch]
        + [
            pltpu.SemaphoreType.DMA((75,)),
            pltpu.SemaphoreType.DMA((75,)),
            pltpu.SemaphoreType.DMA((30,)),
            pltpu.SemaphoreType.DMA((3,)),
        ],
        compiler_params=pltpu.CompilerParams(
            collective_id=2, has_side_effects=True, vmem_limit_bytes=63 * 1024 * 1024
        ),
        name="backward_pass",
    )(*row, *shared, *weights, *gains, bounds, *more)


def local(
    tokens, lengths, pictures, first_gain, mix_weight, query_gain, key_gain, out_weight,
    second_gain, up_weight, down_weight, cotangent,
):
    chip, core, zp, zq = here()
    chips = lax.axis_size("chip")
    square = chips == 4
    rows = ("chip", "core")
    _, part, model = tokens.shape
    length = 4 * part
    half = 2 * part
    width = HEADS // 2 * HEAD
    pics = lengths.shape[1]
    shard = mix_weight.shape[0]

    hidden = up_weight.shape[1]
    tile = hidden // 8
    gains = [gain[None] for gain in (first_gain, query_gain, key_gain, second_gain)]
    if square:
        forward = forward_pass(
            True, pics, tokens, cotangent, lengths, mix_weight, *gains, up_weight, out_weight
        )
        up_half, out_matrix = forward[19:]
        down_half = down_weight
        gain_second = forward[5]
    else:
        gather = lambda weight: lax.all_gather(weight, rows, axis=0, tiled=True)
        half_of = lambda weight, axis: pick(weight, core, axis)
        mix_half = half_of(gather(mix_weight).reshape(model, 3, 2, width), 2).reshape(model, 3 * width)
        up_half = half_of(gather(up_weight).reshape(model, 4, 2, tile), 2).reshape(model, 4 * tile)
        down_half = half_of(gather(down_weight).reshape(4, 2, tile, model), 1).reshape(4 * tile, model)
        out_matrix = gather(out_weight)
        gains = lax.all_gather(jnp.concatenate(gains), rows, axis=0, tiled=False)
        gains = gains.transpose(1, 0, 2).reshape(4, 1, model).astype(F32)
        gain_second = gains[3]
        gain_qk = half_of(gains[1:3].reshape(2, 2, width), 1).reshape(1, model)
        forward = forward_pass(False, pics, tokens, cotangent, lengths, mix_half, gains[0], gain_qk)
    own_tokens, bounds, mix_half, grad_tokens, gain_first, _, gain_qk = forward[:7]
    normed, qk, v, raw, out, aug = forward[7:13]
    shared_normed, shared_qk, shared_v, shared_raw, shared_out, shared_aug = forward[13:19]

    def collect(mine, cross, third):
        mine = lax.ppermute(mine, COLUMN, KEEP)
        cross = lax.ppermute(cross, COLUMN, CROSS)
        third = lax.ppermute(third, COLUMN, KEEP)
        return jnp.stack([jnp.where(zq == 0, mine, cross), jnp.where(zq == 0, cross, mine), third])

    output, middle_grad, grad, shared_grad, out_grad, second_gain_grad, packed, far = dense(
        square, out, shared_out, own_tokens, grad_tokens, cotangent, out_matrix, gain_second, bounds,
        up_half, down_half,
    )
    row_side = (aug, qk, v, out, grad, raw, normed)
    shared_side = (shared_aug, shared_qk, shared_v, shared_out, shared_grad, shared_raw, shared_normed)
    weights = (mix_half, own_tokens, middle_grad)
    gains = (gain_first, gain_qk, second_gain_grad)
    if square:
        input_out, mix_out, gains_out, up_out, down_out, outw_out = backward_pass(
            True, pics, row_side, shared_side, weights, gains, bounds, packed, far, out_grad
        )
        gains_out = gains_out[:4, :shard]
        mix_out, up_out, down_out, outw_out = (
            array.astype(F32) for array in (mix_out, up_out, down_out, outw_out)
        )
    else:
        input_grad, mix_grad, gain_grads = backward_pass(
            False, pics, row_side, shared_side, weights, gains, bounds
        )

        def reduce(grad):
            return lax.psum(lax.psum_scatter(grad, rows, scatter_dimension=0, tiled=True), SEQ).astype(F32)

        first, second = input_grad[:part], input_grad[part:half]
        input_out = collect(
            jnp.where(zq == 0, first, second), jnp.where(zq == 0, second, first), input_grad[half:]
        )
        own_core = jnp.arange(2) == core
        eighth = model // 8
        down_grad = packed[:, None, :tile]
        down_out = reduce(jnp.where(own_core[None, :, None, None], down_grad, 0).reshape(hidden, model))
        up_grad = packed[:, tile : 2 * tile].reshape(4, 2, 2 * eighth, 2, tile).transpose(0, 2, 1, 3, 4)
        up_grad = up_grad.reshape(model, 4, 1, tile)
        up_out = reduce(jnp.where(own_core[None, None, :, None], up_grad, 0).reshape(model, hidden))
        out_grad = out_grad.reshape(model, 1, width)
        outw_out = reduce(jnp.where(own_core[None, :, None], out_grad, 0).reshape(model, model))
        mix_out = reduce(
            jnp.where(own_core[None, None, :, None], mix_grad.reshape(model, 3, 1, width), 0).reshape(model, 6 * width)
        )
        gain_grads = gain_grads[:4].reshape(4, 2 * chips, shard).transpose(1, 0, 2).astype(BF16)
        gains_out = reduce(gain_grads).reshape(4, shard)
    return (
        output, input_out, gains_out[0], mix_out, gains_out[1], gains_out[2], outw_out, gains_out[3],
        up_out, down_out,
    )


def solution(mesh):
    fsdp = mesh.shape["fsdp"]
    split = Mesh(mesh.devices.reshape(fsdp // 2, 2, 2, 2), ("chip", "core", "zp", "zq"))
    rows = ("chip", "core")
    return jax.shard_map(
        local,
        mesh=split,
        in_specs=(
            P(rows, SEQ, None),
            P(rows, None),
            P(rows, SEQ),
            P(rows),
            P(rows, None),
            P(rows),
            P(rows),
            P(rows, None),
            P(rows),
            P(rows, None),
            P(rows, None),
            P(rows, SEQ, None),
        ),
        out_specs=(
            P(rows, SEQ, None),
            P(rows, SEQ, None),
            P(rows),
            P(rows, None),
            P(rows),
            P(rows),
            P(rows, None),
            P(rows),
            P(rows, None),
            P(rows, None),
        ),
        check_vma=False,
    )
```

```python
import functools

import jax
import jax.numpy as jnp
from jax import lax
from jax.experimental import pallas as pl
from jax.experimental.pallas import tpu as pltpu
from jax.sharding import Mesh, PartitionSpec as P

HEADS = 12
HEAD = 64
EPSILON = 1e-06
BLOCK = 256
STEP = 512
MARK = 32.0
EXP2_FACTOR = HEAD**-0.5 * 1.4426950408889634
F32 = jnp.float32
BF16 = jnp.bfloat16
VMEM_LIMIT = 56 * 1024 * 1024

SEQ = ("zp", "zq")
COLUMN = ("core", "zp", "zq")
KEEP = [
    (core * 4 + z, (z // 2) * 4 + 2 * core + z % 2) for core in range(2) for z in range(4)
]
CROSS = [
    (core * 4 + z, (z // 2) * 4 + 2 * core + 1 - z % 2) for core in range(2) for z in range(4)
]


def swap(array, name, bit=1):
    count = lax.axis_size(name)
    return lax.ppermute(array, name, [(i, i ^ bit) for i in range(count)])


def pick(array, index, axis=0):
    return lax.dynamic_index_in_dim(array, index, axis, keepdims=False)


def group_ones(scale, size=128):
    row = lax.broadcasted_iota(jnp.int32, (size, size), 0) // HEAD
    column = lax.broadcasted_iota(jnp.int32, (size, size), 1) // HEAD
    return jnp.where(row == column, scale, 0.0).astype(BF16)


def group_sum(values, ones):
    return jnp.dot(values.astype(BF16), ones, preferred_element_type=F32)


def group_sum_fine(values, ones):
    high = values.astype(BF16)
    return group_sum(high, ones) + group_sum(values - high.astype(F32), ones)


def project_kernel(x_ref, gain_ref, weight_ref, qkg_ref, normed_ref, qk_ref, v_ref, raw_ref):
    both = qk_ref.shape[1]
    x = x_ref[...].astype(F32)
    center = x - jnp.mean(x, axis=-1, keepdims=True)
    spread = jnp.mean(center * center, axis=-1, keepdims=True)
    normed = (center * lax.rsqrt(spread + EPSILON) * gain_ref[...]).astype(BF16)
    normed_ref[...] = normed
    ones = group_ones(1.0 / HEAD, 256)
    for at in range(0, both, 256):
        lanes = slice(at, at + 256)
        raw = jnp.dot(normed, weight_ref[:, lanes], preferred_element_type=F32)
        raw_ref[:, lanes] = raw.astype(BF16)
        c = raw - group_sum(raw, ones)
        n = c * lax.rsqrt(group_sum(c * c, ones) + EPSILON)
        qk_ref[:, lanes] = (n * qkg_ref[:, lanes]).astype(BF16)
    v_ref[...] = jnp.dot(normed, weight_ref[:, both:], preferred_element_type=F32).astype(BF16)


def nt(a, b):
    return lax.dot_general(a, b, (((1,), (1,)), ((), ())), preferred_element_type=F32)


def tn(a, b):
    return lax.dot_general(a, b, (((0,), (0,)), ((), ())), preferred_element_type=F32)


def slots(queries, length, part):
    at = lax.broadcasted_iota(jnp.int32, (queries, 128), 0)
    if queries == length:
        return at
    return at % part + part * (lax.axis_index("zq") + 2 * (at // part))


def own_rows(ref, start, count, queries, part):
    if queries == ref.shape[0]:
        return ref[pl.ds(start, count), :]
    zq = lax.axis_index("zq")
    pieces = [
        ref[pl.ds(pl.multiple_of((zq + 2 * i) * part, part), part), :]
        for i in range(start // part, (start + count) // part)
    ]
    return jnp.concatenate(pieces, axis=0)


def query_marks(bounds_ref, place, queries, length, part, pics):
    at = slots(queries, length, part)
    inside = (at >= bounds_ref[0:1, :]) & (at < bounds_ref[2:3, :])
    values = jnp.where(inside, MARK, 0.0)
    return jnp.where(place == pics, MARK, values).astype(BF16)


def key_marks(bounds_ref, place, length, pics):
    at = lax.broadcasted_iota(jnp.int32, (length, 128), 0)
    inside = (at >= bounds_ref[0:1, :]) & (at < bounds_ref[1:2, :])
    values = jnp.where(inside, MARK, 0.0)
    values = jnp.where(place == pics, -MARK, values)
    return jnp.where((place > pics) & (place < pics + 4), 1.0, values).astype(BF16)


def attend_kernel(pics, q_ref, k_ref, v_ref, bounds_ref, out_ref, aug_ref, kaug, vaug, qaug):
    length = k_ref.shape[0]
    queries = out_ref.shape[0]
    part = length // 4
    lane = lax.broadcasted_iota(jnp.int32, (1, 128), 1)
    place = lane % HEAD
    sides = [lane < HEAD, lane >= HEAD]
    kmarks = key_marks(bounds_ref, place, length, pics)
    qmarks = query_marks(bounds_ref, place, queries, length, part, pics)
    qaug[...] = qmarks
    for h in range(2):
        kaug[h] = jnp.where(sides[h], k_ref[...], kmarks)
        vaug[h] = jnp.where(sides[h], v_ref[...], jnp.ones_like(v_ref))
    for b in range(queries // STEP):
        rows = pl.ds(b * STEP, STEP)
        mine = own_rows(q_ref, b * STEP, STEP, queries, part)
        query = [jnp.where(sides[h], mine, qaug[rows, :]) for h in range(2)]
        total = [jnp.zeros((STEP, 128), F32)] * 2
        for j in range(length // STEP):
            keys = pl.ds(j * STEP, STEP)
            scores = [nt(query[h], kaug[h, keys, :]) for h in range(2)]
            weights = [jnp.exp2(x * EXP2_FACTOR).astype(BF16) for x in scores]
            total = [
                total[h] + jnp.dot(weights[h], vaug[h, keys, :], preferred_element_type=F32) for h in range(2)
            ]
        results = []
        for h in range(2):
            results.append(total[h] / pltpu.roll(total[h], HEAD, 1))
            log_total = jnp.log(jnp.where(sides[h], 1.0, total[h])) * -(HEAD**0.5)
            first = log_total.astype(BF16)
            rest = log_total - first.astype(F32)
            middle = rest.astype(BF16)
            last = (rest - middle.astype(F32)).astype(BF16)
            logs = jnp.where(place == pics + 1, first, jnp.where(place == pics + 2, middle, last))
            slot = jnp.logical_not(sides[h]) & (place > pics) & (place < pics + 4)
            aug_ref[h, rows, :] = jnp.where(slot, logs, query[h])
        out_ref[rows, :] = jnp.where(sides[0], results[0], results[1]).astype(BF16)


def head_norm_back(e, raw, gain, means):
    raw = raw.astype(F32)
    c = raw - group_sum(raw, means)
    r = lax.rsqrt(group_sum(c * c, means) + EPSILON)
    n = c * r
    t = e * gain
    grad = r * (t - group_sum(t, means) - n * group_sum(t * n, means))
    return grad.astype(BF16), jnp.sum(e * n, axis=0, keepdims=True)


def attend_back_kernel(
    pics, aug_ref, k_ref, v_ref, out_ref, do_ref, rawq_ref, rawk_ref, qg_ref, kg_ref, bounds_ref,
    dq_ref, dk_ref, dv_ref, qgg_ref, kgg_ref, kaug, vaug, doaug, qsum, ksum,
):
    length = k_ref.shape[0]
    queries = do_ref.shape[0]
    part = length // 4
    whole = queries == length
    lane = lax.broadcasted_iota(jnp.int32, (1, 128), 1)
    place = lane % HEAD
    sides = [lane < HEAD, lane >= HEAD]
    kmarks = key_marks(bounds_ref, place, length, pics)
    vmarks = jnp.where(place < 2, 1.0, 0.0).astype(BF16)
    ones = group_ones(1.0)
    inner = group_sum_fine(do_ref[...].astype(F32) * out_ref[...].astype(F32), ones)
    inner = -pltpu.roll(inner, HEAD, 1)
    inner_high = inner.astype(BF16)
    inner_low = (inner - inner_high.astype(F32)).astype(BF16)
    zero = jnp.zeros((), BF16)
    gmarks = jnp.where(place == 0, inner_high, jnp.where(place == 1, inner_low, zero))
    for h in range(2):
        kaug[h] = jnp.where(sides[h], k_ref[...], kmarks)
        vaug[h] = jnp.where(sides[h], v_ref[...], vmarks)
        doaug[h] = jnp.where(sides[h], do_ref[...], gmarks)
    for b in range(length // STEP):
        keys = pl.ds(b * STEP, STEP)
        key = [kaug[h, keys, :] for h in range(2)]
        value = [vaug[h, keys, :] for h in range(2)]
        dk = [jnp.zeros((STEP, 128), F32)] * 2
        dv = [jnp.zeros((STEP, 128), F32)] * 2
        for j in range(queries // STEP):
            rows = pl.ds(j * STEP, STEP)
            query = [aug_ref[h, rows, :] for h in range(2)]
            grad = [doaug[h, rows, :] for h in range(2)]
            scores = [nt(key[h], query[h]) for h in range(2)]
            soft_grad = [nt(value[h], grad[h]) for h in range(2)]
            weights = [jnp.exp2(x * EXP2_FACTOR) for x in scores]
            score_grad = [(weights[h] * soft_grad[h]).astype(BF16) for h in range(2)]
            for h in range(2):
                part_sum = tn(score_grad[h], key[h])
                if b == 0:
                    qsum[h, rows, :] = part_sum
                else:
                    qsum[h, rows, :] += part_sum
                dk[h] = dk[h] + jnp.dot(score_grad[h], query[h], preferred_element_type=F32)
                dv[h] = dv[h] + jnp.dot(weights[h].astype(BF16), grad[h], preferred_element_type=F32)
        ksum[keys, :] = jnp.where(sides[0], dk[0], dk[1]) * HEAD**-0.5
        dv_ref[keys, :] = jnp.where(sides[0], dv[0], dv[1]).astype(BF16)

    means = group_ones(1.0 / HEAD)
    gain_sum = jnp.zeros((1, 128), F32)
    for b in range(queries // part):
        rows = pl.ds(b * part, part)
        e = jnp.where(sides[0], qsum[0, rows, :], qsum[1, rows, :]) * HEAD**-0.5
        raw = own_rows(rawq_ref, b * part, part, queries, part)
        dq_ref[rows, :], more = head_norm_back(e.astype(BF16).astype(F32), raw, qg_ref[...], means)
        gain_sum = gain_sum + more
    qgg_ref[...] = gain_sum
    gain_sum = jnp.zeros((1, 128), F32)
    for b in range(length // part):
        rows = pl.ds(b * part, part)
        e = ksum[rows, :].astype(BF16)
        if whole:
            dk_ref[rows, :], more = head_norm_back(e.astype(F32), rawk_ref[rows, :], kg_ref[...], means)
            gain_sum = gain_sum + more
        else:
            dk_ref[rows, :] = e
    kgg_ref[...] = gain_sum


def shared_keys_kernel(dk_ref, dv_ref, gotk_ref, gotv_ref, rawk_ref, kg_ref, outk_ref, outv_ref, kgg_ref):
    count = outk_ref.shape[0]
    part = count // 2
    means = group_ones(1.0 / HEAD)
    gain_sum = jnp.zeros((1, 128), F32)
    for b in range(2):
        rows = pl.ds(b * part, part)
        own = lambda ref: own_rows(ref, b * part, part, count, part)
        e = own(dk_ref).astype(F32) + gotk_ref[rows, :].astype(F32)
        outk_ref[rows, :], more = head_norm_back(e, own(rawk_ref), kg_ref[...], means)
        gain_sum = gain_sum + more
        outv_ref[rows, :] = (own(dv_ref).astype(F32) + gotv_ref[rows, :].astype(F32)).astype(BF16)
    kgg_ref[...] = gain_sum


def gelu_pair(h):
    size = jnp.abs(h)
    bell = jnp.exp2(h * h * -0.7213475204444817)
    t = 1.0 / (1.0 + 0.23164189 * size)
    series = t * (0.127414796 + t * (-0.142248368 + t * (0.7107068705 + t * (-0.7265760135 + t * 0.5307027145))))
    tail = series * bell
    below = jnp.where(h < 0.0, tail, 1.0 - tail)
    return h * below, below + h * (bell * 0.3989422804014327)


def norm_parts(values):
    center = values - jnp.mean(values, axis=-1, keepdims=True)
    spread = lax.rsqrt(jnp.mean(center * center, axis=-1, keepdims=True) + EPSILON)
    return center * spread, spread


def norm_back(upstream, n, r, gain):
    t = upstream * gain
    grad = r * (t - jnp.mean(t, axis=-1, keepdims=True) - n * jnp.mean(t * n, axis=-1, keepdims=True))
    return grad, jnp.sum(upstream * n, axis=0, keepdims=True)


MESH_ID = pl.DeviceIdType.MESH


def here():
    return lax.axis_index("chip"), lax.axis_index("core"), lax.axis_index("zp"), lax.axis_index("zq")


def remote(source, target, sems, at, device):
    sent, got = sems
    return pltpu.make_async_remote_copy(
        src_ref=source, dst_ref=target, send_sem=sent.at[at], recv_sem=got.at[at],
        device_id=device, device_id_type=MESH_ID,
    )


def greet(devices, maybe=None, moves=None):
    barrier = pltpu.get_barrier_semaphore()
    for device in devices:
        pl.semaphore_signal(barrier, inc=1, device_id=device, device_id_type=MESH_ID)
    if maybe is None:
        pl.semaphore_wait(barrier, len(devices))
        return

    @pl.when(moves)
    def _():
        pl.semaphore_signal(barrier, inc=1, device_id=maybe, device_id_type=MESH_ID)

    pl.semaphore_wait(barrier, len(devices) + jnp.where(moves, 1, 0))


def rows_at(start, count):
    return pl.ds(pl.multiple_of(start, 16), count)


class Moves:
    def __init__(self, moved, stays, crossed, moves):
        self.moved, self.stays, self.crossed, self.moves = moved, stays, crossed, moves

    def each(self, act):
        if self.crossed is not None:
            act(self.crossed)

        @pl.when(self.moves)
        def _():
            for copy in self.moved:
                act(copy)

        @pl.when(jnp.logical_not(self.moves))
        def _():
            for copy in self.stays:
                act(copy)

    def start(self):
        self.each(lambda copy: copy.start())

    def wait(self):
        self.each(lambda copy: copy.wait())


class Line:
    def __init__(self, parts, whole, right, left, sems, at):
        chip, core, zp, zq = here()
        self.z = 2 * zp + zq
        up, down = jnp.minimum(self.z + 1, 3), jnp.maximum(self.z - 1, 0)
        self.next = (chip, core, up // 2, up % 2)
        self.last = (chip, core, down // 2, down % 2)
        self.parts, self.whole, self.right, self.left = parts, whole, right, left
        self.sems, self.at, self.sends = sems, at, []

    def at_chip(self, z, *acts):
        @pl.when(self.z == z)
        def _():
            for act in acts:
                act()

    def part_copy(self, c, rightward):
        if rightward:
            return remote(self.parts.at[c], self.right.at[3 - c], self.sems, self.at + 3 - c, self.next)
        return remote(self.parts.at[c], self.left.at[c], self.sems, self.at + 3 + c, self.last)

    def whole_copy(self, c, rightward):
        if rightward:
            return remote(self.whole.at[c], self.whole.at[c], self.sems, self.at + 6 + c, self.next)
        return remote(self.whole.at[c], self.whole.at[c], self.sems, self.at + 8 + c, self.last)

    def send(self, z, make, c, rightward):
        self.sends.append((z, make, c, rightward))
        return lambda: make(c, rightward).start()

    def take(self, c, rightward):
        def act():
            self.part_copy(c, rightward).wait_recv()
            came = self.right[3 - c] if rightward else self.left[c]
            self.parts[c] = add(self.parts[c], came).astype(BF16)

        return act

    def got(self, c, rightward):
        return lambda: self.whole_copy(c, rightward).wait_recv()

    def start(self):
        part = self.part_copy
        self.at_chip(0, *[self.send(0, part, c, True) for c in (3, 2, 1)])
        self.at_chip(3, *[self.send(3, part, c, False) for c in (0, 1, 2)])

    def first(self):
        self.at_chip(1, self.take(3, True), self.send(1, self.part_copy, 3, True))
        self.at_chip(2, self.take(0, False), self.send(2, self.part_copy, 0, False))

    def second(self):
        part = self.part_copy
        self.at_chip(
            1, self.take(2, True), self.send(1, part, 2, True), self.take(0, False), self.send(1, part, 0, False)
        )
        self.at_chip(
            2, self.take(1, False), self.send(2, part, 1, False), self.take(3, True), self.send(2, part, 3, True)
        )

    def third(self):
        self.at_chip(0, self.take(0, False))
        self.at_chip(1, self.take(1, True), self.take(1, False))
        self.at_chip(2, self.take(2, True), self.take(2, False))
        self.at_chip(3, self.take(3, True))
        self.whole[self.z] = self.parts[self.z]
        for z in range(4):
            acts = [self.send(z, self.whole_copy, z, True)] if z < 3 else []
            acts += [self.send(z, self.whole_copy, z, False)] if z > 0 else []
            self.at_chip(z, *acts)

    def fourth(self):
        whole = self.whole_copy
        for z in (1, 2):
            self.at_chip(
                z, self.got(z - 1, True), self.send(z, whole, z - 1, True), self.got(z + 1, False),
                self.send(z, whole, z + 1, False),
            )

    def fifth(self):
        whole = self.whole_copy
        self.at_chip(1, self.got(3, False), self.send(1, whole, 3, False))
        self.at_chip(2, self.got(0, True), self.send(2, whole, 0, True))

    def sixth(self):
        self.at_chip(0, *[self.got(c, False) for c in (1, 2, 3)])
        self.at_chip(3, *[self.got(c, True) for c in (2, 1, 0)])

    def wait_sends(self):
        for z in range(4):
            mine = [make(c, rightward) for at, make, c, rightward in self.sends if at == z]
            self.at_chip(z, *[copy.wait_send for copy in mine])


def write_bounds(pics, lens_ref, bounds_ref, zp, zq, length):
    lane = lax.broadcasted_iota(jnp.int32, (8, 128), 1)
    lens = jnp.where(zp == 0, lens_ref[0], lens_ref[1])
    ends = lens
    for hop in (1, 2, 4, 8):
        ends = ends + jnp.where(lane >= hop, pltpu.roll(ends, hop, 1), 0)
    starts = ends - lens
    last = (lens > 0) & (pltpu.roll(lens, 127, 1) == 0)
    query_ends = jnp.where(last, length, ends)
    total = jnp.max(jnp.where(lane < pics, ends, 0), axis=1, keepdims=True)

    def both(values):
        values = jnp.where(lane < HEAD, jnp.where(lane < pics, values, 2 * length), 0)
        return values + pltpu.roll(values, HEAD, 1)

    tables = [both(starts), both(ends), both(query_ends), jnp.broadcast_to(total, (8, 128))]
    for t in range(4):
        table = tables[t]
        bounds_ref[0, t : t + 1, :] = jnp.where(zq == 0, table[0:1], table[1:2])
        bounds_ref[1, t : t + 1, :] = table[2:3]
    bounds_ref[:, 4:, :] = jnp.zeros((2, 4, 128), jnp.int32)


def forward_kernel(square, pics, *refs):
    refs = list(refs)
    take = lambda count: [refs.pop(0) for _ in range(count)]
    tokens_ref, cot_ref, lengths_ref, weight_in = take(4)
    if square:
        gain_in = take(4)
        up_in, outw_ref = take(2)
    else:
        gain_first_in, gain_qk_in = take(2)
    x_out, bounds_ref, mix_hbm, cot_hbm, gain_first, second_ref, gain_qk = take(7)
    names = ("normed", "qk", "v", "raw", "out", "aug")
    outs = [dict(zip(names, take(6))) for _ in range(2)]
    if square:
        up_hbm, outw_hbm = take(2)
    row_ref, shared_ref, cot_out, lens_ref, lens_out = take(5)
    scratch = [dict(zip(names, take(6))) for _ in range(2)]
    kaug, vaug, qaug = take(3)
    if square:
        mix_ref, gains_ref, up_ref, mix_out, gains_out, up_out, outw_out = take(7)
    sent, got, local_sem, write_sem = take(4)

    chip, core, zp, zq = here()
    z = 2 * zp + zq
    part = tokens_ref.shape[1]
    half, length = 2 * part, 4 * part
    sems = (sent, got)
    partner = (chip, 1 - core, zp, zq)
    side = (chip, core, zp, 1 - zq)
    keep = (chip, zp, core, zq)
    cross = (chip, zp, core, 1 - zq)
    moves = core != zp
    near_x = (chip ^ 1, core, zp, zq)
    near_y = (chip ^ 2, core, zp, zq)
    greet([partner, side, cross] + ([near_x, near_y] if square else []), keep, moves)

    def quarter(ref, index):
        return ref.at[rows_at(index * part, part)]

    own_row = remote(tokens_ref.at[zq], quarter(row_ref, z), sems, 0, keep)
    own_shared = remote(tokens_ref.at[2], quarter(shared_ref, z), sems, 2, keep)
    stay_row = pltpu.make_async_copy(tokens_ref.at[zq], quarter(row_ref, z), local_sem.at[0])
    stay_shared = pltpu.make_async_copy(tokens_ref.at[2], quarter(shared_ref, z), local_sem.at[1])

    @pl.when(moves)
    def _():
        own_row.start()

    @pl.when(jnp.logical_not(moves))
    def _():
        stay_row.start()

    cross_row = remote(tokens_ref.at[1 - zq], quarter(row_ref, z), sems, 1, cross)
    cross_row.start()

    @pl.when(moves)
    def _():
        own_shared.start()

    @pl.when(jnp.logical_not(moves))
    def _():
        stay_shared.start()

    lens_ref[...] = jnp.zeros_like(lens_ref)
    lens_ref[: lengths_ref.shape[0], :pics] = lengths_ref[...]
    lens_copy = remote(lens_ref, lens_out.at[core], sems, 8, partner)
    lens_copy.start()
    lens_stay = pltpu.make_async_copy(lens_ref, lens_out.at[core], local_sem.at[2])
    lens_stay.start()
    waits = []
    if square:
        shard = mix_ref.shape[1]
        tile = up_ref.shape[2] // 4
        width = mix_ref.shape[2] // 3
        for h in range(2):
            for i in range(3):
                mix_ref[h, :, i * width : (i + 1) * width] = weight_in[:, (2 * i + h) * width : (2 * i + h + 1) * width]
        gains_ref[...] = jnp.zeros_like(gains_ref)
        for i in range(4):
            gains_ref[i : i + 1, :shard] = gain_in[i][...].astype(F32)
        mine, theirs = 2 * chip + core, 2 * chip + 1 - core
        slot = [9]

        def send(source, target, device):
            copy = remote(source, target, sems, slot[0], device)
            slot[0] += 1
            copy.start()
            waits.append(copy)
            return copy

        def stay(source, target, at):
            copy = pltpu.make_async_copy(source, target, local_sem.at[at])
            copy.start()
            return copy

        def block(ref, start, count):
            return ref.at[rows_at(start, count)]

        mix_piece = lambda index: (block(mix_out, index * shard, shard), gains_out.at[index])

        def send_mix(sources, index, device):
            return [send(source, target, device) for source, target in zip(sources, mix_piece(index))]

        def arrived(copies):
            for copy in copies:
                copy.wait_recv()

        x_mine, y_other = 2 * (chip ^ 1) + core, 2 * (chip ^ 2) + 1 - core
        to_core = send_mix((mix_ref.at[1 - core], gains_ref), mine, partner)
        a_x = send_mix((mix_ref.at[core], gains_ref), mine, near_x)
        a_y = send_mix((mix_ref.at[core], gains_ref), mine, near_y)
        for h in range(2):
            for i in range(4):
                up_ref[h, :, i * tile : (i + 1) * tile] = up_in[:, (2 * i + h) * tile : (2 * i + h + 1) * tile]
        up_core = send(up_ref.at[1 - core], block(up_out, mine * shard, shard), partner)
        out_core = send(outw_ref, block(outw_out, mine * shard, shard), partner)
        stays = [
            stay(mix_ref.at[core], mix_piece(mine)[0], 3),
            stay(gains_ref, gains_out.at[mine], 4),
            stay(up_ref.at[core], block(up_out, mine * shard, shard), 5),
            stay(outw_ref, block(outw_out, mine * shard, shard), 6),
        ]
        arrived(to_core)
        b_x = send_mix(mix_piece(theirs), theirs, near_x)
        b_y = send_mix(mix_piece(theirs), theirs, near_y)
        arrived(a_x)
        a_far = send_mix(mix_piece(x_mine), x_mine, near_y)
        arrived(b_y)
        b_far = send_mix(mix_piece(y_other), y_other, near_x)
        for copy in stays:
            copy.wait()
        arrived([up_core])
        ohalf = shard // 2

        def bundle(first, from_chip):
            same, twin = 2 * from_chip + core, 2 * from_chip + 1 - core
            part_of = 0 if first else 1
            return [
                block(up_out, (same if first else twin) * shard, shard),
                block(outw_out, same * shard + part_of * ohalf, ohalf),
            ]

        def send_bundle(first, from_chip, device):
            return [send(ref, ref, device) for ref in bundle(first, from_chip)]

        first_x = send_bundle(True, chip, near_x)
        first_y = send_bundle(True, chip, near_y)
        second_x = send_bundle(False, chip, near_x)
        second_y = send_bundle(False, chip, near_y)

    lens_copy.wait()
    lens_stay.wait()
    write_bounds(pics, lens_out, bounds_ref, zp, zq, length)
    if square:
        arrived(a_y + b_x + a_far + b_far)
        for p in range(gains_out.shape[0]):
            lanes = slice(p * shard, (p + 1) * shard)
            values = gains_out[p, :, :shard]
            gain_first[:, lanes] = values[0:1]
            second_ref[:, lanes] = values[3:4]
            half_pieces = gains_out.shape[0] // 2

            @pl.when(core == p // half_pieces)
            def _():
                at = (p % half_pieces) * shard
                gain_qk[:, at : at + shard] = values[1:2]
                gain_qk[:, width + at : width + at + shard] = values[2:3]
        weight = mix_out
    else:
        weight = weight_in
        width = weight.shape[1] // 3
        second_ref[...] = jnp.zeros_like(second_ref)
        gain_first[...] = gain_first_in[...]
        gain_qk[...] = gain_qk_in[...]
    writes = []

    def write(source, target, at):
        copy = pltpu.make_async_copy(source, target, write_sem.at[at])
        copy.start()
        writes.append(copy)

    write(weight, mix_hbm, 0)
    first, second = 2 * core + zq, 2 * core + 1 - zq
    other_first, other_second = 2 * (1 - core) + zq, 2 * (1 - core) + 1 - zq

    def forwarded(ref, index, at):
        return remote(quarter(ref, index), quarter(ref, index), sems, at, partner)

    def project(tokens, bufs, at):
        rows = rows_at(at * part, part)
        project_kernel(
            tokens.at[rows], gain_first, weight, gain_qk, bufs["normed"].at[rows], bufs["qk"].at[rows],
            bufs["v"].at[rows], bufs["raw"].at[rows],
        )

    def project_row(i, _):
        @pl.when(i == 0)
        def _():
            @pl.when(moves)
            def _():
                own_row.wait_recv()

            @pl.when(jnp.logical_not(moves))
            def _():
                stay_row.wait()

            forwarded(row_ref, first, 3).start()

        @pl.when(i == 1)
        def _():
            cross_row.wait_recv()
            forwarded(row_ref, second, 4).start()

        @pl.when(i == 2)
        def _():
            forwarded(row_ref, other_first, 3).wait_recv()

        @pl.when(i == 3)
        def _():
            forwarded(row_ref, other_second, 4).wait_recv()

        order = jnp.where(i == 0, first, jnp.where(i == 1, second, jnp.where(i == 2, other_first, other_second)))
        project(row_ref, scratch[0], order)
        return 0

    row_one, row_two = forwarded(row_ref, first, 3), forwarded(row_ref, second, 4)

    def attend(bufs, bounds):
        def one(p, _):
            lanes = pl.ds(pl.multiple_of(p * 128, 128), 128)
            attend_kernel(
                pics, bufs["qk"].at[:, lanes],
                bufs["qk"].at[:, pl.ds(pl.multiple_of(width + p * 128, 128), 128)], bufs["v"].at[:, lanes], bounds,
                bufs["out"].at[:, lanes], bufs["aug"].at[pl.ds(2 * p, 2)], kaug, vaug, qaug.at[pl.ds(0, bufs["out"].shape[0])],
            )
            return 0

        lax.fori_loop(0, width // 128, one, 0)

    lax.fori_loop(0, 4, project_row, 0)
    for i, name in enumerate(("normed", "qk", "v", "raw")):
        write(scratch[0][name], outs[0][name], 1 + i)
    write(row_ref.at[rows_at(core * half, half)], x_out.at[pl.ds(0, half)], 5)

    @pl.when(moves)
    def _():
        own_shared.wait_recv()

    @pl.when(jnp.logical_not(moves))
    def _():
        stay_shared.wait()

    to_side = remote(quarter(shared_ref, first), quarter(shared_ref, first), sems, 5, side)
    to_side.start()
    shared_one = remote(quarter(shared_ref, first), quarter(shared_ref, first), sems, 6, partner)
    shared_one.start()
    attend(scratch[0], bounds_ref.at[0])
    cot_moves = Moves(
        [remote(cot_ref.at[zq], cot_out, sems, 43, keep)],
        [pltpu.make_async_copy(cot_ref.at[zq], cot_out, local_sem.at[0])],
        None,
        moves,
    )
    cot_moves.start()
    write(scratch[0]["out"], outs[0]["out"], 6)
    write(scratch[0]["aug"], outs[0]["aug"], 7)
    to_side.wait_recv()
    shared_two = forwarded(shared_ref, second, 7)
    shared_two.start()
    if square:
        arrived(first_x + second_y)
        far_first = send_bundle(True, chip ^ 1, near_y)
        far_second = send_bundle(False, chip ^ 2, near_x)
    shared_one.wait_recv()
    shared_two.wait_recv()

    def project_shared(i, _):
        project(shared_ref, scratch[1], i)
        return 0

    lax.fori_loop(0, 4, project_shared, 0)
    for i, name in enumerate(("normed", "qk", "v", "raw")):
        write(scratch[1][name], outs[1][name], 8 + i)
    write(shared_ref.at[rows_at(first * part, part)], x_out.at[pl.ds(half, part)], 12)
    attend(scratch[1], bounds_ref.at[1])
    write(scratch[1]["out"], outs[1]["out"], 13)
    write(scratch[1]["aug"], outs[1]["aug"], 14)

    if square:
        arrived(first_y + second_x + far_first + far_second)
        sent_pieces = []
        for c in (chip ^ 1, chip ^ 2, chip ^ 3):
            target = block(outw_out, (2 * c + core) * shard, shard)
            sent_pieces.append(send(target, target, partner))
        write(up_out, up_hbm, 15)
        arrived(sent_pieces + [out_core])
        write(outw_out, outw_hbm, 17)
        for copy in waits:
            copy.wait_send()
    cot_moves.wait()
    write(cot_out, cot_hbm, 18)
    for copy in (row_one, row_two, shared_one, shared_two, to_side, cross_row):
        copy.wait_send()

    @pl.when(moves)
    def _():
        own_row.wait_send()
        own_shared.wait_send()

    for copy in writes:
        copy.wait()


def forward_pass(square, pics, tokens, cotangent, lengths, weight, *more):
    _, part, model = tokens.shape
    length, half, width = 4 * part, 2 * part, model // 2
    near = pl.BlockSpec(memory_space=pltpu.VMEM)
    anywhere = pl.BlockSpec(memory_space=pl.ANY)
    low = lambda *shape: (shape, BF16)
    wide = lambda *shape: (shape, F32)
    outs = [
        (low(3 * part, model), anywhere),
        (((2, 8, 128), jnp.int32), near),
        (low(model, 3 * width), anywhere),
        (low(part, model), anywhere),
        (wide(1, model), near),
        (wide(1, model), near),
        (wide(1, model), near),
    ]
    bufs = []
    for queries in (length, half):
        shapes = [
            low(length, model), low(length, 2 * width), low(length, width), low(length, 2 * width),
            low(queries, width), low(2 * (width // 128), queries, 128),
        ]
        outs += [(shape, anywhere) for shape in shapes]
        bufs += shapes
    table = ((8, 128), jnp.int32)
    scratch = [low(length, model), low(length, model), low(part, model), table, ((2, 8, 128), jnp.int32)] + bufs
    scratch += [low(2, length, 128), low(2, length, 128), low(length, 128)]
    if square:
        up, _ = more[4:]
        shard, hidden = up.shape
        landed = [low(model, hidden // 2), low(model, model)]
        outs += [(shape, anywhere) for shape in landed]
        scratch += [low(2, shard, 3 * width), wide(8, 128), low(2, shard, hidden // 2)]
        scratch += [low(model, 3 * width), wide(8, 8, 128)] + landed
    return pl.pallas_call(
        functools.partial(forward_kernel, square, pics),
        in_specs=[near] * (4 + len(more)),
        out_specs=[spec for _, spec in outs],
        out_shape=[jax.ShapeDtypeStruct(*shape) for shape, _ in outs],
        scratch_shapes=[pltpu.VMEM(*shape) for shape in scratch]
        + [
            pltpu.SemaphoreType.DMA((49,)),
            pltpu.SemaphoreType.DMA((49,)),
            pltpu.SemaphoreType.DMA((8,)),
            pltpu.SemaphoreType.DMA((19,)),
        ],
        compiler_params=pltpu.CompilerParams(
            collective_id=0, has_side_effects=True, vmem_limit_bytes=60 * 1024 * 1024
        ),
        name="forward_pass",
    )(tokens, cotangent, lengths, weight, *more)


def dense_kernel(
    square, out_ref, shared_ref, x, grad_ref, cot_ref, outw_ref, gain_ref, bounds_ref, up_ref, down_ref,
    output_ref, midg_ref, row_grad, shared_grad, outg_ref, gaing_ref, packed_ref, far_ref,
    att_other, second, turned, grad, cot_in, hidden_all, pre_all, forward, backward, middle, up, down,
    results, parts_out, parts_in, heads_out, cols_out, cols_in, stage, far_in,
    sent, got, load_sem, write_sem, local_sem,
):
    chip, core, zp, zq = here()
    sems = (sent, got)
    partner = (chip, 1 - core, zp, zq)
    keep = (chip, zp, core, zq)
    cross = (chip, zp, core, 1 - zq)
    moves = core != zp
    near_x = (chip ^ 1, core, zp, zq)
    near_y = (chip ^ 2, core, zp, zq)
    tokens, model = midg_ref.shape
    part = tokens // 3
    half = 2 * part
    width = out_ref.shape[1]
    units = up.shape[1]
    tile = units // 4
    other = 1 - core
    mine, theirs = pl.ds(0, tokens), pl.ds(tokens, tokens)
    own_down = down.at[rows_at(chip * tile, tile)] if square else down
    loads = [
        pltpu.make_async_copy(up_ref, up, load_sem.at[0]),
        pltpu.make_async_copy(down_ref, own_down, load_sem.at[1]),
    ]
    for copy in loads:
        copy.start()
    greet([partner, cross] + ([near_x, near_y] if square else []), keep, moves)
    att_sends = [
        remote(out_ref.at[rows_at(other * half, half)], att_other.at[pl.ds(0, half)], sems, 0, partner),
        remote(shared_ref.at[rows_at(other * part, part)], att_other.at[pl.ds(half, part)], sems, 1, partner),
    ]
    for copy in att_sends:
        copy.start()
    cot_move = Moves(
        [remote(cot_ref.at[2], cot_in.at[1], sems, 11, keep)],
        [pltpu.make_async_copy(cot_ref.at[2], cot_in.at[1], local_sem.at[0])],
        remote(cot_ref.at[1 - zq], cot_in.at[0], sems, 22, cross),
        moves,
    )
    cot_move.start()

    def down_half(index, which):
        return down.at[rows_at(index * tile + which * (tile // 2), tile // 2)]

    def send_down(index, which, at, device):
        copy = remote(down_half(index, which), down_half(index, which), sems, at, device)
        copy.start()
        return copy

    slot = lax.broadcasted_iota(jnp.int32, (part, 1), 0)
    filled, shared_filled = bounds_ref[0, 3:4, 0:1], bounds_ref[1, 3:4, 0:1]
    none = jnp.zeros((), BF16)

    def take_grad(values, at, start, limit, sem):
        rows = rows_at(at, part)
        grad[rows, :] = jnp.where(slot + start < limit, values, none)
        copy = remote(grad.at[rows], grad.at[rows_at(tokens + at, part)], sems, sem, partner)
        copy.start()
        return copy

    grad_sends = [take_grad(grad_ref[...], zq * part, (2 * core + zq) * part, filled, 2)]

    own_rows_of = lambda b: (
        out_ref[rows_at(core * half + b * part, part), :] if b < 2 else shared_ref[rows_at(core * part, part), :]
    )
    own_weight = outw_ref[rows_at(core * width, width), :]
    other_weight = outw_ref[rows_at(other * width, width), :]
    blocks = [pl.ds(b * part, part) for b in range(3)]
    for b in range(3):
        middle[blocks[b], :] = x[blocks[b], :].astype(F32) + jnp.dot(
            own_rows_of(b), own_weight, preferred_element_type=F32
        )
    for copy in loads:
        copy.wait()
    if square:
        down_sends = [
            send_down(chip, 0, 12, near_x), send_down(chip, 1, 13, near_y), send_down(chip, 0, 14, near_y),
            send_down(chip, 1, 15, near_x),
        ]
    for copy in att_sends:
        copy.wait_recv()
    for rows in blocks:
        value = middle[rows, :] + jnp.dot(att_other[rows, :], other_weight, preferred_element_type=F32)
        middle[rows, :] = value
        second[rows, :] = (norm_parts(value)[0] * gain_ref[...]).astype(BF16)
    second_send = remote(second.at[mine], second.at[theirs], sems, 3, partner)
    second_send.start()

    def hidden_forward(start):
        rows = pl.ds(start, tokens)

        def one_tile(i, _):
            here_units = pl.ds(pl.multiple_of(i * tile, 128), tile)
            hidden, slope = gelu_pair(jnp.dot(second[rows, :], up[:, here_units], preferred_element_type=F32))
            hidden_all[rows, here_units] = hidden.astype(BF16)
            pre_all[rows, here_units] = slope.astype(BF16)
            return 0

        lax.fori_loop(0, 4, one_tile, 0)

    def hidden_backward(start):
        rows = pl.ds(start, tokens)

        def one_tile(i, _):
            here_units = pl.ds(pl.multiple_of(i * tile, 128), tile)
            pre_grad = nt(grad[rows, :], down[rows_at(i * tile, tile), :]) * pre_all[rows, here_units].astype(F32)
            pre_all[rows, here_units] = pre_grad.astype(BF16)
            return 0

        lax.fori_loop(0, 4, one_tile, 0)

    hidden_forward(0)
    if square:
        down_sends[0].wait_recv()
        down_sends[1].wait_recv()
        down_sends += [send_down(chip ^ 1, 0, 16, near_y), send_down(chip ^ 2, 1, 17, near_x)]
    second_send.wait_recv()
    hidden_forward(tokens)
    if square:
        for copy in down_sends[2:]:
            copy.wait_recv()
    for b in range(3):
        rows, there = pl.ds(tokens + b * part, part), blocks[b]
        parts_out[0, there, :] = jnp.dot(hidden_all[rows, :], down[...], preferred_element_type=F32).astype(BF16)
    first_part = remote(parts_out.at[0], parts_in.at[0], sems, 4, partner)
    first_part.start()
    for rows in blocks:
        forward[rows, :] = middle[rows, :] + jnp.dot(hidden_all[rows, :], down[...], preferred_element_type=F32)
    first_part.wait_recv()
    for rows in blocks:
        results[rows, :] = (forward[rows, :] + parts_in[0, rows, :].astype(F32)).astype(BF16)
    kept_rows, third_rows = results.at[rows_at(zq * part, part)], results.at[pl.ds(half, part)]
    output_moves = Moves(
        [
            remote(kept_rows, output_ref.at[zq], sems, 19, keep),
            remote(third_rows, output_ref.at[2], sems, 20, keep),
        ],
        [
            pltpu.make_async_copy(kept_rows, output_ref.at[zq], local_sem.at[1]),
            pltpu.make_async_copy(third_rows, output_ref.at[2], local_sem.at[2]),
        ],
        remote(results.at[rows_at((1 - zq) * part, part)], output_ref.at[zq], sems, 21, cross),
        moves,
    )
    output_moves.start()
    cot_move.wait()
    grad_sends.append(take_grad(cot_in[0], (1 - zq) * part, (2 * core + 1 - zq) * part, filled, 18))
    grad_sends.append(take_grad(cot_in[1], half, (2 * core + zq) * part, shared_filled, 23))
    hidden_backward(0)
    for copy in grad_sends:
        copy.wait_recv()
    hidden_backward(tokens)
    for b in range(3):
        rows, there = pl.ds(tokens + b * part, part), blocks[b]
        parts_out[1, there, :] = nt(pre_all[rows, :], up[...]).astype(BF16)
    second_part = remote(parts_out.at[1], parts_in.at[1], sems, 5, partner)
    second_part.start()
    for rows in blocks:
        backward[rows, :] = nt(pre_all[rows, :], up[...])

    turned[...] = second[...].T
    quarter = model // 4
    far_sends = [
        remote(stage.at[0, pl.ds(0, tile)], far_in.at[0], sems, 9, near_y),
        remote(stage.at[0, pl.ds(tile, tile)], far_in.at[1], sems, 10, near_x),
    ]

    def weight_grads(i, _):
        target = chip ^ (3 - i) if square else 3 - i
        place = jnp.where(i == 0, 0, 1 + i % 2)

        @pl.when(i == 3)
        def _():
            pltpu.make_async_copy(stage.at[place], packed_ref.at[target], write_sem.at[place]).wait()

        here_units = pl.ds(pl.multiple_of(target * tile, 128), tile)
        stage[place, pl.ds(0, tile), :] = tn(hidden_all[:, here_units], grad[...]).astype(BF16)
        values = jnp.dot(
            turned[rows_at(target * quarter, quarter), :], pre_all[...], preferred_element_type=F32
        ).astype(BF16)
        for j in range(2):
            stage[place, pl.ds(tile + j * quarter, quarter), :] = values[:, j * model : (j + 1) * model]
        pltpu.make_async_copy(stage.at[place], packed_ref.at[target], write_sem.at[place]).start()
        if square:

            @pl.when(i == 0)
            def _():
                for copy in far_sends:
                    copy.start()

        return 0

    lax.fori_loop(0, 4, weight_grads, 0)

    second_send.wait_send()
    second_part.wait_recv()
    gain_sum = jnp.zeros(gaing_ref.shape, F32)
    for rows in blocks:
        n, r = norm_parts(middle[rows, :])
        upstream = backward[rows, :] + parts_in[1, rows, :].astype(F32)
        more, gain_more = norm_back(upstream, n, r, gain_ref[...])
        gain_sum = gain_sum + gain_more
        value = grad[rows, :].astype(F32) + more
        midg_ref[rows, :] = value
        branch = value.astype(BF16)
        second[rows, :] = branch
        heads_out[rows, :] = nt(branch, other_weight).astype(BF16)
    gaing_ref[...] = gain_sum
    head_sends = [
        remote(heads_out.at[pl.ds(0, half)], row_grad.at[rows_at(core * half, half)], sems, 6, partner),
        remote(heads_out.at[pl.ds(half, part)], shared_grad.at[rows_at(core * part, part)], sems, 7, partner),
    ]
    for copy in head_sends:
        copy.start()
    branch = second[mine, :]
    forward[rows_at(core * width, width), :] = tn(
        out_ref[rows_at(core * half, half), :], second[pl.ds(0, half), :]
    ) + tn(shared_ref[rows_at(core * part, part), :], second[pl.ds(half, part), :])
    forward[rows_at(other * width, width), :] = tn(att_other[...], branch)
    lanes = lambda side: pl.ds(pl.multiple_of(side * width, 128), width)
    cols_out[...] = forward[pl.ds(0, model), lanes(other)].astype(BF16)
    cols_send = remote(cols_out, cols_in, sems, 8, partner)
    cols_send.start()
    for b in range(3):
        value = nt(second[blocks[b], :], own_weight).astype(BF16)
        if b < 2:
            row_grad[rows_at(core * half + b * part, part), :] = value
        else:
            shared_grad[rows_at(core * part, part), :] = value
    cols_send.wait_recv()
    outg_ref[...] = (forward[pl.ds(0, model), lanes(core)] + cols_in[...].astype(F32)).astype(BF16)
    for copy in head_sends:
        copy.wait_recv()
    for copy in att_sends + head_sends + grad_sends + [first_part, second_part, cols_send]:
        copy.wait_send()
    if square:
        for copy in down_sends:
            copy.wait_send()
        for copy in far_sends:
            copy.wait()
    far_write = pltpu.make_async_copy(far_in, far_ref, load_sem.at[0])
    far_write.start()
    for place in range(3):
        pltpu.make_async_copy(stage.at[place], packed_ref.at[0], write_sem.at[place]).wait()
    output_moves.wait()
    far_write.wait()


def dense(square, out, shared_out, x, grad, cotangent, out_matrix, gain, bounds, up, down):
    model = x.shape[1]
    tokens = x.shape[0]
    part = tokens // 3
    length, width = out.shape
    units = up.shape[1]
    tile = units // 4
    anywhere = pl.BlockSpec(memory_space=pl.ANY)
    near = pl.BlockSpec(memory_space=pltpu.VMEM)
    both = 2 * tokens
    low = lambda *shape: pltpu.VMEM(shape, BF16)
    wide = lambda *shape: pltpu.VMEM(shape, F32)
    return pl.pallas_call(
        functools.partial(dense_kernel, square),
        in_specs=[near] * 4 + [anywhere] + [near] * 3 + [anywhere] * 2,
        out_specs=[anywhere] + [near] * 5 + [anywhere, anywhere],
        out_shape=[
            jax.ShapeDtypeStruct((3, part, model), BF16),
            jax.ShapeDtypeStruct((tokens, model), F32),
            jax.ShapeDtypeStruct((length, width), BF16),
            jax.ShapeDtypeStruct((length // 2, width), BF16),
            jax.ShapeDtypeStruct((model, width), BF16),
            jax.ShapeDtypeStruct((1, model), F32),
            jax.ShapeDtypeStruct((4, 2 * tile, model), BF16),
            jax.ShapeDtypeStruct((2, tile, model), BF16),
        ],
        scratch_shapes=[
            low(tokens, width), low(both, model), low(model, both), low(both, model), low(2, part, model),
            low(both, units), low(both, units), wide(tokens, model), wide(tokens, model), wide(tokens, model),
            low(model, units), low(units, model), low(tokens, model), low(2, tokens, model), low(2, tokens, model),
            low(tokens, width), low(model, width), low(model, width), low(3, 2 * tile, model), low(2, tile, model),
            pltpu.SemaphoreType.DMA((24,)),
            pltpu.SemaphoreType.DMA((24,)),
            pltpu.SemaphoreType.DMA((2,)),
            pltpu.SemaphoreType.DMA((3,)),
            pltpu.SemaphoreType.DMA((3,)),
        ],
        compiler_params=pltpu.CompilerParams(
            collective_id=1, has_side_effects=True, vmem_limit_bytes=63 * 1024 * 1024
        ),
        name="dense",
    )(out, shared_out, x, grad, cotangent, out_matrix, gain, bounds, up, down)


def add(*terms):
    total = terms[0].astype(F32)
    for term in terms[1:]:
        total = total + term.astype(F32)
    return total


def backward_kernel(square, pics, *refs):
    refs = list(refs)
    take = lambda count: [refs.pop(0) for _ in range(count)]
    names = ("aug", "qk", "v", "out", "do", "raw", "normed")
    row_in = dict(zip(names, take(7)))
    shared_in = dict(zip(names, take(7)))
    mix_in, x_in, midg_in, gain_first, gain_qk, gain_second_grad, bounds_ref = take(7)
    if square:
        packed_in, far_ref, outg_in = take(3)
        grad_out, total_ref, gains_ref, up_ref, down_ref, outw_ref = take(6)
    else:
        grad_own, mix_grad_ref, gains_sum = take(3)
    names = names[:-1]
    row = dict(zip(names, take(6)))
    shared = dict(zip(names, take(6)))
    normed, weight, x, midg = take(4)
    kaug, vaug, doaug, qsum, ksum, mixed, part_k, part_v, got_k, got_v = take(10)
    gain_sums, parts_out, parts_in = take(3)
    if square:
        grad_own, payload, gains_sum, outg = take(4)
        held, far_in, onward_out, onward_in, direct_in, line, whole_line, line_right, line_left = take(9)
        up_out, up_got = take(2)
        relay, final, core_got, chunks, chunk_whole, chunk_right, chunk_left, gain_parts, gain_got = take(9)
    sent, got, load_sem, local_sem = take(4)

    chip, core, zp, zq = here()
    z = 2 * zp + zq
    sems = (sent, got)
    partner = (chip, 1 - core, zp, zq)
    keep = (chip, zp, core, zq)
    cross = (chip, zp, core, 1 - zq)
    moves = core != zp
    near_x = (chip ^ 1, core, zp, zq)
    near_y = (chip ^ 2, core, zp, zq)
    along = [(chip, core, zp, 1 - zq), (chip, core, 1 - zp, zq), (chip, core, 1 - zp, 1 - zq)]
    tokens, model = x.shape
    part = tokens // 3
    half, length = 2 * part, 4 * part
    width = model // 2
    queries = half
    waits = []

    def load(source, target, at):
        copy = pltpu.make_async_copy(source, target, load_sem.at[at])
        copy.start()
        return copy

    def send(source, target, at, device):
        copy = remote(source, target, sems, at, device)
        copy.start()
        waits.append(copy)
        return copy

    if square:
        rows_count = packed_in.shape[1]
        span = rows_count // 2
        first_half, second_half = pl.ds(0, span), pl.ds(span, span)
        held_loads = [
            load(packed_in.at[chip ^ 1, first_half], held.at[0], 24),
            load(packed_in.at[chip ^ 2, second_half], held.at[1], 25),
            load(packed_in.at[chip, first_half], held.at[2], 26),
            load(packed_in.at[chip, second_half], held.at[3], 27),
        ]
        far_loads = [load(far_ref.at[i], far_in.at[i], 28 + i) for i in range(2)]
    keys_of = lambda ref: ref.at[:, pl.ds(width, width)]
    load_bufs = lambda source, target, at: [
        load(keys_of(source[name]) if name == "qk" else source[name], target[name], at + i)
        for i, name in enumerate(names)
    ]
    shared_loads = load_bufs(shared_in, shared, 0)
    row_loads = load_bufs(row_in, row, 6)
    late_loads = [
        load(row_in["normed"], normed.at[pl.ds(0, length)], 12),
        load(shared_in["normed"].at[rows_at(zq * part, part)], normed.at[pl.ds(length, part)], 13),
        load(
            shared_in["normed"].at[rows_at((2 + zq) * part, part)], normed.at[pl.ds(length + part, part)], 14
        ),
        load(mix_in, weight, 15),
        load(x_in, x, 16),
        load(midg_in, midg, 17),
    ]
    if square:
        late_loads.append(load(outg_in, outg, 18))
    if square:
        greet([partner, cross, near_x, near_y] + along, keep, moves)
        for copy in held_loads + far_loads:
            copy.wait()
        onward_out[0] = add(far_in[0], held[0]).astype(BF16)
        bulk_on_x = send(onward_out.at[0], onward_in.at[0], 11, near_x)
        onward_out[1] = add(far_in[1], held[1]).astype(BF16)
        bulk_on_y = send(onward_out.at[1], onward_in.at[1], 12, near_y)
        bulk_x = send(packed_in.at[chip ^ 1, second_half], direct_in.at[0], 2, near_x)
        bulk_y = send(packed_in.at[chip ^ 2, first_half], direct_in.at[1], 3, near_y)

        bulk_line = Line(line, whole_line, line_right, line_left, sems, 14)
        mix_line = Line(chunks, chunk_whole, chunk_right, chunk_left, sems, 26)
    else:
        greet([partner, along[0]])

    gain_sums[...] = jnp.zeros_like(gain_sums)

    def attend_back(bufs, bounds, count, q_lanes_to, k_to, v_to, at, between=None):
        def one(p, _):
            if between is not None:
                pl.when(p == 2)(between)
            lanes = pl.ds(pl.multiple_of(p * 128, 128), 128)
            key_lanes = pl.ds(pl.multiple_of(width + p * 128, 128), 128)
            attend_back_kernel(
                pics, bufs["aug"].at[pl.ds(2 * p, 2)], bufs["qk"].at[:, lanes], bufs["v"].at[:, lanes],
                bufs["out"].at[:, lanes], bufs["do"].at[:, lanes], bufs["raw"].at[:, lanes],
                bufs["raw"].at[:, key_lanes], gain_qk.at[:, lanes], gain_qk.at[:, key_lanes], bounds,
                q_lanes_to(p), k_to(p), v_to(p), gain_sums.at[pl.ds(at, 1), lanes], gain_sums.at[pl.ds(at + 1, 1), lanes],
                kaug, vaug, doaug.at[:, pl.ds(0, count)], qsum.at[:, pl.ds(0, count)], ksum,
            )
            return 0

        lax.fori_loop(0, width // 128, one, 0)

    def mixed_at(start, count, side):
        return lambda p: mixed.at[pl.ds(start, count), pl.ds(pl.multiple_of(side * width + p * 128, 128), 128)]

    whole_lanes = lambda ref: lambda p: ref.at[:, pl.ds(pl.multiple_of(p * 128, 128), 128)]
    for copy in shared_loads:
        copy.wait()
    attend_back(
        shared, bounds_ref.at[1], queries, mixed_at(length, queries, 0), whole_lanes(part_k), whole_lanes(part_v), 0
    )
    side_sends = []
    for i in range(2):
        theirs = rows_at((2 * i + 1 - zq) * part, part)
        there = pl.ds(i * part, part)
        side_sends.append(send(part_k.at[theirs], got_k.at[there], 7 + 2 * i, along[0]))
        side_sends.append(send(part_v.at[theirs], got_v.at[there], 8 + 2 * i, along[0]))
    for copy in row_loads:
        copy.wait()
    def start_line():
        for copy in (bulk_y, bulk_on_x, bulk_x, bulk_on_y):
            copy.wait_recv()
        first_sum = add(held[2], onward_in[0], direct_in[1]).astype(BF16)
        second_half_sum = add(held[3], onward_in[1], direct_in[0]).astype(BF16)
        for i in range(2):
            line[i] = first_sum[i * quarter_rows : (i + 1) * quarter_rows]
            line[2 + i] = second_half_sum[i * quarter_rows : (i + 1) * quarter_rows]
        bulk_line.start()

    if square:
        quarter_rows = rows_count // 4
    attend_back(
        row, bounds_ref.at[0], length, mixed_at(0, length, 0), mixed_at(0, length, 1), mixed_at(0, length, 2), 2,
        start_line if square else None,
    )

    if square:
        bulk_line.first()
    for copy in side_sends:
        copy.wait_recv()

    def shared_pair(p, _):
        lanes = pl.ds(pl.multiple_of(p * 128, 128), 128)
        key_lanes = pl.ds(pl.multiple_of(width + p * 128, 128), 128)
        shared_keys_kernel(
            part_k.at[:, lanes], part_v.at[:, lanes], got_k.at[:, lanes], got_v.at[:, lanes],
            shared["raw"].at[:, key_lanes], gain_qk.at[:, key_lanes], mixed_at(length, queries, 1)(p),
            mixed_at(length, queries, 2)(p), gain_sums.at[pl.ds(4, 1), lanes],
        )
        return 0

    lax.fori_loop(0, width // 128, shared_pair, 0)
    for copy in late_loads:
        copy.wait()
    other = 1 - core
    block_rows = lambda side, b: (
        rows_at(side * half + b * part, part) if b < 2 else rows_at(length + side * part, part)
    )
    for b in range(3):
        parts_out[pl.ds(b * part, part), :] = nt(mixed[block_rows(other, b), :], weight[...]).astype(BF16)
    part_send = send(parts_out, parts_in, 13, partner)
    if square:
        bulk_line.second()
    shard = model // 8
    if square:
        for i in range(3):
            lanes = slice(i * width, (i + 1) * width)
            value = tn(normed[...], mixed[:, lanes]).astype(BF16)
            for p in range(8):
                payload[p, :shard, lanes] = value[p * shard : (p + 1) * shard]
        bulk_line.third()
    else:
        for i in range(3):
            lanes = slice(i * width, (i + 1) * width)
            mix_grad_ref[:, lanes] = tn(normed[...], mixed[:, lanes]).astype(BF16)
    part_send.wait_recv()
    first_sum_gain = jnp.zeros((1, model), F32)
    for b in range(3):
        rows = pl.ds(b * part, part)
        upstream = nt(mixed[block_rows(core, b), :], weight[...]) + parts_in[rows, :].astype(F32)
        n, r = norm_parts(x[rows, :].astype(F32))
        value, more = norm_back(upstream, n, r, gain_first[...])
        first_sum_gain = first_sum_gain + more
        grad_own[rows, :] = (midg[rows, :] + value).astype(BF16)
    gains_sum[...] = jnp.zeros_like(gains_sum)
    gains_sum[0:1, :] = first_sum_gain
    mine_lanes = pl.ds(pl.multiple_of(core * width, 128), width)
    gains_sum[1:2, mine_lanes] = gain_sums[0:1, :] + gain_sums[2:3, :]
    gains_sum[2:3, mine_lanes] = gain_sums[3:4, :] + gain_sums[4:5, :]
    gains_sum[3:4, :] = gain_second_grad[...]

    if square:
        kept_rows, third_rows = grad_own.at[rows_at(zq * part, part)], grad_own.at[pl.ds(half, part)]
        grad_moves = Moves(
            [
                remote(kept_rows, grad_out.at[zq], sems, 0, keep),
                remote(third_rows, grad_out.at[2], sems, 1, keep),
            ],
            [
                pltpu.make_async_copy(kept_rows, grad_out.at[zq], local_sem.at[0]),
                pltpu.make_async_copy(third_rows, grad_out.at[2], local_sem.at[1]),
            ],
            remote(grad_own.at[rows_at((1 - zq) * part, part)], grad_out.at[zq], sems, 4, cross),
            moves,
        )
        grad_moves.start()
        gain_row = shard + shard // 3
        for p in range(8):
            payload[p, gain_row:, :] = jnp.zeros((16, 3 * width), BF16)
            payload[p, gain_row:, :shard] = gains_sum[:, p * shard : (p + 1) * shard].astype(BF16)
            for i in range(3):
                at = p * shard + i * (shard // 3)
                payload[p, shard:gain_row, i * width : (i + 1) * width] = outg[at : at + shard // 3, :]
        mine, theirs = 2 * chip + core, 2 * chip + 1 - core
        x_mine, x_other = 2 * (chip ^ 1) + core, 2 * (chip ^ 1) + 1 - core
        y_mine, y_other = 2 * (chip ^ 2) + core, 2 * (chip ^ 2) + 1 - core
        far_mine, far_other = 2 * (chip ^ 3) + core, 2 * (chip ^ 3) + 1 - core
        first = send(payload.at[far_mine], relay.at[0], 38, near_y)
        second = send(payload.at[far_other], relay.at[1], 39, near_x)
        direct_x = send(payload.at[x_other], final.at[0], 40, near_x)
        direct_y = send(payload.at[y_mine], final.at[1], 41, near_y)

        first.wait_recv()
        relay[2] = add(relay[0], payload[x_mine]).astype(BF16)
        onward_x = send(relay.at[2], final.at[2], 42, near_x)
        second.wait_recv()
        relay[3] = add(relay[1], payload[y_other]).astype(BF16)
        onward_y = send(relay.at[3], final.at[3], 43, near_y)
        bulk_line.fourth()
        direct_x.wait_recv()
        onward_y.wait_recv()
        relay[4] = add(payload[theirs], final[0], final[3]).astype(BF16)
        to_core = send(relay.at[4], core_got, 44, partner)
        direct_y.wait_recv()
        onward_x.wait_recv()
        kept = add(payload[mine], final[1], final[2])
        quarter = gain_row // 2
        for i in range(2):
            chunks[2 * core + i] = kept[i * quarter : (i + 1) * quarter].astype(BF16)
        to_core.wait_recv()
        for i in range(2):
            chunks[2 * (1 - core) + i] = core_got[i * quarter : (i + 1) * quarter]
        gain_parts[0] = (kept[gain_row:] + core_got[gain_row:].astype(F32)).astype(BF16)
        mix_line.start()
        gain_lanes = pl.ds(0, 128)
        gain_sends = [
            send(gain_parts.at[0, :, gain_lanes], gain_got.at[i, :, gain_lanes], 45 + i, along[i]) for i in range(3)
        ]
        bulk_line.fifth()
        mix_line.first()
        mix_line.second()
        mix_line.third()
        for copy in gain_sends:
            copy.wait_recv()
        gains_ref[...] = add(
            gain_parts[0, :, :128], gain_got[0, :, :128], gain_got[1, :, :128], gain_got[2, :, :128]
        )
        mix_line.fourth()
        bulk_line.sixth()

        def place(index, values):
            side, up = index // 2, index % 2
            lanes_of = lambda p: slice((2 * p + side) * width, (2 * p + side + 1) * width)
            below = shard - quarter
            for p in range(3):
                part_of = values[:, p * width : (p + 1) * width]
                if up == 0:
                    total_ref[0:quarter, lanes_of(p)] = part_of
                else:
                    total_ref[quarter:shard, lanes_of(p)] = part_of[:below]
                    rows = slice(p * (shard // 3), (p + 1) * (shard // 3))
                    outw_ref[rows, side * width : (side + 1) * width] = part_of[below:]

        flat = jnp.concatenate([whole_line[i] for i in range(4)], axis=0)
        tile = down_ref.shape[0]
        down_ref[...] = flat[:tile]
        ups = [flat[tile + 2 * shard * i : tile + 2 * shard * (i + 1)] for i in range(2)]
        for i in range(2):
            up_out[i] = jnp.where(core == 0, ups[i][shard:], ups[i][:shard])
        up_send = send(up_out, up_got, 48, partner)

        def place_up(side, i, values):
            for j in range(2):
                lanes = pl.ds(pl.multiple_of((2 * (2 * i + j) + side) * tile, 128), tile)
                up_ref[:, lanes] = values[:, j * tile : (j + 1) * tile]

        for i in range(2):
            place_up(core, i, jnp.where(core == 0, ups[i][:shard], ups[i][shard:]))
        up_send.wait_recv()
        for i in range(2):
            place_up(other, i, up_got[i])
        mix_line.fifth()
        mix_line.sixth()
        for i in range(4):
            place(i, chunk_whole[i])
        bulk_line.wait_sends()
        mix_line.wait_sends()
        grad_moves.wait()
    for copy in waits:
        copy.wait_send()


def backward_pass(square, pics, row, shared, weights, gains, bounds, *more):
    length, model = row[1].shape
    width = model // 2
    part = length // 4
    half, tokens = 2 * part, 3 * part
    shard = model // 8
    near = pl.BlockSpec(memory_space=pltpu.VMEM)
    anywhere = pl.BlockSpec(memory_space=pl.ANY)
    low = lambda *shape: (shape, BF16)
    wide = lambda *shape: (shape, F32)
    if square:
        rows = more[0].shape[1]
        tile = rows // 2
        outs = [
            (low(3, part, model), anywhere),
            (low(shard, 6 * width), near),
            (wide(16, 128), near),
            (low(shard, 8 * tile), near),
            (low(tile, model), near),
            (low(shard, model), near),
        ]
    else:
        outs = [(low(tokens, model), near), (low(model, 3 * width), near), (wide(16, model), near)]
    scratch = []
    for queries in (length, half):
        scratch += [
            low(2 * (width // 128), queries, 128), low(length, width), low(length, width), low(queries, width),
            low(queries, width), low(length, 2 * width),
        ]
    scratch += [
        low(length + half, model), low(model, 3 * width), low(tokens, model), wide(tokens, model),
        low(2, length, 128), low(2, length, 128), low(2, length, 128), wide(2, length, 128), wide(length, 128),
        low(length + half, 3 * width), low(length, width), low(length, width), low(half, width), low(half, width),
        wide(8, width), low(tokens, model), low(tokens, model),
    ]
    if square:
        span = rows // 2
        pieces = shard + shard // 3 + 16
        chunk = (pieces - 16) // 2
        scratch += [
            low(tokens, model), low(8, pieces, 3 * width), wide(16, model), low(model, width),
            low(4, span, model), low(2, span, model), low(2, span, model), low(2, span, model), low(2, span, model),
            low(4, rows // 4, model), low(4, rows // 4, model), low(3, rows // 4, model), low(3, rows // 4, model),
            low(2, shard, model), low(2, shard, model),
            low(5, pieces, 3 * width), low(4, pieces, 3 * width), low(pieces, 3 * width), low(4, chunk, 3 * width),
            low(4, chunk, 3 * width), low(3, chunk, 3 * width), low(3, chunk, 3 * width), low(1, 16, 3 * width),
            low(3, 16, 3 * width),
        ]
    return pl.pallas_call(
        functools.partial(backward_kernel, square, pics),
        in_specs=[anywhere] * 17 + [near] * 4 + [anywhere] * len(more),
        out_specs=[spec for _, spec in outs],
        out_shape=[jax.ShapeDtypeStruct(*shape) for shape, _ in outs],
        scratch_shapes=[pltpu.VMEM(*shape) for shape in scratch]
        + [
            pltpu.SemaphoreType.DMA((49,)),
            pltpu.SemaphoreType.DMA((49,)),
            pltpu.SemaphoreType.DMA((30,)),
            pltpu.SemaphoreType.DMA((2,)),
        ],
        compiler_params=pltpu.CompilerParams(
            collective_id=2, has_side_effects=True, vmem_limit_bytes=62 * 1024 * 1024
        ),
        name="backward_pass",
    )(*row, *shared, *weights, *gains, bounds, *more)


def local(
    tokens, lengths, pictures, first_gain, mix_weight, query_gain, key_gain, out_weight,
    second_gain, up_weight, down_weight, cotangent,
):
    chip, core, zp, zq = here()
    chips = lax.axis_size("chip")
    square = chips == 4
    rows = ("chip", "core")
    _, part, model = tokens.shape
    length = 4 * part
    half = 2 * part
    width = HEADS // 2 * HEAD
    pics = lengths.shape[1]
    shard = mix_weight.shape[0]

    hidden = up_weight.shape[1]
    tile = hidden // 8
    gains = [gain[None] for gain in (first_gain, query_gain, key_gain, second_gain)]
    if square:
        forward = forward_pass(
            True, pics, tokens, cotangent, lengths, mix_weight, *gains, up_weight, out_weight
        )
        up_half, out_matrix = forward[19:]
        down_half = down_weight
        gain_second = forward[5]
    else:
        gather = lambda weight: lax.all_gather(weight, rows, axis=0, tiled=True)
        half_of = lambda weight, axis: pick(weight, core, axis)
        mix_half = half_of(gather(mix_weight).reshape(model, 3, 2, width), 2).reshape(model, 3 * width)
        up_half = half_of(gather(up_weight).reshape(model, 4, 2, tile), 2).reshape(model, 4 * tile)
        down_half = half_of(gather(down_weight).reshape(4, 2, tile, model), 1).reshape(4 * tile, model)
        out_matrix = gather(out_weight)
        gains = lax.all_gather(jnp.concatenate(gains), rows, axis=0, tiled=False)
        gains = gains.transpose(1, 0, 2).reshape(4, 1, model).astype(F32)
        gain_second = gains[3]
        gain_qk = half_of(gains[1:3].reshape(2, 2, width), 1).reshape(1, model)
        forward = forward_pass(False, pics, tokens, cotangent, lengths, mix_half, gains[0], gain_qk)
    own_tokens, bounds, mix_half, grad_tokens, gain_first, _, gain_qk = forward[:7]
    normed, qk, v, raw, out, aug = forward[7:13]
    shared_normed, shared_qk, shared_v, shared_raw, shared_out, shared_aug = forward[13:19]

    def collect(mine, cross, third):
        mine = lax.ppermute(mine, COLUMN, KEEP)
        cross = lax.ppermute(cross, COLUMN, CROSS)
        third = lax.ppermute(third, COLUMN, KEEP)
        return jnp.stack([jnp.where(zq == 0, mine, cross), jnp.where(zq == 0, cross, mine), third])

    output, middle_grad, grad, shared_grad, out_grad, second_gain_grad, packed, far = dense(
        square, out, shared_out, own_tokens, grad_tokens, cotangent, out_matrix, gain_second, bounds,
        up_half, down_half,
    )
    row_side = (aug, qk, v, out, grad, raw, normed)
    shared_side = (shared_aug, shared_qk, shared_v, shared_out, shared_grad, shared_raw, shared_normed)
    weights = (mix_half, own_tokens, middle_grad)
    gains = (gain_first, gain_qk, second_gain_grad)
    if square:
        input_out, mix_out, gains_out, up_out, down_out, outw_out = backward_pass(
            True, pics, row_side, shared_side, weights, gains, bounds, packed, far, out_grad
        )
        gains_out = gains_out[:4, :shard]
        mix_out, up_out, down_out, outw_out = (
            array.astype(F32) for array in (mix_out, up_out, down_out, outw_out)
        )
    else:
        input_grad, mix_grad, gain_grads = backward_pass(
            False, pics, row_side, shared_side, weights, gains, bounds
        )

        def reduce(grad):
            return lax.psum(lax.psum_scatter(grad, rows, scatter_dimension=0, tiled=True), SEQ).astype(F32)

        first, second = input_grad[:part], input_grad[part:half]
        input_out = collect(
            jnp.where(zq == 0, first, second), jnp.where(zq == 0, second, first), input_grad[half:]
        )
        own_core = jnp.arange(2) == core
        eighth = model // 8
        down_grad = packed[:, None, :tile]
        down_out = reduce(jnp.where(own_core[None, :, None, None], down_grad, 0).reshape(hidden, model))
        up_grad = packed[:, tile : 2 * tile].reshape(4, 2, 2 * eighth, 2, tile).transpose(0, 2, 1, 3, 4)
        up_grad = up_grad.reshape(model, 4, 1, tile)
        up_out = reduce(jnp.where(own_core[None, None, :, None], up_grad, 0).reshape(model, hidden))
        out_grad = out_grad.reshape(model, 1, width)
        outw_out = reduce(jnp.where(own_core[None, :, None], out_grad, 0).reshape(model, model))
        mix_out = reduce(
            jnp.where(own_core[None, None, :, None], mix_grad.reshape(model, 3, 1, width), 0).reshape(model, 6 * width)
        )
        gain_grads = gain_grads[:4].reshape(4, 2 * chips, shard).transpose(1, 0, 2).astype(BF16)
        gains_out = reduce(gain_grads).reshape(4, shard)
    return (
        output, input_out, gains_out[0], mix_out, gains_out[1], gains_out[2], outw_out, gains_out[3],
        up_out, down_out,
    )


def solution(mesh):
    fsdp = mesh.shape["fsdp"]
    split = Mesh(mesh.devices.reshape(fsdp // 2, 2, 2, 2), ("chip", "core", "zp", "zq"))
    rows = ("chip", "core")
    return jax.shard_map(
        local,
        mesh=split,
        in_specs=(
            P(rows, SEQ, None),
            P(rows, None),
            P(rows, SEQ),
            P(rows),
            P(rows, None),
            P(rows),
            P(rows),
            P(rows, None),
            P(rows),
            P(rows, None),
            P(rows, None),
            P(rows, SEQ, None),
        ),
        out_specs=(
            P(rows, SEQ, None),
            P(rows, SEQ, None),
            P(rows),
            P(rows, None),
            P(rows),
            P(rows),
            P(rows, None),
            P(rows),
            P(rows, None),
            P(rows, None),
        ),
        check_vma=False,
    )
```

```python
import functools

import jax
import jax.numpy as jnp
from jax import lax
from jax.experimental import pallas as pl
from jax.experimental.pallas import tpu as pltpu
from jax.sharding import Mesh, PartitionSpec as P

HEADS = 12
HEAD = 64
EPSILON = 1e-06
BLOCK = 256
STEP = 512
MARK = 32.0
EXP2_FACTOR = HEAD**-0.5 * 1.4426950408889634
F32 = jnp.float32
BF16 = jnp.bfloat16
VMEM_LIMIT = 56 * 1024 * 1024

SEQ = ("zp", "zq")
COLUMN = ("core", "zp", "zq")
KEEP = [
    (core * 4 + z, (z // 2) * 4 + 2 * core + z % 2) for core in range(2) for z in range(4)
]
CROSS = [
    (core * 4 + z, (z // 2) * 4 + 2 * core + 1 - z % 2) for core in range(2) for z in range(4)
]


def swap(array, name, bit=1):
    count = lax.axis_size(name)
    return lax.ppermute(array, name, [(i, i ^ bit) for i in range(count)])


def pick(array, index, axis=0):
    return lax.dynamic_index_in_dim(array, index, axis, keepdims=False)


def group_ones(scale, size=128):
    row = lax.broadcasted_iota(jnp.int32, (size, size), 0) // HEAD
    column = lax.broadcasted_iota(jnp.int32, (size, size), 1) // HEAD
    return jnp.where(row == column, scale, 0.0).astype(BF16)


def group_sum(values, ones):
    return jnp.dot(values.astype(BF16), ones, preferred_element_type=F32)


def group_sum_fine(values, ones):
    high = values.astype(BF16)
    return group_sum(high, ones) + group_sum(values - high.astype(F32), ones)


def project_kernel(x_ref, gain_ref, weight_ref, qkg_ref, normed_ref, qk_ref, v_ref, raw_ref):
    both = qk_ref.shape[1]
    x = x_ref[...].astype(F32)
    center = x - jnp.mean(x, axis=-1, keepdims=True)
    spread = jnp.mean(center * center, axis=-1, keepdims=True)
    normed = (center * lax.rsqrt(spread + EPSILON) * gain_ref[...]).astype(BF16)
    normed_ref[...] = normed
    ones = group_ones(1.0 / HEAD, 256)
    for at in range(0, both, 256):
        lanes = slice(at, at + 256)
        raw = jnp.dot(normed, weight_ref[:, lanes], preferred_element_type=F32)
        raw_ref[:, lanes] = raw.astype(BF16)
        c = raw - group_sum(raw, ones)
        n = c * lax.rsqrt(group_sum(c * c, ones) + EPSILON)
        qk_ref[:, lanes] = (n * qkg_ref[:, lanes]).astype(BF16)
    v_ref[...] = jnp.dot(normed, weight_ref[:, both:], preferred_element_type=F32).astype(BF16)


def nt(a, b):
    return lax.dot_general(a, b, (((1,), (1,)), ((), ())), preferred_element_type=F32)


def tn(a, b):
    return lax.dot_general(a, b, (((0,), (0,)), ((), ())), preferred_element_type=F32)


def slots(queries, length, part):
    at = lax.broadcasted_iota(jnp.int32, (queries, 128), 0)
    if queries == length:
        return at
    return at % part + part * (lax.axis_index("zq") + 2 * (at // part))


def own_rows(ref, start, count, queries, part):
    if queries == ref.shape[0]:
        return ref[pl.ds(start, count), :]
    zq = lax.axis_index("zq")
    pieces = [
        ref[pl.ds(pl.multiple_of((zq + 2 * i) * part, part), part), :]
        for i in range(start // part, (start + count) // part)
    ]
    return jnp.concatenate(pieces, axis=0)


def query_marks(bounds_ref, place, queries, length, part, pics):
    at = slots(queries, length, part)
    inside = (at >= bounds_ref[0:1, :]) & (at < bounds_ref[2:3, :])
    values = jnp.where(inside, MARK, 0.0)
    return jnp.where(place == pics, MARK, values).astype(BF16)


def key_marks(bounds_ref, place, length, pics):
    at = lax.broadcasted_iota(jnp.int32, (length, 128), 0)
    inside = (at >= bounds_ref[0:1, :]) & (at < bounds_ref[1:2, :])
    values = jnp.where(inside, MARK, 0.0)
    values = jnp.where(place == pics, -MARK, values)
    return jnp.where((place > pics) & (place < pics + 4), 1.0, values).astype(BF16)


def attend_kernel(pics, q_ref, k_ref, v_ref, bounds_ref, out_ref, aug_ref, kaug, vaug, qaug):
    length = k_ref.shape[0]
    queries = out_ref.shape[0]
    part = length // 4
    lane = lax.broadcasted_iota(jnp.int32, (1, 128), 1)
    place = lane % HEAD
    sides = [lane < HEAD, lane >= HEAD]
    kmarks = key_marks(bounds_ref, place, length, pics)
    qmarks = query_marks(bounds_ref, place, queries, length, part, pics)
    qaug[...] = qmarks
    for h in range(2):
        kaug[h] = jnp.where(sides[h], k_ref[...], kmarks)
        vaug[h] = jnp.where(sides[h], v_ref[...], jnp.ones_like(v_ref))
    for b in range(queries // STEP):
        rows = pl.ds(b * STEP, STEP)
        mine = own_rows(q_ref, b * STEP, STEP, queries, part)
        query = [jnp.where(sides[h], mine, qaug[rows, :]) for h in range(2)]
        total = [jnp.zeros((STEP, 128), F32)] * 2
        for j in range(length // STEP):
            keys = pl.ds(j * STEP, STEP)
            scores = [nt(query[h], kaug[h, keys, :]) for h in range(2)]
            weights = [jnp.exp2(x * EXP2_FACTOR).astype(BF16) for x in scores]
            total = [
                total[h] + jnp.dot(weights[h], vaug[h, keys, :], preferred_element_type=F32) for h in range(2)
            ]
        results = []
        for h in range(2):
            results.append(total[h] / pltpu.roll(total[h], HEAD, 1))
            log_total = jnp.log(jnp.where(sides[h], 1.0, total[h])) * -(HEAD**0.5)
            first = log_total.astype(BF16)
            rest = log_total - first.astype(F32)
            middle = rest.astype(BF16)
            last = (rest - middle.astype(F32)).astype(BF16)
            logs = jnp.where(place == pics + 1, first, jnp.where(place == pics + 2, middle, last))
            slot = jnp.logical_not(sides[h]) & (place > pics) & (place < pics + 4)
            aug_ref[h, rows, :] = jnp.where(slot, logs, query[h])
        out_ref[rows, :] = jnp.where(sides[0], results[0], results[1]).astype(BF16)


def head_norm_back(e, raw, gain, means):
    raw = raw.astype(F32)
    c = raw - group_sum(raw, means)
    r = lax.rsqrt(group_sum(c * c, means) + EPSILON)
    n = c * r
    t = e * gain
    grad = r * (t - group_sum(t, means) - n * group_sum(t * n, means))
    return grad.astype(BF16), jnp.sum(e * n, axis=0, keepdims=True)


def attend_back_kernel(
    pics, aug_ref, k_ref, v_ref, out_ref, do_ref, rawq_ref, rawk_ref, qg_ref, kg_ref, bounds_ref,
    dq_ref, dk_ref, dv_ref, qgg_ref, kgg_ref, kaug, vaug, doaug, qsum, ksum,
):
    length = k_ref.shape[0]
    queries = do_ref.shape[0]
    part = length // 4
    whole = queries == length
    lane = lax.broadcasted_iota(jnp.int32, (1, 128), 1)
    place = lane % HEAD
    sides = [lane < HEAD, lane >= HEAD]
    kmarks = key_marks(bounds_ref, place, length, pics)
    vmarks = jnp.where(place < 2, 1.0, 0.0).astype(BF16)
    ones = group_ones(1.0)
    inner = group_sum_fine(do_ref[...].astype(F32) * out_ref[...].astype(F32), ones)
    inner = -pltpu.roll(inner, HEAD, 1)
    inner_high = inner.astype(BF16)
    inner_low = (inner - inner_high.astype(F32)).astype(BF16)
    zero = jnp.zeros((), BF16)
    gmarks = jnp.where(place == 0, inner_high, jnp.where(place == 1, inner_low, zero))
    for h in range(2):
        kaug[h] = jnp.where(sides[h], k_ref[...], kmarks)
        vaug[h] = jnp.where(sides[h], v_ref[...], vmarks)
        doaug[h] = jnp.where(sides[h], do_ref[...], gmarks)
    for b in range(length // STEP):
        keys = pl.ds(b * STEP, STEP)
        key = [kaug[h, keys, :] for h in range(2)]
        value = [vaug[h, keys, :] for h in range(2)]
        dk = [jnp.zeros((STEP, 128), F32)] * 2
        dv = [jnp.zeros((STEP, 128), F32)] * 2
        for j in range(queries // STEP):
            rows = pl.ds(j * STEP, STEP)
            query = [aug_ref[h, rows, :] for h in range(2)]
            grad = [doaug[h, rows, :] for h in range(2)]
            scores = [nt(key[h], query[h]) for h in range(2)]
            soft_grad = [nt(value[h], grad[h]) for h in range(2)]
            weights = [jnp.exp2(x * EXP2_FACTOR) for x in scores]
            score_grad = [(weights[h] * soft_grad[h]).astype(BF16) for h in range(2)]
            for h in range(2):
                part_sum = tn(score_grad[h], key[h])
                if b == 0:
                    qsum[h, rows, :] = part_sum
                else:
                    qsum[h, rows, :] += part_sum
                dk[h] = dk[h] + jnp.dot(score_grad[h], query[h], preferred_element_type=F32)
                dv[h] = dv[h] + jnp.dot(weights[h].astype(BF16), grad[h], preferred_element_type=F32)
        ksum[keys, :] = jnp.where(sides[0], dk[0], dk[1]) * HEAD**-0.5
        dv_ref[keys, :] = jnp.where(sides[0], dv[0], dv[1]).astype(BF16)

    means = group_ones(1.0 / HEAD)
    gain_sum = jnp.zeros((1, 128), F32)
    for b in range(queries // part):
        rows = pl.ds(b * part, part)
        e = jnp.where(sides[0], qsum[0, rows, :], qsum[1, rows, :]) * HEAD**-0.5
        raw = own_rows(rawq_ref, b * part, part, queries, part)
        dq_ref[rows, :], more = head_norm_back(e.astype(BF16).astype(F32), raw, qg_ref[...], means)
        gain_sum = gain_sum + more
    qgg_ref[...] = gain_sum
    gain_sum = jnp.zeros((1, 128), F32)
    for b in range(length // part):
        rows = pl.ds(b * part, part)
        e = ksum[rows, :].astype(BF16)
        if whole:
            dk_ref[rows, :], more = head_norm_back(e.astype(F32), rawk_ref[rows, :], kg_ref[...], means)
            gain_sum = gain_sum + more
        else:
            dk_ref[rows, :] = e
    kgg_ref[...] = gain_sum


def shared_keys_kernel(dk_ref, dv_ref, gotk_ref, gotv_ref, rawk_ref, kg_ref, outk_ref, outv_ref, kgg_ref):
    count = outk_ref.shape[0]
    part = count // 2
    means = group_ones(1.0 / HEAD)
    gain_sum = jnp.zeros((1, 128), F32)
    for b in range(2):
        rows = pl.ds(b * part, part)
        own = lambda ref: own_rows(ref, b * part, part, count, part)
        e = own(dk_ref).astype(F32) + gotk_ref[rows, :].astype(F32)
        outk_ref[rows, :], more = head_norm_back(e, own(rawk_ref), kg_ref[...], means)
        gain_sum = gain_sum + more
        outv_ref[rows, :] = (own(dv_ref).astype(F32) + gotv_ref[rows, :].astype(F32)).astype(BF16)
    kgg_ref[...] = gain_sum


def gelu_pair(h):
    size = jnp.abs(h)
    bell = jnp.exp2(h * h * -0.7213475204444817)
    t = 1.0 / (1.0 + 0.23164189 * size)
    series = t * (0.127414796 + t * (-0.142248368 + t * (0.7107068705 + t * (-0.7265760135 + t * 0.5307027145))))
    tail = series * bell
    below = jnp.where(h < 0.0, tail, 1.0 - tail)
    return h * below, below + h * (bell * 0.3989422804014327)


def norm_parts(values):
    center = values - jnp.mean(values, axis=-1, keepdims=True)
    spread = lax.rsqrt(jnp.mean(center * center, axis=-1, keepdims=True) + EPSILON)
    return center * spread, spread


def norm_back(upstream, n, r, gain):
    t = upstream * gain
    grad = r * (t - jnp.mean(t, axis=-1, keepdims=True) - n * jnp.mean(t * n, axis=-1, keepdims=True))
    return grad, jnp.sum(upstream * n, axis=0, keepdims=True)


MESH_ID = pl.DeviceIdType.MESH


def here():
    return lax.axis_index("chip"), lax.axis_index("core"), lax.axis_index("zp"), lax.axis_index("zq")


def remote(source, target, sems, at, device):
    sent, got = sems
    return pltpu.make_async_remote_copy(
        src_ref=source, dst_ref=target, send_sem=sent.at[at], recv_sem=got.at[at],
        device_id=device, device_id_type=MESH_ID,
    )


def greet(devices, maybe=None, moves=None):
    barrier = pltpu.get_barrier_semaphore()
    for device in devices:
        pl.semaphore_signal(barrier, inc=1, device_id=device, device_id_type=MESH_ID)
    if maybe is None:
        pl.semaphore_wait(barrier, len(devices))
        return

    @pl.when(moves)
    def _():
        pl.semaphore_signal(barrier, inc=1, device_id=maybe, device_id_type=MESH_ID)

    pl.semaphore_wait(barrier, len(devices) + jnp.where(moves, 1, 0))


def rows_at(start, count):
    return pl.ds(pl.multiple_of(start, 16), count)


class Moves:
    def __init__(self, moved, stays, crossed, moves):
        self.moved, self.stays, self.crossed, self.moves = moved, stays, crossed, moves

    def each(self, act):
        if self.crossed is not None:
            act(self.crossed)

        @pl.when(self.moves)
        def _():
            for copy in self.moved:
                act(copy)

        @pl.when(jnp.logical_not(self.moves))
        def _():
            for copy in self.stays:
                act(copy)

    def start(self):
        self.each(lambda copy: copy.start())

    def wait(self):
        self.each(lambda copy: copy.wait())


class Line:
    def __init__(self, parts, whole, right, left, sems, at):
        chip, core, zp, zq = here()
        self.z = 2 * zp + zq
        up, down = jnp.minimum(self.z + 1, 3), jnp.maximum(self.z - 1, 0)
        self.next = (chip, core, up // 2, up % 2)
        self.last = (chip, core, down // 2, down % 2)
        self.parts, self.whole, self.right, self.left = parts, whole, right, left
        self.sems, self.at, self.sends = sems, at, []

    def at_chip(self, z, *acts):
        @pl.when(self.z == z)
        def _():
            for act in acts:
                act()

    def part_copy(self, c, rightward):
        if rightward:
            return remote(self.parts.at[c], self.right.at[3 - c], self.sems, self.at + 3 - c, self.next)
        return remote(self.parts.at[c], self.left.at[c], self.sems, self.at + 3 + c, self.last)

    def whole_copy(self, c, rightward):
        if rightward:
            return remote(self.whole.at[c], self.whole.at[c], self.sems, self.at + 6 + c, self.next)
        return remote(self.whole.at[c], self.whole.at[c], self.sems, self.at + 8 + c, self.last)

    def send(self, z, make, c, rightward):
        self.sends.append((z, make, c, rightward))
        return lambda: make(c, rightward).start()

    def take(self, c, rightward):
        def act():
            self.part_copy(c, rightward).wait_recv()
            came = self.right[3 - c] if rightward else self.left[c]
            self.parts[c] = add(self.parts[c], came).astype(BF16)

        return act

    def got(self, c, rightward):
        return lambda: self.whole_copy(c, rightward).wait_recv()

    def start(self):
        part = self.part_copy
        self.at_chip(0, *[self.send(0, part, c, True) for c in (3, 2, 1)])
        self.at_chip(3, *[self.send(3, part, c, False) for c in (0, 1, 2)])

    def first(self):
        self.at_chip(1, self.take(3, True), self.send(1, self.part_copy, 3, True))
        self.at_chip(2, self.take(0, False), self.send(2, self.part_copy, 0, False))

    def second(self):
        part = self.part_copy
        self.at_chip(
            1, self.take(2, True), self.send(1, part, 2, True), self.take(0, False), self.send(1, part, 0, False)
        )
        self.at_chip(
            2, self.take(1, False), self.send(2, part, 1, False), self.take(3, True), self.send(2, part, 3, True)
        )

    def third(self):
        self.at_chip(0, self.take(0, False))
        self.at_chip(1, self.take(1, True), self.take(1, False))
        self.at_chip(2, self.take(2, True), self.take(2, False))
        self.at_chip(3, self.take(3, True))
        self.whole[self.z] = self.parts[self.z]
        for z in range(4):
            acts = [self.send(z, self.whole_copy, z, True)] if z < 3 else []
            acts += [self.send(z, self.whole_copy, z, False)] if z > 0 else []
            self.at_chip(z, *acts)

    def fourth(self):
        whole = self.whole_copy
        for z in (1, 2):
            self.at_chip(
                z, self.got(z - 1, True), self.send(z, whole, z - 1, True), self.got(z + 1, False),
                self.send(z, whole, z + 1, False),
            )

    def fifth(self):
        whole = self.whole_copy
        self.at_chip(1, self.got(3, False), self.send(1, whole, 3, False))
        self.at_chip(2, self.got(0, True), self.send(2, whole, 0, True))

    def sixth(self):
        self.at_chip(0, *[self.got(c, False) for c in (1, 2, 3)])
        self.at_chip(3, *[self.got(c, True) for c in (2, 1, 0)])

    def wait_sends(self):
        for z in range(4):
            mine = [make(c, rightward) for at, make, c, rightward in self.sends if at == z]
            self.at_chip(z, *[copy.wait_send for copy in mine])


def write_bounds(pics, lens_ref, bounds_ref, zp, zq, length):
    lane = lax.broadcasted_iota(jnp.int32, (8, 128), 1)
    lens = jnp.where(zp == 0, lens_ref[0], lens_ref[1])
    ends = lens
    for hop in (1, 2, 4, 8):
        ends = ends + jnp.where(lane >= hop, pltpu.roll(ends, hop, 1), 0)
    starts = ends - lens
    last = (lens > 0) & (pltpu.roll(lens, 127, 1) == 0)
    query_ends = jnp.where(last, length, ends)
    total = jnp.max(jnp.where(lane < pics, ends, 0), axis=1, keepdims=True)

    def both(values):
        values = jnp.where(lane < HEAD, jnp.where(lane < pics, values, 2 * length), 0)
        return values + pltpu.roll(values, HEAD, 1)

    tables = [both(starts), both(ends), both(query_ends), jnp.broadcast_to(total, (8, 128))]
    for t in range(4):
        table = tables[t]
        bounds_ref[0, t : t + 1, :] = jnp.where(zq == 0, table[0:1], table[1:2])
        bounds_ref[1, t : t + 1, :] = table[2:3]
    bounds_ref[:, 4:, :] = jnp.zeros((2, 4, 128), jnp.int32)


def forward_kernel(square, pics, *refs):
    refs = list(refs)
    take = lambda count: [refs.pop(0) for _ in range(count)]
    tokens_ref, cot_ref, lengths_ref, weight_in = take(4)
    if square:
        gain_in = take(4)
        up_in, outw_ref = take(2)
    else:
        gain_first_in, gain_qk_in = take(2)
    x_out, bounds_ref, mix_hbm, cot_hbm, gain_first, second_ref, gain_qk = take(7)
    names = ("normed", "qk", "v", "raw", "out", "aug")
    outs = [dict(zip(names, take(6))) for _ in range(2)]
    if square:
        up_hbm, outw_hbm = take(2)
    row_ref, shared_ref, cot_out, lens_ref, lens_out = take(5)
    scratch = [dict(zip(names, take(6))) for _ in range(2)]
    kaug, vaug, qaug = take(3)
    if square:
        mix_ref, gains_ref, up_ref, mix_out, gains_out, up_out, outw_out = take(7)
    sent, got, local_sem, write_sem = take(4)

    chip, core, zp, zq = here()
    z = 2 * zp + zq
    part = tokens_ref.shape[1]
    half, length = 2 * part, 4 * part
    sems = (sent, got)
    partner = (chip, 1 - core, zp, zq)
    side = (chip, core, zp, 1 - zq)
    keep = (chip, zp, core, zq)
    cross = (chip, zp, core, 1 - zq)
    moves = core != zp
    near_x = (chip ^ 1, core, zp, zq)
    near_y = (chip ^ 2, core, zp, zq)
    greet([partner, side, cross] + ([near_x, near_y] if square else []), keep, moves)

    def quarter(ref, index):
        return ref.at[rows_at(index * part, part)]

    own_row = remote(tokens_ref.at[zq], quarter(row_ref, z), sems, 0, keep)
    own_shared = remote(tokens_ref.at[2], quarter(shared_ref, z), sems, 2, keep)
    stay_row = pltpu.make_async_copy(tokens_ref.at[zq], quarter(row_ref, z), local_sem.at[0])
    stay_shared = pltpu.make_async_copy(tokens_ref.at[2], quarter(shared_ref, z), local_sem.at[1])

    @pl.when(moves)
    def _():
        own_row.start()

    @pl.when(jnp.logical_not(moves))
    def _():
        stay_row.start()

    cross_row = remote(tokens_ref.at[1 - zq], quarter(row_ref, z), sems, 1, cross)
    cross_row.start()

    lens_ref[...] = jnp.zeros_like(lens_ref)
    lens_ref[: lengths_ref.shape[0], :pics] = lengths_ref[...]
    lens_copy = remote(lens_ref, lens_out.at[core], sems, 8, partner)
    lens_copy.start()
    lens_stay = pltpu.make_async_copy(lens_ref, lens_out.at[core], local_sem.at[2])
    lens_stay.start()
    waits = []
    if square:
        shard = mix_ref.shape[1]
        tile = up_ref.shape[2] // 4
        width = mix_ref.shape[2] // 3
        for h in range(2):
            for i in range(3):
                mix_ref[h, :, i * width : (i + 1) * width] = weight_in[:, (2 * i + h) * width : (2 * i + h + 1) * width]
        gains_ref[...] = jnp.zeros_like(gains_ref)
        for i in range(4):
            gains_ref[i : i + 1, :shard] = gain_in[i][...].astype(F32)
        mine, theirs = 2 * chip + core, 2 * chip + 1 - core
        slot = [9]

        def send(source, target, device):
            copy = remote(source, target, sems, slot[0], device)
            slot[0] += 1
            copy.start()
            waits.append(copy)
            return copy

        def stay(source, target, at):
            copy = pltpu.make_async_copy(source, target, local_sem.at[at])
            copy.start()
            return copy

        def block(ref, start, count):
            return ref.at[rows_at(start, count)]

        mix_piece = lambda index: (block(mix_out, index * shard, shard), gains_out.at[index])

        def send_mix(sources, index, device):
            return [send(source, target, device) for source, target in zip(sources, mix_piece(index))]

        def arrived(copies):
            for copy in copies:
                copy.wait_recv()

        x_mine, y_other = 2 * (chip ^ 1) + core, 2 * (chip ^ 2) + 1 - core
        to_core = send_mix((mix_ref.at[1 - core], gains_ref), mine, partner)
        a_x = send_mix((mix_ref.at[core], gains_ref), mine, near_x)
        a_y = send_mix((mix_ref.at[core], gains_ref), mine, near_y)
        for h in range(2):
            for i in range(4):
                up_ref[h, :, i * tile : (i + 1) * tile] = up_in[:, (2 * i + h) * tile : (2 * i + h + 1) * tile]
        up_core = send(up_ref.at[1 - core], block(up_out, mine * shard, shard), partner)
        out_core = send(outw_ref, block(outw_out, mine * shard, shard), partner)
        stays = [
            stay(mix_ref.at[core], mix_piece(mine)[0], 3),
            stay(gains_ref, gains_out.at[mine], 4),
            stay(up_ref.at[core], block(up_out, mine * shard, shard), 5),
            stay(outw_ref, block(outw_out, mine * shard, shard), 6),
        ]
        arrived(to_core)
        b_x = send_mix(mix_piece(theirs), theirs, near_x)
        b_y = send_mix(mix_piece(theirs), theirs, near_y)
        arrived(a_x)
        a_far = send_mix(mix_piece(x_mine), x_mine, near_y)
        arrived(b_y)
        b_far = send_mix(mix_piece(y_other), y_other, near_x)
        for copy in stays:
            copy.wait()
        arrived([up_core])
        ohalf = shard // 2

        def bundle(first, from_chip):
            same, twin = 2 * from_chip + core, 2 * from_chip + 1 - core
            part_of = 0 if first else 1
            return [
                block(up_out, (same if first else twin) * shard, shard),
                block(outw_out, same * shard + part_of * ohalf, ohalf),
            ]

        def send_bundle(first, from_chip, device):
            return [send(ref, ref, device) for ref in bundle(first, from_chip)]

        first_x = send_bundle(True, chip, near_x)
        first_y = send_bundle(True, chip, near_y)
        second_x = send_bundle(False, chip, near_x)
        second_y = send_bundle(False, chip, near_y)

    cross_row.wait_send()

    @pl.when(moves)
    def _():
        own_row.wait_send()
        own_shared.start()

    @pl.when(jnp.logical_not(moves))
    def _():
        stay_shared.start()

    lens_copy.wait()
    lens_stay.wait()
    write_bounds(pics, lens_out, bounds_ref, zp, zq, length)
    if square:
        arrived(a_y + b_x + a_far + b_far)
        for p in range(gains_out.shape[0]):
            lanes = slice(p * shard, (p + 1) * shard)
            values = gains_out[p, :, :shard]
            gain_first[:, lanes] = values[0:1]
            second_ref[:, lanes] = values[3:4]
            half_pieces = gains_out.shape[0] // 2

            @pl.when(core == p // half_pieces)
            def _():
                at = (p % half_pieces) * shard
                gain_qk[:, at : at + shard] = values[1:2]
                gain_qk[:, width + at : width + at + shard] = values[2:3]
        weight = mix_out
    else:
        weight = weight_in
        width = weight.shape[1] // 3
        second_ref[...] = jnp.zeros_like(second_ref)
        gain_first[...] = gain_first_in[...]
        gain_qk[...] = gain_qk_in[...]
    writes = []

    def write(source, target, at):
        copy = pltpu.make_async_copy(source, target, write_sem.at[at])
        copy.start()
        writes.append(copy)

    write(weight, mix_hbm, 0)
    first, second = 2 * core + zq, 2 * core + 1 - zq
    other_first, other_second = 2 * (1 - core) + zq, 2 * (1 - core) + 1 - zq

    def forwarded(ref, index, at):
        return remote(quarter(ref, index), quarter(ref, index), sems, at, partner)

    def project(tokens, bufs, at):
        rows = rows_at(at * part, part)
        project_kernel(
            tokens.at[rows], gain_first, weight, gain_qk, bufs["normed"].at[rows], bufs["qk"].at[rows],
            bufs["v"].at[rows], bufs["raw"].at[rows],
        )

    def project_row(i, _):
        @pl.when(i == 0)
        def _():
            @pl.when(moves)
            def _():
                own_row.wait_recv()

            @pl.when(jnp.logical_not(moves))
            def _():
                stay_row.wait()

            forwarded(row_ref, first, 3).start()

        @pl.when(i == 1)
        def _():
            cross_row.wait_recv()
            forwarded(row_ref, second, 4).start()

        @pl.when(i == 2)
        def _():
            forwarded(row_ref, other_first, 3).wait_recv()

        @pl.when(i == 3)
        def _():
            forwarded(row_ref, other_second, 4).wait_recv()

        order = jnp.where(i == 0, first, jnp.where(i == 1, second, jnp.where(i == 2, other_first, other_second)))
        project(row_ref, scratch[0], order)
        return 0

    row_one, row_two = forwarded(row_ref, first, 3), forwarded(row_ref, second, 4)

    def attend(bufs, bounds):
        def one(p, _):
            lanes = pl.ds(pl.multiple_of(p * 128, 128), 128)
            attend_kernel(
                pics, bufs["qk"].at[:, lanes],
                bufs["qk"].at[:, pl.ds(pl.multiple_of(width + p * 128, 128), 128)], bufs["v"].at[:, lanes], bounds,
                bufs["out"].at[:, lanes], bufs["aug"].at[pl.ds(2 * p, 2)], kaug, vaug, qaug.at[pl.ds(0, bufs["out"].shape[0])],
            )
            return 0

        lax.fori_loop(0, width // 128, one, 0)

    lax.fori_loop(0, 4, project_row, 0)
    for i, name in enumerate(("normed", "qk", "v", "raw")):
        write(scratch[0][name], outs[0][name], 1 + i)
    write(row_ref.at[rows_at(core * half, half)], x_out.at[pl.ds(0, half)], 5)

    @pl.when(moves)
    def _():
        own_shared.wait_recv()

    @pl.when(jnp.logical_not(moves))
    def _():
        stay_shared.wait()

    to_side = remote(quarter(shared_ref, first), quarter(shared_ref, first), sems, 5, side)
    to_side.start()
    shared_one = remote(quarter(shared_ref, first), quarter(shared_ref, first), sems, 6, partner)
    shared_one.start()
    attend(scratch[0], bounds_ref.at[0])
    cot_moves = Moves(
        [remote(cot_ref.at[zq], cot_out, sems, 43, keep)],
        [pltpu.make_async_copy(cot_ref.at[zq], cot_out, local_sem.at[0])],
        None,
        moves,
    )
    cot_moves.start()
    write(scratch[0]["out"], outs[0]["out"], 6)
    write(scratch[0]["aug"], outs[0]["aug"], 7)
    to_side.wait_recv()
    shared_two = forwarded(shared_ref, second, 7)
    shared_two.start()
    if square:
        arrived(first_x + second_y)
        far_first = send_bundle(True, chip ^ 1, near_y)
        far_second = send_bundle(False, chip ^ 2, near_x)
    shared_one.wait_recv()
    shared_two.wait_recv()

    def project_shared(i, _):
        project(shared_ref, scratch[1], i)
        return 0

    lax.fori_loop(0, 4, project_shared, 0)
    for i, name in enumerate(("normed", "qk", "v", "raw")):
        write(scratch[1][name], outs[1][name], 8 + i)
    write(shared_ref.at[rows_at(first * part, part)], x_out.at[pl.ds(half, part)], 12)
    attend(scratch[1], bounds_ref.at[1])
    write(scratch[1]["out"], outs[1]["out"], 13)
    write(scratch[1]["aug"], outs[1]["aug"], 14)

    if square:
        arrived(first_y + second_x + far_first + far_second)
        sent_pieces = []
        for c in (chip ^ 1, chip ^ 2, chip ^ 3):
            target = block(outw_out, (2 * c + core) * shard, shard)
            sent_pieces.append(send(target, target, partner))
        write(up_out, up_hbm, 15)
        arrived(sent_pieces + [out_core])
        write(outw_out, outw_hbm, 17)
        for copy in waits:
            copy.wait_send()
    cot_moves.wait()
    write(cot_out, cot_hbm, 18)
    for copy in (row_one, row_two, shared_one, shared_two, to_side):
        copy.wait_send()

    @pl.when(moves)
    def _():
        own_shared.wait_send()

    for copy in writes:
        copy.wait()


def forward_pass(square, pics, tokens, cotangent, lengths, weight, *more):
    _, part, model = tokens.shape
    length, half, width = 4 * part, 2 * part, model // 2
    near = pl.BlockSpec(memory_space=pltpu.VMEM)
    anywhere = pl.BlockSpec(memory_space=pl.ANY)
    low = lambda *shape: (shape, BF16)
    wide = lambda *shape: (shape, F32)
    outs = [
        (low(3 * part, model), anywhere),
        (((2, 8, 128), jnp.int32), near),
        (low(model, 3 * width), anywhere),
        (low(part, model), anywhere),
        (wide(1, model), near),
        (wide(1, model), near),
        (wide(1, model), near),
    ]
    bufs = []
    for queries in (length, half):
        shapes = [
            low(length, model), low(length, 2 * width), low(length, width), low(length, 2 * width),
            low(queries, width), low(2 * (width // 128), queries, 128),
        ]
        outs += [(shape, anywhere) for shape in shapes]
        bufs += shapes
    table = ((8, 128), jnp.int32)
    scratch = [low(length, model), low(length, model), low(part, model), table, ((2, 8, 128), jnp.int32)] + bufs
    scratch += [low(2, length, 128), low(2, length, 128), low(length, 128)]
    if square:
        up, _ = more[4:]
        shard, hidden = up.shape
        landed = [low(model, hidden // 2), low(model, model)]
        outs += [(shape, anywhere) for shape in landed]
        scratch += [low(2, shard, 3 * width), wide(8, 128), low(2, shard, hidden // 2)]
        scratch += [low(model, 3 * width), wide(8, 8, 128)] + landed
    return pl.pallas_call(
        functools.partial(forward_kernel, square, pics),
        in_specs=[near] * (4 + len(more)),
        out_specs=[spec for _, spec in outs],
        out_shape=[jax.ShapeDtypeStruct(*shape) for shape, _ in outs],
        scratch_shapes=[pltpu.VMEM(*shape) for shape in scratch]
        + [
            pltpu.SemaphoreType.DMA((49,)),
            pltpu.SemaphoreType.DMA((49,)),
            pltpu.SemaphoreType.DMA((8,)),
            pltpu.SemaphoreType.DMA((19,)),
        ],
        compiler_params=pltpu.CompilerParams(
            collective_id=0, has_side_effects=True, vmem_limit_bytes=60 * 1024 * 1024
        ),
        name="forward_pass",
    )(tokens, cotangent, lengths, weight, *more)


def dense_kernel(
    square, out_ref, shared_ref, x, grad_ref, cot_ref, outw_ref, gain_ref, bounds_ref, up_ref, down_ref,
    output_ref, midg_ref, row_grad, shared_grad, outg_ref, gaing_ref, packed_ref, far_ref,
    att_other, second, turned, grad, cot_in, hidden_all, pre_all, forward, backward, middle, up, down,
    results, parts_out, parts_in, heads_out, cols_out, cols_in, stage, far_in,
    sent, got, load_sem, write_sem, local_sem,
):
    chip, core, zp, zq = here()
    sems = (sent, got)
    partner = (chip, 1 - core, zp, zq)
    keep = (chip, zp, core, zq)
    cross = (chip, zp, core, 1 - zq)
    moves = core != zp
    near_x = (chip ^ 1, core, zp, zq)
    near_y = (chip ^ 2, core, zp, zq)
    tokens, model = midg_ref.shape
    part = tokens // 3
    half = 2 * part
    width = out_ref.shape[1]
    units = up.shape[1]
    tile = units // 4
    other = 1 - core
    mine, theirs = pl.ds(0, tokens), pl.ds(tokens, tokens)
    own_down = down.at[rows_at(chip * tile, tile)] if square else down
    loads = [
        pltpu.make_async_copy(up_ref, up, load_sem.at[0]),
        pltpu.make_async_copy(down_ref, own_down, load_sem.at[1]),
    ]
    for copy in loads:
        copy.start()
    greet([partner, cross] + ([near_x, near_y] if square else []), keep, moves)
    att_sends = [
        remote(out_ref.at[rows_at(other * half, half)], att_other.at[pl.ds(0, half)], sems, 0, partner),
        remote(shared_ref.at[rows_at(other * part, part)], att_other.at[pl.ds(half, part)], sems, 1, partner),
    ]
    for copy in att_sends:
        copy.start()
    cot_move = Moves(
        [remote(cot_ref.at[2], cot_in.at[1], sems, 11, keep)],
        [pltpu.make_async_copy(cot_ref.at[2], cot_in.at[1], local_sem.at[0])],
        remote(cot_ref.at[1 - zq], cot_in.at[0], sems, 22, cross),
        moves,
    )
    cot_move.start()

    def down_half(index, which):
        return down.at[rows_at(index * tile + which * (tile // 2), tile // 2)]

    def send_down(index, which, at, device):
        copy = remote(down_half(index, which), down_half(index, which), sems, at, device)
        copy.start()
        return copy

    slot = lax.broadcasted_iota(jnp.int32, (part, 1), 0)
    filled, shared_filled = bounds_ref[0, 3:4, 0:1], bounds_ref[1, 3:4, 0:1]
    none = jnp.zeros((), BF16)

    def take_grad(values, at, start, limit, sem):
        rows = rows_at(at, part)
        grad[rows, :] = jnp.where(slot + start < limit, values, none)
        copy = remote(grad.at[rows], grad.at[rows_at(tokens + at, part)], sems, sem, partner)
        copy.start()
        return copy

    grad_sends = [take_grad(grad_ref[...], zq * part, (2 * core + zq) * part, filled, 2)]

    own_rows_of = lambda b: (
        out_ref[rows_at(core * half + b * part, part), :] if b < 2 else shared_ref[rows_at(core * part, part), :]
    )
    own_weight = outw_ref[rows_at(core * width, width), :]
    other_weight = outw_ref[rows_at(other * width, width), :]
    blocks = [pl.ds(b * part, part) for b in range(3)]
    for b in range(3):
        middle[blocks[b], :] = x[blocks[b], :].astype(F32) + jnp.dot(
            own_rows_of(b), own_weight, preferred_element_type=F32
        )
    for copy in loads:
        copy.wait()
    if square:
        down_sends = [
            send_down(chip, 0, 12, near_x), send_down(chip, 1, 13, near_y), send_down(chip, 0, 14, near_y),
            send_down(chip, 1, 15, near_x),
        ]
    for copy in att_sends:
        copy.wait_recv()
    for rows in blocks:
        value = middle[rows, :] + jnp.dot(att_other[rows, :], other_weight, preferred_element_type=F32)
        middle[rows, :] = value
        second[rows, :] = (norm_parts(value)[0] * gain_ref[...]).astype(BF16)
    second_send = remote(second.at[mine], second.at[theirs], sems, 3, partner)
    second_send.start()

    def hidden_forward(start):
        rows = pl.ds(start, tokens)

        def one_tile(i, _):
            here_units = pl.ds(pl.multiple_of(i * tile, 128), tile)
            hidden, slope = gelu_pair(jnp.dot(second[rows, :], up[:, here_units], preferred_element_type=F32))
            hidden_all[rows, here_units] = hidden.astype(BF16)
            pre_all[rows, here_units] = slope.astype(BF16)
            return 0

        lax.fori_loop(0, 4, one_tile, 0)

    def hidden_backward(start):
        rows = pl.ds(start, tokens)

        def one_tile(i, _):
            here_units = pl.ds(pl.multiple_of(i * tile, 128), tile)
            pre_grad = nt(grad[rows, :], down[rows_at(i * tile, tile), :]) * pre_all[rows, here_units].astype(F32)
            pre_all[rows, here_units] = pre_grad.astype(BF16)
            return 0

        lax.fori_loop(0, 4, one_tile, 0)

    hidden_forward(0)
    if square:
        down_sends[0].wait_recv()
        down_sends[1].wait_recv()
        down_sends += [send_down(chip ^ 1, 0, 16, near_y), send_down(chip ^ 2, 1, 17, near_x)]
    second_send.wait_recv()
    hidden_forward(tokens)
    if square:
        for copy in down_sends[2:]:
            copy.wait_recv()
    for b in range(3):
        rows, there = pl.ds(tokens + b * part, part), blocks[b]
        parts_out[0, there, :] = jnp.dot(hidden_all[rows, :], down[...], preferred_element_type=F32).astype(BF16)
    first_part = remote(parts_out.at[0], parts_in.at[0], sems, 4, partner)
    first_part.start()
    for rows in blocks:
        forward[rows, :] = middle[rows, :] + jnp.dot(hidden_all[rows, :], down[...], preferred_element_type=F32)
    turned[...] = second[...].T
    first_part.wait_recv()
    for rows in blocks:
        results[rows, :] = (forward[rows, :] + parts_in[0, rows, :].astype(F32)).astype(BF16)
    kept_rows, third_rows = results.at[rows_at(zq * part, part)], results.at[pl.ds(half, part)]
    output_moves = Moves(
        [
            remote(kept_rows, output_ref.at[zq], sems, 19, keep),
            remote(third_rows, output_ref.at[2], sems, 20, keep),
        ],
        [
            pltpu.make_async_copy(kept_rows, output_ref.at[zq], local_sem.at[1]),
            pltpu.make_async_copy(third_rows, output_ref.at[2], local_sem.at[2]),
        ],
        remote(results.at[rows_at((1 - zq) * part, part)], output_ref.at[zq], sems, 21, cross),
        moves,
    )
    output_moves.start()
    cot_move.wait()
    grad_sends.append(take_grad(cot_in[0], (1 - zq) * part, (2 * core + 1 - zq) * part, filled, 18))
    grad_sends.append(take_grad(cot_in[1], half, (2 * core + zq) * part, shared_filled, 23))
    hidden_backward(0)
    for copy in grad_sends:
        copy.wait_recv()
    hidden_backward(tokens)
    quarter = model // 4
    far_sends = [
        remote(stage.at[0, pl.ds(0, tile)], far_in.at[0], sems, 9, near_y),
        remote(stage.at[0, pl.ds(tile, tile)], far_in.at[1], sems, 10, near_x),
    ]

    def weight_grads(i, _):
        target = chip ^ (3 - i) if square else 3 - i
        place = jnp.where(i == 0, 0, 1 + i % 2)

        @pl.when(i == 3)
        def _():
            pltpu.make_async_copy(stage.at[place], packed_ref.at[target], write_sem.at[place]).wait()

        here_units = pl.ds(pl.multiple_of(target * tile, 128), tile)
        stage[place, pl.ds(0, tile), :] = tn(hidden_all[:, here_units], grad[...]).astype(BF16)
        values = jnp.dot(
            turned[rows_at(target * quarter, quarter), :], pre_all[...], preferred_element_type=F32
        ).astype(BF16)
        for j in range(2):
            stage[place, pl.ds(tile + j * quarter, quarter), :] = values[:, j * model : (j + 1) * model]
        pltpu.make_async_copy(stage.at[place], packed_ref.at[target], write_sem.at[place]).start()
        if square:

            @pl.when(i == 0)
            def _():
                for copy in far_sends:
                    copy.start()

        return 0

    lax.fori_loop(0, 4, weight_grads, 0)

    for b in range(3):
        rows, there = pl.ds(tokens + b * part, part), blocks[b]
        parts_out[1, there, :] = nt(pre_all[rows, :], up[...]).astype(BF16)
    second_part = remote(parts_out.at[1], parts_in.at[1], sems, 5, partner)
    second_part.start()
    for rows in blocks:
        backward[rows, :] = nt(pre_all[rows, :], up[...])
    second_send.wait_send()
    second_part.wait_recv()
    gain_sum = jnp.zeros(gaing_ref.shape, F32)
    for rows in blocks:
        n, r = norm_parts(middle[rows, :])
        upstream = backward[rows, :] + parts_in[1, rows, :].astype(F32)
        more, gain_more = norm_back(upstream, n, r, gain_ref[...])
        gain_sum = gain_sum + gain_more
        value = grad[rows, :].astype(F32) + more
        midg_ref[rows, :] = value
        branch = value.astype(BF16)
        second[rows, :] = branch
        heads_out[rows, :] = nt(branch, other_weight).astype(BF16)
    gaing_ref[...] = gain_sum
    head_sends = [
        remote(heads_out.at[pl.ds(0, half)], row_grad.at[rows_at(core * half, half)], sems, 6, partner),
        remote(heads_out.at[pl.ds(half, part)], shared_grad.at[rows_at(core * part, part)], sems, 7, partner),
    ]
    for copy in head_sends:
        copy.start()
    branch = second[mine, :]
    forward[rows_at(core * width, width), :] = tn(
        out_ref[rows_at(core * half, half), :], second[pl.ds(0, half), :]
    ) + tn(shared_ref[rows_at(core * part, part), :], second[pl.ds(half, part), :])
    forward[rows_at(other * width, width), :] = tn(att_other[...], branch)
    lanes = lambda side: pl.ds(pl.multiple_of(side * width, 128), width)
    cols_out[...] = forward[pl.ds(0, model), lanes(other)].astype(BF16)
    cols_send = remote(cols_out, cols_in, sems, 8, partner)
    cols_send.start()
    for b in range(3):
        value = nt(second[blocks[b], :], own_weight).astype(BF16)
        if b < 2:
            row_grad[rows_at(core * half + b * part, part), :] = value
        else:
            shared_grad[rows_at(core * part, part), :] = value
    cols_send.wait_recv()
    outg_ref[...] = (forward[pl.ds(0, model), lanes(core)] + cols_in[...].astype(F32)).astype(BF16)
    for copy in head_sends:
        copy.wait_recv()
    for copy in att_sends + head_sends + grad_sends + [first_part, second_part, cols_send]:
        copy.wait_send()
    if square:
        for copy in down_sends:
            copy.wait_send()
        for copy in far_sends:
            copy.wait()
    far_write = pltpu.make_async_copy(far_in, far_ref, load_sem.at[0])
    far_write.start()
    for place in range(3):
        pltpu.make_async_copy(stage.at[place], packed_ref.at[0], write_sem.at[place]).wait()
    output_moves.wait()
    far_write.wait()


def dense(square, out, shared_out, x, grad, cotangent, out_matrix, gain, bounds, up, down):
    model = x.shape[1]
    tokens = x.shape[0]
    part = tokens // 3
    length, width = out.shape
    units = up.shape[1]
    tile = units // 4
    anywhere = pl.BlockSpec(memory_space=pl.ANY)
    near = pl.BlockSpec(memory_space=pltpu.VMEM)
    both = 2 * tokens
    low = lambda *shape: pltpu.VMEM(shape, BF16)
    wide = lambda *shape: pltpu.VMEM(shape, F32)
    return pl.pallas_call(
        functools.partial(dense_kernel, square),
        in_specs=[near] * 4 + [anywhere] + [near] * 3 + [anywhere] * 2,
        out_specs=[anywhere] + [near] * 5 + [anywhere, anywhere],
        out_shape=[
            jax.ShapeDtypeStruct((3, part, model), BF16),
            jax.ShapeDtypeStruct((tokens, model), F32),
            jax.ShapeDtypeStruct((length, width), BF16),
            jax.ShapeDtypeStruct((length // 2, width), BF16),
            jax.ShapeDtypeStruct((model, width), BF16),
            jax.ShapeDtypeStruct((1, model), F32),
            jax.ShapeDtypeStruct((4, 2 * tile, model), BF16),
            jax.ShapeDtypeStruct((2, tile, model), BF16),
        ],
        scratch_shapes=[
            low(tokens, width), low(both, model), low(model, both), low(both, model), low(2, part, model),
            low(both, units), low(both, units), wide(tokens, model), wide(tokens, model), wide(tokens, model),
            low(model, units), low(units, model), low(tokens, model), low(2, tokens, model), low(2, tokens, model),
            low(tokens, width), low(model, width), low(model, width), low(3, 2 * tile, model), low(2, tile, model),
            pltpu.SemaphoreType.DMA((24,)),
            pltpu.SemaphoreType.DMA((24,)),
            pltpu.SemaphoreType.DMA((2,)),
            pltpu.SemaphoreType.DMA((3,)),
            pltpu.SemaphoreType.DMA((3,)),
        ],
        compiler_params=pltpu.CompilerParams(
            collective_id=1, has_side_effects=True, vmem_limit_bytes=63 * 1024 * 1024
        ),
        name="dense",
    )(out, shared_out, x, grad, cotangent, out_matrix, gain, bounds, up, down)


def add(*terms):
    total = terms[0].astype(F32)
    for term in terms[1:]:
        total = total + term.astype(F32)
    return total


def backward_kernel(square, pics, *refs):
    refs = list(refs)
    take = lambda count: [refs.pop(0) for _ in range(count)]
    names = ("aug", "qk", "v", "out", "do", "raw", "normed")
    row_in = dict(zip(names, take(7)))
    shared_in = dict(zip(names, take(7)))
    mix_in, x_in, midg_in, gain_first, gain_qk, gain_second_grad, bounds_ref = take(7)
    if square:
        packed_in, far_ref, outg_in = take(3)
        grad_out, total_ref, gains_ref, up_ref, down_ref, outw_ref = take(6)
    else:
        grad_own, mix_grad_ref, gains_sum = take(3)
    names = names[:-1]
    row = dict(zip(names, take(6)))
    shared = dict(zip(names, take(6)))
    normed, weight, x, midg = take(4)
    kaug, vaug, doaug, qsum, ksum, mixed, part_k, part_v, got_k, got_v = take(10)
    gain_sums, parts_out, parts_in = take(3)
    if square:
        grad_own, payload, gains_sum, outg = take(4)
        held, far_in, onward_out, onward_in, direct_in, line, whole_line, line_right, line_left = take(9)
        up_out, up_got = take(2)
        relay, final, core_got, chunks, chunk_whole, chunk_right, chunk_left, gain_parts, gain_got = take(9)
    sent, got, load_sem, local_sem = take(4)

    chip, core, zp, zq = here()
    z = 2 * zp + zq
    sems = (sent, got)
    partner = (chip, 1 - core, zp, zq)
    keep = (chip, zp, core, zq)
    cross = (chip, zp, core, 1 - zq)
    moves = core != zp
    near_x = (chip ^ 1, core, zp, zq)
    near_y = (chip ^ 2, core, zp, zq)
    along = [(chip, core, zp, 1 - zq), (chip, core, 1 - zp, zq), (chip, core, 1 - zp, 1 - zq)]
    tokens, model = x.shape
    part = tokens // 3
    half, length = 2 * part, 4 * part
    width = model // 2
    queries = half
    waits = []

    def load(source, target, at):
        copy = pltpu.make_async_copy(source, target, load_sem.at[at])
        copy.start()
        return copy

    def send(source, target, at, device):
        copy = remote(source, target, sems, at, device)
        copy.start()
        waits.append(copy)
        return copy

    if square:
        rows_count = packed_in.shape[1]
        span = rows_count // 2
        first_half, second_half = pl.ds(0, span), pl.ds(span, span)
        held_loads = [
            load(packed_in.at[chip ^ 1, first_half], held.at[0], 24),
            load(packed_in.at[chip ^ 2, second_half], held.at[1], 25),
            load(packed_in.at[chip, first_half], held.at[2], 26),
            load(packed_in.at[chip, second_half], held.at[3], 27),
        ]
        far_loads = [load(far_ref.at[i], far_in.at[i], 28 + i) for i in range(2)]
    keys_of = lambda ref: ref.at[:, pl.ds(width, width)]
    load_bufs = lambda source, target, at: [
        load(keys_of(source[name]) if name == "qk" else source[name], target[name], at + i)
        for i, name in enumerate(names)
    ]
    shared_loads = load_bufs(shared_in, shared, 0)
    row_loads = load_bufs(row_in, row, 6)
    late_loads = [
        load(row_in["normed"], normed.at[pl.ds(0, length)], 12),
        load(shared_in["normed"].at[rows_at(zq * part, part)], normed.at[pl.ds(length, part)], 13),
        load(
            shared_in["normed"].at[rows_at((2 + zq) * part, part)], normed.at[pl.ds(length + part, part)], 14
        ),
        load(mix_in, weight, 15),
        load(x_in, x, 16),
        load(midg_in, midg, 17),
    ]
    if square:
        late_loads.append(load(outg_in, outg, 18))
    if square:
        greet([partner, cross, near_x, near_y] + along, keep, moves)
        for copy in held_loads + far_loads:
            copy.wait()
        onward_out[0] = add(far_in[0], held[0]).astype(BF16)
        bulk_on_x = send(onward_out.at[0], onward_in.at[0], 11, near_x)
        onward_out[1] = add(far_in[1], held[1]).astype(BF16)
        bulk_on_y = send(onward_out.at[1], onward_in.at[1], 12, near_y)
        bulk_x = send(packed_in.at[chip ^ 1, second_half], direct_in.at[0], 2, near_x)
        bulk_y = send(packed_in.at[chip ^ 2, first_half], direct_in.at[1], 3, near_y)

        bulk_line = Line(line, whole_line, line_right, line_left, sems, 14)
        mix_line = Line(chunks, chunk_whole, chunk_right, chunk_left, sems, 26)
    else:
        greet([partner, along[0]])

    gain_sums[...] = jnp.zeros_like(gain_sums)

    def attend_back(bufs, bounds, count, q_lanes_to, k_to, v_to, at, between=None):
        def one(p, _):
            if between is not None:
                pl.when(p == 2)(between)
            lanes = pl.ds(pl.multiple_of(p * 128, 128), 128)
            key_lanes = pl.ds(pl.multiple_of(width + p * 128, 128), 128)
            attend_back_kernel(
                pics, bufs["aug"].at[pl.ds(2 * p, 2)], bufs["qk"].at[:, lanes], bufs["v"].at[:, lanes],
                bufs["out"].at[:, lanes], bufs["do"].at[:, lanes], bufs["raw"].at[:, lanes],
                bufs["raw"].at[:, key_lanes], gain_qk.at[:, lanes], gain_qk.at[:, key_lanes], bounds,
                q_lanes_to(p), k_to(p), v_to(p), gain_sums.at[pl.ds(at, 1), lanes], gain_sums.at[pl.ds(at + 1, 1), lanes],
                kaug, vaug, doaug.at[:, pl.ds(0, count)], qsum.at[:, pl.ds(0, count)], ksum,
            )
            return 0

        lax.fori_loop(0, width // 128, one, 0)

    def mixed_at(start, count, side):
        return lambda p: mixed.at[pl.ds(start, count), pl.ds(pl.multiple_of(side * width + p * 128, 128), 128)]

    whole_lanes = lambda ref: lambda p: ref.at[:, pl.ds(pl.multiple_of(p * 128, 128), 128)]
    for copy in shared_loads:
        copy.wait()
    attend_back(
        shared, bounds_ref.at[1], queries, mixed_at(length, queries, 0), whole_lanes(part_k), whole_lanes(part_v), 0
    )
    side_sends = []
    for i in range(2):
        theirs = rows_at((2 * i + 1 - zq) * part, part)
        there = pl.ds(i * part, part)
        side_sends.append(send(part_k.at[theirs], got_k.at[there], 7 + 2 * i, along[0]))
        side_sends.append(send(part_v.at[theirs], got_v.at[there], 8 + 2 * i, along[0]))
    for copy in row_loads:
        copy.wait()
    def start_line():
        for copy in (bulk_y, bulk_on_x, bulk_x, bulk_on_y):
            copy.wait_recv()
        first_sum = add(held[2], onward_in[0], direct_in[1]).astype(BF16)
        second_half_sum = add(held[3], onward_in[1], direct_in[0]).astype(BF16)
        for i in range(2):
            line[i] = first_sum[i * quarter_rows : (i + 1) * quarter_rows]
            line[2 + i] = second_half_sum[i * quarter_rows : (i + 1) * quarter_rows]
        bulk_line.start()

    if square:
        quarter_rows = rows_count // 4
    attend_back(
        row, bounds_ref.at[0], length, mixed_at(0, length, 0), mixed_at(0, length, 1), mixed_at(0, length, 2), 2,
        start_line if square else None,
    )

    if square:
        bulk_line.first()
    for copy in side_sends:
        copy.wait_recv()

    def shared_pair(p, _):
        lanes = pl.ds(pl.multiple_of(p * 128, 128), 128)
        key_lanes = pl.ds(pl.multiple_of(width + p * 128, 128), 128)
        shared_keys_kernel(
            part_k.at[:, lanes], part_v.at[:, lanes], got_k.at[:, lanes], got_v.at[:, lanes],
            shared["raw"].at[:, key_lanes], gain_qk.at[:, key_lanes], mixed_at(length, queries, 1)(p),
            mixed_at(length, queries, 2)(p), gain_sums.at[pl.ds(4, 1), lanes],
        )
        return 0

    lax.fori_loop(0, width // 128, shared_pair, 0)
    for copy in late_loads:
        copy.wait()
    other = 1 - core
    block_rows = lambda side, b: (
        rows_at(side * half + b * part, part) if b < 2 else rows_at(length + side * part, part)
    )
    for b in range(3):
        parts_out[pl.ds(b * part, part), :] = nt(mixed[block_rows(other, b), :], weight[...]).astype(BF16)
    part_send = send(parts_out, parts_in, 13, partner)
    if square:
        bulk_line.second()
    shard = model // 8
    if square:
        for i in range(3):
            lanes = slice(i * width, (i + 1) * width)
            value = tn(normed[...], mixed[:, lanes]).astype(BF16)
            for p in range(8):
                payload[p, :shard, lanes] = value[p * shard : (p + 1) * shard]
        bulk_line.third()
    else:
        for i in range(3):
            lanes = slice(i * width, (i + 1) * width)
            mix_grad_ref[:, lanes] = tn(normed[...], mixed[:, lanes]).astype(BF16)
    part_send.wait_recv()
    first_sum_gain = jnp.zeros((1, model), F32)
    for b in range(3):
        rows = pl.ds(b * part, part)
        upstream = nt(mixed[block_rows(core, b), :], weight[...]) + parts_in[rows, :].astype(F32)
        n, r = norm_parts(x[rows, :].astype(F32))
        value, more = norm_back(upstream, n, r, gain_first[...])
        first_sum_gain = first_sum_gain + more
        grad_own[rows, :] = (midg[rows, :] + value).astype(BF16)
    gains_sum[...] = jnp.zeros_like(gains_sum)
    gains_sum[0:1, :] = first_sum_gain
    mine_lanes = pl.ds(pl.multiple_of(core * width, 128), width)
    gains_sum[1:2, mine_lanes] = gain_sums[0:1, :] + gain_sums[2:3, :]
    gains_sum[2:3, mine_lanes] = gain_sums[3:4, :] + gain_sums[4:5, :]
    gains_sum[3:4, :] = gain_second_grad[...]

    if square:
        kept_rows, third_rows = grad_own.at[rows_at(zq * part, part)], grad_own.at[pl.ds(half, part)]
        grad_moves = Moves(
            [
                remote(kept_rows, grad_out.at[zq], sems, 0, keep),
                remote(third_rows, grad_out.at[2], sems, 1, keep),
            ],
            [
                pltpu.make_async_copy(kept_rows, grad_out.at[zq], local_sem.at[0]),
                pltpu.make_async_copy(third_rows, grad_out.at[2], local_sem.at[1]),
            ],
            remote(grad_own.at[rows_at((1 - zq) * part, part)], grad_out.at[zq], sems, 4, cross),
            moves,
        )
        grad_moves.start()
        gain_row = shard + shard // 3
        for p in range(8):
            payload[p, gain_row:, :] = jnp.zeros((16, 3 * width), BF16)
            payload[p, gain_row:, :shard] = gains_sum[:, p * shard : (p + 1) * shard].astype(BF16)
            for i in range(3):
                at = p * shard + i * (shard // 3)
                payload[p, shard:gain_row, i * width : (i + 1) * width] = outg[at : at + shard // 3, :]
        mine, theirs = 2 * chip + core, 2 * chip + 1 - core
        x_mine, x_other = 2 * (chip ^ 1) + core, 2 * (chip ^ 1) + 1 - core
        y_mine, y_other = 2 * (chip ^ 2) + core, 2 * (chip ^ 2) + 1 - core
        far_mine, far_other = 2 * (chip ^ 3) + core, 2 * (chip ^ 3) + 1 - core
        first = send(payload.at[far_mine], relay.at[0], 38, near_y)
        second = send(payload.at[far_other], relay.at[1], 39, near_x)
        direct_x = send(payload.at[x_other], final.at[0], 40, near_x)
        direct_y = send(payload.at[y_mine], final.at[1], 41, near_y)

        first.wait_recv()
        relay[2] = add(relay[0], payload[x_mine]).astype(BF16)
        onward_x = send(relay.at[2], final.at[2], 42, near_x)
        second.wait_recv()
        relay[3] = add(relay[1], payload[y_other]).astype(BF16)
        onward_y = send(relay.at[3], final.at[3], 43, near_y)
        bulk_line.fourth()
        direct_x.wait_recv()
        onward_y.wait_recv()
        relay[4] = add(payload[theirs], final[0], final[3]).astype(BF16)
        to_core = send(relay.at[4], core_got, 44, partner)
        direct_y.wait_recv()
        onward_x.wait_recv()
        kept = add(payload[mine], final[1], final[2])
        quarter = gain_row // 2
        for i in range(2):
            chunks[2 * core + i] = kept[i * quarter : (i + 1) * quarter].astype(BF16)
        to_core.wait_recv()
        for i in range(2):
            chunks[2 * (1 - core) + i] = core_got[i * quarter : (i + 1) * quarter]
        gain_parts[0] = (kept[gain_row:] + core_got[gain_row:].astype(F32)).astype(BF16)
        mix_line.start()
        gain_lanes = pl.ds(0, 128)
        gain_sends = [
            send(gain_parts.at[0, :, gain_lanes], gain_got.at[i, :, gain_lanes], 45 + i, along[i]) for i in range(3)
        ]
        bulk_line.fifth()
        mix_line.first()
        mix_line.second()
        mix_line.third()
        for copy in gain_sends:
            copy.wait_recv()
        gains_ref[...] = add(
            gain_parts[0, :, :128], gain_got[0, :, :128], gain_got[1, :, :128], gain_got[2, :, :128]
        )
        mix_line.fourth()
        bulk_line.sixth()

        def place(index, values):
            side, up = index // 2, index % 2
            lanes_of = lambda p: slice((2 * p + side) * width, (2 * p + side + 1) * width)
            below = shard - quarter
            for p in range(3):
                part_of = values[:, p * width : (p + 1) * width]
                if up == 0:
                    total_ref[0:quarter, lanes_of(p)] = part_of
                else:
                    total_ref[quarter:shard, lanes_of(p)] = part_of[:below]
                    rows = slice(p * (shard // 3), (p + 1) * (shard // 3))
                    outw_ref[rows, side * width : (side + 1) * width] = part_of[below:]

        flat = jnp.concatenate([whole_line[i] for i in range(4)], axis=0)
        tile = down_ref.shape[0]
        down_ref[...] = flat[:tile]
        ups = [flat[tile + 2 * shard * i : tile + 2 * shard * (i + 1)] for i in range(2)]
        for i in range(2):
            up_out[i] = jnp.where(core == 0, ups[i][shard:], ups[i][:shard])
        up_send = send(up_out, up_got, 48, partner)

        def place_up(side, i, values):
            for j in range(2):
                lanes = pl.ds(pl.multiple_of((2 * (2 * i + j) + side) * tile, 128), tile)
                up_ref[:, lanes] = values[:, j * tile : (j + 1) * tile]

        for i in range(2):
            place_up(core, i, jnp.where(core == 0, ups[i][:shard], ups[i][shard:]))
        up_send.wait_recv()
        for i in range(2):
            place_up(other, i, up_got[i])
        mix_line.fifth()
        mix_line.sixth()
        for i in range(4):
            place(i, chunk_whole[i])
        bulk_line.wait_sends()
        mix_line.wait_sends()
        grad_moves.wait()
    for copy in waits:
        copy.wait_send()


def backward_pass(square, pics, row, shared, weights, gains, bounds, *more):
    length, model = row[1].shape
    width = model // 2
    part = length // 4
    half, tokens = 2 * part, 3 * part
    shard = model // 8
    near = pl.BlockSpec(memory_space=pltpu.VMEM)
    anywhere = pl.BlockSpec(memory_space=pl.ANY)
    low = lambda *shape: (shape, BF16)
    wide = lambda *shape: (shape, F32)
    if square:
        rows = more[0].shape[1]
        tile = rows // 2
        outs = [
            (low(3, part, model), anywhere),
            (low(shard, 6 * width), near),
            (wide(16, 128), near),
            (low(shard, 8 * tile), near),
            (low(tile, model), near),
            (low(shard, model), near),
        ]
    else:
        outs = [(low(tokens, model), near), (low(model, 3 * width), near), (wide(16, model), near)]
    scratch = []
    for queries in (length, half):
        scratch += [
            low(2 * (width // 128), queries, 128), low(length, width), low(length, width), low(queries, width),
            low(queries, width), low(length, 2 * width),
        ]
    scratch += [
        low(length + half, model), low(model, 3 * width), low(tokens, model), wide(tokens, model),
        low(2, length, 128), low(2, length, 128), low(2, length, 128), wide(2, length, 128), wide(length, 128),
        low(length + half, 3 * width), low(length, width), low(length, width), low(half, width), low(half, width),
        wide(8, width), low(tokens, model), low(tokens, model),
    ]
    if square:
        span = rows // 2
        pieces = shard + shard // 3 + 16
        chunk = (pieces - 16) // 2
        scratch += [
            low(tokens, model), low(8, pieces, 3 * width), wide(16, model), low(model, width),
            low(4, span, model), low(2, span, model), low(2, span, model), low(2, span, model), low(2, span, model),
            low(4, rows // 4, model), low(4, rows // 4, model), low(3, rows // 4, model), low(3, rows // 4, model),
            low(2, shard, model), low(2, shard, model),
            low(5, pieces, 3 * width), low(4, pieces, 3 * width), low(pieces, 3 * width), low(4, chunk, 3 * width),
            low(4, chunk, 3 * width), low(3, chunk, 3 * width), low(3, chunk, 3 * width), low(1, 16, 3 * width),
            low(3, 16, 3 * width),
        ]
    return pl.pallas_call(
        functools.partial(backward_kernel, square, pics),
        in_specs=[anywhere] * 17 + [near] * 4 + [anywhere] * len(more),
        out_specs=[spec for _, spec in outs],
        out_shape=[jax.ShapeDtypeStruct(*shape) for shape, _ in outs],
        scratch_shapes=[pltpu.VMEM(*shape) for shape in scratch]
        + [
            pltpu.SemaphoreType.DMA((49,)),
            pltpu.SemaphoreType.DMA((49,)),
            pltpu.SemaphoreType.DMA((30,)),
            pltpu.SemaphoreType.DMA((2,)),
        ],
        compiler_params=pltpu.CompilerParams(
            collective_id=2, has_side_effects=True, vmem_limit_bytes=62 * 1024 * 1024
        ),
        name="backward_pass",
    )(*row, *shared, *weights, *gains, bounds, *more)


def local(
    tokens, lengths, pictures, first_gain, mix_weight, query_gain, key_gain, out_weight,
    second_gain, up_weight, down_weight, cotangent,
):
    chip, core, zp, zq = here()
    chips = lax.axis_size("chip")
    square = chips == 4
    rows = ("chip", "core")
    _, part, model = tokens.shape
    length = 4 * part
    half = 2 * part
    width = HEADS // 2 * HEAD
    pics = lengths.shape[1]
    shard = mix_weight.shape[0]

    hidden = up_weight.shape[1]
    tile = hidden // 8
    gains = [gain[None] for gain in (first_gain, query_gain, key_gain, second_gain)]
    if square:
        forward = forward_pass(
            True, pics, tokens, cotangent, lengths, mix_weight, *gains, up_weight, out_weight
        )
        up_half, out_matrix = forward[19:]
        down_half = down_weight
        gain_second = forward[5]
    else:
        gather = lambda weight: lax.all_gather(weight, rows, axis=0, tiled=True)
        half_of = lambda weight, axis: pick(weight, core, axis)
        mix_half = half_of(gather(mix_weight).reshape(model, 3, 2, width), 2).reshape(model, 3 * width)
        up_half = half_of(gather(up_weight).reshape(model, 4, 2, tile), 2).reshape(model, 4 * tile)
        down_half = half_of(gather(down_weight).reshape(4, 2, tile, model), 1).reshape(4 * tile, model)
        out_matrix = gather(out_weight)
        gains = lax.all_gather(jnp.concatenate(gains), rows, axis=0, tiled=False)
        gains = gains.transpose(1, 0, 2).reshape(4, 1, model).astype(F32)
        gain_second = gains[3]
        gain_qk = half_of(gains[1:3].reshape(2, 2, width), 1).reshape(1, model)
        forward = forward_pass(False, pics, tokens, cotangent, lengths, mix_half, gains[0], gain_qk)
    own_tokens, bounds, mix_half, grad_tokens, gain_first, _, gain_qk = forward[:7]
    normed, qk, v, raw, out, aug = forward[7:13]
    shared_normed, shared_qk, shared_v, shared_raw, shared_out, shared_aug = forward[13:19]

    def collect(mine, cross, third):
        mine = lax.ppermute(mine, COLUMN, KEEP)
        cross = lax.ppermute(cross, COLUMN, CROSS)
        third = lax.ppermute(third, COLUMN, KEEP)
        return jnp.stack([jnp.where(zq == 0, mine, cross), jnp.where(zq == 0, cross, mine), third])

    output, middle_grad, grad, shared_grad, out_grad, second_gain_grad, packed, far = dense(
        square, out, shared_out, own_tokens, grad_tokens, cotangent, out_matrix, gain_second, bounds,
        up_half, down_half,
    )
    row_side = (aug, qk, v, out, grad, raw, normed)
    shared_side = (shared_aug, shared_qk, shared_v, shared_out, shared_grad, shared_raw, shared_normed)
    weights = (mix_half, own_tokens, middle_grad)
    gains = (gain_first, gain_qk, second_gain_grad)
    if square:
        input_out, mix_out, gains_out, up_out, down_out, outw_out = backward_pass(
            True, pics, row_side, shared_side, weights, gains, bounds, packed, far, out_grad
        )
        gains_out = gains_out[:4, :shard]
        mix_out, up_out, down_out, outw_out = (
            array.astype(F32) for array in (mix_out, up_out, down_out, outw_out)
        )
    else:
        input_grad, mix_grad, gain_grads = backward_pass(
            False, pics, row_side, shared_side, weights, gains, bounds
        )

        def reduce(grad):
            return lax.psum(lax.psum_scatter(grad, rows, scatter_dimension=0, tiled=True), SEQ).astype(F32)

        first, second = input_grad[:part], input_grad[part:half]
        input_out = collect(
            jnp.where(zq == 0, first, second), jnp.where(zq == 0, second, first), input_grad[half:]
        )
        own_core = jnp.arange(2) == core
        eighth = model // 8
        down_grad = packed[:, None, :tile]
        down_out = reduce(jnp.where(own_core[None, :, None, None], down_grad, 0).reshape(hidden, model))
        up_grad = packed[:, tile : 2 * tile].reshape(4, 2, 2 * eighth, 2, tile).transpose(0, 2, 1, 3, 4)
        up_grad = up_grad.reshape(model, 4, 1, tile)
        up_out = reduce(jnp.where(own_core[None, None, :, None], up_grad, 0).reshape(model, hidden))
        out_grad = out_grad.reshape(model, 1, width)
        outw_out = reduce(jnp.where(own_core[None, :, None], out_grad, 0).reshape(model, model))
        mix_out = reduce(
            jnp.where(own_core[None, None, :, None], mix_grad.reshape(model, 3, 1, width), 0).reshape(model, 6 * width)
        )
        gain_grads = gain_grads[:4].reshape(4, 2 * chips, shard).transpose(1, 0, 2).astype(BF16)
        gains_out = reduce(gain_grads).reshape(4, shard)
    return (
        output, input_out, gains_out[0], mix_out, gains_out[1], gains_out[2], outw_out, gains_out[3],
        up_out, down_out,
    )


def solution(mesh):
    fsdp = mesh.shape["fsdp"]
    split = Mesh(mesh.devices.reshape(fsdp // 2, 2, 2, 2), ("chip", "core", "zp", "zq"))
    rows = ("chip", "core")
    return jax.shard_map(
        local,
        mesh=split,
        in_specs=(
            P(rows, SEQ, None),
            P(rows, None),
            P(rows, SEQ),
            P(rows),
            P(rows, None),
            P(rows),
            P(rows),
            P(rows, None),
            P(rows),
            P(rows, None),
            P(rows, None),
            P(rows, SEQ, None),
        ),
        out_specs=(
            P(rows, SEQ, None),
            P(rows, SEQ, None),
            P(rows),
            P(rows, None),
            P(rows),
            P(rows),
            P(rows, None),
            P(rows),
            P(rows, None),
            P(rows, None),
        ),
        check_vma=False,
    )
```

```python
import functools

import jax
import jax.numpy as jnp
from jax import lax
from jax.experimental import pallas as pl
from jax.experimental.pallas import tpu as pltpu
from jax.sharding import Mesh, PartitionSpec as P

HEADS = 12
HEAD = 64
EPSILON = 1e-06
BLOCK = 256
STEP = 512
MARK = 32.0
EXP2_FACTOR = HEAD**-0.5 * 1.4426950408889634
F32 = jnp.float32
BF16 = jnp.bfloat16
VMEM_LIMIT = 56 * 1024 * 1024

SEQ = ("zp", "zq")
COLUMN = ("core", "zp", "zq")
KEEP = [
    (core * 4 + z, (z // 2) * 4 + 2 * core + z % 2) for core in range(2) for z in range(4)
]
CROSS = [
    (core * 4 + z, (z // 2) * 4 + 2 * core + 1 - z % 2) for core in range(2) for z in range(4)
]


def swap(array, name, bit=1):
    count = lax.axis_size(name)
    return lax.ppermute(array, name, [(i, i ^ bit) for i in range(count)])


def pick(array, index, axis=0):
    return lax.dynamic_index_in_dim(array, index, axis, keepdims=False)


def group_ones(scale, size=128):
    row = lax.broadcasted_iota(jnp.int32, (size, size), 0) // HEAD
    column = lax.broadcasted_iota(jnp.int32, (size, size), 1) // HEAD
    return jnp.where(row == column, scale, 0.0).astype(BF16)


def group_sum(values, ones):
    return jnp.dot(values.astype(BF16), ones, preferred_element_type=F32)


def group_sum_fine(values, ones):
    high = values.astype(BF16)
    return group_sum(high, ones) + group_sum(values - high.astype(F32), ones)


def project_kernel(x_ref, gain_ref, weight_ref, qkg_ref, normed_ref, qk_ref, v_ref, raw_ref):
    both = qk_ref.shape[1]
    x = x_ref[...].astype(F32)
    center = x - jnp.mean(x, axis=-1, keepdims=True)
    spread = jnp.mean(center * center, axis=-1, keepdims=True)
    normed = (center * lax.rsqrt(spread + EPSILON) * gain_ref[...]).astype(BF16)
    normed_ref[...] = normed
    ones = group_ones(1.0 / HEAD, 256)
    for at in range(0, both, 256):
        lanes = slice(at, at + 256)
        raw = jnp.dot(normed, weight_ref[:, lanes], preferred_element_type=F32)
        raw_ref[:, lanes] = raw.astype(BF16)
        c = raw - group_sum(raw, ones)
        n = c * lax.rsqrt(group_sum(c * c, ones) + EPSILON)
        qk_ref[:, lanes] = (n * qkg_ref[:, lanes]).astype(BF16)
    v_ref[...] = jnp.dot(normed, weight_ref[:, both:], preferred_element_type=F32).astype(BF16)


def nt(a, b):
    return lax.dot_general(a, b, (((1,), (1,)), ((), ())), preferred_element_type=F32)


def tn(a, b):
    return lax.dot_general(a, b, (((0,), (0,)), ((), ())), preferred_element_type=F32)


def slots(queries, length, part):
    at = lax.broadcasted_iota(jnp.int32, (queries, 128), 0)
    if queries == length:
        return at
    return at % part + part * (lax.axis_index("zq") + 2 * (at // part))


def own_rows(ref, start, count, queries, part):
    if queries == ref.shape[0]:
        return ref[pl.ds(start, count), :]
    zq = lax.axis_index("zq")
    pieces = [
        ref[pl.ds(pl.multiple_of((zq + 2 * i) * part, part), part), :]
        for i in range(start // part, (start + count) // part)
    ]
    return jnp.concatenate(pieces, axis=0)


def query_marks(bounds_ref, place, queries, length, part, pics):
    at = slots(queries, length, part)
    inside = (at >= bounds_ref[0:1, :]) & (at < bounds_ref[2:3, :])
    values = jnp.where(inside, MARK, 0.0)
    return jnp.where(place == pics, MARK, values).astype(BF16)


def key_marks(bounds_ref, place, length, pics):
    at = lax.broadcasted_iota(jnp.int32, (length, 128), 0)
    inside = (at >= bounds_ref[0:1, :]) & (at < bounds_ref[1:2, :])
    values = jnp.where(inside, MARK, 0.0)
    values = jnp.where(place == pics, -MARK, values)
    return jnp.where((place > pics) & (place < pics + 4), 1.0, values).astype(BF16)


def attend_kernel(pics, q_ref, k_ref, v_ref, bounds_ref, out_ref, aug_ref, kaug, vaug, qaug):
    length = k_ref.shape[0]
    queries = out_ref.shape[0]
    part = length // 4
    lane = lax.broadcasted_iota(jnp.int32, (1, 128), 1)
    place = lane % HEAD
    sides = [lane < HEAD, lane >= HEAD]
    kmarks = key_marks(bounds_ref, place, length, pics)
    qmarks = query_marks(bounds_ref, place, queries, length, part, pics)
    qaug[...] = qmarks
    for h in range(2):
        kaug[h] = jnp.where(sides[h], k_ref[...], kmarks)
        vaug[h] = jnp.where(sides[h], v_ref[...], jnp.ones_like(v_ref))
    for b in range(queries // STEP):
        rows = pl.ds(b * STEP, STEP)
        mine = own_rows(q_ref, b * STEP, STEP, queries, part)
        query = [jnp.where(sides[h], mine, qaug[rows, :]) for h in range(2)]
        total = [jnp.zeros((STEP, 128), F32)] * 2
        for j in range(length // STEP):
            keys = pl.ds(j * STEP, STEP)
            scores = [nt(query[h], kaug[h, keys, :]) for h in range(2)]
            weights = [jnp.exp2(x * EXP2_FACTOR).astype(BF16) for x in scores]
            total = [
                total[h] + jnp.dot(weights[h], vaug[h, keys, :], preferred_element_type=F32) for h in range(2)
            ]
        results = []
        for h in range(2):
            results.append(total[h] / pltpu.roll(total[h], HEAD, 1))
            log_total = jnp.log(jnp.where(sides[h], 1.0, total[h])) * -(HEAD**0.5)
            first = log_total.astype(BF16)
            rest = log_total - first.astype(F32)
            middle = rest.astype(BF16)
            last = (rest - middle.astype(F32)).astype(BF16)
            logs = jnp.where(place == pics + 1, first, jnp.where(place == pics + 2, middle, last))
            slot = jnp.logical_not(sides[h]) & (place > pics) & (place < pics + 4)
            aug_ref[h, rows, :] = jnp.where(slot, logs, query[h])
        out_ref[rows, :] = jnp.where(sides[0], results[0], results[1]).astype(BF16)


def head_norm_back(e, raw, gain, means):
    raw = raw.astype(F32)
    c = raw - group_sum(raw, means)
    r = lax.rsqrt(group_sum(c * c, means) + EPSILON)
    n = c * r
    t = e * gain
    grad = r * (t - group_sum(t, means) - n * group_sum(t * n, means))
    return grad.astype(BF16), jnp.sum(e * n, axis=0, keepdims=True)


def attend_back_kernel(
    pics, aug_ref, k_ref, v_ref, out_ref, do_ref, rawq_ref, rawk_ref, qg_ref, kg_ref, bounds_ref,
    dq_ref, dk_ref, dv_ref, qgg_ref, kgg_ref, kaug, vaug, doaug, qsum, ksum,
):
    length = k_ref.shape[0]
    queries = do_ref.shape[0]
    part = length // 4
    whole = queries == length
    lane = lax.broadcasted_iota(jnp.int32, (1, 128), 1)
    place = lane % HEAD
    sides = [lane < HEAD, lane >= HEAD]
    kmarks = key_marks(bounds_ref, place, length, pics)
    vmarks = jnp.where(place < 2, 1.0, 0.0).astype(BF16)
    ones = group_ones(1.0)
    inner = group_sum_fine(do_ref[...].astype(F32) * out_ref[...].astype(F32), ones)
    inner = -pltpu.roll(inner, HEAD, 1)
    inner_high = inner.astype(BF16)
    inner_low = (inner - inner_high.astype(F32)).astype(BF16)
    zero = jnp.zeros((), BF16)
    gmarks = jnp.where(place == 0, inner_high, jnp.where(place == 1, inner_low, zero))
    for h in range(2):
        kaug[h] = jnp.where(sides[h], k_ref[...], kmarks)
        vaug[h] = jnp.where(sides[h], v_ref[...], vmarks)
        doaug[h] = jnp.where(sides[h], do_ref[...], gmarks)
    for b in range(length // STEP):
        keys = pl.ds(b * STEP, STEP)
        key = [kaug[h, keys, :] for h in range(2)]
        value = [vaug[h, keys, :] for h in range(2)]
        dk = [jnp.zeros((STEP, 128), F32)] * 2
        dv = [jnp.zeros((STEP, 128), F32)] * 2
        for j in range(queries // STEP):
            rows = pl.ds(j * STEP, STEP)
            query = [aug_ref[h, rows, :] for h in range(2)]
            grad = [doaug[h, rows, :] for h in range(2)]
            scores = [nt(key[h], query[h]) for h in range(2)]
            soft_grad = [nt(value[h], grad[h]) for h in range(2)]
            weights = [jnp.exp2(x * EXP2_FACTOR) for x in scores]
            score_grad = [(weights[h] * soft_grad[h]).astype(BF16) for h in range(2)]
            for h in range(2):
                part_sum = tn(score_grad[h], key[h])
                if b == 0:
                    qsum[h, rows, :] = part_sum
                else:
                    qsum[h, rows, :] += part_sum
                dk[h] = dk[h] + jnp.dot(score_grad[h], query[h], preferred_element_type=F32)
                dv[h] = dv[h] + jnp.dot(weights[h].astype(BF16), grad[h], preferred_element_type=F32)
        ksum[keys, :] = jnp.where(sides[0], dk[0], dk[1]) * HEAD**-0.5
        dv_ref[keys, :] = jnp.where(sides[0], dv[0], dv[1]).astype(BF16)

    means = group_ones(1.0 / HEAD)
    gain_sum = jnp.zeros((1, 128), F32)
    for b in range(queries // part):
        rows = pl.ds(b * part, part)
        e = jnp.where(sides[0], qsum[0, rows, :], qsum[1, rows, :]) * HEAD**-0.5
        raw = own_rows(rawq_ref, b * part, part, queries, part)
        dq_ref[rows, :], more = head_norm_back(e.astype(BF16).astype(F32), raw, qg_ref[...], means)
        gain_sum = gain_sum + more
    qgg_ref[...] = gain_sum
    gain_sum = jnp.zeros((1, 128), F32)
    for b in range(length // part):
        rows = pl.ds(b * part, part)
        e = ksum[rows, :].astype(BF16)
        if whole:
            dk_ref[rows, :], more = head_norm_back(e.astype(F32), rawk_ref[rows, :], kg_ref[...], means)
            gain_sum = gain_sum + more
        else:
            dk_ref[rows, :] = e
    kgg_ref[...] = gain_sum


def shared_keys_kernel(dk_ref, dv_ref, gotk_ref, gotv_ref, rawk_ref, kg_ref, outk_ref, outv_ref, kgg_ref):
    count = outk_ref.shape[0]
    part = count // 2
    means = group_ones(1.0 / HEAD)
    gain_sum = jnp.zeros((1, 128), F32)
    for b in range(2):
        rows = pl.ds(b * part, part)
        own = lambda ref: own_rows(ref, b * part, part, count, part)
        e = own(dk_ref).astype(F32) + gotk_ref[rows, :].astype(F32)
        outk_ref[rows, :], more = head_norm_back(e, own(rawk_ref), kg_ref[...], means)
        gain_sum = gain_sum + more
        outv_ref[rows, :] = (own(dv_ref).astype(F32) + gotv_ref[rows, :].astype(F32)).astype(BF16)
    kgg_ref[...] = gain_sum


def gelu_pair(h):
    size = jnp.abs(h)
    bell = jnp.exp2(h * h * -0.7213475204444817)
    t = 1.0 / (1.0 + 0.23164189 * size)
    series = t * (0.127414796 + t * (-0.142248368 + t * (0.7107068705 + t * (-0.7265760135 + t * 0.5307027145))))
    tail = series * bell
    below = jnp.where(h < 0.0, tail, 1.0 - tail)
    return h * below, below + h * (bell * 0.3989422804014327)


def norm_parts(values):
    center = values - jnp.mean(values, axis=-1, keepdims=True)
    spread = lax.rsqrt(jnp.mean(center * center, axis=-1, keepdims=True) + EPSILON)
    return center * spread, spread


def norm_back(upstream, n, r, gain):
    t = upstream * gain
    grad = r * (t - jnp.mean(t, axis=-1, keepdims=True) - n * jnp.mean(t * n, axis=-1, keepdims=True))
    return grad, jnp.sum(upstream * n, axis=0, keepdims=True)


MESH_ID = pl.DeviceIdType.MESH


def here():
    return lax.axis_index("chip"), lax.axis_index("core"), lax.axis_index("zp"), lax.axis_index("zq")


def remote(source, target, sems, at, device):
    sent, got = sems
    return pltpu.make_async_remote_copy(
        src_ref=source, dst_ref=target, send_sem=sent.at[at], recv_sem=got.at[at],
        device_id=device, device_id_type=MESH_ID,
    )


def greet(devices, maybe=None, moves=None):
    barrier = pltpu.get_barrier_semaphore()
    for device in devices:
        pl.semaphore_signal(barrier, inc=1, device_id=device, device_id_type=MESH_ID)
    if maybe is None:
        pl.semaphore_wait(barrier, len(devices))
        return

    @pl.when(moves)
    def _():
        pl.semaphore_signal(barrier, inc=1, device_id=maybe, device_id_type=MESH_ID)

    pl.semaphore_wait(barrier, len(devices) + jnp.where(moves, 1, 0))


def rows_at(start, count):
    return pl.ds(pl.multiple_of(start, 16), count)


class Moves:
    def __init__(self, moved, stays, crossed, moves):
        self.moved, self.stays, self.crossed, self.moves = moved, stays, crossed, moves

    def each(self, act):
        if self.crossed is not None:
            act(self.crossed)

        @pl.when(self.moves)
        def _():
            for copy in self.moved:
                act(copy)

        @pl.when(jnp.logical_not(self.moves))
        def _():
            for copy in self.stays:
                act(copy)

    def start(self):
        self.each(lambda copy: copy.start())

    def wait(self):
        self.each(lambda copy: copy.wait())


class Line:
    def __init__(self, parts, whole, right, left, sems, at):
        chip, core, zp, zq = here()
        self.z = 2 * zp + zq
        up, down = jnp.minimum(self.z + 1, 3), jnp.maximum(self.z - 1, 0)
        self.next = (chip, core, up // 2, up % 2)
        self.last = (chip, core, down // 2, down % 2)
        self.parts, self.whole, self.right, self.left = parts, whole, right, left
        self.sems, self.at, self.sends = sems, at, []

    def at_chip(self, z, *acts):
        @pl.when(self.z == z)
        def _():
            for act in acts:
                act()

    def part_copy(self, c, rightward):
        if rightward:
            return remote(self.parts.at[c], self.right.at[3 - c], self.sems, self.at + 3 - c, self.next)
        return remote(self.parts.at[c], self.left.at[c], self.sems, self.at + 3 + c, self.last)

    def whole_copy(self, c, rightward):
        if rightward:
            return remote(self.whole.at[c], self.whole.at[c], self.sems, self.at + 6 + c, self.next)
        return remote(self.whole.at[c], self.whole.at[c], self.sems, self.at + 8 + c, self.last)

    def send(self, z, make, c, rightward):
        self.sends.append((z, make, c, rightward))
        return lambda: make(c, rightward).start()

    def take(self, c, rightward):
        def act():
            self.part_copy(c, rightward).wait_recv()
            came = self.right[3 - c] if rightward else self.left[c]
            self.parts[c] = add(self.parts[c], came).astype(BF16)

        return act

    def got(self, c, rightward):
        return lambda: self.whole_copy(c, rightward).wait_recv()

    def start(self):
        part = self.part_copy
        self.at_chip(0, *[self.send(0, part, c, True) for c in (3, 2, 1)])
        self.at_chip(3, *[self.send(3, part, c, False) for c in (0, 1, 2)])

    def first(self):
        self.at_chip(1, self.take(3, True), self.send(1, self.part_copy, 3, True))
        self.at_chip(2, self.take(0, False), self.send(2, self.part_copy, 0, False))

    def second(self):
        part = self.part_copy
        self.at_chip(
            1, self.take(2, True), self.send(1, part, 2, True), self.take(0, False), self.send(1, part, 0, False)
        )
        self.at_chip(
            2, self.take(1, False), self.send(2, part, 1, False), self.take(3, True), self.send(2, part, 3, True)
        )

    def third(self):
        self.at_chip(0, self.take(0, False))
        self.at_chip(1, self.take(1, True), self.take(1, False))
        self.at_chip(2, self.take(2, True), self.take(2, False))
        self.at_chip(3, self.take(3, True))
        self.whole[self.z] = self.parts[self.z]
        for z in range(4):
            acts = [self.send(z, self.whole_copy, z, True)] if z < 3 else []
            acts += [self.send(z, self.whole_copy, z, False)] if z > 0 else []
            self.at_chip(z, *acts)

    def fourth(self):
        whole = self.whole_copy
        for z in (1, 2):
            self.at_chip(
                z, self.got(z - 1, True), self.send(z, whole, z - 1, True), self.got(z + 1, False),
                self.send(z, whole, z + 1, False),
            )

    def fifth(self):
        whole = self.whole_copy
        self.at_chip(1, self.got(3, False), self.send(1, whole, 3, False))
        self.at_chip(2, self.got(0, True), self.send(2, whole, 0, True))

    def sixth(self):
        self.at_chip(0, *[self.got(c, False) for c in (1, 2, 3)])
        self.at_chip(3, *[self.got(c, True) for c in (2, 1, 0)])

    def wait_sends(self):
        for z in range(4):
            mine = [make(c, rightward) for at, make, c, rightward in self.sends if at == z]
            self.at_chip(z, *[copy.wait_send for copy in mine])


def write_bounds(pics, lens_ref, bounds_ref, zp, zq, length):
    lane = lax.broadcasted_iota(jnp.int32, (8, 128), 1)
    lens = jnp.where(zp == 0, lens_ref[0], lens_ref[1])
    ends = lens
    for hop in (1, 2, 4, 8):
        ends = ends + jnp.where(lane >= hop, pltpu.roll(ends, hop, 1), 0)
    starts = ends - lens
    last = (lens > 0) & (pltpu.roll(lens, 127, 1) == 0)
    query_ends = jnp.where(last, length, ends)
    total = jnp.max(jnp.where(lane < pics, ends, 0), axis=1, keepdims=True)

    def both(values):
        values = jnp.where(lane < HEAD, jnp.where(lane < pics, values, 2 * length), 0)
        return values + pltpu.roll(values, HEAD, 1)

    tables = [both(starts), both(ends), both(query_ends), jnp.broadcast_to(total, (8, 128))]
    for t in range(4):
        table = tables[t]
        bounds_ref[0, t : t + 1, :] = jnp.where(zq == 0, table[0:1], table[1:2])
        bounds_ref[1, t : t + 1, :] = table[2:3]
    bounds_ref[:, 4:, :] = jnp.zeros((2, 4, 128), jnp.int32)


def forward_kernel(square, pics, *refs):
    refs = list(refs)
    take = lambda count: [refs.pop(0) for _ in range(count)]
    tokens_ref, cot_ref, lengths_ref, weight_in = take(4)
    if square:
        gain_in = take(4)
        up_in, outw_ref = take(2)
    else:
        gain_first_in, gain_qk_in = take(2)
    x_out, bounds_ref, mix_hbm, cot_hbm, gain_first, second_ref, gain_qk = take(7)
    names = ("normed", "qk", "v", "raw", "out", "aug")
    outs = [dict(zip(names, take(6))) for _ in range(2)]
    if square:
        up_hbm, outw_hbm = take(2)
    row_ref, shared_ref, cot_out, lens_ref, lens_out = take(5)
    scratch = [dict(zip(names, take(6))) for _ in range(2)]
    kaug, vaug, qaug = take(3)
    if square:
        mix_ref, gains_ref, up_ref, mix_out, gains_out, up_out, outw_out = take(7)
    sent, got, local_sem, write_sem = take(4)

    chip, core, zp, zq = here()
    z = 2 * zp + zq
    part = tokens_ref.shape[1]
    half, length = 2 * part, 4 * part
    sems = (sent, got)
    partner = (chip, 1 - core, zp, zq)
    side = (chip, core, zp, 1 - zq)
    keep = (chip, zp, core, zq)
    cross = (chip, zp, core, 1 - zq)
    moves = core != zp
    near_x = (chip ^ 1, core, zp, zq)
    near_y = (chip ^ 2, core, zp, zq)
    greet([partner, side, cross] + ([near_x, near_y] if square else []), keep, moves)

    def quarter(ref, index):
        return ref.at[rows_at(index * part, part)]

    own_row = remote(tokens_ref.at[zq], quarter(row_ref, z), sems, 0, keep)
    own_shared = remote(tokens_ref.at[2], quarter(shared_ref, z), sems, 2, keep)
    stay_row = pltpu.make_async_copy(tokens_ref.at[zq], quarter(row_ref, z), local_sem.at[0])
    stay_shared = pltpu.make_async_copy(tokens_ref.at[2], quarter(shared_ref, z), local_sem.at[1])

    @pl.when(moves)
    def _():
        own_row.start()

    @pl.when(jnp.logical_not(moves))
    def _():
        stay_row.start()

    cross_row = remote(tokens_ref.at[1 - zq], quarter(row_ref, z), sems, 1, cross)
    cross_row.start()

    @pl.when(moves)
    def _():
        own_shared.start()

    @pl.when(jnp.logical_not(moves))
    def _():
        stay_shared.start()

    lens_ref[...] = jnp.zeros_like(lens_ref)
    lens_ref[: lengths_ref.shape[0], :pics] = lengths_ref[...]
    lens_copy = remote(lens_ref, lens_out.at[core], sems, 8, partner)
    lens_copy.start()
    lens_stay = pltpu.make_async_copy(lens_ref, lens_out.at[core], local_sem.at[2])
    lens_stay.start()
    waits = []
    if square:
        shard = mix_ref.shape[1]
        tile = up_ref.shape[2] // 4
        width = mix_ref.shape[2] // 3
        for h in range(2):
            for i in range(3):
                mix_ref[h, :, i * width : (i + 1) * width] = weight_in[:, (2 * i + h) * width : (2 * i + h + 1) * width]
        gains_ref[...] = jnp.zeros_like(gains_ref)
        for i in range(4):
            gains_ref[i : i + 1, :shard] = gain_in[i][...].astype(F32)
        mine, theirs = 2 * chip + core, 2 * chip + 1 - core
        slot = [9]

        def send(source, target, device):
            copy = remote(source, target, sems, slot[0], device)
            slot[0] += 1
            copy.start()
            waits.append(copy)
            return copy

        def stay(source, target, at):
            copy = pltpu.make_async_copy(source, target, local_sem.at[at])
            copy.start()
            return copy

        def block(ref, start, count):
            return ref.at[rows_at(start, count)]

        mix_piece = lambda index: (block(mix_out, index * shard, shard), gains_out.at[index])

        def send_mix(sources, index, device):
            return [send(source, target, device) for source, target in zip(sources, mix_piece(index))]

        def arrived(copies):
            for copy in copies:
                copy.wait_recv()

        x_mine, y_other = 2 * (chip ^ 1) + core, 2 * (chip ^ 2) + 1 - core
        to_core = send_mix((mix_ref.at[1 - core], gains_ref), mine, partner)
        a_x = send_mix((mix_ref.at[core], gains_ref), mine, near_x)
        a_y = send_mix((mix_ref.at[core], gains_ref), mine, near_y)
        for h in range(2):
            for i in range(4):
                up_ref[h, :, i * tile : (i + 1) * tile] = up_in[:, (2 * i + h) * tile : (2 * i + h + 1) * tile]
        up_core = send(up_ref.at[1 - core], block(up_out, mine * shard, shard), partner)
        out_core = send(outw_ref, block(outw_out, mine * shard, shard), partner)
        stays = [
            stay(mix_ref.at[core], mix_piece(mine)[0], 3),
            stay(gains_ref, gains_out.at[mine], 4),
            stay(up_ref.at[core], block(up_out, mine * shard, shard), 5),
            stay(outw_ref, block(outw_out, mine * shard, shard), 6),
        ]
        arrived(to_core)
        b_x = send_mix(mix_piece(theirs), theirs, near_x)
        b_y = send_mix(mix_piece(theirs), theirs, near_y)
        arrived(a_x)
        a_far = send_mix(mix_piece(x_mine), x_mine, near_y)
        arrived(b_y)
        b_far = send_mix(mix_piece(y_other), y_other, near_x)
        for copy in stays:
            copy.wait()
        arrived([up_core])
        ohalf = shard // 2

        def bundle(first, from_chip):
            same, twin = 2 * from_chip + core, 2 * from_chip + 1 - core
            part_of = 0 if first else 1
            return [
                block(up_out, (same if first else twin) * shard, shard),
                block(outw_out, same * shard + part_of * ohalf, ohalf),
            ]

        def send_bundle(first, from_chip, device):
            return [send(ref, ref, device) for ref in bundle(first, from_chip)]

        first_x = send_bundle(True, chip, near_x)
        first_y = send_bundle(True, chip, near_y)
        second_x = send_bundle(False, chip, near_x)
        second_y = send_bundle(False, chip, near_y)

    lens_copy.wait()
    lens_stay.wait()
    write_bounds(pics, lens_out, bounds_ref, zp, zq, length)
    if square:
        arrived(a_y + b_x + a_far + b_far)
        for p in range(gains_out.shape[0]):
            lanes = slice(p * shard, (p + 1) * shard)
            values = gains_out[p, :, :shard]
            gain_first[:, lanes] = values[0:1]
            second_ref[:, lanes] = values[3:4]
            half_pieces = gains_out.shape[0] // 2

            @pl.when(core == p // half_pieces)
            def _():
                at = (p % half_pieces) * shard
                gain_qk[:, at : at + shard] = values[1:2]
                gain_qk[:, width + at : width + at + shard] = values[2:3]
        weight = mix_out
    else:
        weight = weight_in
        width = weight.shape[1] // 3
        second_ref[...] = jnp.zeros_like(second_ref)
        gain_first[...] = gain_first_in[...]
        gain_qk[...] = gain_qk_in[...]
    writes = []

    def write(source, target, at):
        copy = pltpu.make_async_copy(source, target, write_sem.at[at])
        copy.start()
        writes.append(copy)

    write(weight, mix_hbm, 0)
    first, second = 2 * core + zq, 2 * core + 1 - zq
    other_first, other_second = 2 * (1 - core) + zq, 2 * (1 - core) + 1 - zq

    def forwarded(ref, index, at):
        return remote(quarter(ref, index), quarter(ref, index), sems, at, partner)

    def project(tokens, bufs, at):
        rows = rows_at(at * part, part)
        project_kernel(
            tokens.at[rows], gain_first, weight, gain_qk, bufs["normed"].at[rows], bufs["qk"].at[rows],
            bufs["v"].at[rows], bufs["raw"].at[rows],
        )

    def project_row(i, _):
        @pl.when(i == 0)
        def _():
            @pl.when(moves)
            def _():
                own_row.wait_recv()

            @pl.when(jnp.logical_not(moves))
            def _():
                stay_row.wait()

            forwarded(row_ref, first, 3).start()

        @pl.when(i == 1)
        def _():
            cross_row.wait_recv()
            forwarded(row_ref, second, 4).start()

        @pl.when(i == 2)
        def _():
            forwarded(row_ref, other_first, 3).wait_recv()

        @pl.when(i == 3)
        def _():
            forwarded(row_ref, other_second, 4).wait_recv()

        order = jnp.where(i == 0, first, jnp.where(i == 1, second, jnp.where(i == 2, other_first, other_second)))
        project(row_ref, scratch[0], order)
        return 0

    row_one, row_two = forwarded(row_ref, first, 3), forwarded(row_ref, second, 4)

    def attend(bufs, bounds):
        def one(p, _):
            lanes = pl.ds(pl.multiple_of(p * 128, 128), 128)
            attend_kernel(
                pics, bufs["qk"].at[:, lanes],
                bufs["qk"].at[:, pl.ds(pl.multiple_of(width + p * 128, 128), 128)], bufs["v"].at[:, lanes], bounds,
                bufs["out"].at[:, lanes], bufs["aug"].at[pl.ds(2 * p, 2)], kaug, vaug, qaug.at[pl.ds(0, bufs["out"].shape[0])],
            )
            return 0

        lax.fori_loop(0, width // 128, one, 0)

    lax.fori_loop(0, 4, project_row, 0)
    for i, name in enumerate(("normed", "qk", "v", "raw")):
        write(scratch[0][name], outs[0][name], 1 + i)
    write(row_ref.at[rows_at(core * half, half)], x_out.at[pl.ds(0, half)], 5)

    @pl.when(moves)
    def _():
        own_shared.wait_recv()

    @pl.when(jnp.logical_not(moves))
    def _():
        stay_shared.wait()

    to_side = remote(quarter(shared_ref, first), quarter(shared_ref, first), sems, 5, side)
    to_side.start()
    shared_one = remote(quarter(shared_ref, first), quarter(shared_ref, first), sems, 6, partner)
    shared_one.start()
    attend(scratch[0], bounds_ref.at[0])
    cot_moves = Moves(
        [remote(cot_ref.at[zq], cot_out, sems, 43, keep)],
        [pltpu.make_async_copy(cot_ref.at[zq], cot_out, local_sem.at[0])],
        None,
        moves,
    )
    cot_moves.start()
    write(scratch[0]["out"], outs[0]["out"], 6)
    write(scratch[0]["aug"], outs[0]["aug"], 7)
    to_side.wait_recv()
    shared_two = forwarded(shared_ref, second, 7)
    shared_two.start()
    if square:
        arrived(first_x + second_y)
        far_first = send_bundle(True, chip ^ 1, near_y)
        far_second = send_bundle(False, chip ^ 2, near_x)
    shared_one.wait_recv()
    shared_two.wait_recv()

    def project_shared(i, _):
        project(shared_ref, scratch[1], i)
        return 0

    lax.fori_loop(0, 4, project_shared, 0)
    for i, name in enumerate(("normed", "qk", "v", "raw")):
        write(scratch[1][name], outs[1][name], 8 + i)
    write(shared_ref.at[rows_at(first * part, part)], x_out.at[pl.ds(half, part)], 12)
    attend(scratch[1], bounds_ref.at[1])
    write(scratch[1]["out"], outs[1]["out"], 13)
    write(scratch[1]["aug"], outs[1]["aug"], 14)

    if square:
        arrived(first_y + second_x + far_first + far_second)
        sent_pieces = []
        for c in (chip ^ 1, chip ^ 2, chip ^ 3):
            target = block(outw_out, (2 * c + core) * shard, shard)
            sent_pieces.append(send(target, target, partner))
        write(up_out, up_hbm, 15)
        arrived(sent_pieces + [out_core])
        write(outw_out, outw_hbm, 17)
        for copy in waits:
            copy.wait_send()
    cot_moves.wait()
    write(cot_out, cot_hbm, 18)
    for copy in (row_one, row_two, shared_one, shared_two, to_side, cross_row):
        copy.wait_send()

    @pl.when(moves)
    def _():
        own_row.wait_send()
        own_shared.wait_send()

    for copy in writes:
        copy.wait()


def forward_pass(square, pics, tokens, cotangent, lengths, weight, *more):
    _, part, model = tokens.shape
    length, half, width = 4 * part, 2 * part, model // 2
    near = pl.BlockSpec(memory_space=pltpu.VMEM)
    anywhere = pl.BlockSpec(memory_space=pl.ANY)
    low = lambda *shape: (shape, BF16)
    wide = lambda *shape: (shape, F32)
    outs = [
        (low(3 * part, model), anywhere),
        (((2, 8, 128), jnp.int32), near),
        (low(model, 3 * width), anywhere),
        (low(part, model), anywhere),
        (wide(1, model), near),
        (wide(1, model), near),
        (wide(1, model), near),
    ]
    bufs = []
    for queries in (length, half):
        shapes = [
            low(length, model), low(length, 2 * width), low(length, width), low(length, 2 * width),
            low(queries, width), low(2 * (width // 128), queries, 128),
        ]
        outs += [(shape, anywhere) for shape in shapes]
        bufs += shapes
    table = ((8, 128), jnp.int32)
    scratch = [low(length, model), low(length, model), low(part, model), table, ((2, 8, 128), jnp.int32)] + bufs
    scratch += [low(2, length, 128), low(2, length, 128), low(length, 128)]
    if square:
        up, _ = more[4:]
        shard, hidden = up.shape
        landed = [low(model, hidden // 2), low(model, model)]
        outs += [(shape, anywhere) for shape in landed]
        scratch += [low(2, shard, 3 * width), wide(8, 128), low(2, shard, hidden // 2)]
        scratch += [low(model, 3 * width), wide(8, 8, 128)] + landed
    return pl.pallas_call(
        functools.partial(forward_kernel, square, pics),
        in_specs=[near] * (4 + len(more)),
        out_specs=[spec for _, spec in outs],
        out_shape=[jax.ShapeDtypeStruct(*shape) for shape, _ in outs],
        scratch_shapes=[pltpu.VMEM(*shape) for shape in scratch]
        + [
            pltpu.SemaphoreType.DMA((49,)),
            pltpu.SemaphoreType.DMA((49,)),
            pltpu.SemaphoreType.DMA((8,)),
            pltpu.SemaphoreType.DMA((19,)),
        ],
        compiler_params=pltpu.CompilerParams(
            collective_id=0, has_side_effects=True, vmem_limit_bytes=60 * 1024 * 1024
        ),
        name="forward_pass",
    )(tokens, cotangent, lengths, weight, *more)


def dense_kernel(
    square, out_ref, shared_ref, x, grad_ref, cot_ref, outw_ref, gain_ref, bounds_ref, up_ref, down_ref,
    output_ref, midg_ref, row_grad, shared_grad, outg_ref, gaing_ref, packed_ref, far_ref,
    att_other, second, turned, grad, cot_in, hidden_all, pre_all, forward, backward, middle, up, down,
    results, parts_out, parts_in, heads_out, cols_out, cols_in, stage, far_in,
    sent, got, load_sem, write_sem, local_sem,
):
    chip, core, zp, zq = here()
    sems = (sent, got)
    partner = (chip, 1 - core, zp, zq)
    keep = (chip, zp, core, zq)
    cross = (chip, zp, core, 1 - zq)
    moves = core != zp
    near_x = (chip ^ 1, core, zp, zq)
    near_y = (chip ^ 2, core, zp, zq)
    tokens, model = midg_ref.shape
    part = tokens // 3
    half = 2 * part
    width = out_ref.shape[1]
    units = up.shape[1]
    tile = units // 4
    other = 1 - core
    mine, theirs = pl.ds(0, tokens), pl.ds(tokens, tokens)
    own_down = down.at[rows_at(chip * tile, tile)] if square else down
    loads = [
        pltpu.make_async_copy(up_ref, up, load_sem.at[0]),
        pltpu.make_async_copy(down_ref, own_down, load_sem.at[1]),
    ]
    for copy in loads:
        copy.start()
    greet([partner, cross] + ([near_x, near_y] if square else []), keep, moves)
    att_sends = [
        remote(out_ref.at[rows_at(other * half, half)], att_other.at[pl.ds(0, half)], sems, 0, partner),
        remote(shared_ref.at[rows_at(other * part, part)], att_other.at[pl.ds(half, part)], sems, 1, partner),
    ]
    for copy in att_sends:
        copy.start()
    cot_move = Moves(
        [remote(cot_ref.at[2], cot_in.at[1], sems, 11, keep)],
        [pltpu.make_async_copy(cot_ref.at[2], cot_in.at[1], local_sem.at[0])],
        remote(cot_ref.at[1 - zq], cot_in.at[0], sems, 22, cross),
        moves,
    )
    cot_move.start()

    def down_half(index, which):
        return down.at[rows_at(index * tile + which * (tile // 2), tile // 2)]

    def send_down(index, which, at, device):
        copy = remote(down_half(index, which), down_half(index, which), sems, at, device)
        copy.start()
        return copy

    slot = lax.broadcasted_iota(jnp.int32, (part, 1), 0)
    filled, shared_filled = bounds_ref[0, 3:4, 0:1], bounds_ref[1, 3:4, 0:1]
    none = jnp.zeros((), BF16)

    def take_grad(values, at, start, limit, sem):
        rows = rows_at(at, part)
        grad[rows, :] = jnp.where(slot + start < limit, values, none)
        copy = remote(grad.at[rows], grad.at[rows_at(tokens + at, part)], sems, sem, partner)
        copy.start()
        return copy

    grad_sends = [take_grad(grad_ref[...], zq * part, (2 * core + zq) * part, filled, 2)]

    own_rows_of = lambda b: (
        out_ref[rows_at(core * half + b * part, part), :] if b < 2 else shared_ref[rows_at(core * part, part), :]
    )
    own_weight = outw_ref[rows_at(core * width, width), :]
    other_weight = outw_ref[rows_at(other * width, width), :]
    blocks = [pl.ds(b * part, part) for b in range(3)]
    for b in range(3):
        middle[blocks[b], :] = x[blocks[b], :].astype(F32) + jnp.dot(
            own_rows_of(b), own_weight, preferred_element_type=F32
        )
    for copy in loads:
        copy.wait()
    if square:
        down_sends = [
            send_down(chip, 0, 12, near_x), send_down(chip, 1, 13, near_y), send_down(chip, 0, 14, near_y),
            send_down(chip, 1, 15, near_x),
        ]
    for copy in att_sends:
        copy.wait_recv()
    for rows in blocks:
        value = middle[rows, :] + jnp.dot(att_other[rows, :], other_weight, preferred_element_type=F32)
        middle[rows, :] = value
        second[rows, :] = (norm_parts(value)[0] * gain_ref[...]).astype(BF16)
    second_send = remote(second.at[mine], second.at[theirs], sems, 3, partner)
    second_send.start()

    def hidden_forward(start):
        rows = pl.ds(start, tokens)

        def one_tile(i, _):
            here_units = pl.ds(pl.multiple_of(i * tile, 128), tile)
            hidden, slope = gelu_pair(jnp.dot(second[rows, :], up[:, here_units], preferred_element_type=F32))
            hidden_all[rows, here_units] = hidden.astype(BF16)
            pre_all[rows, here_units] = slope.astype(BF16)
            return 0

        lax.fori_loop(0, 4, one_tile, 0)

    def hidden_backward(start):
        rows = pl.ds(start, tokens)

        def one_tile(i, _):
            here_units = pl.ds(pl.multiple_of(i * tile, 128), tile)
            pre_grad = nt(grad[rows, :], down[rows_at(i * tile, tile), :]) * pre_all[rows, here_units].astype(F32)
            pre_all[rows, here_units] = pre_grad.astype(BF16)
            return 0

        lax.fori_loop(0, 4, one_tile, 0)

    hidden_forward(0)
    if square:
        down_sends[0].wait_recv()
        down_sends[1].wait_recv()
        down_sends += [send_down(chip ^ 1, 0, 16, near_y), send_down(chip ^ 2, 1, 17, near_x)]
    second_send.wait_recv()
    hidden_forward(tokens)
    if square:
        for copy in down_sends[2:]:
            copy.wait_recv()
    for b in range(3):
        rows, there = pl.ds(tokens + b * part, part), blocks[b]
        parts_out[0, there, :] = jnp.dot(hidden_all[rows, :], down[...], preferred_element_type=F32).astype(BF16)
    first_part = remote(parts_out.at[0], parts_in.at[0], sems, 4, partner)
    first_part.start()
    for rows in blocks:
        forward[rows, :] = middle[rows, :] + jnp.dot(hidden_all[rows, :], down[...], preferred_element_type=F32)
    turned[...] = second[...].T
    first_part.wait_recv()
    for rows in blocks:
        results[rows, :] = (forward[rows, :] + parts_in[0, rows, :].astype(F32)).astype(BF16)
    kept_rows, third_rows = results.at[rows_at(zq * part, part)], results.at[pl.ds(half, part)]
    output_moves = Moves(
        [
            remote(kept_rows, output_ref.at[zq], sems, 19, keep),
            remote(third_rows, output_ref.at[2], sems, 20, keep),
        ],
        [
            pltpu.make_async_copy(kept_rows, output_ref.at[zq], local_sem.at[1]),
            pltpu.make_async_copy(third_rows, output_ref.at[2], local_sem.at[2]),
        ],
        remote(results.at[rows_at((1 - zq) * part, part)], output_ref.at[zq], sems, 21, cross),
        moves,
    )
    output_moves.start()
    cot_move.wait()
    grad_sends.append(take_grad(cot_in[0], (1 - zq) * part, (2 * core + 1 - zq) * part, filled, 18))
    grad_sends.append(take_grad(cot_in[1], half, (2 * core + zq) * part, shared_filled, 23))
    hidden_backward(0)
    for copy in grad_sends:
        copy.wait_recv()
    hidden_backward(tokens)
    quarter = model // 4
    far_sends = [
        remote(stage.at[0, pl.ds(0, tile)], far_in.at[0], sems, 9, near_y),
        remote(stage.at[0, pl.ds(tile, tile)], far_in.at[1], sems, 10, near_x),
    ]

    def weight_grads(i, _):
        target = chip ^ (3 - i) if square else 3 - i
        place = jnp.where(i == 0, 0, 1 + i % 2)

        @pl.when(i == 3)
        def _():
            pltpu.make_async_copy(stage.at[place], packed_ref.at[target], write_sem.at[place]).wait()

        here_units = pl.ds(pl.multiple_of(target * tile, 128), tile)
        stage[place, pl.ds(0, tile), :] = tn(hidden_all[:, here_units], grad[...]).astype(BF16)
        values = jnp.dot(
            turned[rows_at(target * quarter, quarter), :], pre_all[...], preferred_element_type=F32
        ).astype(BF16)
        for j in range(2):
            stage[place, pl.ds(tile + j * quarter, quarter), :] = values[:, j * model : (j + 1) * model]
        pltpu.make_async_copy(stage.at[place], packed_ref.at[target], write_sem.at[place]).start()
        if square:

            @pl.when(i == 0)
            def _():
                for copy in far_sends:
                    copy.start()

        return 0

    lax.fori_loop(0, 4, weight_grads, 0)

    for b in range(3):
        rows, there = pl.ds(tokens + b * part, part), blocks[b]
        parts_out[1, there, :] = nt(pre_all[rows, :], up[...]).astype(BF16)
    second_part = remote(parts_out.at[1], parts_in.at[1], sems, 5, partner)
    second_part.start()
    for rows in blocks:
        backward[rows, :] = nt(pre_all[rows, :], up[...])
    second_send.wait_send()
    second_part.wait_recv()
    gain_sum = jnp.zeros(gaing_ref.shape, F32)
    for rows in blocks:
        n, r = norm_parts(middle[rows, :])
        upstream = backward[rows, :] + parts_in[1, rows, :].astype(F32)
        more, gain_more = norm_back(upstream, n, r, gain_ref[...])
        gain_sum = gain_sum + gain_more
        value = grad[rows, :].astype(F32) + more
        midg_ref[rows, :] = value
        branch = value.astype(BF16)
        second[rows, :] = branch
        heads_out[rows, :] = nt(branch, other_weight).astype(BF16)
    gaing_ref[...] = gain_sum
    head_sends = [
        remote(heads_out.at[pl.ds(0, half)], row_grad.at[rows_at(core * half, half)], sems, 6, partner),
        remote(heads_out.at[pl.ds(half, part)], shared_grad.at[rows_at(core * part, part)], sems, 7, partner),
    ]
    for copy in head_sends:
        copy.start()
    branch = second[mine, :]
    forward[rows_at(core * width, width), :] = tn(
        out_ref[rows_at(core * half, half), :], second[pl.ds(0, half), :]
    ) + tn(shared_ref[rows_at(core * part, part), :], second[pl.ds(half, part), :])
    forward[rows_at(other * width, width), :] = tn(att_other[...], branch)
    lanes = lambda side: pl.ds(pl.multiple_of(side * width, 128), width)
    cols_out[...] = forward[pl.ds(0, model), lanes(other)].astype(BF16)
    cols_send = remote(cols_out, cols_in, sems, 8, partner)
    cols_send.start()
    for b in range(3):
        value = nt(second[blocks[b], :], own_weight).astype(BF16)
        if b < 2:
            row_grad[rows_at(core * half + b * part, part), :] = value
        else:
            shared_grad[rows_at(core * part, part), :] = value
    cols_send.wait_recv()
    outg_ref[...] = (forward[pl.ds(0, model), lanes(core)] + cols_in[...].astype(F32)).astype(BF16)
    for copy in head_sends:
        copy.wait_recv()
    for copy in att_sends + head_sends + grad_sends + [first_part, second_part, cols_send]:
        copy.wait_send()
    if square:
        for copy in down_sends:
            copy.wait_send()
        for copy in far_sends:
            copy.wait()
    far_write = pltpu.make_async_copy(far_in, far_ref, load_sem.at[0])
    far_write.start()
    for place in range(3):
        pltpu.make_async_copy(stage.at[place], packed_ref.at[0], write_sem.at[place]).wait()
    output_moves.wait()
    far_write.wait()


def dense(square, out, shared_out, x, grad, cotangent, out_matrix, gain, bounds, up, down):
    model = x.shape[1]
    tokens = x.shape[0]
    part = tokens // 3
    length, width = out.shape
    units = up.shape[1]
    tile = units // 4
    anywhere = pl.BlockSpec(memory_space=pl.ANY)
    near = pl.BlockSpec(memory_space=pltpu.VMEM)
    both = 2 * tokens
    low = lambda *shape: pltpu.VMEM(shape, BF16)
    wide = lambda *shape: pltpu.VMEM(shape, F32)
    return pl.pallas_call(
        functools.partial(dense_kernel, square),
        in_specs=[near] * 4 + [anywhere] + [near] * 3 + [anywhere] * 2,
        out_specs=[anywhere] + [near] * 5 + [anywhere, anywhere],
        out_shape=[
            jax.ShapeDtypeStruct((3, part, model), BF16),
            jax.ShapeDtypeStruct((tokens, model), F32),
            jax.ShapeDtypeStruct((length, width), BF16),
            jax.ShapeDtypeStruct((length // 2, width), BF16),
            jax.ShapeDtypeStruct((model, width), BF16),
            jax.ShapeDtypeStruct((1, model), F32),
            jax.ShapeDtypeStruct((4, 2 * tile, model), BF16),
            jax.ShapeDtypeStruct((2, tile, model), BF16),
        ],
        scratch_shapes=[
            low(tokens, width), low(both, model), low(model, both), low(both, model), low(2, part, model),
            low(both, units), low(both, units), wide(tokens, model), wide(tokens, model), wide(tokens, model),
            low(model, units), low(units, model), low(tokens, model), low(2, tokens, model), low(2, tokens, model),
            low(tokens, width), low(model, width), low(model, width), low(3, 2 * tile, model), low(2, tile, model),
            pltpu.SemaphoreType.DMA((24,)),
            pltpu.SemaphoreType.DMA((24,)),
            pltpu.SemaphoreType.DMA((2,)),
            pltpu.SemaphoreType.DMA((3,)),
            pltpu.SemaphoreType.DMA((3,)),
        ],
        compiler_params=pltpu.CompilerParams(
            collective_id=1, has_side_effects=True, vmem_limit_bytes=63 * 1024 * 1024
        ),
        name="dense",
    )(out, shared_out, x, grad, cotangent, out_matrix, gain, bounds, up, down)


def add(*terms):
    total = terms[0].astype(F32)
    for term in terms[1:]:
        total = total + term.astype(F32)
    return total


def backward_kernel(square, pics, *refs):
    refs = list(refs)
    take = lambda count: [refs.pop(0) for _ in range(count)]
    names = ("aug", "qk", "v", "out", "do", "raw", "normed")
    row_in = dict(zip(names, take(7)))
    shared_in = dict(zip(names, take(7)))
    mix_in, x_in, midg_in, gain_first, gain_qk, gain_second_grad, bounds_ref = take(7)
    if square:
        packed_in, far_ref, outg_in = take(3)
        grad_out, total_ref, gains_ref, up_ref, down_ref, outw_ref = take(6)
    else:
        grad_own, mix_grad_ref, gains_sum = take(3)
    names = names[:-1]
    row = dict(zip(names, take(6)))
    shared = dict(zip(names, take(6)))
    normed, weight, x, midg = take(4)
    kaug, vaug, doaug, qsum, ksum, mixed, part_k, part_v, got_k, got_v = take(10)
    gain_sums, parts_out, parts_in = take(3)
    if square:
        grad_own, payload, gains_sum, outg = take(4)
        held, far_in, onward_out, onward_in, direct_in, line, whole_line, line_right, line_left = take(9)
        up_out, up_got = take(2)
        relay, final, core_got, chunks, chunk_whole, chunk_right, chunk_left, gain_parts, gain_got = take(9)
    sent, got, load_sem, local_sem = take(4)

    chip, core, zp, zq = here()
    z = 2 * zp + zq
    sems = (sent, got)
    partner = (chip, 1 - core, zp, zq)
    keep = (chip, zp, core, zq)
    cross = (chip, zp, core, 1 - zq)
    moves = core != zp
    near_x = (chip ^ 1, core, zp, zq)
    near_y = (chip ^ 2, core, zp, zq)
    along = [(chip, core, zp, 1 - zq), (chip, core, 1 - zp, zq), (chip, core, 1 - zp, 1 - zq)]
    tokens, model = x.shape
    part = tokens // 3
    half, length = 2 * part, 4 * part
    width = model // 2
    queries = half
    waits = []

    def load(source, target, at):
        copy = pltpu.make_async_copy(source, target, load_sem.at[at])
        copy.start()
        return copy

    def send(source, target, at, device):
        copy = remote(source, target, sems, at, device)
        copy.start()
        waits.append(copy)
        return copy

    if square:
        rows_count = packed_in.shape[1]
        span = rows_count // 2
        first_half, second_half = pl.ds(0, span), pl.ds(span, span)
        held_loads = [
            load(packed_in.at[chip ^ 1, first_half], held.at[0], 24),
            load(packed_in.at[chip ^ 2, second_half], held.at[1], 25),
            load(packed_in.at[chip, first_half], held.at[2], 26),
            load(packed_in.at[chip, second_half], held.at[3], 27),
        ]
        far_loads = [load(far_ref.at[i], far_in.at[i], 28 + i) for i in range(2)]
    keys_of = lambda ref: ref.at[:, pl.ds(width, width)]
    load_bufs = lambda source, target, at: [
        load(keys_of(source[name]) if name == "qk" else source[name], target[name], at + i)
        for i, name in enumerate(names)
    ]
    shared_loads = load_bufs(shared_in, shared, 0)
    row_loads = load_bufs(row_in, row, 6)
    late_loads = [
        load(row_in["normed"], normed.at[pl.ds(0, length)], 12),
        load(shared_in["normed"].at[rows_at(zq * part, part)], normed.at[pl.ds(length, part)], 13),
        load(
            shared_in["normed"].at[rows_at((2 + zq) * part, part)], normed.at[pl.ds(length + part, part)], 14
        ),
        load(mix_in, weight, 15),
        load(x_in, x, 16),
        load(midg_in, midg, 17),
    ]
    if square:
        late_loads.append(load(outg_in, outg, 18))
    if square:
        greet([partner, cross, near_x, near_y] + along, keep, moves)
        bulk_x = send(packed_in.at[chip ^ 1, second_half], direct_in.at[0], 2, near_x)
        bulk_y = send(packed_in.at[chip ^ 2, first_half], direct_in.at[1], 3, near_y)
        for copy in held_loads + far_loads:
            copy.wait()
        onward_out[0] = add(far_in[0], held[0]).astype(BF16)
        bulk_on_x = send(onward_out.at[0], onward_in.at[0], 11, near_x)
        onward_out[1] = add(far_in[1], held[1]).astype(BF16)
        bulk_on_y = send(onward_out.at[1], onward_in.at[1], 12, near_y)

        bulk_line = Line(line, whole_line, line_right, line_left, sems, 14)
        mix_line = Line(chunks, chunk_whole, chunk_right, chunk_left, sems, 26)
    else:
        greet([partner, along[0]])

    gain_sums[...] = jnp.zeros_like(gain_sums)

    def attend_back(bufs, bounds, count, q_lanes_to, k_to, v_to, at, between=None):
        def one(p, _):
            if between is not None:
                pl.when(p == 2)(between)
            lanes = pl.ds(pl.multiple_of(p * 128, 128), 128)
            key_lanes = pl.ds(pl.multiple_of(width + p * 128, 128), 128)
            attend_back_kernel(
                pics, bufs["aug"].at[pl.ds(2 * p, 2)], bufs["qk"].at[:, lanes], bufs["v"].at[:, lanes],
                bufs["out"].at[:, lanes], bufs["do"].at[:, lanes], bufs["raw"].at[:, lanes],
                bufs["raw"].at[:, key_lanes], gain_qk.at[:, lanes], gain_qk.at[:, key_lanes], bounds,
                q_lanes_to(p), k_to(p), v_to(p), gain_sums.at[pl.ds(at, 1), lanes], gain_sums.at[pl.ds(at + 1, 1), lanes],
                kaug, vaug, doaug.at[:, pl.ds(0, count)], qsum.at[:, pl.ds(0, count)], ksum,
            )
            return 0

        lax.fori_loop(0, width // 128, one, 0)

    def mixed_at(start, count, side):
        return lambda p: mixed.at[pl.ds(start, count), pl.ds(pl.multiple_of(side * width + p * 128, 128), 128)]

    whole_lanes = lambda ref: lambda p: ref.at[:, pl.ds(pl.multiple_of(p * 128, 128), 128)]
    for copy in shared_loads:
        copy.wait()
    attend_back(
        shared, bounds_ref.at[1], queries, mixed_at(length, queries, 0), whole_lanes(part_k), whole_lanes(part_v), 0
    )
    side_sends = []
    for i in range(2):
        theirs = rows_at((2 * i + 1 - zq) * part, part)
        there = pl.ds(i * part, part)
        side_sends.append(send(part_k.at[theirs], got_k.at[there], 7 + 2 * i, along[0]))
        side_sends.append(send(part_v.at[theirs], got_v.at[there], 8 + 2 * i, along[0]))
    for copy in row_loads:
        copy.wait()
    def start_line():
        for copy in (bulk_y, bulk_on_x, bulk_x, bulk_on_y):
            copy.wait_recv()
        first_sum = add(held[2], onward_in[0], direct_in[1]).astype(BF16)
        second_half_sum = add(held[3], onward_in[1], direct_in[0]).astype(BF16)
        for i in range(2):
            line[i] = first_sum[i * quarter_rows : (i + 1) * quarter_rows]
            line[2 + i] = second_half_sum[i * quarter_rows : (i + 1) * quarter_rows]
        bulk_line.start()

    if square:
        quarter_rows = rows_count // 4
    attend_back(
        row, bounds_ref.at[0], length, mixed_at(0, length, 0), mixed_at(0, length, 1), mixed_at(0, length, 2), 2,
        start_line if square else None,
    )

    if square:
        bulk_line.first()
    for copy in side_sends:
        copy.wait_recv()

    def shared_pair(p, _):
        lanes = pl.ds(pl.multiple_of(p * 128, 128), 128)
        key_lanes = pl.ds(pl.multiple_of(width + p * 128, 128), 128)
        shared_keys_kernel(
            part_k.at[:, lanes], part_v.at[:, lanes], got_k.at[:, lanes], got_v.at[:, lanes],
            shared["raw"].at[:, key_lanes], gain_qk.at[:, key_lanes], mixed_at(length, queries, 1)(p),
            mixed_at(length, queries, 2)(p), gain_sums.at[pl.ds(4, 1), lanes],
        )
        return 0

    lax.fori_loop(0, width // 128, shared_pair, 0)
    for copy in late_loads:
        copy.wait()
    other = 1 - core
    block_rows = lambda side, b: (
        rows_at(side * half + b * part, part) if b < 2 else rows_at(length + side * part, part)
    )
    for b in range(3):
        parts_out[pl.ds(b * part, part), :] = nt(mixed[block_rows(other, b), :], weight[...]).astype(BF16)
    part_send = send(parts_out, parts_in, 13, partner)
    if square:
        bulk_line.second()
    shard = model // 8
    if square:
        for i in range(3):
            lanes = slice(i * width, (i + 1) * width)
            value = tn(normed[...], mixed[:, lanes]).astype(BF16)
            for p in range(8):
                payload[p, :shard, lanes] = value[p * shard : (p + 1) * shard]
        bulk_line.third()
    else:
        for i in range(3):
            lanes = slice(i * width, (i + 1) * width)
            mix_grad_ref[:, lanes] = tn(normed[...], mixed[:, lanes]).astype(BF16)
    part_send.wait_recv()
    first_sum_gain = jnp.zeros((1, model), F32)
    for b in range(3):
        rows = pl.ds(b * part, part)
        upstream = nt(mixed[block_rows(core, b), :], weight[...]) + parts_in[rows, :].astype(F32)
        n, r = norm_parts(x[rows, :].astype(F32))
        value, more = norm_back(upstream, n, r, gain_first[...])
        first_sum_gain = first_sum_gain + more
        grad_own[rows, :] = (midg[rows, :] + value).astype(BF16)
    gains_sum[...] = jnp.zeros_like(gains_sum)
    gains_sum[0:1, :] = first_sum_gain
    mine_lanes = pl.ds(pl.multiple_of(core * width, 128), width)
    gains_sum[1:2, mine_lanes] = gain_sums[0:1, :] + gain_sums[2:3, :]
    gains_sum[2:3, mine_lanes] = gain_sums[3:4, :] + gain_sums[4:5, :]
    gains_sum[3:4, :] = gain_second_grad[...]

    if square:
        kept_rows, third_rows = grad_own.at[rows_at(zq * part, part)], grad_own.at[pl.ds(half, part)]
        grad_moves = Moves(
            [
                remote(kept_rows, grad_out.at[zq], sems, 0, keep),
                remote(third_rows, grad_out.at[2], sems, 1, keep),
            ],
            [
                pltpu.make_async_copy(kept_rows, grad_out.at[zq], local_sem.at[0]),
                pltpu.make_async_copy(third_rows, grad_out.at[2], local_sem.at[1]),
            ],
            remote(grad_own.at[rows_at((1 - zq) * part, part)], grad_out.at[zq], sems, 4, cross),
            moves,
        )
        grad_moves.start()
        gain_row = shard + shard // 3
        for p in range(8):
            payload[p, gain_row:, :] = jnp.zeros((16, 3 * width), BF16)
            payload[p, gain_row:, :shard] = gains_sum[:, p * shard : (p + 1) * shard].astype(BF16)
            for i in range(3):
                at = p * shard + i * (shard // 3)
                payload[p, shard:gain_row, i * width : (i + 1) * width] = outg[at : at + shard // 3, :]
        mine, theirs = 2 * chip + core, 2 * chip + 1 - core
        x_mine, x_other = 2 * (chip ^ 1) + core, 2 * (chip ^ 1) + 1 - core
        y_mine, y_other = 2 * (chip ^ 2) + core, 2 * (chip ^ 2) + 1 - core
        far_mine, far_other = 2 * (chip ^ 3) + core, 2 * (chip ^ 3) + 1 - core
        first = send(payload.at[far_mine], relay.at[0], 38, near_y)
        second = send(payload.at[far_other], relay.at[1], 39, near_x)
        direct_x = send(payload.at[x_other], final.at[0], 40, near_x)
        direct_y = send(payload.at[y_mine], final.at[1], 41, near_y)

        first.wait_recv()
        relay[2] = add(relay[0], payload[x_mine]).astype(BF16)
        onward_x = send(relay.at[2], final.at[2], 42, near_x)
        second.wait_recv()
        relay[3] = add(relay[1], payload[y_other]).astype(BF16)
        onward_y = send(relay.at[3], final.at[3], 43, near_y)
        bulk_line.fourth()
        direct_x.wait_recv()
        onward_y.wait_recv()
        relay[4] = add(payload[theirs], final[0], final[3]).astype(BF16)
        to_core = send(relay.at[4], core_got, 44, partner)
        direct_y.wait_recv()
        onward_x.wait_recv()
        kept = add(payload[mine], final[1], final[2])
        quarter = gain_row // 2
        for i in range(2):
            chunks[2 * core + i] = kept[i * quarter : (i + 1) * quarter].astype(BF16)
        to_core.wait_recv()
        for i in range(2):
            chunks[2 * (1 - core) + i] = core_got[i * quarter : (i + 1) * quarter]
        gain_parts[0] = (kept[gain_row:] + core_got[gain_row:].astype(F32)).astype(BF16)
        mix_line.start()
        gain_lanes = pl.ds(0, 128)
        gain_sends = [
            send(gain_parts.at[0, :, gain_lanes], gain_got.at[i, :, gain_lanes], 45 + i, along[i]) for i in range(3)
        ]
        bulk_line.fifth()
        mix_line.first()
        mix_line.second()
        mix_line.third()
        for copy in gain_sends:
            copy.wait_recv()
        gains_ref[...] = add(
            gain_parts[0, :, :128], gain_got[0, :, :128], gain_got[1, :, :128], gain_got[2, :, :128]
        )
        mix_line.fourth()
        bulk_line.sixth()

        def place(index, values):
            side, up = index // 2, index % 2
            lanes_of = lambda p: slice((2 * p + side) * width, (2 * p + side + 1) * width)
            below = shard - quarter
            for p in range(3):
                part_of = values[:, p * width : (p + 1) * width]
                if up == 0:
                    total_ref[0:quarter, lanes_of(p)] = part_of
                else:
                    total_ref[quarter:shard, lanes_of(p)] = part_of[:below]
                    rows = slice(p * (shard // 3), (p + 1) * (shard // 3))
                    outw_ref[rows, side * width : (side + 1) * width] = part_of[below:]

        flat = jnp.concatenate([whole_line[i] for i in range(4)], axis=0)
        tile = down_ref.shape[0]
        down_ref[...] = flat[:tile]
        ups = [flat[tile + 2 * shard * i : tile + 2 * shard * (i + 1)] for i in range(2)]
        for i in range(2):
            up_out[i] = jnp.where(core == 0, ups[i][shard:], ups[i][:shard])
        up_send = send(up_out, up_got, 48, partner)

        def place_up(side, i, values):
            for j in range(2):
                lanes = pl.ds(pl.multiple_of((2 * (2 * i + j) + side) * tile, 128), tile)
                up_ref[:, lanes] = values[:, j * tile : (j + 1) * tile]

        for i in range(2):
            place_up(core, i, jnp.where(core == 0, ups[i][:shard], ups[i][shard:]))
        up_send.wait_recv()
        for i in range(2):
            place_up(other, i, up_got[i])
        mix_line.fifth()
        mix_line.sixth()
        for i in range(4):
            place(i, chunk_whole[i])
        bulk_line.wait_sends()
        mix_line.wait_sends()
        grad_moves.wait()
    for copy in waits:
        copy.wait_send()


def backward_pass(square, pics, row, shared, weights, gains, bounds, *more):
    length, model = row[1].shape
    width = model // 2
    part = length // 4
    half, tokens = 2 * part, 3 * part
    shard = model // 8
    near = pl.BlockSpec(memory_space=pltpu.VMEM)
    anywhere = pl.BlockSpec(memory_space=pl.ANY)
    low = lambda *shape: (shape, BF16)
    wide = lambda *shape: (shape, F32)
    if square:
        rows = more[0].shape[1]
        tile = rows // 2
        outs = [
            (low(3, part, model), anywhere),
            (low(shard, 6 * width), near),
            (wide(16, 128), near),
            (low(shard, 8 * tile), near),
            (low(tile, model), near),
            (low(shard, model), near),
        ]
    else:
        outs = [(low(tokens, model), near), (low(model, 3 * width), near), (wide(16, model), near)]
    scratch = []
    for queries in (length, half):
        scratch += [
            low(2 * (width // 128), queries, 128), low(length, width), low(length, width), low(queries, width),
            low(queries, width), low(length, 2 * width),
        ]
    scratch += [
        low(length + half, model), low(model, 3 * width), low(tokens, model), wide(tokens, model),
        low(2, length, 128), low(2, length, 128), low(2, length, 128), wide(2, length, 128), wide(length, 128),
        low(length + half, 3 * width), low(length, width), low(length, width), low(half, width), low(half, width),
        wide(8, width), low(tokens, model), low(tokens, model),
    ]
    if square:
        span = rows // 2
        pieces = shard + shard // 3 + 16
        chunk = (pieces - 16) // 2
        scratch += [
            low(tokens, model), low(8, pieces, 3 * width), wide(16, model), low(model, width),
            low(4, span, model), low(2, span, model), low(2, span, model), low(2, span, model), low(2, span, model),
            low(4, rows // 4, model), low(4, rows // 4, model), low(3, rows // 4, model), low(3, rows // 4, model),
            low(2, shard, model), low(2, shard, model),
            low(5, pieces, 3 * width), low(4, pieces, 3 * width), low(pieces, 3 * width), low(4, chunk, 3 * width),
            low(4, chunk, 3 * width), low(3, chunk, 3 * width), low(3, chunk, 3 * width), low(1, 16, 3 * width),
            low(3, 16, 3 * width),
        ]
    return pl.pallas_call(
        functools.partial(backward_kernel, square, pics),
        in_specs=[anywhere] * 17 + [near] * 4 + [anywhere] * len(more),
        out_specs=[spec for _, spec in outs],
        out_shape=[jax.ShapeDtypeStruct(*shape) for shape, _ in outs],
        scratch_shapes=[pltpu.VMEM(*shape) for shape in scratch]
        + [
            pltpu.SemaphoreType.DMA((49,)),
            pltpu.SemaphoreType.DMA((49,)),
            pltpu.SemaphoreType.DMA((30,)),
            pltpu.SemaphoreType.DMA((2,)),
        ],
        compiler_params=pltpu.CompilerParams(
            collective_id=2, has_side_effects=True, vmem_limit_bytes=62 * 1024 * 1024
        ),
        name="backward_pass",
    )(*row, *shared, *weights, *gains, bounds, *more)


def local(
    tokens, lengths, pictures, first_gain, mix_weight, query_gain, key_gain, out_weight,
    second_gain, up_weight, down_weight, cotangent,
):
    chip, core, zp, zq = here()
    chips = lax.axis_size("chip")
    square = chips == 4
    rows = ("chip", "core")
    _, part, model = tokens.shape
    length = 4 * part
    half = 2 * part
    width = HEADS // 2 * HEAD
    pics = lengths.shape[1]
    shard = mix_weight.shape[0]

    hidden = up_weight.shape[1]
    tile = hidden // 8
    gains = [gain[None] for gain in (first_gain, query_gain, key_gain, second_gain)]
    if square:
        forward = forward_pass(
            True, pics, tokens, cotangent, lengths, mix_weight, *gains, up_weight, out_weight
        )
        up_half, out_matrix = forward[19:]
        down_half = down_weight
        gain_second = forward[5]
    else:
        gather = lambda weight: lax.all_gather(weight, rows, axis=0, tiled=True)
        half_of = lambda weight, axis: pick(weight, core, axis)
        mix_half = half_of(gather(mix_weight).reshape(model, 3, 2, width), 2).reshape(model, 3 * width)
        up_half = half_of(gather(up_weight).reshape(model, 4, 2, tile), 2).reshape(model, 4 * tile)
        down_half = half_of(gather(down_weight).reshape(4, 2, tile, model), 1).reshape(4 * tile, model)
        out_matrix = gather(out_weight)
        gains = lax.all_gather(jnp.concatenate(gains), rows, axis=0, tiled=False)
        gains = gains.transpose(1, 0, 2).reshape(4, 1, model).astype(F32)
        gain_second = gains[3]
        gain_qk = half_of(gains[1:3].reshape(2, 2, width), 1).reshape(1, model)
        forward = forward_pass(False, pics, tokens, cotangent, lengths, mix_half, gains[0], gain_qk)
    own_tokens, bounds, mix_half, grad_tokens, gain_first, _, gain_qk = forward[:7]
    normed, qk, v, raw, out, aug = forward[7:13]
    shared_normed, shared_qk, shared_v, shared_raw, shared_out, shared_aug = forward[13:19]

    def collect(mine, cross, third):
        mine = lax.ppermute(mine, COLUMN, KEEP)
        cross = lax.ppermute(cross, COLUMN, CROSS)
        third = lax.ppermute(third, COLUMN, KEEP)
        return jnp.stack([jnp.where(zq == 0, mine, cross), jnp.where(zq == 0, cross, mine), third])

    output, middle_grad, grad, shared_grad, out_grad, second_gain_grad, packed, far = dense(
        square, out, shared_out, own_tokens, grad_tokens, cotangent, out_matrix, gain_second, bounds,
        up_half, down_half,
    )
    row_side = (aug, qk, v, out, grad, raw, normed)
    shared_side = (shared_aug, shared_qk, shared_v, shared_out, shared_grad, shared_raw, shared_normed)
    weights = (mix_half, own_tokens, middle_grad)
    gains = (gain_first, gain_qk, second_gain_grad)
    if square:
        input_out, mix_out, gains_out, up_out, down_out, outw_out = backward_pass(
            True, pics, row_side, shared_side, weights, gains, bounds, packed, far, out_grad
        )
        gains_out = gains_out[:4, :shard]
        mix_out, up_out, down_out, outw_out = (
            array.astype(F32) for array in (mix_out, up_out, down_out, outw_out)
        )
    else:
        input_grad, mix_grad, gain_grads = backward_pass(
            False, pics, row_side, shared_side, weights, gains, bounds
        )

        def reduce(grad):
            return lax.psum(lax.psum_scatter(grad, rows, scatter_dimension=0, tiled=True), SEQ).astype(F32)

        first, second = input_grad[:part], input_grad[part:half]
        input_out = collect(
            jnp.where(zq == 0, first, second), jnp.where(zq == 0, second, first), input_grad[half:]
        )
        own_core = jnp.arange(2) == core
        eighth = model // 8
        down_grad = packed[:, None, :tile]
        down_out = reduce(jnp.where(own_core[None, :, None, None], down_grad, 0).reshape(hidden, model))
        up_grad = packed[:, tile : 2 * tile].reshape(4, 2, 2 * eighth, 2, tile).transpose(0, 2, 1, 3, 4)
        up_grad = up_grad.reshape(model, 4, 1, tile)
        up_out = reduce(jnp.where(own_core[None, None, :, None], up_grad, 0).reshape(model, hidden))
        out_grad = out_grad.reshape(model, 1, width)
        outw_out = reduce(jnp.where(own_core[None, :, None], out_grad, 0).reshape(model, model))
        mix_out = reduce(
            jnp.where(own_core[None, None, :, None], mix_grad.reshape(model, 3, 1, width), 0).reshape(model, 6 * width)
        )
        gain_grads = gain_grads[:4].reshape(4, 2 * chips, shard).transpose(1, 0, 2).astype(BF16)
        gains_out = reduce(gain_grads).reshape(4, shard)
    return (
        output, input_out, gains_out[0], mix_out, gains_out[1], gains_out[2], outw_out, gains_out[3],
        up_out, down_out,
    )


def solution(mesh):
    fsdp = mesh.shape["fsdp"]
    split = Mesh(mesh.devices.reshape(fsdp // 2, 2, 2, 2), ("chip", "core", "zp", "zq"))
    rows = ("chip", "core")
    return jax.shard_map(
        local,
        mesh=split,
        in_specs=(
            P(rows, SEQ, None),
            P(rows, None),
            P(rows, SEQ),
            P(rows),
            P(rows, None),
            P(rows),
            P(rows),
            P(rows, None),
            P(rows),
            P(rows, None),
            P(rows, None),
            P(rows, SEQ, None),
        ),
        out_specs=(
            P(rows, SEQ, None),
            P(rows, SEQ, None),
            P(rows),
            P(rows, None),
            P(rows),
            P(rows),
            P(rows, None),
            P(rows),
            P(rows, None),
            P(rows, None),
        ),
        check_vma=False,
    )
```

```python
import functools

import jax
import jax.numpy as jnp
from jax import lax
from jax.experimental import pallas as pl
from jax.experimental.pallas import tpu as pltpu
from jax.sharding import Mesh, PartitionSpec as P

HEADS = 12
HEAD = 64
EPSILON = 1e-06
BLOCK = 256
STEP = 512
MARK = 32.0
EXP2_FACTOR = HEAD**-0.5 * 1.4426950408889634
F32 = jnp.float32
BF16 = jnp.bfloat16
VMEM_LIMIT = 56 * 1024 * 1024

SEQ = ("zp", "zq")
COLUMN = ("core", "zp", "zq")
KEEP = [
    (core * 4 + z, (z // 2) * 4 + 2 * core + z % 2) for core in range(2) for z in range(4)
]
CROSS = [
    (core * 4 + z, (z // 2) * 4 + 2 * core + 1 - z % 2) for core in range(2) for z in range(4)
]


def swap(array, name, bit=1):
    count = lax.axis_size(name)
    return lax.ppermute(array, name, [(i, i ^ bit) for i in range(count)])


def pick(array, index, axis=0):
    return lax.dynamic_index_in_dim(array, index, axis, keepdims=False)


def group_ones(scale, size=128):
    row = lax.broadcasted_iota(jnp.int32, (size, size), 0) // HEAD
    column = lax.broadcasted_iota(jnp.int32, (size, size), 1) // HEAD
    return jnp.where(row == column, scale, 0.0).astype(BF16)


def group_sum(values, ones):
    return jnp.dot(values.astype(BF16), ones, preferred_element_type=F32)


def group_sum_fine(values, ones):
    high = values.astype(BF16)
    return group_sum(high, ones) + group_sum(values - high.astype(F32), ones)


def project_kernel(x_ref, gain_ref, weight_ref, qkg_ref, normed_ref, qk_ref, v_ref, raw_ref):
    both = qk_ref.shape[1]
    x = x_ref[...].astype(F32)
    center = x - jnp.mean(x, axis=-1, keepdims=True)
    spread = jnp.mean(center * center, axis=-1, keepdims=True)
    normed = (center * lax.rsqrt(spread + EPSILON) * gain_ref[...]).astype(BF16)
    normed_ref[...] = normed
    ones = group_ones(1.0 / HEAD, 256)
    for at in range(0, both, 256):
        lanes = slice(at, at + 256)
        raw = jnp.dot(normed, weight_ref[:, lanes], preferred_element_type=F32)
        raw_ref[:, lanes] = raw.astype(BF16)
        c = raw - group_sum(raw, ones)
        n = c * lax.rsqrt(group_sum(c * c, ones) + EPSILON)
        qk_ref[:, lanes] = (n * qkg_ref[:, lanes]).astype(BF16)
    v_ref[...] = jnp.dot(normed, weight_ref[:, both:], preferred_element_type=F32).astype(BF16)


def nt(a, b):
    return lax.dot_general(a, b, (((1,), (1,)), ((), ())), preferred_element_type=F32)


def tn(a, b):
    return lax.dot_general(a, b, (((0,), (0,)), ((), ())), preferred_element_type=F32)


def slots(queries, length, part):
    at = lax.broadcasted_iota(jnp.int32, (queries, 128), 0)
    if queries == length:
        return at
    return at % part + part * (lax.axis_index("zq") + 2 * (at // part))


def own_rows(ref, start, count, queries, part):
    if queries == ref.shape[0]:
        return ref[pl.ds(start, count), :]
    zq = lax.axis_index("zq")
    pieces = [
        ref[pl.ds(pl.multiple_of((zq + 2 * i) * part, part), part), :]
        for i in range(start // part, (start + count) // part)
    ]
    return jnp.concatenate(pieces, axis=0)


def query_marks(bounds_ref, place, queries, length, part, pics):
    at = slots(queries, length, part)
    inside = (at >= bounds_ref[0:1, :]) & (at < bounds_ref[2:3, :])
    values = jnp.where(inside, MARK, 0.0)
    return jnp.where(place == pics, MARK, values).astype(BF16)


def key_marks(bounds_ref, place, length, pics):
    at = lax.broadcasted_iota(jnp.int32, (length, 128), 0)
    inside = (at >= bounds_ref[0:1, :]) & (at < bounds_ref[1:2, :])
    values = jnp.where(inside, MARK, 0.0)
    values = jnp.where(place == pics, -MARK, values)
    return jnp.where((place > pics) & (place < pics + 4), 1.0, values).astype(BF16)


def attend_kernel(pics, q_ref, k_ref, v_ref, bounds_ref, out_ref, aug_ref, kaug, vaug, qaug):
    length = k_ref.shape[0]
    queries = out_ref.shape[0]
    part = length // 4
    lane = lax.broadcasted_iota(jnp.int32, (1, 128), 1)
    place = lane % HEAD
    sides = [lane < HEAD, lane >= HEAD]
    kmarks = key_marks(bounds_ref, place, length, pics)
    qmarks = query_marks(bounds_ref, place, queries, length, part, pics)
    qaug[...] = qmarks
    for h in range(2):
        kaug[h] = jnp.where(sides[h], k_ref[...], kmarks)
        vaug[h] = jnp.where(sides[h], v_ref[...], jnp.ones_like(v_ref))
    for b in range(queries // STEP):
        rows = pl.ds(b * STEP, STEP)
        mine = own_rows(q_ref, b * STEP, STEP, queries, part)
        query = [jnp.where(sides[h], mine, qaug[rows, :]) for h in range(2)]
        total = [jnp.zeros((STEP, 128), F32)] * 2
        for j in range(length // STEP):
            keys = pl.ds(j * STEP, STEP)
            scores = [nt(query[h], kaug[h, keys, :]) for h in range(2)]
            weights = [jnp.exp2(x * EXP2_FACTOR).astype(BF16) for x in scores]
            total = [
                total[h] + jnp.dot(weights[h], vaug[h, keys, :], preferred_element_type=F32) for h in range(2)
            ]
        results = []
        for h in range(2):
            results.append(total[h] / pltpu.roll(total[h], HEAD, 1))
            log_total = jnp.log(jnp.where(sides[h], 1.0, total[h])) * -(HEAD**0.5)
            first = log_total.astype(BF16)
            rest = log_total - first.astype(F32)
            middle = rest.astype(BF16)
            last = (rest - middle.astype(F32)).astype(BF16)
            logs = jnp.where(place == pics + 1, first, jnp.where(place == pics + 2, middle, last))
            slot = jnp.logical_not(sides[h]) & (place > pics) & (place < pics + 4)
            aug_ref[h, rows, :] = jnp.where(slot, logs, query[h])
        out_ref[rows, :] = jnp.where(sides[0], results[0], results[1]).astype(BF16)


def head_norm_back(e, raw, gain, means):
    raw = raw.astype(F32)
    c = raw - group_sum(raw, means)
    r = lax.rsqrt(group_sum(c * c, means) + EPSILON)
    n = c * r
    t = e * gain
    grad = r * (t - group_sum(t, means) - n * group_sum(t * n, means))
    return grad.astype(BF16), jnp.sum(e * n, axis=0, keepdims=True)


def attend_back_kernel(
    pics, aug_ref, k_ref, v_ref, out_ref, do_ref, rawq_ref, rawk_ref, qg_ref, kg_ref, bounds_ref,
    dq_ref, dk_ref, dv_ref, qgg_ref, kgg_ref, kaug, vaug, doaug, qsum, ksum,
):
    length = k_ref.shape[0]
    queries = do_ref.shape[0]
    part = length // 4
    whole = queries == length
    lane = lax.broadcasted_iota(jnp.int32, (1, 128), 1)
    place = lane % HEAD
    sides = [lane < HEAD, lane >= HEAD]
    kmarks = key_marks(bounds_ref, place, length, pics)
    vmarks = jnp.where(place < 2, 1.0, 0.0).astype(BF16)
    ones = group_ones(1.0)
    inner = group_sum_fine(do_ref[...].astype(F32) * out_ref[...].astype(F32), ones)
    inner = -pltpu.roll(inner, HEAD, 1)
    inner_high = inner.astype(BF16)
    inner_low = (inner - inner_high.astype(F32)).astype(BF16)
    zero = jnp.zeros((), BF16)
    gmarks = jnp.where(place == 0, inner_high, jnp.where(place == 1, inner_low, zero))
    for h in range(2):
        kaug[h] = jnp.where(sides[h], k_ref[...], kmarks)
        vaug[h] = jnp.where(sides[h], v_ref[...], vmarks)
        doaug[h] = jnp.where(sides[h], do_ref[...], gmarks)
    for b in range(length // STEP):
        keys = pl.ds(b * STEP, STEP)
        key = [kaug[h, keys, :] for h in range(2)]
        value = [vaug[h, keys, :] for h in range(2)]
        dk = [jnp.zeros((STEP, 128), F32)] * 2
        dv = [jnp.zeros((STEP, 128), F32)] * 2
        for j in range(queries // STEP):
            rows = pl.ds(j * STEP, STEP)
            query = [aug_ref[h, rows, :] for h in range(2)]
            grad = [doaug[h, rows, :] for h in range(2)]
            scores = [nt(key[h], query[h]) for h in range(2)]
            soft_grad = [nt(value[h], grad[h]) for h in range(2)]
            weights = [jnp.exp2(x * EXP2_FACTOR) for x in scores]
            score_grad = [(weights[h] * soft_grad[h]).astype(BF16) for h in range(2)]
            for h in range(2):
                part_sum = tn(score_grad[h], key[h])
                if b == 0:
                    qsum[h, rows, :] = part_sum
                else:
                    qsum[h, rows, :] += part_sum
                dk[h] = dk[h] + jnp.dot(score_grad[h], query[h], preferred_element_type=F32)
                dv[h] = dv[h] + jnp.dot(weights[h].astype(BF16), grad[h], preferred_element_type=F32)
        ksum[keys, :] = jnp.where(sides[0], dk[0], dk[1]) * HEAD**-0.5
        dv_ref[keys, :] = jnp.where(sides[0], dv[0], dv[1]).astype(BF16)

    means = group_ones(1.0 / HEAD)
    gain_sum = jnp.zeros((1, 128), F32)
    for b in range(queries // part):
        rows = pl.ds(b * part, part)
        e = jnp.where(sides[0], qsum[0, rows, :], qsum[1, rows, :]) * HEAD**-0.5
        raw = own_rows(rawq_ref, b * part, part, queries, part)
        dq_ref[rows, :], more = head_norm_back(e.astype(BF16).astype(F32), raw, qg_ref[...], means)
        gain_sum = gain_sum + more
    qgg_ref[...] = gain_sum
    gain_sum = jnp.zeros((1, 128), F32)
    for b in range(length // part):
        rows = pl.ds(b * part, part)
        e = ksum[rows, :].astype(BF16)
        if whole:
            dk_ref[rows, :], more = head_norm_back(e.astype(F32), rawk_ref[rows, :], kg_ref[...], means)
            gain_sum = gain_sum + more
        else:
            dk_ref[rows, :] = e
    kgg_ref[...] = gain_sum


def shared_keys_kernel(dk_ref, dv_ref, gotk_ref, gotv_ref, rawk_ref, kg_ref, outk_ref, outv_ref, kgg_ref):
    count = outk_ref.shape[0]
    part = count // 2
    means = group_ones(1.0 / HEAD)
    gain_sum = jnp.zeros((1, 128), F32)
    for b in range(2):
        rows = pl.ds(b * part, part)
        own = lambda ref: own_rows(ref, b * part, part, count, part)
        e = own(dk_ref).astype(F32) + gotk_ref[rows, :].astype(F32)
        outk_ref[rows, :], more = head_norm_back(e, own(rawk_ref), kg_ref[...], means)
        gain_sum = gain_sum + more
        outv_ref[rows, :] = (own(dv_ref).astype(F32) + gotv_ref[rows, :].astype(F32)).astype(BF16)
    kgg_ref[...] = gain_sum


def gelu_pair(h):
    size = jnp.abs(h)
    bell = jnp.exp2(h * h * -0.7213475204444817)
    t = 1.0 / (1.0 + 0.23164189 * size)
    series = t * (0.127414796 + t * (-0.142248368 + t * (0.7107068705 + t * (-0.7265760135 + t * 0.5307027145))))
    tail = series * bell
    below = jnp.where(h < 0.0, tail, 1.0 - tail)
    return h * below, below + h * (bell * 0.3989422804014327)


def norm_parts(values):
    center = values - jnp.mean(values, axis=-1, keepdims=True)
    spread = lax.rsqrt(jnp.mean(center * center, axis=-1, keepdims=True) + EPSILON)
    return center * spread, spread


def norm_back(upstream, n, r, gain):
    t = upstream * gain
    grad = r * (t - jnp.mean(t, axis=-1, keepdims=True) - n * jnp.mean(t * n, axis=-1, keepdims=True))
    return grad, jnp.sum(upstream * n, axis=0, keepdims=True)


MESH_ID = pl.DeviceIdType.MESH


def here():
    return lax.axis_index("chip"), lax.axis_index("core"), lax.axis_index("zp"), lax.axis_index("zq")


def remote(source, target, sems, at, device):
    sent, got = sems
    return pltpu.make_async_remote_copy(
        src_ref=source, dst_ref=target, send_sem=sent.at[at], recv_sem=got.at[at],
        device_id=device, device_id_type=MESH_ID,
    )


def greet(devices, maybe=None, moves=None):
    barrier = pltpu.get_barrier_semaphore()
    for device in devices:
        pl.semaphore_signal(barrier, inc=1, device_id=device, device_id_type=MESH_ID)
    if maybe is None:
        pl.semaphore_wait(barrier, len(devices))
        return

    @pl.when(moves)
    def _():
        pl.semaphore_signal(barrier, inc=1, device_id=maybe, device_id_type=MESH_ID)

    pl.semaphore_wait(barrier, len(devices) + jnp.where(moves, 1, 0))


def rows_at(start, count):
    return pl.ds(pl.multiple_of(start, 16), count)


class Moves:
    def __init__(self, moved, stays, crossed, moves):
        self.moved, self.stays, self.crossed, self.moves = moved, stays, crossed, moves

    def each(self, act):
        if self.crossed is not None:
            act(self.crossed)

        @pl.when(self.moves)
        def _():
            for copy in self.moved:
                act(copy)

        @pl.when(jnp.logical_not(self.moves))
        def _():
            for copy in self.stays:
                act(copy)

    def start(self):
        self.each(lambda copy: copy.start())

    def wait(self):
        self.each(lambda copy: copy.wait())


class Line:
    def __init__(self, parts, whole, right, left, sems, at):
        chip, core, zp, zq = here()
        self.z = 2 * zp + zq
        up, down = jnp.minimum(self.z + 1, 3), jnp.maximum(self.z - 1, 0)
        self.next = (chip, core, up // 2, up % 2)
        self.last = (chip, core, down // 2, down % 2)
        self.parts, self.whole, self.right, self.left = parts, whole, right, left
        self.sems, self.at, self.sends = sems, at, []

    def at_chip(self, z, *acts):
        @pl.when(self.z == z)
        def _():
            for act in acts:
                act()

    def part_copy(self, c, rightward):
        if rightward:
            return remote(self.parts.at[c], self.right.at[3 - c], self.sems, self.at + 3 - c, self.next)
        return remote(self.parts.at[c], self.left.at[c], self.sems, self.at + 3 + c, self.last)

    def whole_copy(self, c, rightward):
        if rightward:
            return remote(self.whole.at[c], self.whole.at[c], self.sems, self.at + 6 + c, self.next)
        return remote(self.whole.at[c], self.whole.at[c], self.sems, self.at + 8 + c, self.last)

    def send(self, z, make, c, rightward):
        self.sends.append((z, make, c, rightward))
        return lambda: make(c, rightward).start()

    def take(self, c, rightward):
        def act():
            self.part_copy(c, rightward).wait_recv()
            came = self.right[3 - c] if rightward else self.left[c]
            self.parts[c] = add(self.parts[c], came).astype(BF16)

        return act

    def got(self, c, rightward):
        return lambda: self.whole_copy(c, rightward).wait_recv()

    def start(self):
        part = self.part_copy
        self.at_chip(0, *[self.send(0, part, c, True) for c in (3, 2, 1)])
        self.at_chip(3, *[self.send(3, part, c, False) for c in (0, 1, 2)])

    def first(self):
        self.at_chip(1, self.take(3, True), self.send(1, self.part_copy, 3, True))
        self.at_chip(2, self.take(0, False), self.send(2, self.part_copy, 0, False))

    def second(self):
        part = self.part_copy
        self.at_chip(
            1, self.take(2, True), self.send(1, part, 2, True), self.take(0, False), self.send(1, part, 0, False)
        )
        self.at_chip(
            2, self.take(1, False), self.send(2, part, 1, False), self.take(3, True), self.send(2, part, 3, True)
        )

    def third(self):
        self.at_chip(0, self.take(0, False))
        self.at_chip(1, self.take(1, True), self.take(1, False))
        self.at_chip(2, self.take(2, True), self.take(2, False))
        self.at_chip(3, self.take(3, True))
        self.whole[self.z] = self.parts[self.z]
        for z in range(4):
            acts = [self.send(z, self.whole_copy, z, True)] if z < 3 else []
            acts += [self.send(z, self.whole_copy, z, False)] if z > 0 else []
            self.at_chip(z, *acts)

    def fourth(self):
        whole = self.whole_copy
        for z in (1, 2):
            self.at_chip(
                z, self.got(z - 1, True), self.send(z, whole, z - 1, True), self.got(z + 1, False),
                self.send(z, whole, z + 1, False),
            )

    def fifth(self):
        whole = self.whole_copy
        self.at_chip(1, self.got(3, False), self.send(1, whole, 3, False))
        self.at_chip(2, self.got(0, True), self.send(2, whole, 0, True))

    def sixth(self):
        self.at_chip(0, *[self.got(c, False) for c in (1, 2, 3)])
        self.at_chip(3, *[self.got(c, True) for c in (2, 1, 0)])

    def wait_sends(self):
        for z in range(4):
            mine = [make(c, rightward) for at, make, c, rightward in self.sends if at == z]
            self.at_chip(z, *[copy.wait_send for copy in mine])


def write_bounds(pics, lens_ref, bounds_ref, zp, zq, length):
    lane = lax.broadcasted_iota(jnp.int32, (8, 128), 1)
    lens = jnp.where(zp == 0, lens_ref[0], lens_ref[1])
    ends = lens
    for hop in (1, 2, 4, 8):
        ends = ends + jnp.where(lane >= hop, pltpu.roll(ends, hop, 1), 0)
    starts = ends - lens
    last = (lens > 0) & (pltpu.roll(lens, 127, 1) == 0)
    query_ends = jnp.where(last, length, ends)
    total = jnp.max(jnp.where(lane < pics, ends, 0), axis=1, keepdims=True)

    def both(values):
        values = jnp.where(lane < HEAD, jnp.where(lane < pics, values, 2 * length), 0)
        return values + pltpu.roll(values, HEAD, 1)

    tables = [both(starts), both(ends), both(query_ends), jnp.broadcast_to(total, (8, 128))]
    for t in range(4):
        table = tables[t]
        bounds_ref[0, t : t + 1, :] = jnp.where(zq == 0, table[0:1], table[1:2])
        bounds_ref[1, t : t + 1, :] = table[2:3]
    bounds_ref[:, 4:, :] = jnp.zeros((2, 4, 128), jnp.int32)


def forward_kernel(square, pics, *refs):
    refs = list(refs)
    take = lambda count: [refs.pop(0) for _ in range(count)]
    tokens_ref, cot_ref, lengths_ref, weight_in = take(4)
    if square:
        gain_in = take(4)
        up_in, outw_ref = take(2)
    else:
        gain_first_in, gain_qk_in = take(2)
    x_out, bounds_ref, mix_hbm, cot_hbm, gain_first, second_ref, gain_qk = take(7)
    names = ("normed", "qk", "v", "raw", "out", "aug")
    outs = [dict(zip(names, take(6))) for _ in range(2)]
    if square:
        up_hbm, outw_hbm = take(2)
    row_ref, shared_ref, cot_out, lens_ref, lens_out = take(5)
    scratch = [dict(zip(names, take(6))) for _ in range(2)]
    kaug, vaug, qaug = take(3)
    if square:
        mix_ref, gains_ref, up_ref, mix_out, gains_out, up_out, outw_out = take(7)
    sent, got, local_sem, write_sem = take(4)

    chip, core, zp, zq = here()
    z = 2 * zp + zq
    part = tokens_ref.shape[1]
    half, length = 2 * part, 4 * part
    sems = (sent, got)
    partner = (chip, 1 - core, zp, zq)
    side = (chip, core, zp, 1 - zq)
    keep = (chip, zp, core, zq)
    cross = (chip, zp, core, 1 - zq)
    moves = core != zp
    near_x = (chip ^ 1, core, zp, zq)
    near_y = (chip ^ 2, core, zp, zq)
    greet([partner, side, cross] + ([near_x, near_y] if square else []), keep, moves)

    def quarter(ref, index):
        return ref.at[rows_at(index * part, part)]

    own_row = remote(tokens_ref.at[zq], quarter(row_ref, z), sems, 0, keep)
    own_shared = remote(tokens_ref.at[2], quarter(shared_ref, z), sems, 2, keep)
    stay_row = pltpu.make_async_copy(tokens_ref.at[zq], quarter(row_ref, z), local_sem.at[0])
    stay_shared = pltpu.make_async_copy(tokens_ref.at[2], quarter(shared_ref, z), local_sem.at[1])

    @pl.when(moves)
    def _():
        own_row.start()

    @pl.when(jnp.logical_not(moves))
    def _():
        stay_row.start()

    cross_row = remote(tokens_ref.at[1 - zq], quarter(row_ref, z), sems, 1, cross)
    cross_row.start()

    @pl.when(moves)
    def _():
        own_shared.start()

    @pl.when(jnp.logical_not(moves))
    def _():
        stay_shared.start()

    lens_ref[...] = jnp.zeros_like(lens_ref)
    lens_ref[: lengths_ref.shape[0], :pics] = lengths_ref[...]
    lens_copy = remote(lens_ref, lens_out.at[core], sems, 8, partner)
    lens_copy.start()
    lens_stay = pltpu.make_async_copy(lens_ref, lens_out.at[core], local_sem.at[2])
    lens_stay.start()
    waits = []
    if square:
        shard = mix_ref.shape[1]
        tile = up_ref.shape[2] // 4
        width = mix_ref.shape[2] // 3
        for h in range(2):
            for i in range(3):
                mix_ref[h, :, i * width : (i + 1) * width] = weight_in[:, (2 * i + h) * width : (2 * i + h + 1) * width]
        gains_ref[...] = jnp.zeros_like(gains_ref)
        for i in range(4):
            gains_ref[i : i + 1, :shard] = gain_in[i][...].astype(F32)
        mine, theirs = 2 * chip + core, 2 * chip + 1 - core
        slot = [9]

        def send(source, target, device):
            copy = remote(source, target, sems, slot[0], device)
            slot[0] += 1
            copy.start()
            waits.append(copy)
            return copy

        def stay(source, target, at):
            copy = pltpu.make_async_copy(source, target, local_sem.at[at])
            copy.start()
            return copy

        def block(ref, start, count):
            return ref.at[rows_at(start, count)]

        mix_piece = lambda index: (block(mix_out, index * shard, shard), gains_out.at[index])

        def send_mix(sources, index, device):
            return [send(source, target, device) for source, target in zip(sources, mix_piece(index))]

        def arrived(copies):
            for copy in copies:
                copy.wait_recv()

        x_mine, y_other = 2 * (chip ^ 1) + core, 2 * (chip ^ 2) + 1 - core
        to_core = send_mix((mix_ref.at[1 - core], gains_ref), mine, partner)
        a_x = send_mix((mix_ref.at[core], gains_ref), mine, near_x)
        a_y = send_mix((mix_ref.at[core], gains_ref), mine, near_y)
        for h in range(2):
            for i in range(4):
                up_ref[h, :, i * tile : (i + 1) * tile] = up_in[:, (2 * i + h) * tile : (2 * i + h + 1) * tile]
        up_core = send(up_ref.at[1 - core], block(up_out, mine * shard, shard), partner)
        out_core = send(outw_ref, block(outw_out, mine * shard, shard), partner)
        stays = [
            stay(mix_ref.at[core], mix_piece(mine)[0], 3),
            stay(gains_ref, gains_out.at[mine], 4),
            stay(up_ref.at[core], block(up_out, mine * shard, shard), 5),
            stay(outw_ref, block(outw_out, mine * shard, shard), 6),
        ]
        arrived(to_core)
        b_x = send_mix(mix_piece(theirs), theirs, near_x)
        b_y = send_mix(mix_piece(theirs), theirs, near_y)
        arrived(a_x)
        a_far = send_mix(mix_piece(x_mine), x_mine, near_y)
        arrived(b_y)
        b_far = send_mix(mix_piece(y_other), y_other, near_x)
        for copy in stays:
            copy.wait()
        arrived([up_core])
        ohalf = shard // 2

        def bundle(first, from_chip):
            same, twin = 2 * from_chip + core, 2 * from_chip + 1 - core
            part_of = 0 if first else 1
            return [
                block(up_out, (same if first else twin) * shard, shard),
                block(outw_out, same * shard + part_of * ohalf, ohalf),
            ]

        def send_bundle(first, from_chip, device):
            return [send(ref, ref, device) for ref in bundle(first, from_chip)]

        first_x = send_bundle(True, chip, near_x)
        first_y = send_bundle(True, chip, near_y)
        second_x = send_bundle(False, chip, near_x)
        second_y = send_bundle(False, chip, near_y)

    lens_copy.wait()
    lens_stay.wait()
    write_bounds(pics, lens_out, bounds_ref, zp, zq, length)
    if square:
        arrived(a_y + b_x + a_far + b_far)
        for p in range(gains_out.shape[0]):
            lanes = slice(p * shard, (p + 1) * shard)
            values = gains_out[p, :, :shard]
            gain_first[:, lanes] = values[0:1]
            second_ref[:, lanes] = values[3:4]
            half_pieces = gains_out.shape[0] // 2

            @pl.when(core == p // half_pieces)
            def _():
                at = (p % half_pieces) * shard
                gain_qk[:, at : at + shard] = values[1:2]
                gain_qk[:, width + at : width + at + shard] = values[2:3]
        weight = mix_out
    else:
        weight = weight_in
        width = weight.shape[1] // 3
        second_ref[...] = jnp.zeros_like(second_ref)
        gain_first[...] = gain_first_in[...]
        gain_qk[...] = gain_qk_in[...]
    writes = []

    def write(source, target, at):
        copy = pltpu.make_async_copy(source, target, write_sem.at[at])
        copy.start()
        writes.append(copy)

    write(weight, mix_hbm, 0)
    first, second = 2 * core + zq, 2 * core + 1 - zq
    other_first, other_second = 2 * (1 - core) + zq, 2 * (1 - core) + 1 - zq

    def forwarded(ref, index, at):
        return remote(quarter(ref, index), quarter(ref, index), sems, at, partner)

    def project(tokens, bufs, at):
        rows = rows_at(at * part, part)
        project_kernel(
            tokens.at[rows], gain_first, weight, gain_qk, bufs["normed"].at[rows], bufs["qk"].at[rows],
            bufs["v"].at[rows], bufs["raw"].at[rows],
        )

    def project_row(i, _):
        @pl.when(i == 0)
        def _():
            @pl.when(moves)
            def _():
                own_row.wait_recv()

            @pl.when(jnp.logical_not(moves))
            def _():
                stay_row.wait()

            forwarded(row_ref, first, 3).start()

        @pl.when(i == 1)
        def _():
            cross_row.wait_recv()
            forwarded(row_ref, second, 4).start()

        @pl.when(i == 2)
        def _():
            forwarded(row_ref, other_first, 3).wait_recv()

        @pl.when(i == 3)
        def _():
            forwarded(row_ref, other_second, 4).wait_recv()

        order = jnp.where(i == 0, first, jnp.where(i == 1, second, jnp.where(i == 2, other_first, other_second)))
        project(row_ref, scratch[0], order)
        return 0

    row_one, row_two = forwarded(row_ref, first, 3), forwarded(row_ref, second, 4)

    def attend(bufs, bounds):
        def one(p, _):
            lanes = pl.ds(pl.multiple_of(p * 128, 128), 128)
            attend_kernel(
                pics, bufs["qk"].at[:, lanes],
                bufs["qk"].at[:, pl.ds(pl.multiple_of(width + p * 128, 128), 128)], bufs["v"].at[:, lanes], bounds,
                bufs["out"].at[:, lanes], bufs["aug"].at[pl.ds(2 * p, 2)], kaug, vaug, qaug.at[pl.ds(0, bufs["out"].shape[0])],
            )
            return 0

        lax.fori_loop(0, width // 128, one, 0)

    lax.fori_loop(0, 4, project_row, 0)
    for i, name in enumerate(("normed", "qk", "v", "raw")):
        write(scratch[0][name], outs[0][name], 1 + i)
    write(row_ref.at[rows_at(core * half, half)], x_out.at[pl.ds(0, half)], 5)

    @pl.when(moves)
    def _():
        own_shared.wait_recv()

    @pl.when(jnp.logical_not(moves))
    def _():
        stay_shared.wait()

    to_side = remote(quarter(shared_ref, first), quarter(shared_ref, first), sems, 5, side)
    to_side.start()
    shared_one = remote(quarter(shared_ref, first), quarter(shared_ref, first), sems, 6, partner)
    shared_one.start()
    attend(scratch[0], bounds_ref.at[0])
    cot_moves = Moves(
        [remote(cot_ref.at[zq], cot_out, sems, 43, keep)],
        [pltpu.make_async_copy(cot_ref.at[zq], cot_out, local_sem.at[0])],
        None,
        moves,
    )
    cot_moves.start()
    write(scratch[0]["out"], outs[0]["out"], 6)
    write(scratch[0]["aug"], outs[0]["aug"], 7)
    to_side.wait_recv()
    shared_two = forwarded(shared_ref, second, 7)
    shared_two.start()
    if square:
        arrived(first_x + second_y)
        far_first = send_bundle(True, chip ^ 1, near_y)
        far_second = send_bundle(False, chip ^ 2, near_x)
    shared_one.wait_recv()
    shared_two.wait_recv()

    def project_shared(i, _):
        project(shared_ref, scratch[1], i)
        return 0

    lax.fori_loop(0, 4, project_shared, 0)
    for i, name in enumerate(("normed", "qk", "v", "raw")):
        write(scratch[1][name], outs[1][name], 8 + i)
    write(shared_ref.at[rows_at(first * part, part)], x_out.at[pl.ds(half, part)], 12)
    attend(scratch[1], bounds_ref.at[1])
    write(scratch[1]["out"], outs[1]["out"], 13)
    write(scratch[1]["aug"], outs[1]["aug"], 14)

    if square:
        arrived(first_y + second_x + far_first + far_second)
        sent_pieces = []
        for c in (chip ^ 1, chip ^ 2, chip ^ 3):
            target = block(outw_out, (2 * c + core) * shard, shard)
            sent_pieces.append(send(target, target, partner))
        write(up_out, up_hbm, 15)
        arrived(sent_pieces + [out_core])
        write(outw_out, outw_hbm, 17)
        for copy in waits:
            copy.wait_send()
    cot_moves.wait()
    write(cot_out, cot_hbm, 18)
    for copy in (row_one, row_two, shared_one, shared_two, to_side, cross_row):
        copy.wait_send()

    @pl.when(moves)
    def _():
        own_row.wait_send()
        own_shared.wait_send()

    for copy in writes:
        copy.wait()


def forward_pass(square, pics, tokens, cotangent, lengths, weight, *more):
    _, part, model = tokens.shape
    length, half, width = 4 * part, 2 * part, model // 2
    near = pl.BlockSpec(memory_space=pltpu.VMEM)
    anywhere = pl.BlockSpec(memory_space=pl.ANY)
    low = lambda *shape: (shape, BF16)
    wide = lambda *shape: (shape, F32)
    outs = [
        (low(3 * part, model), anywhere),
        (((2, 8, 128), jnp.int32), near),
        (low(model, 3 * width), anywhere),
        (low(part, model), anywhere),
        (wide(1, model), near),
        (wide(1, model), near),
        (wide(1, model), near),
    ]
    bufs = []
    for queries in (length, half):
        shapes = [
            low(length, model), low(length, 2 * width), low(length, width), low(length, 2 * width),
            low(queries, width), low(2 * (width // 128), queries, 128),
        ]
        outs += [(shape, anywhere) for shape in shapes]
        bufs += shapes
    table = ((8, 128), jnp.int32)
    scratch = [low(length, model), low(length, model), low(part, model), table, ((2, 8, 128), jnp.int32)] + bufs
    scratch += [low(2, length, 128), low(2, length, 128), low(length, 128)]
    if square:
        up, _ = more[4:]
        shard, hidden = up.shape
        landed = [low(model, hidden // 2), low(model, model)]
        outs += [(shape, anywhere) for shape in landed]
        scratch += [low(2, shard, 3 * width), wide(8, 128), low(2, shard, hidden // 2)]
        scratch += [low(model, 3 * width), wide(8, 8, 128)] + landed
    return pl.pallas_call(
        functools.partial(forward_kernel, square, pics),
        in_specs=[near] * (4 + len(more)),
        out_specs=[spec for _, spec in outs],
        out_shape=[jax.ShapeDtypeStruct(*shape) for shape, _ in outs],
        scratch_shapes=[pltpu.VMEM(*shape) for shape in scratch]
        + [
            pltpu.SemaphoreType.DMA((49,)),
            pltpu.SemaphoreType.DMA((49,)),
            pltpu.SemaphoreType.DMA((8,)),
            pltpu.SemaphoreType.DMA((19,)),
        ],
        compiler_params=pltpu.CompilerParams(
            collective_id=0, has_side_effects=True, vmem_limit_bytes=60 * 1024 * 1024
        ),
        name="forward_pass",
    )(tokens, cotangent, lengths, weight, *more)


def dense_kernel(
    square, out_ref, shared_ref, x, grad_ref, cot_ref, outw_ref, gain_ref, bounds_ref, up_ref, down_ref,
    output_ref, midg_ref, row_grad, shared_grad, outg_ref, gaing_ref, packed_ref, far_ref,
    att_other, second, turned, grad, cot_in, hidden_all, pre_all, forward, backward, middle, up, down,
    results, parts_out, parts_in, heads_out, cols_out, cols_in, stage, far_in,
    sent, got, load_sem, write_sem, local_sem,
):
    chip, core, zp, zq = here()
    sems = (sent, got)
    partner = (chip, 1 - core, zp, zq)
    keep = (chip, zp, core, zq)
    cross = (chip, zp, core, 1 - zq)
    moves = core != zp
    near_x = (chip ^ 1, core, zp, zq)
    near_y = (chip ^ 2, core, zp, zq)
    tokens, model = midg_ref.shape
    part = tokens // 3
    half = 2 * part
    width = out_ref.shape[1]
    units = up.shape[1]
    tile = units // 4
    other = 1 - core
    mine, theirs = pl.ds(0, tokens), pl.ds(tokens, tokens)
    own_down = down.at[rows_at(chip * tile, tile)] if square else down
    loads = [
        pltpu.make_async_copy(up_ref, up, load_sem.at[0]),
        pltpu.make_async_copy(down_ref, own_down, load_sem.at[1]),
    ]
    for copy in loads:
        copy.start()
    greet([partner, cross] + ([near_x, near_y] if square else []), keep, moves)
    att_sends = [
        remote(out_ref.at[rows_at(other * half, half)], att_other.at[pl.ds(0, half)], sems, 0, partner),
        remote(shared_ref.at[rows_at(other * part, part)], att_other.at[pl.ds(half, part)], sems, 1, partner),
    ]
    for copy in att_sends:
        copy.start()
    cot_move = Moves(
        [remote(cot_ref.at[2], cot_in.at[1], sems, 11, keep)],
        [pltpu.make_async_copy(cot_ref.at[2], cot_in.at[1], local_sem.at[0])],
        remote(cot_ref.at[1 - zq], cot_in.at[0], sems, 22, cross),
        moves,
    )
    cot_move.start()

    def down_half(index, which):
        return down.at[rows_at(index * tile + which * (tile // 2), tile // 2)]

    def send_down(index, which, at, device):
        copy = remote(down_half(index, which), down_half(index, which), sems, at, device)
        copy.start()
        return copy

    slot = lax.broadcasted_iota(jnp.int32, (part, 1), 0)
    filled, shared_filled = bounds_ref[0, 3:4, 0:1], bounds_ref[1, 3:4, 0:1]
    none = jnp.zeros((), BF16)

    def take_grad(values, at, start, limit, sem):
        rows = rows_at(at, part)
        grad[rows, :] = jnp.where(slot + start < limit, values, none)
        copy = remote(grad.at[rows], grad.at[rows_at(tokens + at, part)], sems, sem, partner)
        copy.start()
        return copy

    grad_sends = [take_grad(grad_ref[...], zq * part, (2 * core + zq) * part, filled, 2)]

    own_rows_of = lambda b: (
        out_ref[rows_at(core * half + b * part, part), :] if b < 2 else shared_ref[rows_at(core * part, part), :]
    )
    own_weight = outw_ref[rows_at(core * width, width), :]
    other_weight = outw_ref[rows_at(other * width, width), :]
    blocks = [pl.ds(b * part, part) for b in range(3)]
    for b in range(3):
        middle[blocks[b], :] = x[blocks[b], :].astype(F32) + jnp.dot(
            own_rows_of(b), own_weight, preferred_element_type=F32
        )
    for copy in loads:
        copy.wait()
    if square:
        down_sends = [
            send_down(chip, 0, 12, near_x), send_down(chip, 1, 13, near_y), send_down(chip, 0, 14, near_y),
            send_down(chip, 1, 15, near_x),
        ]
    for copy in att_sends:
        copy.wait_recv()
    for rows in blocks:
        value = middle[rows, :] + jnp.dot(att_other[rows, :], other_weight, preferred_element_type=F32)
        middle[rows, :] = value
        second[rows, :] = (norm_parts(value)[0] * gain_ref[...]).astype(BF16)
    second_send = remote(second.at[mine], second.at[theirs], sems, 3, partner)
    second_send.start()

    def hidden_forward(start):
        rows = pl.ds(start, tokens)

        def one_tile(i, _):
            here_units = pl.ds(pl.multiple_of(i * tile, 128), tile)
            hidden, slope = gelu_pair(jnp.dot(second[rows, :], up[:, here_units], preferred_element_type=F32))
            hidden_all[rows, here_units] = hidden.astype(BF16)
            pre_all[rows, here_units] = slope.astype(BF16)
            return 0

        lax.fori_loop(0, 4, one_tile, 0)

    def hidden_backward(start):
        rows = pl.ds(start, tokens)

        def one_tile(i, _):
            here_units = pl.ds(pl.multiple_of(i * tile, 128), tile)
            pre_grad = nt(grad[rows, :], down[rows_at(i * tile, tile), :]) * pre_all[rows, here_units].astype(F32)
            pre_all[rows, here_units] = pre_grad.astype(BF16)
            return 0

        lax.fori_loop(0, 4, one_tile, 0)

    hidden_forward(0)
    if square:
        down_sends[0].wait_recv()
        down_sends[1].wait_recv()
        down_sends += [send_down(chip ^ 1, 0, 16, near_y), send_down(chip ^ 2, 1, 17, near_x)]
    second_send.wait_recv()
    hidden_forward(tokens)
    if square:
        for copy in down_sends[2:]:
            copy.wait_recv()
    for b in range(3):
        rows, there = pl.ds(tokens + b * part, part), blocks[b]
        parts_out[0, there, :] = jnp.dot(hidden_all[rows, :], down[...], preferred_element_type=F32).astype(BF16)
    first_part = remote(parts_out.at[0], parts_in.at[0], sems, 4, partner)
    first_part.start()
    for rows in blocks:
        forward[rows, :] = middle[rows, :] + jnp.dot(hidden_all[rows, :], down[...], preferred_element_type=F32)
    turned[...] = second[...].T
    first_part.wait_recv()
    for rows in blocks:
        results[rows, :] = (forward[rows, :] + parts_in[0, rows, :].astype(F32)).astype(BF16)
    kept_rows, third_rows = results.at[rows_at(zq * part, part)], results.at[pl.ds(half, part)]
    output_moves = Moves(
        [
            remote(kept_rows, output_ref.at[zq], sems, 19, keep),
            remote(third_rows, output_ref.at[2], sems, 20, keep),
        ],
        [
            pltpu.make_async_copy(kept_rows, output_ref.at[zq], local_sem.at[1]),
            pltpu.make_async_copy(third_rows, output_ref.at[2], local_sem.at[2]),
        ],
        remote(results.at[rows_at((1 - zq) * part, part)], output_ref.at[zq], sems, 21, cross),
        moves,
    )
    output_moves.start()
    cot_move.wait()
    grad_sends.append(take_grad(cot_in[0], (1 - zq) * part, (2 * core + 1 - zq) * part, filled, 18))
    grad_sends.append(take_grad(cot_in[1], half, (2 * core + zq) * part, shared_filled, 23))
    hidden_backward(0)
    for copy in grad_sends:
        copy.wait_recv()
    hidden_backward(tokens)
    quarter = model // 4
    far_sends = [
        remote(stage.at[0, pl.ds(0, tile)], far_in.at[0], sems, 9, near_y),
        remote(stage.at[0, pl.ds(tile, tile)], far_in.at[1], sems, 10, near_x),
    ]

    def weight_grads(i, _):
        target = chip ^ (3 - i) if square else 3 - i
        place = jnp.where(i == 0, 0, 1 + i % 2)

        @pl.when(i == 3)
        def _():
            pltpu.make_async_copy(stage.at[place], packed_ref.at[target], write_sem.at[place]).wait()

        here_units = pl.ds(pl.multiple_of(target * tile, 128), tile)
        stage[place, pl.ds(0, tile), :] = tn(hidden_all[:, here_units], grad[...]).astype(BF16)
        values = jnp.dot(
            turned[rows_at(target * quarter, quarter), :], pre_all[...], preferred_element_type=F32
        ).astype(BF16)
        for j in range(2):
            stage[place, pl.ds(tile + j * quarter, quarter), :] = values[:, j * model : (j + 1) * model]
        pltpu.make_async_copy(stage.at[place], packed_ref.at[target], write_sem.at[place]).start()
        if square:

            @pl.when(i == 0)
            def _():
                for copy in far_sends:
                    copy.start()

        return 0

    lax.fori_loop(0, 4, weight_grads, 0)

    for b in range(3):
        rows, there = pl.ds(tokens + b * part, part), blocks[b]
        parts_out[1, there, :] = nt(pre_all[rows, :], up[...]).astype(BF16)
    second_part = remote(parts_out.at[1], parts_in.at[1], sems, 5, partner)
    second_part.start()
    for rows in blocks:
        backward[rows, :] = nt(pre_all[rows, :], up[...])
    second_send.wait_send()
    second_part.wait_recv()
    gain_sum = jnp.zeros(gaing_ref.shape, F32)
    for rows in blocks:
        n, r = norm_parts(middle[rows, :])
        upstream = backward[rows, :] + parts_in[1, rows, :].astype(F32)
        more, gain_more = norm_back(upstream, n, r, gain_ref[...])
        gain_sum = gain_sum + gain_more
        value = grad[rows, :].astype(F32) + more
        midg_ref[rows, :] = value
        branch = value.astype(BF16)
        second[rows, :] = branch
        heads_out[rows, :] = nt(branch, other_weight).astype(BF16)
    gaing_ref[...] = gain_sum
    head_sends = [
        remote(heads_out.at[pl.ds(0, half)], row_grad.at[rows_at(core * half, half)], sems, 6, partner),
        remote(heads_out.at[pl.ds(half, part)], shared_grad.at[rows_at(core * part, part)], sems, 7, partner),
    ]
    for copy in head_sends:
        copy.start()
    branch = second[mine, :]
    forward[rows_at(core * width, width), :] = tn(
        out_ref[rows_at(core * half, half), :], second[pl.ds(0, half), :]
    ) + tn(shared_ref[rows_at(core * part, part), :], second[pl.ds(half, part), :])
    forward[rows_at(other * width, width), :] = tn(att_other[...], branch)
    lanes = lambda side: pl.ds(pl.multiple_of(side * width, 128), width)
    cols_out[...] = forward[pl.ds(0, model), lanes(other)].astype(BF16)
    cols_send = remote(cols_out, cols_in, sems, 8, partner)
    cols_send.start()
    for b in range(3):
        value = nt(second[blocks[b], :], own_weight).astype(BF16)
        if b < 2:
            row_grad[rows_at(core * half + b * part, part), :] = value
        else:
            shared_grad[rows_at(core * part, part), :] = value
    cols_send.wait_recv()
    outg_ref[...] = (forward[pl.ds(0, model), lanes(core)] + cols_in[...].astype(F32)).astype(BF16)
    for copy in head_sends:
        copy.wait_recv()
    for copy in att_sends + head_sends + grad_sends + [first_part, second_part, cols_send]:
        copy.wait_send()
    if square:
        for copy in down_sends:
            copy.wait_send()
        for copy in far_sends:
            copy.wait()
    far_write = pltpu.make_async_copy(far_in, far_ref, load_sem.at[0])
    far_write.start()
    for place in range(3):
        pltpu.make_async_copy(stage.at[place], packed_ref.at[0], write_sem.at[place]).wait()
    output_moves.wait()
    far_write.wait()


def dense(square, out, shared_out, x, grad, cotangent, out_matrix, gain, bounds, up, down):
    model = x.shape[1]
    tokens = x.shape[0]
    part = tokens // 3
    length, width = out.shape
    units = up.shape[1]
    tile = units // 4
    anywhere = pl.BlockSpec(memory_space=pl.ANY)
    near = pl.BlockSpec(memory_space=pltpu.VMEM)
    both = 2 * tokens
    low = lambda *shape: pltpu.VMEM(shape, BF16)
    wide = lambda *shape: pltpu.VMEM(shape, F32)
    return pl.pallas_call(
        functools.partial(dense_kernel, square),
        in_specs=[near] * 4 + [anywhere] + [near] * 3 + [anywhere] * 2,
        out_specs=[anywhere] + [near] * 5 + [anywhere, anywhere],
        out_shape=[
            jax.ShapeDtypeStruct((3, part, model), BF16),
            jax.ShapeDtypeStruct((tokens, model), F32),
            jax.ShapeDtypeStruct((length, width), BF16),
            jax.ShapeDtypeStruct((length // 2, width), BF16),
            jax.ShapeDtypeStruct((model, width), BF16),
            jax.ShapeDtypeStruct((1, model), F32),
            jax.ShapeDtypeStruct((4, 2 * tile, model), BF16),
            jax.ShapeDtypeStruct((2, tile, model), BF16),
        ],
        scratch_shapes=[
            low(tokens, width), low(both, model), low(model, both), low(both, model), low(2, part, model),
            low(both, units), low(both, units), wide(tokens, model), wide(tokens, model), wide(tokens, model),
            low(model, units), low(units, model), low(tokens, model), low(2, tokens, model), low(2, tokens, model),
            low(tokens, width), low(model, width), low(model, width), low(3, 2 * tile, model), low(2, tile, model),
            pltpu.SemaphoreType.DMA((24,)),
            pltpu.SemaphoreType.DMA((24,)),
            pltpu.SemaphoreType.DMA((2,)),
            pltpu.SemaphoreType.DMA((3,)),
            pltpu.SemaphoreType.DMA((3,)),
        ],
        compiler_params=pltpu.CompilerParams(
            collective_id=1, has_side_effects=True, vmem_limit_bytes=63 * 1024 * 1024
        ),
        name="dense",
    )(out, shared_out, x, grad, cotangent, out_matrix, gain, bounds, up, down)


def add(*terms):
    total = terms[0].astype(F32)
    for term in terms[1:]:
        total = total + term.astype(F32)
    return total


def backward_kernel(square, pics, *refs):
    refs = list(refs)
    take = lambda count: [refs.pop(0) for _ in range(count)]
    names = ("aug", "qk", "v", "out", "do", "raw", "normed")
    row_in = dict(zip(names, take(7)))
    shared_in = dict(zip(names, take(7)))
    mix_in, x_in, midg_in, gain_first, gain_qk, gain_second_grad, bounds_ref = take(7)
    if square:
        packed_in, far_ref, outg_in = take(3)
        grad_out, total_ref, gains_ref, up_ref, down_ref, outw_ref = take(6)
    else:
        grad_own, mix_grad_ref, gains_sum = take(3)
    names = names[:-1]
    row = dict(zip(names, take(6)))
    shared = dict(zip(names, take(6)))
    normed, weight, x, midg = take(4)
    kaug, vaug, doaug, qsum, ksum, mixed, part_k, part_v, got_k, got_v = take(10)
    gain_sums, parts_out, parts_in = take(3)
    if square:
        grad_own, payload, gains_sum, outg = take(4)
        held, far_in, onward_out, onward_in, direct_in, line, whole_line, line_right, line_left = take(9)
        up_out, up_got = take(2)
        relay, final, core_got, chunks, chunk_whole, chunk_right, chunk_left, gain_parts, gain_got = take(9)
    sent, got, load_sem, local_sem = take(4)

    chip, core, zp, zq = here()
    z = 2 * zp + zq
    sems = (sent, got)
    partner = (chip, 1 - core, zp, zq)
    keep = (chip, zp, core, zq)
    cross = (chip, zp, core, 1 - zq)
    moves = core != zp
    near_x = (chip ^ 1, core, zp, zq)
    near_y = (chip ^ 2, core, zp, zq)
    along = [(chip, core, zp, 1 - zq), (chip, core, 1 - zp, zq), (chip, core, 1 - zp, 1 - zq)]
    tokens, model = x.shape
    part = tokens // 3
    half, length = 2 * part, 4 * part
    width = model // 2
    queries = half
    waits = []

    def load(source, target, at):
        copy = pltpu.make_async_copy(source, target, load_sem.at[at])
        copy.start()
        return copy

    def send(source, target, at, device):
        copy = remote(source, target, sems, at, device)
        copy.start()
        waits.append(copy)
        return copy

    if square:
        rows_count = packed_in.shape[1]
        span = rows_count // 2
        first_half, second_half = pl.ds(0, span), pl.ds(span, span)
        held_loads = [
            load(packed_in.at[chip ^ 1, first_half], held.at[0], 24),
            load(packed_in.at[chip ^ 2, second_half], held.at[1], 25),
            load(packed_in.at[chip, first_half], held.at[2], 26),
            load(packed_in.at[chip, second_half], held.at[3], 27),
        ]
        far_loads = [load(far_ref.at[i], far_in.at[i], 28 + i) for i in range(2)]
    keys_of = lambda ref: ref.at[:, pl.ds(width, width)]
    load_bufs = lambda source, target, at: [
        load(keys_of(source[name]) if name == "qk" else source[name], target[name], at + i)
        for i, name in enumerate(names)
    ]
    shared_loads = load_bufs(shared_in, shared, 0)
    row_loads = load_bufs(row_in, row, 6)
    late_loads = [
        load(row_in["normed"], normed.at[pl.ds(0, length)], 12),
        load(shared_in["normed"].at[rows_at(zq * part, part)], normed.at[pl.ds(length, part)], 13),
        load(
            shared_in["normed"].at[rows_at((2 + zq) * part, part)], normed.at[pl.ds(length + part, part)], 14
        ),
        load(mix_in, weight, 15),
        load(x_in, x, 16),
        load(midg_in, midg, 17),
    ]
    if square:
        late_loads.append(load(outg_in, outg, 18))
    if square:
        greet([partner, cross, near_x, near_y] + along, keep, moves)
        bulk_x = send(packed_in.at[chip ^ 1, second_half], direct_in.at[0], 2, near_x)
        bulk_y = send(packed_in.at[chip ^ 2, first_half], direct_in.at[1], 3, near_y)
        for copy in held_loads + far_loads:
            copy.wait()
        onward_out[0] = add(far_in[0], held[0]).astype(BF16)
        bulk_on_x = send(onward_out.at[0], onward_in.at[0], 11, near_x)
        onward_out[1] = add(far_in[1], held[1]).astype(BF16)
        bulk_on_y = send(onward_out.at[1], onward_in.at[1], 12, near_y)

        bulk_line = Line(line, whole_line, line_right, line_left, sems, 14)
        mix_line = Line(chunks, chunk_whole, chunk_right, chunk_left, sems, 26)
    else:
        greet([partner, along[0]])

    gain_sums[...] = jnp.zeros_like(gain_sums)

    def attend_back(bufs, bounds, count, q_lanes_to, k_to, v_to, at, between=None):
        def one(p, _):
            if between is not None:
                pl.when(p == 2)(between)
            lanes = pl.ds(pl.multiple_of(p * 128, 128), 128)
            key_lanes = pl.ds(pl.multiple_of(width + p * 128, 128), 128)
            attend_back_kernel(
                pics, bufs["aug"].at[pl.ds(2 * p, 2)], bufs["qk"].at[:, lanes], bufs["v"].at[:, lanes],
                bufs["out"].at[:, lanes], bufs["do"].at[:, lanes], bufs["raw"].at[:, lanes],
                bufs["raw"].at[:, key_lanes], gain_qk.at[:, lanes], gain_qk.at[:, key_lanes], bounds,
                q_lanes_to(p), k_to(p), v_to(p), gain_sums.at[pl.ds(at, 1), lanes], gain_sums.at[pl.ds(at + 1, 1), lanes],
                kaug, vaug, doaug.at[:, pl.ds(0, count)], qsum.at[:, pl.ds(0, count)], ksum,
            )
            return 0

        lax.fori_loop(0, width // 128, one, 0)

    def mixed_at(start, count, side):
        return lambda p: mixed.at[pl.ds(start, count), pl.ds(pl.multiple_of(side * width + p * 128, 128), 128)]

    whole_lanes = lambda ref: lambda p: ref.at[:, pl.ds(pl.multiple_of(p * 128, 128), 128)]
    for copy in shared_loads:
        copy.wait()
    attend_back(
        shared, bounds_ref.at[1], queries, mixed_at(length, queries, 0), whole_lanes(part_k), whole_lanes(part_v), 0
    )
    side_sends = []
    for i in range(2):
        theirs = rows_at((2 * i + 1 - zq) * part, part)
        there = pl.ds(i * part, part)
        side_sends.append(send(part_k.at[theirs], got_k.at[there], 7 + 2 * i, along[0]))
        side_sends.append(send(part_v.at[theirs], got_v.at[there], 8 + 2 * i, along[0]))
    for copy in row_loads:
        copy.wait()
    def start_line():
        for copy in (bulk_y, bulk_on_x, bulk_x, bulk_on_y):
            copy.wait_recv()
        first_sum = add(held[2], onward_in[0], direct_in[1]).astype(BF16)
        second_half_sum = add(held[3], onward_in[1], direct_in[0]).astype(BF16)
        for i in range(2):
            line[i] = first_sum[i * quarter_rows : (i + 1) * quarter_rows]
            line[2 + i] = second_half_sum[i * quarter_rows : (i + 1) * quarter_rows]
        bulk_line.start()

    if square:
        quarter_rows = rows_count // 4
    attend_back(
        row, bounds_ref.at[0], length, mixed_at(0, length, 0), mixed_at(0, length, 1), mixed_at(0, length, 2), 2,
        start_line if square else None,
    )

    if square:
        bulk_line.first()
    for copy in side_sends:
        copy.wait_recv()

    def shared_pair(p, _):
        lanes = pl.ds(pl.multiple_of(p * 128, 128), 128)
        key_lanes = pl.ds(pl.multiple_of(width + p * 128, 128), 128)
        shared_keys_kernel(
            part_k.at[:, lanes], part_v.at[:, lanes], got_k.at[:, lanes], got_v.at[:, lanes],
            shared["raw"].at[:, key_lanes], gain_qk.at[:, key_lanes], mixed_at(length, queries, 1)(p),
            mixed_at(length, queries, 2)(p), gain_sums.at[pl.ds(4, 1), lanes],
        )
        return 0

    lax.fori_loop(0, width // 128, shared_pair, 0)
    for copy in late_loads:
        copy.wait()
    other = 1 - core
    block_rows = lambda side, b: (
        rows_at(side * half + b * part, part) if b < 2 else rows_at(length + side * part, part)
    )
    for b in range(3):
        parts_out[pl.ds(b * part, part), :] = nt(mixed[block_rows(other, b), :], weight[...]).astype(BF16)
    part_send = send(parts_out, parts_in, 13, partner)
    if square:
        bulk_line.second()
    shard = model // 8
    if square:
        for i in range(3):
            lanes = slice(i * width, (i + 1) * width)
            value = tn(normed[...], mixed[:, lanes]).astype(BF16)
            for p in range(8):
                payload[p, :shard, lanes] = value[p * shard : (p + 1) * shard]
        bulk_line.third()
    else:
        for i in range(3):
            lanes = slice(i * width, (i + 1) * width)
            mix_grad_ref[:, lanes] = tn(normed[...], mixed[:, lanes]).astype(BF16)
    part_send.wait_recv()
    first_sum_gain = jnp.zeros((1, model), F32)
    for b in range(3):
        rows = pl.ds(b * part, part)
        upstream = nt(mixed[block_rows(core, b), :], weight[...]) + parts_in[rows, :].astype(F32)
        n, r = norm_parts(x[rows, :].astype(F32))
        value, more = norm_back(upstream, n, r, gain_first[...])
        first_sum_gain = first_sum_gain + more
        grad_own[rows, :] = (midg[rows, :] + value).astype(BF16)
    gains_sum[...] = jnp.zeros_like(gains_sum)
    gains_sum[0:1, :] = first_sum_gain
    mine_lanes = pl.ds(pl.multiple_of(core * width, 128), width)
    gains_sum[1:2, mine_lanes] = gain_sums[0:1, :] + gain_sums[2:3, :]
    gains_sum[2:3, mine_lanes] = gain_sums[3:4, :] + gain_sums[4:5, :]
    gains_sum[3:4, :] = gain_second_grad[...]

    if square:
        kept_rows, third_rows = grad_own.at[rows_at(zq * part, part)], grad_own.at[pl.ds(half, part)]
        grad_moves = Moves(
            [
                remote(kept_rows, grad_out.at[zq], sems, 0, keep),
                remote(third_rows, grad_out.at[2], sems, 1, keep),
            ],
            [
                pltpu.make_async_copy(kept_rows, grad_out.at[zq], local_sem.at[0]),
                pltpu.make_async_copy(third_rows, grad_out.at[2], local_sem.at[1]),
            ],
            remote(grad_own.at[rows_at((1 - zq) * part, part)], grad_out.at[zq], sems, 4, cross),
            moves,
        )
        grad_moves.start()
        gain_row = shard + shard // 3
        for p in range(8):
            payload[p, gain_row:, :] = jnp.zeros((16, 3 * width), BF16)
            payload[p, gain_row:, :shard] = gains_sum[:, p * shard : (p + 1) * shard].astype(BF16)
            for i in range(3):
                at = p * shard + i * (shard // 3)
                payload[p, shard:gain_row, i * width : (i + 1) * width] = outg[at : at + shard // 3, :]
        mine, theirs = 2 * chip + core, 2 * chip + 1 - core
        x_mine, x_other = 2 * (chip ^ 1) + core, 2 * (chip ^ 1) + 1 - core
        y_mine, y_other = 2 * (chip ^ 2) + core, 2 * (chip ^ 2) + 1 - core
        far_mine, far_other = 2 * (chip ^ 3) + core, 2 * (chip ^ 3) + 1 - core
        first = send(payload.at[far_mine], relay.at[0], 38, near_y)
        second = send(payload.at[far_other], relay.at[1], 39, near_x)
        direct_x = send(payload.at[x_other], final.at[0], 40, near_x)
        direct_y = send(payload.at[y_mine], final.at[1], 41, near_y)

        first.wait_recv()
        relay[2] = add(relay[0], payload[x_mine]).astype(BF16)
        onward_x = send(relay.at[2], final.at[2], 42, near_x)
        second.wait_recv()
        relay[3] = add(relay[1], payload[y_other]).astype(BF16)
        onward_y = send(relay.at[3], final.at[3], 43, near_y)
        bulk_line.fourth()
        direct_x.wait_recv()
        onward_y.wait_recv()
        relay[4] = add(payload[theirs], final[0], final[3]).astype(BF16)
        to_core = send(relay.at[4], core_got, 44, partner)
        direct_y.wait_recv()
        onward_x.wait_recv()
        kept = add(payload[mine], final[1], final[2])
        quarter = gain_row // 2
        for i in range(2):
            chunks[2 * core + i] = kept[i * quarter : (i + 1) * quarter].astype(BF16)
        to_core.wait_recv()
        for i in range(2):
            chunks[2 * (1 - core) + i] = core_got[i * quarter : (i + 1) * quarter]
        gain_parts[0] = (kept[gain_row:] + core_got[gain_row:].astype(F32)).astype(BF16)
        mix_line.start()
        gain_lanes = pl.ds(0, 128)
        gain_sends = [
            send(gain_parts.at[0, :, gain_lanes], gain_got.at[i, :, gain_lanes], 45 + i, along[i]) for i in range(3)
        ]
        bulk_line.fifth()
        mix_line.first()
        mix_line.second()
        mix_line.third()
        for copy in gain_sends:
            copy.wait_recv()
        gains_ref[...] = add(
            gain_parts[0, :, :128], gain_got[0, :, :128], gain_got[1, :, :128], gain_got[2, :, :128]
        )
        mix_line.fourth()
        bulk_line.sixth()

        def place(index, values):
            side, up = index // 2, index % 2
            lanes_of = lambda p: slice((2 * p + side) * width, (2 * p + side + 1) * width)
            below = shard - quarter
            for p in range(3):
                part_of = values[:, p * width : (p + 1) * width]
                if up == 0:
                    total_ref[0:quarter, lanes_of(p)] = part_of
                else:
                    total_ref[quarter:shard, lanes_of(p)] = part_of[:below]
                    rows = slice(p * (shard // 3), (p + 1) * (shard // 3))
                    outw_ref[rows, side * width : (side + 1) * width] = part_of[below:]

        flat = jnp.concatenate([whole_line[i] for i in range(4)], axis=0)
        tile = down_ref.shape[0]
        ups = [flat[tile + 2 * shard * i : tile + 2 * shard * (i + 1)] for i in range(2)]
        for i in range(2):
            up_out[i] = jnp.where(core == 0, ups[i][shard:], ups[i][:shard])
        up_send = send(up_out, up_got, 48, partner)
        mix_line.fifth()
        down_ref[...] = flat[:tile]

        def place_up(side, i, values):
            for j in range(2):
                lanes = pl.ds(pl.multiple_of((2 * (2 * i + j) + side) * tile, 128), tile)
                up_ref[:, lanes] = values[:, j * tile : (j + 1) * tile]

        for i in range(2):
            place_up(core, i, jnp.where(core == 0, ups[i][:shard], ups[i][shard:]))
        up_send.wait_recv()
        for i in range(2):
            place_up(other, i, up_got[i])
        mix_line.sixth()
        for i in range(4):
            place(i, chunk_whole[i])
        bulk_line.wait_sends()
        mix_line.wait_sends()
        grad_moves.wait()
    for copy in waits:
        copy.wait_send()


def backward_pass(square, pics, row, shared, weights, gains, bounds, *more):
    length, model = row[1].shape
    width = model // 2
    part = length // 4
    half, tokens = 2 * part, 3 * part
    shard = model // 8
    near = pl.BlockSpec(memory_space=pltpu.VMEM)
    anywhere = pl.BlockSpec(memory_space=pl.ANY)
    low = lambda *shape: (shape, BF16)
    wide = lambda *shape: (shape, F32)
    if square:
        rows = more[0].shape[1]
        tile = rows // 2
        outs = [
            (low(3, part, model), anywhere),
            (low(shard, 6 * width), near),
            (wide(16, 128), near),
            (low(shard, 8 * tile), near),
            (low(tile, model), near),
            (low(shard, model), near),
        ]
    else:
        outs = [(low(tokens, model), near), (low(model, 3 * width), near), (wide(16, model), near)]
    scratch = []
    for queries in (length, half):
        scratch += [
            low(2 * (width // 128), queries, 128), low(length, width), low(length, width), low(queries, width),
            low(queries, width), low(length, 2 * width),
        ]
    scratch += [
        low(length + half, model), low(model, 3 * width), low(tokens, model), wide(tokens, model),
        low(2, length, 128), low(2, length, 128), low(2, length, 128), wide(2, length, 128), wide(length, 128),
        low(length + half, 3 * width), low(length, width), low(length, width), low(half, width), low(half, width),
        wide(8, width), low(tokens, model), low(tokens, model),
    ]
    if square:
        span = rows // 2
        pieces = shard + shard // 3 + 16
        chunk = (pieces - 16) // 2
        scratch += [
            low(tokens, model), low(8, pieces, 3 * width), wide(16, model), low(model, width),
            low(4, span, model), low(2, span, model), low(2, span, model), low(2, span, model), low(2, span, model),
            low(4, rows // 4, model), low(4, rows // 4, model), low(3, rows // 4, model), low(3, rows // 4, model),
            low(2, shard, model), low(2, shard, model),
            low(5, pieces, 3 * width), low(4, pieces, 3 * width), low(pieces, 3 * width), low(4, chunk, 3 * width),
            low(4, chunk, 3 * width), low(3, chunk, 3 * width), low(3, chunk, 3 * width), low(1, 16, 3 * width),
            low(3, 16, 3 * width),
        ]
    return pl.pallas_call(
        functools.partial(backward_kernel, square, pics),
        in_specs=[anywhere] * 17 + [near] * 4 + [anywhere] * len(more),
        out_specs=[spec for _, spec in outs],
        out_shape=[jax.ShapeDtypeStruct(*shape) for shape, _ in outs],
        scratch_shapes=[pltpu.VMEM(*shape) for shape in scratch]
        + [
            pltpu.SemaphoreType.DMA((49,)),
            pltpu.SemaphoreType.DMA((49,)),
            pltpu.SemaphoreType.DMA((30,)),
            pltpu.SemaphoreType.DMA((2,)),
        ],
        compiler_params=pltpu.CompilerParams(
            collective_id=2, has_side_effects=True, vmem_limit_bytes=62 * 1024 * 1024
        ),
        name="backward_pass",
    )(*row, *shared, *weights, *gains, bounds, *more)


def local(
    tokens, lengths, pictures, first_gain, mix_weight, query_gain, key_gain, out_weight,
    second_gain, up_weight, down_weight, cotangent,
):
    chip, core, zp, zq = here()
    chips = lax.axis_size("chip")
    square = chips == 4
    rows = ("chip", "core")
    _, part, model = tokens.shape
    length = 4 * part
    half = 2 * part
    width = HEADS // 2 * HEAD
    pics = lengths.shape[1]
    shard = mix_weight.shape[0]

    hidden = up_weight.shape[1]
    tile = hidden // 8
    gains = [gain[None] for gain in (first_gain, query_gain, key_gain, second_gain)]
    if square:
        forward = forward_pass(
            True, pics, tokens, cotangent, lengths, mix_weight, *gains, up_weight, out_weight
        )
        up_half, out_matrix = forward[19:]
        down_half = down_weight
        gain_second = forward[5]
    else:
        gather = lambda weight: lax.all_gather(weight, rows, axis=0, tiled=True)
        half_of = lambda weight, axis: pick(weight, core, axis)
        mix_half = half_of(gather(mix_weight).reshape(model, 3, 2, width), 2).reshape(model, 3 * width)
        up_half = half_of(gather(up_weight).reshape(model, 4, 2, tile), 2).reshape(model, 4 * tile)
        down_half = half_of(gather(down_weight).reshape(4, 2, tile, model), 1).reshape(4 * tile, model)
        out_matrix = gather(out_weight)
        gains = lax.all_gather(jnp.concatenate(gains), rows, axis=0, tiled=False)
        gains = gains.transpose(1, 0, 2).reshape(4, 1, model).astype(F32)
        gain_second = gains[3]
        gain_qk = half_of(gains[1:3].reshape(2, 2, width), 1).reshape(1, model)
        forward = forward_pass(False, pics, tokens, cotangent, lengths, mix_half, gains[0], gain_qk)
    own_tokens, bounds, mix_half, grad_tokens, gain_first, _, gain_qk = forward[:7]
    normed, qk, v, raw, out, aug = forward[7:13]
    shared_normed, shared_qk, shared_v, shared_raw, shared_out, shared_aug = forward[13:19]

    def collect(mine, cross, third):
        mine = lax.ppermute(mine, COLUMN, KEEP)
        cross = lax.ppermute(cross, COLUMN, CROSS)
        third = lax.ppermute(third, COLUMN, KEEP)
        return jnp.stack([jnp.where(zq == 0, mine, cross), jnp.where(zq == 0, cross, mine), third])

    output, middle_grad, grad, shared_grad, out_grad, second_gain_grad, packed, far = dense(
        square, out, shared_out, own_tokens, grad_tokens, cotangent, out_matrix, gain_second, bounds,
        up_half, down_half,
    )
    row_side = (aug, qk, v, out, grad, raw, normed)
    shared_side = (shared_aug, shared_qk, shared_v, shared_out, shared_grad, shared_raw, shared_normed)
    weights = (mix_half, own_tokens, middle_grad)
    gains = (gain_first, gain_qk, second_gain_grad)
    if square:
        input_out, mix_out, gains_out, up_out, down_out, outw_out = backward_pass(
            True, pics, row_side, shared_side, weights, gains, bounds, packed, far, out_grad
        )
        gains_out = gains_out[:4, :shard]
        mix_out, up_out, down_out, outw_out = (
            array.astype(F32) for array in (mix_out, up_out, down_out, outw_out)
        )
    else:
        input_grad, mix_grad, gain_grads = backward_pass(
            False, pics, row_side, shared_side, weights, gains, bounds
        )

        def reduce(grad):
            return lax.psum(lax.psum_scatter(grad, rows, scatter_dimension=0, tiled=True), SEQ).astype(F32)

        first, second = input_grad[:part], input_grad[part:half]
        input_out = collect(
            jnp.where(zq == 0, first, second), jnp.where(zq == 0, second, first), input_grad[half:]
        )
        own_core = jnp.arange(2) == core
        eighth = model // 8
        down_grad = packed[:, None, :tile]
        down_out = reduce(jnp.where(own_core[None, :, None, None], down_grad, 0).reshape(hidden, model))
        up_grad = packed[:, tile : 2 * tile].reshape(4, 2, 2 * eighth, 2, tile).transpose(0, 2, 1, 3, 4)
        up_grad = up_grad.reshape(model, 4, 1, tile)
        up_out = reduce(jnp.where(own_core[None, None, :, None], up_grad, 0).reshape(model, hidden))
        out_grad = out_grad.reshape(model, 1, width)
        outw_out = reduce(jnp.where(own_core[None, :, None], out_grad, 0).reshape(model, model))
        mix_out = reduce(
            jnp.where(own_core[None, None, :, None], mix_grad.reshape(model, 3, 1, width), 0).reshape(model, 6 * width)
        )
        gain_grads = gain_grads[:4].reshape(4, 2 * chips, shard).transpose(1, 0, 2).astype(BF16)
        gains_out = reduce(gain_grads).reshape(4, shard)
    return (
        output, input_out, gains_out[0], mix_out, gains_out[1], gains_out[2], outw_out, gains_out[3],
        up_out, down_out,
    )


def solution(mesh):
    fsdp = mesh.shape["fsdp"]
    split = Mesh(mesh.devices.reshape(fsdp // 2, 2, 2, 2), ("chip", "core", "zp", "zq"))
    rows = ("chip", "core")
    return jax.shard_map(
        local,
        mesh=split,
        in_specs=(
            P(rows, SEQ, None),
            P(rows, None),
            P(rows, SEQ),
            P(rows),
            P(rows, None),
            P(rows),
            P(rows),
            P(rows, None),
            P(rows),
            P(rows, None),
            P(rows, None),
            P(rows, SEQ, None),
        ),
        out_specs=(
            P(rows, SEQ, None),
            P(rows, SEQ, None),
            P(rows),
            P(rows, None),
            P(rows),
            P(rows),
            P(rows, None),
            P(rows),
            P(rows, None),
            P(rows, None),
        ),
        check_vma=False,
    )
```

```python
import functools

import jax
import jax.numpy as jnp
from jax import lax
from jax.experimental import pallas as pl
from jax.experimental.pallas import tpu as pltpu
from jax.sharding import Mesh, PartitionSpec as P

HEADS = 12
HEAD = 64
EPSILON = 1e-06
BLOCK = 256
STEP = 512
MARK = 32.0
EXP2_FACTOR = HEAD**-0.5 * 1.4426950408889634
F32 = jnp.float32
BF16 = jnp.bfloat16
VMEM_LIMIT = 56 * 1024 * 1024

SEQ = ("zp", "zq")
COLUMN = ("core", "zp", "zq")
KEEP = [
    (core * 4 + z, (z // 2) * 4 + 2 * core + z % 2) for core in range(2) for z in range(4)
]
CROSS = [
    (core * 4 + z, (z // 2) * 4 + 2 * core + 1 - z % 2) for core in range(2) for z in range(4)
]


def swap(array, name, bit=1):
    count = lax.axis_size(name)
    return lax.ppermute(array, name, [(i, i ^ bit) for i in range(count)])


def pick(array, index, axis=0):
    return lax.dynamic_index_in_dim(array, index, axis, keepdims=False)


def group_ones(scale, size=128):
    row = lax.broadcasted_iota(jnp.int32, (size, size), 0) // HEAD
    column = lax.broadcasted_iota(jnp.int32, (size, size), 1) // HEAD
    return jnp.where(row == column, scale, 0.0).astype(BF16)


def group_sum(values, ones):
    return jnp.dot(values.astype(BF16), ones, preferred_element_type=F32)


def group_sum_fine(values, ones):
    high = values.astype(BF16)
    return group_sum(high, ones) + group_sum(values - high.astype(F32), ones)


def project_kernel(x_ref, gain_ref, weight_ref, qkg_ref, normed_ref, qk_ref, v_ref, raw_ref):
    both = qk_ref.shape[1]
    x = x_ref[...].astype(F32)
    center = x - jnp.mean(x, axis=-1, keepdims=True)
    spread = jnp.mean(center * center, axis=-1, keepdims=True)
    normed = (center * lax.rsqrt(spread + EPSILON) * gain_ref[...]).astype(BF16)
    normed_ref[...] = normed
    ones = group_ones(1.0 / HEAD, 256)
    for at in range(0, both, 256):
        lanes = slice(at, at + 256)
        raw = jnp.dot(normed, weight_ref[:, lanes], preferred_element_type=F32)
        raw_ref[:, lanes] = raw.astype(BF16)
        c = raw - group_sum(raw, ones)
        n = c * lax.rsqrt(group_sum(c * c, ones) + EPSILON)
        qk_ref[:, lanes] = (n * qkg_ref[:, lanes]).astype(BF16)
    v_ref[...] = jnp.dot(normed, weight_ref[:, both:], preferred_element_type=F32).astype(BF16)


def nt(a, b):
    return lax.dot_general(a, b, (((1,), (1,)), ((), ())), preferred_element_type=F32)


def tn(a, b):
    return lax.dot_general(a, b, (((0,), (0,)), ((), ())), preferred_element_type=F32)


def slots(queries, length, part):
    at = lax.broadcasted_iota(jnp.int32, (queries, 128), 0)
    if queries == length:
        return at
    return at % part + part * (lax.axis_index("zq") + 2 * (at // part))


def own_rows(ref, start, count, queries, part):
    if queries == ref.shape[0]:
        return ref[pl.ds(start, count), :]
    zq = lax.axis_index("zq")
    pieces = [
        ref[pl.ds(pl.multiple_of((zq + 2 * i) * part, part), part), :]
        for i in range(start // part, (start + count) // part)
    ]
    return jnp.concatenate(pieces, axis=0)


def query_marks(bounds_ref, place, queries, length, part, pics):
    at = slots(queries, length, part)
    inside = (at >= bounds_ref[0:1, :]) & (at < bounds_ref[2:3, :])
    values = jnp.where(inside, MARK, 0.0)
    return jnp.where(place == pics, MARK, values).astype(BF16)


def key_marks(bounds_ref, place, length, pics):
    at = lax.broadcasted_iota(jnp.int32, (length, 128), 0)
    inside = (at >= bounds_ref[0:1, :]) & (at < bounds_ref[1:2, :])
    values = jnp.where(inside, MARK, 0.0)
    values = jnp.where(place == pics, -MARK, values)
    return jnp.where((place > pics) & (place < pics + 4), 1.0, values).astype(BF16)


def attend_kernel(pics, q_ref, k_ref, v_ref, bounds_ref, out_ref, aug_ref, kaug, vaug, qaug):
    length = k_ref.shape[0]
    queries = out_ref.shape[0]
    part = length // 4
    lane = lax.broadcasted_iota(jnp.int32, (1, 128), 1)
    place = lane % HEAD
    sides = [lane < HEAD, lane >= HEAD]
    kmarks = key_marks(bounds_ref, place, length, pics)
    qmarks = query_marks(bounds_ref, place, queries, length, part, pics)
    qaug[...] = qmarks
    for h in range(2):
        kaug[h] = jnp.where(sides[h], k_ref[...], kmarks)
        vaug[h] = jnp.where(sides[h], v_ref[...], jnp.ones_like(v_ref))
    for b in range(queries // STEP):
        rows = pl.ds(b * STEP, STEP)
        mine = own_rows(q_ref, b * STEP, STEP, queries, part)
        query = [jnp.where(sides[h], mine, qaug[rows, :]) for h in range(2)]
        total = [jnp.zeros((STEP, 128), F32)] * 2
        for j in range(length // STEP):
            keys = pl.ds(j * STEP, STEP)
            scores = [nt(query[h], kaug[h, keys, :]) for h in range(2)]
            weights = [jnp.exp2(x * EXP2_FACTOR).astype(BF16) for x in scores]
            total = [
                total[h] + jnp.dot(weights[h], vaug[h, keys, :], preferred_element_type=F32) for h in range(2)
            ]
        results = []
        for h in range(2):
            results.append(total[h] / pltpu.roll(total[h], HEAD, 1))
            log_total = jnp.log(jnp.where(sides[h], 1.0, total[h])) * -(HEAD**0.5)
            first = log_total.astype(BF16)
            rest = log_total - first.astype(F32)
            middle = rest.astype(BF16)
            last = (rest - middle.astype(F32)).astype(BF16)
            logs = jnp.where(place == pics + 1, first, jnp.where(place == pics + 2, middle, last))
            slot = jnp.logical_not(sides[h]) & (place > pics) & (place < pics + 4)
            aug_ref[h, rows, :] = jnp.where(slot, logs, query[h])
        out_ref[rows, :] = jnp.where(sides[0], results[0], results[1]).astype(BF16)


def head_norm_back(e, raw, gain, means):
    raw = raw.astype(F32)
    c = raw - group_sum(raw, means)
    r = lax.rsqrt(group_sum(c * c, means) + EPSILON)
    n = c * r
    t = e * gain
    grad = r * (t - group_sum(t, means) - n * group_sum(t * n, means))
    return grad.astype(BF16), jnp.sum(e * n, axis=0, keepdims=True)


def attend_back_kernel(
    pics, aug_ref, k_ref, v_ref, out_ref, do_ref, rawq_ref, rawk_ref, qg_ref, kg_ref, bounds_ref,
    dq_ref, dk_ref, dv_ref, qgg_ref, kgg_ref, kaug, vaug, doaug, qsum, ksum,
):
    length = k_ref.shape[0]
    queries = do_ref.shape[0]
    part = length // 4
    whole = queries == length
    lane = lax.broadcasted_iota(jnp.int32, (1, 128), 1)
    place = lane % HEAD
    sides = [lane < HEAD, lane >= HEAD]
    kmarks = key_marks(bounds_ref, place, length, pics)
    vmarks = jnp.where(place < 2, 1.0, 0.0).astype(BF16)
    ones = group_ones(1.0)
    inner = group_sum_fine(do_ref[...].astype(F32) * out_ref[...].astype(F32), ones)
    inner = -pltpu.roll(inner, HEAD, 1)
    inner_high = inner.astype(BF16)
    inner_low = (inner - inner_high.astype(F32)).astype(BF16)
    zero = jnp.zeros((), BF16)
    gmarks = jnp.where(place == 0, inner_high, jnp.where(place == 1, inner_low, zero))
    for h in range(2):
        kaug[h] = jnp.where(sides[h], k_ref[...], kmarks)
        vaug[h] = jnp.where(sides[h], v_ref[...], vmarks)
        doaug[h] = jnp.where(sides[h], do_ref[...], gmarks)
    for b in range(length // STEP):
        keys = pl.ds(b * STEP, STEP)
        key = [kaug[h, keys, :] for h in range(2)]
        value = [vaug[h, keys, :] for h in range(2)]
        dk = [jnp.zeros((STEP, 128), F32)] * 2
        dv = [jnp.zeros((STEP, 128), F32)] * 2
        for j in range(queries // STEP):
            rows = pl.ds(j * STEP, STEP)
            query = [aug_ref[h, rows, :] for h in range(2)]
            grad = [doaug[h, rows, :] for h in range(2)]
            scores = [nt(key[h], query[h]) for h in range(2)]
            soft_grad = [nt(value[h], grad[h]) for h in range(2)]
            weights = [jnp.exp2(x * EXP2_FACTOR) for x in scores]
            score_grad = [(weights[h] * soft_grad[h]).astype(BF16) for h in range(2)]
            for h in range(2):
                part_sum = tn(score_grad[h], key[h])
                if b == 0:
                    qsum[h, rows, :] = part_sum
                else:
                    qsum[h, rows, :] += part_sum
                dk[h] = dk[h] + jnp.dot(score_grad[h], query[h], preferred_element_type=F32)
                dv[h] = dv[h] + jnp.dot(weights[h].astype(BF16), grad[h], preferred_element_type=F32)
        ksum[keys, :] = jnp.where(sides[0], dk[0], dk[1]) * HEAD**-0.5
        dv_ref[keys, :] = jnp.where(sides[0], dv[0], dv[1]).astype(BF16)

    means = group_ones(1.0 / HEAD)
    gain_sum = jnp.zeros((1, 128), F32)
    for b in range(queries // part):
        rows = pl.ds(b * part, part)
        e = jnp.where(sides[0], qsum[0, rows, :], qsum[1, rows, :]) * HEAD**-0.5
        raw = own_rows(rawq_ref, b * part, part, queries, part)
        dq_ref[rows, :], more = head_norm_back(e.astype(BF16).astype(F32), raw, qg_ref[...], means)
        gain_sum = gain_sum + more
    qgg_ref[...] = gain_sum
    gain_sum = jnp.zeros((1, 128), F32)
    for b in range(length // part):
        rows = pl.ds(b * part, part)
        e = ksum[rows, :].astype(BF16)
        if whole:
            dk_ref[rows, :], more = head_norm_back(e.astype(F32), rawk_ref[rows, :], kg_ref[...], means)
            gain_sum = gain_sum + more
        else:
            dk_ref[rows, :] = e
    kgg_ref[...] = gain_sum


def shared_keys_kernel(dk_ref, dv_ref, gotk_ref, gotv_ref, rawk_ref, kg_ref, outk_ref, outv_ref, kgg_ref):
    count = outk_ref.shape[0]
    part = count // 2
    means = group_ones(1.0 / HEAD)
    gain_sum = jnp.zeros((1, 128), F32)
    for b in range(2):
        rows = pl.ds(b * part, part)
        own = lambda ref: own_rows(ref, b * part, part, count, part)
        e = own(dk_ref).astype(F32) + gotk_ref[rows, :].astype(F32)
        outk_ref[rows, :], more = head_norm_back(e, own(rawk_ref), kg_ref[...], means)
        gain_sum = gain_sum + more
        outv_ref[rows, :] = (own(dv_ref).astype(F32) + gotv_ref[rows, :].astype(F32)).astype(BF16)
    kgg_ref[...] = gain_sum


def gelu_pair(h):
    size = jnp.abs(h)
    bell = jnp.exp2(h * h * -0.7213475204444817)
    t = 1.0 / (1.0 + 0.23164189 * size)
    series = t * (0.127414796 + t * (-0.142248368 + t * (0.7107068705 + t * (-0.7265760135 + t * 0.5307027145))))
    tail = series * bell
    below = jnp.where(h < 0.0, tail, 1.0 - tail)
    return h * below, below + h * (bell * 0.3989422804014327)


def norm_parts(values):
    center = values - jnp.mean(values, axis=-1, keepdims=True)
    spread = lax.rsqrt(jnp.mean(center * center, axis=-1, keepdims=True) + EPSILON)
    return center * spread, spread


def norm_back(upstream, n, r, gain):
    t = upstream * gain
    grad = r * (t - jnp.mean(t, axis=-1, keepdims=True) - n * jnp.mean(t * n, axis=-1, keepdims=True))
    return grad, jnp.sum(upstream * n, axis=0, keepdims=True)


MESH_ID = pl.DeviceIdType.MESH


def here():
    return lax.axis_index("chip"), lax.axis_index("core"), lax.axis_index("zp"), lax.axis_index("zq")


def remote(source, target, sems, at, device):
    sent, got = sems
    return pltpu.make_async_remote_copy(
        src_ref=source, dst_ref=target, send_sem=sent.at[at], recv_sem=got.at[at],
        device_id=device, device_id_type=MESH_ID,
    )


def greet(devices, maybe=None, moves=None):
    barrier = pltpu.get_barrier_semaphore()
    for device in devices:
        pl.semaphore_signal(barrier, inc=1, device_id=device, device_id_type=MESH_ID)
    if maybe is None:
        pl.semaphore_wait(barrier, len(devices))
        return

    @pl.when(moves)
    def _():
        pl.semaphore_signal(barrier, inc=1, device_id=maybe, device_id_type=MESH_ID)

    pl.semaphore_wait(barrier, len(devices) + jnp.where(moves, 1, 0))


def rows_at(start, count):
    return pl.ds(pl.multiple_of(start, 16), count)


class Moves:
    def __init__(self, moved, stays, crossed, moves):
        self.moved, self.stays, self.crossed, self.moves = moved, stays, crossed, moves

    def each(self, act):
        if self.crossed is not None:
            act(self.crossed)

        @pl.when(self.moves)
        def _():
            for copy in self.moved:
                act(copy)

        @pl.when(jnp.logical_not(self.moves))
        def _():
            for copy in self.stays:
                act(copy)

    def start(self):
        self.each(lambda copy: copy.start())

    def wait(self):
        self.each(lambda copy: copy.wait())


class Line:
    def __init__(self, parts, whole, right, left, sems, at):
        chip, core, zp, zq = here()
        self.z = 2 * zp + zq
        up, down = jnp.minimum(self.z + 1, 3), jnp.maximum(self.z - 1, 0)
        self.next = (chip, core, up // 2, up % 2)
        self.last = (chip, core, down // 2, down % 2)
        self.parts, self.whole, self.right, self.left = parts, whole, right, left
        self.sems, self.at, self.sends = sems, at, []

    def at_chip(self, z, *acts):
        @pl.when(self.z == z)
        def _():
            for act in acts:
                act()

    def part_copy(self, c, rightward):
        if rightward:
            return remote(self.parts.at[c], self.right.at[3 - c], self.sems, self.at + 3 - c, self.next)
        return remote(self.parts.at[c], self.left.at[c], self.sems, self.at + 3 + c, self.last)

    def whole_copy(self, c, rightward):
        if rightward:
            return remote(self.whole.at[c], self.whole.at[c], self.sems, self.at + 6 + c, self.next)
        return remote(self.whole.at[c], self.whole.at[c], self.sems, self.at + 8 + c, self.last)

    def send(self, z, make, c, rightward):
        self.sends.append((z, make, c, rightward))
        return lambda: make(c, rightward).start()

    def take(self, c, rightward):
        def act():
            self.part_copy(c, rightward).wait_recv()
            came = self.right[3 - c] if rightward else self.left[c]
            self.parts[c] = add(self.parts[c], came).astype(BF16)

        return act

    def got(self, c, rightward):
        return lambda: self.whole_copy(c, rightward).wait_recv()

    def start(self):
        part = self.part_copy
        self.at_chip(0, *[self.send(0, part, c, True) for c in (3, 2, 1)])
        self.at_chip(3, *[self.send(3, part, c, False) for c in (0, 1, 2)])

    def first(self):
        self.at_chip(1, self.take(3, True), self.send(1, self.part_copy, 3, True))
        self.at_chip(2, self.take(0, False), self.send(2, self.part_copy, 0, False))

    def second(self):
        part = self.part_copy
        self.at_chip(
            1, self.take(2, True), self.send(1, part, 2, True), self.take(0, False), self.send(1, part, 0, False)
        )
        self.at_chip(
            2, self.take(1, False), self.send(2, part, 1, False), self.take(3, True), self.send(2, part, 3, True)
        )

    def third(self):
        self.at_chip(0, self.take(0, False))
        self.at_chip(1, self.take(1, True), self.take(1, False))
        self.at_chip(2, self.take(2, True), self.take(2, False))
        self.at_chip(3, self.take(3, True))
        self.whole[self.z] = self.parts[self.z]
        for z in range(4):
            acts = [self.send(z, self.whole_copy, z, True)] if z < 3 else []
            acts += [self.send(z, self.whole_copy, z, False)] if z > 0 else []
            self.at_chip(z, *acts)

    def fourth(self):
        whole = self.whole_copy
        for z in (1, 2):
            self.at_chip(
                z, self.got(z - 1, True), self.send(z, whole, z - 1, True), self.got(z + 1, False),
                self.send(z, whole, z + 1, False),
            )

    def fifth(self):
        whole = self.whole_copy
        self.at_chip(1, self.got(3, False), self.send(1, whole, 3, False))
        self.at_chip(2, self.got(0, True), self.send(2, whole, 0, True))

    def sixth(self):
        self.at_chip(0, *[self.got(c, False) for c in (1, 2, 3)])
        self.at_chip(3, *[self.got(c, True) for c in (2, 1, 0)])

    def wait_sends(self):
        for z in range(4):
            mine = [make(c, rightward) for at, make, c, rightward in self.sends if at == z]
            self.at_chip(z, *[copy.wait_send for copy in mine])


def write_bounds(pics, lens_ref, bounds_ref, zp, zq, length):
    lane = lax.broadcasted_iota(jnp.int32, (8, 128), 1)
    lens = jnp.where(zp == 0, lens_ref[0], lens_ref[1])
    ends = lens
    for hop in (1, 2, 4, 8):
        ends = ends + jnp.where(lane >= hop, pltpu.roll(ends, hop, 1), 0)
    starts = ends - lens
    last = (lens > 0) & (pltpu.roll(lens, 127, 1) == 0)
    query_ends = jnp.where(last, length, ends)
    total = jnp.max(jnp.where(lane < pics, ends, 0), axis=1, keepdims=True)

    def both(values):
        values = jnp.where(lane < HEAD, jnp.where(lane < pics, values, 2 * length), 0)
        return values + pltpu.roll(values, HEAD, 1)

    tables = [both(starts), both(ends), both(query_ends), jnp.broadcast_to(total, (8, 128))]
    for t in range(4):
        table = tables[t]
        bounds_ref[0, t : t + 1, :] = jnp.where(zq == 0, table[0:1], table[1:2])
        bounds_ref[1, t : t + 1, :] = table[2:3]
    bounds_ref[:, 4:, :] = jnp.zeros((2, 4, 128), jnp.int32)


def forward_kernel(square, pics, *refs):
    refs = list(refs)
    take = lambda count: [refs.pop(0) for _ in range(count)]
    tokens_ref, cot_ref, lengths_ref, weight_in = take(4)
    if square:
        gain_in = take(4)
        up_in, outw_ref = take(2)
    else:
        gain_first_in, gain_qk_in = take(2)
    x_out, bounds_ref, mix_hbm, cot_hbm, gain_first, second_ref, gain_qk = take(7)
    names = ("normed", "qk", "v", "raw", "out", "aug")
    outs = [dict(zip(names, take(6))) for _ in range(2)]
    if square:
        up_hbm, outw_hbm = take(2)
    row_ref, shared_ref, cot_out, lens_ref, lens_out = take(5)
    scratch = [dict(zip(names, take(6))) for _ in range(2)]
    kaug, vaug, qaug = take(3)
    if square:
        mix_ref, gains_ref, up_ref, mix_out, gains_out, up_out, outw_out = take(7)
    sent, got, local_sem, write_sem = take(4)

    chip, core, zp, zq = here()
    z = 2 * zp + zq
    part = tokens_ref.shape[1]
    half, length = 2 * part, 4 * part
    sems = (sent, got)
    partner = (chip, 1 - core, zp, zq)
    side = (chip, core, zp, 1 - zq)
    keep = (chip, zp, core, zq)
    cross = (chip, zp, core, 1 - zq)
    moves = core != zp
    near_x = (chip ^ 1, core, zp, zq)
    near_y = (chip ^ 2, core, zp, zq)
    greet([partner, side, cross] + ([near_x, near_y] if square else []), keep, moves)

    def quarter(ref, index):
        return ref.at[rows_at(index * part, part)]

    own_row = remote(tokens_ref.at[zq], quarter(row_ref, z), sems, 0, keep)
    own_shared = remote(tokens_ref.at[2], quarter(shared_ref, z), sems, 2, keep)
    stay_row = pltpu.make_async_copy(tokens_ref.at[zq], quarter(row_ref, z), local_sem.at[0])
    stay_shared = pltpu.make_async_copy(tokens_ref.at[2], quarter(shared_ref, z), local_sem.at[1])

    @pl.when(moves)
    def _():
        own_row.start()

    @pl.when(jnp.logical_not(moves))
    def _():
        stay_row.start()

    cross_row = remote(tokens_ref.at[1 - zq], quarter(row_ref, z), sems, 1, cross)
    cross_row.start()

    @pl.when(moves)
    def _():
        own_shared.start()

    @pl.when(jnp.logical_not(moves))
    def _():
        stay_shared.start()

    lens_ref[...] = jnp.zeros_like(lens_ref)
    lens_ref[: lengths_ref.shape[0], :pics] = lengths_ref[...]
    lens_copy = remote(lens_ref, lens_out.at[core], sems, 8, partner)
    lens_copy.start()
    lens_stay = pltpu.make_async_copy(lens_ref, lens_out.at[core], local_sem.at[2])
    lens_stay.start()
    waits = []
    if square:
        shard = mix_ref.shape[1]
        tile = up_ref.shape[2] // 4
        width = mix_ref.shape[2] // 3
        for h in range(2):
            for i in range(3):
                mix_ref[h, :, i * width : (i + 1) * width] = weight_in[:, (2 * i + h) * width : (2 * i + h + 1) * width]
        gains_ref[...] = jnp.zeros_like(gains_ref)
        for i in range(4):
            gains_ref[i : i + 1, :shard] = gain_in[i][...].astype(F32)
        mine, theirs = 2 * chip + core, 2 * chip + 1 - core
        slot = [9]

        def send(source, target, device):
            copy = remote(source, target, sems, slot[0], device)
            slot[0] += 1
            copy.start()
            waits.append(copy)
            return copy

        def stay(source, target, at):
            copy = pltpu.make_async_copy(source, target, local_sem.at[at])
            copy.start()
            return copy

        def block(ref, start, count):
            return ref.at[rows_at(start, count)]

        mix_piece = lambda index: (block(mix_out, index * shard, shard), gains_out.at[index])

        def send_mix(sources, index, device):
            return [send(source, target, device) for source, target in zip(sources, mix_piece(index))]

        def arrived(copies):
            for copy in copies:
                copy.wait_recv()

        x_mine, y_other = 2 * (chip ^ 1) + core, 2 * (chip ^ 2) + 1 - core
        to_core = send_mix((mix_ref.at[1 - core], gains_ref), mine, partner)
        a_x = send_mix((mix_ref.at[core], gains_ref), mine, near_x)
        a_y = send_mix((mix_ref.at[core], gains_ref), mine, near_y)
        for h in range(2):
            for i in range(4):
                up_ref[h, :, i * tile : (i + 1) * tile] = up_in[:, (2 * i + h) * tile : (2 * i + h + 1) * tile]
        up_core = send(up_ref.at[1 - core], block(up_out, mine * shard, shard), partner)
        out_core = send(outw_ref, block(outw_out, mine * shard, shard), partner)
        stays = [
            stay(mix_ref.at[core], mix_piece(mine)[0], 3),
            stay(gains_ref, gains_out.at[mine], 4),
            stay(up_ref.at[core], block(up_out, mine * shard, shard), 5),
            stay(outw_ref, block(outw_out, mine * shard, shard), 6),
        ]
        arrived(to_core)
        b_x = send_mix(mix_piece(theirs), theirs, near_x)
        b_y = send_mix(mix_piece(theirs), theirs, near_y)
        arrived(a_x)
        a_far = send_mix(mix_piece(x_mine), x_mine, near_y)
        arrived(b_y)
        b_far = send_mix(mix_piece(y_other), y_other, near_x)
        for copy in stays:
            copy.wait()
        arrived([up_core])
        ohalf = shard // 2

        def bundle(first, from_chip):
            same, twin = 2 * from_chip + core, 2 * from_chip + 1 - core
            part_of = 0 if first else 1
            return [
                block(up_out, (same if first else twin) * shard, shard),
                block(outw_out, same * shard + part_of * ohalf, ohalf),
            ]

        def send_bundle(first, from_chip, device):
            return [send(ref, ref, device) for ref in bundle(first, from_chip)]

        first_x = send_bundle(True, chip, near_x)
        first_y = send_bundle(True, chip, near_y)
        second_x = send_bundle(False, chip, near_x)
        second_y = send_bundle(False, chip, near_y)

    lens_copy.wait()
    lens_stay.wait()
    write_bounds(pics, lens_out, bounds_ref, zp, zq, length)
    if square:
        arrived(a_y + b_x + a_far + b_far)
        for p in range(gains_out.shape[0]):
            lanes = slice(p * shard, (p + 1) * shard)
            values = gains_out[p, :, :shard]
            gain_first[:, lanes] = values[0:1]
            second_ref[:, lanes] = values[3:4]
            half_pieces = gains_out.shape[0] // 2

            @pl.when(core == p // half_pieces)
            def _():
                at = (p % half_pieces) * shard
                gain_qk[:, at : at + shard] = values[1:2]
                gain_qk[:, width + at : width + at + shard] = values[2:3]
        weight = mix_out
    else:
        weight = weight_in
        width = weight.shape[1] // 3
        second_ref[...] = jnp.zeros_like(second_ref)
        gain_first[...] = gain_first_in[...]
        gain_qk[...] = gain_qk_in[...]
    writes = []

    def write(source, target, at):
        copy = pltpu.make_async_copy(source, target, write_sem.at[at])
        copy.start()
        writes.append(copy)

    write(weight, mix_hbm, 0)
    first, second = 2 * core + zq, 2 * core + 1 - zq
    other_first, other_second = 2 * (1 - core) + zq, 2 * (1 - core) + 1 - zq

    def forwarded(ref, index, at):
        return remote(quarter(ref, index), quarter(ref, index), sems, at, partner)

    def project(tokens, bufs, at):
        rows = rows_at(at * part, part)
        project_kernel(
            tokens.at[rows], gain_first, weight, gain_qk, bufs["normed"].at[rows], bufs["qk"].at[rows],
            bufs["v"].at[rows], bufs["raw"].at[rows],
        )

    def project_row(i, _):
        @pl.when(i == 0)
        def _():
            @pl.when(moves)
            def _():
                own_row.wait_recv()

            @pl.when(jnp.logical_not(moves))
            def _():
                stay_row.wait()

            forwarded(row_ref, first, 3).start()

        @pl.when(i == 1)
        def _():
            cross_row.wait_recv()
            forwarded(row_ref, second, 4).start()

        @pl.when(i == 2)
        def _():
            forwarded(row_ref, other_first, 3).wait_recv()

        @pl.when(i == 3)
        def _():
            forwarded(row_ref, other_second, 4).wait_recv()

        order = jnp.where(i == 0, first, jnp.where(i == 1, second, jnp.where(i == 2, other_first, other_second)))
        project(row_ref, scratch[0], order)
        return 0

    row_one, row_two = forwarded(row_ref, first, 3), forwarded(row_ref, second, 4)

    def attend(bufs, bounds):
        def one(p, _):
            lanes = pl.ds(pl.multiple_of(p * 128, 128), 128)
            attend_kernel(
                pics, bufs["qk"].at[:, lanes],
                bufs["qk"].at[:, pl.ds(pl.multiple_of(width + p * 128, 128), 128)], bufs["v"].at[:, lanes], bounds,
                bufs["out"].at[:, lanes], bufs["aug"].at[pl.ds(2 * p, 2)], kaug, vaug, qaug.at[pl.ds(0, bufs["out"].shape[0])],
            )
            return 0

        lax.fori_loop(0, width // 128, one, 0)

    lax.fori_loop(0, 4, project_row, 0)
    for i, name in enumerate(("normed", "qk", "v", "raw")):
        write(scratch[0][name], outs[0][name], 1 + i)
    write(row_ref.at[rows_at(core * half, half)], x_out.at[pl.ds(0, half)], 5)

    @pl.when(moves)
    def _():
        own_shared.wait_recv()

    @pl.when(jnp.logical_not(moves))
    def _():
        stay_shared.wait()

    to_side = remote(quarter(shared_ref, first), quarter(shared_ref, first), sems, 5, side)
    to_side.start()
    shared_one = remote(quarter(shared_ref, first), quarter(shared_ref, first), sems, 6, partner)
    shared_one.start()
    attend(scratch[0], bounds_ref.at[0])
    cot_moves = Moves(
        [remote(cot_ref.at[zq], cot_out, sems, 43, keep)],
        [pltpu.make_async_copy(cot_ref.at[zq], cot_out, local_sem.at[0])],
        None,
        moves,
    )
    cot_moves.start()
    write(scratch[0]["out"], outs[0]["out"], 6)
    write(scratch[0]["aug"], outs[0]["aug"], 7)
    to_side.wait_recv()
    shared_two = forwarded(shared_ref, second, 7)
    shared_two.start()
    if square:
        arrived(first_x + second_y)
        far_first = send_bundle(True, chip ^ 1, near_y)
        far_second = send_bundle(False, chip ^ 2, near_x)
    shared_one.wait_recv()
    shared_two.wait_recv()

    def project_shared(i, _):
        project(shared_ref, scratch[1], i)
        return 0

    lax.fori_loop(0, 4, project_shared, 0)
    for i, name in enumerate(("normed", "qk", "v", "raw")):
        write(scratch[1][name], outs[1][name], 8 + i)
    write(shared_ref.at[rows_at(first * part, part)], x_out.at[pl.ds(half, part)], 12)
    if square:
        arrived(first_y + second_x + far_first + far_second)
        sent_pieces = []
        for c in (chip ^ 1, chip ^ 2, chip ^ 3):
            target = block(outw_out, (2 * c + core) * shard, shard)
            sent_pieces.append(send(target, target, partner))
        write(up_out, up_hbm, 15)
    attend(scratch[1], bounds_ref.at[1])
    write(scratch[1]["out"], outs[1]["out"], 13)
    write(scratch[1]["aug"], outs[1]["aug"], 14)

    if square:
        arrived(sent_pieces + [out_core])
        write(outw_out, outw_hbm, 17)
        for copy in waits:
            copy.wait_send()
    cot_moves.wait()
    write(cot_out, cot_hbm, 18)
    for copy in (row_one, row_two, shared_one, shared_two, to_side, cross_row):
        copy.wait_send()

    @pl.when(moves)
    def _():
        own_row.wait_send()
        own_shared.wait_send()

    for copy in writes:
        copy.wait()


def forward_pass(square, pics, tokens, cotangent, lengths, weight, *more):
    _, part, model = tokens.shape
    length, half, width = 4 * part, 2 * part, model // 2
    near = pl.BlockSpec(memory_space=pltpu.VMEM)
    anywhere = pl.BlockSpec(memory_space=pl.ANY)
    low = lambda *shape: (shape, BF16)
    wide = lambda *shape: (shape, F32)
    outs = [
        (low(3 * part, model), anywhere),
        (((2, 8, 128), jnp.int32), near),
        (low(model, 3 * width), anywhere),
        (low(part, model), anywhere),
        (wide(1, model), near),
        (wide(1, model), near),
        (wide(1, model), near),
    ]
    bufs = []
    for queries in (length, half):
        shapes = [
            low(length, model), low(length, 2 * width), low(length, width), low(length, 2 * width),
            low(queries, width), low(2 * (width // 128), queries, 128),
        ]
        outs += [(shape, anywhere) for shape in shapes]
        bufs += shapes
    table = ((8, 128), jnp.int32)
    scratch = [low(length, model), low(length, model), low(part, model), table, ((2, 8, 128), jnp.int32)] + bufs
    scratch += [low(2, length, 128), low(2, length, 128), low(length, 128)]
    if square:
        up, _ = more[4:]
        shard, hidden = up.shape
        landed = [low(model, hidden // 2), low(model, model)]
        outs += [(shape, anywhere) for shape in landed]
        scratch += [low(2, shard, 3 * width), wide(8, 128), low(2, shard, hidden // 2)]
        scratch += [low(model, 3 * width), wide(8, 8, 128)] + landed
    return pl.pallas_call(
        functools.partial(forward_kernel, square, pics),
        in_specs=[near] * (4 + len(more)),
        out_specs=[spec for _, spec in outs],
        out_shape=[jax.ShapeDtypeStruct(*shape) for shape, _ in outs],
        scratch_shapes=[pltpu.VMEM(*shape) for shape in scratch]
        + [
            pltpu.SemaphoreType.DMA((49,)),
            pltpu.SemaphoreType.DMA((49,)),
            pltpu.SemaphoreType.DMA((8,)),
            pltpu.SemaphoreType.DMA((19,)),
        ],
        compiler_params=pltpu.CompilerParams(
            collective_id=0, has_side_effects=True, vmem_limit_bytes=60 * 1024 * 1024
        ),
        name="forward_pass",
    )(tokens, cotangent, lengths, weight, *more)


def dense_kernel(
    square, out_ref, shared_ref, x, grad_ref, cot_ref, outw_ref, gain_ref, bounds_ref, up_ref, down_ref,
    output_ref, midg_ref, row_grad, shared_grad, outg_ref, gaing_ref, packed_ref, far_ref,
    att_other, second, turned, grad, cot_in, hidden_all, pre_all, forward, backward, middle, up, down,
    results, parts_out, parts_in, heads_out, cols_out, cols_in, stage, far_in,
    sent, got, load_sem, write_sem, local_sem,
):
    chip, core, zp, zq = here()
    sems = (sent, got)
    partner = (chip, 1 - core, zp, zq)
    keep = (chip, zp, core, zq)
    cross = (chip, zp, core, 1 - zq)
    moves = core != zp
    near_x = (chip ^ 1, core, zp, zq)
    near_y = (chip ^ 2, core, zp, zq)
    tokens, model = midg_ref.shape
    part = tokens // 3
    half = 2 * part
    width = out_ref.shape[1]
    units = up.shape[1]
    tile = units // 4
    other = 1 - core
    mine, theirs = pl.ds(0, tokens), pl.ds(tokens, tokens)
    own_down = down.at[rows_at(chip * tile, tile)] if square else down
    loads = [
        pltpu.make_async_copy(up_ref, up, load_sem.at[0]),
        pltpu.make_async_copy(down_ref, own_down, load_sem.at[1]),
    ]
    for copy in loads:
        copy.start()
    greet([partner, cross] + ([near_x, near_y] if square else []), keep, moves)
    att_sends = [
        remote(out_ref.at[rows_at(other * half, half)], att_other.at[pl.ds(0, half)], sems, 0, partner),
        remote(shared_ref.at[rows_at(other * part, part)], att_other.at[pl.ds(half, part)], sems, 1, partner),
    ]
    for copy in att_sends:
        copy.start()
    cot_move = Moves(
        [remote(cot_ref.at[2], cot_in.at[1], sems, 11, keep)],
        [pltpu.make_async_copy(cot_ref.at[2], cot_in.at[1], local_sem.at[0])],
        remote(cot_ref.at[1 - zq], cot_in.at[0], sems, 22, cross),
        moves,
    )
    cot_move.start()

    def down_half(index, which):
        return down.at[rows_at(index * tile + which * (tile // 2), tile // 2)]

    def send_down(index, which, at, device):
        copy = remote(down_half(index, which), down_half(index, which), sems, at, device)
        copy.start()
        return copy

    slot = lax.broadcasted_iota(jnp.int32, (part, 1), 0)
    filled, shared_filled = bounds_ref[0, 3:4, 0:1], bounds_ref[1, 3:4, 0:1]
    none = jnp.zeros((), BF16)

    def take_grad(values, at, start, limit, sem):
        rows = rows_at(at, part)
        grad[rows, :] = jnp.where(slot + start < limit, values, none)
        copy = remote(grad.at[rows], grad.at[rows_at(tokens + at, part)], sems, sem, partner)
        copy.start()
        return copy

    grad_sends = [take_grad(grad_ref[...], zq * part, (2 * core + zq) * part, filled, 2)]

    own_rows_of = lambda b: (
        out_ref[rows_at(core * half + b * part, part), :] if b < 2 else shared_ref[rows_at(core * part, part), :]
    )
    own_weight = outw_ref[rows_at(core * width, width), :]
    other_weight = outw_ref[rows_at(other * width, width), :]
    blocks = [pl.ds(b * part, part) for b in range(3)]
    for b in range(3):
        middle[blocks[b], :] = x[blocks[b], :].astype(F32) + jnp.dot(
            own_rows_of(b), own_weight, preferred_element_type=F32
        )
    for copy in loads:
        copy.wait()
    if square:
        down_sends = [
            send_down(chip, 0, 12, near_x), send_down(chip, 1, 13, near_y), send_down(chip, 0, 14, near_y),
            send_down(chip, 1, 15, near_x),
        ]
    for copy in att_sends:
        copy.wait_recv()
    for rows in blocks:
        value = middle[rows, :] + jnp.dot(att_other[rows, :], other_weight, preferred_element_type=F32)
        middle[rows, :] = value
        second[rows, :] = (norm_parts(value)[0] * gain_ref[...]).astype(BF16)
    second_send = remote(second.at[mine], second.at[theirs], sems, 3, partner)
    second_send.start()

    def hidden_forward(start):
        rows = pl.ds(start, tokens)

        def one_tile(i, _):
            here_units = pl.ds(pl.multiple_of(i * tile, 128), tile)
            hidden, slope = gelu_pair(jnp.dot(second[rows, :], up[:, here_units], preferred_element_type=F32))
            hidden_all[rows, here_units] = hidden.astype(BF16)
            pre_all[rows, here_units] = slope.astype(BF16)
            return 0

        lax.fori_loop(0, 4, one_tile, 0)

    def hidden_backward(start):
        rows = pl.ds(start, tokens)

        def one_tile(i, _):
            here_units = pl.ds(pl.multiple_of(i * tile, 128), tile)
            pre_grad = nt(grad[rows, :], down[rows_at(i * tile, tile), :]) * pre_all[rows, here_units].astype(F32)
            pre_all[rows, here_units] = pre_grad.astype(BF16)
            return 0

        lax.fori_loop(0, 4, one_tile, 0)

    hidden_forward(0)
    if square:
        down_sends[0].wait_recv()
        down_sends[1].wait_recv()
        down_sends += [send_down(chip ^ 1, 0, 16, near_y), send_down(chip ^ 2, 1, 17, near_x)]
    second_send.wait_recv()
    hidden_forward(tokens)
    if square:
        for copy in down_sends[2:]:
            copy.wait_recv()
    for b in range(3):
        rows, there = pl.ds(tokens + b * part, part), blocks[b]
        parts_out[0, there, :] = jnp.dot(hidden_all[rows, :], down[...], preferred_element_type=F32).astype(BF16)
    first_part = remote(parts_out.at[0], parts_in.at[0], sems, 4, partner)
    first_part.start()
    for rows in blocks:
        forward[rows, :] = middle[rows, :] + jnp.dot(hidden_all[rows, :], down[...], preferred_element_type=F32)
    turned[...] = second[...].T
    first_part.wait_recv()
    for rows in blocks:
        results[rows, :] = (forward[rows, :] + parts_in[0, rows, :].astype(F32)).astype(BF16)
    kept_rows, third_rows = results.at[rows_at(zq * part, part)], results.at[pl.ds(half, part)]
    output_moves = Moves(
        [
            remote(kept_rows, output_ref.at[zq], sems, 19, keep),
            remote(third_rows, output_ref.at[2], sems, 20, keep),
        ],
        [
            pltpu.make_async_copy(kept_rows, output_ref.at[zq], local_sem.at[1]),
            pltpu.make_async_copy(third_rows, output_ref.at[2], local_sem.at[2]),
        ],
        remote(results.at[rows_at((1 - zq) * part, part)], output_ref.at[zq], sems, 21, cross),
        moves,
    )
    output_moves.start()
    cot_move.wait()
    grad_sends.append(take_grad(cot_in[0], (1 - zq) * part, (2 * core + 1 - zq) * part, filled, 18))
    grad_sends.append(take_grad(cot_in[1], half, (2 * core + zq) * part, shared_filled, 23))
    hidden_backward(0)
    for copy in grad_sends:
        copy.wait_recv()
    hidden_backward(tokens)
    quarter = model // 4
    far_sends = [
        remote(stage.at[0, pl.ds(0, tile)], far_in.at[0], sems, 9, near_y),
        remote(stage.at[0, pl.ds(tile, tile)], far_in.at[1], sems, 10, near_x),
    ]

    def weight_grads(i, _):
        target = chip ^ (3 - i) if square else 3 - i
        place = jnp.where(i == 0, 0, 1 + i % 2)

        @pl.when(i == 3)
        def _():
            pltpu.make_async_copy(stage.at[place], packed_ref.at[target], write_sem.at[place]).wait()

        here_units = pl.ds(pl.multiple_of(target * tile, 128), tile)
        stage[place, pl.ds(0, tile), :] = tn(hidden_all[:, here_units], grad[...]).astype(BF16)
        values = jnp.dot(
            turned[rows_at(target * quarter, quarter), :], pre_all[...], preferred_element_type=F32
        ).astype(BF16)
        for j in range(2):
            stage[place, pl.ds(tile + j * quarter, quarter), :] = values[:, j * model : (j + 1) * model]
        pltpu.make_async_copy(stage.at[place], packed_ref.at[target], write_sem.at[place]).start()
        if square:

            @pl.when(i == 0)
            def _():
                for copy in far_sends:
                    copy.start()

        return 0

    lax.fori_loop(0, 4, weight_grads, 0)

    for b in range(3):
        rows, there = pl.ds(tokens + b * part, part), blocks[b]
        parts_out[1, there, :] = nt(pre_all[rows, :], up[...]).astype(BF16)
    second_part = remote(parts_out.at[1], parts_in.at[1], sems, 5, partner)
    second_part.start()
    for rows in blocks:
        backward[rows, :] = nt(pre_all[rows, :], up[...])
    second_send.wait_send()
    second_part.wait_recv()
    gain_sum = jnp.zeros(gaing_ref.shape, F32)
    for rows in blocks:
        n, r = norm_parts(middle[rows, :])
        upstream = backward[rows, :] + parts_in[1, rows, :].astype(F32)
        more, gain_more = norm_back(upstream, n, r, gain_ref[...])
        gain_sum = gain_sum + gain_more
        value = grad[rows, :].astype(F32) + more
        midg_ref[rows, :] = value
        branch = value.astype(BF16)
        second[rows, :] = branch
        heads_out[rows, :] = nt(branch, other_weight).astype(BF16)
    gaing_ref[...] = gain_sum
    head_sends = [
        remote(heads_out.at[pl.ds(0, half)], row_grad.at[rows_at(core * half, half)], sems, 6, partner),
        remote(heads_out.at[pl.ds(half, part)], shared_grad.at[rows_at(core * part, part)], sems, 7, partner),
    ]
    for copy in head_sends:
        copy.start()
    branch = second[mine, :]
    forward[rows_at(core * width, width), :] = tn(
        out_ref[rows_at(core * half, half), :], second[pl.ds(0, half), :]
    ) + tn(shared_ref[rows_at(core * part, part), :], second[pl.ds(half, part), :])
    forward[rows_at(other * width, width), :] = tn(att_other[...], branch)
    lanes = lambda side: pl.ds(pl.multiple_of(side * width, 128), width)
    cols_out[...] = forward[pl.ds(0, model), lanes(other)].astype(BF16)
    cols_send = remote(cols_out, cols_in, sems, 8, partner)
    cols_send.start()
    for b in range(3):
        value = nt(second[blocks[b], :], own_weight).astype(BF16)
        if b < 2:
            row_grad[rows_at(core * half + b * part, part), :] = value
        else:
            shared_grad[rows_at(core * part, part), :] = value
    cols_send.wait_recv()
    outg_ref[...] = (forward[pl.ds(0, model), lanes(core)] + cols_in[...].astype(F32)).astype(BF16)
    for copy in head_sends:
        copy.wait_recv()
    for copy in att_sends + head_sends + grad_sends + [first_part, second_part, cols_send]:
        copy.wait_send()
    if square:
        for copy in down_sends:
            copy.wait_send()
        for copy in far_sends:
            copy.wait()
    far_write = pltpu.make_async_copy(far_in, far_ref, load_sem.at[0])
    far_write.start()
    for place in range(3):
        pltpu.make_async_copy(stage.at[place], packed_ref.at[0], write_sem.at[place]).wait()
    output_moves.wait()
    far_write.wait()


def dense(square, out, shared_out, x, grad, cotangent, out_matrix, gain, bounds, up, down):
    model = x.shape[1]
    tokens = x.shape[0]
    part = tokens // 3
    length, width = out.shape
    units = up.shape[1]
    tile = units // 4
    anywhere = pl.BlockSpec(memory_space=pl.ANY)
    near = pl.BlockSpec(memory_space=pltpu.VMEM)
    both = 2 * tokens
    low = lambda *shape: pltpu.VMEM(shape, BF16)
    wide = lambda *shape: pltpu.VMEM(shape, F32)
    return pl.pallas_call(
        functools.partial(dense_kernel, square),
        in_specs=[near] * 4 + [anywhere] + [near] * 3 + [anywhere] * 2,
        out_specs=[anywhere] + [near] * 5 + [anywhere, anywhere],
        out_shape=[
            jax.ShapeDtypeStruct((3, part, model), BF16),
            jax.ShapeDtypeStruct((tokens, model), F32),
            jax.ShapeDtypeStruct((length, width), BF16),
            jax.ShapeDtypeStruct((length // 2, width), BF16),
            jax.ShapeDtypeStruct((model, width), BF16),
            jax.ShapeDtypeStruct((1, model), F32),
            jax.ShapeDtypeStruct((4, 2 * tile, model), BF16),
            jax.ShapeDtypeStruct((2, tile, model), BF16),
        ],
        scratch_shapes=[
            low(tokens, width), low(both, model), low(model, both), low(both, model), low(2, part, model),
            low(both, units), low(both, units), wide(tokens, model), wide(tokens, model), wide(tokens, model),
            low(model, units), low(units, model), low(tokens, model), low(2, tokens, model), low(2, tokens, model),
            low(tokens, width), low(model, width), low(model, width), low(3, 2 * tile, model), low(2, tile, model),
            pltpu.SemaphoreType.DMA((24,)),
            pltpu.SemaphoreType.DMA((24,)),
            pltpu.SemaphoreType.DMA((2,)),
            pltpu.SemaphoreType.DMA((3,)),
            pltpu.SemaphoreType.DMA((3,)),
        ],
        compiler_params=pltpu.CompilerParams(
            collective_id=1, has_side_effects=True, vmem_limit_bytes=63 * 1024 * 1024
        ),
        name="dense",
    )(out, shared_out, x, grad, cotangent, out_matrix, gain, bounds, up, down)


def add(*terms):
    total = terms[0].astype(F32)
    for term in terms[1:]:
        total = total + term.astype(F32)
    return total


def backward_kernel(square, pics, *refs):
    refs = list(refs)
    take = lambda count: [refs.pop(0) for _ in range(count)]
    names = ("aug", "qk", "v", "out", "do", "raw", "normed")
    row_in = dict(zip(names, take(7)))
    shared_in = dict(zip(names, take(7)))
    mix_in, x_in, midg_in, gain_first, gain_qk, gain_second_grad, bounds_ref = take(7)
    if square:
        packed_in, far_ref, outg_in = take(3)
        grad_out, total_ref, gains_ref, up_ref, down_ref, outw_ref = take(6)
    else:
        grad_own, mix_grad_ref, gains_sum = take(3)
    names = names[:-1]
    row = dict(zip(names, take(6)))
    shared = dict(zip(names, take(6)))
    normed, weight, x, midg = take(4)
    kaug, vaug, doaug, qsum, ksum, mixed, part_k, part_v, got_k, got_v = take(10)
    gain_sums, parts_out, parts_in = take(3)
    if square:
        grad_own, payload, gains_sum, outg = take(4)
        held, far_in, onward_out, onward_in, direct_in, line, whole_line, line_right, line_left = take(9)
        up_out, up_got = take(2)
        relay, final, core_got, chunks, chunk_whole, chunk_right, chunk_left, gain_parts, gain_got = take(9)
    sent, got, load_sem, local_sem = take(4)

    chip, core, zp, zq = here()
    z = 2 * zp + zq
    sems = (sent, got)
    partner = (chip, 1 - core, zp, zq)
    keep = (chip, zp, core, zq)
    cross = (chip, zp, core, 1 - zq)
    moves = core != zp
    near_x = (chip ^ 1, core, zp, zq)
    near_y = (chip ^ 2, core, zp, zq)
    along = [(chip, core, zp, 1 - zq), (chip, core, 1 - zp, zq), (chip, core, 1 - zp, 1 - zq)]
    tokens, model = x.shape
    part = tokens // 3
    half, length = 2 * part, 4 * part
    width = model // 2
    queries = half
    waits = []

    def load(source, target, at):
        copy = pltpu.make_async_copy(source, target, load_sem.at[at])
        copy.start()
        return copy

    def send(source, target, at, device):
        copy = remote(source, target, sems, at, device)
        copy.start()
        waits.append(copy)
        return copy

    if square:
        rows_count = packed_in.shape[1]
        span = rows_count // 2
        first_half, second_half = pl.ds(0, span), pl.ds(span, span)
        held_loads = [
            load(packed_in.at[chip ^ 1, first_half], held.at[0], 24),
            load(packed_in.at[chip ^ 2, second_half], held.at[1], 25),
            load(packed_in.at[chip, first_half], held.at[2], 26),
            load(packed_in.at[chip, second_half], held.at[3], 27),
        ]
        far_loads = [load(far_ref.at[i], far_in.at[i], 28 + i) for i in range(2)]
    keys_of = lambda ref: ref.at[:, pl.ds(width, width)]
    load_bufs = lambda source, target, at: [
        load(keys_of(source[name]) if name == "qk" else source[name], target[name], at + i)
        for i, name in enumerate(names)
    ]
    shared_loads = load_bufs(shared_in, shared, 0)
    row_loads = load_bufs(row_in, row, 6)
    late_loads = [
        load(row_in["normed"], normed.at[pl.ds(0, length)], 12),
        load(shared_in["normed"].at[rows_at(zq * part, part)], normed.at[pl.ds(length, part)], 13),
        load(
            shared_in["normed"].at[rows_at((2 + zq) * part, part)], normed.at[pl.ds(length + part, part)], 14
        ),
        load(mix_in, weight, 15),
        load(x_in, x, 16),
        load(midg_in, midg, 17),
    ]
    if square:
        late_loads.append(load(outg_in, outg, 18))
    if square:
        greet([partner, cross, near_x, near_y] + along, keep, moves)
        bulk_x = send(packed_in.at[chip ^ 1, second_half], direct_in.at[0], 2, near_x)
        bulk_y = send(packed_in.at[chip ^ 2, first_half], direct_in.at[1], 3, near_y)
        for copy in held_loads + far_loads:
            copy.wait()
        onward_out[0] = add(far_in[0], held[0]).astype(BF16)
        bulk_on_x = send(onward_out.at[0], onward_in.at[0], 11, near_x)
        onward_out[1] = add(far_in[1], held[1]).astype(BF16)
        bulk_on_y = send(onward_out.at[1], onward_in.at[1], 12, near_y)

        bulk_line = Line(line, whole_line, line_right, line_left, sems, 14)
        mix_line = Line(chunks, chunk_whole, chunk_right, chunk_left, sems, 26)
    else:
        greet([partner, along[0]])

    gain_sums[...] = jnp.zeros_like(gain_sums)

    def attend_back(bufs, bounds, count, q_lanes_to, k_to, v_to, at, between=None):
        def one(p, _):
            if between is not None:
                pl.when(p == 2)(between)
            lanes = pl.ds(pl.multiple_of(p * 128, 128), 128)
            key_lanes = pl.ds(pl.multiple_of(width + p * 128, 128), 128)
            attend_back_kernel(
                pics, bufs["aug"].at[pl.ds(2 * p, 2)], bufs["qk"].at[:, lanes], bufs["v"].at[:, lanes],
                bufs["out"].at[:, lanes], bufs["do"].at[:, lanes], bufs["raw"].at[:, lanes],
                bufs["raw"].at[:, key_lanes], gain_qk.at[:, lanes], gain_qk.at[:, key_lanes], bounds,
                q_lanes_to(p), k_to(p), v_to(p), gain_sums.at[pl.ds(at, 1), lanes], gain_sums.at[pl.ds(at + 1, 1), lanes],
                kaug, vaug, doaug.at[:, pl.ds(0, count)], qsum.at[:, pl.ds(0, count)], ksum,
            )
            return 0

        lax.fori_loop(0, width // 128, one, 0)

    def mixed_at(start, count, side):
        return lambda p: mixed.at[pl.ds(start, count), pl.ds(pl.multiple_of(side * width + p * 128, 128), 128)]

    whole_lanes = lambda ref: lambda p: ref.at[:, pl.ds(pl.multiple_of(p * 128, 128), 128)]
    for copy in shared_loads:
        copy.wait()
    attend_back(
        shared, bounds_ref.at[1], queries, mixed_at(length, queries, 0), whole_lanes(part_k), whole_lanes(part_v), 0
    )
    side_sends = []
    for i in range(2):
        theirs = rows_at((2 * i + 1 - zq) * part, part)
        there = pl.ds(i * part, part)
        side_sends.append(send(part_k.at[theirs], got_k.at[there], 7 + 2 * i, along[0]))
        side_sends.append(send(part_v.at[theirs], got_v.at[there], 8 + 2 * i, along[0]))
    for copy in row_loads:
        copy.wait()
    def start_line():
        for copy in (bulk_y, bulk_on_x, bulk_x, bulk_on_y):
            copy.wait_recv()
        first_sum = add(held[2], onward_in[0], direct_in[1]).astype(BF16)
        second_half_sum = add(held[3], onward_in[1], direct_in[0]).astype(BF16)
        for i in range(2):
            line[i] = first_sum[i * quarter_rows : (i + 1) * quarter_rows]
            line[2 + i] = second_half_sum[i * quarter_rows : (i + 1) * quarter_rows]
        bulk_line.start()

    if square:
        quarter_rows = rows_count // 4
    attend_back(
        row, bounds_ref.at[0], length, mixed_at(0, length, 0), mixed_at(0, length, 1), mixed_at(0, length, 2), 2,
        start_line if square else None,
    )

    if square:
        bulk_line.first()
    for copy in side_sends:
        copy.wait_recv()

    def shared_pair(p, _):
        lanes = pl.ds(pl.multiple_of(p * 128, 128), 128)
        key_lanes = pl.ds(pl.multiple_of(width + p * 128, 128), 128)
        shared_keys_kernel(
            part_k.at[:, lanes], part_v.at[:, lanes], got_k.at[:, lanes], got_v.at[:, lanes],
            shared["raw"].at[:, key_lanes], gain_qk.at[:, key_lanes], mixed_at(length, queries, 1)(p),
            mixed_at(length, queries, 2)(p), gain_sums.at[pl.ds(4, 1), lanes],
        )
        return 0

    lax.fori_loop(0, width // 128, shared_pair, 0)
    for copy in late_loads:
        copy.wait()
    other = 1 - core
    block_rows = lambda side, b: (
        rows_at(side * half + b * part, part) if b < 2 else rows_at(length + side * part, part)
    )
    for b in range(3):
        parts_out[pl.ds(b * part, part), :] = nt(mixed[block_rows(other, b), :], weight[...]).astype(BF16)
    part_send = send(parts_out, parts_in, 13, partner)
    if square:
        bulk_line.second()
    shard = model // 8
    if square:
        for i in range(3):
            lanes = slice(i * width, (i + 1) * width)
            value = tn(normed[...], mixed[:, lanes]).astype(BF16)
            for p in range(8):
                payload[p, :shard, lanes] = value[p * shard : (p + 1) * shard]
        bulk_line.third()
    else:
        for i in range(3):
            lanes = slice(i * width, (i + 1) * width)
            mix_grad_ref[:, lanes] = tn(normed[...], mixed[:, lanes]).astype(BF16)
    part_send.wait_recv()
    first_sum_gain = jnp.zeros((1, model), F32)
    for b in range(3):
        rows = pl.ds(b * part, part)
        upstream = nt(mixed[block_rows(core, b), :], weight[...]) + parts_in[rows, :].astype(F32)
        n, r = norm_parts(x[rows, :].astype(F32))
        value, more = norm_back(upstream, n, r, gain_first[...])
        first_sum_gain = first_sum_gain + more
        grad_own[rows, :] = (midg[rows, :] + value).astype(BF16)
    gains_sum[...] = jnp.zeros_like(gains_sum)
    gains_sum[0:1, :] = first_sum_gain
    mine_lanes = pl.ds(pl.multiple_of(core * width, 128), width)
    gains_sum[1:2, mine_lanes] = gain_sums[0:1, :] + gain_sums[2:3, :]
    gains_sum[2:3, mine_lanes] = gain_sums[3:4, :] + gain_sums[4:5, :]
    gains_sum[3:4, :] = gain_second_grad[...]

    if square:
        kept_rows, third_rows = grad_own.at[rows_at(zq * part, part)], grad_own.at[pl.ds(half, part)]
        grad_moves = Moves(
            [
                remote(kept_rows, grad_out.at[zq], sems, 0, keep),
                remote(third_rows, grad_out.at[2], sems, 1, keep),
            ],
            [
                pltpu.make_async_copy(kept_rows, grad_out.at[zq], local_sem.at[0]),
                pltpu.make_async_copy(third_rows, grad_out.at[2], local_sem.at[1]),
            ],
            remote(grad_own.at[rows_at((1 - zq) * part, part)], grad_out.at[zq], sems, 4, cross),
            moves,
        )
        grad_moves.start()
        gain_row = shard + shard // 3
        for p in range(8):
            payload[p, gain_row:, :] = jnp.zeros((16, 3 * width), BF16)
            payload[p, gain_row:, :shard] = gains_sum[:, p * shard : (p + 1) * shard].astype(BF16)
            for i in range(3):
                at = p * shard + i * (shard // 3)
                payload[p, shard:gain_row, i * width : (i + 1) * width] = outg[at : at + shard // 3, :]
        mine, theirs = 2 * chip + core, 2 * chip + 1 - core
        x_mine, x_other = 2 * (chip ^ 1) + core, 2 * (chip ^ 1) + 1 - core
        y_mine, y_other = 2 * (chip ^ 2) + core, 2 * (chip ^ 2) + 1 - core
        far_mine, far_other = 2 * (chip ^ 3) + core, 2 * (chip ^ 3) + 1 - core
        first = send(payload.at[far_mine], relay.at[0], 38, near_y)
        second = send(payload.at[far_other], relay.at[1], 39, near_x)
        direct_x = send(payload.at[x_other], final.at[0], 40, near_x)
        direct_y = send(payload.at[y_mine], final.at[1], 41, near_y)

        first.wait_recv()
        relay[2] = add(relay[0], payload[x_mine]).astype(BF16)
        onward_x = send(relay.at[2], final.at[2], 42, near_x)
        second.wait_recv()
        relay[3] = add(relay[1], payload[y_other]).astype(BF16)
        onward_y = send(relay.at[3], final.at[3], 43, near_y)
        bulk_line.fourth()
        direct_x.wait_recv()
        onward_y.wait_recv()
        relay[4] = add(payload[theirs], final[0], final[3]).astype(BF16)
        to_core = send(relay.at[4], core_got, 44, partner)
        direct_y.wait_recv()
        onward_x.wait_recv()
        kept = add(payload[mine], final[1], final[2])
        quarter = gain_row // 2
        for i in range(2):
            chunks[2 * core + i] = kept[i * quarter : (i + 1) * quarter].astype(BF16)
        to_core.wait_recv()
        for i in range(2):
            chunks[2 * (1 - core) + i] = core_got[i * quarter : (i + 1) * quarter]
        gain_parts[0] = (kept[gain_row:] + core_got[gain_row:].astype(F32)).astype(BF16)
        mix_line.start()
        gain_lanes = pl.ds(0, 128)
        gain_sends = [
            send(gain_parts.at[0, :, gain_lanes], gain_got.at[i, :, gain_lanes], 45 + i, along[i]) for i in range(3)
        ]
        bulk_line.fifth()
        mix_line.first()
        mix_line.second()
        mix_line.third()
        for copy in gain_sends:
            copy.wait_recv()
        gains_ref[...] = add(
            gain_parts[0, :, :128], gain_got[0, :, :128], gain_got[1, :, :128], gain_got[2, :, :128]
        )
        mix_line.fourth()
        bulk_line.sixth()

        def place(index, values):
            side, up = index // 2, index % 2
            lanes_of = lambda p: slice((2 * p + side) * width, (2 * p + side + 1) * width)
            below = shard - quarter
            for p in range(3):
                part_of = values[:, p * width : (p + 1) * width]
                if up == 0:
                    total_ref[0:quarter, lanes_of(p)] = part_of
                else:
                    total_ref[quarter:shard, lanes_of(p)] = part_of[:below]
                    rows = slice(p * (shard // 3), (p + 1) * (shard // 3))
                    outw_ref[rows, side * width : (side + 1) * width] = part_of[below:]

        flat = jnp.concatenate([whole_line[i] for i in range(4)], axis=0)
        tile = down_ref.shape[0]
        ups = [flat[tile + 2 * shard * i : tile + 2 * shard * (i + 1)] for i in range(2)]
        for i in range(2):
            up_out[i] = jnp.where(core == 0, ups[i][shard:], ups[i][:shard])
        up_send = send(up_out, up_got, 48, partner)
        mix_line.fifth()
        down_ref[...] = flat[:tile]

        def place_up(side, i, values):
            for j in range(2):
                lanes = pl.ds(pl.multiple_of((2 * (2 * i + j) + side) * tile, 128), tile)
                up_ref[:, lanes] = values[:, j * tile : (j + 1) * tile]

        for i in range(2):
            place_up(core, i, jnp.where(core == 0, ups[i][:shard], ups[i][shard:]))
        up_send.wait_recv()
        for i in range(2):
            place_up(other, i, up_got[i])
        mix_line.sixth()
        for i in range(4):
            place(i, chunk_whole[i])
        bulk_line.wait_sends()
        mix_line.wait_sends()
        grad_moves.wait()
    for copy in waits:
        copy.wait_send()


def backward_pass(square, pics, row, shared, weights, gains, bounds, *more):
    length, model = row[1].shape
    width = model // 2
    part = length // 4
    half, tokens = 2 * part, 3 * part
    shard = model // 8
    near = pl.BlockSpec(memory_space=pltpu.VMEM)
    anywhere = pl.BlockSpec(memory_space=pl.ANY)
    low = lambda *shape: (shape, BF16)
    wide = lambda *shape: (shape, F32)
    if square:
        rows = more[0].shape[1]
        tile = rows // 2
        outs = [
            (low(3, part, model), anywhere),
            (low(shard, 6 * width), near),
            (wide(16, 128), near),
            (low(shard, 8 * tile), near),
            (low(tile, model), near),
            (low(shard, model), near),
        ]
    else:
        outs = [(low(tokens, model), near), (low(model, 3 * width), near), (wide(16, model), near)]
    scratch = []
    for queries in (length, half):
        scratch += [
            low(2 * (width // 128), queries, 128), low(length, width), low(length, width), low(queries, width),
            low(queries, width), low(length, 2 * width),
        ]
    scratch += [
        low(length + half, model), low(model, 3 * width), low(tokens, model), wide(tokens, model),
        low(2, length, 128), low(2, length, 128), low(2, length, 128), wide(2, length, 128), wide(length, 128),
        low(length + half, 3 * width), low(length, width), low(length, width), low(half, width), low(half, width),
        wide(8, width), low(tokens, model), low(tokens, model),
    ]
    if square:
        span = rows // 2
        pieces = shard + shard // 3 + 16
        chunk = (pieces - 16) // 2
        scratch += [
            low(tokens, model), low(8, pieces, 3 * width), wide(16, model), low(model, width),
            low(4, span, model), low(2, span, model), low(2, span, model), low(2, span, model), low(2, span, model),
            low(4, rows // 4, model), low(4, rows // 4, model), low(3, rows // 4, model), low(3, rows // 4, model),
            low(2, shard, model), low(2, shard, model),
            low(5, pieces, 3 * width), low(4, pieces, 3 * width), low(pieces, 3 * width), low(4, chunk, 3 * width),
            low(4, chunk, 3 * width), low(3, chunk, 3 * width), low(3, chunk, 3 * width), low(1, 16, 3 * width),
            low(3, 16, 3 * width),
        ]
    return pl.pallas_call(
        functools.partial(backward_kernel, square, pics),
        in_specs=[anywhere] * 17 + [near] * 4 + [anywhere] * len(more),
        out_specs=[spec for _, spec in outs],
        out_shape=[jax.ShapeDtypeStruct(*shape) for shape, _ in outs],
        scratch_shapes=[pltpu.VMEM(*shape) for shape in scratch]
        + [
            pltpu.SemaphoreType.DMA((49,)),
            pltpu.SemaphoreType.DMA((49,)),
            pltpu.SemaphoreType.DMA((30,)),
            pltpu.SemaphoreType.DMA((2,)),
        ],
        compiler_params=pltpu.CompilerParams(
            collective_id=2, has_side_effects=True, vmem_limit_bytes=62 * 1024 * 1024
        ),
        name="backward_pass",
    )(*row, *shared, *weights, *gains, bounds, *more)


def local(
    tokens, lengths, pictures, first_gain, mix_weight, query_gain, key_gain, out_weight,
    second_gain, up_weight, down_weight, cotangent,
):
    chip, core, zp, zq = here()
    chips = lax.axis_size("chip")
    square = chips == 4
    rows = ("chip", "core")
    _, part, model = tokens.shape
    length = 4 * part
    half = 2 * part
    width = HEADS // 2 * HEAD
    pics = lengths.shape[1]
    shard = mix_weight.shape[0]

    hidden = up_weight.shape[1]
    tile = hidden // 8
    gains = [gain[None] for gain in (first_gain, query_gain, key_gain, second_gain)]
    if square:
        forward = forward_pass(
            True, pics, tokens, cotangent, lengths, mix_weight, *gains, up_weight, out_weight
        )
        up_half, out_matrix = forward[19:]
        down_half = down_weight
        gain_second = forward[5]
    else:
        gather = lambda weight: lax.all_gather(weight, rows, axis=0, tiled=True)
        half_of = lambda weight, axis: pick(weight, core, axis)
        mix_half = half_of(gather(mix_weight).reshape(model, 3, 2, width), 2).reshape(model, 3 * width)
        up_half = half_of(gather(up_weight).reshape(model, 4, 2, tile), 2).reshape(model, 4 * tile)
        down_half = half_of(gather(down_weight).reshape(4, 2, tile, model), 1).reshape(4 * tile, model)
        out_matrix = gather(out_weight)
        gains = lax.all_gather(jnp.concatenate(gains), rows, axis=0, tiled=False)
        gains = gains.transpose(1, 0, 2).reshape(4, 1, model).astype(F32)
        gain_second = gains[3]
        gain_qk = half_of(gains[1:3].reshape(2, 2, width), 1).reshape(1, model)
        forward = forward_pass(False, pics, tokens, cotangent, lengths, mix_half, gains[0], gain_qk)
    own_tokens, bounds, mix_half, grad_tokens, gain_first, _, gain_qk = forward[:7]
    normed, qk, v, raw, out, aug = forward[7:13]
    shared_normed, shared_qk, shared_v, shared_raw, shared_out, shared_aug = forward[13:19]

    def collect(mine, cross, third):
        mine = lax.ppermute(mine, COLUMN, KEEP)
        cross = lax.ppermute(cross, COLUMN, CROSS)
        third = lax.ppermute(third, COLUMN, KEEP)
        return jnp.stack([jnp.where(zq == 0, mine, cross), jnp.where(zq == 0, cross, mine), third])

    output, middle_grad, grad, shared_grad, out_grad, second_gain_grad, packed, far = dense(
        square, out, shared_out, own_tokens, grad_tokens, cotangent, out_matrix, gain_second, bounds,
        up_half, down_half,
    )
    row_side = (aug, qk, v, out, grad, raw, normed)
    shared_side = (shared_aug, shared_qk, shared_v, shared_out, shared_grad, shared_raw, shared_normed)
    weights = (mix_half, own_tokens, middle_grad)
    gains = (gain_first, gain_qk, second_gain_grad)
    if square:
        input_out, mix_out, gains_out, up_out, down_out, outw_out = backward_pass(
            True, pics, row_side, shared_side, weights, gains, bounds, packed, far, out_grad
        )
        gains_out = gains_out[:4, :shard]
        mix_out, up_out, down_out, outw_out = (
            array.astype(F32) for array in (mix_out, up_out, down_out, outw_out)
        )
    else:
        input_grad, mix_grad, gain_grads = backward_pass(
            False, pics, row_side, shared_side, weights, gains, bounds
        )

        def reduce(grad):
            return lax.psum(lax.psum_scatter(grad, rows, scatter_dimension=0, tiled=True), SEQ).astype(F32)

        first, second = input_grad[:part], input_grad[part:half]
        input_out = collect(
            jnp.where(zq == 0, first, second), jnp.where(zq == 0, second, first), input_grad[half:]
        )
        own_core = jnp.arange(2) == core
        eighth = model // 8
        down_grad = packed[:, None, :tile]
        down_out = reduce(jnp.where(own_core[None, :, None, None], down_grad, 0).reshape(hidden, model))
        up_grad = packed[:, tile : 2 * tile].reshape(4, 2, 2 * eighth, 2, tile).transpose(0, 2, 1, 3, 4)
        up_grad = up_grad.reshape(model, 4, 1, tile)
        up_out = reduce(jnp.where(own_core[None, None, :, None], up_grad, 0).reshape(model, hidden))
        out_grad = out_grad.reshape(model, 1, width)
        outw_out = reduce(jnp.where(own_core[None, :, None], out_grad, 0).reshape(model, model))
        mix_out = reduce(
            jnp.where(own_core[None, None, :, None], mix_grad.reshape(model, 3, 1, width), 0).reshape(model, 6 * width)
        )
        gain_grads = gain_grads[:4].reshape(4, 2 * chips, shard).transpose(1, 0, 2).astype(BF16)
        gains_out = reduce(gain_grads).reshape(4, shard)
    return (
        output, input_out, gains_out[0], mix_out, gains_out[1], gains_out[2], outw_out, gains_out[3],
        up_out, down_out,
    )


def solution(mesh):
    fsdp = mesh.shape["fsdp"]
    split = Mesh(mesh.devices.reshape(fsdp // 2, 2, 2, 2), ("chip", "core", "zp", "zq"))
    rows = ("chip", "core")
    return jax.shard_map(
        local,
        mesh=split,
        in_specs=(
            P(rows, SEQ, None),
            P(rows, None),
            P(rows, SEQ),
            P(rows),
            P(rows, None),
            P(rows),
            P(rows),
            P(rows, None),
            P(rows),
            P(rows, None),
            P(rows, None),
            P(rows, SEQ, None),
        ),
        out_specs=(
            P(rows, SEQ, None),
            P(rows, SEQ, None),
            P(rows),
            P(rows, None),
            P(rows),
            P(rows),
            P(rows, None),
            P(rows),
            P(rows, None),
            P(rows, None),
        ),
        check_vma=False,
    )
```
